32 devices in a mesh: grp: 4 (over z), dev: 8 (over y, x, core).
Axes of the slice: x: 2, y: 2, z: 4, core: 2. Of those that a mesh axis runs over, the one named last changes fastest.
Arguments:
- inputs: bfloat16 [8, 2048, 1024], P('grp', 'dev'), may hold values from -6 to 6
- cotangent: bfloat16 [8, 2048, 1024], P('grp', 'dev'), may hold values from -6 to 6
- weight_slots: float32 [768, 128, 128], P(('grp', 'dev')), may hold values from -0.1875 to 0.1875
- slot_block: int32 [768], replicated, may hold values from 0 to 767, each once
- left_stats: float32 [768, 128, 128], P(('grp', 'dev')), may hold values from -491.52 to 503316.48, as said below
- right_stats: float32 [768, 128, 128], P(('grp', 'dev')), may hold values from -491.52 to 503316.48, as said below
- left_roots: float32 [768, 128, 128], P(('grp', 'dev')), may hold values from -0.0031570555 to 0.053095133, as said below
- right_roots: float32 [768, 128, 128], P(('grp', 'dev')), may hold values from -0.0031570555 to 0.053095133, as said below
- vectors: float32 [12288], replicated, may hold values from -0.9 to 1.5
- span_start: int32 [8], P('grp'), may hold values from 0 to 1792, as said below
Outputs:
- activations: bfloat16 [8, 2048, 1024], P('grp', 'dev')
- input_grad: float32 [8, 2048, 1024], P('grp', 'dev')
- weight_grads: float32 [768, 128, 128], P(('grp', 'dev'))
- new_left: float32 [768, 128, 128], P(('grp', 'dev'))
- new_right: float32 [768, 128, 128], P(('grp', 'dev'))
- new_weights: float32 [768, 128, 128], P(('grp', 'dev'))
- vector_grads: float32 [12288], replicated
- new_vectors: float32 [12288], replicated
The draws below stay inside these ranges and needn't reach their ends.
Inputs may be any that keep to these rules, and one draw needn't show every extreme that they name: `slot_block`: each block number once. `span_start`: a multiple of 256; each span lies inside its sequence. `left_stats`: symmetric matrices. `right_stats`: symmetric matrices. `left_roots`: symmetric matrices. `right_roots`: symmetric matrices.
All inputs are finite; a program needn't handle non-finite values.
Results may differ from the reference program's by a relative error of at most 0.012.
Values may be sent and summed in bfloat16 or wider, within the bound.
A program may use at most 320 MiB of HBM per device.

```python
import math
import jax
import jax.numpy as jnp
from jax import lax

D = 1024
H = 16
FF = 4096
SB = 128
PIC = 256
SEQLEN = 2048
NSEQ = 8
TOKENS = 16384
NBLK = 768


def draw_span_start(key, part):
    key = jax.random.fold_in(key, 3)
    return (jax.random.randint(key, (NSEQ,), 0, SEQLEN // PIC, dtype=jnp.int32) * PIC).astype(jnp.int32)


def draw_vectors(key, part):
    key = jax.random.fold_in(key, 5)
    key_gain, key_shift = jax.random.split(key)
    entry_count = 8 * D + FF
    places = jnp.arange(entry_count)
    is_gain = (places < D) | (places >= 5 * D) & (places < 6 * D)
    gains = jax.random.uniform(key_gain, (entry_count,), jnp.float32, 0.7, 1.3)
    shifts = 0.3 * jax.random.truncated_normal(key_shift, -3.0, 3.0, (entry_count,), jnp.float32)
    return jnp.where(is_gain, gains, shifts)


def statistics_draw(key):
    key_diag, key_noise = jax.random.split(key)
    grad_square = 0.06 * TOKENS
    level = SB * grad_square
    diagonal = level * jnp.exp(jax.random.uniform(key_diag, (NBLK, SB), jnp.float32, 0.0, math.log(4.0)))
    noise = jax.random.uniform(key_noise, (NBLK, SB, SB), jnp.float32, -1.0, 1.0) * (0.25 * grad_square)
    symmetric = noise + jnp.swapaxes(noise, 1, 2)
    identity = jnp.eye(SB, dtype=jnp.float32)
    return symmetric * (1.0 - identity) + diagonal[:, :, None] * identity


def roots_draw(key):
    key_diag, key_noise = jax.random.split(key)
    level = SB * 0.06 * TOKENS
    diagonal = (level * jnp.exp(jax.random.uniform(key_diag, (NBLK, SB), jnp.float32, 0.0, math.log(4.0)))) ** (-0.25)
    base_root = (2.0 * level) ** (-0.25)
    noise = jax.random.uniform(key_noise, (NBLK, SB, SB), jnp.float32, -1.0, 1.0) * (0.4 * base_root / math.sqrt(SB))
    symmetric = noise + jnp.swapaxes(noise, 1, 2)
    identity = jnp.eye(SB, dtype=jnp.float32)
    return symmetric * (1.0 - identity) + diagonal[:, :, None] * identity


def draw_left_stats(key, part):
    key = jax.random.fold_in(key, 7)
    return statistics_draw(key)


def draw_right_stats(key, part):
    key = jax.random.fold_in(key, 9)
    return statistics_draw(key)


def draw_left_roots(key, part):
    key = jax.random.fold_in(key, 13)
    return roots_draw(key)


def draw_right_roots(key, part):
    key = jax.random.fold_in(key, 17)
    return roots_draw(key)


def block_scale(rng, extent, cuts, least, top_value):
    level = 1.0
    for dim, parts in cuts:
        draws = jax.random.uniform(jax.random.fold_in(jax.random.fold_in(rng, 6), dim), (parts,), jnp.float32, least / len(cuts), top_value / len(cuts))
        level = level * jnp.repeat(jnp.exp(draws), extent[dim] // parts).reshape((-1,) + (1,) * (len(extent) - 1 - dim))
    return level


def bell_draw(rng, shape, scale, reach, cuts=(), kind=jnp.bfloat16):
    level = block_scale(rng, shape, cuts, -0.22, 0.18) if cuts else 1.0
    entries = jax.random.normal(rng, shape, jnp.float32) * scale * level
    return jnp.minimum(jnp.maximum(entries, -reach), reach).astype(kind)


def setup_inputs(seed: int = 0) -> dict:
    splits = jax.random.split(jax.random.key(seed), 11)
    inputs = bell_draw(splits[0], (NSEQ, SEQLEN, D), 1.0, 6.0, ((0, 4), (1, 8)))
    cotangent = bell_draw(splits[1], (NSEQ, SEQLEN, D), 1.0, 6.0, ((0, 4), (1, 8)))
    weight_slots = bell_draw(splits[2], (NBLK, SB, SB), D ** -0.5, 0.1875, ((0, 32),), jnp.float32)
    slot_block = jax.random.permutation(splits[3], NBLK).astype(jnp.int32)
    left_stats = draw_left_stats(jax.random.fold_in(splits[10], 71), 0)
    right_stats = draw_right_stats(jax.random.fold_in(splits[10], 71), 0)
    left_roots = draw_left_roots(jax.random.fold_in(splits[10], 71), 0)
    right_roots = draw_right_roots(jax.random.fold_in(splits[10], 71), 0)
    vectors = draw_vectors(jax.random.fold_in(splits[10], 71), 0)
    span_start = draw_span_start(jax.random.fold_in(splits[10], 71), 0)
    return {"inputs": inputs, "cotangent": cotangent, "weight_slots": weight_slots, "slot_block": slot_block, "left_stats": left_stats, "right_stats": right_stats, "left_roots": left_roots, "right_roots": right_roots, "vectors": vectors, "span_start": span_start}


@jax.custom_vjp
def low(v):
    return lax.optimization_barrier(v.astype(jnp.bfloat16)).astype(jnp.float32)

@jax.custom_vjp
def low_back(v):
    return v

def low_keep(v):
    return (low(v), None)

def low_pass(kept, grad):
    return (grad,)

def back_keep(v):
    return (v, None)

def back_low(kept, grad):
    return (low(grad),)
low.defvjp(low_keep, low_pass)
low_back.defvjp(back_keep, back_low)
eps = 1e-05
weight_rate = 0.5
vector_rate = 0.5
big_negative = -1e+30
highest = lax.Precision.HIGHEST

def round_both(value):
    return low(low_back(value))

def layer_norm(values, gain, shift):
    middle = lax.optimization_barrier(jnp.mean(values, axis=-1, keepdims=True))
    centred = values - middle
    spread = lax.optimization_barrier(jnp.mean(centred * centred, axis=-1, keepdims=True))
    return centred * lax.rsqrt(spread + eps) * gain + shift

def gelu_tanh(values):
    return 0.5 * values * (1.0 + jnp.tanh(0.7978845608028654 * (values + 0.044715 * values * values * values)))

def invert_order(slot_block):
    places = jnp.arange(slot_block.shape[0], dtype=jnp.int32)
    matches = (slot_block[None, :] == places[:, None]).astype(jnp.int32)
    return lax.optimization_barrier(jnp.sum(matches * places[None, :], axis=1)).astype(jnp.int32)

def from_blocks(blocks, row_size, col_size, block_side):
    block_grid = blocks.reshape(row_size // block_side, col_size // block_side, block_side, block_side)
    return block_grid.transpose(0, 2, 1, 3).reshape(row_size, col_size)

def to_blocks(matrix, block_side):
    row_size, col_size = matrix.shape
    block_grid = matrix.reshape(row_size // block_side, block_side, col_size // block_side, block_side)
    return block_grid.transpose(0, 2, 1, 3).reshape(-1, block_side, block_side)

def split_matrices(ordered, model_width, hidden_width, block_side):
    shapes_list = [(model_width, 3 * model_width), (model_width, model_width), (model_width, hidden_width), (hidden_width, model_width)]
    matrices = []
    block_start = 0
    for row_size, col_size in shapes_list:
        block_count = row_size * col_size // (block_side * block_side)
        matrices.append(from_blocks(ordered[block_start:block_start + block_count], row_size, col_size, block_side))
        block_start = block_start + block_count
    return matrices

def split_vectors(vectors, model_width):
    pieces = [vectors[index_now * model_width:(index_now + 1) * model_width] for index_now in range(8)]
    return pieces + [vectors[8 * model_width:]]

def score_bias(query_pos, key_pos, span_first, slopes, span_width):
    distance = jnp.abs(query_pos[:, None] - key_pos[None, :]).astype(jnp.float32)
    penalty = -slopes[:, None, None] * distance[None, :, :]
    query_in = (query_pos[None, :] >= span_first[:, None]) & (query_pos[None, :] < span_first[:, None] + span_width)
    key_in = (key_pos[None, :] >= span_first[:, None]) & (key_pos[None, :] < span_first[:, None] + span_width)
    causal = key_pos[None, :] <= query_pos[:, None]
    visible = causal[None, :, :] | query_in[:, :, None] & key_in[:, None, :]
    return (penalty, visible[:, None, :, :])

def attend_sequence(queries, key_rows, values, span_first, slopes, score_scale):
    seq_len = queries.shape[0]
    block_rows = min(512, seq_len)
    key_pos = jnp.arange(seq_len, dtype=jnp.int32)

    def one_block(block_start):
        query_block = lax.dynamic_slice_in_dim(queries, block_start, block_rows, 0)
        query_pos = block_start + jnp.arange(block_rows, dtype=jnp.int32)
        scores = jnp.einsum('qhd,khd->hqk', query_block, key_rows, precision=highest) * score_scale
        penalty, visible = score_bias(query_pos, key_pos, span_first[None], slopes, PIC)
        scores = low_back(scores + penalty)
        scores = jnp.where(visible[0], scores, big_negative)
        probs = low(jax.nn.softmax(scores, axis=-1))
        return jnp.einsum('hqk,khd->qhd', probs, values, precision=highest)
    starts = jnp.arange(seq_len // block_rows, dtype=jnp.int32) * block_rows
    outcome = lax.map(jax.checkpoint(one_block), starts)
    return outcome.reshape(queries.shape)

def layer_forward(in_rows, w_qkv, w_out, w_up, w_down, vectors, span_start):
    model_width = in_rows.shape[-1]
    head_count = H
    head_size = model_width // head_count
    score_scale = head_size ** (-0.5)
    slopes = jnp.exp2(-8.0 * (jnp.arange(head_count, dtype=jnp.float32) + 1.0) / head_count)
    gain_one, shift_one, bias_query, bias_value, bias_out, gain_two, shift_two, bias_down, bias_up = split_vectors(vectors, model_width)
    normed_one = low(layer_norm(in_rows, gain_one, shift_one))
    joined = jnp.einsum('nsd,de->nse', normed_one, low(w_qkv), precision=highest)
    queries = round_both(joined[..., :model_width] + bias_query)
    key_rows = round_both(joined[..., model_width:2 * model_width])
    values = round_both(joined[..., 2 * model_width:] + bias_value)
    head_shape = queries.shape[:2] + (head_count, head_size)

    def per_sequence(packed):
        query_seq, key_seq, value_seq, span_first = packed
        return attend_sequence(query_seq, key_seq, value_seq, span_first, slopes, score_scale)
    attended = lax.map(per_sequence, (queries.reshape(head_shape), key_rows.reshape(head_shape), values.reshape(head_shape), span_start))
    attended = round_both(attended.reshape(queries.shape))
    branch = low_back(jnp.einsum('nsd,de->nse', attended, low(w_out), precision=highest) + bias_out)
    middle = in_rows + branch
    normed_two = low(layer_norm(middle, gain_two, shift_two))
    pre_act = low_back(jnp.einsum('nsd,df->nsf', normed_two, low(w_up), precision=highest) + bias_up)
    activated = low(gelu_tanh(pre_act))
    return middle + jnp.einsum('nsf,fd->nsd', activated, low(w_down), precision=highest) + bias_down

def reference(inputs, cotangent, weight_slots, slot_block, left_stats, right_stats, left_roots, right_roots, vectors, span_start):
    block_side = weight_slots.shape[1]
    slot_of = invert_order(slot_block)
    ordered = jnp.take(weight_slots, slot_of, axis=0)
    w_qkv, w_out, w_up, w_down = split_matrices(ordered, D, FF, block_side)

    def forward(in_rows, mat_qkv, mat_out, mat_up, mat_down, vector_all):
        return layer_forward(in_rows, mat_qkv, mat_out, mat_up, mat_down, vector_all, span_start)
    outcome, pullback = jax.vjp(forward, inputs.astype(jnp.float32), w_qkv, w_out, w_up, w_down, vectors)
    in_grad, grad_qkv, grad_out, grad_up, grad_down, vector_grads = pullback(cotangent.astype(jnp.float32))
    blocks = jnp.concatenate([to_blocks(grad_qkv, block_side), to_blocks(grad_out, block_side), to_blocks(grad_up, block_side), to_blocks(grad_down, block_side)], axis=0)
    weight_grads = jnp.take(blocks, slot_block, axis=0)
    new_left = 0.5 * left_stats + 0.5 * jnp.einsum('bij,bkj->bik', weight_grads, weight_grads, precision=highest)
    new_right = 0.5 * right_stats + 0.5 * jnp.einsum('bji,bjk->bik', weight_grads, weight_grads, precision=highest)
    shaped = jnp.einsum('bij,bjk->bik', left_roots, weight_grads, precision=highest)
    shaped = jnp.einsum('bij,bjk->bik', shaped, right_roots, precision=highest)
    new_weights = weight_slots - weight_rate * shaped
    new_vectors = vectors - vector_rate / math.sqrt(TOKENS) * vector_grads
    return (outcome.astype(jnp.bfloat16), in_grad, weight_grads, new_left, new_right, new_weights, vector_grads, new_vectors)
```

```python
import functools
import math

import jax
import jax.numpy as jnp
from jax import lax
from jax.experimental import pallas as pl
from jax.experimental.pallas import tpu as pltpu
from jax.sharding import PartitionSpec as P

H = 16
FF = 4096
PIC = 256

eps = 1e-05
weight_rate = 0.5
vector_rate = 0.5
big_negative = -1e30
highest = lax.Precision.HIGHEST
F32 = jnp.float32
BF16 = jnp.bfloat16
LOG2E = 1.4426950408889634
MIB = 1024 * 1024

GAIN1, SHIFT1, BQ, BV, BO, GAIN2, SHIFT2, BDOWN, BUP = range(9)


def dot_nn(a, b):
    return lax.dot_general(a, b, (((1,), (0,)), ((), ())), preferred_element_type=F32)


def dot_nt(a, b):
    return lax.dot_general(a, b, (((1,), (1,)), ((), ())), preferred_element_type=F32)


def invert_order(slot_block):
    places = jnp.arange(slot_block.shape[0], dtype=jnp.int32)
    matches = (slot_block[None, :] == places[:, None]).astype(jnp.int32)
    return jnp.sum(matches * places[None, :], axis=1)


def vmem():
    return pl.BlockSpec(memory_space=pltpu.VMEM)


def smem():
    return pl.BlockSpec(memory_space=pltpu.SMEM)


def hbm():
    return pl.BlockSpec(memory_space=pl.ANY)


def sds(shape, dtype):
    return jax.ShapeDtypeStruct(shape, dtype)


def params(mib=58, **kw):
    return pltpu.CompilerParams(vmem_limit_bytes=mib * MIB, **kw)


def layer_stats(v):
    middle = jnp.mean(v, axis=-1, keepdims=True)
    centred = v - middle
    spread = jnp.mean(centred * centred, axis=-1, keepdims=True)
    return centred, lax.rsqrt(spread + eps)


def fold_rows(v):
    return jnp.sum(v.reshape(v.shape[0] // 8, 8, v.shape[1]), axis=0)


def fetch_block(gath, slot, dst, row, col, sem, side):
    return pltpu.make_async_copy(
        gath.at[slot], dst.at[pl.ds(row, side), pl.ds(col, side)], sem
    )


def qkv_kernel(slot_ref, x_ref, vec_ref, gath, h1_ref, out_ref, wbuf, sems, *, nd):
    rows, width = x_ref.shape
    side = gath.shape[1]
    per = width // side
    lanes = out_ref.shape[3]
    for part in range(3):
        @pl.loop(0, per)
        def _(i):
            for j in range(per):
                slot = slot_ref[i * 3 * per + part * per + j]
                fetch_block(gath, slot, wbuf.at[part], pl.multiple_of(i * side, side), j * side, sems.at[part], side).start()

    chunk = 32
    gain = vec_ref[GAIN1:GAIN1 + 1, :]
    shift = vec_ref[SHIFT1:SHIFT1 + 1, :]

    @pl.loop(0, rows // chunk)
    def _(r):
        at = pl.ds(pl.multiple_of(r * chunk, chunk), chunk)
        centred, inv = layer_stats(x_ref[at, :].astype(F32))
        h1_ref[at, :] = (centred * inv * gain + shift).astype(BF16)

    for part in range(3):
        pltpu.make_async_copy(wbuf.at[part], wbuf.at[part], sems.at[part]).wait()
        for half in range(2):
            cols = slice(half * width // 2, (half + 1) * width // 2)
            res = dot_nn(h1_ref[...], wbuf[part, :, cols])
            if part == 0:
                res = res + vec_ref[BQ:BQ + 1, cols]
            if part == 2:
                res = res + vec_ref[BV:BV + 1, cols]
            res = res.astype(BF16)
            for d in range(nd // 2):
                out_ref[half * (nd // 2) + d, part, :, :] = res[:, d * lanes:(d + 1) * lanes]


def run_qkv(slot_of, x, vec, gath, nd):
    rows, width = x.shape
    lanes = width // nd
    return pl.pallas_call(
        functools.partial(qkv_kernel, nd=nd),
        out_shape=(sds((rows, width), BF16), sds((nd, 3, rows, lanes), BF16)),
        in_specs=[smem(), vmem(), vmem(), hbm()],
        out_specs=(vmem(), vmem()),
        scratch_shapes=[pltpu.VMEM((3, width, width), BF16), pltpu.SemaphoreType.DMA((3,))],
        compiler_params=params(),
        name="qkv",
    )(slot_of, x, vec, gath)


def bias_tables(slope_ref, below, diag, hpd, tok):
    u = lax.broadcasted_iota(jnp.int32, (tok, tok), 0)
    t = lax.broadcasted_iota(jnp.int32, (tok, tok), 1)
    ub = lax.broadcasted_iota(jnp.int32, (tok, 128), 0).astype(F32)
    near = jnp.minimum(u, 2 * t - u).astype(F32)
    for h in range(hpd):
        slope = slope_ref[h] * LOG2E
        below[h] = slope * ub
        full = slope * near
        diag[h, 1] = full
        diag[h, 0] = jnp.where(u <= t, full, big_negative)


def widen(b, tok):
    return jnp.concatenate([b] * (tok // 128), axis=1)


def head_mask(h, lanes, hpd, tok):
    lane = lax.broadcasted_iota(jnp.int32, (tok, lanes), 1)
    size = lanes // hpd
    return (lane >= h * size) & (lane < (h + 1) * size)


def attn_fwd_kernel(span_ref, slope_ref, qkv_ref, o_ref, ot_ref, lse_ref, vt, below, diag, *, hpd):
    nb, _, _, tok, lanes = qkv_ref.shape
    size = lanes // hpd
    scale = size ** (-0.5) * LOG2E
    seq = pl.program_id(0)
    start = span_ref[seq]
    bias_tables(slope_ref, below, diag, hpd, tok)

    @pl.loop(0, nb)
    def _(j):
        vt[:, pl.ds(pl.multiple_of(j * tok, tok), tok)] = qkv_ref[j, 2, 0].astype(F32).T.astype(BF16)

    @pl.loop(0, nb)
    def _(i):
        at_i = pl.ds(pl.multiple_of(i * tok, tok), tok)
        q = qkv_ref[i, 0, 0]
        k = qkv_ref[i, 1, 0]
        flag = (start == i * tok).astype(jnp.int32)
        qs = []
        state = []
        for h in range(hpd):
            qh = jnp.where(head_mask(h, lanes, hpd, tok), q, 0).astype(BF16) if hpd > 1 else q
            qs.append(qh)
            s = dot_nt(k, qh) * scale + diag[h, flag]
            m = jnp.max(s, axis=0, keepdims=True)
            p = jnp.exp2(s - m)
            total = jnp.sum(p, axis=0, keepdims=True)
            acc = dot_nn(vt[h * size:(h + 1) * size, at_i], p.astype(BF16))
            state.append((m, total, acc))

        def body(j, state):
            at_j = pl.ds(pl.multiple_of(j * tok, tok), tok)
            kj = qkv_ref[j, 1, 0]
            new = []
            for h in range(hpd):
                m, total, acc = state[h]
                shift = (slope_ref[h] * LOG2E) * ((j - i) * tok).astype(F32)
                s = dot_nt(kj, qs[h]) * scale + widen(below[h], tok)
                top = jnp.maximum(m, jnp.max(s, axis=0, keepdims=True) + shift)
                p = jnp.exp2(s - (top - shift))
                decay = jnp.exp2(m - top)
                total = total * decay + jnp.sum(p, axis=0, keepdims=True)
                acc = acc * decay + dot_nn(vt[h * size:(h + 1) * size, at_j], p.astype(BF16))
                new.append((top, total, acc))
            return tuple(new)

        state = lax.fori_loop(0, i, body, tuple(state))
        outs = []
        for h in range(hpd):
            m, total, acc = state[h]
            out = acc / total
            ot_ref[0, h * size:(h + 1) * size, at_i] = out
            lse_ref[0, h:h + 1, at_i] = m + jnp.log2(total)
            outs.append(out)
        out = jnp.concatenate(outs, axis=0) if hpd > 1 else outs[0]
        o_ref[i, 0] = out.T.astype(BF16)


def run_attn_fwd(span, slopes, qkv, hpd):
    nb, _, seqs, tok, lanes = qkv.shape
    t = nb * tok
    return pl.pallas_call(
        functools.partial(attn_fwd_kernel, hpd=hpd),
        grid=(seqs,),
        out_shape=(
            sds((nb, seqs, tok, lanes), BF16),
            sds((seqs, lanes, t), F32),
            sds((seqs, hpd, t), F32),
        ),
        in_specs=[
            smem(),
            smem(),
            pl.BlockSpec((nb, 3, 1, tok, lanes), lambda s: (0, 0, s, 0, 0)),
        ],
        out_specs=(
            pl.BlockSpec((nb, 1, tok, lanes), lambda s: (0, s, 0, 0)),
            pl.BlockSpec((1, lanes, t), lambda s: (s, 0, 0)),
            pl.BlockSpec((1, hpd, t), lambda s: (s, 0, 0)),
        ),
        scratch_shapes=[
            pltpu.VMEM((lanes, t), BF16),
            pltpu.VMEM((hpd, tok, 128), F32),
            pltpu.VMEM((hpd, 2, tok, tok), F32),
        ],
        compiler_params=params(),
        name="attn_fwd",
    )(span, slopes, qkv)


def attn_bwd_kernel(
    span_ref, slope_ref, qkv_ref, do_ref, ot_ref, lse_ref, out_ref,
    kt, qm, dom, delta, dqt, below, diag, *, hpd
):
    nb, _, _, tok, lanes = qkv_ref.shape
    size = lanes // hpd
    unit = size ** (-0.5)
    scale = unit * LOG2E
    seq = pl.program_id(0)
    start = span_ref[seq]
    bias_tables(slope_ref, below, diag, hpd, tok)

    @pl.loop(0, nb)
    def _(j):
        at_j = pl.ds(pl.multiple_of(j * tok, tok), tok)
        kt[:, at_j] = qkv_ref[j, 1, 0].astype(F32).T.astype(BF16)
        q = qkv_ref[j, 0, 0]
        do = do_ref[j, 0]
        for h in range(hpd):
            if hpd > 1:
                mask = head_mask(h, lanes, hpd, tok)
                qm[h, j] = jnp.where(mask, q, 0).astype(BF16)
                dom[h, j] = jnp.where(mask, do, 0).astype(BF16)
            else:
                qm[h, j] = q
                dom[h, j] = do
        prod = do.astype(F32).T * ot_ref[0, :, at_j]
        for h in range(hpd):
            delta[h:h + 1, at_j] = jnp.sum(prod[h * size:(h + 1) * size], axis=0, keepdims=True)
        dqt[:, at_j] = jnp.zeros((lanes, tok), F32)

    @pl.loop(0, nb)
    def _(j):
        at_j = pl.ds(pl.multiple_of(j * tok, tok), tok)
        k = qkv_ref[j, 1, 0]
        v = qkv_ref[j, 2, 0]
        flag = (start == j * tok).astype(jnp.int32)

        def tile(i, h, dk, dv, bias, low):
            at_i = pl.ds(pl.multiple_of(i * tok, tok), tok)
            qh = qm[h, i]
            doh = dom[h, i]
            s = dot_nt(k, qh) * scale + bias
            p = jnp.exp2(s - low)
            dp = dot_nt(v, doh)
            ds = (p * (dp - delta[h:h + 1, at_i])).astype(BF16)
            dv = dv + dot_nn(p.astype(BF16), doh)
            dk = dk + dot_nn(ds, qh)
            rows = slice(h * size, (h + 1) * size)
            dqt[rows, at_i] += dot_nn(kt[rows, at_j], ds)
            return dk, dv

        dk = jnp.zeros((tok, lanes), F32)
        dv = jnp.zeros((tok, lanes), F32)
        for h in range(hpd):
            dk, dv = tile(j, h, dk, dv, diag[h, flag], lse_ref[0, h:h + 1, at_j])

        def body(i, carry):
            dk, dv = carry
            at_i = pl.ds(pl.multiple_of(i * tok, tok), tok)
            for h in range(hpd):
                shift = (slope_ref[h] * LOG2E) * ((j - i) * tok).astype(F32)
                dk, dv = tile(i, h, dk, dv, widen(below[h], tok), lse_ref[0, h:h + 1, at_i] - shift)
            return dk, dv

        dk, dv = lax.fori_loop(j + 1, nb, body, (dk, dv))
        out_ref[j, 1, 0] = (dk * unit).astype(BF16)
        out_ref[j, 2, 0] = dv.astype(BF16)

    @pl.loop(0, nb)
    def _(j):
        at_j = pl.ds(pl.multiple_of(j * tok, tok), tok)
        out_ref[j, 0, 0] = (dqt[:, at_j].T * unit).astype(BF16)


def run_attn_bwd(span, slopes, qkv, do, ot, lse, hpd):
    nb, _, seqs, tok, lanes = qkv.shape
    t = nb * tok
    return pl.pallas_call(
        functools.partial(attn_bwd_kernel, hpd=hpd),
        grid=(seqs,),
        out_shape=sds(qkv.shape, BF16),
        in_specs=[
            smem(),
            smem(),
            pl.BlockSpec((nb, 3, 1, tok, lanes), lambda s: (0, 0, s, 0, 0)),
            pl.BlockSpec((nb, 1, tok, lanes), lambda s: (0, s, 0, 0)),
            pl.BlockSpec((1, lanes, t), lambda s: (s, 0, 0)),
            pl.BlockSpec((1, hpd, t), lambda s: (s, 0, 0)),
        ],
        out_specs=pl.BlockSpec((nb, 3, 1, tok, lanes), lambda s: (0, 0, s, 0, 0)),
        scratch_shapes=[
            pltpu.VMEM((lanes, t), BF16),
            pltpu.VMEM((hpd, nb, tok, lanes), BF16),
            pltpu.VMEM((hpd, nb, tok, lanes), BF16),
            pltpu.VMEM((max(hpd, 8), t), F32),
            pltpu.VMEM((lanes, t), F32),
            pltpu.VMEM((hpd, tok, 128), F32),
            pltpu.VMEM((hpd, 2, tok, tok), F32),
        ],
        compiler_params=params(),
        name="attn_bwd",
    )(span, slopes, qkv, do, ot, lse)


def mlp_kernel(
    slot_ref, o_ref, x_ref, dy_ref, vec_ref, gath,
    act_ref, att_ref, h2_ref, g_ref, dz_ref, da_ref, dx1_ref, do_ref, sums_ref,
    wo, wup, wdn, x1, acc, dh2, sem_o, sem_t, *, nd, first_o, first_up, first_dn, tile
):
    rows, width = x_ref.shape
    side = gath.shape[1]
    per = width // side
    ff = g_ref.shape[1]
    tiles = ff // tile
    cols = tile // side
    lanes = o_ref.shape[2]
    fper = ff // side

    @pl.loop(0, per)
    def _(i):
        for j in range(per):
            fetch_block(gath, slot_ref[first_o + i * per + j], wo, pl.multiple_of(i * side, side), j * side, sem_o.at[0], side).start()

    def fetch_tile(f):
        @pl.loop(0, per)
        def _(i):
            for j in range(cols):
                fetch_block(gath, slot_ref[first_up + i * fper + f * cols + j], wup.at[f], pl.multiple_of(i * side, side), j * side, sem_t.at[f], side).start()
            for j in range(cols):
                fetch_block(gath, slot_ref[first_dn + (f * cols + j) * per + i], wdn.at[f], j * side, pl.multiple_of(i * side, side), sem_t.at[f], side).start()

    fetch_tile(0)
    fetch_tile(1)
    for d in range(nd):
        att_ref[:, d * lanes:(d + 1) * lanes] = o_ref[d]
    pltpu.make_async_copy(wo, wo, sem_o.at[0]).wait()
    for half in range(2):
        c = slice(half * width // 2, (half + 1) * width // 2)
        x1[:, c] = x_ref[:, c].astype(F32) + dot_nn(att_ref[...], wo[:, c]) + vec_ref[BO:BO + 1, c]

    chunk = 32

    def rows_at(r):
        return pl.ds(pl.multiple_of(r * chunk, chunk), chunk)

    @pl.loop(0, rows // chunk)
    def _(r):
        at = rows_at(r)
        centred, inv = layer_stats(x1[at, :])
        h2_ref[at, :] = (centred * inv * vec_ref[GAIN2:GAIN2 + 1, :] + vec_ref[SHIFT2:SHIFT2 + 1, :]).astype(BF16)
        acc[at, :] = x1[at, :] + vec_ref[BDOWN:BDOWN + 1, :]
        dh2[at, :] = jnp.zeros((chunk, width), F32)

    @pl.loop(0, tiles)
    def _(f):
        @pl.when(f + 2 < tiles)
        def _():
            fetch_tile(f + 2)
        pltpu.make_async_copy(wup.at[f], wup.at[f], sem_t.at[f]).wait()
        pltpu.make_async_copy(wdn.at[f], wdn.at[f], sem_t.at[f]).wait()
        per_row = width // tile
        bias = vec_ref[pl.ds(BUP + f // per_row, 1), pl.ds(pl.multiple_of((f % per_row) * tile, tile), tile)]
        at_f = pl.ds(pl.multiple_of(f * tile, tile), tile)
        z = dot_nn(h2_ref[...], wup[f]) + bias
        dg = dot_nt(dy_ref[...], wdn[f])
        z2 = z * z
        th = jnp.tanh(0.7978845608028654 * (z + 0.044715 * z2 * z))
        g = (0.5 * z * (1.0 + th)).astype(BF16)
        slope = 0.5 * (1.0 + th) + 0.5 * z * (1.0 - th * th) * (
            0.7978845608028654 * (1.0 + 3.0 * 0.044715 * z2)
        )
        dz = (dg * slope).astype(BF16)
        g_ref[:, at_f] = g
        dz_ref[:, at_f] = dz
        sums_ref[pl.ds(pl.multiple_of(8 * (4 + f // per_row), 8), 8), pl.ds(pl.multiple_of((f % per_row) * tile, tile), tile)] = fold_rows(dz.astype(F32))
        acc[...] += dot_nn(g, wdn[f])
        dh2[...] += dot_nt(dz, wup[f])

    zero = jnp.zeros((8, width), F32)

    def finish(r, carry):
        s_bo, s_gain, s_shift, s_bdown = carry
        at = rows_at(r)
        act_ref[at, :] = acc[at, :].astype(BF16)
        centred, inv = layer_stats(x1[at, :])
        hat = centred * inv
        dh = dh2[at, :]
        dhg = dh * vec_ref[GAIN2:GAIN2 + 1, :]
        back = inv * (
            dhg
            - jnp.mean(dhg, axis=-1, keepdims=True)
            - hat * jnp.mean(dhg * hat, axis=-1, keepdims=True)
        )
        dy = dy_ref[at, :].astype(F32)
        dx1 = dy + back
        dx1_ref[at, :] = dx1
        da = dx1.astype(BF16)
        da_ref[at, :] = da
        return (
            s_bo + fold_rows(da.astype(F32)),
            s_gain + fold_rows(dh * hat),
            s_shift + fold_rows(dh),
            s_bdown + fold_rows(dy),
        )

    carry = lax.fori_loop(0, rows // chunk, finish, (zero, zero, zero, zero))
    for n in range(4):
        sums_ref[8 * n:8 * n + 8, :] = carry[n]
    for half in range(2):
        c = slice(half * width // 2, (half + 1) * width // 2)
        res = dot_nt(da_ref[...], wo[c, :]).astype(BF16)
        for d in range(nd // 2):
            do_ref[half * (nd // 2) + d] = res[:, d * lanes:(d + 1) * lanes]


def run_mlp(slot_of, o, x, dy, vec, gath, nd):
    rows, width = x.shape
    side = gath.shape[1]
    lanes = width // nd
    per = width // side
    first_o = 3 * per * per
    first_up = first_o + per * per
    first_dn = first_up + per * (FF // side)
    tile = 512
    return pl.pallas_call(
        functools.partial(
            mlp_kernel, nd=nd, first_o=first_o, first_up=first_up, first_dn=first_dn, tile=tile
        ),
        out_shape=(
            sds((rows, width), BF16),
            sds((rows, width), BF16),
            sds((rows, width), BF16),
            sds((rows, FF), BF16),
            sds((rows, FF), BF16),
            sds((rows, width), BF16),
            sds((rows, width), F32),
            sds((nd, rows, lanes), BF16),
            sds((8 * (4 + FF // width), width), F32),
        ),
        in_specs=[smem(), vmem(), vmem(), vmem(), vmem(), hbm()],
        out_specs=tuple([vmem()] * 9),
        scratch_shapes=[
            pltpu.VMEM((width, width), BF16),
            pltpu.VMEM((FF // tile, width, tile), BF16),
            pltpu.VMEM((FF // tile, tile, width), BF16),
            pltpu.VMEM((rows, width), F32),
            pltpu.VMEM((rows, width), F32),
            pltpu.VMEM((rows, width), F32),
            pltpu.SemaphoreType.DMA((1,)),
            pltpu.SemaphoreType.DMA((FF // tile,)),
        ],
        compiler_params=params(),
        name="mlp",
    )(slot_of, o, x, dy, vec, gath)


def dh1_kernel(
    slot_ref, dqkv_ref, x_ref, dx1_ref, vec_ref, gath, ig_ref, cat_ref, sums_ref,
    wbuf, dh1, sems, *, nd
):
    rows, width = x_ref.shape
    side = gath.shape[1]
    per = width // side
    lanes = dqkv_ref.shape[3]
    for part in range(3):
        @pl.loop(0, per)
        def _(i):
            for j in range(per):
                slot = slot_ref[i * 3 * per + part * per + j]
                fetch_block(gath, slot, wbuf.at[part], pl.multiple_of(i * side, side), j * side, sems.at[part], side).start()

    for part in range(3):
        for d in range(nd):
            at = part * width + d * lanes
            cat_ref[:, at:at + lanes] = dqkv_ref[d, part]
    for part in range(3):
        pltpu.make_async_copy(wbuf.at[part], wbuf.at[part], sems.at[part]).wait()
        for half in range(2):
            c = slice(half * width // 2, (half + 1) * width // 2)
            res = dot_nt(cat_ref[:, part * width:(part + 1) * width], wbuf[part, c, :])
            if part == 0:
                dh1[:, c] = res
            else:
                dh1[:, c] += res

    chunk = 32
    zero = jnp.zeros((8, width), F32)

    def finish(r, carry):
        s_gain, s_shift, s_bq, s_bv = carry
        at = pl.ds(pl.multiple_of(r * chunk, chunk), chunk)
        centred, inv = layer_stats(x_ref[at, :].astype(F32))
        hat = centred * inv
        dh = dh1[at, :]
        dhg = dh * vec_ref[GAIN1:GAIN1 + 1, :]
        back = inv * (
            dhg
            - jnp.mean(dhg, axis=-1, keepdims=True)
            - hat * jnp.mean(dhg * hat, axis=-1, keepdims=True)
        )
        ig_ref[at, :] = dx1_ref[at, :] + back
        return (
            s_gain + fold_rows(dh * hat),
            s_shift + fold_rows(dh),
            s_bq + fold_rows(cat_ref[at, 0:width].astype(F32)),
            s_bv + fold_rows(cat_ref[at, 2 * width:3 * width].astype(F32)),
        )

    carry = lax.fori_loop(0, rows // chunk, finish, (zero, zero, zero, zero))
    for n in range(4):
        sums_ref[8 * n:8 * n + 8, :] = carry[n]


def run_dh1(slot_of, dqkv, x, dx1, vec, gath, nd):
    rows, width = x.shape
    return pl.pallas_call(
        functools.partial(dh1_kernel, nd=nd),
        out_shape=(
            sds((rows, width), F32),
            sds((rows, 3 * width), BF16),
            sds((32, width), F32),
        ),
        in_specs=[smem(), vmem(), vmem(), vmem(), vmem(), hbm()],
        out_specs=(vmem(), vmem(), vmem()),
        scratch_shapes=[
            pltpu.VMEM((3, width, width), BF16),
            pltpu.VMEM((rows, width), F32),
            pltpu.SemaphoreType.DMA((3,)),
        ],
        compiler_params=params(),
        name="dh1",
    )(slot_of, dqkv, x, dx1, vec, gath)


def wgrad_kernel(
    slot_ref, h1, att, h2, g, dqkv, da, dz, dy, out,
    v_a, v_b, a_t, stage, sem_in, sem_out, *, side, tile
):
    rows, width = h1.shape
    per = width // side
    cols = tile // side
    ff = g.shape[1]
    runs = [(h2, 0, dz, 4 * per * per, ff // side)]
    for c in range(ff // width):
        first = 4 * per * per + per * (ff // side) + c * per * per
        runs.append((g, c * width, dy, first, per))
    runs.append((att, 0, da, 3 * per * per, per))
    runs.append((h1, 0, dqkv, 0, 3 * per))

    def loads(n):
        a, at, b, _, _ = runs[n]
        copies = [pltpu.make_async_copy(a.at[:, pl.ds(at, width)], v_a.at[n % 2], sem_in.at[n % 2, 0])]
        fresh = n == 0 or runs[n - 1][2] is not b
        if fresh:
            wide = b.shape[1]
            copies.append(
                pltpu.make_async_copy(b, v_b.at[slot_b[n], :, pl.ds(0, wide)], sem_in.at[n % 2, 1])
            )
        return copies

    slot_b = []
    for n in range(len(runs)):
        if n == 0:
            slot_b.append(0)
        elif runs[n - 1][2] is runs[n][2]:
            slot_b.append(slot_b[-1])
        else:
            slot_b.append(1 - slot_b[-1])

    started = {0: loads(0)}
    for copy in started[0]:
        copy.start()
    count = 0

    def out_wait(slot):
        pltpu.make_async_copy(stage.at[slot], stage.at[slot], sem_out.at[slot]).wait()

    for n in range(len(runs)):
        _, _, b, first, stride = runs[n]
        if n + 1 < len(runs):
            started[n + 1] = loads(n + 1)
            for copy in started[n + 1]:
                copy.start()
        for copy in started[n]:
            copy.wait()
        for r in range(width // 256):
            c = slice(r * 256, (r + 1) * 256)
            a_t[c, :] = v_a[n % 2, :, c].astype(F32).T.astype(BF16)
        sb = slot_b[n]
        base = count

        def step(t, base=base, first=first, stride=stride, sb=sb):
            slot = (base + t) % 2

            @pl.when(base + t >= 2)
            def _():
                out_wait(slot)
            res = dot_nn(a_t[...], v_b[sb, :, pl.ds(pl.multiple_of(t * tile, tile), tile)]).astype(BF16)
            for i in range(per):
                for j in range(cols):
                    stage[slot, i * cols + j] = res[i * side:(i + 1) * side, j * side:(j + 1) * side]
            for i in range(per):
                for j in range(cols):
                    dst = slot_ref[first + i * stride + t * cols + j]
                    pltpu.make_async_copy(stage.at[slot, i * cols + j], out.at[dst], sem_out.at[slot]).start()

        steps = b.shape[1] // tile
        pl.loop(0, steps)(step)
        count += steps
    out_wait(0)
    out_wait(1)


def run_wgrad(slot_of, h1, att, h2, g, dqkv, da, dz, dy, side):
    rows, width = h1.shape
    tile = 512
    blocks = slot_of.shape[0]
    return pl.pallas_call(
        functools.partial(wgrad_kernel, side=side, tile=tile),
        out_shape=sds((blocks, side, side), BF16),
        in_specs=[smem()] + [hbm()] * 8,
        out_specs=hbm(),
        scratch_shapes=[
            pltpu.VMEM((2, rows, width), BF16),
            pltpu.VMEM((2, rows, FF), BF16),
            pltpu.VMEM((width, rows), BF16),
            pltpu.VMEM((2, (width // side) * (tile // side), side, side), BF16),
            pltpu.SemaphoreType.DMA((2, 2)),
            pltpu.SemaphoreType.DMA((2,)),
        ],
        compiler_params=params(),
        name="wgrad",
    )(slot_of, h1, att, h2, g, dqkv, da, dz, dy)


def local(
    inputs,
    cotangent,
    weight_slots,
    slot_block,
    left_stats,
    right_stats,
    left_roots,
    right_roots,
    vectors,
    span_start,
):
    seq_count, tok_count, width = inputs.shape
    rows = seq_count * tok_count
    nd = lax.axis_size("dev")
    ng = lax.axis_size("grp")
    side = weight_slots.shape[1]
    hpd = H // nd
    lanes = width // nd
    head = lax.axis_index("dev") * hpd + jnp.arange(hpd, dtype=jnp.int32)
    slopes = jnp.exp2(-8.0 * (head.astype(F32) + 1.0) / H)
    slot_of = invert_order(slot_block)
    vec = vectors.reshape(-1, width)
    x = inputs.reshape(rows, width)
    dy = cotangent.reshape(rows, width)

    gath = lax.all_gather(weight_slots.astype(BF16), ("grp", "dev"), axis=0, tiled=True)
    h1, qkv = run_qkv(slot_of, x, vec, gath, nd)
    qkv = lax.all_to_all(qkv, "dev", 0, 0, tiled=True)
    qkv = qkv.reshape(nd, 3, seq_count, tok_count, lanes)
    o, ot, lse = run_attn_fwd(span_start, slopes, qkv, hpd)
    o = lax.all_to_all(o, "dev", 0, 0, tiled=True).reshape(nd, rows, lanes)
    act, att, h2, g, dz, da, dx1, do, sums2 = run_mlp(slot_of, o, x, dy, vec, gath, nd)
    do = lax.all_to_all(do, "dev", 0, 0, tiled=True)
    do = do.reshape(nd, seq_count, tok_count, lanes)
    dqkv = run_attn_bwd(span_start, slopes, qkv, do, ot, lse, hpd)
    dqkv = lax.all_to_all(dqkv, "dev", 0, 0, tiled=True).reshape(nd, 3, rows, lanes)
    ig, cat, sums1 = run_dh1(slot_of, dqkv, x, dx1, vec, gath, nd)
    grads = run_wgrad(slot_of, h1, att, h2, g, cat, da, dz, dy, side)

    s2 = jnp.sum(sums2.reshape(-1, 8, width), axis=1)
    s1 = jnp.sum(sums1.reshape(-1, 8, width), axis=1)
    bo, gain2, shift2, bdown = [s2[n:n + 1] for n in range(4)]
    gain1, shift1, bq, bv = [s1[n:n + 1] for n in range(4)]
    local_vector = jnp.concatenate(
        [gain1, shift1, bq, bv, bo, gain2, shift2, bdown, s2[4:]], axis=0
    ).reshape(-1)
    vector_grads = lax.psum(local_vector, ("grp", "dev"))
    tokens_all = rows * nd * ng
    new_vectors = vectors - vector_rate / math.sqrt(tokens_all) * vector_grads

    weight_grads = lax.psum_scatter(grads, ("grp", "dev"), scatter_dimension=0, tiled=True)
    weight_grads = weight_grads.astype(F32)
    new_left = 0.5 * left_stats + 0.5 * jnp.einsum(
        "bij,bkj->bik", weight_grads, weight_grads, precision=highest
    )
    new_right = 0.5 * right_stats + 0.5 * jnp.einsum(
        "bji,bjk->bik", weight_grads, weight_grads, precision=highest
    )
    shaped = jnp.einsum("bij,bjk->bik", left_roots, weight_grads, precision=highest)
    shaped = jnp.einsum("bij,bjk->bik", shaped, right_roots, precision=highest)
    new_weights = weight_slots - weight_rate * shaped
    return (
        act.reshape(inputs.shape),
        ig.reshape(inputs.shape),
        weight_grads,
        new_left,
        new_right,
        new_weights,
        vector_grads,
        new_vectors,
    )


def solution(mesh):
    return jax.shard_map(
        local,
        mesh=mesh,
        in_specs=(
            P("grp", "dev", None),
            P("grp", "dev", None),
            P(("grp", "dev"), None, None),
            P(),
            P(("grp", "dev"), None, None),
            P(("grp", "dev"), None, None),
            P(("grp", "dev"), None, None),
            P(("grp", "dev"), None, None),
            P(),
            P("grp"),
        ),
        out_specs=(
            P("grp", "dev", None),
            P("grp", "dev", None),
            P(("grp", "dev"), None, None),
            P(("grp", "dev"), None, None),
            P(("grp", "dev"), None, None),
            P(("grp", "dev"), None, None),
            P(),
            P(),
        ),
        check_vma=False,
    )
```

```python
import functools
import math

import jax
import jax.numpy as jnp
from jax import lax
from jax.experimental import pallas as pl
from jax.experimental.pallas import tpu as pltpu
from jax.sharding import PartitionSpec as P

H = 16
FF = 4096
PIC = 256

eps = 1e-05
weight_rate = 0.5
vector_rate = 0.5
big_negative = -1e30
highest = lax.Precision.HIGHEST
F32 = jnp.float32
BF16 = jnp.bfloat16
LOG2E = 1.4426950408889634
MIB = 1024 * 1024

GAIN1, SHIFT1, BQ, BV, BO, GAIN2, SHIFT2, BDOWN, BUP = range(9)


def dot_nn(a, b):
    return lax.dot_general(a, b, (((1,), (0,)), ((), ())), preferred_element_type=F32)


def dot_nt(a, b):
    return lax.dot_general(a, b, (((1,), (1,)), ((), ())), preferred_element_type=F32)


def invert_order(slot_block):
    places = jnp.arange(slot_block.shape[0], dtype=jnp.int32)
    matches = (slot_block[None, :] == places[:, None]).astype(jnp.int32)
    return jnp.sum(matches * places[None, :], axis=1)


def vmem():
    return pl.BlockSpec(memory_space=pltpu.VMEM)


def smem():
    return pl.BlockSpec(memory_space=pltpu.SMEM)


def hbm():
    return pl.BlockSpec(memory_space=pl.ANY)


def sds(shape, dtype):
    return jax.ShapeDtypeStruct(shape, dtype)


def params(mib=58, **kw):
    return pltpu.CompilerParams(vmem_limit_bytes=mib * MIB, **kw)


def layer_stats(v):
    middle = jnp.mean(v, axis=-1, keepdims=True)
    centred = v - middle
    spread = jnp.mean(centred * centred, axis=-1, keepdims=True)
    return centred, lax.rsqrt(spread + eps)


def fold_rows(v):
    return jnp.sum(v.reshape(v.shape[0] // 8, 8, v.shape[1]), axis=0)


def fetch_block(gath, slot, dst, row, col, sem, side):
    return pltpu.make_async_copy(
        gath.at[slot], dst.at[pl.ds(row, side), pl.ds(col, side)], sem
    )


def qkv_kernel(slot_ref, x_ref, vec_ref, gath, h1_ref, out_ref, wbuf, sems, *, nd):
    rows, width = x_ref.shape
    side = gath.shape[1]
    per = width // side
    lanes = out_ref.shape[3]
    for part in range(3):
        @pl.loop(0, per)
        def _(i):
            for j in range(per):
                slot = slot_ref[i * 3 * per + part * per + j]
                fetch_block(gath, slot, wbuf.at[part], pl.multiple_of(i * side, side), j * side, sems.at[part], side).start()

    chunk = 32
    gain = vec_ref[GAIN1:GAIN1 + 1, :]
    shift = vec_ref[SHIFT1:SHIFT1 + 1, :]

    @pl.loop(0, rows // chunk)
    def _(r):
        at = pl.ds(pl.multiple_of(r * chunk, chunk), chunk)
        centred, inv = layer_stats(x_ref[at, :].astype(F32))
        h1_ref[at, :] = (centred * inv * gain + shift).astype(BF16)

    for part in range(3):
        pltpu.make_async_copy(wbuf.at[part], wbuf.at[part], sems.at[part]).wait()
        for half in range(2):
            cols = slice(half * width // 2, (half + 1) * width // 2)
            res = dot_nn(h1_ref[...], wbuf[part, :, cols])
            if part == 0:
                res = res + vec_ref[BQ:BQ + 1, cols]
            if part == 2:
                res = res + vec_ref[BV:BV + 1, cols]
            res = res.astype(BF16)
            for d in range(nd // 2):
                out_ref[half * (nd // 2) + d, part, :, :] = res[:, d * lanes:(d + 1) * lanes]


def run_qkv(slot_of, x, vec, gath, nd):
    rows, width = x.shape
    lanes = width // nd
    return pl.pallas_call(
        functools.partial(qkv_kernel, nd=nd),
        out_shape=(sds((rows, width), BF16), sds((nd, 3, rows, lanes), BF16)),
        in_specs=[smem(), vmem(), vmem(), hbm()],
        out_specs=(vmem(), vmem()),
        scratch_shapes=[pltpu.VMEM((3, width, width), BF16), pltpu.SemaphoreType.DMA((3,))],
        compiler_params=params(),
        name="qkv",
    )(slot_of, x, vec, gath)


def bias_tables(slope_ref, below, diag, hpd, tok):
    u = lax.broadcasted_iota(jnp.int32, (tok, tok), 0)
    t = lax.broadcasted_iota(jnp.int32, (tok, tok), 1)
    ub = lax.broadcasted_iota(jnp.int32, (tok, 128), 0).astype(F32)
    near = jnp.minimum(u, 2 * t - u).astype(F32)
    for h in range(hpd):
        slope = slope_ref[h] * LOG2E
        below[h] = slope * ub
        full = slope * near
        diag[h, 1] = full
        diag[h, 0] = jnp.where(u <= t, full, big_negative)


def widen(b, tok):
    return jnp.concatenate([b] * (tok // 128), axis=1)


def head_mask(h, lanes, hpd, tok):
    lane = lax.broadcasted_iota(jnp.int32, (tok, lanes), 1)
    size = lanes // hpd
    return (lane >= h * size) & (lane < (h + 1) * size)


def attn_fwd_kernel(span_ref, slope_ref, qkv_ref, o_ref, ot_ref, lse_ref, vt, below, diag, *, hpd):
    nb, _, _, tok, lanes = qkv_ref.shape
    size = lanes // hpd
    scale = size ** (-0.5) * LOG2E
    seq = pl.program_id(0)
    start = span_ref[seq]
    bias_tables(slope_ref, below, diag, hpd, tok)

    @pl.loop(0, nb)
    def _(j):
        vt[:, pl.ds(pl.multiple_of(j * tok, tok), tok)] = qkv_ref[j, 2, 0].astype(F32).T.astype(BF16)

    @pl.loop(0, nb)
    def _(i):
        at_i = pl.ds(pl.multiple_of(i * tok, tok), tok)
        q = qkv_ref[i, 0, 0]
        k = qkv_ref[i, 1, 0]
        flag = (start == i * tok).astype(jnp.int32)
        qs = []
        state = []
        for h in range(hpd):
            qh = jnp.where(head_mask(h, lanes, hpd, tok), q, 0).astype(BF16) if hpd > 1 else q
            qs.append(qh)
            s = dot_nt(k, qh) * scale + diag[h, flag]
            m = jnp.max(s, axis=0, keepdims=True)
            p = jnp.exp2(s - m)
            total = jnp.sum(p, axis=0, keepdims=True)
            acc = dot_nn(vt[h * size:(h + 1) * size, at_i], p.astype(BF16))
            state.append((m, total, acc))

        def body(j, state):
            at_j = pl.ds(pl.multiple_of(j * tok, tok), tok)
            kj = qkv_ref[j, 1, 0]
            new = []
            for h in range(hpd):
                m, total, acc = state[h]
                shift = (slope_ref[h] * LOG2E) * ((j - i) * tok).astype(F32)
                s = dot_nt(kj, qs[h]) * scale + widen(below[h], tok)
                top = jnp.maximum(m, jnp.max(s, axis=0, keepdims=True) + shift)
                p = jnp.exp2(s - (top - shift))
                decay = jnp.exp2(m - top)
                total = total * decay + jnp.sum(p, axis=0, keepdims=True)
                acc = acc * decay + dot_nn(vt[h * size:(h + 1) * size, at_j], p.astype(BF16))
                new.append((top, total, acc))
            return tuple(new)

        state = lax.fori_loop(0, i, body, tuple(state))
        outs = []
        for h in range(hpd):
            m, total, acc = state[h]
            out = acc / total
            ot_ref[0, h * size:(h + 1) * size, at_i] = out
            lse_ref[0, h:h + 1, at_i] = m + jnp.log2(total)
            outs.append(out)
        out = jnp.concatenate(outs, axis=0) if hpd > 1 else outs[0]
        o_ref[i, 0] = out.T.astype(BF16)


def run_attn_fwd(span, slopes, qkv, hpd):
    nb, _, seqs, tok, lanes = qkv.shape
    t = nb * tok
    return pl.pallas_call(
        functools.partial(attn_fwd_kernel, hpd=hpd),
        grid=(seqs,),
        out_shape=(
            sds((nb, seqs, tok, lanes), BF16),
            sds((seqs, lanes, t), F32),
            sds((seqs, hpd, t), F32),
        ),
        in_specs=[
            smem(),
            smem(),
            pl.BlockSpec((nb, 3, 1, tok, lanes), lambda s: (0, 0, s, 0, 0)),
        ],
        out_specs=(
            pl.BlockSpec((nb, 1, tok, lanes), lambda s: (0, s, 0, 0)),
            pl.BlockSpec((1, lanes, t), lambda s: (s, 0, 0)),
            pl.BlockSpec((1, hpd, t), lambda s: (s, 0, 0)),
        ),
        scratch_shapes=[
            pltpu.VMEM((lanes, t), BF16),
            pltpu.VMEM((hpd, tok, 128), F32),
            pltpu.VMEM((hpd, 2, tok, tok), F32),
        ],
        compiler_params=params(),
        name="attn_fwd",
    )(span, slopes, qkv)


def attn_bwd_kernel(
    span_ref, slope_ref, qkv_ref, do_ref, ot_ref, lse_ref, out_ref,
    kt, qm, dom, delta, dqt, below, diag, *, hpd
):
    nb, _, _, tok, lanes = qkv_ref.shape
    size = lanes // hpd
    unit = size ** (-0.5)
    scale = unit * LOG2E
    seq = pl.program_id(0)
    start = span_ref[seq]
    bias_tables(slope_ref, below, diag, hpd, tok)

    @pl.loop(0, nb)
    def _(j):
        at_j = pl.ds(pl.multiple_of(j * tok, tok), tok)
        kt[:, at_j] = qkv_ref[j, 1, 0].astype(F32).T.astype(BF16)
        q = qkv_ref[j, 0, 0]
        do = do_ref[j, 0]
        for h in range(hpd):
            if hpd > 1:
                mask = head_mask(h, lanes, hpd, tok)
                qm[h, j] = jnp.where(mask, q, 0).astype(BF16)
                dom[h, j] = jnp.where(mask, do, 0).astype(BF16)
            else:
                qm[h, j] = q
                dom[h, j] = do
        prod = do.astype(F32).T * ot_ref[0, :, at_j]
        for h in range(hpd):
            delta[h:h + 1, at_j] = jnp.sum(prod[h * size:(h + 1) * size], axis=0, keepdims=True)
        dqt[:, at_j] = jnp.zeros((lanes, tok), F32)

    @pl.loop(0, nb)
    def _(j):
        at_j = pl.ds(pl.multiple_of(j * tok, tok), tok)
        k = qkv_ref[j, 1, 0]
        v = qkv_ref[j, 2, 0]
        flag = (start == j * tok).astype(jnp.int32)

        def tile(i, h, dk, dv, bias, low):
            at_i = pl.ds(pl.multiple_of(i * tok, tok), tok)
            qh = qm[h, i]
            doh = dom[h, i]
            s = dot_nt(k, qh) * scale + bias
            p = jnp.exp2(s - low)
            dp = dot_nt(v, doh)
            ds = (p * (dp - delta[h:h + 1, at_i])).astype(BF16)
            dv = dv + dot_nn(p.astype(BF16), doh)
            dk = dk + dot_nn(ds, qh)
            rows = slice(h * size, (h + 1) * size)
            dqt[rows, at_i] += dot_nn(kt[rows, at_j], ds)
            return dk, dv

        dk = jnp.zeros((tok, lanes), F32)
        dv = jnp.zeros((tok, lanes), F32)
        for h in range(hpd):
            dk, dv = tile(j, h, dk, dv, diag[h, flag], lse_ref[0, h:h + 1, at_j])

        def body(i, carry):
            dk, dv = carry
            at_i = pl.ds(pl.multiple_of(i * tok, tok), tok)
            for h in range(hpd):
                shift = (slope_ref[h] * LOG2E) * ((j - i) * tok).astype(F32)
                dk, dv = tile(i, h, dk, dv, widen(below[h], tok), lse_ref[0, h:h + 1, at_i] - shift)
            return dk, dv

        dk, dv = lax.fori_loop(j + 1, nb, body, (dk, dv))
        out_ref[j, 1, 0] = (dk * unit).astype(BF16)
        out_ref[j, 2, 0] = dv.astype(BF16)

    @pl.loop(0, nb)
    def _(j):
        at_j = pl.ds(pl.multiple_of(j * tok, tok), tok)
        out_ref[j, 0, 0] = (dqt[:, at_j].T * unit).astype(BF16)


def run_attn_bwd(span, slopes, qkv, do, ot, lse, hpd):
    nb, _, seqs, tok, lanes = qkv.shape
    t = nb * tok
    return pl.pallas_call(
        functools.partial(attn_bwd_kernel, hpd=hpd),
        grid=(seqs,),
        out_shape=sds(qkv.shape, BF16),
        in_specs=[
            smem(),
            smem(),
            pl.BlockSpec((nb, 3, 1, tok, lanes), lambda s: (0, 0, s, 0, 0)),
            pl.BlockSpec((nb, 1, tok, lanes), lambda s: (0, s, 0, 0)),
            pl.BlockSpec((1, lanes, t), lambda s: (s, 0, 0)),
            pl.BlockSpec((1, hpd, t), lambda s: (s, 0, 0)),
        ],
        out_specs=pl.BlockSpec((nb, 3, 1, tok, lanes), lambda s: (0, 0, s, 0, 0)),
        scratch_shapes=[
            pltpu.VMEM((lanes, t), BF16),
            pltpu.VMEM((hpd, nb, tok, lanes), BF16),
            pltpu.VMEM((hpd, nb, tok, lanes), BF16),
            pltpu.VMEM((max(hpd, 8), t), F32),
            pltpu.VMEM((lanes, t), F32),
            pltpu.VMEM((hpd, tok, 128), F32),
            pltpu.VMEM((hpd, 2, tok, tok), F32),
        ],
        compiler_params=params(),
        name="attn_bwd",
    )(span, slopes, qkv, do, ot, lse)


def mlp_kernel(
    slot_ref, o_ref, x_ref, dy_ref, vec_ref, gath,
    act_ref, att_ref, h2_ref, g_ref, dz_ref, da_ref, dx1_ref, do_ref, sums_ref,
    wo, wup, wdn, x1, acc, dh2, sem_o, sem_t, *, nd, first_o, first_up, first_dn, tile
):
    rows, width = x_ref.shape
    side = gath.shape[1]
    per = width // side
    ff = g_ref.shape[1]
    tiles = ff // tile
    cols = tile // side
    lanes = o_ref.shape[2]
    fper = ff // side

    @pl.loop(0, per)
    def _(i):
        for j in range(per):
            fetch_block(gath, slot_ref[first_o + i * per + j], wo, pl.multiple_of(i * side, side), j * side, sem_o.at[0], side).start()

    def fetch_tile(f):
        @pl.loop(0, per)
        def _(i):
            for j in range(cols):
                fetch_block(gath, slot_ref[first_up + i * fper + f * cols + j], wup.at[f], pl.multiple_of(i * side, side), j * side, sem_t.at[f], side).start()
            for j in range(cols):
                fetch_block(gath, slot_ref[first_dn + (f * cols + j) * per + i], wdn.at[f], j * side, pl.multiple_of(i * side, side), sem_t.at[f], side).start()

    fetch_tile(0)
    fetch_tile(1)
    for d in range(nd):
        att_ref[:, d * lanes:(d + 1) * lanes] = o_ref[d]
    pltpu.make_async_copy(wo, wo, sem_o.at[0]).wait()
    for half in range(2):
        c = slice(half * width // 2, (half + 1) * width // 2)
        x1[:, c] = x_ref[:, c].astype(F32) + dot_nn(att_ref[...], wo[:, c]) + vec_ref[BO:BO + 1, c]

    chunk = 32

    def rows_at(r):
        return pl.ds(pl.multiple_of(r * chunk, chunk), chunk)

    @pl.loop(0, rows // chunk)
    def _(r):
        at = rows_at(r)
        centred, inv = layer_stats(x1[at, :])
        h2_ref[at, :] = (centred * inv * vec_ref[GAIN2:GAIN2 + 1, :] + vec_ref[SHIFT2:SHIFT2 + 1, :]).astype(BF16)
        acc[at, :] = x1[at, :] + vec_ref[BDOWN:BDOWN + 1, :]
        dh2[at, :] = jnp.zeros((chunk, width), F32)

    @pl.loop(0, tiles)
    def _(f):
        @pl.when(f + 2 < tiles)
        def _():
            fetch_tile(f + 2)
        pltpu.make_async_copy(wup.at[f], wup.at[f], sem_t.at[f]).wait()
        pltpu.make_async_copy(wdn.at[f], wdn.at[f], sem_t.at[f]).wait()
        per_row = width // tile
        bias = vec_ref[pl.ds(BUP + f // per_row, 1), pl.ds(pl.multiple_of((f % per_row) * tile, tile), tile)]
        at_f = pl.ds(pl.multiple_of(f * tile, tile), tile)
        z = dot_nn(h2_ref[...], wup[f]) + bias
        dg = dot_nt(dy_ref[...], wdn[f])
        z2 = z * z
        th = jnp.tanh(0.7978845608028654 * (z + 0.044715 * z2 * z))
        g = (0.5 * z * (1.0 + th)).astype(BF16)
        slope = 0.5 * (1.0 + th) + 0.5 * z * (1.0 - th * th) * (
            0.7978845608028654 * (1.0 + 3.0 * 0.044715 * z2)
        )
        dz = (dg * slope).astype(BF16)
        g_ref[:, at_f] = g
        dz_ref[:, at_f] = dz
        sums_ref[pl.ds(pl.multiple_of(8 * (4 + f // per_row), 8), 8), pl.ds(pl.multiple_of((f % per_row) * tile, tile), tile)] = fold_rows(dz.astype(F32))
        acc[...] += dot_nn(g, wdn[f])
        dh2[...] += dot_nt(dz, wup[f])

    zero = jnp.zeros((8, width), F32)

    def finish(r, carry):
        s_bo, s_gain, s_shift, s_bdown = carry
        at = rows_at(r)
        act_ref[at, :] = acc[at, :].astype(BF16)
        centred, inv = layer_stats(x1[at, :])
        hat = centred * inv
        dh = dh2[at, :]
        dhg = dh * vec_ref[GAIN2:GAIN2 + 1, :]
        back = inv * (
            dhg
            - jnp.mean(dhg, axis=-1, keepdims=True)
            - hat * jnp.mean(dhg * hat, axis=-1, keepdims=True)
        )
        dy = dy_ref[at, :].astype(F32)
        dx1 = dy + back
        dx1_ref[at, :] = dx1
        da = dx1.astype(BF16)
        da_ref[at, :] = da
        return (
            s_bo + fold_rows(da.astype(F32)),
            s_gain + fold_rows(dh * hat),
            s_shift + fold_rows(dh),
            s_bdown + fold_rows(dy),
        )

    carry = lax.fori_loop(0, rows // chunk, finish, (zero, zero, zero, zero))
    for n in range(4):
        sums_ref[8 * n:8 * n + 8, :] = carry[n]
    for half in range(2):
        c = slice(half * width // 2, (half + 1) * width // 2)
        res = dot_nt(da_ref[...], wo[c, :]).astype(BF16)
        for d in range(nd // 2):
            do_ref[half * (nd // 2) + d] = res[:, d * lanes:(d + 1) * lanes]


def run_mlp(slot_of, o, x, dy, vec, gath, nd):
    rows, width = x.shape
    side = gath.shape[1]
    lanes = width // nd
    per = width // side
    first_o = 3 * per * per
    first_up = first_o + per * per
    first_dn = first_up + per * (FF // side)
    tile = 512
    return pl.pallas_call(
        functools.partial(
            mlp_kernel, nd=nd, first_o=first_o, first_up=first_up, first_dn=first_dn, tile=tile
        ),
        out_shape=(
            sds((rows, width), BF16),
            sds((rows, width), BF16),
            sds((rows, width), BF16),
            sds((rows, FF), BF16),
            sds((rows, FF), BF16),
            sds((rows, width), BF16),
            sds((rows, width), F32),
            sds((nd, rows, lanes), BF16),
            sds((8 * (4 + FF // width), width), F32),
        ),
        in_specs=[smem(), vmem(), vmem(), vmem(), vmem(), hbm()],
        out_specs=tuple([vmem()] * 9),
        scratch_shapes=[
            pltpu.VMEM((width, width), BF16),
            pltpu.VMEM((FF // tile, width, tile), BF16),
            pltpu.VMEM((FF // tile, tile, width), BF16),
            pltpu.VMEM((rows, width), F32),
            pltpu.VMEM((rows, width), F32),
            pltpu.VMEM((rows, width), F32),
            pltpu.SemaphoreType.DMA((1,)),
            pltpu.SemaphoreType.DMA((FF // tile,)),
        ],
        compiler_params=params(),
        name="mlp",
    )(slot_of, o, x, dy, vec, gath)


def dh1_kernel(
    slot_ref, dqkv_ref, x_ref, dx1_ref, vec_ref, gath, ig_ref, cat_ref, sums_ref,
    wbuf, dh1, sems, *, nd
):
    rows, width = x_ref.shape
    side = gath.shape[1]
    per = width // side
    lanes = dqkv_ref.shape[3]
    for part in range(3):
        @pl.loop(0, per)
        def _(i):
            for j in range(per):
                slot = slot_ref[i * 3 * per + part * per + j]
                fetch_block(gath, slot, wbuf.at[part], pl.multiple_of(i * side, side), j * side, sems.at[part], side).start()

    for part in range(3):
        for d in range(nd):
            at = part * width + d * lanes
            cat_ref[:, at:at + lanes] = dqkv_ref[d, part]
    for part in range(3):
        pltpu.make_async_copy(wbuf.at[part], wbuf.at[part], sems.at[part]).wait()
        for half in range(2):
            c = slice(half * width // 2, (half + 1) * width // 2)
            res = dot_nt(cat_ref[:, part * width:(part + 1) * width], wbuf[part, c, :])
            if part == 0:
                dh1[:, c] = res
            else:
                dh1[:, c] += res

    chunk = 32
    zero = jnp.zeros((8, width), F32)

    def finish(r, carry):
        s_gain, s_shift, s_bq, s_bv = carry
        at = pl.ds(pl.multiple_of(r * chunk, chunk), chunk)
        centred, inv = layer_stats(x_ref[at, :].astype(F32))
        hat = centred * inv
        dh = dh1[at, :]
        dhg = dh * vec_ref[GAIN1:GAIN1 + 1, :]
        back = inv * (
            dhg
            - jnp.mean(dhg, axis=-1, keepdims=True)
            - hat * jnp.mean(dhg * hat, axis=-1, keepdims=True)
        )
        ig_ref[at, :] = dx1_ref[at, :] + back
        return (
            s_gain + fold_rows(dh * hat),
            s_shift + fold_rows(dh),
            s_bq + fold_rows(cat_ref[at, 0:width].astype(F32)),
            s_bv + fold_rows(cat_ref[at, 2 * width:3 * width].astype(F32)),
        )

    carry = lax.fori_loop(0, rows // chunk, finish, (zero, zero, zero, zero))
    for n in range(4):
        sums_ref[8 * n:8 * n + 8, :] = carry[n]


def run_dh1(slot_of, dqkv, x, dx1, vec, gath, nd):
    rows, width = x.shape
    return pl.pallas_call(
        functools.partial(dh1_kernel, nd=nd),
        out_shape=(
            sds((rows, width), F32),
            sds((rows, 3 * width), BF16),
            sds((32, width), F32),
        ),
        in_specs=[smem(), vmem(), vmem(), vmem(), vmem(), hbm()],
        out_specs=(vmem(), vmem(), vmem()),
        scratch_shapes=[
            pltpu.VMEM((3, width, width), BF16),
            pltpu.VMEM((rows, width), F32),
            pltpu.SemaphoreType.DMA((3,)),
        ],
        compiler_params=params(),
        name="dh1",
    )(slot_of, dqkv, x, dx1, vec, gath)


def wgrad_kernel(
    slot_ref, h1, att, h2, g, dqkv, da, dz, dy, out,
    v_a, v_b, a_t, stage, sem_in, sem_out, *, side, tile
):
    rows, width = h1.shape
    per = width // side
    cols = tile // side
    ff = g.shape[1]
    runs = [(h2, 0, dz, 4 * per * per, ff // side)]
    for c in range(ff // width):
        first = 4 * per * per + per * (ff // side) + c * per * per
        runs.append((g, c * width, dy, first, per))
    runs.append((att, 0, da, 3 * per * per, per))
    runs.append((h1, 0, dqkv, 0, 3 * per))

    def loads(n):
        a, at, b, _, _ = runs[n]
        copies = [pltpu.make_async_copy(a.at[:, pl.ds(at, width)], v_a.at[n % 2], sem_in.at[n % 2, 0])]
        fresh = n == 0 or runs[n - 1][2] is not b
        if fresh:
            wide = b.shape[1]
            copies.append(
                pltpu.make_async_copy(b, v_b.at[slot_b[n], :, pl.ds(0, wide)], sem_in.at[n % 2, 1])
            )
        return copies

    slot_b = []
    for n in range(len(runs)):
        if n == 0:
            slot_b.append(0)
        elif runs[n - 1][2] is runs[n][2]:
            slot_b.append(slot_b[-1])
        else:
            slot_b.append(1 - slot_b[-1])

    started = {0: loads(0)}
    for copy in started[0]:
        copy.start()
    count = 0

    def out_wait(slot):
        pltpu.make_async_copy(stage.at[slot], stage.at[slot], sem_out.at[slot]).wait()

    for n in range(len(runs)):
        _, _, b, first, stride = runs[n]
        if n + 1 < len(runs):
            started[n + 1] = loads(n + 1)
            for copy in started[n + 1]:
                copy.start()
        for copy in started[n]:
            copy.wait()
        for r in range(width // 256):
            c = slice(r * 256, (r + 1) * 256)
            a_t[c, :] = v_a[n % 2, :, c].astype(F32).T.astype(BF16)
        sb = slot_b[n]
        base = count

        def step(t, base=base, first=first, stride=stride, sb=sb):
            slot = (base + t) % 2

            @pl.when(base + t >= 2)
            def _():
                out_wait(slot)
            res = dot_nn(a_t[...], v_b[sb, :, pl.ds(pl.multiple_of(t * tile, tile), tile)]).astype(BF16)
            for i in range(per):
                for j in range(cols):
                    stage[slot, i * cols + j] = res[i * side:(i + 1) * side, j * side:(j + 1) * side]
            for i in range(per):
                for j in range(cols):
                    dst = slot_ref[first + i * stride + t * cols + j]
                    pltpu.make_async_copy(stage.at[slot, i * cols + j], out.at[dst], sem_out.at[slot]).start()

        steps = b.shape[1] // tile
        pl.loop(0, steps)(step)
        count += steps
    out_wait(0)
    out_wait(1)


def run_wgrad(slot_of, h1, att, h2, g, dqkv, da, dz, dy, side):
    rows, width = h1.shape
    tile = 512
    blocks = slot_of.shape[0]
    return pl.pallas_call(
        functools.partial(wgrad_kernel, side=side, tile=tile),
        out_shape=sds((blocks, side, side), BF16),
        in_specs=[smem()] + [hbm()] * 8,
        out_specs=hbm(),
        scratch_shapes=[
            pltpu.VMEM((2, rows, width), BF16),
            pltpu.VMEM((2, rows, FF), BF16),
            pltpu.VMEM((width, rows), BF16),
            pltpu.VMEM((2, (width // side) * (tile // side), side, side), BF16),
            pltpu.SemaphoreType.DMA((2, 2)),
            pltpu.SemaphoreType.DMA((2,)),
        ],
        compiler_params=params(),
        name="wgrad",
    )(slot_of, h1, att, h2, g, dqkv, da, dz, dy)


MESH = pl.DeviceIdType.MESH


def whereami():
    g = lax.axis_index("grp")
    d = lax.axis_index("dev")
    core = lax.rem(d, 2)
    x = lax.rem(d // 2, 2)
    y = d // 4
    over_x = d + 2 - 4 * x
    over_y = d + 4 - 8 * y
    across = over_x + 4 - 8 * y
    sibling = d + 1 - 2 * core
    return g, d, over_x, over_y, across, sibling


def near_order(t, g, ng):
    t = ng - 1 - t
    low = jnp.where(t < ng - 1 - g, ng - 1 - t, t - (ng - 1 - g))
    high = jnp.where(t < g, t, ng - 1 - (t - g))
    return jnp.where(2 * g < ng, low, high)


def greet(g, ng, peers):
    barrier = pltpu.get_barrier_semaphore()
    for peer in peers:
        pl.semaphore_signal(barrier, inc=1, device_id=(g, peer), device_id_type=MESH)

    d = lax.axis_index("dev")

    @pl.when(g > 0)
    def _():
        pl.semaphore_signal(barrier, inc=1, device_id=(g - 1, d), device_id_type=MESH)

    @pl.when(g < ng - 1)
    def _():
        pl.semaphore_signal(barrier, inc=1, device_id=(g + 1, d), device_id_type=MESH)

    ends = (g > 0).astype(jnp.int32) + (g < ng - 1).astype(jnp.int32)
    pl.semaphore_wait(barrier, len(peers) + ends)


def remote(src, dst, send, recv, device):
    return pltpu.make_async_remote_copy(
        src_ref=src, dst_ref=dst, send_sem=send, recv_sem=recv, device_id=device, device_id_type=MESH
    )


def arrived(ref, sem):
    pltpu.make_async_copy(ref, ref, sem).wait()


def gather_kernel(w_ref, out, own, local_sem, zs, zr, ss, sr, *, ng, nd):
    count = w_ref.shape[0]
    half = count // 2
    g, d, over_x, over_y, across, sibling = whereami()
    own[...] = w_ref[...].astype(BF16)
    greet(g, ng, (over_x, over_y, sibling))

    def region(gz, dev, first=0, size=count):
        return out.at[pl.ds((gz * nd + dev) * count + first, size)]

    kinds = (
        (d, 0, count, over_x),
        (d, 0, count, over_y),
        (d, 0, count, sibling),
        (over_x, 0, half, over_y),
        (over_y, half, count - half, over_x),
        (over_x, 0, count, sibling),
        (over_y, 0, count, sibling),
        (across, 0, half, sibling),
        (across, half, count - half, sibling),
    )

    def plane(n, gz, src=None):
        dev, first, size, to = kinds[n]
        at = region(gz, dev, first, size)
        return remote(at if src is None else src, at, ss.at[n, gz], sr.at[n, gz], (g, to))

    def line(gz, up, src=None):
        at = region(gz, d)
        to = g + 1 if up else g - 1
        return remote(at if src is None else src, at, zs.at[gz, int(up)], zr.at[gz], (to, d))

    def landed(n, gz, dev, first, size):
        arrived(region(gz, dev, first, size), sr.at[n, gz])

    mine = pltpu.make_async_copy(own, region(g, d), local_sem.at[0])
    mine.start()

    def column(t):
        gz = near_order(t, g, ng)
        if t == 0:
            @pl.when(g < ng - 1)
            def _():
                line(gz, True, own).start()

            @pl.when(g > 0)
            def _():
                line(gz, False, own).start()
            for n in range(3):
                plane(n, gz, own).start()
            return
        arrived(region(gz, d), zr.at[gz])

        @pl.when((gz < g) & (g < ng - 1))
        def _():
            line(gz, True).start()

        @pl.when((gz > g) & (g > 0))
        def _():
            line(gz, False).start()
        for n in range(3):
            plane(n, gz).start()

    def sides(t):
        gz = near_order(t, g, ng)
        landed(0, gz, over_x, 0, count)
        plane(3, gz).start()
        plane(5, gz).start()
        landed(1, gz, over_y, 0, count)
        plane(4, gz).start()
        plane(6, gz).start()

    def corner(t):
        gz = near_order(t, g, ng)
        landed(3, gz, across, 0, half)
        plane(7, gz).start()
        landed(4, gz, across, half, count - half)
        plane(8, gz).start()

    plan = [(t, f) for t in range(ng) for f in (0, 1, 2)]
    lag = {0: 0, 1: 2.5, 2: 4.5}
    for t, f in sorted(plan, key=lambda e: e[0] * 1.0 + lag[e[1]]):
        (column, sides, corner)[f](t)

    other = sibling
    o_x = sibling + over_x - d
    o_y = sibling + over_y - d
    o_d = sibling + across - d
    for t in range(ng):
        gz = near_order(t, g, ng)
        landed(2, gz, other, 0, count)
        landed(5, gz, o_x, 0, count)
        landed(6, gz, o_y, 0, count)
        landed(7, gz, o_d, 0, half)
        landed(8, gz, o_d, half, count - half)
    mine.wait()
    for t in range(ng):
        gz = near_order(t, g, ng)
        for n in range(9):
            plane(n, gz).wait_send()

        @pl.when((gz <= g) & (g < ng - 1))
        def _():
            line(gz, True).wait_send()

        @pl.when((gz >= g) & (g > 0))
        def _():
            line(gz, False).wait_send()


def run_gather(w, ng, nd):
    count, side, _ = w.shape
    return pl.pallas_call(
        functools.partial(gather_kernel, ng=ng, nd=nd),
        out_shape=sds((ng * nd * count, side, side), BF16),
        in_specs=[vmem()],
        out_specs=hbm(),
        scratch_shapes=[
            pltpu.VMEM((count, side, side), BF16),
            pltpu.SemaphoreType.DMA((1,)),
            pltpu.SemaphoreType.DMA((ng, 2)),
            pltpu.SemaphoreType.DMA((ng,)),
            pltpu.SemaphoreType.DMA((9, ng)),
            pltpu.SemaphoreType.DMA((9, ng)),
        ],
        compiler_params=params(collective_id=0, has_side_effects=True),
        name="gather",
    )(w)


def scatter_kernel(
    grads, vec_ref, out_ref, vout_ref,
    mine, r0, r1y, r1x, r2x, r2y, ru, rd, vwork, vxy, vz,
    load, s0, w0, s1, w1, s2, w2, sz, wz, vs, vw, *, ng, nd
):
    count = out_ref.shape[0]
    half = count // 2
    rest = count - half
    g, d, over_x, over_y, across, sibling = whereami()
    columns = (d, over_x, over_y, across)
    low = slice(0, half)
    high = slice(half, count)

    def region(gz, dev):
        return grads.at[pl.ds((gz * nd + dev) * count, count)]

    def order(t):
        return near_order(ng - 1 - t, g, ng)

    for t in range(ng):
        for c in range(4):
            pltpu.make_async_copy(region(order(t), columns[c]), mine.at[order(t), c], load.at[order(t), c]).start()
    vwork[0] = vec_ref[...]
    greet(g, ng, (over_x, over_y, sibling))

    def to_sibling(gz, c):
        return remote(
            region(gz, columns[c] + sibling - d), r0.at[gz, c], s0.at[gz, c], w0.at[gz, c], (g, sibling)
        )

    peers = (sibling, over_x, over_y)

    def vec_copy(n):
        return remote(vwork.at[n], vxy.at[n], vs.at[n], vw.at[n], (g, peers[n]))

    vec_copy(0).start()
    for t in range(ng):
        for c in range(4):
            to_sibling(order(t), c).start()

    def add(dst, src, size):
        @pl.loop(0, size)
        def _(i):
            dst[i] = (dst[i].astype(F32) + src[i].astype(F32)).astype(BF16)

    def cut(ref, part):
        return ref.at[pl.ds(part.start, part.stop - part.start)]

    first = (
        (2, low, r1y, 0, over_y),
        (3, low, r1y, 1, over_y),
        (1, high, r1x, 0, over_x),
        (3, high, r1x, 1, over_x),
    )
    second = ((1, low, r2x, over_x), (2, high, r2y, over_y))

    def copy1(n, gz):
        c, part, buf, at, to = first[n]
        return remote(cut(mine.at[gz, c], part), buf.at[gz, at], s1.at[n, gz], w1.at[n, gz], (g, to))

    def copy2(n, gz):
        c, part, buf, to = second[n]
        return remote(cut(mine.at[gz, c], part), buf.at[gz], s2.at[n, gz], w2.at[n, gz], (g, to))

    def line(gz, up):
        to = g + 1 if up else g - 1
        buf = ru if up else rd
        return remote(mine.at[gz, 0], buf.at[gz], sz.at[gz], wz.at[gz, int(up)], (to, d))

    def stage0(t):
        gz = order(t)
        for c in (3, 2, 1, 0):
            pltpu.make_async_copy(region(gz, columns[c]), mine.at[gz, c], load.at[gz, c]).wait()
            arrived(r0.at[gz, c], w0.at[gz, c])
            add(mine.at[gz, c], r0.at[gz, c], count)
            if c == 3:
                copy1(1, gz).start()
                copy1(3, gz).start()
            if c == 2:
                copy1(0, gz).start()
            if c == 1:
                copy1(2, gz).start()

    def stage1(t):
        gz = order(t)
        arrived(r1y.at[gz, 1], w1.at[1, gz])
        add(cut(mine.at[gz, 1], low), r1y.at[gz, 1], half)
        copy2(0, gz).start()
        arrived(r1x.at[gz, 1], w1.at[3, gz])
        add(cut(mine.at[gz, 2], high), r1x.at[gz, 1], rest)
        copy2(1, gz).start()
        arrived(r1y.at[gz, 0], w1.at[0, gz])
        add(cut(mine.at[gz, 0], low), r1y.at[gz, 0], half)
        arrived(r1x.at[gz, 0], w1.at[2, gz])
        add(cut(mine.at[gz, 0], high), r1x.at[gz, 0], rest)

    def stage2(t):
        gz = order(t)
        arrived(r2x.at[gz], w2.at[0, gz])
        add(cut(mine.at[gz, 0], low), r2x.at[gz], half)
        arrived(r2y.at[gz], w2.at[1, gz])
        add(cut(mine.at[gz, 0], high), r2y.at[gz], rest)
        if t == ng - 1:
            return

        @pl.when(gz > g)
        def _():
            @pl.when(g > 0)
            def _():
                arrived(ru.at[gz], wz.at[gz, 1])
                add(mine.at[gz, 0], ru.at[gz], count)
            line(gz, True).start()

        @pl.when(gz < g)
        def _():
            @pl.when(g < ng - 1)
            def _():
                arrived(rd.at[gz], wz.at[gz, 0])
                add(mine.at[gz, 0], rd.at[gz], count)
            line(gz, False).start()

    def vec_step(n):
        arrived(vxy.at[n], vw.at[n])
        total = vwork[n] + vxy[n]
        if n < 2:
            vwork[n + 1] = total
            vec_copy(n + 1).start()
        else:
            vz[g] = total

    def vec_line(gz, up):
        to = g + 1 if up else g - 1
        return remote(vz.at[gz], vz.at[gz], vs.at[3 + 2 * gz + int(up)], vw.at[3 + gz], (to, d))

    stage0(0)
    vec_step(0)
    stage0(1)
    vec_step(1)
    stage1(0)
    for t in range(2, ng):
        stage0(t)
        stage1(t - 1)
        stage2(t - 2)
        if t == 2:
            vec_step(2)

            @pl.when(g < ng - 1)
            def _():
                vec_line(g, True).start()

            @pl.when(g > 0)
            def _():
                vec_line(g, False).start()
    stage1(ng - 1)
    for n in range(1, ng):
        gz = near_order(n, g, ng)
        arrived(vz.at[gz], vw.at[3 + gz])

        @pl.when((gz < g) & (g < ng - 1))
        def _():
            vec_line(gz, True).start()

        @pl.when((gz > g) & (g > 0))
        def _():
            vec_line(gz, False).start()
    stage2(ng - 2)
    stage2(ng - 1)

    total = vz[0]
    for z in range(1, ng):
        total = total + vz[z]
    vout_ref[...] = total

    @pl.when(g > 0)
    def _():
        arrived(ru.at[g], wz.at[g, 1])

    @pl.when(g < ng - 1)
    def _():
        arrived(rd.at[g], wz.at[g, 0])

    @pl.loop(0, count)
    def _(i):
        out_ref[i] = mine[g, 0, i].astype(F32)

    @pl.when(g > 0)
    def _():
        @pl.loop(0, count)
        def _(i):
            out_ref[i] += ru[g, i].astype(F32)

    @pl.when(g < ng - 1)
    def _():
        @pl.loop(0, count)
        def _(i):
            out_ref[i] += rd[g, i].astype(F32)

    for t in range(ng):
        gz = order(t)
        for c in range(4):
            to_sibling(gz, c).wait_send()
        for n in range(4):
            copy1(n, gz).wait_send()
        for n in range(2):
            copy2(n, gz).wait_send()
        if t < ng - 1:
            arrived(mine.at[gz, 0], sz.at[gz])
    for n in range(3):
        vec_copy(n).wait_send()
    for n in range(ng):
        gz = near_order(n, g, ng)

        @pl.when((gz <= g) & (g < ng - 1))
        def _():
            vec_line(gz, True).wait_send()

        @pl.when((gz >= g) & (g > 0))
        def _():
            vec_line(gz, False).wait_send()


def run_scatter(grads, vec, ng, nd):
    blocks, side, _ = grads.shape
    count = blocks // (ng * nd)
    half = count // 2
    dma = pltpu.SemaphoreType.DMA

    def buf(*lead):
        return pltpu.VMEM(lead + (side, side), BF16)

    return pl.pallas_call(
        functools.partial(scatter_kernel, ng=ng, nd=nd),
        out_shape=(sds((count, side, side), F32), sds(vec.shape, F32)),
        in_specs=[hbm(), vmem()],
        out_specs=(vmem(), vmem()),
        scratch_shapes=[
            buf(ng, 4, count),
            buf(ng, 4, count),
            buf(ng, 2, half),
            buf(ng, 2, count - half),
            buf(ng, half),
            buf(ng, count - half),
            buf(ng, count),
            buf(ng, count),
            pltpu.VMEM((3,) + vec.shape, F32),
            pltpu.VMEM((3,) + vec.shape, F32),
            pltpu.VMEM((ng,) + vec.shape, F32),
            dma((ng, 4)),
            dma((ng, 4)),
            dma((ng, 4)),
            dma((4, ng)),
            dma((4, ng)),
            dma((2, ng)),
            dma((2, ng)),
            dma((ng,)),
            dma((ng, 2)),
            dma((3 + 2 * ng,)),
            dma((3 + ng,)),
        ],
        compiler_params=params(collective_id=1, has_side_effects=True),
        name="scatter",
    )(grads, vec)


def local(
    inputs,
    cotangent,
    weight_slots,
    slot_block,
    left_stats,
    right_stats,
    left_roots,
    right_roots,
    vectors,
    span_start,
):
    seq_count, tok_count, width = inputs.shape
    rows = seq_count * tok_count
    nd = lax.axis_size("dev")
    ng = lax.axis_size("grp")
    side = weight_slots.shape[1]
    hpd = H // nd
    lanes = width // nd
    head = lax.axis_index("dev") * hpd + jnp.arange(hpd, dtype=jnp.int32)
    slopes = jnp.exp2(-8.0 * (head.astype(F32) + 1.0) / H)
    slot_of = invert_order(slot_block)
    vec = vectors.reshape(-1, width)
    x = inputs.reshape(rows, width)
    dy = cotangent.reshape(rows, width)

    direct = nd == 8
    if direct:
        gath = run_gather(weight_slots, ng, nd)
    else:
        gath = lax.all_gather(weight_slots.astype(BF16), ("grp", "dev"), axis=0, tiled=True)
    h1, qkv = run_qkv(slot_of, x, vec, gath, nd)
    qkv = lax.all_to_all(qkv, "dev", 0, 0, tiled=True)
    qkv = qkv.reshape(nd, 3, seq_count, tok_count, lanes)
    o, ot, lse = run_attn_fwd(span_start, slopes, qkv, hpd)
    o = lax.all_to_all(o, "dev", 0, 0, tiled=True).reshape(nd, rows, lanes)
    act, att, h2, g, dz, da, dx1, do, sums2 = run_mlp(slot_of, o, x, dy, vec, gath, nd)
    do = lax.all_to_all(do, "dev", 0, 0, tiled=True)
    do = do.reshape(nd, seq_count, tok_count, lanes)
    dqkv = run_attn_bwd(span_start, slopes, qkv, do, ot, lse, hpd)
    dqkv = lax.all_to_all(dqkv, "dev", 0, 0, tiled=True).reshape(nd, 3, rows, lanes)
    ig, cat, sums1 = run_dh1(slot_of, dqkv, x, dx1, vec, gath, nd)
    grads = run_wgrad(slot_of, h1, att, h2, g, cat, da, dz, dy, side)

    s2 = jnp.sum(sums2.reshape(-1, 8, width), axis=1)
    s1 = jnp.sum(sums1.reshape(-1, 8, width), axis=1)
    bo, gain2, shift2, bdown = [s2[n:n + 1] for n in range(4)]
    gain1, shift1, bq, bv = [s1[n:n + 1] for n in range(4)]
    local_vector = jnp.concatenate(
        [gain1, shift1, bq, bv, bo, gain2, shift2, bdown, s2[4:]], axis=0
    )
    if direct:
        weight_grads, vector_grads = run_scatter(grads, local_vector, ng, nd)
        vector_grads = vector_grads.reshape(-1)
    else:
        vector_grads = lax.psum(local_vector.reshape(-1), ("grp", "dev"))
        weight_grads = lax.psum_scatter(grads, ("grp", "dev"), scatter_dimension=0, tiled=True)
        weight_grads = weight_grads.astype(F32)
    tokens_all = rows * nd * ng
    new_vectors = vectors - vector_rate / math.sqrt(tokens_all) * vector_grads

    new_left = 0.5 * left_stats + 0.5 * jnp.einsum(
        "bij,bkj->bik", weight_grads, weight_grads, precision=highest
    )
    new_right = 0.5 * right_stats + 0.5 * jnp.einsum(
        "bji,bjk->bik", weight_grads, weight_grads, precision=highest
    )
    shaped = jnp.einsum("bij,bjk->bik", left_roots, weight_grads, precision=highest)
    shaped = jnp.einsum("bij,bjk->bik", shaped, right_roots, precision=highest)
    new_weights = weight_slots - weight_rate * shaped
    return (
        act.reshape(inputs.shape),
        ig.reshape(inputs.shape),
        weight_grads,
        new_left,
        new_right,
        new_weights,
        vector_grads,
        new_vectors,
    )


def solution(mesh):
    return jax.shard_map(
        local,
        mesh=mesh,
        in_specs=(
            P("grp", "dev", None),
            P("grp", "dev", None),
            P(("grp", "dev"), None, None),
            P(),
            P(("grp", "dev"), None, None),
            P(("grp", "dev"), None, None),
            P(("grp", "dev"), None, None),
            P(("grp", "dev"), None, None),
            P(),
            P("grp"),
        ),
        out_specs=(
            P("grp", "dev", None),
            P("grp", "dev", None),
            P(("grp", "dev"), None, None),
            P(("grp", "dev"), None, None),
            P(("grp", "dev"), None, None),
            P(("grp", "dev"), None, None),
            P(),
            P(),
        ),
        check_vma=False,
    )
```

```python
import functools
import math

import jax
import jax.numpy as jnp
from jax import lax
from jax.experimental import pallas as pl
from jax.experimental.pallas import tpu as pltpu
from jax.sharding import PartitionSpec as P

H = 16
FF = 4096
PIC = 256

eps = 1e-05
weight_rate = 0.5
vector_rate = 0.5
big_negative = -1e30
highest = lax.Precision.HIGHEST
F32 = jnp.float32
BF16 = jnp.bfloat16
LOG2E = 1.4426950408889634
MIB = 1024 * 1024

GAIN1, SHIFT1, BQ, BV, BO, GAIN2, SHIFT2, BDOWN, BUP = range(9)


def dot_nn(a, b):
    return lax.dot_general(a, b, (((1,), (0,)), ((), ())), preferred_element_type=F32)


def dot_nt(a, b):
    return lax.dot_general(a, b, (((1,), (1,)), ((), ())), preferred_element_type=F32)


def invert_order(slot_block):
    places = jnp.arange(slot_block.shape[0], dtype=jnp.int32)
    matches = (slot_block[None, :] == places[:, None]).astype(jnp.int32)
    return jnp.sum(matches * places[None, :], axis=1)


def vmem():
    return pl.BlockSpec(memory_space=pltpu.VMEM)


def smem():
    return pl.BlockSpec(memory_space=pltpu.SMEM)


def hbm():
    return pl.BlockSpec(memory_space=pl.ANY)


def sds(shape, dtype):
    return jax.ShapeDtypeStruct(shape, dtype)


def params(mib=58, **kw):
    return pltpu.CompilerParams(vmem_limit_bytes=mib * MIB, **kw)


def layer_stats(v):
    middle = jnp.mean(v, axis=-1, keepdims=True)
    centred = v - middle
    spread = jnp.mean(centred * centred, axis=-1, keepdims=True)
    return centred, lax.rsqrt(spread + eps)


def fold_rows(v):
    return jnp.sum(v.reshape(v.shape[0] // 8, 8, v.shape[1]), axis=0)


def fetch_block(gath, slot, dst, row, col, sem, side):
    return pltpu.make_async_copy(
        gath.at[slot], dst.at[pl.ds(row, side), pl.ds(col, side)], sem
    )


def qkv_kernel(slot_ref, x_ref, vec_ref, gath, h1_ref, out_ref, wbuf, sems, *, nd):
    rows, width = x_ref.shape
    side = gath.shape[1]
    per = width // side
    lanes = out_ref.shape[3]
    for part in range(3):
        @pl.loop(0, per)
        def _(i):
            for j in range(per):
                slot = slot_ref[i * 3 * per + part * per + j]
                fetch_block(gath, slot, wbuf.at[part], pl.multiple_of(i * side, side), j * side, sems.at[part], side).start()

    chunk = 32
    gain = vec_ref[GAIN1:GAIN1 + 1, :]
    shift = vec_ref[SHIFT1:SHIFT1 + 1, :]

    @pl.loop(0, rows // chunk)
    def _(r):
        at = pl.ds(pl.multiple_of(r * chunk, chunk), chunk)
        centred, inv = layer_stats(x_ref[at, :].astype(F32))
        h1_ref[at, :] = (centred * inv * gain + shift).astype(BF16)

    for part in range(3):
        pltpu.make_async_copy(wbuf.at[part], wbuf.at[part], sems.at[part]).wait()
        for half in range(2):
            cols = slice(half * width // 2, (half + 1) * width // 2)
            res = dot_nn(h1_ref[...], wbuf[part, :, cols])
            if part == 0:
                res = res + vec_ref[BQ:BQ + 1, cols]
            if part == 2:
                res = res + vec_ref[BV:BV + 1, cols]
            res = res.astype(BF16)
            for d in range(nd // 2):
                out_ref[half * (nd // 2) + d, part, :, :] = res[:, d * lanes:(d + 1) * lanes]


def run_qkv(slot_of, x, vec, gath, nd):
    rows, width = x.shape
    lanes = width // nd
    return pl.pallas_call(
        functools.partial(qkv_kernel, nd=nd),
        out_shape=(sds((rows, width), BF16), sds((nd, 3, rows, lanes), BF16)),
        in_specs=[smem(), vmem(), vmem(), hbm()],
        out_specs=(vmem(), vmem()),
        scratch_shapes=[pltpu.VMEM((3, width, width), BF16), pltpu.SemaphoreType.DMA((3,))],
        compiler_params=params(),
        name="qkv",
    )(slot_of, x, vec, gath)


MESH = pl.DeviceIdType.MESH


def remote(src, dst, send, recv, device):
    return pltpu.make_async_remote_copy(
        src_ref=src, dst_ref=dst, send_sem=send, recv_sem=recv, device_id=device, device_id_type=MESH
    )


def arrived(ref, sem):
    pltpu.make_async_copy(ref, ref, sem).wait()


def greet_plane(g, d, nd):
    barrier = pltpu.get_barrier_semaphore()
    for p in range(1, nd):
        pl.semaphore_signal(barrier, inc=1, device_id=(g, lax.rem(d + p, nd)), device_id_type=MESH)
    pl.semaphore_wait(barrier, nd - 1)


def parts3(v):
    hi = v.astype(BF16)
    mid = (v - hi.astype(F32)).astype(BF16)
    lo = (v - hi.astype(F32) - mid.astype(F32)).astype(BF16)
    return hi.astype(F32), mid.astype(F32), lo.astype(F32)


def own_lanes(h, shape, hpd, lanes):
    lane = lax.broadcasted_iota(jnp.int32, shape, 1)
    size = lanes // hpd
    return (lane >= h * size) & (lane < (h + 1) * size)


def place(values, base, tok, width):
    lane = lax.broadcasted_iota(jnp.int32, (tok, width), 1)
    out = jnp.zeros((tok, width), F32)
    for n, v in enumerate(values):
        out = jnp.where(lane == base + n, v, out)
    return out


def spare(h, hpd, lanes):
    return (lanes // hpd) * (1 - h) if hpd > 1 else 0


def q_columns(q, h, hpd, slope, extra):
    tok, lanes = q.shape
    scaled = q.astype(F32) * ((lanes // hpd) ** (-0.5) * LOG2E)
    hi = scaled.astype(BF16)
    low = scaled - hi.astype(F32)
    row = jnp.full((tok, 128), 0.0, F32)
    near = [row + p for p in parts3(jnp.full((tok, 128), slope, F32))]
    far = [row + p for p in parts3(jnp.full((tok, 128), slope * tok, F32))]
    columns = place(near + far + extra, spare(h, hpd, lanes), tok, 128)
    if hpd > 1:
        own = own_lanes(h, (tok, lanes), hpd, lanes)
        return jnp.concatenate(
            [jnp.where(own, hi.astype(F32), 0.0), jnp.where(own, low, columns)], axis=1
        ).astype(BF16)
    return jnp.concatenate([hi.astype(F32), low, columns], axis=1).astype(BF16)


def k_columns(k, h, j, hpd, extra):
    tok, lanes = k.shape
    u = lax.broadcasted_iota(jnp.int32, (tok, 128), 0).astype(F32)
    block = jnp.full((tok, 128), j, jnp.int32).astype(F32)
    columns = place([u] * 3 + [block] * 3 + [1.0] * extra, spare(h, hpd, lanes), tok, 128)
    wide = k.astype(F32)
    if hpd > 1:
        own = own_lanes(h, (tok, lanes), hpd, lanes)
        return jnp.concatenate([wide, jnp.where(own, wide, columns)], axis=1).astype(BF16)
    return jnp.concatenate([wide, wide, columns], axis=1).astype(BF16)


def far_side(slope, tok):
    u = lax.broadcasted_iota(jnp.int32, (tok, tok), 0)
    t = lax.broadcasted_iota(jnp.int32, (tok, tok), 1)
    after = u > t
    return (
        jnp.where(after, big_negative, 0.0),
        jnp.where(after, (2.0 * slope) * (t - u).astype(F32), 0.0),
    )


def attn_fwd_kernel(
    span_ref, slope_ref, src, got, o_got, o32_ref, lse_ref,
    qa, ka, vt, scores, corr, o_out, ss, sr, os, orr, loc, *, hpd, nd
):
    nb, _, seqs, tok, lanes = got.shape
    size = lanes // hpd
    t_all = nb * tok
    g = lax.axis_index("grp")
    d = lax.axis_index("dev")

    for q in range(seqs):
        pltpu.make_async_copy(src.at[d, :, q], got.at[d, :, q], loc.at[q]).start()
    greet_plane(g, d, nd)

    def send(q, p):
        to = lax.rem(d + p, nd)
        return remote(src.at[to, :, q], got.at[d, :, q], ss.at[q, p], sr.at[q, p], (g, to))

    for q in range(seqs):
        @pl.loop(1, nd)
        def _(p):
            send(q, p).start()

    def send_o(q, i, p):
        return remote(o_out.at[i, q], o_got.at[d, q], os.at[q, i], orr.at[q, p], (g, i))

    for h in range(hpd):
        mask, span = far_side(slope_ref[h] * LOG2E, tok)
        zero = jnp.zeros((tok, tok), F32)
        gone = jnp.full((tok, tok), big_negative, F32)
        for flag, table in enumerate((mask, span)):
            corr[h, 0, flag, 0:tok] = table
            corr[h, 0, flag, tok:] = gone
            corr[h, 1, flag, 0:tok] = zero
            corr[h, 1, flag, tok:] = table

    for q in range(seqs):
        pltpu.make_async_copy(src.at[d, :, q], got.at[d, :, q], loc.at[q]).wait()

        @pl.loop(1, nd)
        def _(p):
            arrived(got.at[lax.rem(d + nd - p, nd), :, q], sr.at[q, p])

        @pl.loop(0, nb)
        def _(j):
            at_j = pl.ds(pl.multiple_of(j * tok, tok), tok)
            vt[0:lanes, at_j] = got[j, 2, q].astype(F32).T.astype(BF16)
            for h in range(hpd):
                qa[h, j] = q_columns(got[j, 0, q], h, hpd, slope_ref[h] * LOG2E, [])
                ka[h, at_j, :] = k_columns(got[j, 1, q], h, j, hpd, 0)

        start = span_ref[q]
        pair = 2 * tok

        @pl.loop(0, nb)
        def _(i):
            flag = (start == i * tok).astype(jnp.int32)
            parity = lax.rem(i, 2)
            last = i // 2

            def at_pair(n):
                return pl.ds(pl.multiple_of(n * pair, pair), pair)

            def fold_max(v):
                return jnp.max(v.reshape(pair // 8, 8, tok), axis=0)

            def score(n, tops):
                new = []
                for h in range(hpd):
                    s = dot_nt(ka[h, at_pair(n), :], qa[h, i])
                    scores[h, at_pair(n), :] = s
                    new.append(jnp.maximum(tops[h], fold_max(s)))
                return tuple(new)

            tops = lax.fori_loop(
                0, last, score, tuple([jnp.full((8, tok), big_negative, F32)] * hpd)
            )
            top = []
            for h in range(hpd):
                s = dot_nt(ka[h, at_pair(last), :], qa[h, i]) + corr[h, parity, flag]
                scores[h, at_pair(last), :] = s
                top.append(jnp.max(jnp.maximum(tops[h], fold_max(s)), axis=0, keepdims=True))

            def weigh(n, state):
                new = []
                for h in range(hpd):
                    acc, total = state[h]
                    p = jnp.exp2(scores[h, at_pair(n), :] - top[h])
                    total = total + jnp.sum(p.reshape(pair // 8, 8, tok), axis=0)
                    acc = acc + dot_nn(vt[h * size:(h + 1) * size, at_pair(n)], p.astype(BF16))
                    new.append((acc, total))
                return tuple(new)

            state = lax.fori_loop(
                0,
                last + 1,
                weigh,
                tuple([(jnp.zeros((size, tok), F32), jnp.zeros((8, tok), F32))] * hpd),
            )
            outs = []
            logs = []
            for h in range(hpd):
                acc, total = state[h]
                total = jnp.sum(total, axis=0, keepdims=True)
                outs.append(acc / total)
                logs.append(jnp.broadcast_to(top[h] + jnp.log2(total), (128 // hpd, tok)))
            out = (jnp.concatenate(outs, axis=0) if hpd > 1 else outs[0]).T
            o32_ref[i, q] = out
            o_out[i, q] = out.astype(BF16)
            lse_ref[i, q] = (jnp.concatenate(logs, axis=0) if hpd > 1 else logs[0]).T

            @pl.when(i == d)
            def _():
                pltpu.make_async_copy(o_out.at[i, q], o_got.at[d, q], os.at[q, i]).start()

            @pl.when(i != d)
            def _():
                send_o(q, i, lax.rem(i - d + nd, nd)).start()

    for q in range(seqs):
        @pl.loop(1, nd)
        def _(p):
            arrived(o_got.at[lax.rem(d + nd - p, nd), q], orr.at[q, p])
            send(q, p).wait_send()

        @pl.loop(0, nd)
        def _(i):
            arrived(o_out.at[i, q], os.at[q, i])


def run_attn_fwd(span, slopes, qkv, hpd):
    nb, _, seqs, tok, lanes = qkv.shape
    t = nb * tok
    dma = pltpu.SemaphoreType.DMA
    return pl.pallas_call(
        functools.partial(attn_fwd_kernel, hpd=hpd, nd=nb),
        out_shape=(
            sds(qkv.shape, BF16),
            sds((nb, seqs, tok, lanes), BF16),
            sds((nb, seqs, tok, lanes), F32),
            sds((nb, seqs, tok, 128), F32),
        ),
        in_specs=[smem(), smem(), hbm()],
        out_specs=(vmem(), vmem(), vmem(), vmem()),
        scratch_shapes=[
            pltpu.VMEM((hpd, nb, tok, 256), BF16),
            pltpu.VMEM((hpd, t, 256), BF16),
            pltpu.VMEM((lanes, t), BF16),
            pltpu.VMEM((hpd, t, tok), F32),
            pltpu.VMEM((hpd, 2, 2, 2 * tok, tok), F32),
            pltpu.VMEM((nb, seqs, tok, lanes), BF16),
            dma((seqs, nb)),
            dma((seqs, nb)),
            dma((seqs, nb)),
            dma((seqs, nb)),
            dma((seqs,)),
        ],
        compiler_params=params(collective_id=2, has_side_effects=True),
        name="attn_fwd",
    )(span, slopes, qkv)


def attn_bwd_kernel(
    span_ref, slope_ref, qkv_ref, do_src, o32_ref, lse_ref, got,
    do_got, out, qa, ka, kt, va, qm, da, dm, dqt, corr, ss, sr, gs, gr, loc, *, hpd, nd
):
    nb, _, seqs, tok, lanes = qkv_ref.shape
    size = lanes // hpd
    unit = size ** (-0.5)
    g = lax.axis_index("grp")
    d = lax.axis_index("dev")

    def own_copy(q):
        return pltpu.make_async_copy(do_src.at[d, q], do_got.at[d, q], loc.at[q])

    for q in range(seqs):
        own_copy(q).start()
    greet_plane(g, d, nd)

    def send(q, p):
        to = lax.rem(d + p, nd)
        return remote(do_src.at[to, q], do_got.at[d, q], ss.at[q, p], sr.at[q, p], (g, to))

    for q in range(seqs):
        @pl.loop(1, nd)
        def _(p):
            send(q, p).start()

    def back(q, kind, p):
        to = lax.rem(d + p, nd)
        at = pl.ds(kind, 1 + kind)
        return remote(
            out.at[to, at, q], got.at[d, at, q], gs.at[q, kind, p], gr.at[q, kind, p], (g, to)
        )

    def back_own(q, kind):
        at = pl.ds(kind, 1 + kind)
        return pltpu.make_async_copy(out.at[d, at, q], got.at[d, at, q], gs.at[q, kind, 0])

    for h in range(hpd):
        mask, span = far_side(slope_ref[h] * LOG2E, tok)
        corr[h, 0] = mask
        corr[h, 1] = span

    for q in range(seqs):
        @pl.loop(0, nb)
        def _(j):
            at_j = pl.ds(pl.multiple_of(j * tok, tok), tok)
            qj = qkv_ref[j, 0, q]
            kj = qkv_ref[j, 1, q]
            vj = qkv_ref[j, 2, q].astype(F32)
            kt[:, at_j] = kj.astype(F32).T.astype(BF16)
            dqt[:, at_j] = jnp.zeros((lanes, tok), F32)
            for h in range(hpd):
                low = lse_ref[j, q][:, h * (128 // hpd):h * (128 // hpd) + 1]
                extra = [-p for p in parts3(low)]
                qa[h, j] = q_columns(qj, h, hpd, slope_ref[h] * LOG2E, extra)
                ka[h, j] = k_columns(kj, h, j, hpd, 3)
                if hpd > 1:
                    own = own_lanes(h, (tok, lanes), hpd, lanes)
                    qm[h, j] = jnp.where(own, qj.astype(F32), 0.0).astype(BF16)
                    va[h, j] = jnp.where(
                        own, vj, place([1.0] * 3, spare(h, hpd, lanes), tok, lanes)
                    ).astype(BF16)
                else:
                    qm[h, j] = qj
                    va[h, j] = jnp.concatenate(
                        [vj, place([1.0] * 3, 0, tok, lanes)], axis=1
                    ).astype(BF16)

        own_copy(q).wait()

        @pl.loop(1, nd)
        def _(p):
            arrived(do_got.at[lax.rem(d + nd - p, nd), q], sr.at[q, p])

        @pl.loop(0, nb)
        def _(j):
            do = do_got[j, q].astype(F32)
            prod = do * o32_ref[j, q]
            for h in range(hpd):
                if hpd > 1:
                    own = own_lanes(h, (tok, lanes), hpd, lanes)
                    delta = jnp.sum(jnp.where(own, prod, 0.0), axis=1, keepdims=True)
                    extra = place([-p for p in parts3(delta)], spare(h, hpd, lanes), tok, lanes)
                    da[h, j] = jnp.where(own, do, extra).astype(BF16)
                    dm[h, j] = jnp.where(own, do, 0.0).astype(BF16)
                else:
                    delta = jnp.sum(prod, axis=1, keepdims=True)
                    extra = place([-p for p in parts3(delta)], 0, tok, lanes)
                    da[h, j] = jnp.concatenate([do, extra], axis=1).astype(BF16)
                    dm[h, j] = do.astype(BF16)

        start = span_ref[q]

        @pl.loop(0, nb)
        def _(n):
            j = lax.rem(d + n, nb)
            at_j = pl.ds(pl.multiple_of(j * tok, tok), tok)
            flag = (start == j * tok).astype(jnp.int32)

            def tile(i, h, dk, dv, near):
                at_i = pl.ds(pl.multiple_of(i * tok, tok), tok)
                s = dot_nt(ka[h, j], qa[h, i])
                if near:
                    s = s + corr[h, flag]
                p = jnp.exp2(s)
                ds = (p * dot_nt(va[h, j], da[h, i])).astype(BF16)
                dv = dv + dot_nn(p.astype(BF16), dm[h, i])
                dk = dk + dot_nn(ds, qm[h, i])
                rows = slice(h * size, (h + 1) * size)
                dqt[rows, at_i] += dot_nn(kt[rows, at_j], ds)
                return dk, dv

            dk = jnp.zeros((tok, lanes), F32)
            dv = jnp.zeros((tok, lanes), F32)
            for h in range(hpd):
                dk, dv = tile(j, h, dk, dv, True)

            def body(i, carry):
                dk, dv = carry
                for h in range(hpd):
                    dk, dv = tile(i, h, dk, dv, False)
                return dk, dv

            dk, dv = lax.fori_loop(j + 1, nb, body, (dk, dv))
            out[j, 1, q] = (dk * unit).astype(BF16)
            out[j, 2, q] = dv.astype(BF16)

            @pl.when(n == 0)
            def _():
                back_own(q, 1).start()

            @pl.when(n > 0)
            def _():
                back(q, 1, n).start()

        @pl.loop(0, nb)
        def _(n):
            j = lax.rem(d + n, nb)
            at_j = pl.ds(pl.multiple_of(j * tok, tok), tok)
            out[j, 0, q] = (dqt[:, at_j].T * unit).astype(BF16)

            @pl.when(n == 0)
            def _():
                back_own(q, 0).start()

            @pl.when(n > 0)
            def _():
                back(q, 0, n).start()

    for q in range(seqs):
        for kind in range(2):
            back_own(q, kind).wait()

        @pl.loop(1, nd)
        def _(p):
            send(q, p).wait_send()
            source = lax.rem(d + nd - p, nd)
            for kind in range(2):
                back(q, kind, p).wait_send()
                arrived(got.at[source, pl.ds(kind, 1 + kind), q], gr.at[q, kind, p])


def run_attn_bwd(span, slopes, qkv, do, o32, lse, hpd):
    nb, _, seqs, tok, lanes = qkv.shape
    t = nb * tok
    dma = pltpu.SemaphoreType.DMA
    wide = 128 if hpd == 1 else lanes
    return pl.pallas_call(
        functools.partial(attn_bwd_kernel, hpd=hpd, nd=nb),
        out_shape=sds(qkv.shape, BF16),
        in_specs=[smem(), smem(), vmem(), hbm(), vmem(), vmem()],
        out_specs=vmem(),
        scratch_shapes=[
            pltpu.VMEM((nb, seqs, tok, lanes), BF16),
            pltpu.VMEM(qkv.shape, BF16),
            pltpu.VMEM((hpd, nb, tok, 256), BF16),
            pltpu.VMEM((hpd, nb, tok, 256), BF16),
            pltpu.VMEM((lanes, t), BF16),
            pltpu.VMEM((hpd, nb, tok, wide), BF16),
            pltpu.VMEM((hpd, nb, tok, lanes), BF16),
            pltpu.VMEM((hpd, nb, tok, wide), BF16),
            pltpu.VMEM((hpd, nb, tok, lanes), BF16),
            pltpu.VMEM((lanes, t), F32),
            pltpu.VMEM((hpd, 2, tok, tok), F32),
            dma((seqs, nb)),
            dma((seqs, nb)),
            dma((seqs, 2, nb)),
            dma((seqs, 2, nb)),
            dma((seqs,)),
        ],
        compiler_params=params(collective_id=3, has_side_effects=True),
        name="attn_bwd",
    )(span, slopes, qkv, do, o32, lse)


def mlp_kernel(
    slot_ref, o_ref, x_ref, dy_ref, vec_ref, gath,
    act_ref, att_ref, h2_ref, g_ref, dz_ref, da_ref, dx1_ref, do_ref, sums_ref,
    wo, wup, wdn, x1, acc, dh2, sem_o, sem_t, *, nd, first_o, first_up, first_dn, tile
):
    rows, width = x_ref.shape
    side = gath.shape[1]
    per = width // side
    ff = g_ref.shape[1]
    tiles = ff // tile
    cols = tile // side
    lanes = o_ref.shape[2]
    fper = ff // side

    @pl.loop(0, per)
    def _(i):
        for j in range(per):
            fetch_block(gath, slot_ref[first_o + i * per + j], wo, pl.multiple_of(i * side, side), j * side, sem_o.at[0], side).start()

    def fetch_tile(f):
        @pl.loop(0, per)
        def _(i):
            for j in range(cols):
                fetch_block(gath, slot_ref[first_up + i * fper + f * cols + j], wup.at[f], pl.multiple_of(i * side, side), j * side, sem_t.at[f], side).start()
            for j in range(cols):
                fetch_block(gath, slot_ref[first_dn + (f * cols + j) * per + i], wdn.at[f], j * side, pl.multiple_of(i * side, side), sem_t.at[f], side).start()

    fetch_tile(0)
    fetch_tile(1)
    for d in range(nd):
        att_ref[:, d * lanes:(d + 1) * lanes] = o_ref[d]
    pltpu.make_async_copy(wo, wo, sem_o.at[0]).wait()
    for half in range(2):
        c = slice(half * width // 2, (half + 1) * width // 2)
        x1[:, c] = x_ref[:, c].astype(F32) + dot_nn(att_ref[...], wo[:, c]) + vec_ref[BO:BO + 1, c]

    chunk = 32

    def rows_at(r):
        return pl.ds(pl.multiple_of(r * chunk, chunk), chunk)

    @pl.loop(0, rows // chunk)
    def _(r):
        at = rows_at(r)
        centred, inv = layer_stats(x1[at, :])
        h2_ref[at, :] = (centred * inv * vec_ref[GAIN2:GAIN2 + 1, :] + vec_ref[SHIFT2:SHIFT2 + 1, :]).astype(BF16)
        acc[at, :] = x1[at, :] + vec_ref[BDOWN:BDOWN + 1, :]
        dh2[at, :] = jnp.zeros((chunk, width), F32)

    @pl.loop(0, tiles)
    def _(f):
        @pl.when(f + 2 < tiles)
        def _():
            fetch_tile(f + 2)
        pltpu.make_async_copy(wup.at[f], wup.at[f], sem_t.at[f]).wait()
        pltpu.make_async_copy(wdn.at[f], wdn.at[f], sem_t.at[f]).wait()
        per_row = width // tile
        bias = vec_ref[pl.ds(BUP + f // per_row, 1), pl.ds(pl.multiple_of((f % per_row) * tile, tile), tile)]
        at_f = pl.ds(pl.multiple_of(f * tile, tile), tile)
        z = dot_nn(h2_ref[...], wup[f]) + bias
        dg = dot_nt(dy_ref[...], wdn[f])
        z2 = z * z
        th = jnp.tanh(0.7978845608028654 * (z + 0.044715 * z2 * z))
        g = (0.5 * z * (1.0 + th)).astype(BF16)
        slope = 0.5 * (1.0 + th) + 0.5 * z * (1.0 - th * th) * (
            0.7978845608028654 * (1.0 + 3.0 * 0.044715 * z2)
        )
        dz = (dg * slope).astype(BF16)
        g_ref[:, at_f] = g
        dz_ref[:, at_f] = dz
        sums_ref[pl.ds(pl.multiple_of(8 * (4 + f // per_row), 8), 8), pl.ds(pl.multiple_of((f % per_row) * tile, tile), tile)] = fold_rows(dz.astype(F32))
        acc[...] += dot_nn(g, wdn[f])
        dh2[...] += dot_nt(dz, wup[f])

    zero = jnp.zeros((8, width), F32)

    def finish(r, carry):
        s_bo, s_gain, s_shift, s_bdown = carry
        at = rows_at(r)
        act_ref[at, :] = acc[at, :].astype(BF16)
        centred, inv = layer_stats(x1[at, :])
        hat = centred * inv
        dh = dh2[at, :]
        dhg = dh * vec_ref[GAIN2:GAIN2 + 1, :]
        back = inv * (
            dhg
            - jnp.mean(dhg, axis=-1, keepdims=True)
            - hat * jnp.mean(dhg * hat, axis=-1, keepdims=True)
        )
        dy = dy_ref[at, :].astype(F32)
        dx1 = dy + back
        dx1_ref[at, :] = dx1
        da = dx1.astype(BF16)
        da_ref[at, :] = da
        return (
            s_bo + fold_rows(da.astype(F32)),
            s_gain + fold_rows(dh * hat),
            s_shift + fold_rows(dh),
            s_bdown + fold_rows(dy),
        )

    carry = lax.fori_loop(0, rows // chunk, finish, (zero, zero, zero, zero))
    for n in range(4):
        sums_ref[8 * n:8 * n + 8, :] = carry[n]
    for half in range(2):
        c = slice(half * width // 2, (half + 1) * width // 2)
        res = dot_nt(da_ref[...], wo[c, :]).astype(BF16)
        for d in range(nd // 2):
            do_ref[half * (nd // 2) + d] = res[:, d * lanes:(d + 1) * lanes]


def run_mlp(slot_of, o, x, dy, vec, gath, nd):
    rows, width = x.shape
    side = gath.shape[1]
    lanes = width // nd
    per = width // side
    first_o = 3 * per * per
    first_up = first_o + per * per
    first_dn = first_up + per * (FF // side)
    tile = 512
    return pl.pallas_call(
        functools.partial(
            mlp_kernel, nd=nd, first_o=first_o, first_up=first_up, first_dn=first_dn, tile=tile
        ),
        out_shape=(
            sds((rows, width), BF16),
            sds((rows, width), BF16),
            sds((rows, width), BF16),
            sds((rows, FF), BF16),
            sds((rows, FF), BF16),
            sds((rows, width), BF16),
            sds((rows, width), F32),
            sds((nd, rows, lanes), BF16),
            sds((8 * (4 + FF // width), width), F32),
        ),
        in_specs=[smem(), vmem(), vmem(), vmem(), vmem(), hbm()],
        out_specs=tuple([vmem()] * 9),
        scratch_shapes=[
            pltpu.VMEM((width, width), BF16),
            pltpu.VMEM((FF // tile, width, tile), BF16),
            pltpu.VMEM((FF // tile, tile, width), BF16),
            pltpu.VMEM((rows, width), F32),
            pltpu.VMEM((rows, width), F32),
            pltpu.VMEM((rows, width), F32),
            pltpu.SemaphoreType.DMA((1,)),
            pltpu.SemaphoreType.DMA((FF // tile,)),
        ],
        compiler_params=params(),
        name="mlp",
    )(slot_of, o, x, dy, vec, gath)


def dh1_kernel(
    slot_ref, dqkv_ref, x_ref, dx1_ref, vec_ref, gath, ig_ref, cat_ref, sums_ref,
    wbuf, dh1, sems, *, nd
):
    rows, width = x_ref.shape
    side = gath.shape[1]
    per = width // side
    lanes = dqkv_ref.shape[3]
    for part in range(3):
        @pl.loop(0, per)
        def _(i):
            for j in range(per):
                slot = slot_ref[i * 3 * per + part * per + j]
                fetch_block(gath, slot, wbuf.at[part], pl.multiple_of(i * side, side), j * side, sems.at[part], side).start()

    for part in range(3):
        for d in range(nd):
            at = part * width + d * lanes
            cat_ref[:, at:at + lanes] = dqkv_ref[d, part]
    for part in range(3):
        pltpu.make_async_copy(wbuf.at[part], wbuf.at[part], sems.at[part]).wait()
        for half in range(2):
            c = slice(half * width // 2, (half + 1) * width // 2)
            res = dot_nt(cat_ref[:, part * width:(part + 1) * width], wbuf[part, c, :])
            if part == 0:
                dh1[:, c] = res
            else:
                dh1[:, c] += res

    chunk = 32
    zero = jnp.zeros((8, width), F32)

    def finish(r, carry):
        s_gain, s_shift, s_bq, s_bv = carry
        at = pl.ds(pl.multiple_of(r * chunk, chunk), chunk)
        centred, inv = layer_stats(x_ref[at, :].astype(F32))
        hat = centred * inv
        dh = dh1[at, :]
        dhg = dh * vec_ref[GAIN1:GAIN1 + 1, :]
        back = inv * (
            dhg
            - jnp.mean(dhg, axis=-1, keepdims=True)
            - hat * jnp.mean(dhg * hat, axis=-1, keepdims=True)
        )
        ig_ref[at, :] = dx1_ref[at, :] + back
        return (
            s_gain + fold_rows(dh * hat),
            s_shift + fold_rows(dh),
            s_bq + fold_rows(cat_ref[at, 0:width].astype(F32)),
            s_bv + fold_rows(cat_ref[at, 2 * width:3 * width].astype(F32)),
        )

    carry = lax.fori_loop(0, rows // chunk, finish, (zero, zero, zero, zero))
    for n in range(4):
        sums_ref[8 * n:8 * n + 8, :] = carry[n]


def run_dh1(slot_of, dqkv, x, dx1, vec, gath, nd):
    rows, width = x.shape
    return pl.pallas_call(
        functools.partial(dh1_kernel, nd=nd),
        out_shape=(
            sds((rows, width), F32),
            sds((rows, 3 * width), BF16),
            sds((32, width), F32),
        ),
        in_specs=[smem(), vmem(), vmem(), vmem(), vmem(), hbm()],
        out_specs=(vmem(), vmem(), vmem()),
        scratch_shapes=[
            pltpu.VMEM((3, width, width), BF16),
            pltpu.VMEM((rows, width), F32),
            pltpu.SemaphoreType.DMA((3,)),
        ],
        compiler_params=params(),
        name="dh1",
    )(slot_of, dqkv, x, dx1, vec, gath)


def wgrad_kernel(
    slot_ref, h1, att, h2, g, dqkv, da, dz, dy, out,
    v_a, v_b, a_t, stage, sem_in, sem_out, *, side, tile
):
    rows, width = h1.shape
    per = width // side
    cols = tile // side
    ff = g.shape[1]
    runs = [(h2, 0, dz, 4 * per * per, ff // side)]
    for c in range(ff // width):
        first = 4 * per * per + per * (ff // side) + c * per * per
        runs.append((g, c * width, dy, first, per))
    runs.append((att, 0, da, 3 * per * per, per))
    runs.append((h1, 0, dqkv, 0, 3 * per))

    def loads(n):
        a, at, b, _, _ = runs[n]
        copies = [pltpu.make_async_copy(a.at[:, pl.ds(at, width)], v_a.at[n % 2], sem_in.at[n % 2, 0])]
        fresh = n == 0 or runs[n - 1][2] is not b
        if fresh:
            wide = b.shape[1]
            copies.append(
                pltpu.make_async_copy(b, v_b.at[slot_b[n], :, pl.ds(0, wide)], sem_in.at[n % 2, 1])
            )
        return copies

    slot_b = []
    for n in range(len(runs)):
        if n == 0:
            slot_b.append(0)
        elif runs[n - 1][2] is runs[n][2]:
            slot_b.append(slot_b[-1])
        else:
            slot_b.append(1 - slot_b[-1])

    started = {0: loads(0)}
    for copy in started[0]:
        copy.start()
    count = 0

    def out_wait(slot):
        pltpu.make_async_copy(stage.at[slot], stage.at[slot], sem_out.at[slot]).wait()

    for n in range(len(runs)):
        _, _, b, first, stride = runs[n]
        if n + 1 < len(runs):
            started[n + 1] = loads(n + 1)
            for copy in started[n + 1]:
                copy.start()
        for copy in started[n]:
            copy.wait()
        for r in range(width // 256):
            c = slice(r * 256, (r + 1) * 256)
            a_t[c, :] = v_a[n % 2, :, c].astype(F32).T.astype(BF16)
        sb = slot_b[n]
        base = count

        def step(t, base=base, first=first, stride=stride, sb=sb):
            slot = (base + t) % 2

            @pl.when(base + t >= 2)
            def _():
                out_wait(slot)
            res = dot_nn(a_t[...], v_b[sb, :, pl.ds(pl.multiple_of(t * tile, tile), tile)]).astype(BF16)
            for i in range(per):
                for j in range(cols):
                    stage[slot, i * cols + j] = res[i * side:(i + 1) * side, j * side:(j + 1) * side]
            for i in range(per):
                for j in range(cols):
                    dst = slot_ref[first + i * stride + t * cols + j]
                    pltpu.make_async_copy(stage.at[slot, i * cols + j], out.at[dst], sem_out.at[slot]).start()

        steps = b.shape[1] // tile
        pl.loop(0, steps)(step)
        count += steps
    out_wait(0)
    out_wait(1)


def run_wgrad(slot_of, h1, att, h2, g, dqkv, da, dz, dy, side):
    rows, width = h1.shape
    tile = 512
    blocks = slot_of.shape[0]
    return pl.pallas_call(
        functools.partial(wgrad_kernel, side=side, tile=tile),
        out_shape=sds((blocks, side, side), BF16),
        in_specs=[smem()] + [hbm()] * 8,
        out_specs=hbm(),
        scratch_shapes=[
            pltpu.VMEM((2, rows, width), BF16),
            pltpu.VMEM((2, rows, FF), BF16),
            pltpu.VMEM((width, rows), BF16),
            pltpu.VMEM((2, (width // side) * (tile // side), side, side), BF16),
            pltpu.SemaphoreType.DMA((2, 2)),
            pltpu.SemaphoreType.DMA((2,)),
        ],
        compiler_params=params(),
        name="wgrad",
    )(slot_of, h1, att, h2, g, dqkv, da, dz, dy)


def whereami():
    g = lax.axis_index("grp")
    d = lax.axis_index("dev")
    core = lax.rem(d, 2)
    x = lax.rem(d // 2, 2)
    y = d // 4
    over_x = d + 2 - 4 * x
    over_y = d + 4 - 8 * y
    across = over_x + 4 - 8 * y
    sibling = d + 1 - 2 * core
    return g, d, over_x, over_y, across, sibling


def near_order(t, g, ng):
    t = ng - 1 - t
    low = jnp.where(t < ng - 1 - g, ng - 1 - t, t - (ng - 1 - g))
    high = jnp.where(t < g, t, ng - 1 - (t - g))
    return jnp.where(2 * g < ng, low, high)


def greet(g, ng, peers):
    barrier = pltpu.get_barrier_semaphore()
    for peer in peers:
        pl.semaphore_signal(barrier, inc=1, device_id=(g, peer), device_id_type=MESH)

    d = lax.axis_index("dev")

    @pl.when(g > 0)
    def _():
        pl.semaphore_signal(barrier, inc=1, device_id=(g - 1, d), device_id_type=MESH)

    @pl.when(g < ng - 1)
    def _():
        pl.semaphore_signal(barrier, inc=1, device_id=(g + 1, d), device_id_type=MESH)

    ends = (g > 0).astype(jnp.int32) + (g < ng - 1).astype(jnp.int32)
    pl.semaphore_wait(barrier, len(peers) + ends)


def gather_kernel(w_ref, out, own, local_sem, zs, zr, ss, sr, *, ng, nd):
    count = w_ref.shape[0]
    half = count // 2
    g, d, over_x, over_y, across, sibling = whereami()
    own[...] = w_ref[...].astype(BF16)
    greet(g, ng, (over_x, over_y, sibling))

    def region(gz, dev, first=0, size=count):
        return out.at[pl.ds((gz * nd + dev) * count + first, size)]

    kinds = (
        (d, 0, count, over_x),
        (d, 0, count, over_y),
        (d, 0, count, sibling),
        (over_x, 0, half, over_y),
        (over_y, half, count - half, over_x),
        (over_x, 0, count, sibling),
        (over_y, 0, count, sibling),
        (across, 0, half, sibling),
        (across, half, count - half, sibling),
    )

    def plane(n, gz, src=None):
        dev, first, size, to = kinds[n]
        at = region(gz, dev, first, size)
        return remote(at if src is None else src, at, ss.at[n, gz], sr.at[n, gz], (g, to))

    def line(gz, up, src=None):
        at = region(gz, d)
        to = g + 1 if up else g - 1
        return remote(at if src is None else src, at, zs.at[gz, int(up)], zr.at[gz], (to, d))

    def landed(n, gz, dev, first, size):
        arrived(region(gz, dev, first, size), sr.at[n, gz])

    mine = pltpu.make_async_copy(own, region(g, d), local_sem.at[0])
    mine.start()

    def column(t):
        gz = near_order(t, g, ng)
        if t == 0:
            @pl.when(g < ng - 1)
            def _():
                line(gz, True, own).start()

            @pl.when(g > 0)
            def _():
                line(gz, False, own).start()
            for n in range(3):
                plane(n, gz, own).start()
            return
        arrived(region(gz, d), zr.at[gz])

        @pl.when((gz < g) & (g < ng - 1))
        def _():
            line(gz, True).start()

        @pl.when((gz > g) & (g > 0))
        def _():
            line(gz, False).start()
        for n in range(3):
            plane(n, gz).start()

    def sides(t):
        gz = near_order(t, g, ng)
        landed(0, gz, over_x, 0, count)
        plane(3, gz).start()
        plane(5, gz).start()
        landed(1, gz, over_y, 0, count)
        plane(4, gz).start()
        plane(6, gz).start()

    def corner(t):
        gz = near_order(t, g, ng)
        landed(3, gz, across, 0, half)
        plane(7, gz).start()
        landed(4, gz, across, half, count - half)
        plane(8, gz).start()

    plan = [(t, f) for t in range(ng) for f in (0, 1, 2)]
    lag = {0: 0, 1: 2.5, 2: 4.5}
    for t, f in sorted(plan, key=lambda e: e[0] * 1.0 + lag[e[1]]):
        (column, sides, corner)[f](t)

    other = sibling
    o_x = sibling + over_x - d
    o_y = sibling + over_y - d
    o_d = sibling + across - d
    for t in range(ng):
        gz = near_order(t, g, ng)
        landed(2, gz, other, 0, count)
        landed(5, gz, o_x, 0, count)
        landed(6, gz, o_y, 0, count)
        landed(7, gz, o_d, 0, half)
        landed(8, gz, o_d, half, count - half)
    mine.wait()
    for t in range(ng):
        gz = near_order(t, g, ng)
        for n in range(9):
            plane(n, gz).wait_send()

        @pl.when((gz <= g) & (g < ng - 1))
        def _():
            line(gz, True).wait_send()

        @pl.when((gz >= g) & (g > 0))
        def _():
            line(gz, False).wait_send()


def run_gather(w, ng, nd):
    count, side, _ = w.shape
    return pl.pallas_call(
        functools.partial(gather_kernel, ng=ng, nd=nd),
        out_shape=sds((ng * nd * count, side, side), BF16),
        in_specs=[vmem()],
        out_specs=hbm(),
        scratch_shapes=[
            pltpu.VMEM((count, side, side), BF16),
            pltpu.SemaphoreType.DMA((1,)),
            pltpu.SemaphoreType.DMA((ng, 2)),
            pltpu.SemaphoreType.DMA((ng,)),
            pltpu.SemaphoreType.DMA((9, ng)),
            pltpu.SemaphoreType.DMA((9, ng)),
        ],
        compiler_params=params(collective_id=0, has_side_effects=True),
        name="gather",
    )(w)


def scatter_kernel(
    grads, vec_ref, out_ref, vout_ref,
    mine, r0, r1y, r1x, r2x, r2y, ru, rd, vwork, vxy, vz,
    load, s0, w0, s1, w1, s2, w2, sz, wz, vs, vw, *, ng, nd
):
    count = out_ref.shape[0]
    half = count // 2
    rest = count - half
    g, d, over_x, over_y, across, sibling = whereami()
    columns = (d, over_x, over_y, across)
    low = slice(0, half)
    high = slice(half, count)

    def region(gz, dev):
        return grads.at[pl.ds((gz * nd + dev) * count, count)]

    def order(t):
        return near_order(ng - 1 - t, g, ng)

    for t in range(ng):
        for c in range(4):
            pltpu.make_async_copy(region(order(t), columns[c]), mine.at[order(t), c], load.at[order(t), c]).start()
    vwork[0] = vec_ref[...]
    greet(g, ng, (over_x, over_y, sibling))

    def to_sibling(gz, c):
        return remote(
            region(gz, columns[c] + sibling - d), r0.at[gz, c], s0.at[gz, c], w0.at[gz, c], (g, sibling)
        )

    peers = (sibling, over_x, over_y)

    def vec_copy(n):
        return remote(vwork.at[n], vxy.at[n], vs.at[n], vw.at[n], (g, peers[n]))

    vec_copy(0).start()
    for t in range(ng):
        for c in range(4):
            to_sibling(order(t), c).start()

    def add(dst, src, size):
        @pl.loop(0, size)
        def _(i):
            dst[i] = (dst[i].astype(F32) + src[i].astype(F32)).astype(BF16)

    def cut(ref, part):
        return ref.at[pl.ds(part.start, part.stop - part.start)]

    first = (
        (2, low, r1y, 0, over_y),
        (3, low, r1y, 1, over_y),
        (1, high, r1x, 0, over_x),
        (3, high, r1x, 1, over_x),
    )
    second = ((1, low, r2x, over_x), (2, high, r2y, over_y))

    def copy1(n, gz):
        c, part, buf, at, to = first[n]
        return remote(cut(mine.at[gz, c], part), buf.at[gz, at], s1.at[n, gz], w1.at[n, gz], (g, to))

    def copy2(n, gz):
        c, part, buf, to = second[n]
        return remote(cut(mine.at[gz, c], part), buf.at[gz], s2.at[n, gz], w2.at[n, gz], (g, to))

    def line(gz, up):
        to = g + 1 if up else g - 1
        buf = ru if up else rd
        return remote(mine.at[gz, 0], buf.at[gz], sz.at[gz], wz.at[gz, int(up)], (to, d))

    def stage0(t):
        gz = order(t)
        for c in (3, 2, 1, 0):
            pltpu.make_async_copy(region(gz, columns[c]), mine.at[gz, c], load.at[gz, c]).wait()
            arrived(r0.at[gz, c], w0.at[gz, c])
            add(mine.at[gz, c], r0.at[gz, c], count)
            if c == 3:
                copy1(1, gz).start()
                copy1(3, gz).start()
            if c == 2:
                copy1(0, gz).start()
            if c == 1:
                copy1(2, gz).start()

    def stage1(t):
        gz = order(t)
        arrived(r1y.at[gz, 1], w1.at[1, gz])
        add(cut(mine.at[gz, 1], low), r1y.at[gz, 1], half)
        copy2(0, gz).start()
        arrived(r1x.at[gz, 1], w1.at[3, gz])
        add(cut(mine.at[gz, 2], high), r1x.at[gz, 1], rest)
        copy2(1, gz).start()
        arrived(r1y.at[gz, 0], w1.at[0, gz])
        add(cut(mine.at[gz, 0], low), r1y.at[gz, 0], half)
        arrived(r1x.at[gz, 0], w1.at[2, gz])
        add(cut(mine.at[gz, 0], high), r1x.at[gz, 0], rest)

    def stage2(t):
        gz = order(t)
        arrived(r2x.at[gz], w2.at[0, gz])
        add(cut(mine.at[gz, 0], low), r2x.at[gz], half)
        arrived(r2y.at[gz], w2.at[1, gz])
        add(cut(mine.at[gz, 0], high), r2y.at[gz], rest)
        if t == ng - 1:
            return

        @pl.when(gz > g)
        def _():
            @pl.when(g > 0)
            def _():
                arrived(ru.at[gz], wz.at[gz, 1])
                add(mine.at[gz, 0], ru.at[gz], count)
            line(gz, True).start()

        @pl.when(gz < g)
        def _():
            @pl.when(g < ng - 1)
            def _():
                arrived(rd.at[gz], wz.at[gz, 0])
                add(mine.at[gz, 0], rd.at[gz], count)
            line(gz, False).start()

    def vec_step(n):
        arrived(vxy.at[n], vw.at[n])
        total = vwork[n] + vxy[n]
        if n < 2:
            vwork[n + 1] = total
            vec_copy(n + 1).start()
        else:
            vz[g] = total

    def vec_line(gz, up):
        to = g + 1 if up else g - 1
        return remote(vz.at[gz], vz.at[gz], vs.at[3 + 2 * gz + int(up)], vw.at[3 + gz], (to, d))

    stage0(0)
    vec_step(0)
    stage0(1)
    vec_step(1)
    stage1(0)
    for t in range(2, ng):
        stage0(t)
        stage1(t - 1)
        stage2(t - 2)
        if t == 2:
            vec_step(2)

            @pl.when(g < ng - 1)
            def _():
                vec_line(g, True).start()

            @pl.when(g > 0)
            def _():
                vec_line(g, False).start()
    stage1(ng - 1)
    for n in range(1, ng):
        gz = near_order(n, g, ng)
        arrived(vz.at[gz], vw.at[3 + gz])

        @pl.when((gz < g) & (g < ng - 1))
        def _():
            vec_line(gz, True).start()

        @pl.when((gz > g) & (g > 0))
        def _():
            vec_line(gz, False).start()
    stage2(ng - 2)
    stage2(ng - 1)

    total = vz[0]
    for z in range(1, ng):
        total = total + vz[z]
    vout_ref[...] = total

    @pl.when(g > 0)
    def _():
        arrived(ru.at[g], wz.at[g, 1])

    @pl.when(g < ng - 1)
    def _():
        arrived(rd.at[g], wz.at[g, 0])

    @pl.loop(0, count)
    def _(i):
        out_ref[i] = mine[g, 0, i].astype(F32)

    @pl.when(g > 0)
    def _():
        @pl.loop(0, count)
        def _(i):
            out_ref[i] += ru[g, i].astype(F32)

    @pl.when(g < ng - 1)
    def _():
        @pl.loop(0, count)
        def _(i):
            out_ref[i] += rd[g, i].astype(F32)

    for t in range(ng):
        gz = order(t)
        for c in range(4):
            to_sibling(gz, c).wait_send()
        for n in range(4):
            copy1(n, gz).wait_send()
        for n in range(2):
            copy2(n, gz).wait_send()
        if t < ng - 1:
            arrived(mine.at[gz, 0], sz.at[gz])
    for n in range(3):
        vec_copy(n).wait_send()
    for n in range(ng):
        gz = near_order(n, g, ng)

        @pl.when((gz <= g) & (g < ng - 1))
        def _():
            vec_line(gz, True).wait_send()

        @pl.when((gz >= g) & (g > 0))
        def _():
            vec_line(gz, False).wait_send()


def run_scatter(grads, vec, ng, nd):
    blocks, side, _ = grads.shape
    count = blocks // (ng * nd)
    half = count // 2
    dma = pltpu.SemaphoreType.DMA

    def buf(*lead):
        return pltpu.VMEM(lead + (side, side), BF16)

    return pl.pallas_call(
        functools.partial(scatter_kernel, ng=ng, nd=nd),
        out_shape=(sds((count, side, side), F32), sds(vec.shape, F32)),
        in_specs=[hbm(), vmem()],
        out_specs=(vmem(), vmem()),
        scratch_shapes=[
            buf(ng, 4, count),
            buf(ng, 4, count),
            buf(ng, 2, half),
            buf(ng, 2, count - half),
            buf(ng, half),
            buf(ng, count - half),
            buf(ng, count),
            buf(ng, count),
            pltpu.VMEM((3,) + vec.shape, F32),
            pltpu.VMEM((3,) + vec.shape, F32),
            pltpu.VMEM((ng,) + vec.shape, F32),
            dma((ng, 4)),
            dma((ng, 4)),
            dma((ng, 4)),
            dma((4, ng)),
            dma((4, ng)),
            dma((2, ng)),
            dma((2, ng)),
            dma((ng,)),
            dma((ng, 2)),
            dma((3 + 2 * ng,)),
            dma((3 + ng,)),
        ],
        compiler_params=params(collective_id=1, has_side_effects=True),
        name="scatter",
    )(grads, vec)


def local(
    inputs,
    cotangent,
    weight_slots,
    slot_block,
    left_stats,
    right_stats,
    left_roots,
    right_roots,
    vectors,
    span_start,
):
    seq_count, tok_count, width = inputs.shape
    rows = seq_count * tok_count
    nd = lax.axis_size("dev")
    ng = lax.axis_size("grp")
    side = weight_slots.shape[1]
    hpd = H // nd
    lanes = width // nd
    head = lax.axis_index("dev") * hpd + jnp.arange(hpd, dtype=jnp.int32)
    slopes = jnp.exp2(-8.0 * (head.astype(F32) + 1.0) / H)
    slot_of = invert_order(slot_block)
    vec = vectors.reshape(-1, width)
    x = inputs.reshape(rows, width)
    dy = cotangent.reshape(rows, width)

    direct = nd == 8
    if direct:
        gath = run_gather(weight_slots, ng, nd)
    else:
        gath = lax.all_gather(weight_slots.astype(BF16), ("grp", "dev"), axis=0, tiled=True)
    h1, qkv = run_qkv(slot_of, x, vec, gath, nd)
    qkv, o, o32, lse = run_attn_fwd(
        span_start, slopes, qkv.reshape(nd, 3, seq_count, tok_count, lanes), hpd
    )
    act, att, h2, g, dz, da, dx1, do, sums2 = run_mlp(
        slot_of, o.reshape(nd, rows, lanes), x, dy, vec, gath, nd
    )
    do = do.reshape(nd, seq_count, tok_count, lanes)
    dqkv = run_attn_bwd(span_start, slopes, qkv, do, o32, lse, hpd).reshape(nd, 3, rows, lanes)
    ig, cat, sums1 = run_dh1(slot_of, dqkv, x, dx1, vec, gath, nd)
    grads = run_wgrad(slot_of, h1, att, h2, g, cat, da, dz, dy, side)

    s2 = jnp.sum(sums2.reshape(-1, 8, width), axis=1)
    s1 = jnp.sum(sums1.reshape(-1, 8, width), axis=1)
    bo, gain2, shift2, bdown = [s2[n:n + 1] for n in range(4)]
    gain1, shift1, bq, bv = [s1[n:n + 1] for n in range(4)]
    local_vector = jnp.concatenate(
        [gain1, shift1, bq, bv, bo, gain2, shift2, bdown, s2[4:]], axis=0
    )
    if direct:
        weight_grads, vector_grads = run_scatter(grads, local_vector, ng, nd)
        vector_grads = vector_grads.reshape(-1)
    else:
        vector_grads = lax.psum(local_vector.reshape(-1), ("grp", "dev"))
        weight_grads = lax.psum_scatter(grads, ("grp", "dev"), scatter_dimension=0, tiled=True)
        weight_grads = weight_grads.astype(F32)
    tokens_all = rows * nd * ng
    new_vectors = vectors - vector_rate / math.sqrt(tokens_all) * vector_grads

    new_left = 0.5 * left_stats + 0.5 * jnp.einsum(
        "bij,bkj->bik", weight_grads, weight_grads, precision=highest
    )
    new_right = 0.5 * right_stats + 0.5 * jnp.einsum(
        "bji,bjk->bik", weight_grads, weight_grads, precision=highest
    )
    shaped = jnp.einsum("bij,bjk->bik", left_roots, weight_grads, precision=highest)
    shaped = jnp.einsum("bij,bjk->bik", shaped, right_roots, precision=highest)
    new_weights = weight_slots - weight_rate * shaped
    return (
        act.reshape(inputs.shape),
        ig.reshape(inputs.shape),
        weight_grads,
        new_left,
        new_right,
        new_weights,
        vector_grads,
        new_vectors,
    )


def solution(mesh):
    return jax.shard_map(
        local,
        mesh=mesh,
        in_specs=(
            P("grp", "dev", None),
            P("grp", "dev", None),
            P(("grp", "dev"), None, None),
            P(),
            P(("grp", "dev"), None, None),
            P(("grp", "dev"), None, None),
            P(("grp", "dev"), None, None),
            P(("grp", "dev"), None, None),
            P(),
            P("grp"),
        ),
        out_specs=(
            P("grp", "dev", None),
            P("grp", "dev", None),
            P(("grp", "dev"), None, None),
            P(("grp", "dev"), None, None),
            P(("grp", "dev"), None, None),
            P(("grp", "dev"), None, None),
            P(),
            P(),
        ),
        check_vma=False,
    )
```

```python
import functools
import math

import jax
import jax.numpy as jnp
from jax import lax
from jax.experimental import pallas as pl
from jax.experimental.pallas import tpu as pltpu
from jax.sharding import PartitionSpec as P

H = 16
FF = 4096
PIC = 256

eps = 1e-05
weight_rate = 0.5
vector_rate = 0.5
big_negative = -1e30
highest = lax.Precision.HIGHEST
F32 = jnp.float32
BF16 = jnp.bfloat16
LOG2E = 1.4426950408889634
MIB = 1024 * 1024

GAIN1, SHIFT1, BQ, BV, BO, GAIN2, SHIFT2, BDOWN, BUP = range(9)


def dot_nn(a, b):
    return lax.dot_general(a, b, (((1,), (0,)), ((), ())), preferred_element_type=F32)


def dot_nt(a, b):
    return lax.dot_general(a, b, (((1,), (1,)), ((), ())), preferred_element_type=F32)


def invert_order(slot_block):
    places = jnp.arange(slot_block.shape[0], dtype=jnp.int32)
    matches = (slot_block[None, :] == places[:, None]).astype(jnp.int32)
    return jnp.sum(matches * places[None, :], axis=1)


def vmem():
    return pl.BlockSpec(memory_space=pltpu.VMEM)


def smem():
    return pl.BlockSpec(memory_space=pltpu.SMEM)


def hbm():
    return pl.BlockSpec(memory_space=pl.ANY)


def sds(shape, dtype):
    return jax.ShapeDtypeStruct(shape, dtype)


def params(mib=58, **kw):
    return pltpu.CompilerParams(vmem_limit_bytes=mib * MIB, **kw)


def layer_stats(v):
    middle = jnp.mean(v, axis=-1, keepdims=True)
    centred = v - middle
    spread = jnp.mean(centred * centred, axis=-1, keepdims=True)
    return centred, lax.rsqrt(spread + eps)


def fold_rows(v):
    return jnp.sum(v.reshape(v.shape[0] // 8, 8, v.shape[1]), axis=0)


def fetch_block(gath, slot, dst, row, col, sem, side):
    return pltpu.make_async_copy(
        gath.at[slot], dst.at[pl.ds(row, side), pl.ds(col, side)], sem
    )


def qkv_kernel(slot_ref, x_ref, vec_ref, gath, h1_ref, out_ref, wbuf, sems, *, nd):
    rows, width = x_ref.shape
    side = gath.shape[1]
    per = width // side
    lanes = out_ref.shape[3]
    for part in range(3):
        @pl.loop(0, per)
        def _(i):
            for j in range(per):
                slot = slot_ref[i * 3 * per + part * per + j]
                fetch_block(gath, slot, wbuf.at[part], pl.multiple_of(i * side, side), j * side, sems.at[part], side).start()

    chunk = 32
    gain = vec_ref[GAIN1:GAIN1 + 1, :]
    shift = vec_ref[SHIFT1:SHIFT1 + 1, :]

    @pl.loop(0, rows // chunk)
    def _(r):
        at = pl.ds(pl.multiple_of(r * chunk, chunk), chunk)
        centred, inv = layer_stats(x_ref[at, :].astype(F32))
        h1_ref[at, :] = (centred * inv * gain + shift).astype(BF16)

    for part in range(3):
        pltpu.make_async_copy(wbuf.at[part], wbuf.at[part], sems.at[part]).wait()
        for half in range(2):
            cols = slice(half * width // 2, (half + 1) * width // 2)
            res = dot_nn(h1_ref[...], wbuf[part, :, cols])
            if part == 0:
                res = res + vec_ref[BQ:BQ + 1, cols]
            if part == 2:
                res = res + vec_ref[BV:BV + 1, cols]
            res = res.astype(BF16)
            for d in range(nd // 2):
                out_ref[half * (nd // 2) + d, part, :, :] = res[:, d * lanes:(d + 1) * lanes]


def run_qkv(slot_of, x, vec, gath, nd):
    rows, width = x.shape
    lanes = width // nd
    return pl.pallas_call(
        functools.partial(qkv_kernel, nd=nd),
        out_shape=(sds((rows, width), BF16), sds((nd, 3, rows, lanes), BF16)),
        in_specs=[smem(), vmem(), vmem(), hbm()],
        out_specs=(vmem(), vmem()),
        scratch_shapes=[pltpu.VMEM((3, width, width), BF16), pltpu.SemaphoreType.DMA((3,))],
        compiler_params=params(),
        name="qkv",
    )(slot_of, x, vec, gath)


MESH = pl.DeviceIdType.MESH


def remote(src, dst, send, recv, device):
    return pltpu.make_async_remote_copy(
        src_ref=src, dst_ref=dst, send_sem=send, recv_sem=recv, device_id=device, device_id_type=MESH
    )


def arrived(ref, sem):
    pltpu.make_async_copy(ref, ref, sem).wait()


def cut(ref, first, size):
    return ref.at[pl.ds(first, size)]


def greet_plane(g, d, nd):
    barrier = pltpu.get_barrier_semaphore()
    for p in range(1, nd):
        pl.semaphore_signal(barrier, inc=1, device_id=(g, lax.rem(d + p, nd)), device_id_type=MESH)
    pl.semaphore_wait(barrier, nd - 1)


def parts3(v):
    hi = v.astype(BF16)
    mid = (v - hi.astype(F32)).astype(BF16)
    lo = (v - hi.astype(F32) - mid.astype(F32)).astype(BF16)
    return hi.astype(F32), mid.astype(F32), lo.astype(F32)


def own_lanes(h, shape, hpd, lanes):
    lane = lax.broadcasted_iota(jnp.int32, shape, 1)
    size = lanes // hpd
    return (lane >= h * size) & (lane < (h + 1) * size)


def place(values, base, tok, width):
    lane = lax.broadcasted_iota(jnp.int32, (tok, width), 1)
    out = jnp.zeros((tok, width), F32)
    for n, v in enumerate(values):
        out = jnp.where(lane == base + n, v, out)
    return out


def spare(h, hpd, lanes):
    return (lanes // hpd) * (1 - h) if hpd > 1 else 0


def q_columns(q, h, hpd, slope, extra):
    tok, lanes = q.shape
    scaled = q.astype(F32) * ((lanes // hpd) ** (-0.5) * LOG2E)
    hi = scaled.astype(BF16)
    low = scaled - hi.astype(F32)
    row = jnp.full((tok, 128), 0.0, F32)
    near = [row + p for p in parts3(jnp.full((tok, 128), slope, F32))]
    far = [row + p for p in parts3(jnp.full((tok, 128), slope * tok, F32))]
    columns = place(near + far + extra, spare(h, hpd, lanes), tok, 128)
    if hpd > 1:
        own = own_lanes(h, (tok, lanes), hpd, lanes)
        return jnp.concatenate(
            [jnp.where(own, hi.astype(F32), 0.0), jnp.where(own, low, columns)], axis=1
        ).astype(BF16)
    return jnp.concatenate([hi.astype(F32), low, columns], axis=1).astype(BF16)


def k_columns(k, h, j, hpd, extra):
    tok, lanes = k.shape
    u = lax.broadcasted_iota(jnp.int32, (tok, 128), 0).astype(F32)
    block = jnp.full((tok, 128), j, jnp.int32).astype(F32)
    columns = place([u] * 3 + [block] * 3 + [1.0] * extra, spare(h, hpd, lanes), tok, 128)
    wide = k.astype(F32)
    if hpd > 1:
        own = own_lanes(h, (tok, lanes), hpd, lanes)
        return jnp.concatenate([wide, jnp.where(own, wide, columns)], axis=1).astype(BF16)
    return jnp.concatenate([wide, wide, columns], axis=1).astype(BF16)


def far_side(slope, tok):
    u = lax.broadcasted_iota(jnp.int32, (tok, tok), 0)
    t = lax.broadcasted_iota(jnp.int32, (tok, tok), 1)
    after = u > t
    return (
        jnp.where(after, big_negative, 0.0),
        jnp.where(after, (2.0 * slope) * (t - u).astype(F32), 0.0),
    )


def attn_fwd_kernel(
    span_ref, slope_ref, src, got, o_got, o32_ref, lse_ref,
    qa, ka, vt, scores, corr, o_out, ss, sr, os, orr, loc, *, hpd, nd
):
    nb, _, seqs, tok, lanes = got.shape
    size = lanes // hpd
    t_all = nb * tok
    g = lax.axis_index("grp")
    d = lax.axis_index("dev")

    for q in range(seqs):
        pltpu.make_async_copy(src.at[d, :, q], got.at[d, :, q], loc.at[q]).start()
    greet_plane(g, d, nd)

    def send(q, p):
        to = lax.rem(d + p, nd)
        return remote(src.at[to, :, q], got.at[d, :, q], ss.at[q, p], sr.at[q, p], (g, to))

    for q in range(seqs):
        @pl.loop(1, nd)
        def _(p):
            send(q, p).start()

    def send_o(q, i, p):
        return remote(o_out.at[i, q], o_got.at[d, q], os.at[q, i], orr.at[q, p], (g, i))

    for h in range(hpd):
        mask, span = far_side(slope_ref[h] * LOG2E, tok)
        zero = jnp.zeros((tok, tok), F32)
        gone = jnp.full((tok, tok), big_negative, F32)
        for flag, table in enumerate((mask, span)):
            corr[h, 0, flag, 0:tok] = table
            corr[h, 0, flag, tok:] = gone
            corr[h, 1, flag, 0:tok] = zero
            corr[h, 1, flag, tok:] = table

    for q in range(seqs):
        pltpu.make_async_copy(src.at[d, :, q], got.at[d, :, q], loc.at[q]).wait()

        @pl.loop(1, nd)
        def _(p):
            arrived(got.at[lax.rem(d + nd - p, nd), :, q], sr.at[q, p])

        @pl.loop(0, nb)
        def _(j):
            at_j = pl.ds(pl.multiple_of(j * tok, tok), tok)
            vt[0:lanes, at_j] = got[j, 2, q].astype(F32).T.astype(BF16)
            for h in range(hpd):
                qa[h, j] = q_columns(got[j, 0, q], h, hpd, slope_ref[h] * LOG2E, [])
                ka[h, at_j, :] = k_columns(got[j, 1, q], h, j, hpd, 0)

        start = span_ref[q]
        pair = 2 * tok

        @pl.loop(0, nb)
        def _(i):
            flag = (start == i * tok).astype(jnp.int32)
            parity = lax.rem(i, 2)
            last = i // 2

            def at_pair(n):
                return pl.ds(pl.multiple_of(n * pair, pair), pair)

            def fold_max(v):
                return jnp.max(v.reshape(pair // 8, 8, tok), axis=0)

            def score(n, tops):
                new = []
                for h in range(hpd):
                    s = dot_nt(ka[h, at_pair(n), :], qa[h, i])
                    scores[h, at_pair(n), :] = s
                    new.append(jnp.maximum(tops[h], fold_max(s)))
                return tuple(new)

            tops = lax.fori_loop(
                0, last, score, tuple([jnp.full((8, tok), big_negative, F32)] * hpd)
            )
            top = []
            for h in range(hpd):
                s = dot_nt(ka[h, at_pair(last), :], qa[h, i]) + corr[h, parity, flag]
                scores[h, at_pair(last), :] = s
                top.append(jnp.max(jnp.maximum(tops[h], fold_max(s)), axis=0, keepdims=True))

            def weigh(n, state):
                new = []
                for h in range(hpd):
                    acc, total = state[h]
                    p = jnp.exp2(scores[h, at_pair(n), :] - top[h])
                    total = total + jnp.sum(p.reshape(pair // 8, 8, tok), axis=0)
                    acc = acc + dot_nn(vt[h * size:(h + 1) * size, at_pair(n)], p.astype(BF16))
                    new.append((acc, total))
                return tuple(new)

            state = lax.fori_loop(
                0,
                last + 1,
                weigh,
                tuple([(jnp.zeros((size, tok), F32), jnp.zeros((8, tok), F32))] * hpd),
            )
            outs = []
            logs = []
            for h in range(hpd):
                acc, total = state[h]
                total = jnp.sum(total, axis=0, keepdims=True)
                outs.append(acc / total)
                logs.append(jnp.broadcast_to(top[h] + jnp.log2(total), (128 // hpd, tok)))
            out = (jnp.concatenate(outs, axis=0) if hpd > 1 else outs[0]).T
            o32_ref[i, q] = out
            o_out[i, q] = out.astype(BF16)
            lse_ref[i, q] = (jnp.concatenate(logs, axis=0) if hpd > 1 else logs[0]).T

            @pl.when(i == d)
            def _():
                pltpu.make_async_copy(o_out.at[i, q], o_got.at[d, q], os.at[q, i]).start()

            @pl.when(i != d)
            def _():
                send_o(q, i, lax.rem(i - d + nd, nd)).start()

    for q in range(seqs):
        @pl.loop(1, nd)
        def _(p):
            arrived(o_got.at[lax.rem(d + nd - p, nd), q], orr.at[q, p])
            send(q, p).wait_send()

        @pl.loop(0, nd)
        def _(i):
            arrived(o_out.at[i, q], os.at[q, i])


def run_attn_fwd(span, slopes, qkv, hpd):
    nb, _, seqs, tok, lanes = qkv.shape
    t = nb * tok
    dma = pltpu.SemaphoreType.DMA
    return pl.pallas_call(
        functools.partial(attn_fwd_kernel, hpd=hpd, nd=nb),
        out_shape=(
            sds(qkv.shape, BF16),
            sds((nb, seqs, tok, lanes), BF16),
            sds((nb, seqs, tok, lanes), F32),
            sds((nb, seqs, tok, 128), F32),
        ),
        in_specs=[smem(), smem(), hbm()],
        out_specs=(vmem(), vmem(), vmem(), vmem()),
        scratch_shapes=[
            pltpu.VMEM((hpd, nb, tok, 256), BF16),
            pltpu.VMEM((hpd, t, 256), BF16),
            pltpu.VMEM((lanes, t), BF16),
            pltpu.VMEM((hpd, t, tok), F32),
            pltpu.VMEM((hpd, 2, 2, 2 * tok, tok), F32),
            pltpu.VMEM((nb, seqs, tok, lanes), BF16),
            dma((seqs, nb)),
            dma((seqs, nb)),
            dma((seqs, nb)),
            dma((seqs, nb)),
            dma((seqs,)),
        ],
        compiler_params=params(collective_id=2, has_side_effects=True),
        name="attn_fwd",
    )(span, slopes, qkv)


def attn_bwd_kernel(
    span_ref, slope_ref, qkv_ref, do_src, o32_ref, lse_ref, got,
    do_got, out, qa, ka, kt, va, qm, da, dm, dqt, corr, ss, sr, gs, gr, loc, *, hpd, nd
):
    nb, _, seqs, tok, lanes = qkv_ref.shape
    size = lanes // hpd
    unit = size ** (-0.5)
    g = lax.axis_index("grp")
    d = lax.axis_index("dev")

    def own_copy(q):
        return pltpu.make_async_copy(do_src.at[d, q], do_got.at[d, q], loc.at[q])

    for q in range(seqs):
        own_copy(q).start()
    greet_plane(g, d, nd)

    def send(q, p):
        to = lax.rem(d + p, nd)
        return remote(do_src.at[to, q], do_got.at[d, q], ss.at[q, p], sr.at[q, p], (g, to))

    for q in range(seqs):
        @pl.loop(1, nd)
        def _(p):
            send(q, p).start()

    def back(q, kind, p):
        to = lax.rem(d + p, nd)
        at = pl.ds(kind, 1 + kind)
        return remote(
            out.at[to, at, q], got.at[d, at, q], gs.at[q, kind, p], gr.at[q, kind, p], (g, to)
        )

    def back_own(q, kind):
        at = pl.ds(kind, 1 + kind)
        return pltpu.make_async_copy(out.at[d, at, q], got.at[d, at, q], gs.at[q, kind, 0])

    for h in range(hpd):
        mask, span = far_side(slope_ref[h] * LOG2E, tok)
        corr[h, 0] = mask
        corr[h, 1] = span

    for q in range(seqs):
        @pl.loop(0, nb)
        def _(j):
            at_j = pl.ds(pl.multiple_of(j * tok, tok), tok)
            qj = qkv_ref[j, 0, q]
            kj = qkv_ref[j, 1, q]
            vj = qkv_ref[j, 2, q].astype(F32)
            kt[:, at_j] = kj.astype(F32).T.astype(BF16)
            dqt[:, at_j] = jnp.zeros((lanes, tok), F32)
            for h in range(hpd):
                low = lse_ref[j, q][:, h * (128 // hpd):h * (128 // hpd) + 1]
                extra = [-p for p in parts3(low)]
                qa[h, j] = q_columns(qj, h, hpd, slope_ref[h] * LOG2E, extra)
                ka[h, j] = k_columns(kj, h, j, hpd, 3)
                if hpd > 1:
                    own = own_lanes(h, (tok, lanes), hpd, lanes)
                    qm[h, j] = jnp.where(own, qj.astype(F32), 0.0).astype(BF16)
                    va[h, j] = jnp.where(
                        own, vj, place([1.0] * 3, spare(h, hpd, lanes), tok, lanes)
                    ).astype(BF16)
                else:
                    qm[h, j] = qj
                    va[h, j] = jnp.concatenate(
                        [vj, place([1.0] * 3, 0, tok, lanes)], axis=1
                    ).astype(BF16)

        own_copy(q).wait()

        @pl.loop(1, nd)
        def _(p):
            arrived(do_got.at[lax.rem(d + nd - p, nd), q], sr.at[q, p])

        @pl.loop(0, nb)
        def _(j):
            do = do_got[j, q].astype(F32)
            prod = do * o32_ref[j, q]
            for h in range(hpd):
                if hpd > 1:
                    own = own_lanes(h, (tok, lanes), hpd, lanes)
                    delta = jnp.sum(jnp.where(own, prod, 0.0), axis=1, keepdims=True)
                    extra = place([-p for p in parts3(delta)], spare(h, hpd, lanes), tok, lanes)
                    da[h, j] = jnp.where(own, do, extra).astype(BF16)
                    dm[h, j] = jnp.where(own, do, 0.0).astype(BF16)
                else:
                    delta = jnp.sum(prod, axis=1, keepdims=True)
                    extra = place([-p for p in parts3(delta)], 0, tok, lanes)
                    da[h, j] = jnp.concatenate([do, extra], axis=1).astype(BF16)
                    dm[h, j] = do.astype(BF16)

        start = span_ref[q]

        @pl.loop(0, nb)
        def _(n):
            j = lax.rem(d + n, nb)
            at_j = pl.ds(pl.multiple_of(j * tok, tok), tok)
            flag = (start == j * tok).astype(jnp.int32)

            def tile(i, h, dk, dv, near):
                at_i = pl.ds(pl.multiple_of(i * tok, tok), tok)
                s = dot_nt(ka[h, j], qa[h, i])
                if near:
                    s = s + corr[h, flag]
                p = jnp.exp2(s)
                ds = (p * dot_nt(va[h, j], da[h, i])).astype(BF16)
                dv = dv + dot_nn(p.astype(BF16), dm[h, i])
                dk = dk + dot_nn(ds, qm[h, i])
                rows = slice(h * size, (h + 1) * size)
                dqt[rows, at_i] += dot_nn(kt[rows, at_j], ds)
                return dk, dv

            dk = jnp.zeros((tok, lanes), F32)
            dv = jnp.zeros((tok, lanes), F32)
            for h in range(hpd):
                dk, dv = tile(j, h, dk, dv, True)

            def body(i, carry):
                dk, dv = carry
                for h in range(hpd):
                    dk, dv = tile(i, h, dk, dv, False)
                return dk, dv

            dk, dv = lax.fori_loop(j + 1, nb, body, (dk, dv))
            out[j, 1, q] = (dk * unit).astype(BF16)
            out[j, 2, q] = dv.astype(BF16)

            @pl.when(n == 0)
            def _():
                back_own(q, 1).start()

            @pl.when(n > 0)
            def _():
                back(q, 1, n).start()

        @pl.loop(0, nb)
        def _(n):
            j = lax.rem(d + n, nb)
            at_j = pl.ds(pl.multiple_of(j * tok, tok), tok)
            out[j, 0, q] = (dqt[:, at_j].T * unit).astype(BF16)

            @pl.when(n == 0)
            def _():
                back_own(q, 0).start()

            @pl.when(n > 0)
            def _():
                back(q, 0, n).start()

    for q in range(seqs):
        for kind in range(2):
            back_own(q, kind).wait()

        @pl.loop(1, nd)
        def _(p):
            send(q, p).wait_send()
            source = lax.rem(d + nd - p, nd)
            for kind in range(2):
                back(q, kind, p).wait_send()
                arrived(got.at[source, pl.ds(kind, 1 + kind), q], gr.at[q, kind, p])


def run_attn_bwd(span, slopes, qkv, do, o32, lse, hpd):
    nb, _, seqs, tok, lanes = qkv.shape
    t = nb * tok
    dma = pltpu.SemaphoreType.DMA
    wide = 128 if hpd == 1 else lanes
    return pl.pallas_call(
        functools.partial(attn_bwd_kernel, hpd=hpd, nd=nb),
        out_shape=sds(qkv.shape, BF16),
        in_specs=[smem(), smem(), vmem(), hbm(), vmem(), vmem()],
        out_specs=vmem(),
        scratch_shapes=[
            pltpu.VMEM((nb, seqs, tok, lanes), BF16),
            pltpu.VMEM(qkv.shape, BF16),
            pltpu.VMEM((hpd, nb, tok, 256), BF16),
            pltpu.VMEM((hpd, nb, tok, 256), BF16),
            pltpu.VMEM((lanes, t), BF16),
            pltpu.VMEM((hpd, nb, tok, wide), BF16),
            pltpu.VMEM((hpd, nb, tok, lanes), BF16),
            pltpu.VMEM((hpd, nb, tok, wide), BF16),
            pltpu.VMEM((hpd, nb, tok, lanes), BF16),
            pltpu.VMEM((lanes, t), F32),
            pltpu.VMEM((hpd, 2, tok, tok), F32),
            dma((seqs, nb)),
            dma((seqs, nb)),
            dma((seqs, 2, nb)),
            dma((seqs, 2, nb)),
            dma((seqs,)),
        ],
        compiler_params=params(collective_id=3, has_side_effects=True),
        name="attn_bwd",
    )(span, slopes, qkv, do, o32, lse)


def mlp_kernel(
    slot_ref, o_ref, x_ref, dy_ref, vec_ref, gath,
    act_ref, att_ref, h2_ref, g_ref, dz_ref, da_ref, dx1_ref, do_ref, sums_ref,
    wo, wup, wdn, x1, acc, dh2, sem_o, sem_t, *, nd, first_o, first_up, first_dn, tile
):
    rows, width = x_ref.shape
    side = gath.shape[1]
    per = width // side
    ff = g_ref.shape[1]
    tiles = ff // tile
    cols = tile // side
    lanes = o_ref.shape[2]
    fper = ff // side

    @pl.loop(0, per)
    def _(i):
        for j in range(per):
            fetch_block(gath, slot_ref[first_o + i * per + j], wo, pl.multiple_of(i * side, side), j * side, sem_o.at[0], side).start()

    def fetch_tile(f):
        @pl.loop(0, per)
        def _(i):
            for j in range(cols):
                fetch_block(gath, slot_ref[first_up + i * fper + f * cols + j], wup.at[f], pl.multiple_of(i * side, side), j * side, sem_t.at[f], side).start()
            for j in range(cols):
                fetch_block(gath, slot_ref[first_dn + (f * cols + j) * per + i], wdn.at[f], j * side, pl.multiple_of(i * side, side), sem_t.at[f], side).start()

    fetch_tile(0)
    fetch_tile(1)
    for d in range(nd):
        att_ref[:, d * lanes:(d + 1) * lanes] = o_ref[d]
    pltpu.make_async_copy(wo, wo, sem_o.at[0]).wait()
    for half in range(2):
        c = slice(half * width // 2, (half + 1) * width // 2)
        x1[:, c] = x_ref[:, c].astype(F32) + dot_nn(att_ref[...], wo[:, c]) + vec_ref[BO:BO + 1, c]

    chunk = 32

    def rows_at(r):
        return pl.ds(pl.multiple_of(r * chunk, chunk), chunk)

    @pl.loop(0, rows // chunk)
    def _(r):
        at = rows_at(r)
        centred, inv = layer_stats(x1[at, :])
        h2_ref[at, :] = (centred * inv * vec_ref[GAIN2:GAIN2 + 1, :] + vec_ref[SHIFT2:SHIFT2 + 1, :]).astype(BF16)
        acc[at, :] = x1[at, :] + vec_ref[BDOWN:BDOWN + 1, :]
        dh2[at, :] = jnp.zeros((chunk, width), F32)

    @pl.loop(0, tiles)
    def _(f):
        @pl.when(f + 2 < tiles)
        def _():
            fetch_tile(f + 2)
        pltpu.make_async_copy(wup.at[f], wup.at[f], sem_t.at[f]).wait()
        pltpu.make_async_copy(wdn.at[f], wdn.at[f], sem_t.at[f]).wait()
        per_row = width // tile
        bias = vec_ref[pl.ds(BUP + f // per_row, 1), pl.ds(pl.multiple_of((f % per_row) * tile, tile), tile)]
        at_f = pl.ds(pl.multiple_of(f * tile, tile), tile)
        z = dot_nn(h2_ref[...], wup[f]) + bias
        dg = dot_nt(dy_ref[...], wdn[f])
        z2 = z * z
        th = jnp.tanh(0.7978845608028654 * (z + 0.044715 * z2 * z))
        g = (0.5 * z * (1.0 + th)).astype(BF16)
        slope = 0.5 * (1.0 + th) + 0.5 * z * (1.0 - th * th) * (
            0.7978845608028654 * (1.0 + 3.0 * 0.044715 * z2)
        )
        dz = (dg * slope).astype(BF16)
        g_ref[:, at_f] = g
        dz_ref[:, at_f] = dz
        sums_ref[pl.ds(pl.multiple_of(8 * (4 + f // per_row), 8), 8), pl.ds(pl.multiple_of((f % per_row) * tile, tile), tile)] = fold_rows(dz.astype(F32))
        acc[...] += dot_nn(g, wdn[f])
        dh2[...] += dot_nt(dz, wup[f])

    zero = jnp.zeros((8, width), F32)

    def finish(r, carry):
        s_bo, s_gain, s_shift, s_bdown = carry
        at = rows_at(r)
        act_ref[at, :] = acc[at, :].astype(BF16)
        centred, inv = layer_stats(x1[at, :])
        hat = centred * inv
        dh = dh2[at, :]
        dhg = dh * vec_ref[GAIN2:GAIN2 + 1, :]
        back = inv * (
            dhg
            - jnp.mean(dhg, axis=-1, keepdims=True)
            - hat * jnp.mean(dhg * hat, axis=-1, keepdims=True)
        )
        dy = dy_ref[at, :].astype(F32)
        dx1 = dy + back
        dx1_ref[at, :] = dx1
        da = dx1.astype(BF16)
        da_ref[at, :] = da
        return (
            s_bo + fold_rows(da.astype(F32)),
            s_gain + fold_rows(dh * hat),
            s_shift + fold_rows(dh),
            s_bdown + fold_rows(dy),
        )

    carry = lax.fori_loop(0, rows // chunk, finish, (zero, zero, zero, zero))
    for n in range(4):
        sums_ref[8 * n:8 * n + 8, :] = carry[n]
    for half in range(2):
        c = slice(half * width // 2, (half + 1) * width // 2)
        res = dot_nt(da_ref[...], wo[c, :]).astype(BF16)
        for d in range(nd // 2):
            do_ref[half * (nd // 2) + d] = res[:, d * lanes:(d + 1) * lanes]


def run_mlp(slot_of, o, x, dy, vec, gath, nd):
    rows, width = x.shape
    side = gath.shape[1]
    lanes = width // nd
    per = width // side
    first_o = 3 * per * per
    first_up = first_o + per * per
    first_dn = first_up + per * (FF // side)
    tile = 512
    return pl.pallas_call(
        functools.partial(
            mlp_kernel, nd=nd, first_o=first_o, first_up=first_up, first_dn=first_dn, tile=tile
        ),
        out_shape=(
            sds((rows, width), BF16),
            sds((rows, width), BF16),
            sds((rows, width), BF16),
            sds((rows, FF), BF16),
            sds((rows, FF), BF16),
            sds((rows, width), BF16),
            sds((rows, width), F32),
            sds((nd, rows, lanes), BF16),
            sds((8 * (4 + FF // width), width), F32),
        ),
        in_specs=[smem(), vmem(), vmem(), vmem(), vmem(), hbm()],
        out_specs=tuple([vmem()] * 9),
        scratch_shapes=[
            pltpu.VMEM((width, width), BF16),
            pltpu.VMEM((FF // tile, width, tile), BF16),
            pltpu.VMEM((FF // tile, tile, width), BF16),
            pltpu.VMEM((rows, width), F32),
            pltpu.VMEM((rows, width), F32),
            pltpu.VMEM((rows, width), F32),
            pltpu.SemaphoreType.DMA((1,)),
            pltpu.SemaphoreType.DMA((FF // tile,)),
        ],
        compiler_params=params(),
        name="mlp",
    )(slot_of, o, x, dy, vec, gath)


def dh1_kernel(
    slot_ref, dqkv_ref, x_ref, dx1_ref, vec_ref, gath, ig_ref, cat_ref, sums_ref,
    wbuf, dh1, sems, *, nd
):
    rows, width = x_ref.shape
    side = gath.shape[1]
    per = width // side
    lanes = dqkv_ref.shape[3]
    for part in range(3):
        @pl.loop(0, per)
        def _(i):
            for j in range(per):
                slot = slot_ref[i * 3 * per + part * per + j]
                fetch_block(gath, slot, wbuf.at[part], pl.multiple_of(i * side, side), j * side, sems.at[part], side).start()

    for part in range(3):
        for d in range(nd):
            at = part * width + d * lanes
            cat_ref[:, at:at + lanes] = dqkv_ref[d, part]
    for part in range(3):
        pltpu.make_async_copy(wbuf.at[part], wbuf.at[part], sems.at[part]).wait()
        for half in range(2):
            c = slice(half * width // 2, (half + 1) * width // 2)
            res = dot_nt(cat_ref[:, part * width:(part + 1) * width], wbuf[part, c, :])
            if part == 0:
                dh1[:, c] = res
            else:
                dh1[:, c] += res

    chunk = 32
    zero = jnp.zeros((8, width), F32)

    def finish(r, carry):
        s_gain, s_shift, s_bq, s_bv = carry
        at = pl.ds(pl.multiple_of(r * chunk, chunk), chunk)
        centred, inv = layer_stats(x_ref[at, :].astype(F32))
        hat = centred * inv
        dh = dh1[at, :]
        dhg = dh * vec_ref[GAIN1:GAIN1 + 1, :]
        back = inv * (
            dhg
            - jnp.mean(dhg, axis=-1, keepdims=True)
            - hat * jnp.mean(dhg * hat, axis=-1, keepdims=True)
        )
        ig_ref[at, :] = dx1_ref[at, :] + back
        return (
            s_gain + fold_rows(dh * hat),
            s_shift + fold_rows(dh),
            s_bq + fold_rows(cat_ref[at, 0:width].astype(F32)),
            s_bv + fold_rows(cat_ref[at, 2 * width:3 * width].astype(F32)),
        )

    carry = lax.fori_loop(0, rows // chunk, finish, (zero, zero, zero, zero))
    for n in range(4):
        sums_ref[8 * n:8 * n + 8, :] = carry[n]


def run_dh1(slot_of, dqkv, x, dx1, vec, gath, nd):
    rows, width = x.shape
    return pl.pallas_call(
        functools.partial(dh1_kernel, nd=nd),
        out_shape=(
            sds((rows, width), F32),
            sds((rows, 3 * width), BF16),
            sds((32, width), F32),
        ),
        in_specs=[smem(), vmem(), vmem(), vmem(), vmem(), hbm()],
        out_specs=(vmem(), vmem(), vmem()),
        scratch_shapes=[
            pltpu.VMEM((3, width, width), BF16),
            pltpu.VMEM((rows, width), F32),
            pltpu.SemaphoreType.DMA((3,)),
        ],
        compiler_params=params(),
        name="dh1",
    )(slot_of, dqkv, x, dx1, vec, gath)


def wgrad_kernel(
    slot_ref, h1, att, h2, g, dqkv, da, dz, dy, out,
    v_a, v_b, a_t, stage, sem_in, sem_out, *, side, tile
):
    rows, width = h1.shape
    per = width // side
    cols = tile // side
    ff = g.shape[1]
    runs = [(h2, 0, dz, 4 * per * per, ff // side)]
    for c in range(ff // width):
        first = 4 * per * per + per * (ff // side) + c * per * per
        runs.append((g, c * width, dy, first, per))
    runs.append((att, 0, da, 3 * per * per, per))
    runs.append((h1, 0, dqkv, 0, 3 * per))

    def loads(n):
        a, at, b, _, _ = runs[n]
        copies = [pltpu.make_async_copy(a.at[:, pl.ds(at, width)], v_a.at[n % 2], sem_in.at[n % 2, 0])]
        fresh = n == 0 or runs[n - 1][2] is not b
        if fresh:
            wide = b.shape[1]
            copies.append(
                pltpu.make_async_copy(b, v_b.at[slot_b[n], :, pl.ds(0, wide)], sem_in.at[n % 2, 1])
            )
        return copies

    slot_b = []
    for n in range(len(runs)):
        if n == 0:
            slot_b.append(0)
        elif runs[n - 1][2] is runs[n][2]:
            slot_b.append(slot_b[-1])
        else:
            slot_b.append(1 - slot_b[-1])

    started = {0: loads(0)}
    for copy in started[0]:
        copy.start()
    count = 0

    def out_wait(slot):
        pltpu.make_async_copy(stage.at[slot], stage.at[slot], sem_out.at[slot]).wait()

    for n in range(len(runs)):
        _, _, b, first, stride = runs[n]
        if n + 1 < len(runs):
            started[n + 1] = loads(n + 1)
            for copy in started[n + 1]:
                copy.start()
        for copy in started[n]:
            copy.wait()
        for r in range(width // 256):
            c = slice(r * 256, (r + 1) * 256)
            a_t[c, :] = v_a[n % 2, :, c].astype(F32).T.astype(BF16)
        sb = slot_b[n]
        base = count

        def step(t, base=base, first=first, stride=stride, sb=sb):
            slot = (base + t) % 2

            @pl.when(base + t >= 2)
            def _():
                out_wait(slot)
            res = dot_nn(a_t[...], v_b[sb, :, pl.ds(pl.multiple_of(t * tile, tile), tile)]).astype(BF16)
            for i in range(per):
                for j in range(cols):
                    stage[slot, i * cols + j] = res[i * side:(i + 1) * side, j * side:(j + 1) * side]
            for i in range(per):
                for j in range(cols):
                    dst = slot_ref[first + i * stride + t * cols + j]
                    pltpu.make_async_copy(stage.at[slot, i * cols + j], out.at[dst], sem_out.at[slot]).start()

        steps = b.shape[1] // tile
        pl.loop(0, steps)(step)
        count += steps
    out_wait(0)
    out_wait(1)


def run_wgrad(slot_of, h1, att, h2, g, dqkv, da, dz, dy, side):
    rows, width = h1.shape
    tile = 512
    blocks = slot_of.shape[0]
    return pl.pallas_call(
        functools.partial(wgrad_kernel, side=side, tile=tile),
        out_shape=sds((blocks, side, side), BF16),
        in_specs=[smem()] + [hbm()] * 8,
        out_specs=hbm(),
        scratch_shapes=[
            pltpu.VMEM((2, rows, width), BF16),
            pltpu.VMEM((2, rows, FF), BF16),
            pltpu.VMEM((width, rows), BF16),
            pltpu.VMEM((2, (width // side) * (tile // side), side, side), BF16),
            pltpu.SemaphoreType.DMA((2, 2)),
            pltpu.SemaphoreType.DMA((2,)),
        ],
        compiler_params=params(),
        name="wgrad",
    )(slot_of, h1, att, h2, g, dqkv, da, dz, dy)


def whereami():
    g = lax.axis_index("grp")
    d = lax.axis_index("dev")
    core = lax.rem(d, 2)
    x = lax.rem(d // 2, 2)
    y = d // 4
    over_x = d + 2 - 4 * x
    over_y = d + 4 - 8 * y
    across = over_x + 4 - 8 * y
    sibling = d + 1 - 2 * core
    return g, d, over_x, over_y, across, sibling


def near_order(t, g, ng):
    t = ng - 1 - t
    low = jnp.where(t < ng - 1 - g, ng - 1 - t, t - (ng - 1 - g))
    high = jnp.where(t < g, t, ng - 1 - (t - g))
    return jnp.where(2 * g < ng, low, high)


def greet(g, ng, peers):
    barrier = pltpu.get_barrier_semaphore()
    for peer in peers:
        pl.semaphore_signal(barrier, inc=1, device_id=(g, peer), device_id_type=MESH)

    d = lax.axis_index("dev")

    @pl.when(g > 0)
    def _():
        pl.semaphore_signal(barrier, inc=1, device_id=(g - 1, d), device_id_type=MESH)

    @pl.when(g < ng - 1)
    def _():
        pl.semaphore_signal(barrier, inc=1, device_id=(g + 1, d), device_id_type=MESH)

    ends = (g > 0).astype(jnp.int32) + (g < ng - 1).astype(jnp.int32)
    pl.semaphore_wait(barrier, len(peers) + ends)


def slot_cuts(count):
    third = 2 * (count // 12)
    first = (count - third) // 2
    return first, count - third - first, third // 2, third // 2


def gather_kernel(w_ref, out, own, local_sem, zs, zr, cs, cr, ss, sr, *, ng, nd):
    count = w_ref.shape[0]
    na, nb, nc1, nc2 = slot_cuts(count)
    flat = na + nb
    nc = nc1 + nc2
    g, d, over_x, over_y, across, sibling = whereami()
    columns = (d, over_x, over_y, across)
    own[...] = w_ref[...].astype(BF16)
    greet(g, ng, (over_x, over_y, sibling))

    def region(gz, dev, first=0, size=count):
        return out.at[pl.ds((gz * nd + dev) * count + first, size)]

    def wide(t):
        return count if t == 0 else flat

    def kind(n, t):
        return (
            (d, 0, wide(t), over_x),
            (d, 0, wide(t), over_y),
            (d, 0, wide(t), sibling),
            (over_x, 0, na, over_y),
            (over_y, na, nb, over_x),
            (over_x, 0, wide(t), sibling),
            (over_y, 0, wide(t), sibling),
            (across, 0, na, sibling),
            (across, na, nb, sibling),
            (over_x, flat, nc1, over_y),
            (over_y, flat + nc1, nc2, over_x),
            (across, flat, nc1, sibling),
            (across, flat + nc1, nc2, sibling),
            (d, flat, nc, sibling),
            (over_x, flat, nc, sibling),
            (over_y, flat, nc, sibling),
            (across, flat, nc, sibling),
        )[n]

    def kinds(t):
        return range(13) if t == 0 else tuple(range(9)) + tuple(range(13, 17))

    def plane(n, t, src=None):
        gz = near_order(t, g, ng)
        dev, first, size, to = kind(n, t)
        at = region(gz, dev, first, size)
        return remote(at if src is None else src, at, ss.at[n, gz], sr.at[n, gz], (g, to))

    def landed(n, t, dev):
        gz = near_order(t, g, ng)
        _, first, size, _ = kind(n, t)
        arrived(region(gz, dev, first, size), sr.at[n, gz])

    def line(gz, up, src=None):
        at = region(gz, d, 0, flat)
        to = g + 1 if up else g - 1
        return remote(at if src is None else src, at, zs.at[gz, int(up)], zr.at[gz], (to, d))

    def corner_line(gz, c, up, src=None):
        at = region(gz, columns[c], flat, nc)
        to = g + 1 if up else g - 1
        return remote(at if src is None else src, at, cs.at[gz, c, int(up)], cr.at[gz, c], (to, d))

    def both_ways(gz, make):
        @pl.when((gz <= g) & (g < ng - 1))
        def _():
            make(True)

        @pl.when((gz >= g) & (g > 0))
        def _():
            make(False)

    mine = pltpu.make_async_copy(own, region(g, d), local_sem.at[0])
    mine.start()

    def column(t):
        gz = near_order(t, g, ng)
        if t == 0:
            both_ways(gz, lambda up: line(gz, up, cut(own, 0, flat)).start())
            for n in range(3):
                plane(n, t, own).start()
            both_ways(gz, lambda up: corner_line(gz, 0, up, cut(own, flat, nc)).start())
            return
        arrived(region(gz, d, 0, flat), zr.at[gz])
        both_ways(gz, lambda up: line(gz, up).start())
        for n in range(3):
            plane(n, t).start()

    def sides(t):
        gz = near_order(t, g, ng)
        landed(0, t, over_x)
        plane(3, t).start()
        if t == 0:
            plane(9, t).start()
            both_ways(gz, lambda up: corner_line(gz, 1, up).start())
        plane(5, t).start()
        landed(1, t, over_y)
        plane(4, t).start()
        if t == 0:
            plane(10, t).start()
            both_ways(gz, lambda up: corner_line(gz, 2, up).start())
        plane(6, t).start()

    def corner(t):
        gz = near_order(t, g, ng)
        if t == 0:
            landed(9, t, across)
            landed(10, t, across)
            both_ways(gz, lambda up: corner_line(gz, 3, up).start())
            plane(11, t).start()
            plane(12, t).start()
        landed(3, t, across)
        plane(7, t).start()
        landed(4, t, across)
        plane(8, t).start()

    def far_corner(t):
        gz = near_order(t, g, ng)
        for c in range(4):
            arrived(region(gz, columns[c], flat, nc), cr.at[gz, c])
            both_ways(gz, lambda up: corner_line(gz, c, up).start())
            plane(13 + c, t).start()

    plan = [(t, f) for t in range(ng) for f in (0, 1, 2, 3) if t > 0 or f < 3]
    lag = {0: 0, 1: 1.5, 2: 2.6, 3: 2.2}
    for t, f in sorted(plan, key=lambda e: e[0] * 1.0 + lag[e[1]]):
        (column, sides, corner, far_corner)[f](t)

    for t in range(ng):
        for n in kinds(t):
            dev, _, _, to = kind(n, t)
            if to is sibling:
                landed(n, t, dev + sibling - d)
    mine.wait()
    for t in range(ng):
        gz = near_order(t, g, ng)
        for n in kinds(t):
            plane(n, t).wait_send()
        both_ways(gz, lambda up: line(gz, up).wait_send())
        for c in range(4):
            both_ways(gz, lambda up: corner_line(gz, c, up).wait_send())


def run_gather(w, ng, nd):
    count, side, _ = w.shape
    dma = pltpu.SemaphoreType.DMA
    return pl.pallas_call(
        functools.partial(gather_kernel, ng=ng, nd=nd),
        out_shape=sds((ng * nd * count, side, side), BF16),
        in_specs=[vmem()],
        out_specs=hbm(),
        scratch_shapes=[
            pltpu.VMEM((count, side, side), BF16),
            dma((1,)),
            dma((ng, 2)),
            dma((ng,)),
            dma((ng, 4, 2)),
            dma((ng, 4)),
            dma((17, ng)),
            dma((17, ng)),
        ],
        compiler_params=params(collective_id=0, has_side_effects=True),
        name="gather",
    )(w)


def add_blocks(dst, src, size):
    step = 4 if size % 4 == 0 else 2 if size % 2 == 0 else 1

    @pl.loop(0, size // step)
    def _(n):
        for k in range(step):
            dst[n * step + k] = dst[n * step + k] + src[n * step + k]


def scatter_kernel(
    grads, vec_ref, out_ref, vout_ref,
    mine, r0, r1y, r1x, r2x, r2y, rz, cz, cy, cx, cx2, cy2, vwork, vxy, vz,
    load, s0, w0, s1, w1, s2, w2, sz, wz, sc, wc, s3, w3, vs, vw, *, ng, nd
):
    count = out_ref.shape[0]
    na, nb, nc1, nc2 = slot_cuts(count)
    flat = na + nb
    nc = nc1 + nc2
    g, d, over_x, over_y, across, sibling = whereami()
    columns = (d, over_x, over_y, across)

    def region(gz, dev):
        return grads.at[pl.ds((gz * nd + dev) * count, count)]

    def order(t):
        return near_order(ng - 1 - t, g, ng)

    for t in range(ng):
        for c in range(4):
            pltpu.make_async_copy(region(order(t), columns[c]), mine.at[order(t), c], load.at[order(t), c]).start()
    vwork[0] = vec_ref[...]
    greet(g, ng, (over_x, over_y, sibling))

    def to_sibling(gz, c):
        return remote(
            region(gz, columns[c] + sibling - d), r0.at[gz, c], s0.at[gz, c], w0.at[gz, c], (g, sibling)
        )

    peers = (sibling, over_x, over_y)

    def vec_copy(n):
        return remote(vwork.at[n], vxy.at[n], vs.at[n], vw.at[n], (g, peers[n]))

    vec_copy(0).start()
    for t in range(ng):
        for c in (3, 2, 1, 0):
            to_sibling(order(t), c).start()

    first = (
        (2, 0, na, r1y, 0, over_y),
        (3, 0, na, r1y, 1, over_y),
        (1, na, nb, r1x, 0, over_x),
        (3, na, nb, r1x, 1, over_x),
    )
    second = ((1, 0, na, r2x, over_x), (2, na, nb, r2y, over_y))
    third = (
        (2, flat, nc1, cy.at[0], over_y),
        (3, flat, nc1, cy.at[1], over_y),
        (1, flat + nc1, nc2, cx.at[0], over_x),
        (3, flat + nc1, nc2, cx.at[1], over_x),
        (1, flat, nc1, cx2, over_x),
        (2, flat + nc1, nc2, cy2, over_y),
    )

    def copy1(n, gz):
        c, at, size, buf, place_at, to = first[n]
        return remote(cut(mine.at[gz, c], at, size), buf.at[gz, place_at], s1.at[n, gz], w1.at[n, gz], (g, to))

    def copy2(n, gz):
        c, at, size, buf, to = second[n]
        return remote(cut(mine.at[gz, c], at, size), buf.at[gz], s2.at[n, gz], w2.at[n, gz], (g, to))

    def copy3(n):
        c, at, size, buf, to = third[n]
        return remote(cut(mine.at[g, c], at, size), buf, s3.at[n], w3.at[n], (g, to))

    def flat_part(gz):
        return cut(mine.at[gz, 0], 0, flat)

    def corner_part(gz):
        return mine.at[gz, :, pl.ds(flat, nc)]

    def line(gz, part, buf, sends, waits, up):
        at = gz if up else jnp.where(gz < g - 1, gz, ng)
        to = g + 1 if up else g - 1
        return remote(part(gz), buf.at[at], sends.at[gz], waits.at[at], (to, d))

    def pass_on(gz, part, buf, sends, waits, gather):
        @pl.when(gz > g)
        def _():
            @pl.when(g > 0)
            def _():
                arrived(buf.at[gz], waits.at[gz])
                gather(gz)
            line(gz, part, buf, sends, waits, True).start()

        @pl.when(gz < g)
        def _():
            @pl.when(g < ng - 1)
            def _():
                arrived(buf.at[gz], waits.at[gz])
                gather(gz)
            line(gz, part, buf, sends, waits, False).start()

    def gather_flat(gz):
        add_blocks(flat_part(gz), rz.at[gz], flat)

    def gather_corner(at, gz):
        for c in range(4):
            add_blocks(cut(mine.at[gz, c], flat, nc), cz.at[at, c], nc)

    def sums0(t):
        gz = order(t)
        for c in (3, 2, 1, 0):
            pltpu.make_async_copy(region(gz, columns[c]), mine.at[gz, c], load.at[gz, c]).wait()
            arrived(r0.at[gz, c], w0.at[gz, c])
            add_blocks(mine.at[gz, c], r0.at[gz, c], count)
            if t < ng - 1:
                sends0(t, c)

    def sends0(t, c):
        gz = order(t)
        for n in {3: (1, 3), 2: (0,), 1: (2,), 0: ()}[c]:
            copy1(n, gz).start()

    def along0(t):
        pass_on(order(t), corner_part, cz, sc, wc, lambda gz: gather_corner(gz, gz))

    def stage1(t):
        gz = order(t)
        arrived(r1y.at[gz, 1], w1.at[1, gz])
        add_blocks(cut(mine.at[gz, 1], 0, na), r1y.at[gz, 1], na)
        copy2(0, gz).start()
        arrived(r1x.at[gz, 1], w1.at[3, gz])
        add_blocks(cut(mine.at[gz, 2], na, nb), r1x.at[gz, 1], nb)
        copy2(1, gz).start()
        arrived(r1y.at[gz, 0], w1.at[0, gz])
        add_blocks(cut(mine.at[gz, 0], 0, na), r1y.at[gz, 0], na)
        arrived(r1x.at[gz, 0], w1.at[2, gz])
        add_blocks(cut(mine.at[gz, 0], na, nb), r1x.at[gz, 0], nb)

    def stage2(t):
        gz = order(t)
        arrived(r2x.at[gz], w2.at[0, gz])
        add_blocks(cut(mine.at[gz, 0], 0, na), r2x.at[gz], na)
        arrived(r2y.at[gz], w2.at[1, gz])
        add_blocks(cut(mine.at[gz, 0], na, nb), r2y.at[gz], nb)
        if t < ng - 1:
            pass_on(gz, flat_part, rz, sz, wz, gather_flat)

    def corner0():
        @pl.when(g > 0)
        def _():
            arrived(cz.at[g], wc.at[g])
            gather_corner(g, g)

        @pl.when(g < ng - 1)
        def _():
            arrived(cz.at[ng], wc.at[ng])
            gather_corner(ng, g)
        for n in range(4):
            copy3(n).start()

    def corner1():
        arrived(cy.at[1], w3.at[1])
        add_blocks(cut(mine.at[g, 1], flat, nc1), cy.at[1], nc1)
        copy3(4).start()
        arrived(cx.at[1], w3.at[3])
        add_blocks(cut(mine.at[g, 2], flat + nc1, nc2), cx.at[1], nc2)
        copy3(5).start()
        arrived(cy.at[0], w3.at[0])
        add_blocks(cut(mine.at[g, 0], flat, nc1), cy.at[0], nc1)
        arrived(cx.at[0], w3.at[2])
        add_blocks(cut(mine.at[g, 0], flat + nc1, nc2), cx.at[0], nc2)

    def corner2():
        arrived(cx2, w3.at[4])
        add_blocks(cut(mine.at[g, 0], flat, nc1), cx2, nc1)
        arrived(cy2, w3.at[5])
        add_blocks(cut(mine.at[g, 0], flat + nc1, nc2), cy2, nc2)

    def vec_step(n):
        arrived(vxy.at[n], vw.at[n])
        total = vwork[n] + vxy[n]
        if n < 2:
            vwork[n + 1] = total
            vec_copy(n + 1).start()
        else:
            vz[g] = total

    def vec_line(gz, up):
        to = g + 1 if up else g - 1
        return remote(vz.at[gz], vz.at[gz], vs.at[3 + 2 * gz + int(up)], vw.at[3 + gz], (to, d))

    last = ng - 1
    sums0(0)
    vec_step(0)
    sums0(1)
    vec_step(1)
    along0(0)
    stage1(0)
    for t in range(2, last):
        sums0(t)
        along0(t - 1)
        stage1(t - 1)
        stage2(t - 2)
    vec_step(2)

    @pl.when(g < ng - 1)
    def _():
        vec_line(g, True).start()

    @pl.when(g > 0)
    def _():
        vec_line(g, False).start()
    sums0(last)
    along0(last - 1)
    stage1(last - 1)
    for c in (3, 2, 1):
        sends0(last, c)
    corner0()
    stage2(last - 2)
    for n in range(1, ng):
        gz = near_order(n, g, ng)
        arrived(vz.at[gz], vw.at[3 + gz])

        @pl.when((gz < g) & (g < ng - 1))
        def _():
            vec_line(gz, True).start()

        @pl.when((gz > g) & (g > 0))
        def _():
            vec_line(gz, False).start()
    total = vz[0]
    for z in range(1, ng):
        total = total + vz[z]
    vout_ref[...] = total
    stage2(last - 1)
    stage1(last)
    corner1()
    stage2(last)
    corner2()

    @pl.when(g > 0)
    def _():
        arrived(rz.at[g], wz.at[g])

    @pl.when(g < ng - 1)
    def _():
        arrived(rz.at[ng], wz.at[ng])

    @pl.when((g > 0) & (g < ng - 1))
    def _():
        @pl.loop(0, flat // 2)
        def _(n):
            for k in range(2):
                i = 2 * n + k
                out_ref[i] = mine[g, 0, i].astype(F32) + rz[g, i].astype(F32) + rz[ng, i].astype(F32)

    @pl.when(g == 0)
    def _():
        @pl.loop(0, flat // 2)
        def _(n):
            for k in range(2):
                i = 2 * n + k
                out_ref[i] = mine[g, 0, i].astype(F32) + rz[ng, i].astype(F32)

    @pl.when((g > 0) & (g == ng - 1))
    def _():
        @pl.loop(0, flat // 2)
        def _(n):
            for k in range(2):
                i = 2 * n + k
                out_ref[i] = mine[g, 0, i].astype(F32) + rz[g, i].astype(F32)

    for i in range(flat, count):
        out_ref[i] = mine[g, 0, i].astype(F32)

    for t in range(ng):
        gz = order(t)
        for c in range(4):
            to_sibling(gz, c).wait_send()
        for n in range(4):
            copy1(n, gz).wait_send()
        for n in range(2):
            copy2(n, gz).wait_send()
        if t < ng - 1:
            arrived(flat_part(gz), sz.at[gz])
            arrived(corner_part(gz), sc.at[gz])
    for n in range(6):
        copy3(n).wait_send()
    for n in range(3):
        vec_copy(n).wait_send()
    for n in range(ng):
        gz = near_order(n, g, ng)

        @pl.when((gz <= g) & (g < ng - 1))
        def _():
            vec_line(gz, True).wait_send()

        @pl.when((gz >= g) & (g > 0))
        def _():
            vec_line(gz, False).wait_send()


def run_scatter(grads, vec, ng, nd):
    blocks, side, _ = grads.shape
    count = blocks // (ng * nd)
    na, nb, nc1, nc2 = slot_cuts(count)
    flat = na + nb
    dma = pltpu.SemaphoreType.DMA

    def buf(*lead):
        return pltpu.VMEM(lead + (side, side), BF16)

    return pl.pallas_call(
        functools.partial(scatter_kernel, ng=ng, nd=nd),
        out_shape=(sds((count, side, side), F32), sds(vec.shape, F32)),
        in_specs=[hbm(), vmem()],
        out_specs=(vmem(), vmem()),
        scratch_shapes=[
            buf(ng, 4, count),
            buf(ng, 4, count),
            buf(ng, 2, na),
            buf(ng, 2, nb),
            buf(ng, na),
            buf(ng, nb),
            buf(ng + 1, flat),
            buf(ng + 1, 4, nc1 + nc2),
            buf(2, nc1),
            buf(2, nc2),
            buf(nc1),
            buf(nc2),
            pltpu.VMEM((3,) + vec.shape, F32),
            pltpu.VMEM((3,) + vec.shape, F32),
            pltpu.VMEM((ng,) + vec.shape, F32),
            dma((ng, 4)),
            dma((ng, 4)),
            dma((ng, 4)),
            dma((4, ng)),
            dma((4, ng)),
            dma((2, ng)),
            dma((2, ng)),
            dma((ng,)),
            dma((ng + 1,)),
            dma((ng,)),
            dma((ng + 1,)),
            dma((6,)),
            dma((6,)),
            dma((3 + 2 * ng,)),
            dma((3 + ng,)),
        ],
        compiler_params=params(collective_id=1, has_side_effects=True),
        name="scatter",
    )(grads, vec)


def blocks_kernel(g_ref, w_ref, ls_ref, rs_ref, lr_ref, rr_ref, wg_out, nl_out, nr_out, nw_out):
    for i in range(g_ref.shape[0]):
        grad = g_ref[i]
        wg_out[i] = grad
        hi = grad.astype(BF16)
        low = (grad - hi.astype(F32)).astype(BF16)
        nl_out[i] = 0.5 * ls_ref[i] + 0.5 * dot_nt(hi, hi)
        turned = grad.T
        hi_t = turned.astype(BF16)
        nr_out[i] = 0.5 * rs_ref[i] + 0.5 * dot_nt(hi_t, hi_t)
        left = lr_ref[i]
        left_hi = left.astype(BF16)
        left_low = (left - left_hi.astype(F32)).astype(BF16)
        shaped = dot_nn(left_hi, hi) + dot_nn(left_hi, low) + dot_nn(left_low, hi)
        right = rr_ref[i]
        right_hi = right.astype(BF16)
        right_low = (right - right_hi.astype(F32)).astype(BF16)
        sh_hi = shaped.astype(BF16)
        sh_low = (shaped - sh_hi.astype(F32)).astype(BF16)
        shaped = dot_nn(sh_hi, right_hi) + dot_nn(sh_low, right_hi) + dot_nn(sh_hi, right_low)
        nw_out[i] = w_ref[i] - weight_rate * shaped


def run_blocks(grads, weights, left_stats, right_stats, left_roots, right_roots):
    count, side, _ = grads.shape
    step = math.gcd(count, 4)
    spec = pl.BlockSpec((step, side, side), lambda n: (n, 0, 0))
    return pl.pallas_call(
        blocks_kernel,
        grid=(count // step,),
        out_shape=tuple([sds(grads.shape, F32)] * 4),
        in_specs=[spec] * 6,
        out_specs=tuple([spec] * 4),
        compiler_params=params(),
        name="blocks",
    )(grads, weights, left_stats, right_stats, left_roots, right_roots)


def local(
    inputs,
    cotangent,
    weight_slots,
    slot_block,
    left_stats,
    right_stats,
    left_roots,
    right_roots,
    vectors,
    span_start,
):
    seq_count, tok_count, width = inputs.shape
    rows = seq_count * tok_count
    nd = lax.axis_size("dev")
    ng = lax.axis_size("grp")
    side = weight_slots.shape[1]
    hpd = H // nd
    lanes = width // nd
    head = lax.axis_index("dev") * hpd + jnp.arange(hpd, dtype=jnp.int32)
    slopes = jnp.exp2(-8.0 * (head.astype(F32) + 1.0) / H)
    slot_of = invert_order(slot_block)
    vec = vectors.reshape(-1, width)
    x = inputs.reshape(rows, width)
    dy = cotangent.reshape(rows, width)

    direct = nd == 8
    if direct:
        gath = run_gather(weight_slots, ng, nd)
    else:
        gath = lax.all_gather(weight_slots.astype(BF16), ("grp", "dev"), axis=0, tiled=True)
    h1, qkv = run_qkv(slot_of, x, vec, gath, nd)
    qkv, o, o32, lse = run_attn_fwd(
        span_start, slopes, qkv.reshape(nd, 3, seq_count, tok_count, lanes), hpd
    )
    act, att, h2, g, dz, da, dx1, do, sums2 = run_mlp(
        slot_of, o.reshape(nd, rows, lanes), x, dy, vec, gath, nd
    )
    do = do.reshape(nd, seq_count, tok_count, lanes)
    dqkv = run_attn_bwd(span_start, slopes, qkv, do, o32, lse, hpd).reshape(nd, 3, rows, lanes)
    ig, cat, sums1 = run_dh1(slot_of, dqkv, x, dx1, vec, gath, nd)
    grads = run_wgrad(slot_of, h1, att, h2, g, cat, da, dz, dy, side)

    s2 = jnp.sum(sums2.reshape(-1, 8, width), axis=1)
    s1 = jnp.sum(sums1.reshape(-1, 8, width), axis=1)
    bo, gain2, shift2, bdown = [s2[n:n + 1] for n in range(4)]
    gain1, shift1, bq, bv = [s1[n:n + 1] for n in range(4)]
    local_vector = jnp.concatenate(
        [gain1, shift1, bq, bv, bo, gain2, shift2, bdown, s2[4:]], axis=0
    )
    if direct:
        weight_grads, vector_grads = run_scatter(grads, local_vector, ng, nd)
        vector_grads = vector_grads.reshape(-1)
    else:
        vector_grads = lax.psum(local_vector.reshape(-1), ("grp", "dev"))
        weight_grads = lax.psum_scatter(grads, ("grp", "dev"), scatter_dimension=0, tiled=True)
        weight_grads = weight_grads.astype(F32)
    tokens_all = rows * nd * ng
    new_vectors = vectors - vector_rate / math.sqrt(tokens_all) * vector_grads

    weight_grads, new_left, new_right, new_weights = run_blocks(
        weight_grads, weight_slots, left_stats, right_stats, left_roots, right_roots
    )
    return (
        act.reshape(inputs.shape),
        ig.reshape(inputs.shape),
        weight_grads,
        new_left,
        new_right,
        new_weights,
        vector_grads,
        new_vectors,
    )


def solution(mesh):
    return jax.shard_map(
        local,
        mesh=mesh,
        in_specs=(
            P("grp", "dev", None),
            P("grp", "dev", None),
            P(("grp", "dev"), None, None),
            P(),
            P(("grp", "dev"), None, None),
            P(("grp", "dev"), None, None),
            P(("grp", "dev"), None, None),
            P(("grp", "dev"), None, None),
            P(),
            P("grp"),
        ),
        out_specs=(
            P("grp", "dev", None),
            P("grp", "dev", None),
            P(("grp", "dev"), None, None),
            P(("grp", "dev"), None, None),
            P(("grp", "dev"), None, None),
            P(("grp", "dev"), None, None),
            P(),
            P(),
        ),
        check_vma=False,
    )
```

```python
import functools
import math

import jax
import jax.numpy as jnp
from jax import lax
from jax.experimental import pallas as pl
from jax.experimental.pallas import tpu as pltpu
from jax.sharding import PartitionSpec as P

H = 16
FF = 4096
PIC = 256

eps = 1e-05
weight_rate = 0.5
vector_rate = 0.5
big_negative = -1e30
highest = lax.Precision.HIGHEST
F32 = jnp.float32
BF16 = jnp.bfloat16
LOG2E = 1.4426950408889634
MIB = 1024 * 1024

GAIN1, SHIFT1, BQ, BV, BO, GAIN2, SHIFT2, BDOWN, BUP = range(9)


def dot_nn(a, b):
    return lax.dot_general(a, b, (((1,), (0,)), ((), ())), preferred_element_type=F32)


def dot_nt(a, b):
    return lax.dot_general(a, b, (((1,), (1,)), ((), ())), preferred_element_type=F32)


def invert_order(slot_block):
    places = jnp.arange(slot_block.shape[0], dtype=jnp.int32)
    matches = (slot_block[None, :] == places[:, None]).astype(jnp.int32)
    return jnp.sum(matches * places[None, :], axis=1)


def vmem():
    return pl.BlockSpec(memory_space=pltpu.VMEM)


def smem():
    return pl.BlockSpec(memory_space=pltpu.SMEM)


def hbm():
    return pl.BlockSpec(memory_space=pl.ANY)


def sds(shape, dtype):
    return jax.ShapeDtypeStruct(shape, dtype)


def params(mib=58, **kw):
    return pltpu.CompilerParams(vmem_limit_bytes=mib * MIB, **kw)


def layer_stats(v):
    middle = jnp.mean(v, axis=-1, keepdims=True)
    centred = v - middle
    spread = jnp.mean(centred * centred, axis=-1, keepdims=True)
    return centred, lax.rsqrt(spread + eps)


def fold_rows(v):
    return jnp.sum(v.reshape(v.shape[0] // 8, 8, v.shape[1]), axis=0)


def fetch_block(gath, slot, dst, row, col, sem, side):
    return pltpu.make_async_copy(
        gath.at[slot], dst.at[pl.ds(row, side), pl.ds(col, side)], sem
    )


def qkv_kernel(slot_ref, x_ref, vec_ref, gath, h1_ref, out_ref, wbuf, sems, *, nd):
    rows, width = x_ref.shape
    side = gath.shape[1]
    per = width // side
    lanes = out_ref.shape[3]
    for part in range(3):
        @pl.loop(0, per)
        def _(i):
            for j in range(per):
                slot = slot_ref[i * 3 * per + part * per + j]
                fetch_block(gath, slot, wbuf.at[part], pl.multiple_of(i * side, side), j * side, sems.at[part], side).start()

    chunk = 32
    gain = vec_ref[GAIN1:GAIN1 + 1, :]
    shift = vec_ref[SHIFT1:SHIFT1 + 1, :]

    @pl.loop(0, rows // chunk)
    def _(r):
        at = pl.ds(pl.multiple_of(r * chunk, chunk), chunk)
        centred, inv = layer_stats(x_ref[at, :].astype(F32))
        h1_ref[at, :] = (centred * inv * gain + shift).astype(BF16)

    for part in range(3):
        pltpu.make_async_copy(wbuf.at[part], wbuf.at[part], sems.at[part]).wait()
        for half in range(2):
            cols = slice(half * width // 2, (half + 1) * width // 2)
            res = dot_nn(h1_ref[...], wbuf[part, :, cols])
            if part == 0:
                res = res + vec_ref[BQ:BQ + 1, cols]
            if part == 2:
                res = res + vec_ref[BV:BV + 1, cols]
            res = res.astype(BF16)
            for d in range(nd // 2):
                out_ref[half * (nd // 2) + d, part, :, :] = res[:, d * lanes:(d + 1) * lanes]


def run_qkv(slot_of, x, vec, gath, nd):
    rows, width = x.shape
    lanes = width // nd
    return pl.pallas_call(
        functools.partial(qkv_kernel, nd=nd),
        out_shape=(sds((rows, width), BF16), sds((nd, 3, rows, lanes), BF16)),
        in_specs=[smem(), vmem(), vmem(), hbm()],
        out_specs=(vmem(), vmem()),
        scratch_shapes=[pltpu.VMEM((3, width, width), BF16), pltpu.SemaphoreType.DMA((3,))],
        compiler_params=params(),
        name="qkv",
    )(slot_of, x, vec, gath)


MESH = pl.DeviceIdType.MESH


def remote(src, dst, send, recv, device):
    return pltpu.make_async_remote_copy(
        src_ref=src, dst_ref=dst, send_sem=send, recv_sem=recv, device_id=device, device_id_type=MESH
    )


def arrived(ref, sem):
    pltpu.make_async_copy(ref, ref, sem).wait()


def cut(ref, first, size):
    return ref.at[pl.ds(first, size)]


def greet_plane(g, d, nd):
    barrier = pltpu.get_barrier_semaphore()
    for p in range(1, nd):
        pl.semaphore_signal(barrier, inc=1, device_id=(g, lax.rem(d + p, nd)), device_id_type=MESH)
    pl.semaphore_wait(barrier, nd - 1)


def parts3(v):
    hi = v.astype(BF16)
    mid = (v - hi.astype(F32)).astype(BF16)
    lo = (v - hi.astype(F32) - mid.astype(F32)).astype(BF16)
    return hi.astype(F32), mid.astype(F32), lo.astype(F32)


def own_lanes(h, shape, hpd, lanes):
    lane = lax.broadcasted_iota(jnp.int32, shape, 1)
    size = lanes // hpd
    return (lane >= h * size) & (lane < (h + 1) * size)


def place(values, base, tok, width):
    lane = lax.broadcasted_iota(jnp.int32, (tok, width), 1)
    out = jnp.zeros((tok, width), F32)
    for n, v in enumerate(values):
        out = jnp.where(lane == base + n, v, out)
    return out


def spare(h, hpd, lanes):
    return (lanes // hpd) * (1 - h) if hpd > 1 else 0


def column_tables(slope_ref, qbase, kbase, kfar, hpd, lanes):
    _, tok, _ = qbase.shape
    u = lax.broadcasted_iota(jnp.int32, (tok, 128), 0).astype(F32)
    for h in range(hpd):
        slope = slope_ref[h] * LOG2E
        base = spare(h, hpd, lanes)
        near = parts3(jnp.full((tok, 128), slope, F32))
        far = parts3(jnp.full((tok, 128), slope * tok, F32))
        qbase[h] = place(near + far, base, tok, 128)
        kbase[h] = place([u] * 3 + [0.0] * 3 + [1.0] * 3, base, tok, 128)
        kfar[h] = place([0.0] * 3 + [1.0] * 3, base, tok, 128)


def q_columns(q, h, hpd, columns, extra):
    tok, lanes = q.shape
    scaled = q.astype(F32) * ((lanes // hpd) ** (-0.5) * LOG2E)
    hi = scaled.astype(BF16).astype(F32)
    low = scaled - hi
    if extra:
        lane = lax.broadcasted_iota(jnp.int32, (tok, 128), 1)
        for n, v in enumerate(extra):
            columns = jnp.where(lane == spare(h, hpd, lanes) + 6 + n, v, columns)
    if hpd > 1:
        own = own_lanes(h, (tok, lanes), hpd, lanes)
        return jnp.concatenate(
            [jnp.where(own, hi, 0.0), jnp.where(own, low, columns)], axis=1
        ).astype(BF16)
    return jnp.concatenate([hi, low, columns], axis=1).astype(BF16)


def k_columns(k, h, hpd, columns):
    tok, lanes = k.shape
    wide = k.astype(F32)
    if hpd > 1:
        own = own_lanes(h, (tok, lanes), hpd, lanes)
        return jnp.concatenate([wide, jnp.where(own, wide, columns)], axis=1).astype(BF16)
    return jnp.concatenate([wide, wide, columns], axis=1).astype(BF16)


def far_side(slope, tok):
    u = lax.broadcasted_iota(jnp.int32, (tok, tok), 0)
    t = lax.broadcasted_iota(jnp.int32, (tok, tok), 1)
    after = u > t
    return (
        jnp.where(after, big_negative, 0.0),
        jnp.where(after, (2.0 * slope) * (t - u).astype(F32), 0.0),
    )


def attn_fwd_kernel(
    span_ref, slope_ref, src, got, o_got, o32_ref, lse_ref,
    qa, ka, vt, scores, corr, qbase, kbase, kfar, o_out, ss, sr, os, orr, loc, *, hpd, nd
):
    nb, _, seqs, tok, lanes = got.shape
    size = lanes // hpd
    pair = 2 * tok
    g = lax.axis_index("grp")
    d = lax.axis_index("dev")

    for q in range(seqs):
        pltpu.make_async_copy(src.at[d, :, q], got.at[d, :, q], loc.at[q]).start()
    greet_plane(g, d, nd)

    def send(q, p):
        to = lax.rem(d + p, nd)
        return remote(src.at[to, :, q], got.at[d, :, q], ss.at[q, p], sr.at[q, p], (g, to))

    def send_all(q):
        @pl.loop(1, nd)
        def _(p):
            send(q, p).start()

    send_all(0)

    def send_o(q, i, p):
        return remote(o_out.at[i, q], o_got.at[d, q], os.at[q, i], orr.at[q, p], (g, i))

    column_tables(slope_ref, qbase, kbase, kfar, hpd, lanes)
    for h in range(hpd):
        mask, span = far_side(slope_ref[h] * LOG2E, tok)
        for n, (one, two) in enumerate(((mask, mask), (span, mask), (mask, span))):
            corr[h, n, 0:tok, 0:tok] = one
            corr[h, n, tok:, tok:] = two
            corr[h, n, 0:tok, tok:] = jnp.zeros((tok, tok), F32)
            corr[h, n, tok:, 0:tok] = jnp.full((tok, tok), big_negative, F32)

    for q in range(seqs):
        pltpu.make_async_copy(src.at[d, :, q], got.at[d, :, q], loc.at[q]).wait()

        @pl.loop(1, nd)
        def _(p):
            arrived(got.at[lax.rem(d + nd - p, nd), :, q], sr.at[q, p])

        if q + 1 < seqs:
            send_all(q + 1)

        @pl.loop(0, nb)
        def _(j):
            at_j = pl.ds(pl.multiple_of(j * tok, tok), tok)
            vt[0:lanes, at_j] = got[j, 2, q].astype(F32).T.astype(BF16)
            block = jnp.full((tok, 128), j, jnp.int32).astype(F32)
            for h in range(hpd):
                qa[h, at_j, :] = q_columns(got[j, 0, q], h, hpd, qbase[h], [])
                ka[h, at_j, :] = k_columns(got[j, 1, q], h, hpd, kbase[h] + block * kfar[h])

        start = span_ref[q]

        @pl.loop(0, nb // 2)
        def _(i):
            flag = (start == i * pair).astype(jnp.int32) + 2 * (start == i * pair + tok).astype(jnp.int32)

            def at_pair(n):
                return pl.ds(pl.multiple_of(n * pair, pair), pair)

            def fold_max(v):
                return jnp.max(v.reshape(pair // 8, 8, pair), axis=0)

            def score(n, tops):
                new = []
                for h in range(hpd):
                    s = dot_nt(ka[h, at_pair(n), :], qa[h, at_pair(i), :])
                    scores[h, at_pair(n), :] = s
                    new.append(jnp.maximum(tops[h], fold_max(s)))
                return tuple(new)

            tops = lax.fori_loop(
                0, i, score, tuple([jnp.full((8, pair), big_negative, F32)] * hpd)
            )
            top = []
            for h in range(hpd):
                s = dot_nt(ka[h, at_pair(i), :], qa[h, at_pair(i), :]) + corr[h, flag]
                scores[h, at_pair(i), :] = s
                top.append(jnp.max(jnp.maximum(tops[h], fold_max(s)), axis=0, keepdims=True))

            def weigh(n, state):
                new = []
                for h in range(hpd):
                    acc, total = state[h]
                    p = jnp.exp2(scores[h, at_pair(n), :] - top[h])
                    total = total + jnp.sum(p.reshape(pair // 8, 8, pair), axis=0)
                    acc = acc + dot_nn(vt[h * size:(h + 1) * size, at_pair(n)], p.astype(BF16))
                    new.append((acc, total))
                return tuple(new)

            state = lax.fori_loop(
                0,
                i + 1,
                weigh,
                tuple([(jnp.zeros((size, pair), F32), jnp.zeros((8, pair), F32))] * hpd),
            )
            outs = []
            logs = []
            for h in range(hpd):
                acc, total = state[h]
                total = jnp.sum(total, axis=0, keepdims=True)
                outs.append(acc / total)
                logs.append(jnp.broadcast_to(top[h] + jnp.log2(total), (128 // hpd, pair)))
            out = (jnp.concatenate(outs, axis=0) if hpd > 1 else outs[0]).T
            log = (jnp.concatenate(logs, axis=0) if hpd > 1 else logs[0]).T
            for k in range(2):
                at = 2 * i + k
                o32_ref[at, q] = out[k * tok:(k + 1) * tok]
                o_out[at, q] = out[k * tok:(k + 1) * tok].astype(BF16)
                lse_ref[at, q] = log[k * tok:(k + 1) * tok]

                @pl.when(at == d)
                def _():
                    pltpu.make_async_copy(o_out.at[at, q], o_got.at[d, q], os.at[q, at]).start()

                @pl.when(at != d)
                def _():
                    send_o(q, at, lax.rem(at - d + nd, nd)).start()

    for q in range(seqs):
        @pl.loop(1, nd)
        def _(p):
            arrived(o_got.at[lax.rem(d + nd - p, nd), q], orr.at[q, p])
            send(q, p).wait_send()

        @pl.loop(0, nd)
        def _(i):
            arrived(o_out.at[i, q], os.at[q, i])


def run_attn_fwd(span, slopes, qkv, hpd):
    nb, _, seqs, tok, lanes = qkv.shape
    t = nb * tok
    dma = pltpu.SemaphoreType.DMA
    return pl.pallas_call(
        functools.partial(attn_fwd_kernel, hpd=hpd, nd=nb),
        out_shape=(
            sds(qkv.shape, BF16),
            sds((nb, seqs, tok, lanes), BF16),
            sds((nb, seqs, tok, lanes), F32),
            sds((nb, seqs, tok, 128), F32),
        ),
        in_specs=[smem(), smem(), hbm()],
        out_specs=(vmem(), vmem(), vmem(), vmem()),
        scratch_shapes=[
            pltpu.VMEM((hpd, t, 256), BF16),
            pltpu.VMEM((hpd, t, 256), BF16),
            pltpu.VMEM((lanes, t), BF16),
            pltpu.VMEM((hpd, t, 2 * tok), F32),
            pltpu.VMEM((hpd, 3, 2 * tok, 2 * tok), F32),
            pltpu.VMEM((hpd, tok, 128), F32),
            pltpu.VMEM((hpd, tok, 128), F32),
            pltpu.VMEM((hpd, tok, 128), F32),
            pltpu.VMEM((nb, seqs, tok, lanes), BF16),
            dma((seqs, nb)),
            dma((seqs, nb)),
            dma((seqs, nb)),
            dma((seqs, nb)),
            dma((seqs,)),
        ],
        compiler_params=params(collective_id=2, has_side_effects=True),
        name="attn_fwd",
    )(span, slopes, qkv)


def attn_bwd_kernel(
    span_ref, slope_ref, qkv_ref, do_src, o32_ref, lse_ref, got,
    do_got, out, qa, ka, kt, va, qm, da, dm, dqt, corr, qbase, kbase, kfar, dk_ref, dv_ref,
    ss, sr, gs, gr, loc, *, hpd, nd
):
    nb, _, seqs, tok, lanes = qkv_ref.shape
    size = lanes // hpd
    unit = size ** (-0.5)
    g = lax.axis_index("grp")
    d = lax.axis_index("dev")

    def own_copy(q):
        return pltpu.make_async_copy(do_src.at[d, q], do_got.at[d, q], loc.at[q])

    for q in range(seqs):
        own_copy(q).start()
    greet_plane(g, d, nd)

    def send(q, p):
        to = lax.rem(d + p, nd)
        return remote(do_src.at[to, q], do_got.at[d, q], ss.at[q, p], sr.at[q, p], (g, to))

    def send_all(q):
        @pl.loop(1, nd)
        def _(p):
            send(q, p).start()

    send_all(0)

    def back(q, kind, p):
        to = lax.rem(d + p, nd)
        at = pl.ds(kind, 1 + kind)
        return remote(
            out.at[to, at, q], got.at[d, at, q], gs.at[q, kind, p], gr.at[q, kind, p], (g, to)
        )

    def back_own(q, kind):
        at = pl.ds(kind, 1 + kind)
        return pltpu.make_async_copy(out.at[d, at, q], got.at[d, at, q], gs.at[q, kind, 0])

    for h in range(hpd):
        mask, span = far_side(slope_ref[h] * LOG2E, tok)
        for n, table in enumerate((mask, span)):
            corr[h, n, :, 0:tok] = table
            corr[h, n, :, tok:] = jnp.zeros((tok, tok), F32)
    column_tables(slope_ref, qbase, kbase, kfar, hpd, lanes)

    for q in range(seqs):
        @pl.loop(0, nb)
        def _(j):
            at_j = pl.ds(pl.multiple_of(j * tok, tok), tok)
            qj = qkv_ref[j, 0, q]
            kj = qkv_ref[j, 1, q]
            vj = qkv_ref[j, 2, q].astype(F32)
            kt[:, at_j] = kj.astype(F32).T.astype(BF16)
            dqt[:, at_j] = jnp.zeros((lanes, tok), F32)
            block = jnp.full((tok, 128), j, jnp.int32).astype(F32)
            for h in range(hpd):
                low = lse_ref[j, q][:, h * (128 // hpd):h * (128 // hpd) + 1]
                extra = [-p for p in parts3(low)]
                qa[h, at_j, :] = q_columns(qj, h, hpd, qbase[h], extra)
                ka[h, j] = k_columns(kj, h, hpd, kbase[h] + block * kfar[h])
                if hpd > 1:
                    own = own_lanes(h, (tok, lanes), hpd, lanes)
                    qm[h, at_j, :] = jnp.where(own, qj.astype(F32), 0.0).astype(BF16)
                    va[h, j] = jnp.where(own, vj, kbase[h]).astype(BF16)
                else:
                    qm[h, at_j, :] = qj
                    va[h, j] = jnp.concatenate([vj, kbase[h][:, 0:lanes]], axis=1).astype(BF16)

        own_copy(q).wait()

        @pl.loop(1, nd)
        def _(p):
            arrived(do_got.at[lax.rem(d + nd - p, nd), q], sr.at[q, p])

        if q + 1 < seqs:
            send_all(q + 1)

        @pl.loop(0, nb)
        def _(j):
            at_j = pl.ds(pl.multiple_of(j * tok, tok), tok)
            do = do_got[j, q].astype(F32)
            prod = do * o32_ref[j, q]
            for h in range(hpd):
                if hpd > 1:
                    own = own_lanes(h, (tok, lanes), hpd, lanes)
                    delta = jnp.sum(jnp.where(own, prod, 0.0), axis=1, keepdims=True)
                    extra = place([-p for p in parts3(delta)], spare(h, hpd, lanes) + 6, tok, lanes)
                    da[h, at_j, :] = jnp.where(own, do, extra).astype(BF16)
                    dm[h, at_j, :] = jnp.where(own, do, 0.0).astype(BF16)
                else:
                    delta = jnp.sum(prod, axis=1, keepdims=True)
                    extra = place([-p for p in parts3(delta)], 6, tok, lanes)
                    da[h, at_j, :] = jnp.concatenate([do, extra], axis=1).astype(BF16)
                    dm[h, at_j, :] = do.astype(BF16)

        start = span_ref[q]

        @pl.loop(0, nb)
        def _(n):
            j = lax.rem(d + n, nb)
            at_j = pl.ds(pl.multiple_of(j * tok, tok), tok)
            flag = (start == j * tok).astype(jnp.int32)

            def tile(i, width, near):
                at_i = pl.ds(pl.multiple_of(i * tok, tok), width)
                dk = None
                for h in range(hpd):
                    s = dot_nt(ka[h, j], qa[h, at_i, :])
                    if near:
                        s = s + corr[h, flag, :, 0:width]
                    p = jnp.exp2(s)
                    ds = (p * dot_nt(va[h, j], da[h, at_i, :])).astype(BF16)
                    dv_h = dot_nn(p.astype(BF16), dm[h, at_i, :])
                    dk_h = dot_nn(ds, qm[h, at_i, :])
                    dk = dk_h if dk is None else dk + dk_h
                    dv = dv_h if h == 0 else dv + dv_h
                    rows = slice(h * size, (h + 1) * size)
                    dqt[rows, at_i] += dot_nn(kt[rows, at_j], ds)
                if near:
                    dk_ref[...] = dk
                    dv_ref[...] = dv
                else:
                    dk_ref[...] += dk
                    dv_ref[...] += dv

            odd = lax.rem(nb - j, 2)

            @pl.when(odd == 1)
            def _():
                tile(j, tok, True)

            @pl.when(odd == 0)
            def _():
                tile(j, 2 * tok, True)

            @pl.loop(0, (nb - j - 1) // 2)
            def _(m):
                tile(j + 2 - odd + 2 * m, 2 * tok, False)

            out[j, 1, q] = (dk_ref[...] * unit).astype(BF16)
            out[j, 2, q] = dv_ref[...].astype(BF16)

            @pl.when(n == 0)
            def _():
                back_own(q, 1).start()

            @pl.when(n > 0)
            def _():
                back(q, 1, n).start()

        @pl.loop(0, nb)
        def _(n):
            j = lax.rem(d + n, nb)
            at_j = pl.ds(pl.multiple_of(j * tok, tok), tok)
            out[j, 0, q] = (dqt[:, at_j].T * unit).astype(BF16)

            @pl.when(n == 0)
            def _():
                back_own(q, 0).start()

            @pl.when(n > 0)
            def _():
                back(q, 0, n).start()

    for q in range(seqs):
        for kind in range(2):
            back_own(q, kind).wait()

        @pl.loop(1, nd)
        def _(p):
            send(q, p).wait_send()
            source = lax.rem(d + nd - p, nd)
            for kind in range(2):
                back(q, kind, p).wait_send()
                arrived(got.at[source, pl.ds(kind, 1 + kind), q], gr.at[q, kind, p])


def run_attn_bwd(span, slopes, qkv, do, o32, lse, hpd):
    nb, _, seqs, tok, lanes = qkv.shape
    t = nb * tok
    dma = pltpu.SemaphoreType.DMA
    wide = 128 if hpd == 1 else lanes
    return pl.pallas_call(
        functools.partial(attn_bwd_kernel, hpd=hpd, nd=nb),
        out_shape=sds(qkv.shape, BF16),
        in_specs=[smem(), smem(), vmem(), hbm(), vmem(), vmem()],
        out_specs=vmem(),
        scratch_shapes=[
            pltpu.VMEM((nb, seqs, tok, lanes), BF16),
            pltpu.VMEM(qkv.shape, BF16),
            pltpu.VMEM((hpd, t, 256), BF16),
            pltpu.VMEM((hpd, nb, tok, 256), BF16),
            pltpu.VMEM((lanes, t), BF16),
            pltpu.VMEM((hpd, nb, tok, wide), BF16),
            pltpu.VMEM((hpd, t, lanes), BF16),
            pltpu.VMEM((hpd, t, wide), BF16),
            pltpu.VMEM((hpd, t, lanes), BF16),
            pltpu.VMEM((lanes, t), F32),
            pltpu.VMEM((hpd, 2, tok, 2 * tok), F32),
            pltpu.VMEM((hpd, tok, 128), F32),
            pltpu.VMEM((hpd, tok, 128), F32),
            pltpu.VMEM((hpd, tok, 128), F32),
            pltpu.VMEM((tok, lanes), F32),
            pltpu.VMEM((tok, lanes), F32),
            dma((seqs, nb)),
            dma((seqs, nb)),
            dma((seqs, 2, nb)),
            dma((seqs, 2, nb)),
            dma((seqs,)),
        ],
        compiler_params=params(collective_id=3, has_side_effects=True),
        name="attn_bwd",
    )(span, slopes, qkv, do, o32, lse)


def mlp_kernel(
    slot_ref, o_ref, x_ref, dy_ref, vec_ref, gath,
    act_ref, att_ref, h2_ref, g_ref, dz_ref, da_ref, dx1_ref, do_ref, sums_ref,
    wo, wup, wdn, x1, acc, dh2, sem_o, sem_t, *, nd, first_o, first_up, first_dn, tile
):
    rows, width = x_ref.shape
    side = gath.shape[1]
    per = width // side
    ff = g_ref.shape[1]
    tiles = ff // tile
    cols = tile // side
    lanes = o_ref.shape[2]
    fper = ff // side

    @pl.loop(0, per)
    def _(i):
        for j in range(per):
            fetch_block(gath, slot_ref[first_o + i * per + j], wo, pl.multiple_of(i * side, side), j * side, sem_o.at[0], side).start()

    def fetch_tile(f):
        @pl.loop(0, per)
        def _(i):
            for j in range(cols):
                fetch_block(gath, slot_ref[first_up + i * fper + f * cols + j], wup.at[f], pl.multiple_of(i * side, side), j * side, sem_t.at[f], side).start()
            for j in range(cols):
                fetch_block(gath, slot_ref[first_dn + (f * cols + j) * per + i], wdn.at[f], j * side, pl.multiple_of(i * side, side), sem_t.at[f], side).start()

    fetch_tile(0)
    fetch_tile(1)
    for d in range(nd):
        att_ref[:, d * lanes:(d + 1) * lanes] = o_ref[d]
    pltpu.make_async_copy(wo, wo, sem_o.at[0]).wait()
    for half in range(2):
        c = slice(half * width // 2, (half + 1) * width // 2)
        x1[:, c] = x_ref[:, c].astype(F32) + dot_nn(att_ref[...], wo[:, c]) + vec_ref[BO:BO + 1, c]

    chunk = 32

    def rows_at(r):
        return pl.ds(pl.multiple_of(r * chunk, chunk), chunk)

    @pl.loop(0, rows // chunk)
    def _(r):
        at = rows_at(r)
        centred, inv = layer_stats(x1[at, :])
        h2_ref[at, :] = (centred * inv * vec_ref[GAIN2:GAIN2 + 1, :] + vec_ref[SHIFT2:SHIFT2 + 1, :]).astype(BF16)
        acc[at, :] = x1[at, :] + vec_ref[BDOWN:BDOWN + 1, :]
        dh2[at, :] = jnp.zeros((chunk, width), F32)

    @pl.loop(0, tiles)
    def _(f):
        @pl.when(f + 2 < tiles)
        def _():
            fetch_tile(f + 2)
        pltpu.make_async_copy(wup.at[f], wup.at[f], sem_t.at[f]).wait()
        pltpu.make_async_copy(wdn.at[f], wdn.at[f], sem_t.at[f]).wait()
        per_row = width // tile
        bias = vec_ref[pl.ds(BUP + f // per_row, 1), pl.ds(pl.multiple_of((f % per_row) * tile, tile), tile)]
        at_f = pl.ds(pl.multiple_of(f * tile, tile), tile)
        z = dot_nn(h2_ref[...], wup[f]) + bias
        dg = dot_nt(dy_ref[...], wdn[f])
        z2 = z * z
        th = jnp.tanh(0.7978845608028654 * (z + 0.044715 * z2 * z))
        g = (0.5 * z * (1.0 + th)).astype(BF16)
        slope = 0.5 * (1.0 + th) + 0.5 * z * (1.0 - th * th) * (
            0.7978845608028654 * (1.0 + 3.0 * 0.044715 * z2)
        )
        dz = (dg * slope).astype(BF16)
        g_ref[:, at_f] = g
        dz_ref[:, at_f] = dz
        sums_ref[pl.ds(pl.multiple_of(8 * (4 + f // per_row), 8), 8), pl.ds(pl.multiple_of((f % per_row) * tile, tile), tile)] = fold_rows(dz.astype(F32))
        acc[...] += dot_nn(g, wdn[f])
        dh2[...] += dot_nt(dz, wup[f])

    zero = jnp.zeros((8, width), F32)

    def finish(r, carry):
        s_bo, s_gain, s_shift, s_bdown = carry
        at = rows_at(r)
        act_ref[at, :] = acc[at, :].astype(BF16)
        centred, inv = layer_stats(x1[at, :])
        hat = centred * inv
        dh = dh2[at, :]
        dhg = dh * vec_ref[GAIN2:GAIN2 + 1, :]
        back = inv * (
            dhg
            - jnp.mean(dhg, axis=-1, keepdims=True)
            - hat * jnp.mean(dhg * hat, axis=-1, keepdims=True)
        )
        dy = dy_ref[at, :].astype(F32)
        dx1 = dy + back
        dx1_ref[at, :] = dx1
        da = dx1.astype(BF16)
        da_ref[at, :] = da
        return (
            s_bo + fold_rows(da.astype(F32)),
            s_gain + fold_rows(dh * hat),
            s_shift + fold_rows(dh),
            s_bdown + fold_rows(dy),
        )

    carry = lax.fori_loop(0, rows // chunk, finish, (zero, zero, zero, zero))
    for n in range(4):
        sums_ref[8 * n:8 * n + 8, :] = carry[n]
    for half in range(2):
        c = slice(half * width // 2, (half + 1) * width // 2)
        res = dot_nt(da_ref[...], wo[c, :]).astype(BF16)
        for d in range(nd // 2):
            do_ref[half * (nd // 2) + d] = res[:, d * lanes:(d + 1) * lanes]


def run_mlp(slot_of, o, x, dy, vec, gath, nd):
    rows, width = x.shape
    side = gath.shape[1]
    lanes = width // nd
    per = width // side
    first_o = 3 * per * per
    first_up = first_o + per * per
    first_dn = first_up + per * (FF // side)
    tile = 512
    return pl.pallas_call(
        functools.partial(
            mlp_kernel, nd=nd, first_o=first_o, first_up=first_up, first_dn=first_dn, tile=tile
        ),
        out_shape=(
            sds((rows, width), BF16),
            sds((rows, width), BF16),
            sds((rows, width), BF16),
            sds((rows, FF), BF16),
            sds((rows, FF), BF16),
            sds((rows, width), BF16),
            sds((rows, width), F32),
            sds((nd, rows, lanes), BF16),
            sds((8 * (4 + FF // width), width), F32),
        ),
        in_specs=[smem(), vmem(), vmem(), vmem(), vmem(), hbm()],
        out_specs=tuple([vmem()] * 9),
        scratch_shapes=[
            pltpu.VMEM((width, width), BF16),
            pltpu.VMEM((FF // tile, width, tile), BF16),
            pltpu.VMEM((FF // tile, tile, width), BF16),
            pltpu.VMEM((rows, width), F32),
            pltpu.VMEM((rows, width), F32),
            pltpu.VMEM((rows, width), F32),
            pltpu.SemaphoreType.DMA((1,)),
            pltpu.SemaphoreType.DMA((FF // tile,)),
        ],
        compiler_params=params(),
        name="mlp",
    )(slot_of, o, x, dy, vec, gath)


def dh1_kernel(
    slot_ref, dqkv_ref, x_ref, dx1_ref, vec_ref, gath, ig_ref, cat_ref, sums_ref,
    wbuf, dh1, sems, *, nd
):
    rows, width = x_ref.shape
    side = gath.shape[1]
    per = width // side
    lanes = dqkv_ref.shape[3]
    for part in range(3):
        @pl.loop(0, per)
        def _(i):
            for j in range(per):
                slot = slot_ref[i * 3 * per + part * per + j]
                fetch_block(gath, slot, wbuf.at[part], pl.multiple_of(i * side, side), j * side, sems.at[part], side).start()

    for part in range(3):
        for d in range(nd):
            at = part * width + d * lanes
            cat_ref[:, at:at + lanes] = dqkv_ref[d, part]
    for part in range(3):
        pltpu.make_async_copy(wbuf.at[part], wbuf.at[part], sems.at[part]).wait()
        for half in range(2):
            c = slice(half * width // 2, (half + 1) * width // 2)
            res = dot_nt(cat_ref[:, part * width:(part + 1) * width], wbuf[part, c, :])
            if part == 0:
                dh1[:, c] = res
            else:
                dh1[:, c] += res

    chunk = 32
    zero = jnp.zeros((8, width), F32)

    def finish(r, carry):
        s_gain, s_shift, s_bq, s_bv = carry
        at = pl.ds(pl.multiple_of(r * chunk, chunk), chunk)
        centred, inv = layer_stats(x_ref[at, :].astype(F32))
        hat = centred * inv
        dh = dh1[at, :]
        dhg = dh * vec_ref[GAIN1:GAIN1 + 1, :]
        back = inv * (
            dhg
            - jnp.mean(dhg, axis=-1, keepdims=True)
            - hat * jnp.mean(dhg * hat, axis=-1, keepdims=True)
        )
        ig_ref[at, :] = dx1_ref[at, :] + back
        return (
            s_gain + fold_rows(dh * hat),
            s_shift + fold_rows(dh),
            s_bq + fold_rows(cat_ref[at, 0:width].astype(F32)),
            s_bv + fold_rows(cat_ref[at, 2 * width:3 * width].astype(F32)),
        )

    carry = lax.fori_loop(0, rows // chunk, finish, (zero, zero, zero, zero))
    for n in range(4):
        sums_ref[8 * n:8 * n + 8, :] = carry[n]


def run_dh1(slot_of, dqkv, x, dx1, vec, gath, nd):
    rows, width = x.shape
    return pl.pallas_call(
        functools.partial(dh1_kernel, nd=nd),
        out_shape=(
            sds((rows, width), F32),
            sds((rows, 3 * width), BF16),
            sds((32, width), F32),
        ),
        in_specs=[smem(), vmem(), vmem(), vmem(), vmem(), hbm()],
        out_specs=(vmem(), vmem(), vmem()),
        scratch_shapes=[
            pltpu.VMEM((3, width, width), BF16),
            pltpu.VMEM((rows, width), F32),
            pltpu.SemaphoreType.DMA((3,)),
        ],
        compiler_params=params(),
        name="dh1",
    )(slot_of, dqkv, x, dx1, vec, gath)


def wgrad_kernel(
    slot_ref, h1, att, h2, g, dqkv, da, dz, dy, out,
    v_a, v_b, a_t, stage, sem_in, sem_out, *, side, tile
):
    rows, width = h1.shape
    per = width // side
    cols = tile // side
    ff = g.shape[1]
    runs = [(h2, 0, dz, 4 * per * per, ff // side)]
    for c in range(ff // width):
        first = 4 * per * per + per * (ff // side) + c * per * per
        runs.append((g, c * width, dy, first, per))
    runs.append((att, 0, da, 3 * per * per, per))
    runs.append((h1, 0, dqkv, 0, 3 * per))

    def loads(n):
        a, at, b, _, _ = runs[n]
        copies = [pltpu.make_async_copy(a.at[:, pl.ds(at, width)], v_a.at[n % 2], sem_in.at[n % 2, 0])]
        fresh = n == 0 or runs[n - 1][2] is not b
        if fresh:
            wide = b.shape[1]
            copies.append(
                pltpu.make_async_copy(b, v_b.at[slot_b[n], :, pl.ds(0, wide)], sem_in.at[n % 2, 1])
            )
        return copies

    slot_b = []
    for n in range(len(runs)):
        if n == 0:
            slot_b.append(0)
        elif runs[n - 1][2] is runs[n][2]:
            slot_b.append(slot_b[-1])
        else:
            slot_b.append(1 - slot_b[-1])

    started = {0: loads(0)}
    for copy in started[0]:
        copy.start()
    count = 0

    def out_wait(slot):
        pltpu.make_async_copy(stage.at[slot], stage.at[slot], sem_out.at[slot]).wait()

    for n in range(len(runs)):
        _, _, b, first, stride = runs[n]
        if n + 1 < len(runs):
            started[n + 1] = loads(n + 1)
            for copy in started[n + 1]:
                copy.start()
        for copy in started[n]:
            copy.wait()
        for r in range(width // 256):
            c = slice(r * 256, (r + 1) * 256)
            a_t[c, :] = v_a[n % 2, :, c].astype(F32).T.astype(BF16)
        sb = slot_b[n]
        base = count

        def step(t, base=base, first=first, stride=stride, sb=sb):
            slot = (base + t) % 2

            @pl.when(base + t >= 2)
            def _():
                out_wait(slot)
            res = dot_nn(a_t[...], v_b[sb, :, pl.ds(pl.multiple_of(t * tile, tile), tile)]).astype(BF16)
            for i in range(per):
                for j in range(cols):
                    stage[slot, i * cols + j] = res[i * side:(i + 1) * side, j * side:(j + 1) * side]
            for i in range(per):
                for j in range(cols):
                    dst = slot_ref[first + i * stride + t * cols + j]
                    pltpu.make_async_copy(stage.at[slot, i * cols + j], out.at[dst], sem_out.at[slot]).start()

        steps = b.shape[1] // tile
        pl.loop(0, steps)(step)
        count += steps
    out_wait(0)
    out_wait(1)


def run_wgrad(slot_of, h1, att, h2, g, dqkv, da, dz, dy, side):
    rows, width = h1.shape
    tile = 512
    blocks = slot_of.shape[0]
    return pl.pallas_call(
        functools.partial(wgrad_kernel, side=side, tile=tile),
        out_shape=sds((blocks, side, side), BF16),
        in_specs=[smem()] + [hbm()] * 8,
        out_specs=hbm(),
        scratch_shapes=[
            pltpu.VMEM((2, rows, width), BF16),
            pltpu.VMEM((2, rows, FF), BF16),
            pltpu.VMEM((width, rows), BF16),
            pltpu.VMEM((2, (width // side) * (tile // side), side, side), BF16),
            pltpu.SemaphoreType.DMA((2, 2)),
            pltpu.SemaphoreType.DMA((2,)),
        ],
        compiler_params=params(),
        name="wgrad",
    )(slot_of, h1, att, h2, g, dqkv, da, dz, dy)


def whereami():
    g = lax.axis_index("grp")
    d = lax.axis_index("dev")
    core = lax.rem(d, 2)
    x = lax.rem(d // 2, 2)
    y = d // 4
    over_x = d + 2 - 4 * x
    over_y = d + 4 - 8 * y
    across = over_x + 4 - 8 * y
    sibling = d + 1 - 2 * core
    return g, d, over_x, over_y, across, sibling


def near_order(t, g, ng):
    t = ng - 1 - t
    low = jnp.where(t < ng - 1 - g, ng - 1 - t, t - (ng - 1 - g))
    high = jnp.where(t < g, t, ng - 1 - (t - g))
    return jnp.where(2 * g < ng, low, high)


def greet(g, ng, peers):
    barrier = pltpu.get_barrier_semaphore()
    for peer in peers:
        pl.semaphore_signal(barrier, inc=1, device_id=(g, peer), device_id_type=MESH)

    d = lax.axis_index("dev")

    @pl.when(g > 0)
    def _():
        pl.semaphore_signal(barrier, inc=1, device_id=(g - 1, d), device_id_type=MESH)

    @pl.when(g < ng - 1)
    def _():
        pl.semaphore_signal(barrier, inc=1, device_id=(g + 1, d), device_id_type=MESH)

    ends = (g > 0).astype(jnp.int32) + (g < ng - 1).astype(jnp.int32)
    pl.semaphore_wait(barrier, len(peers) + ends)


def slot_cuts(count):
    third = 2 * (count // 12)
    first = (count - third) // 2
    return first, count - third - first, third // 2, third // 2


def gather_kernel(w_ref, out, own, local_sem, zs, zr, cs, cr, ss, sr, *, ng, nd):
    count = w_ref.shape[0]
    na, nb, nc1, nc2 = slot_cuts(count)
    flat = na + nb
    nc = nc1 + nc2
    g, d, over_x, over_y, across, sibling = whereami()
    columns = (d, over_x, over_y, across)
    own[...] = w_ref[...].astype(BF16)
    greet(g, ng, (over_x, over_y, sibling))

    def region(gz, dev, first=0, size=count):
        return out.at[pl.ds((gz * nd + dev) * count + first, size)]

    def wide(t):
        return count if t == 0 else flat

    def kind(n, t):
        return (
            (d, 0, wide(t), over_x),
            (d, 0, wide(t), over_y),
            (d, 0, wide(t), sibling),
            (over_x, 0, na, over_y),
            (over_y, na, nb, over_x),
            (over_x, 0, wide(t), sibling),
            (over_y, 0, wide(t), sibling),
            (across, 0, na, sibling),
            (across, na, nb, sibling),
            (over_x, flat, nc1, over_y),
            (over_y, flat + nc1, nc2, over_x),
            (across, flat, nc1, sibling),
            (across, flat + nc1, nc2, sibling),
            (d, flat, nc, sibling),
            (over_x, flat, nc, sibling),
            (over_y, flat, nc, sibling),
            (across, flat, nc, sibling),
        )[n]

    def kinds(t):
        return range(13) if t == 0 else tuple(range(9)) + tuple(range(13, 17))

    def plane(n, t, src=None):
        gz = near_order(t, g, ng)
        dev, first, size, to = kind(n, t)
        at = region(gz, dev, first, size)
        return remote(at if src is None else src, at, ss.at[n, gz], sr.at[n, gz], (g, to))

    def landed(n, t, dev):
        gz = near_order(t, g, ng)
        _, first, size, _ = kind(n, t)
        arrived(region(gz, dev, first, size), sr.at[n, gz])

    def line(gz, up, src=None):
        at = region(gz, d, 0, flat)
        to = g + 1 if up else g - 1
        return remote(at if src is None else src, at, zs.at[gz, int(up)], zr.at[gz], (to, d))

    def corner_line(gz, c, up, src=None):
        at = region(gz, columns[c], flat, nc)
        to = g + 1 if up else g - 1
        return remote(at if src is None else src, at, cs.at[gz, c, int(up)], cr.at[gz, c], (to, d))

    def both_ways(gz, make):
        @pl.when((gz <= g) & (g < ng - 1))
        def _():
            make(True)

        @pl.when((gz >= g) & (g > 0))
        def _():
            make(False)

    mine = pltpu.make_async_copy(own, region(g, d), local_sem.at[0])
    mine.start()

    def column(t):
        gz = near_order(t, g, ng)
        if t == 0:
            both_ways(gz, lambda up: line(gz, up, cut(own, 0, flat)).start())
            for n in range(3):
                plane(n, t, own).start()
            both_ways(gz, lambda up: corner_line(gz, 0, up, cut(own, flat, nc)).start())
            return
        arrived(region(gz, d, 0, flat), zr.at[gz])
        both_ways(gz, lambda up: line(gz, up).start())
        for n in range(3):
            plane(n, t).start()

    def sides(t):
        gz = near_order(t, g, ng)
        landed(0, t, over_x)
        plane(3, t).start()
        if t == 0:
            plane(9, t).start()
            both_ways(gz, lambda up: corner_line(gz, 1, up).start())
        plane(5, t).start()
        landed(1, t, over_y)
        plane(4, t).start()
        if t == 0:
            plane(10, t).start()
            both_ways(gz, lambda up: corner_line(gz, 2, up).start())
        plane(6, t).start()

    def corner(t):
        gz = near_order(t, g, ng)
        if t == 0:
            landed(9, t, across)
            landed(10, t, across)
            both_ways(gz, lambda up: corner_line(gz, 3, up).start())
            plane(11, t).start()
            plane(12, t).start()
        landed(3, t, across)
        plane(7, t).start()
        landed(4, t, across)
        plane(8, t).start()

    def far_corner(t):
        gz = near_order(t, g, ng)
        for c in range(4):
            arrived(region(gz, columns[c], flat, nc), cr.at[gz, c])
            both_ways(gz, lambda up: corner_line(gz, c, up).start())
            plane(13 + c, t).start()

    plan = [(t, f) for t in range(ng) for f in (0, 1, 2, 3) if t > 0 or f < 3]
    lag = {0: 0, 1: 1.5, 2: 2.6, 3: 2.2}
    for t, f in sorted(plan, key=lambda e: e[0] * 1.0 + lag[e[1]]):
        (column, sides, corner, far_corner)[f](t)

    for t in range(ng):
        for n in kinds(t):
            dev, _, _, to = kind(n, t)
            if to is sibling:
                landed(n, t, dev + sibling - d)
    mine.wait()
    for t in range(ng):
        gz = near_order(t, g, ng)
        for n in kinds(t):
            plane(n, t).wait_send()
        both_ways(gz, lambda up: line(gz, up).wait_send())
        for c in range(4):
            both_ways(gz, lambda up: corner_line(gz, c, up).wait_send())


def run_gather(w, ng, nd):
    count, side, _ = w.shape
    dma = pltpu.SemaphoreType.DMA
    return pl.pallas_call(
        functools.partial(gather_kernel, ng=ng, nd=nd),
        out_shape=sds((ng * nd * count, side, side), BF16),
        in_specs=[vmem()],
        out_specs=hbm(),
        scratch_shapes=[
            pltpu.VMEM((count, side, side), BF16),
            dma((1,)),
            dma((ng, 2)),
            dma((ng,)),
            dma((ng, 4, 2)),
            dma((ng, 4)),
            dma((17, ng)),
            dma((17, ng)),
        ],
        compiler_params=params(collective_id=0, has_side_effects=True),
        name="gather",
    )(w)


def add_blocks(dst, src, size):
    step = 4 if size % 4 == 0 else 2 if size % 2 == 0 else 1

    @pl.loop(0, size // step)
    def _(n):
        for k in range(step):
            dst[n * step + k] = dst[n * step + k] + src[n * step + k]


def scatter_kernel(
    grads, vec_ref, out_ref, vout_ref,
    mine, r0, r1y, r1x, r2x, r2y, rz, cz, cy, cx, cx2, cy2, vwork, vxy, vz,
    load, s0, w0, s1, w1, s2, w2, sz, wz, sc, wc, s3, w3, vs, vw, *, ng, nd
):
    count = out_ref.shape[0]
    na, nb, nc1, nc2 = slot_cuts(count)
    flat = na + nb
    nc = nc1 + nc2
    g, d, over_x, over_y, across, sibling = whereami()
    columns = (d, over_x, over_y, across)

    def region(gz, dev):
        return grads.at[pl.ds((gz * nd + dev) * count, count)]

    def order(t):
        return near_order(ng - 1 - t, g, ng)

    for t in range(ng):
        for c in range(4):
            pltpu.make_async_copy(region(order(t), columns[c]), mine.at[order(t), c], load.at[order(t), c]).start()
    vwork[0] = vec_ref[...]
    greet(g, ng, (over_x, over_y, sibling))

    def to_sibling(gz, c):
        return remote(
            region(gz, columns[c] + sibling - d), r0.at[gz, c], s0.at[gz, c], w0.at[gz, c], (g, sibling)
        )

    peers = (sibling, over_x, over_y)

    def vec_copy(n):
        return remote(vwork.at[n], vxy.at[n], vs.at[n], vw.at[n], (g, peers[n]))

    vec_copy(0).start()
    for t in range(ng):
        for c in (3, 2, 1, 0):
            to_sibling(order(t), c).start()

    first = (
        (2, 0, na, r1y, 0, over_y),
        (3, 0, na, r1y, 1, over_y),
        (1, na, nb, r1x, 0, over_x),
        (3, na, nb, r1x, 1, over_x),
    )
    second = ((1, 0, na, r2x, over_x), (2, na, nb, r2y, over_y))
    third = (
        (2, flat, nc1, cy.at[0], over_y),
        (3, flat, nc1, cy.at[1], over_y),
        (1, flat + nc1, nc2, cx.at[0], over_x),
        (3, flat + nc1, nc2, cx.at[1], over_x),
        (1, flat, nc1, cx2, over_x),
        (2, flat + nc1, nc2, cy2, over_y),
    )

    def copy1(n, gz):
        c, at, size, buf, place_at, to = first[n]
        return remote(cut(mine.at[gz, c], at, size), buf.at[gz, place_at], s1.at[n, gz], w1.at[n, gz], (g, to))

    def copy2(n, gz):
        c, at, size, buf, to = second[n]
        return remote(cut(mine.at[gz, c], at, size), buf.at[gz], s2.at[n, gz], w2.at[n, gz], (g, to))

    def copy3(n):
        c, at, size, buf, to = third[n]
        return remote(cut(mine.at[g, c], at, size), buf, s3.at[n], w3.at[n], (g, to))

    def flat_part(gz):
        return cut(mine.at[gz, 0], 0, flat)

    def corner_part(gz):
        return mine.at[gz, :, pl.ds(flat, nc)]

    def line(gz, part, buf, sends, waits, up):
        at = gz if up else jnp.where(gz < g - 1, gz, ng)
        to = g + 1 if up else g - 1
        return remote(part(gz), buf.at[at], sends.at[gz], waits.at[at], (to, d))

    def pass_on(gz, part, buf, sends, waits, gather):
        @pl.when(gz > g)
        def _():
            @pl.when(g > 0)
            def _():
                arrived(buf.at[gz], waits.at[gz])
                gather(gz)
            line(gz, part, buf, sends, waits, True).start()

        @pl.when(gz < g)
        def _():
            @pl.when(g < ng - 1)
            def _():
                arrived(buf.at[gz], waits.at[gz])
                gather(gz)
            line(gz, part, buf, sends, waits, False).start()

    def gather_flat(gz):
        add_blocks(flat_part(gz), rz.at[gz], flat)

    def gather_corner(at, gz):
        for c in range(4):
            add_blocks(cut(mine.at[gz, c], flat, nc), cz.at[at, c], nc)

    def sums0(t):
        gz = order(t)
        for c in (3, 2, 1, 0):
            pltpu.make_async_copy(region(gz, columns[c]), mine.at[gz, c], load.at[gz, c]).wait()
            arrived(r0.at[gz, c], w0.at[gz, c])
            add_blocks(mine.at[gz, c], r0.at[gz, c], count)
            if t < ng - 1:
                sends0(t, c)

    def sends0(t, c):
        gz = order(t)
        for n in {3: (1, 3), 2: (0,), 1: (2,), 0: ()}[c]:
            copy1(n, gz).start()

    def along0(t):
        pass_on(order(t), corner_part, cz, sc, wc, lambda gz: gather_corner(gz, gz))

    def stage1(t):
        gz = order(t)
        arrived(r1y.at[gz, 1], w1.at[1, gz])
        add_blocks(cut(mine.at[gz, 1], 0, na), r1y.at[gz, 1], na)
        copy2(0, gz).start()
        arrived(r1x.at[gz, 1], w1.at[3, gz])
        add_blocks(cut(mine.at[gz, 2], na, nb), r1x.at[gz, 1], nb)
        copy2(1, gz).start()
        arrived(r1y.at[gz, 0], w1.at[0, gz])
        add_blocks(cut(mine.at[gz, 0], 0, na), r1y.at[gz, 0], na)
        arrived(r1x.at[gz, 0], w1.at[2, gz])
        add_blocks(cut(mine.at[gz, 0], na, nb), r1x.at[gz, 0], nb)

    def stage2(t):
        gz = order(t)
        arrived(r2x.at[gz], w2.at[0, gz])
        add_blocks(cut(mine.at[gz, 0], 0, na), r2x.at[gz], na)
        arrived(r2y.at[gz], w2.at[1, gz])
        add_blocks(cut(mine.at[gz, 0], na, nb), r2y.at[gz], nb)
        if t < ng - 1:
            pass_on(gz, flat_part, rz, sz, wz, gather_flat)

    def corner0():
        @pl.when(g > 0)
        def _():
            arrived(cz.at[g], wc.at[g])
            gather_corner(g, g)

        @pl.when(g < ng - 1)
        def _():
            arrived(cz.at[ng], wc.at[ng])
            gather_corner(ng, g)
        for n in range(4):
            copy3(n).start()

    def corner1():
        arrived(cy.at[1], w3.at[1])
        add_blocks(cut(mine.at[g, 1], flat, nc1), cy.at[1], nc1)
        copy3(4).start()
        arrived(cx.at[1], w3.at[3])
        add_blocks(cut(mine.at[g, 2], flat + nc1, nc2), cx.at[1], nc2)
        copy3(5).start()
        arrived(cy.at[0], w3.at[0])
        add_blocks(cut(mine.at[g, 0], flat, nc1), cy.at[0], nc1)
        arrived(cx.at[0], w3.at[2])
        add_blocks(cut(mine.at[g, 0], flat + nc1, nc2), cx.at[0], nc2)

    def corner2():
        arrived(cx2, w3.at[4])
        add_blocks(cut(mine.at[g, 0], flat, nc1), cx2, nc1)
        arrived(cy2, w3.at[5])
        add_blocks(cut(mine.at[g, 0], flat + nc1, nc2), cy2, nc2)

    def vec_step(n):
        arrived(vxy.at[n], vw.at[n])
        total = vwork[n] + vxy[n]
        if n < 2:
            vwork[n + 1] = total
            vec_copy(n + 1).start()
        else:
            vz[g] = total

    def vec_line(gz, up):
        to = g + 1 if up else g - 1
        return remote(vz.at[gz], vz.at[gz], vs.at[3 + 2 * gz + int(up)], vw.at[3 + gz], (to, d))

    last = ng - 1
    sums0(0)
    vec_step(0)
    sums0(1)
    vec_step(1)
    along0(0)
    stage1(0)
    for t in range(2, last):
        sums0(t)
        along0(t - 1)
        stage1(t - 1)
        stage2(t - 2)
    vec_step(2)

    @pl.when(g < ng - 1)
    def _():
        vec_line(g, True).start()

    @pl.when(g > 0)
    def _():
        vec_line(g, False).start()
    sums0(last)
    along0(last - 1)
    stage1(last - 1)
    for c in (3, 2, 1):
        sends0(last, c)
    corner0()
    stage2(last - 2)
    for n in range(1, ng):
        gz = near_order(n, g, ng)
        arrived(vz.at[gz], vw.at[3 + gz])

        @pl.when((gz < g) & (g < ng - 1))
        def _():
            vec_line(gz, True).start()

        @pl.when((gz > g) & (g > 0))
        def _():
            vec_line(gz, False).start()
    total = vz[0]
    for z in range(1, ng):
        total = total + vz[z]
    vout_ref[...] = total
    stage2(last - 1)
    stage1(last)
    corner1()
    stage2(last)
    corner2()

    @pl.when(g > 0)
    def _():
        arrived(rz.at[g], wz.at[g])

    @pl.when(g < ng - 1)
    def _():
        arrived(rz.at[ng], wz.at[ng])

    @pl.when((g > 0) & (g < ng - 1))
    def _():
        @pl.loop(0, flat // 2)
        def _(n):
            for k in range(2):
                i = 2 * n + k
                out_ref[i] = mine[g, 0, i].astype(F32) + rz[g, i].astype(F32) + rz[ng, i].astype(F32)

    @pl.when(g == 0)
    def _():
        @pl.loop(0, flat // 2)
        def _(n):
            for k in range(2):
                i = 2 * n + k
                out_ref[i] = mine[g, 0, i].astype(F32) + rz[ng, i].astype(F32)

    @pl.when((g > 0) & (g == ng - 1))
    def _():
        @pl.loop(0, flat // 2)
        def _(n):
            for k in range(2):
                i = 2 * n + k
                out_ref[i] = mine[g, 0, i].astype(F32) + rz[g, i].astype(F32)

    for i in range(flat, count):
        out_ref[i] = mine[g, 0, i].astype(F32)

    for t in range(ng):
        gz = order(t)
        for c in range(4):
            to_sibling(gz, c).wait_send()
        for n in range(4):
            copy1(n, gz).wait_send()
        for n in range(2):
            copy2(n, gz).wait_send()
        if t < ng - 1:
            arrived(flat_part(gz), sz.at[gz])
            arrived(corner_part(gz), sc.at[gz])
    for n in range(6):
        copy3(n).wait_send()
    for n in range(3):
        vec_copy(n).wait_send()
    for n in range(ng):
        gz = near_order(n, g, ng)

        @pl.when((gz <= g) & (g < ng - 1))
        def _():
            vec_line(gz, True).wait_send()

        @pl.when((gz >= g) & (g > 0))
        def _():
            vec_line(gz, False).wait_send()


def run_scatter(grads, vec, ng, nd):
    blocks, side, _ = grads.shape
    count = blocks // (ng * nd)
    na, nb, nc1, nc2 = slot_cuts(count)
    flat = na + nb
    dma = pltpu.SemaphoreType.DMA

    def buf(*lead):
        return pltpu.VMEM(lead + (side, side), BF16)

    return pl.pallas_call(
        functools.partial(scatter_kernel, ng=ng, nd=nd),
        out_shape=(sds((count, side, side), F32), sds(vec.shape, F32)),
        in_specs=[hbm(), vmem()],
        out_specs=(vmem(), vmem()),
        scratch_shapes=[
            buf(ng, 4, count),
            buf(ng, 4, count),
            buf(ng, 2, na),
            buf(ng, 2, nb),
            buf(ng, na),
            buf(ng, nb),
            buf(ng + 1, flat),
            buf(ng + 1, 4, nc1 + nc2),
            buf(2, nc1),
            buf(2, nc2),
            buf(nc1),
            buf(nc2),
            pltpu.VMEM((3,) + vec.shape, F32),
            pltpu.VMEM((3,) + vec.shape, F32),
            pltpu.VMEM((ng,) + vec.shape, F32),
            dma((ng, 4)),
            dma((ng, 4)),
            dma((ng, 4)),
            dma((4, ng)),
            dma((4, ng)),
            dma((2, ng)),
            dma((2, ng)),
            dma((ng,)),
            dma((ng + 1,)),
            dma((ng,)),
            dma((ng + 1,)),
            dma((6,)),
            dma((6,)),
            dma((3 + 2 * ng,)),
            dma((3 + ng,)),
        ],
        compiler_params=params(collective_id=1, has_side_effects=True),
        name="scatter",
    )(grads, vec)


def blocks_kernel(g_ref, w_ref, ls_ref, rs_ref, lr_ref, rr_ref, wg_out, nl_out, nr_out, nw_out):
    for i in range(g_ref.shape[0]):
        grad = g_ref[i]
        wg_out[i] = grad
        hi = grad.astype(BF16)
        low = (grad - hi.astype(F32)).astype(BF16)
        nl_out[i] = 0.5 * ls_ref[i] + 0.5 * dot_nt(hi, hi)
        turned = grad.T
        hi_t = turned.astype(BF16)
        nr_out[i] = 0.5 * rs_ref[i] + 0.5 * dot_nt(hi_t, hi_t)
        left = lr_ref[i]
        left_hi = left.astype(BF16)
        left_low = (left - left_hi.astype(F32)).astype(BF16)
        shaped = dot_nn(left_hi, hi) + dot_nn(left_hi, low) + dot_nn(left_low, hi)
        right = rr_ref[i]
        right_hi = right.astype(BF16)
        right_low = (right - right_hi.astype(F32)).astype(BF16)
        sh_hi = shaped.astype(BF16)
        sh_low = (shaped - sh_hi.astype(F32)).astype(BF16)
        shaped = dot_nn(sh_hi, right_hi) + dot_nn(sh_low, right_hi) + dot_nn(sh_hi, right_low)
        nw_out[i] = w_ref[i] - weight_rate * shaped


def run_blocks(grads, weights, left_stats, right_stats, left_roots, right_roots):
    count, side, _ = grads.shape
    step = math.gcd(count, 4)
    spec = pl.BlockSpec((step, side, side), lambda n: (n, 0, 0))
    return pl.pallas_call(
        blocks_kernel,
        grid=(count // step,),
        out_shape=tuple([sds(grads.shape, F32)] * 4),
        in_specs=[spec] * 6,
        out_specs=tuple([spec] * 4),
        compiler_params=params(),
        name="blocks",
    )(grads, weights, left_stats, right_stats, left_roots, right_roots)


def local(
    inputs,
    cotangent,
    weight_slots,
    slot_block,
    left_stats,
    right_stats,
    left_roots,
    right_roots,
    vectors,
    span_start,
):
    seq_count, tok_count, width = inputs.shape
    rows = seq_count * tok_count
    nd = lax.axis_size("dev")
    ng = lax.axis_size("grp")
    side = weight_slots.shape[1]
    hpd = H // nd
    lanes = width // nd
    head = lax.axis_index("dev") * hpd + jnp.arange(hpd, dtype=jnp.int32)
    slopes = jnp.exp2(-8.0 * (head.astype(F32) + 1.0) / H)
    slot_of = invert_order(slot_block)
    vec = vectors.reshape(-1, width)
    x = inputs.reshape(rows, width)
    dy = cotangent.reshape(rows, width)

    direct = nd == 8
    if direct:
        gath = run_gather(weight_slots, ng, nd)
    else:
        gath = lax.all_gather(weight_slots.astype(BF16), ("grp", "dev"), axis=0, tiled=True)
    h1, qkv = run_qkv(slot_of, x, vec, gath, nd)
    qkv, o, o32, lse = run_attn_fwd(
        span_start, slopes, qkv.reshape(nd, 3, seq_count, tok_count, lanes), hpd
    )
    act, att, h2, g, dz, da, dx1, do, sums2 = run_mlp(
        slot_of, o.reshape(nd, rows, lanes), x, dy, vec, gath, nd
    )
    do = do.reshape(nd, seq_count, tok_count, lanes)
    dqkv = run_attn_bwd(span_start, slopes, qkv, do, o32, lse, hpd).reshape(nd, 3, rows, lanes)
    ig, cat, sums1 = run_dh1(slot_of, dqkv, x, dx1, vec, gath, nd)
    grads = run_wgrad(slot_of, h1, att, h2, g, cat, da, dz, dy, side)

    s2 = jnp.sum(sums2.reshape(-1, 8, width), axis=1)
    s1 = jnp.sum(sums1.reshape(-1, 8, width), axis=1)
    bo, gain2, shift2, bdown = [s2[n:n + 1] for n in range(4)]
    gain1, shift1, bq, bv = [s1[n:n + 1] for n in range(4)]
    local_vector = jnp.concatenate(
        [gain1, shift1, bq, bv, bo, gain2, shift2, bdown, s2[4:]], axis=0
    )
    if direct:
        weight_grads, vector_grads = run_scatter(grads, local_vector, ng, nd)
        vector_grads = vector_grads.reshape(-1)
    else:
        vector_grads = lax.psum(local_vector.reshape(-1), ("grp", "dev"))
        weight_grads = lax.psum_scatter(grads, ("grp", "dev"), scatter_dimension=0, tiled=True)
        weight_grads = weight_grads.astype(F32)
    tokens_all = rows * nd * ng
    new_vectors = vectors - vector_rate / math.sqrt(tokens_all) * vector_grads

    weight_grads, new_left, new_right, new_weights = run_blocks(
        weight_grads, weight_slots, left_stats, right_stats, left_roots, right_roots
    )
    return (
        act.reshape(inputs.shape),
        ig.reshape(inputs.shape),
        weight_grads,
        new_left,
        new_right,
        new_weights,
        vector_grads,
        new_vectors,
    )


def solution(mesh):
    return jax.shard_map(
        local,
        mesh=mesh,
        in_specs=(
            P("grp", "dev", None),
            P("grp", "dev", None),
            P(("grp", "dev"), None, None),
            P(),
            P(("grp", "dev"), None, None),
            P(("grp", "dev"), None, None),
            P(("grp", "dev"), None, None),
            P(("grp", "dev"), None, None),
            P(),
            P("grp"),
        ),
        out_specs=(
            P("grp", "dev", None),
            P("grp", "dev", None),
            P(("grp", "dev"), None, None),
            P(("grp", "dev"), None, None),
            P(("grp", "dev"), None, None),
            P(("grp", "dev"), None, None),
            P(),
            P(),
        ),
        check_vma=False,
    )
```

```python
import functools
import math

import jax
import jax.numpy as jnp
from jax import lax
from jax.experimental import pallas as pl
from jax.experimental.pallas import tpu as pltpu
from jax.sharding import PartitionSpec as P

H = 16
FF = 4096
PIC = 256

eps = 1e-05
weight_rate = 0.5
vector_rate = 0.5
big_negative = -1e30
highest = lax.Precision.HIGHEST
F32 = jnp.float32
BF16 = jnp.bfloat16
LOG2E = 1.4426950408889634
MIB = 1024 * 1024

GAIN1, SHIFT1, BQ, BV, BO, GAIN2, SHIFT2, BDOWN, BUP = range(9)


def dot_nn(a, b):
    return lax.dot_general(a, b, (((1,), (0,)), ((), ())), preferred_element_type=F32)


def dot_nt(a, b):
    return lax.dot_general(a, b, (((1,), (1,)), ((), ())), preferred_element_type=F32)


def vmem():
    return pl.BlockSpec(memory_space=pltpu.VMEM)


def smem():
    return pl.BlockSpec(memory_space=pltpu.SMEM)


def hbm():
    return pl.BlockSpec(memory_space=pl.ANY)


def sds(shape, dtype):
    return jax.ShapeDtypeStruct(shape, dtype)


def params(mib=58, **kw):
    return pltpu.CompilerParams(vmem_limit_bytes=mib * MIB, **kw)


def layer_stats(v):
    middle = jnp.mean(v, axis=-1, keepdims=True)
    centred = v - middle
    spread = jnp.mean(centred * centred, axis=-1, keepdims=True)
    return centred, lax.rsqrt(spread + eps)


def fold_rows(v):
    return jnp.sum(v.reshape(v.shape[0] // 8, 8, v.shape[1]), axis=0)


def slot_at(slot_ref, block):
    lanes = slot_ref.shape[1]
    return slot_ref[lax.div(block, lanes), lax.rem(block, lanes)]


def fetch_block(gath, slot, dst, row, col, sem, side):
    return pltpu.make_async_copy(
        gath.at[slot], dst.at[pl.ds(row, side), pl.ds(col, side)], sem
    )


def prepare(x_ref, block_ref, vin_ref, h1_ref, slot_ref, vec_ref):
    rows, width = x_ref.shape
    per = width // 128
    for r in range(vec_ref.shape[0]):
        for c in range(per):
            vec_ref[r:r + 1, c * 128:(c + 1) * 128] = vin_ref[per * r + c:per * r + c + 1, :]
    chunk = 32

    @pl.loop(0, rows // chunk)
    def _(r):
        at = pl.ds(pl.multiple_of(r * chunk, chunk), chunk)
        centred, inv = layer_stats(x_ref[at, :].astype(F32))
        h1_ref[at, :] = (
            centred * inv * vec_ref[GAIN1:GAIN1 + 1, :] + vec_ref[SHIFT1:SHIFT1 + 1, :]
        ).astype(BF16)

    tiles, lanes = slot_ref.shape
    line = lax.broadcasted_iota(jnp.int32, (8, lanes), 0)
    lane = lax.broadcasted_iota(jnp.int32, (8, lanes), 1).astype(F32)
    block = lax.broadcasted_iota(jnp.int32, (lanes, lanes), 0)
    for t in range(tiles):
        found = jnp.zeros((8, lanes), F32)
        for r in range(tiles):
            held = (block_ref[r:r + 1, :] == block + t * lanes).astype(F32).astype(BF16)
            found = found + dot_nt(jnp.where(line == 0, lane, float(r)).astype(BF16), held)
        slot_ref[t:t + 1, :] = (found[0:1] + float(lanes) * found[1:2]).astype(jnp.int32)


def prepared_shapes(x, blocks, vin):
    rows, width = x.shape
    return (
        sds((rows, width), BF16),
        sds(blocks.shape, jnp.int32),
        sds((vin.size // width, width), F32),
    )


def run_prepare(x, blocks, vin):
    return pl.pallas_call(
        prepare,
        out_shape=prepared_shapes(x, blocks, vin),
        in_specs=[vmem()] * 3,
        out_specs=tuple([vmem()] * 3),
        compiler_params=params(),
        name="prepare",
    )(x, blocks, vin)


def qkv_kernel(slot_ref, h1_ref, vec_ref, gath, out_ref, wq_out, wbuf, sems, sem_w, *, nd):
    rows, width = h1_ref.shape
    side = gath.shape[1]
    per = width // side
    lanes = out_ref.shape[3]
    for part in range(3):
        @pl.loop(0, per)
        def _(i):
            for j in range(per):
                slot = slot_at(slot_ref, i * 3 * per + part * per + j)
                fetch_block(gath, slot, wbuf.at[part], pl.multiple_of(i * side, side), j * side, sems.at[part], side).start()

    def keep(part):
        return pltpu.make_async_copy(wbuf.at[part], wq_out.at[part], sem_w.at[part])

    for part in range(3):
        pltpu.make_async_copy(wbuf.at[part], wbuf.at[part], sems.at[part]).wait()
        keep(part).start()
        for half in range(2):
            cols = slice(half * width // 2, (half + 1) * width // 2)
            res = dot_nn(h1_ref[...], wbuf[part, :, cols])
            if part == 0:
                res = res + vec_ref[BQ:BQ + 1, cols]
            if part == 2:
                res = res + vec_ref[BV:BV + 1, cols]
            res = res.astype(BF16)
            for d in range(nd // 2):
                out_ref[half * (nd // 2) + d, part, :, :] = res[:, d * lanes:(d + 1) * lanes]
    for part in range(3):
        keep(part).wait()


def run_qkv(slot_of, h1, vec, gath, nd):
    rows, width = h1.shape
    lanes = width // nd
    return pl.pallas_call(
        functools.partial(qkv_kernel, nd=nd),
        out_shape=(sds((nd, 3, rows, lanes), BF16), sds((3, width, width), BF16)),
        in_specs=[smem(), vmem(), vmem(), hbm()],
        out_specs=(vmem(), hbm()),
        scratch_shapes=[
            pltpu.VMEM((3, width, width), BF16),
            pltpu.SemaphoreType.DMA((3,)),
            pltpu.SemaphoreType.DMA((3,)),
        ],
        compiler_params=params(),
        name="qkv",
    )(slot_of, h1, vec, gath)


MESH = pl.DeviceIdType.MESH


def remote(src, dst, send, recv, device):
    return pltpu.make_async_remote_copy(
        src_ref=src, dst_ref=dst, send_sem=send, recv_sem=recv, device_id=device, device_id_type=MESH
    )


def arrived(ref, sem):
    pltpu.make_async_copy(ref, ref, sem).wait()


def cut(ref, first, size):
    return ref.at[pl.ds(first, size)]


def greet_plane(g, d, nd):
    barrier = pltpu.get_barrier_semaphore()
    for p in range(1, nd):
        pl.semaphore_signal(barrier, inc=1, device_id=(g, lax.rem(d + p, nd)), device_id_type=MESH)
    pl.semaphore_wait(barrier, nd - 1)


def landing(ref, part, source, q, tok, lanes, parts):
    if lanes % 128 == 0:
        first = (part * (ref.shape[1] // parts)) + source * lanes
        return ref.at[pl.ds(q * tok, tok), pl.ds(pl.multiple_of(first, lanes), lanes)]
    return ref.at[source, part, q]


def landing_shape(parts, nb, seqs, tok, lanes):
    if lanes % 128 == 0:
        return sds((seqs * tok, parts * nb * lanes), BF16)
    return sds((nb, parts, seqs, tok, lanes), BF16)


def side_by_side(got, parts, rows):
    if got.ndim == 2:
        return got
    nb, _, seqs, tok, lanes = got.shape
    return got.transpose(2, 3, 1, 0, 4).reshape(rows, parts * nb * lanes)


def parts3(v):
    hi = v.astype(BF16)
    mid = (v - hi.astype(F32)).astype(BF16)
    lo = (v - hi.astype(F32) - mid.astype(F32)).astype(BF16)
    return hi.astype(F32), mid.astype(F32), lo.astype(F32)


def own_lanes(h, shape, hpd, lanes):
    lane = lax.broadcasted_iota(jnp.int32, shape, 1)
    size = lanes // hpd
    return (lane >= h * size) & (lane < (h + 1) * size)


def place(values, base, tok, width):
    lane = lax.broadcasted_iota(jnp.int32, (tok, width), 1)
    out = jnp.zeros((tok, width), F32)
    for n, v in enumerate(values):
        out = jnp.where(lane == base + n, v, out)
    return out


def spare(h, hpd, lanes):
    return (lanes // hpd) * (1 - h) if hpd > 1 else 0


def column_tables(slope_ref, qbase, kbase, kfar, hpd, lanes):
    _, tok, _ = qbase.shape
    u = lax.broadcasted_iota(jnp.int32, (tok, 128), 0).astype(F32)
    for h in range(hpd):
        slope = slope_ref[h] * LOG2E
        base = spare(h, hpd, lanes)
        near = parts3(jnp.full((tok, 128), slope, F32))
        far = parts3(jnp.full((tok, 128), slope * tok, F32))
        qbase[h] = place(near + far, base, tok, 128)
        kbase[h] = place([u] * 3 + [0.0] * 3 + [1.0] * 3, base, tok, 128)
        kfar[h] = place([0.0] * 3 + [1.0] * 3, base, tok, 128)


def q_columns(q, h, hpd, columns, extra):
    tok, lanes = q.shape
    scaled = q.astype(F32) * ((lanes // hpd) ** (-0.5) * LOG2E)
    hi = scaled.astype(BF16).astype(F32)
    low = scaled - hi
    if extra:
        lane = lax.broadcasted_iota(jnp.int32, (tok, 128), 1)
        for n, v in enumerate(extra):
            columns = jnp.where(lane == spare(h, hpd, lanes) + 6 + n, v, columns)
    if hpd > 1:
        own = own_lanes(h, (tok, lanes), hpd, lanes)
        return jnp.concatenate(
            [jnp.where(own, hi, 0.0), jnp.where(own, low, columns)], axis=1
        ).astype(BF16)
    return jnp.concatenate([hi, low, columns], axis=1).astype(BF16)


def k_columns(k, h, hpd, columns):
    tok, lanes = k.shape
    wide = k.astype(F32)
    if hpd > 1:
        own = own_lanes(h, (tok, lanes), hpd, lanes)
        return jnp.concatenate([wide, jnp.where(own, wide, columns)], axis=1).astype(BF16)
    return jnp.concatenate([wide, wide, columns], axis=1).astype(BF16)


def far_side(slope, tok):
    u = lax.broadcasted_iota(jnp.int32, (tok, tok), 0)
    t = lax.broadcasted_iota(jnp.int32, (tok, tok), 1)
    after = u > t
    return (
        jnp.where(after, big_negative, 0.0),
        jnp.where(after, (2.0 * slope) * (t - u).astype(F32), 0.0),
    )


def attn_fwd_kernel(
    span_ref, slope_ref, src, got, o_got, o32_ref, lse_ref,
    qa, ka, vt, scores, corr, qbase, kbase, kfar, o_out, ss, sr, os, orr, loc, *, hpd, nd
):
    nb, _, seqs, tok, lanes = got.shape
    size = lanes // hpd
    pair = 2 * tok
    g = lax.axis_index("grp")
    d = lax.axis_index("dev")

    for q in range(seqs):
        pltpu.make_async_copy(src.at[d, :, q], got.at[d, :, q], loc.at[q]).start()
    greet_plane(g, d, nd)

    def send(q, p):
        to = lax.rem(d + p, nd)
        return remote(src.at[to, :, q], got.at[d, :, q], ss.at[q, p], sr.at[q, p], (g, to))

    def send_all(q):
        @pl.loop(1, nd)
        def _(p):
            send(q, p).start()

    send_all(0)

    def o_place(source, q):
        return landing(o_got, 0, source, q, tok, lanes, 1)

    def send_o(q, i, p):
        return remote(o_out.at[i, q], o_place(d, q), os.at[q, i], orr.at[q, p], (g, i))

    column_tables(slope_ref, qbase, kbase, kfar, hpd, lanes)
    for h in range(hpd):
        mask, span = far_side(slope_ref[h] * LOG2E, tok)
        for n, (one, two) in enumerate(((mask, mask), (span, mask), (mask, span))):
            corr[h, n, 0:tok, 0:tok] = one
            corr[h, n, tok:, tok:] = two
            corr[h, n, 0:tok, tok:] = jnp.zeros((tok, tok), F32)
            corr[h, n, tok:, 0:tok] = jnp.full((tok, tok), big_negative, F32)

    for q in range(seqs):
        pltpu.make_async_copy(src.at[d, :, q], got.at[d, :, q], loc.at[q]).wait()

        @pl.loop(1, nd)
        def _(p):
            arrived(got.at[lax.rem(d + nd - p, nd), :, q], sr.at[q, p])

        if q + 1 < seqs:
            send_all(q + 1)

        @pl.loop(0, nb)
        def _(j):
            at_j = pl.ds(pl.multiple_of(j * tok, tok), tok)
            vt[0:lanes, at_j] = got[j, 2, q].astype(F32).T.astype(BF16)
            block = jnp.full((tok, 128), j, jnp.int32).astype(F32)
            for h in range(hpd):
                qa[h, at_j, :] = q_columns(got[j, 0, q], h, hpd, qbase[h], [])
                ka[h, at_j, :] = k_columns(got[j, 1, q], h, hpd, kbase[h] + block * kfar[h])

        start = span_ref[q]

        @pl.loop(0, nb // 2)
        def _(i):
            flag = (start == i * pair).astype(jnp.int32) + 2 * (start == i * pair + tok).astype(jnp.int32)

            def at_pair(n):
                return pl.ds(pl.multiple_of(n * pair, pair), pair)

            def fold_max(v):
                return jnp.max(v.reshape(pair // 8, 8, pair), axis=0)

            def score(n, tops):
                new = []
                for h in range(hpd):
                    s = dot_nt(ka[h, at_pair(n), :], qa[h, at_pair(i), :])
                    scores[h, at_pair(n), :] = s
                    new.append(jnp.maximum(tops[h], fold_max(s)))
                return tuple(new)

            tops = lax.fori_loop(
                0, i, score, tuple([jnp.full((8, pair), big_negative, F32)] * hpd)
            )
            top = []
            for h in range(hpd):
                s = dot_nt(ka[h, at_pair(i), :], qa[h, at_pair(i), :]) + corr[h, flag]
                scores[h, at_pair(i), :] = s
                top.append(jnp.max(jnp.maximum(tops[h], fold_max(s)), axis=0, keepdims=True))

            def weigh(n, state):
                new = []
                for h in range(hpd):
                    acc, total = state[h]
                    p = jnp.exp2(scores[h, at_pair(n), :] - top[h])
                    total = total + jnp.sum(p.reshape(pair // 8, 8, pair), axis=0)
                    acc = acc + dot_nn(vt[h * size:(h + 1) * size, at_pair(n)], p.astype(BF16))
                    new.append((acc, total))
                return tuple(new)

            state = lax.fori_loop(
                0,
                i + 1,
                weigh,
                tuple([(jnp.zeros((size, pair), F32), jnp.zeros((8, pair), F32))] * hpd),
            )
            outs = []
            logs = []
            for h in range(hpd):
                acc, total = state[h]
                total = jnp.sum(total, axis=0, keepdims=True)
                outs.append(acc / total)
                logs.append(jnp.broadcast_to(top[h] + jnp.log2(total), (128 // hpd, pair)))
            out = (jnp.concatenate(outs, axis=0) if hpd > 1 else outs[0]).T
            log = (jnp.concatenate(logs, axis=0) if hpd > 1 else logs[0]).T
            for k in range(2):
                at = 2 * i + k
                o32_ref[at, q] = out[k * tok:(k + 1) * tok]
                o_out[at, q] = out[k * tok:(k + 1) * tok].astype(BF16)
                lse_ref[at, q] = log[k * tok:(k + 1) * tok]

                @pl.when(at == d)
                def _():
                    pltpu.make_async_copy(o_out.at[at, q], o_place(d, q), os.at[q, at]).start()

                @pl.when(at != d)
                def _():
                    send_o(q, at, lax.rem(at - d + nd, nd)).start()

    for q in range(seqs):
        @pl.loop(1, nd)
        def _(p):
            arrived(o_place(lax.rem(d + nd - p, nd), q), orr.at[q, p])
            send(q, p).wait_send()

        @pl.loop(0, nd)
        def _(i):
            arrived(o_out.at[i, q], os.at[q, i])


def run_attn_fwd(span, slopes, qkv, hpd):
    nb, _, seqs, tok, lanes = qkv.shape
    t = nb * tok
    dma = pltpu.SemaphoreType.DMA
    return pl.pallas_call(
        functools.partial(attn_fwd_kernel, hpd=hpd, nd=nb),
        out_shape=(
            sds(qkv.shape, BF16),
            landing_shape(1, nb, seqs, tok, lanes),
            sds((nb, seqs, tok, lanes), F32),
            sds((nb, seqs, tok, 128), F32),
        ),
        in_specs=[smem(), smem(), hbm()],
        out_specs=(vmem(), vmem(), vmem(), vmem()),
        scratch_shapes=[
            pltpu.VMEM((hpd, t, 256), BF16),
            pltpu.VMEM((hpd, t, 256), BF16),
            pltpu.VMEM((lanes, t), BF16),
            pltpu.VMEM((hpd, t, 2 * tok), F32),
            pltpu.VMEM((hpd, 3, 2 * tok, 2 * tok), F32),
            pltpu.VMEM((hpd, tok, 128), F32),
            pltpu.VMEM((hpd, tok, 128), F32),
            pltpu.VMEM((hpd, tok, 128), F32),
            pltpu.VMEM((nb, seqs, tok, lanes), BF16),
            dma((seqs, nb)),
            dma((seqs, nb)),
            dma((seqs, nb)),
            dma((seqs, nb)),
            dma((seqs,)),
        ],
        compiler_params=params(collective_id=2, has_side_effects=True),
        name="attn_fwd",
    )(span, slopes, qkv)


def attn_bwd_kernel(
    span_ref, slope_ref, qkv_ref, do_src, o32_ref, lse_ref, got,
    do_got, out, qa, ka, kt, va, qm, da, dm, dqt, corr, qbase, kbase, kfar, dk_ref, dv_ref,
    ss, sr, gs, gr, loc, *, hpd, nd
):
    nb, _, seqs, tok, lanes = qkv_ref.shape
    size = lanes // hpd
    unit = size ** (-0.5)
    g = lax.axis_index("grp")
    d = lax.axis_index("dev")

    def own_copy(q):
        return pltpu.make_async_copy(do_src.at[d, q], do_got.at[d, q], loc.at[q])

    for q in range(seqs):
        own_copy(q).start()
    greet_plane(g, d, nd)

    def send(q, p):
        to = lax.rem(d + p, nd)
        return remote(do_src.at[to, q], do_got.at[d, q], ss.at[q, p], sr.at[q, p], (g, to))

    def send_all(q):
        @pl.loop(1, nd)
        def _(p):
            send(q, p).start()

    send_all(0)

    def place_back(kind, source, q):
        return landing(got, kind, source, q, tok, lanes, 3)

    def back(q, kind, p):
        to = lax.rem(d + p, nd)
        return remote(
            out.at[to, kind, q], place_back(kind, d, q), gs.at[q, kind, p], gr.at[q, kind, p], (g, to)
        )

    def back_own(q, kind):
        return pltpu.make_async_copy(out.at[d, kind, q], place_back(kind, d, q), gs.at[q, kind, 0])

    for h in range(hpd):
        mask, span = far_side(slope_ref[h] * LOG2E, tok)
        for n, table in enumerate((mask, span)):
            corr[h, n, :, 0:tok] = table
            corr[h, n, :, tok:] = jnp.zeros((tok, tok), F32)
    column_tables(slope_ref, qbase, kbase, kfar, hpd, lanes)

    for q in range(seqs):
        @pl.loop(0, nb)
        def _(j):
            at_j = pl.ds(pl.multiple_of(j * tok, tok), tok)
            qj = qkv_ref[j, 0, q]
            kj = qkv_ref[j, 1, q]
            vj = qkv_ref[j, 2, q].astype(F32)
            kt[:, at_j] = kj.astype(F32).T.astype(BF16)
            dqt[:, at_j] = jnp.zeros((lanes, tok), F32)
            block = jnp.full((tok, 128), j, jnp.int32).astype(F32)
            for h in range(hpd):
                low = lse_ref[j, q][:, h * (128 // hpd):h * (128 // hpd) + 1]
                extra = [-p for p in parts3(low)]
                qa[h, at_j, :] = q_columns(qj, h, hpd, qbase[h], extra)
                ka[h, j] = k_columns(kj, h, hpd, kbase[h] + block * kfar[h])
                if hpd > 1:
                    own = own_lanes(h, (tok, lanes), hpd, lanes)
                    qm[h, at_j, :] = jnp.where(own, qj.astype(F32), 0.0).astype(BF16)
                    va[h, j] = jnp.where(own, vj, kbase[h]).astype(BF16)
                else:
                    qm[h, at_j, :] = qj
                    va[h, j] = jnp.concatenate([vj, kbase[h][:, 0:lanes]], axis=1).astype(BF16)

        own_copy(q).wait()

        @pl.loop(1, nd)
        def _(p):
            arrived(do_got.at[lax.rem(d + nd - p, nd), q], sr.at[q, p])

        if q + 1 < seqs:
            send_all(q + 1)

        @pl.loop(0, nb)
        def _(j):
            at_j = pl.ds(pl.multiple_of(j * tok, tok), tok)
            do = do_got[j, q].astype(F32)
            prod = do * o32_ref[j, q]
            for h in range(hpd):
                if hpd > 1:
                    own = own_lanes(h, (tok, lanes), hpd, lanes)
                    delta = jnp.sum(jnp.where(own, prod, 0.0), axis=1, keepdims=True)
                    extra = place([-p for p in parts3(delta)], spare(h, hpd, lanes) + 6, tok, lanes)
                    da[h, at_j, :] = jnp.where(own, do, extra).astype(BF16)
                    dm[h, at_j, :] = jnp.where(own, do, 0.0).astype(BF16)
                else:
                    delta = jnp.sum(prod, axis=1, keepdims=True)
                    extra = place([-p for p in parts3(delta)], 6, tok, lanes)
                    da[h, at_j, :] = jnp.concatenate([do, extra], axis=1).astype(BF16)
                    dm[h, at_j, :] = do.astype(BF16)

        start = span_ref[q]

        @pl.loop(0, nb)
        def _(n):
            j = lax.rem(d + n, nb)
            at_j = pl.ds(pl.multiple_of(j * tok, tok), tok)
            flag = (start == j * tok).astype(jnp.int32)

            def tile(i, width, near):
                at_i = pl.ds(pl.multiple_of(i * tok, tok), width)
                dk = None
                for h in range(hpd):
                    s = dot_nt(ka[h, j], qa[h, at_i, :])
                    if near:
                        s = s + corr[h, flag, :, 0:width]
                    p = jnp.exp2(s)
                    ds = (p * dot_nt(va[h, j], da[h, at_i, :])).astype(BF16)
                    dv_h = dot_nn(p.astype(BF16), dm[h, at_i, :])
                    dk_h = dot_nn(ds, qm[h, at_i, :])
                    dk = dk_h if dk is None else dk + dk_h
                    dv = dv_h if h == 0 else dv + dv_h
                    rows = slice(h * size, (h + 1) * size)
                    dqt[rows, at_i] += dot_nn(kt[rows, at_j], ds)
                if near:
                    dk_ref[...] = dk
                    dv_ref[...] = dv
                else:
                    dk_ref[...] += dk
                    dv_ref[...] += dv

            odd = lax.rem(nb - j, 2)

            @pl.when(odd == 1)
            def _():
                tile(j, tok, True)

            @pl.when(odd == 0)
            def _():
                tile(j, 2 * tok, True)

            @pl.loop(0, (nb - j - 1) // 2)
            def _(m):
                tile(j + 2 - odd + 2 * m, 2 * tok, False)

            out[j, 1, q] = (dk_ref[...] * unit).astype(BF16)
            out[j, 2, q] = dv_ref[...].astype(BF16)

            for kind in (1, 2):
                @pl.when(n == 0)
                def _():
                    back_own(q, kind).start()

                @pl.when(n > 0)
                def _():
                    back(q, kind, n).start()

        @pl.loop(0, nb)
        def _(n):
            j = lax.rem(d + n, nb)
            at_j = pl.ds(pl.multiple_of(j * tok, tok), tok)
            out[j, 0, q] = (dqt[:, at_j].T * unit).astype(BF16)

            @pl.when(n == 0)
            def _():
                back_own(q, 0).start()

            @pl.when(n > 0)
            def _():
                back(q, 0, n).start()

    for q in range(seqs):
        for kind in range(3):
            back_own(q, kind).wait()

        @pl.loop(1, nd)
        def _(p):
            send(q, p).wait_send()
            source = lax.rem(d + nd - p, nd)
            for kind in range(3):
                back(q, kind, p).wait_send()
                arrived(place_back(kind, source, q), gr.at[q, kind, p])


def run_attn_bwd(span, slopes, qkv, do, o32, lse, hpd):
    nb, _, seqs, tok, lanes = qkv.shape
    t = nb * tok
    dma = pltpu.SemaphoreType.DMA
    wide = 128 if hpd == 1 else lanes
    return pl.pallas_call(
        functools.partial(attn_bwd_kernel, hpd=hpd, nd=nb),
        out_shape=landing_shape(3, nb, seqs, tok, lanes),
        in_specs=[smem(), smem(), vmem(), hbm(), vmem(), vmem()],
        out_specs=vmem(),
        scratch_shapes=[
            pltpu.VMEM((nb, seqs, tok, lanes), BF16),
            pltpu.VMEM(qkv.shape, BF16),
            pltpu.VMEM((hpd, t, 256), BF16),
            pltpu.VMEM((hpd, nb, tok, 256), BF16),
            pltpu.VMEM((lanes, t), BF16),
            pltpu.VMEM((hpd, nb, tok, wide), BF16),
            pltpu.VMEM((hpd, t, lanes), BF16),
            pltpu.VMEM((hpd, t, wide), BF16),
            pltpu.VMEM((hpd, t, lanes), BF16),
            pltpu.VMEM((lanes, t), F32),
            pltpu.VMEM((hpd, 2, tok, 2 * tok), F32),
            pltpu.VMEM((hpd, tok, 128), F32),
            pltpu.VMEM((hpd, tok, 128), F32),
            pltpu.VMEM((hpd, tok, 128), F32),
            pltpu.VMEM((tok, lanes), F32),
            pltpu.VMEM((tok, lanes), F32),
            dma((seqs, nb)),
            dma((seqs, nb)),
            dma((seqs, 3, nb)),
            dma((seqs, 3, nb)),
            dma((seqs,)),
        ],
        compiler_params=params(collective_id=3, has_side_effects=True),
        name="attn_bwd",
    )(span, slopes, qkv, do, o32, lse)


def turn(v):
    return v.astype(F32).T.astype(BF16)


def mlp_kernel(
    slot_ref, att_ref, x_ref, dy_ref, vec_ref, gath,
    act_out, dx1_out, do_out, sums_ref, grads,
    wo, wup, wdn, x1, acc, dh2, h2_ref, h2t, attt, da_ref, act_ref, dx1_ref, do_ref, stage,
    sem_o, sem_t, sem_g, sem_w, *, nd, first_o, first_up, first_dn, tile
):
    rows, width = x_ref.shape
    side = gath.shape[1]
    per = width // side
    tiles = wup.shape[0]
    ff = tiles * tile
    cols = tile // side
    lanes = do_ref.shape[2]
    fper = ff // side

    @pl.loop(0, per)
    def _(i):
        for j in range(per):
            fetch_block(gath, slot_at(slot_ref, first_o + i * per + j), wo, pl.multiple_of(i * side, side), j * side, sem_o.at[0], side).start()

    def fetch_tile(f):
        @pl.loop(0, per)
        def _(i):
            for j in range(cols):
                fetch_block(gath, slot_at(slot_ref, first_up + i * fper + f * cols + j), wup.at[f], pl.multiple_of(i * side, side), j * side, sem_t.at[f], side).start()
            for j in range(cols):
                fetch_block(gath, slot_at(slot_ref, first_dn + (f * cols + j) * per + i), wdn.at[f], j * side, pl.multiple_of(i * side, side), sem_t.at[f], side).start()

    fetch_tile(0)
    fetch_tile(1)
    for r in range(width // 256):
        attt[r * 256:(r + 1) * 256, :] = turn(att_ref[:, r * 256:(r + 1) * 256])
    pltpu.make_async_copy(wo, wo, sem_o.at[0]).wait()
    for half in range(2):
        c = slice(half * width // 2, (half + 1) * width // 2)
        x1[:, c] = x_ref[:, c].astype(F32) + dot_nn(att_ref[...], wo[:, c]) + vec_ref[BO:BO + 1, c]

    chunk = 32

    def rows_at(r):
        return pl.ds(pl.multiple_of(r * chunk, chunk), chunk)

    @pl.loop(0, rows // chunk)
    def _(r):
        at = rows_at(r)
        centred, inv = layer_stats(x1[at, :])
        h2_ref[at, :] = (centred * inv * vec_ref[GAIN2:GAIN2 + 1, :] + vec_ref[SHIFT2:SHIFT2 + 1, :]).astype(BF16)
        acc[at, :] = x1[at, :] + vec_ref[BDOWN:BDOWN + 1, :]
        dh2[at, :] = jnp.zeros((chunk, width), F32)

    for r in range(width // 256):
        h2t[r * 256:(r + 1) * 256, :] = turn(h2_ref[:, r * 256:(r + 1) * 256])

    def put(slot, first, res, down, across):
        for i in range(down):
            for j in range(across):
                stage[slot, first + i * across + j] = res[i * side:(i + 1) * side, j * side:(j + 1) * side]

    def leave(slot, n, block):
        pltpu.make_async_copy(stage.at[slot, n], grads.at[slot_at(slot_ref, block)], sem_g.at[slot]).start()

    def left(slot, size):
        at = stage.at[slot, pl.ds(0, size)]
        pltpu.make_async_copy(at, at, sem_g.at[slot]).wait()

    full = 2 * per * cols

    @pl.loop(0, tiles)
    def _(f):
        @pl.when(f + 2 < tiles)
        def _():
            fetch_tile(f + 2)
        pltpu.make_async_copy(wup.at[f], wup.at[f], sem_t.at[f]).wait()
        pltpu.make_async_copy(wdn.at[f], wdn.at[f], sem_t.at[f]).wait()
        per_row = width // tile
        bias = vec_ref[pl.ds(BUP + f // per_row, 1), pl.ds(pl.multiple_of((f % per_row) * tile, tile), tile)]
        z = dot_nn(h2_ref[...], wup[f]) + bias
        dg = dot_nt(dy_ref[...], wdn[f])
        z2 = z * z
        th = jnp.tanh(0.7978845608028654 * (z + 0.044715 * z2 * z))
        g = (0.5 * z * (1.0 + th)).astype(BF16)
        slope = 0.5 * (1.0 + th) + 0.5 * z * (1.0 - th * th) * (
            0.7978845608028654 * (1.0 + 3.0 * 0.044715 * z2)
        )
        dz = (dg * slope).astype(BF16)
        sums_ref[pl.ds(pl.multiple_of(8 * (4 + f // per_row), 8), 8), pl.ds(pl.multiple_of((f % per_row) * tile, tile), tile)] = fold_rows(dz.astype(F32))
        acc[...] += dot_nn(g, wdn[f])
        dh2[...] += dot_nt(dz, wup[f])
        slot = lax.rem(f, 2)

        @pl.when(f >= 2)
        def _():
            left(slot, full)
        put(slot, 0, dot_nn(turn(g), dy_ref[...]).astype(BF16), cols, per)
        put(slot, per * cols, dot_nn(h2t[...], dz).astype(BF16), per, cols)

        @pl.loop(0, per)
        def _(i):
            for j in range(cols):
                leave(slot, j * per + i, first_dn + (f * cols + j) * per + i)
            for j in range(cols):
                leave(slot, per * cols + i * cols + j, first_up + i * fper + f * cols + j)

    zero = jnp.zeros((8, width), F32)

    def finish(r, carry):
        s_bo, s_gain, s_shift, s_bdown = carry
        at = rows_at(r)
        act_ref[at, :] = acc[at, :].astype(BF16)
        centred, inv = layer_stats(x1[at, :])
        hat = centred * inv
        dh = dh2[at, :]
        dhg = dh * vec_ref[GAIN2:GAIN2 + 1, :]
        back = inv * (
            dhg
            - jnp.mean(dhg, axis=-1, keepdims=True)
            - hat * jnp.mean(dhg * hat, axis=-1, keepdims=True)
        )
        dy = dy_ref[at, :].astype(F32)
        dx1 = dy + back
        dx1_ref[at, :] = dx1
        da = dx1.astype(BF16)
        da_ref[at, :] = da
        return (
            s_bo + fold_rows(da.astype(F32)),
            s_gain + fold_rows(dh * hat),
            s_shift + fold_rows(dh),
            s_bdown + fold_rows(dy),
        )

    carry = lax.fori_loop(0, rows // chunk, finish, (zero, zero, zero, zero))
    for n in range(4):
        sums_ref[8 * n:8 * n + 8, :] = carry[n]
    outs = [
        pltpu.make_async_copy(act_ref, act_out, sem_w.at[0]),
        pltpu.make_async_copy(dx1_ref, dx1_out, sem_w.at[1]),
        pltpu.make_async_copy(do_ref, do_out, sem_w.at[2]),
    ]
    outs[0].start()
    outs[1].start()
    for half in range(2):
        c = slice(half * width // 2, (half + 1) * width // 2)
        res = dot_nt(da_ref[...], wo[c, :]).astype(BF16)
        for d in range(nd // 2):
            do_ref[half * (nd // 2) + d] = res[:, d * lanes:(d + 1) * lanes]
    outs[2].start()
    left(0, full)
    left(1, full)
    half_rows = width // 2
    for half in range(2):
        res = dot_nn(attt[half * half_rows:(half + 1) * half_rows, :], da_ref[...]).astype(BF16)
        put(half, 0, res, per // 2, per)

        @pl.loop(0, per // 2)
        def _(i):
            for j in range(per):
                leave(half, i * per + j, first_o + (half * (per // 2) + i) * per + j)
    for half in range(2):
        left(half, per * per // 2)
    for copy in outs:
        copy.wait()


def run_mlp(slot_of, att, x, dy, vec, gath, nd):
    rows, width = x.shape
    side = gath.shape[1]
    lanes = width // nd
    per = width // side
    first_o = 3 * per * per
    first_up = first_o + per * per
    first_dn = first_up + per * (FF // side)
    tile = 512
    f32_rows = pltpu.VMEM((rows, width), F32)
    bf16_rows = pltpu.VMEM((rows, width), BF16)
    turned = pltpu.VMEM((width, rows), BF16)
    return pl.pallas_call(
        functools.partial(
            mlp_kernel, nd=nd, first_o=first_o, first_up=first_up, first_dn=first_dn, tile=tile
        ),
        out_shape=(
            sds((rows, width), BF16),
            sds((rows, width), F32),
            sds((nd, rows, lanes), BF16),
            sds((8 * (4 + FF // width), width), F32),
            sds(gath.shape, BF16),
        ),
        in_specs=[smem(), vmem(), vmem(), vmem(), vmem(), hbm()],
        out_specs=(hbm(), hbm(), hbm(), vmem(), hbm()),
        scratch_shapes=[
            pltpu.VMEM((width, width), BF16),
            pltpu.VMEM((FF // tile, width, tile), BF16),
            pltpu.VMEM((FF // tile, tile, width), BF16),
            f32_rows,
            f32_rows,
            f32_rows,
            bf16_rows,
            turned,
            turned,
            bf16_rows,
            bf16_rows,
            f32_rows,
            pltpu.VMEM((nd, rows, lanes), BF16),
            pltpu.VMEM((2, 2 * per * (tile // side), side, side), BF16),
            pltpu.SemaphoreType.DMA((1,)),
            pltpu.SemaphoreType.DMA((FF // tile,)),
            pltpu.SemaphoreType.DMA((2,)),
            pltpu.SemaphoreType.DMA((3,)),
        ],
        compiler_params=params(),
        name="mlp",
    )(slot_of, att, x, dy, vec, gath)


def dh1_dot(cat, w, dh1, part, half):
    width = dh1.shape[1]
    c = slice(half * width // 2, (half + 1) * width // 2)
    res = dot_nt(cat[:, part * width:(part + 1) * width], w[part, c, :])
    if part == 0:
        dh1[:, c] = res
    else:
        dh1[:, c] += res


def first_norm_back(cat, x, dh1, dx1, ig, vec_ref):
    rows, width = x.shape
    chunk = 32
    zero = jnp.zeros((8, width), F32)

    def finish(r, carry):
        s_gain, s_shift, s_bq, s_bv = carry
        at = pl.ds(pl.multiple_of(r * chunk, chunk), chunk)
        centred, inv = layer_stats(x[at, :].astype(F32))
        hat = centred * inv
        dh = dh1[at, :]
        dhg = dh * vec_ref[GAIN1:GAIN1 + 1, :]
        back = inv * (
            dhg
            - jnp.mean(dhg, axis=-1, keepdims=True)
            - hat * jnp.mean(dhg * hat, axis=-1, keepdims=True)
        )
        ig[at, :] = dx1[at, :] + back
        return (
            s_gain + fold_rows(dh * hat),
            s_shift + fold_rows(dh),
            s_bq + fold_rows(cat[at, 0:width].astype(F32)),
            s_bv + fold_rows(cat[at, 2 * width:3 * width].astype(F32)),
        )

    return lax.fori_loop(0, rows // chunk, finish, (zero, zero, zero, zero))


def vector_rows(first, sums2):
    rows = [jnp.sum(v, axis=0, keepdims=True) for v in first]
    rows += [jnp.sum(sums2[8 * n:8 * n + 8, :], axis=0, keepdims=True) for n in range(sums2.shape[0] // 8)]
    return rows


def dh1_kernel(cat_ref, x_ref, dx1_ref, vec_ref, wq_ref, sums2_ref, ig_ref, vsum_ref, dh1):
    for part in range(3):
        for half in range(2):
            dh1_dot(cat_ref, wq_ref, dh1, part, half)
    first = first_norm_back(cat_ref, x_ref, dh1, dx1_ref, ig_ref, vec_ref)
    for n, row in enumerate(vector_rows(first, sums2_ref)):
        vsum_ref[n:n + 1, :] = row


def run_dh1(cat, x, dx1, vec, wq, sums2):
    rows, width = x.shape
    return pl.pallas_call(
        dh1_kernel,
        out_shape=(sds((rows, width), F32), sds(vec.shape, F32)),
        in_specs=[vmem()] * 6,
        out_specs=(vmem(), vmem()),
        scratch_shapes=[pltpu.VMEM((rows, width), F32)],
        compiler_params=params(),
        name="dh1",
    )(cat, x, dx1, vec, wq, sums2)


def wgrad_kernel(slot_ref, h1_ref, cat_ref, rest, out, a_t, stage, sem_out, *, side, tile):
    del rest
    rows, width = h1_ref.shape
    per = width // side
    cols = tile // side
    steps = cat_ref.shape[1] // tile
    for r in range(width // 256):
        c = slice(r * 256, (r + 1) * 256)
        a_t[c, :] = turn(h1_ref[:, c])

    def left(slot):
        pltpu.make_async_copy(stage.at[slot], stage.at[slot], sem_out.at[slot]).wait()

    @pl.loop(0, steps)
    def _(t):
        slot = lax.rem(t, 2)

        @pl.when(t >= 2)
        def _():
            left(slot)
        res = dot_nn(a_t[...], cat_ref[:, pl.ds(pl.multiple_of(t * tile, tile), tile)]).astype(BF16)
        for i in range(per):
            for j in range(cols):
                stage[slot, i * cols + j] = res[i * side:(i + 1) * side, j * side:(j + 1) * side]

        @pl.loop(0, per)
        def _(i):
            for j in range(cols):
                dst = slot_at(slot_ref, i * 3 * per + t * cols + j)
                pltpu.make_async_copy(stage.at[slot, i * cols + j], out.at[dst], sem_out.at[slot]).start()

    left(0)
    left(1)


def run_wgrad(slot_of, h1, cat, grads):
    rows, width = h1.shape
    side = grads.shape[1]
    tile = 512
    return pl.pallas_call(
        functools.partial(wgrad_kernel, side=side, tile=tile),
        out_shape=sds(grads.shape, BF16),
        in_specs=[smem(), vmem(), vmem(), hbm()],
        out_specs=hbm(),
        scratch_shapes=[
            pltpu.VMEM((width, rows), BF16),
            pltpu.VMEM((2, (width // side) * (tile // side), side, side), BF16),
            pltpu.SemaphoreType.DMA((2,)),
        ],
        input_output_aliases={3: 0},
        compiler_params=params(),
        name="wgrad",
    )(slot_of, h1, cat, grads)


def whereami():
    g = lax.axis_index("grp")
    d = lax.axis_index("dev")
    core = lax.rem(d, 2)
    x = lax.rem(d // 2, 2)
    y = d // 4
    over_x = d + 2 - 4 * x
    over_y = d + 4 - 8 * y
    across = over_x + 4 - 8 * y
    sibling = d + 1 - 2 * core
    return g, d, over_x, over_y, across, sibling


def near_order(t, g, ng):
    t = ng - 1 - t
    low = jnp.where(t < ng - 1 - g, ng - 1 - t, t - (ng - 1 - g))
    high = jnp.where(t < g, t, ng - 1 - (t - g))
    return jnp.where(2 * g < ng, low, high)


def greet(g, ng, peers):
    barrier = pltpu.get_barrier_semaphore()
    for peer in peers:
        pl.semaphore_signal(barrier, inc=1, device_id=(g, peer), device_id_type=MESH)

    d = lax.axis_index("dev")

    @pl.when(g > 0)
    def _():
        pl.semaphore_signal(barrier, inc=1, device_id=(g - 1, d), device_id_type=MESH)

    @pl.when(g < ng - 1)
    def _():
        pl.semaphore_signal(barrier, inc=1, device_id=(g + 1, d), device_id_type=MESH)

    ends = (g > 0).astype(jnp.int32) + (g < ng - 1).astype(jnp.int32)
    pl.semaphore_wait(barrier, len(peers) + ends)


def slot_cuts(count):
    third = 2 * (count // 12)
    first = (count - third) // 2
    return first, count - third - first, third // 2, third // 2


def gather_kernel(
    w_ref, x_ref, block_ref, vin_ref, out, h1_ref, slot_ref, vec_ref,
    own, local_sem, zs, zr, cs, cr, ss, sr, *, ng, nd
):
    count = w_ref.shape[0]
    na, nb, nc1, nc2 = slot_cuts(count)
    flat = na + nb
    nc = nc1 + nc2
    g, d, over_x, over_y, across, sibling = whereami()
    columns = (d, over_x, over_y, across)
    own[...] = w_ref[...].astype(BF16)
    greet(g, ng, (over_x, over_y, sibling))

    def region(gz, dev, first=0, size=count):
        return out.at[pl.ds((gz * nd + dev) * count + first, size)]

    def wide(t):
        return count if t == 0 else flat

    def kind(n, t):
        return (
            (d, 0, wide(t), over_x),
            (d, 0, wide(t), over_y),
            (d, 0, wide(t), sibling),
            (over_x, 0, na, over_y),
            (over_y, na, nb, over_x),
            (over_x, 0, wide(t), sibling),
            (over_y, 0, wide(t), sibling),
            (across, 0, na, sibling),
            (across, na, nb, sibling),
            (over_x, flat, nc1, over_y),
            (over_y, flat + nc1, nc2, over_x),
            (across, flat, nc1, sibling),
            (across, flat + nc1, nc2, sibling),
            (d, flat, nc, sibling),
            (over_x, flat, nc, sibling),
            (over_y, flat, nc, sibling),
            (across, flat, nc, sibling),
        )[n]

    def kinds(t):
        return range(13) if t == 0 else tuple(range(9)) + tuple(range(13, 17))

    def plane(n, t, src=None):
        gz = near_order(t, g, ng)
        dev, first, size, to = kind(n, t)
        at = region(gz, dev, first, size)
        return remote(at if src is None else src, at, ss.at[n, gz], sr.at[n, gz], (g, to))

    def landed(n, t, dev):
        gz = near_order(t, g, ng)
        _, first, size, _ = kind(n, t)
        arrived(region(gz, dev, first, size), sr.at[n, gz])

    def line(gz, up, src=None):
        at = region(gz, d, 0, flat)
        to = g + 1 if up else g - 1
        return remote(at if src is None else src, at, zs.at[gz, int(up)], zr.at[gz], (to, d))

    def corner_line(gz, c, up, src=None):
        at = region(gz, columns[c], flat, nc)
        to = g + 1 if up else g - 1
        return remote(at if src is None else src, at, cs.at[gz, c, int(up)], cr.at[gz, c], (to, d))

    def both_ways(gz, make):
        @pl.when((gz <= g) & (g < ng - 1))
        def _():
            make(True)

        @pl.when((gz >= g) & (g > 0))
        def _():
            make(False)

    mine = pltpu.make_async_copy(own, region(g, d), local_sem.at[0])
    mine.start()

    def column(t):
        gz = near_order(t, g, ng)
        if t == 0:
            both_ways(gz, lambda up: line(gz, up, cut(own, 0, flat)).start())
            for n in range(3):
                plane(n, t, own).start()
            both_ways(gz, lambda up: corner_line(gz, 0, up, cut(own, flat, nc)).start())
            return
        arrived(region(gz, d, 0, flat), zr.at[gz])
        both_ways(gz, lambda up: line(gz, up).start())
        for n in range(3):
            plane(n, t).start()

    def sides(t):
        gz = near_order(t, g, ng)
        landed(0, t, over_x)
        plane(3, t).start()
        if t == 0:
            plane(9, t).start()
            both_ways(gz, lambda up: corner_line(gz, 1, up).start())
        plane(5, t).start()
        landed(1, t, over_y)
        plane(4, t).start()
        if t == 0:
            plane(10, t).start()
            both_ways(gz, lambda up: corner_line(gz, 2, up).start())
        plane(6, t).start()

    def corner(t):
        gz = near_order(t, g, ng)
        if t == 0:
            landed(9, t, across)
            landed(10, t, across)
            both_ways(gz, lambda up: corner_line(gz, 3, up).start())
            plane(11, t).start()
            plane(12, t).start()
        landed(3, t, across)
        plane(7, t).start()
        landed(4, t, across)
        plane(8, t).start()

    def far_corner(t):
        gz = near_order(t, g, ng)
        for c in range(4):
            arrived(region(gz, columns[c], flat, nc), cr.at[gz, c])
            both_ways(gz, lambda up: corner_line(gz, c, up).start())
            plane(13 + c, t).start()

    plan = [(t, f) for t in range(ng) for f in (0, 1, 2, 3) if t > 0 or f < 3]
    lag = {0: 0, 1: 1.5, 2: 2.6, 3: 2.2}
    for t, f in sorted(plan, key=lambda e: e[0] * 1.0 + lag[e[1]]):
        (column, sides, corner, far_corner)[f](t)
        if (t, f) == (0, 0):
            prepare(x_ref, block_ref, vin_ref, h1_ref, slot_ref, vec_ref)

    for t in range(ng):
        for n in kinds(t):
            dev, _, _, to = kind(n, t)
            if to is sibling:
                landed(n, t, dev + sibling - d)
    mine.wait()
    for t in range(ng):
        gz = near_order(t, g, ng)
        for n in kinds(t):
            plane(n, t).wait_send()
        both_ways(gz, lambda up: line(gz, up).wait_send())
        for c in range(4):
            both_ways(gz, lambda up: corner_line(gz, c, up).wait_send())


def run_gather(w, x, blocks, vin, ng, nd):
    count, side, _ = w.shape
    dma = pltpu.SemaphoreType.DMA
    return pl.pallas_call(
        functools.partial(gather_kernel, ng=ng, nd=nd),
        out_shape=(sds((ng * nd * count, side, side), BF16),) + prepared_shapes(x, blocks, vin),
        in_specs=[vmem()] * 4,
        out_specs=(hbm(), vmem(), vmem(), vmem()),
        scratch_shapes=[
            pltpu.VMEM((count, side, side), BF16),
            dma((1,)),
            dma((ng, 2)),
            dma((ng,)),
            dma((ng, 4, 2)),
            dma((ng, 4)),
            dma((17, ng)),
            dma((17, ng)),
        ],
        compiler_params=params(collective_id=0, has_side_effects=True),
        name="gather",
    )(w, x, blocks, vin)


def add_blocks(dst, src, size):
    step = 4 if size % 4 == 0 else 2 if size % 2 == 0 else 1

    @pl.loop(0, size // step)
    def _(n):
        for k in range(step):
            dst[n * step + k] = dst[n * step + k] + src[n * step + k]


def scatter_kernel(
    grads, sums2_ref, vec_ref, vin_ref, cat_in, x_in, dx1_in, wq_in, out_ref, vout_ref, vnew_ref, ig_out,
    cat, x, dx1, wq, dh1, sem_in, mine, r0, r1y, r1x, r2x, r2y, rz, cz, cy, cx, cx2, cy2, vwork, vxy, vz,
    load, s0, w0, s1, w1, s2, w2, sz, wz, sc, wc, s3, w3, vs, vw, *, ng, nd, rate
):
    count = out_ref.shape[0]
    na, nb, nc1, nc2 = slot_cuts(count)
    flat = na + nb
    nc = nc1 + nc2
    g, d, over_x, over_y, across, sibling = whereami()
    columns = (d, over_x, over_y, across)

    def region(gz, dev):
        return grads.at[pl.ds((gz * nd + dev) * count, count)]

    def order(t):
        return near_order(ng - 1 - t, g, ng)

    for t in range(ng):
        for c in range(4):
            pltpu.make_async_copy(region(order(t), columns[c]), mine.at[order(t), c], load.at[order(t), c]).start()
    greet(g, ng, (over_x, over_y, sibling))

    def to_sibling(gz, c):
        return remote(
            region(gz, columns[c] + sibling - d), r0.at[gz, c], s0.at[gz, c], w0.at[gz, c], (g, sibling)
        )

    peers = (sibling, over_x, over_y)

    def vec_copy(n):
        return remote(vwork.at[n], vxy.at[n], vs.at[n], vw.at[n], (g, peers[n]))

    for t in range(ng):
        for c in (3, 2, 1, 0):
            to_sibling(order(t), c).start()
    inputs = [
        pltpu.make_async_copy(cat_in, cat, sem_in.at[0]),
        pltpu.make_async_copy(wq_in, wq, sem_in.at[1]),
        pltpu.make_async_copy(x_in, x, sem_in.at[2]),
        pltpu.make_async_copy(dx1_in, dx1, sem_in.at[3]),
    ]
    for copy in inputs:
        copy.start()
    input_grad = pltpu.make_async_copy(dx1, ig_out, sem_in.at[4])

    def first_norm():
        for copy in inputs:
            copy.wait()
        for part in range(3):
            for half in range(2):
                dh1_dot(cat, wq, dh1, part, half)
        first = first_norm_back(cat, x, dh1, dx1, dx1, vec_ref)
        input_grad.start()
        for n, row in enumerate(vector_rows(first, sums2_ref)):
            vwork[0, n:n + 1, :] = row
        vec_copy(0).start()

    first = (
        (2, 0, na, r1y, 0, over_y),
        (3, 0, na, r1y, 1, over_y),
        (1, na, nb, r1x, 0, over_x),
        (3, na, nb, r1x, 1, over_x),
    )
    second = ((1, 0, na, r2x, over_x), (2, na, nb, r2y, over_y))
    third = (
        (2, flat, nc1, cy.at[0], over_y),
        (3, flat, nc1, cy.at[1], over_y),
        (1, flat + nc1, nc2, cx.at[0], over_x),
        (3, flat + nc1, nc2, cx.at[1], over_x),
        (1, flat, nc1, cx2, over_x),
        (2, flat + nc1, nc2, cy2, over_y),
    )

    def copy1(n, gz):
        c, at, size, buf, place_at, to = first[n]
        return remote(cut(mine.at[gz, c], at, size), buf.at[gz, place_at], s1.at[n, gz], w1.at[n, gz], (g, to))

    def copy2(n, gz):
        c, at, size, buf, to = second[n]
        return remote(cut(mine.at[gz, c], at, size), buf.at[gz], s2.at[n, gz], w2.at[n, gz], (g, to))

    def copy3(n):
        c, at, size, buf, to = third[n]
        return remote(cut(mine.at[g, c], at, size), buf, s3.at[n], w3.at[n], (g, to))

    def flat_part(gz):
        return cut(mine.at[gz, 0], 0, flat)

    def corner_part(gz):
        return mine.at[gz, :, pl.ds(flat, nc)]

    def line(gz, part, buf, sends, waits, up):
        at = gz if up else jnp.where(gz < g - 1, gz, ng)
        to = g + 1 if up else g - 1
        return remote(part(gz), buf.at[at], sends.at[gz], waits.at[at], (to, d))

    def pass_on(gz, part, buf, sends, waits, gather):
        @pl.when(gz > g)
        def _():
            @pl.when(g > 0)
            def _():
                arrived(buf.at[gz], waits.at[gz])
                gather(gz)
            line(gz, part, buf, sends, waits, True).start()

        @pl.when(gz < g)
        def _():
            @pl.when(g < ng - 1)
            def _():
                arrived(buf.at[gz], waits.at[gz])
                gather(gz)
            line(gz, part, buf, sends, waits, False).start()

    def gather_flat(gz):
        add_blocks(flat_part(gz), rz.at[gz], flat)

    def gather_corner(at, gz):
        for c in range(4):
            add_blocks(cut(mine.at[gz, c], flat, nc), cz.at[at, c], nc)

    def sums0(t):
        gz = order(t)
        for c in (3, 2, 1, 0):
            pltpu.make_async_copy(region(gz, columns[c]), mine.at[gz, c], load.at[gz, c]).wait()
            arrived(r0.at[gz, c], w0.at[gz, c])
            add_blocks(mine.at[gz, c], r0.at[gz, c], count)
            if t < ng - 1:
                sends0(t, c)

    def sends0(t, c):
        gz = order(t)
        for n in {3: (1, 3), 2: (0,), 1: (2,), 0: ()}[c]:
            copy1(n, gz).start()

    def along0(t):
        pass_on(order(t), corner_part, cz, sc, wc, lambda gz: gather_corner(gz, gz))

    def stage1(t):
        gz = order(t)
        arrived(r1y.at[gz, 1], w1.at[1, gz])
        add_blocks(cut(mine.at[gz, 1], 0, na), r1y.at[gz, 1], na)
        copy2(0, gz).start()
        arrived(r1x.at[gz, 1], w1.at[3, gz])
        add_blocks(cut(mine.at[gz, 2], na, nb), r1x.at[gz, 1], nb)
        copy2(1, gz).start()
        arrived(r1y.at[gz, 0], w1.at[0, gz])
        add_blocks(cut(mine.at[gz, 0], 0, na), r1y.at[gz, 0], na)
        arrived(r1x.at[gz, 0], w1.at[2, gz])
        add_blocks(cut(mine.at[gz, 0], na, nb), r1x.at[gz, 0], nb)

    def stage2(t):
        gz = order(t)
        arrived(r2x.at[gz], w2.at[0, gz])
        add_blocks(cut(mine.at[gz, 0], 0, na), r2x.at[gz], na)
        arrived(r2y.at[gz], w2.at[1, gz])
        add_blocks(cut(mine.at[gz, 0], na, nb), r2y.at[gz], nb)
        if t < ng - 1:
            pass_on(gz, flat_part, rz, sz, wz, gather_flat)

    def corner0():
        @pl.when(g > 0)
        def _():
            arrived(cz.at[g], wc.at[g])
            gather_corner(g, g)

        @pl.when(g < ng - 1)
        def _():
            arrived(cz.at[ng], wc.at[ng])
            gather_corner(ng, g)
        for n in range(4):
            copy3(n).start()

    def corner1():
        arrived(cy.at[1], w3.at[1])
        add_blocks(cut(mine.at[g, 1], flat, nc1), cy.at[1], nc1)
        copy3(4).start()
        arrived(cx.at[1], w3.at[3])
        add_blocks(cut(mine.at[g, 2], flat + nc1, nc2), cx.at[1], nc2)
        copy3(5).start()
        arrived(cy.at[0], w3.at[0])
        add_blocks(cut(mine.at[g, 0], flat, nc1), cy.at[0], nc1)
        arrived(cx.at[0], w3.at[2])
        add_blocks(cut(mine.at[g, 0], flat + nc1, nc2), cx.at[0], nc2)

    def corner2():
        arrived(cx2, w3.at[4])
        add_blocks(cut(mine.at[g, 0], flat, nc1), cx2, nc1)
        arrived(cy2, w3.at[5])
        add_blocks(cut(mine.at[g, 0], flat + nc1, nc2), cy2, nc2)

    def vec_step(n):
        arrived(vxy.at[n], vw.at[n])
        total = vwork[n] + vxy[n]
        if n < 2:
            vwork[n + 1] = total
            vec_copy(n + 1).start()
        else:
            vz[g] = total

    def vec_line(gz, up):
        to = g + 1 if up else g - 1
        return remote(vz.at[gz], vz.at[gz], vs.at[3 + 2 * gz + int(up)], vw.at[3 + gz], (to, d))

    last = ng - 1
    sums0(0)
    sums0(1)
    first_norm()
    along0(0)
    stage1(0)
    for t in range(2, last):
        sums0(t)
        along0(t - 1)
        vec_step(t - 2)
        stage1(t - 1)
        stage2(t - 2)
    vec_step(1)
    sums0(last)
    along0(last - 1)
    stage1(last - 1)
    for c in (3, 2, 1):
        sends0(last, c)
    corner0()
    vec_step(2)

    @pl.when(g < ng - 1)
    def _():
        vec_line(g, True).start()

    @pl.when(g > 0)
    def _():
        vec_line(g, False).start()
    stage2(last - 2)
    for n in range(1, ng):
        gz = near_order(n, g, ng)
        arrived(vz.at[gz], vw.at[3 + gz])

        @pl.when((gz < g) & (g < ng - 1))
        def _():
            vec_line(gz, True).start()

        @pl.when((gz > g) & (g > 0))
        def _():
            vec_line(gz, False).start()
    stage2(last - 1)
    stage1(last)
    corner1()
    total = vz[0]
    for z in range(1, ng):
        total = total + vz[z]
    vwork[3] = total
    per = total.shape[1] // 128
    for r in range(total.shape[0]):
        for c in range(per):
            row = vwork[3, r:r + 1, c * 128:(c + 1) * 128]
            n = per * r + c
            vout_ref[n:n + 1, :] = row
            vnew_ref[n:n + 1, :] = vin_ref[n:n + 1, :] - rate * row
    stage2(last)
    corner2()

    @pl.when(g > 0)
    def _():
        arrived(rz.at[g], wz.at[g])

    @pl.when(g < ng - 1)
    def _():
        arrived(rz.at[ng], wz.at[ng])

    @pl.when((g > 0) & (g < ng - 1))
    def _():
        @pl.loop(0, flat // 2)
        def _(n):
            for k in range(2):
                i = 2 * n + k
                out_ref[i] = mine[g, 0, i].astype(F32) + rz[g, i].astype(F32) + rz[ng, i].astype(F32)

    @pl.when(g == 0)
    def _():
        @pl.loop(0, flat // 2)
        def _(n):
            for k in range(2):
                i = 2 * n + k
                out_ref[i] = mine[g, 0, i].astype(F32) + rz[ng, i].astype(F32)

    @pl.when((g > 0) & (g == ng - 1))
    def _():
        @pl.loop(0, flat // 2)
        def _(n):
            for k in range(2):
                i = 2 * n + k
                out_ref[i] = mine[g, 0, i].astype(F32) + rz[g, i].astype(F32)

    for i in range(flat, count):
        out_ref[i] = mine[g, 0, i].astype(F32)

    for t in range(ng):
        gz = order(t)
        for c in range(4):
            to_sibling(gz, c).wait_send()
        for n in range(4):
            copy1(n, gz).wait_send()
        for n in range(2):
            copy2(n, gz).wait_send()
        if t < ng - 1:
            arrived(flat_part(gz), sz.at[gz])
            arrived(corner_part(gz), sc.at[gz])
    input_grad.wait()
    for n in range(6):
        copy3(n).wait_send()
    for n in range(3):
        vec_copy(n).wait_send()
    for n in range(ng):
        gz = near_order(n, g, ng)

        @pl.when((gz <= g) & (g < ng - 1))
        def _():
            vec_line(gz, True).wait_send()

        @pl.when((gz >= g) & (g > 0))
        def _():
            vec_line(gz, False).wait_send()


def run_scatter(grads, sums2, vec, vin, cat, x, dx1, wq, ng, nd, rate):
    blocks, side, _ = grads.shape
    count = blocks // (ng * nd)
    na, nb, nc1, nc2 = slot_cuts(count)
    flat = na + nb
    dma = pltpu.SemaphoreType.DMA

    def buf(*lead):
        return pltpu.VMEM(lead + (side, side), BF16)

    def like(v):
        return pltpu.VMEM(v.shape, v.dtype)

    return pl.pallas_call(
        functools.partial(scatter_kernel, ng=ng, nd=nd, rate=rate),
        out_shape=(
            sds((count, side, side), F32),
            sds(vin.shape, F32),
            sds(vin.shape, F32),
            sds(dx1.shape, F32),
        ),
        in_specs=[hbm(), vmem(), vmem(), vmem()] + [hbm()] * 4,
        out_specs=(vmem(), vmem(), vmem(), hbm()),
        scratch_shapes=[
            like(cat),
            like(x),
            like(dx1),
            like(wq),
            like(dx1),
            dma((5,)),
            buf(ng, 4, count),
            buf(ng, 4, count),
            buf(ng, 2, na),
            buf(ng, 2, nb),
            buf(ng, na),
            buf(ng, nb),
            buf(ng + 1, flat),
            buf(ng + 1, 4, nc1 + nc2),
            buf(2, nc1),
            buf(2, nc2),
            buf(nc1),
            buf(nc2),
            pltpu.VMEM((4,) + vec.shape, F32),
            pltpu.VMEM((3,) + vec.shape, F32),
            pltpu.VMEM((ng,) + vec.shape, F32),
            dma((ng, 4)),
            dma((ng, 4)),
            dma((ng, 4)),
            dma((4, ng)),
            dma((4, ng)),
            dma((2, ng)),
            dma((2, ng)),
            dma((ng,)),
            dma((ng + 1,)),
            dma((ng,)),
            dma((ng + 1,)),
            dma((6,)),
            dma((6,)),
            dma((3 + 2 * ng,)),
            dma((3 + ng,)),
        ],
        compiler_params=params(61, collective_id=1, has_side_effects=True),
        name="scatter",
    )(grads, sums2, vec, vin, cat, x, dx1, wq)


def blocks_kernel(*refs, handed):
    g_ref, w_ref, ls_ref, rs_ref, lr_ref, rr_ref = refs[:6]
    wg_out, nl_out, nr_out, nw_out = refs[6 + handed:10 + handed]
    step = pl.program_id(0)

    def hand_on(n):
        return pltpu.make_async_copy(refs[6 + n], refs[10 + handed + n], refs[-1].at[n])

    @pl.when(step == 0)
    def _():
        for n in range(handed):
            hand_on(n).start()

    for i in range(g_ref.shape[0]):
        grad = g_ref[i]
        wg_out[i] = grad
        hi = grad.astype(BF16)
        low = (grad - hi.astype(F32)).astype(BF16)
        nl_out[i] = 0.5 * ls_ref[i] + 0.5 * dot_nt(hi, hi)
        turned = grad.T
        hi_t = turned.astype(BF16)
        nr_out[i] = 0.5 * rs_ref[i] + 0.5 * dot_nt(hi_t, hi_t)
        left = lr_ref[i]
        left_hi = left.astype(BF16)
        left_low = (left - left_hi.astype(F32)).astype(BF16)
        shaped = dot_nn(left_hi, hi) + dot_nn(left_hi, low) + dot_nn(left_low, hi)
        right = rr_ref[i]
        right_hi = right.astype(BF16)
        right_low = (right - right_hi.astype(F32)).astype(BF16)
        sh_hi = shaped.astype(BF16)
        sh_low = (shaped - sh_hi.astype(F32)).astype(BF16)
        shaped = dot_nn(sh_hi, right_hi) + dot_nn(sh_low, right_hi) + dot_nn(sh_hi, right_low)
        nw_out[i] = w_ref[i] - weight_rate * shaped

    @pl.when(step == pl.num_programs(0) - 1)
    def _():
        for n in range(handed):
            hand_on(n).wait()


def run_blocks(grads, weights, left_stats, right_stats, left_roots, right_roots, *passing):
    count, side, _ = grads.shape
    step = math.gcd(count, 4)
    spec = pl.BlockSpec((step, side, side), lambda n: (n, 0, 0))
    return pl.pallas_call(
        functools.partial(blocks_kernel, handed=len(passing)),
        grid=(count // step,),
        out_shape=tuple([sds(grads.shape, F32)] * 4) + tuple(sds(v.shape, v.dtype) for v in passing),
        in_specs=[spec] * 6 + [hbm()] * len(passing),
        out_specs=tuple([spec] * 4) + tuple([hbm()] * len(passing)),
        scratch_shapes=[pltpu.SemaphoreType.DMA((max(len(passing), 1),))],
        compiler_params=params(),
        name="blocks",
    )(grads, weights, left_stats, right_stats, left_roots, right_roots, *passing)


def local(
    inputs,
    cotangent,
    weight_slots,
    slot_block,
    left_stats,
    right_stats,
    left_roots,
    right_roots,
    vectors,
    span_start,
):
    seq_count, tok_count, width = inputs.shape
    rows = seq_count * tok_count
    nd = lax.axis_size("dev")
    ng = lax.axis_size("grp")
    side = weight_slots.shape[1]
    hpd = H // nd
    lanes = width // nd
    head = lax.axis_index("dev") * hpd + jnp.arange(hpd, dtype=jnp.int32)
    slopes = jnp.exp2(-8.0 * (head.astype(F32) + 1.0) / H)
    vin = vectors.reshape(-1, 128)
    held = slot_block.reshape(-1, 128)
    x = inputs.reshape(rows, width)
    dy = cotangent.reshape(rows, width)
    rate = vector_rate / math.sqrt(rows * nd * ng)

    direct = nd == 8
    if direct:
        gath, h1, slot_of, vec = run_gather(weight_slots, x, held, vin, ng, nd)
    else:
        gath = lax.all_gather(weight_slots.astype(BF16), ("grp", "dev"), axis=0, tiled=True)
        h1, slot_of, vec = run_prepare(x, held, vin)
    qkv, wq = run_qkv(slot_of, h1, vec, gath, nd)
    qkv, o, o32, lse = run_attn_fwd(
        span_start, slopes, qkv.reshape(nd, 3, seq_count, tok_count, lanes), hpd
    )
    att = side_by_side(o, 1, rows)
    act, dx1, do, sums2, grads = run_mlp(slot_of, att, x, dy, vec, gath, nd)
    do = do.reshape(nd, seq_count, tok_count, lanes)
    cat = side_by_side(run_attn_bwd(span_start, slopes, qkv, do, o32, lse, hpd), 3, rows)
    grads = run_wgrad(slot_of, h1, cat, grads)
    if direct:
        weight_grads, vector_grads, new_vectors, ig = run_scatter(
            grads, sums2, vec, vin, cat, x, dx1, wq, ng, nd, rate
        )
        passing = (ig, vector_grads, new_vectors)
    else:
        ig, vsum = run_dh1(cat, x, dx1, vec, wq, sums2)
        vector_grads = lax.psum(vsum.reshape(-1), ("grp", "dev"))
        new_vectors = vectors - rate * vector_grads
        weight_grads = lax.psum_scatter(grads, ("grp", "dev"), scatter_dimension=0, tiled=True)
        weight_grads = weight_grads.astype(F32)
        passing = ()
    weight_grads, new_left, new_right, new_weights, *passed = run_blocks(
        weight_grads, weight_slots, left_stats, right_stats, left_roots, right_roots, *passing
    )
    if direct:
        ig, vector_grads, new_vectors = passed
    return (
        act.reshape(inputs.shape),
        ig.reshape(inputs.shape),
        weight_grads,
        new_left,
        new_right,
        new_weights,
        vector_grads.reshape(-1),
        new_vectors.reshape(-1),
    )


def solution(mesh):
    return jax.shard_map(
        local,
        mesh=mesh,
        in_specs=(
            P("grp", "dev", None),
            P("grp", "dev", None),
            P(("grp", "dev"), None, None),
            P(),
            P(("grp", "dev"), None, None),
            P(("grp", "dev"), None, None),
            P(("grp", "dev"), None, None),
            P(("grp", "dev"), None, None),
            P(),
            P("grp"),
        ),
        out_specs=(
            P("grp", "dev", None),
            P("grp", "dev", None),
            P(("grp", "dev"), None, None),
            P(("grp", "dev"), None, None),
            P(("grp", "dev"), None, None),
            P(("grp", "dev"), None, None),
            P(),
            P(),
        ),
        check_vma=False,
    )
```

```python
import functools
import math

import jax
import jax.numpy as jnp
from jax import lax
from jax.experimental import pallas as pl
from jax.experimental.pallas import tpu as pltpu
from jax.sharding import PartitionSpec as P

H = 16
FF = 4096
PIC = 256

eps = 1e-05
weight_rate = 0.5
vector_rate = 0.5
big_negative = -1e30
highest = lax.Precision.HIGHEST
F32 = jnp.float32
BF16 = jnp.bfloat16
LOG2E = 1.4426950408889634
MIB = 1024 * 1024

GAIN1, SHIFT1, BQ, BV, BO, GAIN2, SHIFT2, BDOWN, BUP = range(9)


def dot_nn(a, b):
    return lax.dot_general(a, b, (((1,), (0,)), ((), ())), preferred_element_type=F32)


def dot_nt(a, b):
    return lax.dot_general(a, b, (((1,), (1,)), ((), ())), preferred_element_type=F32)


def vmem():
    return pl.BlockSpec(memory_space=pltpu.VMEM)


def smem():
    return pl.BlockSpec(memory_space=pltpu.SMEM)


def hbm():
    return pl.BlockSpec(memory_space=pl.ANY)


def sds(shape, dtype):
    return jax.ShapeDtypeStruct(shape, dtype)


def params(mib=58, **kw):
    return pltpu.CompilerParams(vmem_limit_bytes=mib * MIB, **kw)


def layer_stats(v):
    middle = jnp.mean(v, axis=-1, keepdims=True)
    centred = v - middle
    spread = jnp.mean(centred * centred, axis=-1, keepdims=True)
    return centred, lax.rsqrt(spread + eps)


def fold_rows(v):
    return jnp.sum(v.reshape(v.shape[0] // 8, 8, v.shape[1]), axis=0)


def slot_at(slot_ref, block):
    lanes = slot_ref.shape[1]
    if isinstance(block, int):
        return slot_ref[block // lanes, block % lanes]
    return slot_ref[lax.div(block, lanes), lax.rem(block, lanes)]


def fetch_block(gath, slot, dst, row, col, sem, side):
    return pltpu.make_async_copy(
        gath.at[slot], dst.at[pl.ds(row, side), pl.ds(col, side)], sem
    )


def prepare(x_ref, block_ref, vin_ref, h1_ref, slot_ref, vec_ref):
    rows, width = x_ref.shape
    per = width // 128
    for r in range(vec_ref.shape[0]):
        for c in range(per):
            vec_ref[r:r + 1, c * 128:(c + 1) * 128] = vin_ref[per * r + c:per * r + c + 1, :]
    chunk = 16

    @pl.loop(0, rows // chunk)
    def _(r):
        at = pl.ds(pl.multiple_of(r * chunk, chunk), chunk)
        centred, inv = layer_stats(x_ref[at, :].astype(F32))
        h1_ref[at, :] = (
            centred * inv * vec_ref[GAIN1:GAIN1 + 1, :] + vec_ref[SHIFT1:SHIFT1 + 1, :]
        ).astype(BF16)

    tiles, lanes = slot_ref.shape
    line = lax.broadcasted_iota(jnp.int32, (8, lanes), 0)
    lane = lax.broadcasted_iota(jnp.int32, (8, lanes), 1).astype(F32)
    block = lax.broadcasted_iota(jnp.int32, (lanes, lanes), 0)
    for t in range(tiles):
        found = jnp.zeros((8, lanes), F32)
        for r in range(tiles):
            held = (block_ref[r:r + 1, :] == block + t * lanes).astype(F32).astype(BF16)
            found = found + dot_nt(jnp.where(line == 0, lane, float(r)).astype(BF16), held)
        slot_ref[t:t + 1, :] = (found[0:1] + float(lanes) * found[1:2]).astype(jnp.int32)


def prepared_shapes(x, blocks, vin):
    rows, width = x.shape
    return (
        sds((rows, width), BF16),
        sds(blocks.shape, jnp.int32),
        sds((vin.size // width, width), F32),
    )


def run_prepare(x, blocks, vin):
    return pl.pallas_call(
        prepare,
        out_shape=prepared_shapes(x, blocks, vin),
        in_specs=[vmem()] * 3,
        out_specs=tuple([vmem()] * 3),
        compiler_params=params(),
        name="prepare",
    )(x, blocks, vin)


def qkv_kernel(slot_ref, h1_ref, vec_ref, gath, out_ref, wq_out, wbuf, sems, sem_w, *, nd):
    rows, width = h1_ref.shape
    side = gath.shape[1]
    per = width // side
    lanes = out_ref.shape[3]
    for part in range(3):
        for i in range(per):
            for j in range(per):
                slot = slot_at(slot_ref, i * 3 * per + part * per + j)
                fetch_block(gath, slot, wbuf.at[part], i * side, j * side, sems.at[part], side).start()

    def keep(part):
        return pltpu.make_async_copy(wbuf.at[part], wq_out.at[part], sem_w.at[part])

    for part in range(3):
        pltpu.make_async_copy(wbuf.at[part], wbuf.at[part], sems.at[part]).wait()
        keep(part).start()
        for half in range(2):
            cols = slice(half * width // 2, (half + 1) * width // 2)
            res = dot_nn(h1_ref[...], wbuf[part, :, cols])
            if part == 0:
                res = res + vec_ref[BQ:BQ + 1, cols]
            if part == 2:
                res = res + vec_ref[BV:BV + 1, cols]
            res = res.astype(BF16)
            for d in range(nd // 2):
                out_ref[half * (nd // 2) + d, part, :, :] = res[:, d * lanes:(d + 1) * lanes]
    for part in range(3):
        keep(part).wait()


def run_qkv(slot_of, h1, vec, gath, nd):
    rows, width = h1.shape
    lanes = width // nd
    return pl.pallas_call(
        functools.partial(qkv_kernel, nd=nd),
        out_shape=(sds((nd, 3, rows, lanes), BF16), sds((3, width, width), BF16)),
        in_specs=[smem(), vmem(), vmem(), hbm()],
        out_specs=(vmem(), hbm()),
        scratch_shapes=[
            pltpu.VMEM((3, width, width), BF16),
            pltpu.SemaphoreType.DMA((3,)),
            pltpu.SemaphoreType.DMA((3,)),
        ],
        compiler_params=params(),
        name="qkv",
    )(slot_of, h1, vec, gath)


MESH = pl.DeviceIdType.MESH


def remote(src, dst, send, recv, device):
    return pltpu.make_async_remote_copy(
        src_ref=src, dst_ref=dst, send_sem=send, recv_sem=recv, device_id=device, device_id_type=MESH
    )


def arrived(ref, sem):
    pltpu.make_async_copy(ref, ref, sem).wait()


def cut(ref, first, size):
    return ref.at[pl.ds(first, size)]


def greet_plane(g, d, nd):
    barrier = pltpu.get_barrier_semaphore()
    for p in range(1, nd):
        pl.semaphore_signal(barrier, inc=1, device_id=(g, lax.rem(d + p, nd)), device_id_type=MESH)
    pl.semaphore_wait(barrier, nd - 1)


def landing(ref, part, source, q, tok, lanes, parts):
    if lanes % 128 == 0:
        first = (part * (ref.shape[1] // parts)) + source * lanes
        return ref.at[pl.ds(q * tok, tok), pl.ds(pl.multiple_of(first, lanes), lanes)]
    return ref.at[source, part, q]


def landing_shape(parts, nb, seqs, tok, lanes):
    if lanes % 128 == 0:
        return sds((seqs * tok, parts * nb * lanes), BF16)
    return sds((nb, parts, seqs, tok, lanes), BF16)


def side_by_side(got, parts, rows):
    if got.ndim == 2:
        return got
    nb, _, seqs, tok, lanes = got.shape
    return got.transpose(2, 3, 1, 0, 4).reshape(rows, parts * nb * lanes)


def parts3(v):
    hi = v.astype(BF16)
    mid = (v - hi.astype(F32)).astype(BF16)
    lo = (v - hi.astype(F32) - mid.astype(F32)).astype(BF16)
    return hi.astype(F32), mid.astype(F32), lo.astype(F32)


def own_lanes(h, shape, hpd, lanes):
    lane = lax.broadcasted_iota(jnp.int32, shape, 1)
    size = lanes // hpd
    return (lane >= h * size) & (lane < (h + 1) * size)


def place(values, base, tok, width):
    lane = lax.broadcasted_iota(jnp.int32, (tok, width), 1)
    out = jnp.zeros((tok, width), F32)
    for n, v in enumerate(values):
        out = jnp.where(lane == base + n, v, out)
    return out


def spare(h, hpd, lanes):
    return (lanes // hpd) * (1 - h) if hpd > 1 else 0


def column_tables(slope_ref, qbase, kbase, kfar, hpd, lanes):
    _, tok, _ = qbase.shape
    u = lax.broadcasted_iota(jnp.int32, (tok, 128), 0).astype(F32)
    for h in range(hpd):
        slope = slope_ref[h] * LOG2E
        base = spare(h, hpd, lanes)
        near = parts3(jnp.full((tok, 128), slope, F32))
        far = parts3(jnp.full((tok, 128), slope * tok, F32))
        qbase[h] = place(near + far, base, tok, 128)
        kbase[h] = place([u] * 3 + [0.0] * 3 + [1.0] * 3, base, tok, 128)
        kfar[h] = place([0.0] * 3 + [1.0] * 3, base, tok, 128)


def q_columns(q, h, hpd, columns, extra):
    tok, lanes = q.shape
    scaled = q.astype(F32) * ((lanes // hpd) ** (-0.5) * LOG2E)
    hi = scaled.astype(BF16).astype(F32)
    low = scaled - hi
    if extra:
        lane = lax.broadcasted_iota(jnp.int32, (tok, 128), 1)
        for n, v in enumerate(extra):
            columns = jnp.where(lane == spare(h, hpd, lanes) + 6 + n, v, columns)
    if hpd > 1:
        own = own_lanes(h, (tok, lanes), hpd, lanes)
        return jnp.concatenate(
            [jnp.where(own, hi, 0.0), jnp.where(own, low, columns)], axis=1
        ).astype(BF16)
    return jnp.concatenate([hi, low, columns], axis=1).astype(BF16)


def k_columns(k, h, hpd, columns):
    tok, lanes = k.shape
    wide = k.astype(F32)
    if hpd > 1:
        own = own_lanes(h, (tok, lanes), hpd, lanes)
        return jnp.concatenate([wide, jnp.where(own, wide, columns)], axis=1).astype(BF16)
    return jnp.concatenate([wide, wide, columns], axis=1).astype(BF16)


def far_side(slope, tok):
    u = lax.broadcasted_iota(jnp.int32, (tok, tok), 0)
    t = lax.broadcasted_iota(jnp.int32, (tok, tok), 1)
    after = u > t
    return (
        jnp.where(after, big_negative, 0.0),
        jnp.where(after, (2.0 * slope) * (t - u).astype(F32), 0.0),
    )


def attn_fwd_kernel(
    span_ref, slope_ref, src, got, o_got, o32_ref, lse_ref,
    qa, ka, vt, scores, corr, qbase, kbase, kfar, o_out, ss, sr, os, orr, loc, *, hpd, nd
):
    nb, _, seqs, tok, lanes = got.shape
    size = lanes // hpd
    pair = 2 * tok
    g = lax.axis_index("grp")
    d = lax.axis_index("dev")

    for q in range(seqs):
        pltpu.make_async_copy(src.at[d, :, q], got.at[d, :, q], loc.at[q]).start()
    greet_plane(g, d, nd)

    def send(q, p):
        to = lax.rem(d + p, nd)
        return remote(src.at[to, :, q], got.at[d, :, q], ss.at[q, p], sr.at[q, p], (g, to))

    def send_all(q):
        @pl.loop(1, nd)
        def _(p):
            send(q, p).start()

    send_all(0)

    def o_place(source, q):
        return landing(o_got, 0, source, q, tok, lanes, 1)

    def send_o(q, i, p):
        return remote(o_out.at[i, q], o_place(d, q), os.at[q, i], orr.at[q, p], (g, i))

    column_tables(slope_ref, qbase, kbase, kfar, hpd, lanes)
    for h in range(hpd):
        mask, span = far_side(slope_ref[h] * LOG2E, tok)
        for n, (one, two) in enumerate(((mask, mask), (span, mask), (mask, span))):
            corr[h, n, 0:tok, 0:tok] = one
            corr[h, n, tok:, tok:] = two
            corr[h, n, 0:tok, tok:] = jnp.zeros((tok, tok), F32)
            corr[h, n, tok:, 0:tok] = jnp.full((tok, tok), big_negative, F32)

    for q in range(seqs):
        pltpu.make_async_copy(src.at[d, :, q], got.at[d, :, q], loc.at[q]).wait()

        @pl.loop(1, nd)
        def _(p):
            arrived(got.at[lax.rem(d + nd - p, nd), :, q], sr.at[q, p])

        if q + 1 < seqs:
            send_all(q + 1)

        @pl.loop(0, nb)
        def _(j):
            at_j = pl.ds(pl.multiple_of(j * tok, tok), tok)
            vt[0:lanes, at_j] = got[j, 2, q].astype(F32).T.astype(BF16)
            block = jnp.full((tok, 128), j, jnp.int32).astype(F32)
            for h in range(hpd):
                qa[h, at_j, :] = q_columns(got[j, 0, q], h, hpd, qbase[h], [])
                ka[h, at_j, :] = k_columns(got[j, 1, q], h, hpd, kbase[h] + block * kfar[h])

        start = span_ref[q]

        @pl.loop(0, nb // 2)
        def _(i):
            flag = (start == i * pair).astype(jnp.int32) + 2 * (start == i * pair + tok).astype(jnp.int32)

            def at_pair(n):
                return pl.ds(pl.multiple_of(n * pair, pair), pair)

            def fold_max(v):
                return jnp.max(v.reshape(pair // 8, 8, pair), axis=0)

            def score(n, tops):
                new = []
                for h in range(hpd):
                    s = dot_nt(ka[h, at_pair(n), :], qa[h, at_pair(i), :])
                    scores[h, at_pair(n), :] = s
                    new.append(jnp.maximum(tops[h], fold_max(s)))
                return tuple(new)

            tops = lax.fori_loop(
                0, i, score, tuple([jnp.full((8, pair), big_negative, F32)] * hpd)
            )
            top = []
            for h in range(hpd):
                s = dot_nt(ka[h, at_pair(i), :], qa[h, at_pair(i), :]) + corr[h, flag]
                scores[h, at_pair(i), :] = s
                top.append(jnp.max(jnp.maximum(tops[h], fold_max(s)), axis=0, keepdims=True))

            def weigh(n, state):
                new = []
                for h in range(hpd):
                    acc, total = state[h]
                    p = jnp.exp2(scores[h, at_pair(n), :] - top[h])
                    total = total + jnp.sum(p.reshape(pair // 8, 8, pair), axis=0)
                    acc = acc + dot_nn(vt[h * size:(h + 1) * size, at_pair(n)], p.astype(BF16))
                    new.append((acc, total))
                return tuple(new)

            state = lax.fori_loop(
                0,
                i + 1,
                weigh,
                tuple([(jnp.zeros((size, pair), F32), jnp.zeros((8, pair), F32))] * hpd),
            )
            outs = []
            logs = []
            for h in range(hpd):
                acc, total = state[h]
                total = jnp.sum(total, axis=0, keepdims=True)
                outs.append(acc / total)
                logs.append(jnp.broadcast_to(top[h] + jnp.log2(total), (128 // hpd, pair)))
            out = (jnp.concatenate(outs, axis=0) if hpd > 1 else outs[0]).T
            log = (jnp.concatenate(logs, axis=0) if hpd > 1 else logs[0]).T
            for k in range(2):
                at = 2 * i + k
                o32_ref[at, q] = out[k * tok:(k + 1) * tok]
                o_out[at, q] = out[k * tok:(k + 1) * tok].astype(BF16)
                lse_ref[at, q] = log[k * tok:(k + 1) * tok]

                @pl.when(at == d)
                def _():
                    pltpu.make_async_copy(o_out.at[at, q], o_place(d, q), os.at[q, at]).start()

                @pl.when(at != d)
                def _():
                    send_o(q, at, lax.rem(at - d + nd, nd)).start()

    for q in range(seqs):
        @pl.loop(1, nd)
        def _(p):
            arrived(o_place(lax.rem(d + nd - p, nd), q), orr.at[q, p])
            send(q, p).wait_send()

        @pl.loop(0, nd)
        def _(i):
            arrived(o_out.at[i, q], os.at[q, i])


def run_attn_fwd(span, slopes, qkv, hpd):
    nb, _, seqs, tok, lanes = qkv.shape
    t = nb * tok
    dma = pltpu.SemaphoreType.DMA
    return pl.pallas_call(
        functools.partial(attn_fwd_kernel, hpd=hpd, nd=nb),
        out_shape=(
            sds(qkv.shape, BF16),
            landing_shape(1, nb, seqs, tok, lanes),
            sds((nb, seqs, tok, lanes), F32),
            sds((nb, seqs, tok, 128), F32),
        ),
        in_specs=[smem(), smem(), hbm()],
        out_specs=(vmem(), vmem(), vmem(), vmem()),
        scratch_shapes=[
            pltpu.VMEM((hpd, t, 256), BF16),
            pltpu.VMEM((hpd, t, 256), BF16),
            pltpu.VMEM((lanes, t), BF16),
            pltpu.VMEM((hpd, t, 2 * tok), F32),
            pltpu.VMEM((hpd, 3, 2 * tok, 2 * tok), F32),
            pltpu.VMEM((hpd, tok, 128), F32),
            pltpu.VMEM((hpd, tok, 128), F32),
            pltpu.VMEM((hpd, tok, 128), F32),
            pltpu.VMEM((nb, seqs, tok, lanes), BF16),
            dma((seqs, nb)),
            dma((seqs, nb)),
            dma((seqs, nb)),
            dma((seqs, nb)),
            dma((seqs,)),
        ],
        compiler_params=params(collective_id=2, has_side_effects=True),
        name="attn_fwd",
    )(span, slopes, qkv)


def attn_bwd_kernel(
    span_ref, slope_ref, qkv_ref, do_src, o32_ref, lse_ref, got,
    do_got, out, qa, ka, kt, va, qm, da, dm, dqt, corr, qbase, kbase, kfar, dk_ref, dv_ref,
    ss, sr, gs, gr, loc, *, hpd, nd
):
    nb, _, seqs, tok, lanes = qkv_ref.shape
    size = lanes // hpd
    unit = size ** (-0.5)
    g = lax.axis_index("grp")
    d = lax.axis_index("dev")

    def own_copy(q):
        return pltpu.make_async_copy(do_src.at[d, q], do_got.at[d, q], loc.at[q])

    for q in range(seqs):
        own_copy(q).start()
    greet_plane(g, d, nd)

    def send(q, p):
        to = lax.rem(d + p, nd)
        return remote(do_src.at[to, q], do_got.at[d, q], ss.at[q, p], sr.at[q, p], (g, to))

    def send_all(q):
        @pl.loop(1, nd)
        def _(p):
            send(q, p).start()

    send_all(0)

    def place_back(kind, source, q):
        return landing(got, kind, source, q, tok, lanes, 3)

    def back(q, kind, p):
        to = lax.rem(d + p, nd)
        return remote(
            out.at[to, kind, q], place_back(kind, d, q), gs.at[q, kind, p], gr.at[q, kind, p], (g, to)
        )

    def back_own(q, kind):
        return pltpu.make_async_copy(out.at[d, kind, q], place_back(kind, d, q), gs.at[q, kind, 0])

    for h in range(hpd):
        mask, span = far_side(slope_ref[h] * LOG2E, tok)
        for n, table in enumerate((mask, span)):
            corr[h, n, :, 0:tok] = table
            corr[h, n, :, tok:] = jnp.zeros((tok, tok), F32)
    column_tables(slope_ref, qbase, kbase, kfar, hpd, lanes)

    for q in range(seqs):
        @pl.loop(0, nb)
        def _(j):
            at_j = pl.ds(pl.multiple_of(j * tok, tok), tok)
            qj = qkv_ref[j, 0, q]
            kj = qkv_ref[j, 1, q]
            vj = qkv_ref[j, 2, q].astype(F32)
            kt[:, at_j] = kj.astype(F32).T.astype(BF16)
            dqt[:, at_j] = jnp.zeros((lanes, tok), F32)
            block = jnp.full((tok, 128), j, jnp.int32).astype(F32)
            for h in range(hpd):
                low = lse_ref[j, q][:, h * (128 // hpd):h * (128 // hpd) + 1]
                extra = [-p for p in parts3(low)]
                qa[h, at_j, :] = q_columns(qj, h, hpd, qbase[h], extra)
                ka[h, j] = k_columns(kj, h, hpd, kbase[h] + block * kfar[h])
                if hpd > 1:
                    own = own_lanes(h, (tok, lanes), hpd, lanes)
                    qm[h, at_j, :] = jnp.where(own, qj.astype(F32), 0.0).astype(BF16)
                    va[h, j] = jnp.where(own, vj, kbase[h]).astype(BF16)
                else:
                    qm[h, at_j, :] = qj
                    va[h, j] = jnp.concatenate([vj, kbase[h][:, 0:lanes]], axis=1).astype(BF16)

        own_copy(q).wait()

        @pl.loop(1, nd)
        def _(p):
            arrived(do_got.at[lax.rem(d + nd - p, nd), q], sr.at[q, p])

        if q + 1 < seqs:
            send_all(q + 1)

        @pl.loop(0, nb)
        def _(j):
            at_j = pl.ds(pl.multiple_of(j * tok, tok), tok)
            do = do_got[j, q].astype(F32)
            prod = do * o32_ref[j, q]
            for h in range(hpd):
                if hpd > 1:
                    own = own_lanes(h, (tok, lanes), hpd, lanes)
                    delta = jnp.sum(jnp.where(own, prod, 0.0), axis=1, keepdims=True)
                    extra = place([-p for p in parts3(delta)], spare(h, hpd, lanes) + 6, tok, lanes)
                    da[h, at_j, :] = jnp.where(own, do, extra).astype(BF16)
                    dm[h, at_j, :] = jnp.where(own, do, 0.0).astype(BF16)
                else:
                    delta = jnp.sum(prod, axis=1, keepdims=True)
                    extra = place([-p for p in parts3(delta)], 6, tok, lanes)
                    da[h, at_j, :] = jnp.concatenate([do, extra], axis=1).astype(BF16)
                    dm[h, at_j, :] = do.astype(BF16)

        start = span_ref[q]

        @pl.loop(0, nb)
        def _(n):
            j = lax.rem(d + n, nb)
            at_j = pl.ds(pl.multiple_of(j * tok, tok), tok)
            flag = (start == j * tok).astype(jnp.int32)

            def tile(i, width, near):
                at_i = pl.ds(pl.multiple_of(i * tok, tok), width)
                dk = None
                for h in range(hpd):
                    s = dot_nt(ka[h, j], qa[h, at_i, :])
                    if near:
                        s = s + corr[h, flag, :, 0:width]
                    p = jnp.exp2(s)
                    ds = (p * dot_nt(va[h, j], da[h, at_i, :])).astype(BF16)
                    dv_h = dot_nn(p.astype(BF16), dm[h, at_i, :])
                    dk_h = dot_nn(ds, qm[h, at_i, :])
                    dk = dk_h if dk is None else dk + dk_h
                    dv = dv_h if h == 0 else dv + dv_h
                    rows = slice(h * size, (h + 1) * size)
                    dqt[rows, at_i] += dot_nn(kt[rows, at_j], ds)
                if near:
                    dk_ref[...] = dk
                    dv_ref[...] = dv
                else:
                    dk_ref[...] += dk
                    dv_ref[...] += dv

            odd = lax.rem(nb - j, 2)

            @pl.when(odd == 1)
            def _():
                tile(j, tok, True)

            @pl.when(odd == 0)
            def _():
                tile(j, 2 * tok, True)

            @pl.loop(0, (nb - j - 1) // 2)
            def _(m):
                tile(j + 2 - odd + 2 * m, 2 * tok, False)

            out[j, 1, q] = (dk_ref[...] * unit).astype(BF16)
            out[j, 2, q] = dv_ref[...].astype(BF16)

            for kind in (1, 2):
                @pl.when(n == 0)
                def _():
                    back_own(q, kind).start()

                @pl.when(n > 0)
                def _():
                    back(q, kind, n).start()

        @pl.loop(0, nb)
        def _(n):
            j = lax.rem(d + n, nb)
            at_j = pl.ds(pl.multiple_of(j * tok, tok), tok)
            out[j, 0, q] = (dqt[:, at_j].T * unit).astype(BF16)

            @pl.when(n == 0)
            def _():
                back_own(q, 0).start()

            @pl.when(n > 0)
            def _():
                back(q, 0, n).start()

    for q in range(seqs):
        for kind in range(3):
            back_own(q, kind).wait()

        @pl.loop(1, nd)
        def _(p):
            send(q, p).wait_send()
            source = lax.rem(d + nd - p, nd)
            for kind in range(3):
                back(q, kind, p).wait_send()
                arrived(place_back(kind, source, q), gr.at[q, kind, p])


def run_attn_bwd(span, slopes, qkv, do, o32, lse, hpd):
    nb, _, seqs, tok, lanes = qkv.shape
    t = nb * tok
    dma = pltpu.SemaphoreType.DMA
    wide = 128 if hpd == 1 else lanes
    return pl.pallas_call(
        functools.partial(attn_bwd_kernel, hpd=hpd, nd=nb),
        out_shape=landing_shape(3, nb, seqs, tok, lanes),
        in_specs=[smem(), smem(), vmem(), hbm(), vmem(), vmem()],
        out_specs=vmem(),
        scratch_shapes=[
            pltpu.VMEM((nb, seqs, tok, lanes), BF16),
            pltpu.VMEM(qkv.shape, BF16),
            pltpu.VMEM((hpd, t, 256), BF16),
            pltpu.VMEM((hpd, nb, tok, 256), BF16),
            pltpu.VMEM((lanes, t), BF16),
            pltpu.VMEM((hpd, nb, tok, wide), BF16),
            pltpu.VMEM((hpd, t, lanes), BF16),
            pltpu.VMEM((hpd, t, wide), BF16),
            pltpu.VMEM((hpd, t, lanes), BF16),
            pltpu.VMEM((lanes, t), F32),
            pltpu.VMEM((hpd, 2, tok, 2 * tok), F32),
            pltpu.VMEM((hpd, tok, 128), F32),
            pltpu.VMEM((hpd, tok, 128), F32),
            pltpu.VMEM((hpd, tok, 128), F32),
            pltpu.VMEM((tok, lanes), F32),
            pltpu.VMEM((tok, lanes), F32),
            dma((seqs, nb)),
            dma((seqs, nb)),
            dma((seqs, 3, nb)),
            dma((seqs, 3, nb)),
            dma((seqs,)),
        ],
        compiler_params=params(collective_id=3, has_side_effects=True),
        name="attn_bwd",
    )(span, slopes, qkv, do, o32, lse)


def turn(v):
    return v.astype(F32).T.astype(BF16)


def mlp_kernel(
    slot_ref, att_ref, x_ref, dy_ref, vec_ref, gath,
    act_out, dx1_out, do_out, sums_ref, grads,
    wo, wup, wdn, x1, acc, dh2, h2_ref, h2t, attt, da_ref, act_ref, dx1_ref, do_ref, stage,
    sem_o, sem_t, sem_g, sem_w, *, nd, first_o, first_up, first_dn, tile
):
    rows, width = x_ref.shape
    side = gath.shape[1]
    per = width // side
    tiles = wup.shape[0]
    ff = tiles * tile
    cols = tile // side
    lanes = do_ref.shape[2]
    fper = ff // side

    for i in range(per):
        for j in range(per):
            fetch_block(gath, slot_at(slot_ref, first_o + i * per + j), wo, i * side, j * side, sem_o.at[0], side).start()

    def fetch_tile(f):
        for i in range(per):
            for j in range(cols):
                fetch_block(gath, slot_at(slot_ref, first_up + i * fper + f * cols + j), wup.at[f], i * side, j * side, sem_t.at[f], side).start()
            for j in range(cols):
                fetch_block(gath, slot_at(slot_ref, first_dn + (f * cols + j) * per + i), wdn.at[f], j * side, i * side, sem_t.at[f], side).start()

    fetch_tile(0)
    fetch_tile(1)
    for r in range(width // 256):
        attt[r * 256:(r + 1) * 256, :] = turn(att_ref[:, r * 256:(r + 1) * 256])
    pltpu.make_async_copy(wo, wo, sem_o.at[0]).wait()
    for half in range(2):
        c = slice(half * width // 2, (half + 1) * width // 2)
        x1[:, c] = x_ref[:, c].astype(F32) + dot_nn(att_ref[...], wo[:, c]) + vec_ref[BO:BO + 1, c]

    chunk = 16

    def rows_at(r):
        return pl.ds(pl.multiple_of(r * chunk, chunk), chunk)

    @pl.loop(0, rows // chunk)
    def _(r):
        at = rows_at(r)
        centred, inv = layer_stats(x1[at, :])
        h2_ref[at, :] = (centred * inv * vec_ref[GAIN2:GAIN2 + 1, :] + vec_ref[SHIFT2:SHIFT2 + 1, :]).astype(BF16)
        acc[at, :] = x1[at, :] + vec_ref[BDOWN:BDOWN + 1, :]
        dh2[at, :] = jnp.zeros((chunk, width), F32)

    for r in range(width // 256):
        h2t[r * 256:(r + 1) * 256, :] = turn(h2_ref[:, r * 256:(r + 1) * 256])

    def put(slot, first, res, down, across):
        for i in range(down):
            for j in range(across):
                stage[slot, first + i * across + j] = res[i * side:(i + 1) * side, j * side:(j + 1) * side]

    def leave(slot, n, block):
        pltpu.make_async_copy(stage.at[slot, n], grads.at[slot_at(slot_ref, block)], sem_g.at[slot]).start()

    def left(slot, size):
        at = stage.at[slot, pl.ds(0, size)]
        pltpu.make_async_copy(at, at, sem_g.at[slot]).wait()

    full = 2 * per * cols

    @pl.loop(0, tiles)
    def _(f):
        @pl.when(f + 2 < tiles)
        def _():
            fetch_tile(f + 2)
        pltpu.make_async_copy(wup.at[f], wup.at[f], sem_t.at[f]).wait()
        pltpu.make_async_copy(wdn.at[f], wdn.at[f], sem_t.at[f]).wait()
        per_row = width // tile
        bias = vec_ref[pl.ds(BUP + f // per_row, 1), pl.ds(pl.multiple_of((f % per_row) * tile, tile), tile)]
        z = dot_nn(h2_ref[...], wup[f]) + bias
        dg = dot_nt(dy_ref[...], wdn[f])
        z2 = z * z
        th = jnp.tanh(0.7978845608028654 * (z + 0.044715 * z2 * z))
        g = (0.5 * z * (1.0 + th)).astype(BF16)
        slope = 0.5 * (1.0 + th) + 0.5 * z * (1.0 - th * th) * (
            0.7978845608028654 * (1.0 + 3.0 * 0.044715 * z2)
        )
        dz = (dg * slope).astype(BF16)
        sums_ref[pl.ds(pl.multiple_of(8 * (4 + f // per_row), 8), 8), pl.ds(pl.multiple_of((f % per_row) * tile, tile), tile)] = fold_rows(dz.astype(F32))
        acc[...] += dot_nn(g, wdn[f])
        dh2[...] += dot_nt(dz, wup[f])
        slot = lax.rem(f, 2)

        @pl.when(f >= 2)
        def _():
            left(slot, full)
        put(slot, 0, dot_nn(turn(g), dy_ref[...]).astype(BF16), cols, per)
        put(slot, per * cols, dot_nn(h2t[...], dz).astype(BF16), per, cols)

        for i in range(per):
            for j in range(cols):
                leave(slot, j * per + i, first_dn + (f * cols + j) * per + i)
            for j in range(cols):
                leave(slot, per * cols + i * cols + j, first_up + i * fper + f * cols + j)

    zero = jnp.zeros((8, width), F32)

    def finish(r, carry):
        s_bo, s_gain, s_shift, s_bdown = carry
        at = rows_at(r)
        act_ref[at, :] = acc[at, :].astype(BF16)
        centred, inv = layer_stats(x1[at, :])
        hat = centred * inv
        dh = dh2[at, :]
        dhg = dh * vec_ref[GAIN2:GAIN2 + 1, :]
        back = inv * (
            dhg
            - jnp.mean(dhg, axis=-1, keepdims=True)
            - hat * jnp.mean(dhg * hat, axis=-1, keepdims=True)
        )
        dy = dy_ref[at, :].astype(F32)
        dx1 = dy + back
        dx1_ref[at, :] = dx1
        da = dx1.astype(BF16)
        da_ref[at, :] = da
        return (
            s_bo + fold_rows(da.astype(F32)),
            s_gain + fold_rows(dh * hat),
            s_shift + fold_rows(dh),
            s_bdown + fold_rows(dy),
        )

    carry = lax.fori_loop(0, rows // chunk, finish, (zero, zero, zero, zero))
    for n in range(4):
        sums_ref[8 * n:8 * n + 8, :] = carry[n]
    outs = [
        pltpu.make_async_copy(act_ref, act_out, sem_w.at[0]),
        pltpu.make_async_copy(dx1_ref, dx1_out, sem_w.at[1]),
        pltpu.make_async_copy(do_ref, do_out, sem_w.at[2]),
    ]
    outs[0].start()
    outs[1].start()
    for half in range(2):
        c = slice(half * width // 2, (half + 1) * width // 2)
        res = dot_nt(da_ref[...], wo[c, :]).astype(BF16)
        for d in range(nd // 2):
            do_ref[half * (nd // 2) + d] = res[:, d * lanes:(d + 1) * lanes]
    outs[2].start()
    left(0, full)
    left(1, full)
    half_rows = width // 2
    for half in range(2):
        res = dot_nn(attt[half * half_rows:(half + 1) * half_rows, :], da_ref[...]).astype(BF16)
        put(half, 0, res, per // 2, per)

        for i in range(per // 2):
            for j in range(per):
                leave(half, i * per + j, first_o + (half * (per // 2) + i) * per + j)
    for half in range(2):
        left(half, per * per // 2)
    for copy in outs:
        copy.wait()


def run_mlp(slot_of, att, x, dy, vec, gath, nd):
    rows, width = x.shape
    side = gath.shape[1]
    lanes = width // nd
    per = width // side
    first_o = 3 * per * per
    first_up = first_o + per * per
    first_dn = first_up + per * (FF // side)
    tile = 512
    f32_rows = pltpu.VMEM((rows, width), F32)
    bf16_rows = pltpu.VMEM((rows, width), BF16)
    turned = pltpu.VMEM((width, rows), BF16)
    return pl.pallas_call(
        functools.partial(
            mlp_kernel, nd=nd, first_o=first_o, first_up=first_up, first_dn=first_dn, tile=tile
        ),
        out_shape=(
            sds((rows, width), BF16),
            sds((rows, width), F32),
            sds((nd, rows, lanes), BF16),
            sds((8 * (4 + FF // width), width), F32),
            sds(gath.shape, BF16),
        ),
        in_specs=[smem(), vmem(), vmem(), vmem(), vmem(), hbm()],
        out_specs=(hbm(), hbm(), hbm(), vmem(), hbm()),
        scratch_shapes=[
            pltpu.VMEM((width, width), BF16),
            pltpu.VMEM((FF // tile, width, tile), BF16),
            pltpu.VMEM((FF // tile, tile, width), BF16),
            f32_rows,
            f32_rows,
            f32_rows,
            bf16_rows,
            turned,
            turned,
            bf16_rows,
            bf16_rows,
            f32_rows,
            pltpu.VMEM((nd, rows, lanes), BF16),
            pltpu.VMEM((2, 2 * per * (tile // side), side, side), BF16),
            pltpu.SemaphoreType.DMA((1,)),
            pltpu.SemaphoreType.DMA((FF // tile,)),
            pltpu.SemaphoreType.DMA((2,)),
            pltpu.SemaphoreType.DMA((3,)),
        ],
        compiler_params=params(),
        name="mlp",
    )(slot_of, att, x, dy, vec, gath)


def dh1_dot(cat, w, dh1, part, half):
    width = dh1.shape[1]
    c = slice(half * width // 2, (half + 1) * width // 2)
    res = dot_nt(cat[:, part * width:(part + 1) * width], w[part, c, :])
    if part == 0:
        dh1[:, c] = res
    else:
        dh1[:, c] += res


def first_norm_back(cat, x, dh1, dx1, ig, vec_ref):
    rows, width = x.shape
    chunk = 16
    zero = jnp.zeros((8, width), F32)

    def finish(r, carry):
        s_gain, s_shift, s_bq, s_bv = carry
        at = pl.ds(pl.multiple_of(r * chunk, chunk), chunk)
        centred, inv = layer_stats(x[at, :].astype(F32))
        hat = centred * inv
        dh = dh1[at, :]
        dhg = dh * vec_ref[GAIN1:GAIN1 + 1, :]
        back = inv * (
            dhg
            - jnp.mean(dhg, axis=-1, keepdims=True)
            - hat * jnp.mean(dhg * hat, axis=-1, keepdims=True)
        )
        ig[at, :] = dx1[at, :] + back
        return (
            s_gain + fold_rows(dh * hat),
            s_shift + fold_rows(dh),
            s_bq + fold_rows(cat[at, 0:width].astype(F32)),
            s_bv + fold_rows(cat[at, 2 * width:3 * width].astype(F32)),
        )

    return lax.fori_loop(0, rows // chunk, finish, (zero, zero, zero, zero))


def vector_rows(first, sums2):
    rows = [jnp.sum(v, axis=0, keepdims=True) for v in first]
    rows += [jnp.sum(sums2[8 * n:8 * n + 8, :], axis=0, keepdims=True) for n in range(sums2.shape[0] // 8)]
    return rows


def dh1_kernel(cat_ref, x_ref, dx1_ref, vec_ref, wq_ref, sums2_ref, ig_ref, vsum_ref, dh1):
    for part in range(3):
        for half in range(2):
            dh1_dot(cat_ref, wq_ref, dh1, part, half)
    first = first_norm_back(cat_ref, x_ref, dh1, dx1_ref, ig_ref, vec_ref)
    for n, row in enumerate(vector_rows(first, sums2_ref)):
        vsum_ref[n:n + 1, :] = row


def run_dh1(cat, x, dx1, vec, wq, sums2):
    rows, width = x.shape
    return pl.pallas_call(
        dh1_kernel,
        out_shape=(sds((rows, width), F32), sds(vec.shape, F32)),
        in_specs=[vmem()] * 6,
        out_specs=(vmem(), vmem()),
        scratch_shapes=[pltpu.VMEM((rows, width), F32)],
        compiler_params=params(),
        name="dh1",
    )(cat, x, dx1, vec, wq, sums2)


def wgrad_kernel(slot_ref, h1_ref, cat_ref, rest, out, a_t, stage, sem_out, *, side, tile):
    del rest
    rows, width = h1_ref.shape
    per = width // side
    cols = tile // side
    steps = cat_ref.shape[1] // tile
    for r in range(width // 256):
        c = slice(r * 256, (r + 1) * 256)
        a_t[c, :] = turn(h1_ref[:, c])

    def left(slot):
        pltpu.make_async_copy(stage.at[slot], stage.at[slot], sem_out.at[slot]).wait()

    @pl.loop(0, steps)
    def _(t):
        slot = lax.rem(t, 2)

        @pl.when(t >= 2)
        def _():
            left(slot)
        res = dot_nn(a_t[...], cat_ref[:, pl.ds(pl.multiple_of(t * tile, tile), tile)]).astype(BF16)
        for i in range(per):
            for j in range(cols):
                stage[slot, i * cols + j] = res[i * side:(i + 1) * side, j * side:(j + 1) * side]

        for i in range(per):
            for j in range(cols):
                dst = slot_at(slot_ref, i * 3 * per + t * cols + j)
                pltpu.make_async_copy(stage.at[slot, i * cols + j], out.at[dst], sem_out.at[slot]).start()

    left(0)
    left(1)


def run_wgrad(slot_of, h1, cat, grads):
    rows, width = h1.shape
    side = grads.shape[1]
    tile = 512
    return pl.pallas_call(
        functools.partial(wgrad_kernel, side=side, tile=tile),
        out_shape=sds(grads.shape, BF16),
        in_specs=[smem(), vmem(), vmem(), hbm()],
        out_specs=hbm(),
        scratch_shapes=[
            pltpu.VMEM((width, rows), BF16),
            pltpu.VMEM((2, (width // side) * (tile // side), side, side), BF16),
            pltpu.SemaphoreType.DMA((2,)),
        ],
        input_output_aliases={3: 0},
        compiler_params=params(),
        name="wgrad",
    )(slot_of, h1, cat, grads)


def whereami():
    g = lax.axis_index("grp")
    d = lax.axis_index("dev")
    core = lax.rem(d, 2)
    x = lax.rem(d // 2, 2)
    y = d // 4
    over_x = d + 2 - 4 * x
    over_y = d + 4 - 8 * y
    across = over_x + 4 - 8 * y
    sibling = d + 1 - 2 * core
    return g, d, over_x, over_y, across, sibling


def near_order(t, g, ng):
    t = ng - 1 - t
    low = jnp.where(t < ng - 1 - g, ng - 1 - t, t - (ng - 1 - g))
    high = jnp.where(t < g, t, ng - 1 - (t - g))
    return jnp.where(2 * g < ng, low, high)


def greet(g, ng, peers):
    barrier = pltpu.get_barrier_semaphore()
    for peer in peers:
        pl.semaphore_signal(barrier, inc=1, device_id=(g, peer), device_id_type=MESH)

    d = lax.axis_index("dev")

    @pl.when(g > 0)
    def _():
        pl.semaphore_signal(barrier, inc=1, device_id=(g - 1, d), device_id_type=MESH)

    @pl.when(g < ng - 1)
    def _():
        pl.semaphore_signal(barrier, inc=1, device_id=(g + 1, d), device_id_type=MESH)

    ends = (g > 0).astype(jnp.int32) + (g < ng - 1).astype(jnp.int32)
    pl.semaphore_wait(barrier, len(peers) + ends)


def slot_cuts(count):
    third = 2 * (count // 12)
    first = (count - third) // 2
    return first, count - third - first, third // 2, third // 2


def gather_kernel(
    w_ref, x_ref, block_ref, vin_ref, out, h1_ref, slot_ref, vec_ref,
    own, local_sem, zs, zr, cs, cr, ss, sr, *, ng, nd
):
    count = w_ref.shape[0]
    na, nb, nc1, nc2 = slot_cuts(count)
    flat = na + nb
    nc = nc1 + nc2
    g, d, over_x, over_y, across, sibling = whereami()
    columns = (d, over_x, over_y, across)
    own[...] = w_ref[...].astype(BF16)
    greet(g, ng, (over_x, over_y, sibling))

    def region(gz, dev, first=0, size=count):
        return out.at[pl.ds((gz * nd + dev) * count + first, size)]

    def wide(t):
        return count if t == 0 else flat

    def kind(n, t):
        return (
            (d, 0, wide(t), over_x),
            (d, 0, wide(t), over_y),
            (d, 0, wide(t), sibling),
            (over_x, 0, na, over_y),
            (over_y, na, nb, over_x),
            (over_x, 0, wide(t), sibling),
            (over_y, 0, wide(t), sibling),
            (across, 0, na, sibling),
            (across, na, nb, sibling),
            (over_x, flat, nc1, over_y),
            (over_y, flat + nc1, nc2, over_x),
            (across, flat, nc1, sibling),
            (across, flat + nc1, nc2, sibling),
            (d, flat, nc, sibling),
            (over_x, flat, nc, sibling),
            (over_y, flat, nc, sibling),
            (across, flat, nc, sibling),
        )[n]

    def kinds(t):
        return range(13) if t == 0 else tuple(range(9)) + tuple(range(13, 17))

    def plane(n, t, src=None):
        gz = near_order(t, g, ng)
        dev, first, size, to = kind(n, t)
        at = region(gz, dev, first, size)
        return remote(at if src is None else src, at, ss.at[n, gz], sr.at[n, gz], (g, to))

    def landed(n, t, dev):
        gz = near_order(t, g, ng)
        _, first, size, _ = kind(n, t)
        arrived(region(gz, dev, first, size), sr.at[n, gz])

    def line(gz, up, src=None):
        at = region(gz, d, 0, flat)
        to = g + 1 if up else g - 1
        return remote(at if src is None else src, at, zs.at[gz, int(up)], zr.at[gz], (to, d))

    def corner_line(gz, c, up, src=None):
        at = region(gz, columns[c], flat, nc)
        to = g + 1 if up else g - 1
        return remote(at if src is None else src, at, cs.at[gz, c, int(up)], cr.at[gz, c], (to, d))

    def both_ways(gz, make):
        @pl.when((gz <= g) & (g < ng - 1))
        def _():
            make(True)

        @pl.when((gz >= g) & (g > 0))
        def _():
            make(False)

    mine = pltpu.make_async_copy(own, region(g, d), local_sem.at[0])
    mine.start()

    def column(t):
        gz = near_order(t, g, ng)
        if t == 0:
            both_ways(gz, lambda up: line(gz, up, cut(own, 0, flat)).start())
            for n in range(3):
                plane(n, t, own).start()
            both_ways(gz, lambda up: corner_line(gz, 0, up, cut(own, flat, nc)).start())
            return
        arrived(region(gz, d, 0, flat), zr.at[gz])
        both_ways(gz, lambda up: line(gz, up).start())
        for n in range(3):
            plane(n, t).start()

    def sides(t):
        gz = near_order(t, g, ng)
        landed(0, t, over_x)
        plane(3, t).start()
        if t == 0:
            plane(9, t).start()
            both_ways(gz, lambda up: corner_line(gz, 1, up).start())
        plane(5, t).start()
        landed(1, t, over_y)
        plane(4, t).start()
        if t == 0:
            plane(10, t).start()
            both_ways(gz, lambda up: corner_line(gz, 2, up).start())
        plane(6, t).start()

    def corner(t):
        gz = near_order(t, g, ng)
        if t == 0:
            landed(9, t, across)
            landed(10, t, across)
            both_ways(gz, lambda up: corner_line(gz, 3, up).start())
            plane(11, t).start()
            plane(12, t).start()
        landed(3, t, across)
        plane(7, t).start()
        landed(4, t, across)
        plane(8, t).start()

    def far_corner(t):
        gz = near_order(t, g, ng)
        for c in range(4):
            arrived(region(gz, columns[c], flat, nc), cr.at[gz, c])
            both_ways(gz, lambda up: corner_line(gz, c, up).start())
            plane(13 + c, t).start()

    plan = [(t, f) for t in range(ng) for f in (0, 1, 2, 3) if t > 0 or f < 3]
    lag = {0: 0, 1: 1.5, 2: 2.6, 3: 2.2}
    for t, f in sorted(plan, key=lambda e: e[0] * 1.0 + lag[e[1]]):
        (column, sides, corner, far_corner)[f](t)
        if (t, f) == (0, 0):
            prepare(x_ref, block_ref, vin_ref, h1_ref, slot_ref, vec_ref)

    for t in range(ng):
        for n in kinds(t):
            dev, _, _, to = kind(n, t)
            if to is sibling:
                landed(n, t, dev + sibling - d)
    mine.wait()
    for t in range(ng):
        gz = near_order(t, g, ng)
        for n in kinds(t):
            plane(n, t).wait_send()
        both_ways(gz, lambda up: line(gz, up).wait_send())
        for c in range(4):
            both_ways(gz, lambda up: corner_line(gz, c, up).wait_send())


def run_gather(w, x, blocks, vin, ng, nd):
    count, side, _ = w.shape
    dma = pltpu.SemaphoreType.DMA
    return pl.pallas_call(
        functools.partial(gather_kernel, ng=ng, nd=nd),
        out_shape=(sds((ng * nd * count, side, side), BF16),) + prepared_shapes(x, blocks, vin),
        in_specs=[vmem()] * 4,
        out_specs=(hbm(), vmem(), vmem(), vmem()),
        scratch_shapes=[
            pltpu.VMEM((count, side, side), BF16),
            dma((1,)),
            dma((ng, 2)),
            dma((ng,)),
            dma((ng, 4, 2)),
            dma((ng, 4)),
            dma((17, ng)),
            dma((17, ng)),
        ],
        compiler_params=params(collective_id=0, has_side_effects=True),
        name="gather",
    )(w, x, blocks, vin)


def add_blocks(dst, src, size):
    step = 4 if size % 4 == 0 else 2 if size % 2 == 0 else 1

    @pl.loop(0, size // step)
    def _(n):
        for k in range(step):
            dst[n * step + k] = dst[n * step + k] + src[n * step + k]


def scatter_kernel(
    grads, sums2_ref, vec_ref, vin_ref, cat_in, x_in, dx1_in, wq_in, out_ref, vout_ref, vnew_ref, ig_out,
    cat, x, dx1, wq, dh1, sem_in, mine, r0, r1y, r1x, r2x, r2y, rz, cz, cy, cx, cx2, cy2, vwork, vxy, vz,
    load, s0, w0, s1, w1, s2, w2, sz, wz, sc, wc, s3, w3, vs, vw, *, ng, nd, rate
):
    count = out_ref.shape[0]
    na, nb, nc1, nc2 = slot_cuts(count)
    flat = na + nb
    nc = nc1 + nc2
    g, d, over_x, over_y, across, sibling = whereami()
    columns = (d, over_x, over_y, across)

    def region(gz, dev):
        return grads.at[pl.ds((gz * nd + dev) * count, count)]

    def order(t):
        return near_order(ng - 1 - t, g, ng)

    for t in range(ng):
        for c in range(4):
            pltpu.make_async_copy(region(order(t), columns[c]), mine.at[order(t), c], load.at[order(t), c]).start()
    greet(g, ng, (over_x, over_y, sibling))

    def to_sibling(gz, c):
        return remote(
            region(gz, columns[c] + sibling - d), r0.at[gz, c], s0.at[gz, c], w0.at[gz, c], (g, sibling)
        )

    peers = (sibling, over_x, over_y)

    def vec_copy(n):
        return remote(vwork.at[n], vxy.at[n], vs.at[n], vw.at[n], (g, peers[n]))

    for t in range(ng):
        for c in (3, 2, 1, 0):
            to_sibling(order(t), c).start()
    inputs = [
        pltpu.make_async_copy(cat_in, cat, sem_in.at[0]),
        pltpu.make_async_copy(wq_in, wq, sem_in.at[1]),
        pltpu.make_async_copy(x_in, x, sem_in.at[2]),
        pltpu.make_async_copy(dx1_in, dx1, sem_in.at[3]),
    ]
    for copy in inputs:
        copy.start()
    input_grad = pltpu.make_async_copy(dx1, ig_out, sem_in.at[4])

    def first_norm():
        for copy in inputs:
            copy.wait()
        for part in range(3):
            for half in range(2):
                dh1_dot(cat, wq, dh1, part, half)
        first = first_norm_back(cat, x, dh1, dx1, dx1, vec_ref)
        input_grad.start()
        for n, row in enumerate(vector_rows(first, sums2_ref)):
            vwork[0, n:n + 1, :] = row
        vec_copy(0).start()

    first = (
        (2, 0, na, r1y, 0, over_y),
        (3, 0, na, r1y, 1, over_y),
        (1, na, nb, r1x, 0, over_x),
        (3, na, nb, r1x, 1, over_x),
    )
    second = ((1, 0, na, r2x, over_x), (2, na, nb, r2y, over_y))
    third = (
        (2, flat, nc1, cy.at[0], over_y),
        (3, flat, nc1, cy.at[1], over_y),
        (1, flat + nc1, nc2, cx.at[0], over_x),
        (3, flat + nc1, nc2, cx.at[1], over_x),
        (1, flat, nc1, cx2, over_x),
        (2, flat + nc1, nc2, cy2, over_y),
    )

    def copy1(n, gz):
        c, at, size, buf, place_at, to = first[n]
        return remote(cut(mine.at[gz, c], at, size), buf.at[gz, place_at], s1.at[n, gz], w1.at[n, gz], (g, to))

    def copy2(n, gz):
        c, at, size, buf, to = second[n]
        return remote(cut(mine.at[gz, c], at, size), buf.at[gz], s2.at[n, gz], w2.at[n, gz], (g, to))

    def copy3(n):
        c, at, size, buf, to = third[n]
        return remote(cut(mine.at[g, c], at, size), buf, s3.at[n], w3.at[n], (g, to))

    def flat_part(gz):
        return cut(mine.at[gz, 0], 0, flat)

    def corner_part(gz):
        return mine.at[gz, :, pl.ds(flat, nc)]

    def line(gz, part, buf, sends, waits, up):
        at = gz if up else jnp.where(gz < g - 1, gz, ng)
        to = g + 1 if up else g - 1
        return remote(part(gz), buf.at[at], sends.at[gz], waits.at[at], (to, d))

    def pass_on(gz, part, buf, sends, waits, gather):
        @pl.when(gz > g)
        def _():
            @pl.when(g > 0)
            def _():
                arrived(buf.at[gz], waits.at[gz])
                gather(gz)
            line(gz, part, buf, sends, waits, True).start()

        @pl.when(gz < g)
        def _():
            @pl.when(g < ng - 1)
            def _():
                arrived(buf.at[gz], waits.at[gz])
                gather(gz)
            line(gz, part, buf, sends, waits, False).start()

    def gather_flat(gz):
        add_blocks(flat_part(gz), rz.at[gz], flat)

    def gather_corner(at, gz):
        for c in range(4):
            add_blocks(cut(mine.at[gz, c], flat, nc), cz.at[at, c], nc)

    def sums0(t):
        gz = order(t)
        for c in (3, 2, 1, 0):
            pltpu.make_async_copy(region(gz, columns[c]), mine.at[gz, c], load.at[gz, c]).wait()
            arrived(r0.at[gz, c], w0.at[gz, c])
            add_blocks(mine.at[gz, c], r0.at[gz, c], count)
            if t < ng - 1:
                sends0(t, c)

    def sends0(t, c):
        gz = order(t)
        for n in {3: (1, 3), 2: (0,), 1: (2,), 0: ()}[c]:
            copy1(n, gz).start()

    def along0(t):
        pass_on(order(t), corner_part, cz, sc, wc, lambda gz: gather_corner(gz, gz))

    def stage1(t):
        gz = order(t)
        arrived(r1y.at[gz, 1], w1.at[1, gz])
        add_blocks(cut(mine.at[gz, 1], 0, na), r1y.at[gz, 1], na)
        copy2(0, gz).start()
        arrived(r1x.at[gz, 1], w1.at[3, gz])
        add_blocks(cut(mine.at[gz, 2], na, nb), r1x.at[gz, 1], nb)
        copy2(1, gz).start()
        arrived(r1y.at[gz, 0], w1.at[0, gz])
        add_blocks(cut(mine.at[gz, 0], 0, na), r1y.at[gz, 0], na)
        arrived(r1x.at[gz, 0], w1.at[2, gz])
        add_blocks(cut(mine.at[gz, 0], na, nb), r1x.at[gz, 0], nb)

    def stage2(t):
        gz = order(t)
        arrived(r2x.at[gz], w2.at[0, gz])
        add_blocks(cut(mine.at[gz, 0], 0, na), r2x.at[gz], na)
        arrived(r2y.at[gz], w2.at[1, gz])
        add_blocks(cut(mine.at[gz, 0], na, nb), r2y.at[gz], nb)
        if t < ng - 1:
            pass_on(gz, flat_part, rz, sz, wz, gather_flat)

    def corner0():
        @pl.when(g > 0)
        def _():
            arrived(cz.at[g], wc.at[g])
            gather_corner(g, g)

        @pl.when(g < ng - 1)
        def _():
            arrived(cz.at[ng], wc.at[ng])
            gather_corner(ng, g)
        for n in range(4):
            copy3(n).start()

    def corner1():
        arrived(cy.at[1], w3.at[1])
        add_blocks(cut(mine.at[g, 1], flat, nc1), cy.at[1], nc1)
        copy3(4).start()
        arrived(cx.at[1], w3.at[3])
        add_blocks(cut(mine.at[g, 2], flat + nc1, nc2), cx.at[1], nc2)
        copy3(5).start()
        arrived(cy.at[0], w3.at[0])
        add_blocks(cut(mine.at[g, 0], flat, nc1), cy.at[0], nc1)
        arrived(cx.at[0], w3.at[2])
        add_blocks(cut(mine.at[g, 0], flat + nc1, nc2), cx.at[0], nc2)

    def corner2():
        arrived(cx2, w3.at[4])
        add_blocks(cut(mine.at[g, 0], flat, nc1), cx2, nc1)
        arrived(cy2, w3.at[5])
        add_blocks(cut(mine.at[g, 0], flat + nc1, nc2), cy2, nc2)

    def vec_step(n):
        arrived(vxy.at[n], vw.at[n])
        total = vwork[n] + vxy[n]
        if n < 2:
            vwork[n + 1] = total
            vec_copy(n + 1).start()
        else:
            vz[g] = total

    def vec_line(gz, up):
        to = g + 1 if up else g - 1
        return remote(vz.at[gz], vz.at[gz], vs.at[3 + 2 * gz + int(up)], vw.at[3 + gz], (to, d))

    last = ng - 1
    sums0(0)
    sums0(1)
    first_norm()
    along0(0)
    stage1(0)
    for t in range(2, last):
        sums0(t)
        along0(t - 1)
        vec_step(t - 2)
        stage1(t - 1)
        stage2(t - 2)
    vec_step(1)
    sums0(last)
    along0(last - 1)
    stage1(last - 1)
    for c in (3, 2, 1):
        sends0(last, c)
    corner0()
    vec_step(2)

    @pl.when(g < ng - 1)
    def _():
        vec_line(g, True).start()

    @pl.when(g > 0)
    def _():
        vec_line(g, False).start()
    stage2(last - 2)
    for n in range(1, ng):
        gz = near_order(n, g, ng)
        arrived(vz.at[gz], vw.at[3 + gz])

        @pl.when((gz < g) & (g < ng - 1))
        def _():
            vec_line(gz, True).start()

        @pl.when((gz > g) & (g > 0))
        def _():
            vec_line(gz, False).start()
    stage2(last - 1)
    stage1(last)
    corner1()
    total = vz[0]
    for z in range(1, ng):
        total = total + vz[z]
    vwork[3] = total
    per = total.shape[1] // 128
    for r in range(total.shape[0]):
        for c in range(per):
            row = vwork[3, r:r + 1, c * 128:(c + 1) * 128]
            n = per * r + c
            vout_ref[n:n + 1, :] = row
            vnew_ref[n:n + 1, :] = vin_ref[n:n + 1, :] - rate * row
    stage2(last)
    corner2()

    @pl.when(g > 0)
    def _():
        arrived(rz.at[g], wz.at[g])

    @pl.when(g < ng - 1)
    def _():
        arrived(rz.at[ng], wz.at[ng])

    @pl.when((g > 0) & (g < ng - 1))
    def _():
        @pl.loop(0, flat // 2)
        def _(n):
            for k in range(2):
                i = 2 * n + k
                out_ref[i] = mine[g, 0, i].astype(F32) + rz[g, i].astype(F32) + rz[ng, i].astype(F32)

    @pl.when(g == 0)
    def _():
        @pl.loop(0, flat // 2)
        def _(n):
            for k in range(2):
                i = 2 * n + k
                out_ref[i] = mine[g, 0, i].astype(F32) + rz[ng, i].astype(F32)

    @pl.when((g > 0) & (g == ng - 1))
    def _():
        @pl.loop(0, flat // 2)
        def _(n):
            for k in range(2):
                i = 2 * n + k
                out_ref[i] = mine[g, 0, i].astype(F32) + rz[g, i].astype(F32)

    for i in range(flat, count):
        out_ref[i] = mine[g, 0, i].astype(F32)

    for t in range(ng):
        gz = order(t)
        for c in range(4):
            to_sibling(gz, c).wait_send()
        for n in range(4):
            copy1(n, gz).wait_send()
        for n in range(2):
            copy2(n, gz).wait_send()
        if t < ng - 1:
            arrived(flat_part(gz), sz.at[gz])
            arrived(corner_part(gz), sc.at[gz])
    input_grad.wait()
    for n in range(6):
        copy3(n).wait_send()
    for n in range(3):
        vec_copy(n).wait_send()
    for n in range(ng):
        gz = near_order(n, g, ng)

        @pl.when((gz <= g) & (g < ng - 1))
        def _():
            vec_line(gz, True).wait_send()

        @pl.when((gz >= g) & (g > 0))
        def _():
            vec_line(gz, False).wait_send()


def run_scatter(grads, sums2, vec, vin, cat, x, dx1, wq, ng, nd, rate):
    blocks, side, _ = grads.shape
    count = blocks // (ng * nd)
    na, nb, nc1, nc2 = slot_cuts(count)
    flat = na + nb
    dma = pltpu.SemaphoreType.DMA

    def buf(*lead):
        return pltpu.VMEM(lead + (side, side), BF16)

    def like(v):
        return pltpu.VMEM(v.shape, v.dtype)

    return pl.pallas_call(
        functools.partial(scatter_kernel, ng=ng, nd=nd, rate=rate),
        out_shape=(
            sds((count, side, side), F32),
            sds(vin.shape, F32),
            sds(vin.shape, F32),
            sds(dx1.shape, F32),
        ),
        in_specs=[hbm(), vmem(), vmem(), vmem()] + [hbm()] * 4,
        out_specs=(vmem(), vmem(), vmem(), hbm()),
        scratch_shapes=[
            like(cat),
            like(x),
            like(dx1),
            like(wq),
            like(dx1),
            dma((5,)),
            buf(ng, 4, count),
            buf(ng, 4, count),
            buf(ng, 2, na),
            buf(ng, 2, nb),
            buf(ng, na),
            buf(ng, nb),
            buf(ng + 1, flat),
            buf(ng + 1, 4, nc1 + nc2),
            buf(2, nc1),
            buf(2, nc2),
            buf(nc1),
            buf(nc2),
            pltpu.VMEM((4,) + vec.shape, F32),
            pltpu.VMEM((3,) + vec.shape, F32),
            pltpu.VMEM((ng,) + vec.shape, F32),
            dma((ng, 4)),
            dma((ng, 4)),
            dma((ng, 4)),
            dma((4, ng)),
            dma((4, ng)),
            dma((2, ng)),
            dma((2, ng)),
            dma((ng,)),
            dma((ng + 1,)),
            dma((ng,)),
            dma((ng + 1,)),
            dma((6,)),
            dma((6,)),
            dma((3 + 2 * ng,)),
            dma((3 + ng,)),
        ],
        compiler_params=params(61, collective_id=1, has_side_effects=True),
        name="scatter",
    )(grads, sums2, vec, vin, cat, x, dx1, wq)


def blocks_kernel(*refs, handed):
    g_ref, w_ref, ls_ref, rs_ref, lr_ref, rr_ref = refs[:6]
    wg_out, nl_out, nr_out, nw_out = refs[6 + handed:10 + handed]
    for n in range(handed):
        refs[10 + handed + n][...] = refs[6 + n][...]

    for i in range(g_ref.shape[0]):
        grad = g_ref[i]
        wg_out[i] = grad
        hi = grad.astype(BF16)
        low = (grad - hi.astype(F32)).astype(BF16)
        nl_out[i] = 0.5 * ls_ref[i] + 0.5 * dot_nt(hi, hi)
        turned = grad.T
        hi_t = turned.astype(BF16)
        nr_out[i] = 0.5 * rs_ref[i] + 0.5 * dot_nt(hi_t, hi_t)
        left = lr_ref[i]
        left_hi = left.astype(BF16)
        left_low = (left - left_hi.astype(F32)).astype(BF16)
        shaped = dot_nn(left_hi, hi) + dot_nn(left_hi, low) + dot_nn(left_low, hi)
        right = rr_ref[i]
        right_hi = right.astype(BF16)
        right_low = (right - right_hi.astype(F32)).astype(BF16)
        sh_hi = shaped.astype(BF16)
        sh_low = (shaped - sh_hi.astype(F32)).astype(BF16)
        shaped = dot_nn(sh_hi, right_hi) + dot_nn(sh_low, right_hi) + dot_nn(sh_hi, right_low)
        nw_out[i] = w_ref[i] - weight_rate * shaped


def run_blocks(grads, weights, left_stats, right_stats, left_roots, right_roots, *passing):
    count, side, _ = grads.shape
    steps = math.gcd(count, 8)
    step = count // steps
    spec = pl.BlockSpec((step, side, side), lambda n: (n, 0, 0))
    through = []
    for v in passing:
        part = v.shape[0] // steps
        if part % 8 == 0:
            through.append(pl.BlockSpec((part, v.shape[1]), lambda n: (n, 0)))
        else:
            through.append(pl.BlockSpec(v.shape, lambda n: (0, 0)))
    return pl.pallas_call(
        functools.partial(blocks_kernel, handed=len(passing)),
        grid=(steps,),
        out_shape=tuple([sds(grads.shape, F32)] * 4) + tuple(sds(v.shape, v.dtype) for v in passing),
        in_specs=[spec] * 6 + through,
        out_specs=tuple([spec] * 4) + tuple(through),
        compiler_params=params(),
        name="blocks",
    )(grads, weights, left_stats, right_stats, left_roots, right_roots, *passing)


def local(
    inputs,
    cotangent,
    weight_slots,
    slot_block,
    left_stats,
    right_stats,
    left_roots,
    right_roots,
    vectors,
    span_start,
):
    seq_count, tok_count, width = inputs.shape
    rows = seq_count * tok_count
    nd = lax.axis_size("dev")
    ng = lax.axis_size("grp")
    side = weight_slots.shape[1]
    hpd = H // nd
    lanes = width // nd
    head = lax.axis_index("dev") * hpd + jnp.arange(hpd, dtype=jnp.int32)
    slopes = jnp.exp2(-8.0 * (head.astype(F32) + 1.0) / H)
    vin = vectors.reshape(-1, 128)
    held = slot_block.reshape(-1, 128)
    x = inputs.reshape(rows, width)
    dy = cotangent.reshape(rows, width)
    rate = vector_rate / math.sqrt(rows * nd * ng)

    direct = nd == 8
    if direct:
        gath, h1, slot_of, vec = run_gather(weight_slots, x, held, vin, ng, nd)
    else:
        gath = lax.all_gather(weight_slots.astype(BF16), ("grp", "dev"), axis=0, tiled=True)
        h1, slot_of, vec = run_prepare(x, held, vin)
    qkv, wq = run_qkv(slot_of, h1, vec, gath, nd)
    qkv, o, o32, lse = run_attn_fwd(
        span_start, slopes, qkv.reshape(nd, 3, seq_count, tok_count, lanes), hpd
    )
    att = side_by_side(o, 1, rows)
    act, dx1, do, sums2, grads = run_mlp(slot_of, att, x, dy, vec, gath, nd)
    do = do.reshape(nd, seq_count, tok_count, lanes)
    cat = side_by_side(run_attn_bwd(span_start, slopes, qkv, do, o32, lse, hpd), 3, rows)
    grads = run_wgrad(slot_of, h1, cat, grads)
    if direct:
        weight_grads, vector_grads, new_vectors, ig = run_scatter(
            grads, sums2, vec, vin, cat, x, dx1, wq, ng, nd, rate
        )
        passing = (ig, vector_grads, new_vectors)
    else:
        ig, vsum = run_dh1(cat, x, dx1, vec, wq, sums2)
        vector_grads = lax.psum(vsum.reshape(-1), ("grp", "dev"))
        new_vectors = vectors - rate * vector_grads
        weight_grads = lax.psum_scatter(grads, ("grp", "dev"), scatter_dimension=0, tiled=True)
        weight_grads = weight_grads.astype(F32)
        passing = ()
    weight_grads, new_left, new_right, new_weights, *passed = run_blocks(
        weight_grads, weight_slots, left_stats, right_stats, left_roots, right_roots, *passing
    )
    if direct:
        ig, vector_grads, new_vectors = passed
    return (
        act.reshape(inputs.shape),
        ig.reshape(inputs.shape),
        weight_grads,
        new_left,
        new_right,
        new_weights,
        vector_grads.reshape(-1),
        new_vectors.reshape(-1),
    )


def solution(mesh):
    return jax.shard_map(
        local,
        mesh=mesh,
        in_specs=(
            P("grp", "dev", None),
            P("grp", "dev", None),
            P(("grp", "dev"), None, None),
            P(),
            P(("grp", "dev"), None, None),
            P(("grp", "dev"), None, None),
            P(("grp", "dev"), None, None),
            P(("grp", "dev"), None, None),
            P(),
            P("grp"),
        ),
        out_specs=(
            P("grp", "dev", None),
            P("grp", "dev", None),
            P(("grp", "dev"), None, None),
            P(("grp", "dev"), None, None),
            P(("grp", "dev"), None, None),
            P(("grp", "dev"), None, None),
            P(),
            P(),
        ),
        check_vma=False,
    )
```

```python
import functools
import math

import jax
import jax.numpy as jnp
from jax import lax
from jax.experimental import pallas as pl
from jax.experimental.pallas import tpu as pltpu
from jax.sharding import PartitionSpec as P

H = 16
FF = 4096
PIC = 256

eps = 1e-05
weight_rate = 0.5
vector_rate = 0.5
big_negative = -1e30
highest = lax.Precision.HIGHEST
F32 = jnp.float32
BF16 = jnp.bfloat16
LOG2E = 1.4426950408889634
MIB = 1024 * 1024

GAIN1, SHIFT1, BQ, BV, BO, GAIN2, SHIFT2, BDOWN, BUP = range(9)


def dot_nn(a, b):
    return lax.dot_general(a, b, (((1,), (0,)), ((), ())), preferred_element_type=F32)


def dot_nt(a, b):
    return lax.dot_general(a, b, (((1,), (1,)), ((), ())), preferred_element_type=F32)


def vmem():
    return pl.BlockSpec(memory_space=pltpu.VMEM)


def smem():
    return pl.BlockSpec(memory_space=pltpu.SMEM)


def hbm():
    return pl.BlockSpec(memory_space=pl.ANY)


def sds(shape, dtype):
    return jax.ShapeDtypeStruct(shape, dtype)


def params(mib=58, **kw):
    return pltpu.CompilerParams(vmem_limit_bytes=mib * MIB, **kw)


def layer_stats(v):
    middle = jnp.mean(v, axis=-1, keepdims=True)
    centred = v - middle
    spread = jnp.mean(centred * centred, axis=-1, keepdims=True)
    return centred, lax.rsqrt(spread + eps)


def fold_rows(v):
    return jnp.sum(v.reshape(v.shape[0] // 8, 8, v.shape[1]), axis=0)


def slot_at(slot_ref, block):
    lanes = slot_ref.shape[1]
    if isinstance(block, int):
        return slot_ref[block // lanes, block % lanes]
    return slot_ref[lax.div(block, lanes), lax.rem(block, lanes)]


def fetch_block(gath, slot, dst, row, col, sem, side):
    return pltpu.make_async_copy(
        gath.at[slot], dst.at[pl.ds(row, side), pl.ds(col, side)], sem
    )


def prepare(x_ref, block_ref, vin_ref, h1_ref, slot_ref, vec_ref):
    rows, width = x_ref.shape
    per = width // 128
    for r in range(vec_ref.shape[0]):
        for c in range(per):
            vec_ref[r:r + 1, c * 128:(c + 1) * 128] = vin_ref[per * r + c:per * r + c + 1, :]
    chunk = 128

    @pl.loop(0, rows // chunk)
    def _(r):
        at = pl.ds(pl.multiple_of(r * chunk, chunk), chunk)
        centred, inv = layer_stats(x_ref[at, :].astype(F32))
        h1_ref[at, :] = (
            centred * inv * vec_ref[GAIN1:GAIN1 + 1, :] + vec_ref[SHIFT1:SHIFT1 + 1, :]
        ).astype(BF16)

    tiles, lanes = slot_ref.shape
    line = lax.broadcasted_iota(jnp.int32, (8, lanes), 0)
    lane = lax.broadcasted_iota(jnp.int32, (8, lanes), 1).astype(F32)
    block = lax.broadcasted_iota(jnp.int32, (lanes, lanes), 0)
    for t in range(tiles):
        found = jnp.zeros((8, lanes), F32)
        for r in range(tiles):
            held = (block_ref[r:r + 1, :] == block + t * lanes).astype(F32).astype(BF16)
            found = found + dot_nt(jnp.where(line == 0, lane, float(r)).astype(BF16), held)
        slot_ref[t:t + 1, :] = (found[0:1] + float(lanes) * found[1:2]).astype(jnp.int32)


def prepared_shapes(x, blocks, vin):
    rows, width = x.shape
    return (
        sds((rows, width), BF16),
        sds(blocks.shape, jnp.int32),
        sds((vin.size // width, width), F32),
    )


def run_prepare(x, blocks, vin):
    return pl.pallas_call(
        prepare,
        out_shape=prepared_shapes(x, blocks, vin),
        in_specs=[vmem()] * 3,
        out_specs=tuple([vmem()] * 3),
        compiler_params=params(),
        name="prepare",
    )(x, blocks, vin)


def qkv_kernel(slot_ref, h1_ref, vec_ref, gath, out_ref, wq_out, wbuf, sems, sem_w, *, nd):
    rows, width = h1_ref.shape
    side = gath.shape[1]
    per = width // side
    lanes = out_ref.shape[3]
    for part in range(3):
        for i in range(per):
            for j in range(per):
                slot = slot_at(slot_ref, i * 3 * per + part * per + j)
                fetch_block(gath, slot, wbuf.at[part], i * side, j * side, sems.at[part], side).start()

    def keep(part):
        return pltpu.make_async_copy(wbuf.at[part], wq_out.at[part], sem_w.at[part])

    for part in range(3):
        pltpu.make_async_copy(wbuf.at[part], wbuf.at[part], sems.at[part]).wait()
        keep(part).start()
        for half in range(2):
            cols = slice(half * width // 2, (half + 1) * width // 2)
            res = dot_nn(h1_ref[...], wbuf[part, :, cols])
            if part == 0:
                res = res + vec_ref[BQ:BQ + 1, cols]
            if part == 2:
                res = res + vec_ref[BV:BV + 1, cols]
            res = res.astype(BF16)
            for d in range(nd // 2):
                out_ref[half * (nd // 2) + d, part, :, :] = res[:, d * lanes:(d + 1) * lanes]
    for part in range(3):
        keep(part).wait()


def run_qkv(slot_of, h1, vec, gath, nd):
    rows, width = h1.shape
    lanes = width // nd
    return pl.pallas_call(
        functools.partial(qkv_kernel, nd=nd),
        out_shape=(sds((nd, 3, rows, lanes), BF16), sds((3, width, width), BF16)),
        in_specs=[smem(), vmem(), vmem(), hbm()],
        out_specs=(vmem(), hbm()),
        scratch_shapes=[
            pltpu.VMEM((3, width, width), BF16),
            pltpu.SemaphoreType.DMA((3,)),
            pltpu.SemaphoreType.DMA((3,)),
        ],
        compiler_params=params(),
        name="qkv",
    )(slot_of, h1, vec, gath)


MESH = pl.DeviceIdType.MESH


def remote(src, dst, send, recv, device):
    return pltpu.make_async_remote_copy(
        src_ref=src, dst_ref=dst, send_sem=send, recv_sem=recv, device_id=device, device_id_type=MESH
    )


def arrived(ref, sem):
    pltpu.make_async_copy(ref, ref, sem).wait()


def cut(ref, first, size):
    return ref.at[pl.ds(first, size)]


def greet_plane(g, d, nd):
    barrier = pltpu.get_barrier_semaphore()
    for p in range(1, nd):
        pl.semaphore_signal(barrier, inc=1, device_id=(g, lax.rem(d + p, nd)), device_id_type=MESH)
    pl.semaphore_wait(barrier, nd - 1)


def landing(ref, part, source, q, tok, lanes, parts):
    if lanes % 128 == 0:
        first = (part * (ref.shape[1] // parts)) + source * lanes
        return ref.at[pl.ds(q * tok, tok), pl.ds(pl.multiple_of(first, lanes), lanes)]
    return ref.at[source, part, q]


def landing_shape(parts, nb, seqs, tok, lanes):
    if lanes % 128 == 0:
        return sds((seqs * tok, parts * nb * lanes), BF16)
    return sds((nb, parts, seqs, tok, lanes), BF16)


def side_by_side(got, parts, rows):
    if got.ndim == 2:
        return got
    nb, _, seqs, tok, lanes = got.shape
    return got.transpose(2, 3, 1, 0, 4).reshape(rows, parts * nb * lanes)


def parts3(v):
    hi = v.astype(BF16)
    mid = (v - hi.astype(F32)).astype(BF16)
    lo = (v - hi.astype(F32) - mid.astype(F32)).astype(BF16)
    return hi.astype(F32), mid.astype(F32), lo.astype(F32)


def own_lanes(h, shape, hpd, lanes):
    lane = lax.broadcasted_iota(jnp.int32, shape, 1)
    size = lanes // hpd
    return (lane >= h * size) & (lane < (h + 1) * size)


def place(values, base, tok, width):
    lane = lax.broadcasted_iota(jnp.int32, (tok, width), 1)
    out = jnp.zeros((tok, width), F32)
    for n, v in enumerate(values):
        out = jnp.where(lane == base + n, v, out)
    return out


def spare(h, hpd, lanes):
    return (lanes // hpd) * (1 - h) if hpd > 1 else 0


def column_tables(slope_ref, qbase, kbase, kfar, hpd, lanes):
    _, tok, _ = qbase.shape
    u = lax.broadcasted_iota(jnp.int32, (tok, 128), 0).astype(F32)
    for h in range(hpd):
        slope = slope_ref[h] * LOG2E
        base = spare(h, hpd, lanes)
        near = parts3(jnp.full((tok, 128), slope, F32))
        far = parts3(jnp.full((tok, 128), slope * tok, F32))
        qbase[h] = place(near + far, base, tok, 128)
        kbase[h] = place([u] * 3 + [0.0] * 3 + [1.0] * 3, base, tok, 128)
        kfar[h] = place([0.0] * 3 + [1.0] * 3, base, tok, 128)


def q_columns(q, h, hpd, columns, extra):
    tok, lanes = q.shape
    scaled = q.astype(F32) * ((lanes // hpd) ** (-0.5) * LOG2E)
    hi = scaled.astype(BF16).astype(F32)
    low = scaled - hi
    if extra:
        lane = lax.broadcasted_iota(jnp.int32, (tok, 128), 1)
        for n, v in enumerate(extra):
            columns = jnp.where(lane == spare(h, hpd, lanes) + 6 + n, v, columns)
    if hpd > 1:
        own = own_lanes(h, (tok, lanes), hpd, lanes)
        return jnp.concatenate(
            [jnp.where(own, hi, 0.0), jnp.where(own, low, columns)], axis=1
        ).astype(BF16)
    return jnp.concatenate([hi, low, columns], axis=1).astype(BF16)


def k_columns(k, h, hpd, columns):
    tok, lanes = k.shape
    wide = k.astype(F32)
    if hpd > 1:
        own = own_lanes(h, (tok, lanes), hpd, lanes)
        return jnp.concatenate([wide, jnp.where(own, wide, columns)], axis=1).astype(BF16)
    return jnp.concatenate([wide, wide, columns], axis=1).astype(BF16)


def far_side(slope, tok):
    u = lax.broadcasted_iota(jnp.int32, (tok, tok), 0)
    t = lax.broadcasted_iota(jnp.int32, (tok, tok), 1)
    after = u > t
    return (
        jnp.where(after, big_negative, 0.0),
        jnp.where(after, (2.0 * slope) * (t - u).astype(F32), 0.0),
    )


def attn_fwd_kernel(
    span_ref, slope_ref, src, got, o_got, o32_ref, lse_ref,
    qa, ka, vt, scores, corr, qbase, kbase, kfar, o_out, ss, sr, os, orr, loc, *, hpd, nd
):
    nb, _, seqs, tok, lanes = got.shape
    size = lanes // hpd
    pair = 2 * tok
    g = lax.axis_index("grp")
    d = lax.axis_index("dev")

    for q in range(seqs):
        pltpu.make_async_copy(src.at[d, :, q], got.at[d, :, q], loc.at[q]).start()
    greet_plane(g, d, nd)

    def send(q, p):
        to = lax.rem(d + p, nd)
        return remote(src.at[to, :, q], got.at[d, :, q], ss.at[q, p], sr.at[q, p], (g, to))

    def send_all(q):
        @pl.loop(1, nd)
        def _(p):
            send(q, p).start()

    send_all(0)

    def o_place(source, q):
        return landing(o_got, 0, source, q, tok, lanes, 1)

    def send_o(q, i, p):
        return remote(o_out.at[i, q], o_place(d, q), os.at[q, i], orr.at[q, p], (g, i))

    column_tables(slope_ref, qbase, kbase, kfar, hpd, lanes)
    for h in range(hpd):
        mask, span = far_side(slope_ref[h] * LOG2E, tok)
        for n, (one, two) in enumerate(((mask, mask), (span, mask), (mask, span))):
            corr[h, n, 0:tok, 0:tok] = one
            corr[h, n, tok:, tok:] = two
            corr[h, n, 0:tok, tok:] = jnp.zeros((tok, tok), F32)
            corr[h, n, tok:, 0:tok] = jnp.full((tok, tok), big_negative, F32)

    def fold(v, how):
        return how(v.reshape(v.shape[0] // 8, 8, v.shape[1]), axis=0)

    @pl.loop(0, seqs)
    def _(q):
        pltpu.make_async_copy(src.at[d, :, q], got.at[d, :, q], loc.at[q]).wait()

        @pl.loop(1, nd)
        def _(p):
            arrived(got.at[lax.rem(d + nd - p, nd), :, q], sr.at[q, p])

        @pl.when(q + 1 < seqs)
        def _():
            send_all(q + 1)

        @pl.loop(0, nb)
        def _(j):
            at_j = pl.ds(pl.multiple_of(j * tok, tok), tok)
            vt[0:lanes, at_j] = got[j, 2, q].astype(F32).T.astype(BF16)
            block = jnp.full((tok, 128), j, jnp.int32).astype(F32)
            for h in range(hpd):
                qa[h, at_j, :] = q_columns(got[j, 0, q], h, hpd, qbase[h], [])
                ka[h, at_j, :] = k_columns(got[j, 1, q], h, hpd, kbase[h] + block * kfar[h])

        start = span_ref[q]
        for i in range(nb // 2):
            flag = (start == i * pair).astype(jnp.int32) + 2 * (start == i * pair + tok).astype(jnp.int32)
            at_i = slice(i * pair, (i + 1) * pair)
            outs = []
            logs = []
            tops = []
            for h in range(hpd):
                top = None
                for n in range(i + 1):
                    at_n = slice(n * pair, (n + 1) * pair)
                    s = dot_nt(ka[h, at_n, :], qa[h, at_i, :])
                    if n == i:
                        s = s + corr[h, flag]
                    scores[h, at_n, :] = s
                    here = fold(s, jnp.max)
                    top = here if top is None else jnp.maximum(top, here)
                tops.append(jnp.max(top, axis=0, keepdims=True))
            for h in range(hpd):
                acc = total = None
                for n in range(i + 1):
                    at_n = slice(n * pair, (n + 1) * pair)
                    p = jnp.exp2(scores[h, at_n, :] - tops[h])
                    here = fold(p, jnp.sum)
                    part = dot_nn(vt[h * size:(h + 1) * size, at_n], p.astype(BF16))
                    total = here if total is None else total + here
                    acc = part if acc is None else acc + part
                total = jnp.sum(total, axis=0, keepdims=True)
                outs.append(acc / total)
                logs.append(jnp.broadcast_to(tops[h] + jnp.log2(total), (128 // hpd, pair)))
            out = (jnp.concatenate(outs, axis=0) if hpd > 1 else outs[0]).T
            log = (jnp.concatenate(logs, axis=0) if hpd > 1 else logs[0]).T
            for k in range(2):
                at = 2 * i + k
                o32_ref[at, q] = out[k * tok:(k + 1) * tok]
                o_out[at, q] = out[k * tok:(k + 1) * tok].astype(BF16)
                lse_ref[at, q] = log[k * tok:(k + 1) * tok]

                @pl.when(at == d)
                def _():
                    pltpu.make_async_copy(o_out.at[at, q], o_place(d, q), os.at[q, at]).start()

                @pl.when(at != d)
                def _():
                    send_o(q, at, lax.rem(at - d + nd, nd)).start()

    for q in range(seqs):
        @pl.loop(1, nd)
        def _(p):
            arrived(o_place(lax.rem(d + nd - p, nd), q), orr.at[q, p])
            send(q, p).wait_send()

        @pl.loop(0, nd)
        def _(i):
            arrived(o_out.at[i, q], os.at[q, i])


def run_attn_fwd(span, slopes, qkv, hpd):
    nb, _, seqs, tok, lanes = qkv.shape
    t = nb * tok
    dma = pltpu.SemaphoreType.DMA
    return pl.pallas_call(
        functools.partial(attn_fwd_kernel, hpd=hpd, nd=nb),
        out_shape=(
            sds(qkv.shape, BF16),
            landing_shape(1, nb, seqs, tok, lanes),
            sds((nb, seqs, tok, lanes), F32),
            sds((nb, seqs, tok, 128), F32),
        ),
        in_specs=[smem(), smem(), hbm()],
        out_specs=(vmem(), vmem(), vmem(), vmem()),
        scratch_shapes=[
            pltpu.VMEM((hpd, t, 256), BF16),
            pltpu.VMEM((hpd, t, 256), BF16),
            pltpu.VMEM((lanes, t), BF16),
            pltpu.VMEM((hpd, t, 2 * tok), F32),
            pltpu.VMEM((hpd, 3, 2 * tok, 2 * tok), F32),
            pltpu.VMEM((hpd, tok, 128), F32),
            pltpu.VMEM((hpd, tok, 128), F32),
            pltpu.VMEM((hpd, tok, 128), F32),
            pltpu.VMEM((nb, seqs, tok, lanes), BF16),
            dma((seqs, nb)),
            dma((seqs, nb)),
            dma((seqs, nb)),
            dma((seqs, nb)),
            dma((seqs,)),
        ],
        compiler_params=params(collective_id=2, has_side_effects=True),
        name="attn_fwd",
    )(span, slopes, qkv)


def attn_bwd_kernel(
    span_ref, slope_ref, qkv_ref, do_src, o32_ref, lse_ref, got,
    do_got, out, qa, ka, kt, va, qm, da, dm, dqt, corr, qbase, kbase, kfar, dk_ref, dv_ref,
    ss, sr, gs, gr, loc, *, hpd, nd
):
    nb, _, seqs, tok, lanes = qkv_ref.shape
    size = lanes // hpd
    unit = size ** (-0.5)
    g = lax.axis_index("grp")
    d = lax.axis_index("dev")

    def own_copy(q):
        return pltpu.make_async_copy(do_src.at[d, q], do_got.at[d, q], loc.at[q])

    for q in range(seqs):
        own_copy(q).start()
    greet_plane(g, d, nd)

    def send(q, p):
        to = lax.rem(d + p, nd)
        return remote(do_src.at[to, q], do_got.at[d, q], ss.at[q, p], sr.at[q, p], (g, to))

    def send_all(q):
        @pl.loop(1, nd)
        def _(p):
            send(q, p).start()

    send_all(0)

    def place_back(kind, source, q):
        return landing(got, kind, source, q, tok, lanes, 3)

    def back(q, kind, p):
        to = lax.rem(d + p, nd)
        return remote(
            out.at[to, kind, q], place_back(kind, d, q), gs.at[q, kind, p], gr.at[q, kind, p], (g, to)
        )

    def back_own(q, kind):
        return pltpu.make_async_copy(out.at[d, kind, q], place_back(kind, d, q), gs.at[q, kind, 0])

    for h in range(hpd):
        mask, span = far_side(slope_ref[h] * LOG2E, tok)
        for n, table in enumerate((mask, span)):
            corr[h, n, :, 0:tok] = table
            corr[h, n, :, tok:] = jnp.zeros((tok, tok), F32)
    column_tables(slope_ref, qbase, kbase, kfar, hpd, lanes)

    @pl.loop(0, seqs)
    def _(q):
        @pl.loop(0, nb)
        def _(j):
            at_j = pl.ds(pl.multiple_of(j * tok, tok), tok)
            qj = qkv_ref[j, 0, q]
            kj = qkv_ref[j, 1, q]
            vj = qkv_ref[j, 2, q].astype(F32)
            kt[:, at_j] = kj.astype(F32).T.astype(BF16)
            dqt[:, at_j] = jnp.zeros((lanes, tok), F32)
            block = jnp.full((tok, 128), j, jnp.int32).astype(F32)
            for h in range(hpd):
                low = lse_ref[j, q][:, h * (128 // hpd):h * (128 // hpd) + 1]
                extra = [-p for p in parts3(low)]
                qa[h, at_j, :] = q_columns(qj, h, hpd, qbase[h], extra)
                ka[h, j] = k_columns(kj, h, hpd, kbase[h] + block * kfar[h])
                if hpd > 1:
                    own = own_lanes(h, (tok, lanes), hpd, lanes)
                    qm[h, at_j, :] = jnp.where(own, qj.astype(F32), 0.0).astype(BF16)
                    va[h, j] = jnp.where(own, vj, kbase[h]).astype(BF16)
                else:
                    qm[h, at_j, :] = qj
                    va[h, j] = jnp.concatenate([vj, kbase[h][:, 0:lanes]], axis=1).astype(BF16)

        own_copy(q).wait()

        @pl.loop(1, nd)
        def _(p):
            arrived(do_got.at[lax.rem(d + nd - p, nd), q], sr.at[q, p])

        @pl.when(q + 1 < seqs)
        def _():
            send_all(q + 1)

        @pl.loop(0, nb)
        def _(j):
            at_j = pl.ds(pl.multiple_of(j * tok, tok), tok)
            do = do_got[j, q].astype(F32)
            prod = do * o32_ref[j, q]
            for h in range(hpd):
                if hpd > 1:
                    own = own_lanes(h, (tok, lanes), hpd, lanes)
                    delta = jnp.sum(jnp.where(own, prod, 0.0), axis=1, keepdims=True)
                    extra = place([-p for p in parts3(delta)], spare(h, hpd, lanes) + 6, tok, lanes)
                    da[h, at_j, :] = jnp.where(own, do, extra).astype(BF16)
                    dm[h, at_j, :] = jnp.where(own, do, 0.0).astype(BF16)
                else:
                    delta = jnp.sum(prod, axis=1, keepdims=True)
                    extra = place([-p for p in parts3(delta)], 6, tok, lanes)
                    da[h, at_j, :] = jnp.concatenate([do, extra], axis=1).astype(BF16)
                    dm[h, at_j, :] = do.astype(BF16)

        start = span_ref[q]

        @pl.loop(0, nb)
        def _(n):
            j = lax.rem(d + n, nb)
            at_j = pl.ds(pl.multiple_of(j * tok, tok), tok)
            flag = (start == j * tok).astype(jnp.int32)

            def tile(i, width, near):
                at_i = slice(i * tok, i * tok + width)
                dk = None
                for h in range(hpd):
                    s = dot_nt(ka[h, j], qa[h, at_i, :])
                    if near:
                        s = s + corr[h, flag, :, 0:width]
                    p = jnp.exp2(s)
                    ds = (p * dot_nt(va[h, j], da[h, at_i, :])).astype(BF16)
                    dv_h = dot_nn(p.astype(BF16), dm[h, at_i, :])
                    dk_h = dot_nn(ds, qm[h, at_i, :])
                    dk = dk_h if dk is None else dk + dk_h
                    dv = dv_h if h == 0 else dv + dv_h
                    rows = slice(h * size, (h + 1) * size)
                    dqt[rows, at_i] += dot_nn(kt[rows, at_j], ds)
                return dk, dv

            for case in range(nb):
                @pl.when(j == case)
                def _():
                    odd = (nb - case) % 2
                    sums = tile(case, tok if odd else 2 * tok, True)
                    for i in range(case + 2 - odd, nb, 2):
                        more = tile(i, 2 * tok, False)
                        sums = [a + b for a, b in zip(sums, more)]
                    dk_ref[...], dv_ref[...] = sums

            out[j, 1, q] = (dk_ref[...] * unit).astype(BF16)
            out[j, 2, q] = dv_ref[...].astype(BF16)

            for kind in (1, 2):
                @pl.when(n == 0)
                def _():
                    back_own(q, kind).start()

                @pl.when(n > 0)
                def _():
                    back(q, kind, n).start()

        @pl.loop(0, nb)
        def _(n):
            j = lax.rem(d + n, nb)
            at_j = pl.ds(pl.multiple_of(j * tok, tok), tok)
            out[j, 0, q] = (dqt[:, at_j].T * unit).astype(BF16)

            @pl.when(n == 0)
            def _():
                back_own(q, 0).start()

            @pl.when(n > 0)
            def _():
                back(q, 0, n).start()

    for q in range(seqs):
        for kind in range(3):
            back_own(q, kind).wait()

        @pl.loop(1, nd)
        def _(p):
            send(q, p).wait_send()
            source = lax.rem(d + nd - p, nd)
            for kind in range(3):
                back(q, kind, p).wait_send()
                arrived(place_back(kind, source, q), gr.at[q, kind, p])


def run_attn_bwd(span, slopes, qkv, do, o32, lse, hpd):
    nb, _, seqs, tok, lanes = qkv.shape
    t = nb * tok
    dma = pltpu.SemaphoreType.DMA
    wide = 128 if hpd == 1 else lanes
    return pl.pallas_call(
        functools.partial(attn_bwd_kernel, hpd=hpd, nd=nb),
        out_shape=landing_shape(3, nb, seqs, tok, lanes),
        in_specs=[smem(), smem(), vmem(), hbm(), vmem(), vmem()],
        out_specs=vmem(),
        scratch_shapes=[
            pltpu.VMEM((nb, seqs, tok, lanes), BF16),
            pltpu.VMEM(qkv.shape, BF16),
            pltpu.VMEM((hpd, t, 256), BF16),
            pltpu.VMEM((hpd, nb, tok, 256), BF16),
            pltpu.VMEM((lanes, t), BF16),
            pltpu.VMEM((hpd, nb, tok, wide), BF16),
            pltpu.VMEM((hpd, t, lanes), BF16),
            pltpu.VMEM((hpd, t, wide), BF16),
            pltpu.VMEM((hpd, t, lanes), BF16),
            pltpu.VMEM((lanes, t), F32),
            pltpu.VMEM((hpd, 2, tok, 2 * tok), F32),
            pltpu.VMEM((hpd, tok, 128), F32),
            pltpu.VMEM((hpd, tok, 128), F32),
            pltpu.VMEM((hpd, tok, 128), F32),
            pltpu.VMEM((tok, lanes), F32),
            pltpu.VMEM((tok, lanes), F32),
            dma((seqs, nb)),
            dma((seqs, nb)),
            dma((seqs, 3, nb)),
            dma((seqs, 3, nb)),
            dma((seqs,)),
        ],
        compiler_params=params(collective_id=3, has_side_effects=True),
        name="attn_bwd",
    )(span, slopes, qkv, do, o32, lse)


def turn(v):
    return v.astype(F32).T.astype(BF16)


def mlp_kernel(
    slot_ref, att_ref, x_ref, dy_ref, vec_ref, gath,
    act_out, dx1_out, do_out, sums_ref, grads,
    wo, wup, wdn, x1, acc, dh2, h2_ref, h2t, attt, da_ref, act_ref, dx1_ref, g_ref, dz_ref, do_ref, stage,
    sem_o, sem_t, sem_g, sem_w, *, nd, first_o, first_up, first_dn, tile
):
    rows, width = x_ref.shape
    side = gath.shape[1]
    per = width // side
    tiles = wup.shape[0]
    ff = tiles * tile
    cols = tile // side
    lanes = do_ref.shape[2]
    fper = ff // side

    for i in range(per):
        for j in range(per):
            fetch_block(gath, slot_at(slot_ref, first_o + i * per + j), wo, i * side, j * side, sem_o.at[0], side).start()

    def fetch_tile(f):
        for i in range(per):
            for j in range(cols):
                fetch_block(gath, slot_at(slot_ref, first_up + i * fper + f * cols + j), wup.at[f], i * side, j * side, sem_t.at[f], side).start()
            for j in range(cols):
                fetch_block(gath, slot_at(slot_ref, first_dn + (f * cols + j) * per + i), wdn.at[f], j * side, i * side, sem_t.at[f], side).start()

    fetch_tile(0)
    fetch_tile(1)
    for r in range(width // 256):
        attt[r * 256:(r + 1) * 256, :] = turn(att_ref[:, r * 256:(r + 1) * 256])
    pltpu.make_async_copy(wo, wo, sem_o.at[0]).wait()
    for half in range(2):
        c = slice(half * width // 2, (half + 1) * width // 2)
        x1[:, c] = x_ref[:, c].astype(F32) + dot_nn(att_ref[...], wo[:, c]) + vec_ref[BO:BO + 1, c]

    chunk = 128

    def rows_at(r):
        return pl.ds(pl.multiple_of(r * chunk, chunk), chunk)

    @pl.loop(0, rows // chunk)
    def _(r):
        at = rows_at(r)
        centred, inv = layer_stats(x1[at, :])
        h2_ref[at, :] = (centred * inv * vec_ref[GAIN2:GAIN2 + 1, :] + vec_ref[SHIFT2:SHIFT2 + 1, :]).astype(BF16)
        acc[at, :] = x1[at, :] + vec_ref[BDOWN:BDOWN + 1, :]
        dh2[at, :] = jnp.zeros((chunk, width), F32)

    for r in range(width // 256):
        h2t[r * 256:(r + 1) * 256, :] = turn(h2_ref[:, r * 256:(r + 1) * 256])

    def put(slot, first, res, down, across):
        for i in range(down):
            for j in range(across):
                stage[slot, first + i * across + j] = res[i * side:(i + 1) * side, j * side:(j + 1) * side]

    def leave(slot, n, block):
        pltpu.make_async_copy(stage.at[slot, n], grads.at[slot_at(slot_ref, block)], sem_g.at[slot]).start()

    def left(slot, size):
        at = stage.at[slot, pl.ds(0, size)]
        pltpu.make_async_copy(at, at, sem_g.at[slot]).wait()

    full = 2 * per * cols
    piece = 512

    @pl.loop(0, tiles)
    def _(f):
        @pl.when(f + 2 < tiles)
        def _():
            fetch_tile(f + 2)
        pltpu.make_async_copy(wup.at[f], wup.at[f], sem_t.at[f]).wait()
        pltpu.make_async_copy(wdn.at[f], wdn.at[f], sem_t.at[f]).wait()
        for k in range(tile // piece):
            c = slice(k * piece, (k + 1) * piece)
            z = dot_nn(h2_ref[...], wup[f, :, c]) + vec_ref[pl.ds(BUP + f, 1), c]
            dg = dot_nt(dy_ref[...], wdn[f, c, :])
            z2 = z * z
            th = jnp.tanh(z * (0.7978845608028654 + (0.7978845608028654 * 0.044715) * z2))
            half_more = 0.5 + 0.5 * th
            g_ref[:, c] = (z * half_more).astype(BF16)
            slope = half_more + (0.5 * z) * (1.0 - th * th) * (
                0.7978845608028654 + (3.0 * 0.044715 * 0.7978845608028654) * z2
            )
            dz = (dg * slope).astype(BF16)
            dz_ref[:, c] = dz
            sums_ref[pl.ds(pl.multiple_of(8 * (4 + f), 8), 8), c] = fold_rows(dz.astype(F32))
        for k in range(width // piece):
            c = slice(k * piece, (k + 1) * piece)
            acc[:, c] += dot_nn(g_ref[...], wdn[f, :, c])
            dh2[:, c] += dot_nt(dz_ref[...], wup[f, c, :])
        slot = lax.rem(f, 2)

        @pl.when(f >= 2)
        def _():
            left(slot, full)
        per_piece = piece // side
        for k in range(tile // piece):
            c = slice(k * piece, (k + 1) * piece)
            res = dot_nn(turn(g_ref[:, c]), dy_ref[...]).astype(BF16)
            put(slot, k * per_piece * per, res, per_piece, per)
        for k in range(width // piece):
            res = dot_nn(h2t[k * piece:(k + 1) * piece, :], dz_ref[...]).astype(BF16)
            put(slot, per * cols + k * per_piece * cols, res, per_piece, cols)
        for i in range(per):
            for j in range(cols):
                leave(slot, j * per + i, first_dn + (f * cols + j) * per + i)
            for j in range(cols):
                leave(slot, per * cols + i * cols + j, first_up + i * fper + f * cols + j)

    zero = jnp.zeros((8, width), F32)

    def finish(r, carry):
        s_bo, s_gain, s_shift, s_bdown = carry
        at = rows_at(r)
        act_ref[at, :] = acc[at, :].astype(BF16)
        centred, inv = layer_stats(x1[at, :])
        hat = centred * inv
        dh = dh2[at, :]
        dhg = dh * vec_ref[GAIN2:GAIN2 + 1, :]
        back = inv * (
            dhg
            - jnp.mean(dhg, axis=-1, keepdims=True)
            - hat * jnp.mean(dhg * hat, axis=-1, keepdims=True)
        )
        dy = dy_ref[at, :].astype(F32)
        dx1 = dy + back
        dx1_ref[at, :] = dx1
        da = dx1.astype(BF16)
        da_ref[at, :] = da
        return (
            s_bo + fold_rows(da.astype(F32)),
            s_gain + fold_rows(dh * hat),
            s_shift + fold_rows(dh),
            s_bdown + fold_rows(dy),
        )

    carry = lax.fori_loop(0, rows // chunk, finish, (zero, zero, zero, zero))
    for n in range(4):
        sums_ref[8 * n:8 * n + 8, :] = carry[n]
    outs = [
        pltpu.make_async_copy(act_ref, act_out, sem_w.at[0]),
        pltpu.make_async_copy(dx1_ref, dx1_out, sem_w.at[1]),
        pltpu.make_async_copy(do_ref, do_out, sem_w.at[2]),
    ]
    outs[0].start()
    outs[1].start()
    for half in range(2):
        c = slice(half * width // 2, (half + 1) * width // 2)
        res = dot_nt(da_ref[...], wo[c, :]).astype(BF16)
        for d in range(nd // 2):
            do_ref[half * (nd // 2) + d] = res[:, d * lanes:(d + 1) * lanes]
    outs[2].start()
    left(0, full)
    left(1, full)
    half_rows = width // 2
    for half in range(2):
        res = dot_nn(attt[half * half_rows:(half + 1) * half_rows, :], da_ref[...]).astype(BF16)
        put(half, 0, res, per // 2, per)

        for i in range(per // 2):
            for j in range(per):
                leave(half, i * per + j, first_o + (half * (per // 2) + i) * per + j)
    for half in range(2):
        left(half, per * per // 2)
    for copy in outs:
        copy.wait()


def run_mlp(slot_of, att, x, dy, vec, gath, nd):
    rows, width = x.shape
    side = gath.shape[1]
    lanes = width // nd
    per = width // side
    first_o = 3 * per * per
    first_up = first_o + per * per
    first_dn = first_up + per * (FF // side)
    tile = width
    f32_rows = pltpu.VMEM((rows, width), F32)
    bf16_rows = pltpu.VMEM((rows, width), BF16)
    turned = pltpu.VMEM((width, rows), BF16)
    return pl.pallas_call(
        functools.partial(
            mlp_kernel, nd=nd, first_o=first_o, first_up=first_up, first_dn=first_dn, tile=tile
        ),
        out_shape=(
            sds((rows, width), BF16),
            sds((rows, width), F32),
            sds((nd, rows, lanes), BF16),
            sds((8 * (4 + FF // width), width), F32),
            sds(gath.shape, BF16),
        ),
        in_specs=[smem(), vmem(), vmem(), vmem(), vmem(), hbm()],
        out_specs=(hbm(), hbm(), hbm(), vmem(), hbm()),
        scratch_shapes=[
            pltpu.VMEM((width, width), BF16),
            pltpu.VMEM((FF // tile, width, tile), BF16),
            pltpu.VMEM((FF // tile, tile, width), BF16),
            f32_rows,
            f32_rows,
            f32_rows,
            bf16_rows,
            turned,
            turned,
            bf16_rows,
            bf16_rows,
            f32_rows,
            bf16_rows,
            bf16_rows,
            pltpu.VMEM((nd, rows, lanes), BF16),
            pltpu.VMEM((2, 2 * per * (tile // side), side, side), BF16),
            pltpu.SemaphoreType.DMA((1,)),
            pltpu.SemaphoreType.DMA((FF // tile,)),
            pltpu.SemaphoreType.DMA((2,)),
            pltpu.SemaphoreType.DMA((3,)),
        ],
        compiler_params=params(),
        name="mlp",
    )(slot_of, att, x, dy, vec, gath)


def dh1_dot(cat, w, dh1, part, half):
    width = dh1.shape[1]
    c = slice(half * width // 2, (half + 1) * width // 2)
    res = dot_nt(cat[:, part * width:(part + 1) * width], w[part, c, :])
    if part == 0:
        dh1[:, c] = res
    else:
        dh1[:, c] += res


def first_norm_back(cat, x, dh1, dx1, ig, vec_ref):
    rows, width = x.shape
    chunk = 128
    zero = jnp.zeros((8, width), F32)

    def finish(r, carry):
        s_gain, s_shift, s_bq, s_bv = carry
        at = pl.ds(pl.multiple_of(r * chunk, chunk), chunk)
        centred, inv = layer_stats(x[at, :].astype(F32))
        hat = centred * inv
        dh = dh1[at, :]
        dhg = dh * vec_ref[GAIN1:GAIN1 + 1, :]
        back = inv * (
            dhg
            - jnp.mean(dhg, axis=-1, keepdims=True)
            - hat * jnp.mean(dhg * hat, axis=-1, keepdims=True)
        )
        ig[at, :] = dx1[at, :] + back
        return (
            s_gain + fold_rows(dh * hat),
            s_shift + fold_rows(dh),
            s_bq + fold_rows(cat[at, 0:width].astype(F32)),
            s_bv + fold_rows(cat[at, 2 * width:3 * width].astype(F32)),
        )

    return lax.fori_loop(0, rows // chunk, finish, (zero, zero, zero, zero))


def vector_rows(first, sums2):
    rows = [jnp.sum(v, axis=0, keepdims=True) for v in first]
    rows += [jnp.sum(sums2[8 * n:8 * n + 8, :], axis=0, keepdims=True) for n in range(sums2.shape[0] // 8)]
    return rows


def dh1_kernel(cat_ref, x_ref, dx1_ref, vec_ref, wq_ref, sums2_ref, ig_ref, vsum_ref, dh1):
    for part in range(3):
        for half in range(2):
            dh1_dot(cat_ref, wq_ref, dh1, part, half)
    first = first_norm_back(cat_ref, x_ref, dh1, dx1_ref, ig_ref, vec_ref)
    for n, row in enumerate(vector_rows(first, sums2_ref)):
        vsum_ref[n:n + 1, :] = row


def run_dh1(cat, x, dx1, vec, wq, sums2):
    rows, width = x.shape
    return pl.pallas_call(
        dh1_kernel,
        out_shape=(sds((rows, width), F32), sds(vec.shape, F32)),
        in_specs=[vmem()] * 6,
        out_specs=(vmem(), vmem()),
        scratch_shapes=[pltpu.VMEM((rows, width), F32)],
        compiler_params=params(),
        name="dh1",
    )(cat, x, dx1, vec, wq, sums2)


def wgrad_kernel(slot_ref, h1_ref, cat_ref, rest, out, a_t, stage, sem_out, *, side, tile):
    del rest
    rows, width = h1_ref.shape
    per = width // side
    cols = tile // side
    steps = cat_ref.shape[1] // tile
    for r in range(width // 256):
        c = slice(r * 256, (r + 1) * 256)
        a_t[c, :] = turn(h1_ref[:, c])

    def left(slot):
        pltpu.make_async_copy(stage.at[slot], stage.at[slot], sem_out.at[slot]).wait()

    @pl.loop(0, steps)
    def _(t):
        slot = lax.rem(t, 2)

        @pl.when(t >= 2)
        def _():
            left(slot)
        res = dot_nn(a_t[...], cat_ref[:, pl.ds(pl.multiple_of(t * tile, tile), tile)]).astype(BF16)
        for i in range(per):
            for j in range(cols):
                stage[slot, i * cols + j] = res[i * side:(i + 1) * side, j * side:(j + 1) * side]

        for i in range(per):
            for j in range(cols):
                dst = slot_at(slot_ref, i * 3 * per + t * cols + j)
                pltpu.make_async_copy(stage.at[slot, i * cols + j], out.at[dst], sem_out.at[slot]).start()

    left(0)
    left(1)


def run_wgrad(slot_of, h1, cat, grads):
    rows, width = h1.shape
    side = grads.shape[1]
    tile = 512
    return pl.pallas_call(
        functools.partial(wgrad_kernel, side=side, tile=tile),
        out_shape=sds(grads.shape, BF16),
        in_specs=[smem(), vmem(), vmem(), hbm()],
        out_specs=hbm(),
        scratch_shapes=[
            pltpu.VMEM((width, rows), BF16),
            pltpu.VMEM((2, (width // side) * (tile // side), side, side), BF16),
            pltpu.SemaphoreType.DMA((2,)),
        ],
        input_output_aliases={3: 0},
        compiler_params=params(),
        name="wgrad",
    )(slot_of, h1, cat, grads)


def whereami():
    g = lax.axis_index("grp")
    d = lax.axis_index("dev")
    core = lax.rem(d, 2)
    x = lax.rem(d // 2, 2)
    y = d // 4
    over_x = d + 2 - 4 * x
    over_y = d + 4 - 8 * y
    across = over_x + 4 - 8 * y
    sibling = d + 1 - 2 * core
    return g, d, over_x, over_y, across, sibling


def near_order(t, g, ng):
    t = ng - 1 - t
    low = jnp.where(t < ng - 1 - g, ng - 1 - t, t - (ng - 1 - g))
    high = jnp.where(t < g, t, ng - 1 - (t - g))
    return jnp.where(2 * g < ng, low, high)


def greet(g, ng, peers):
    barrier = pltpu.get_barrier_semaphore()
    for peer in peers:
        pl.semaphore_signal(barrier, inc=1, device_id=(g, peer), device_id_type=MESH)

    d = lax.axis_index("dev")

    @pl.when(g > 0)
    def _():
        pl.semaphore_signal(barrier, inc=1, device_id=(g - 1, d), device_id_type=MESH)

    @pl.when(g < ng - 1)
    def _():
        pl.semaphore_signal(barrier, inc=1, device_id=(g + 1, d), device_id_type=MESH)

    ends = (g > 0).astype(jnp.int32) + (g < ng - 1).astype(jnp.int32)
    pl.semaphore_wait(barrier, len(peers) + ends)


def slot_cuts(count):
    third = 2 * (count // 12)
    first = (count - third) // 2
    return first, count - third - first, third // 2, third // 2


def gather_kernel(
    w_ref, x_ref, block_ref, vin_ref, out, h1_ref, slot_ref, vec_ref,
    own, local_sem, zs, zr, cs, cr, ss, sr, *, ng, nd
):
    count = w_ref.shape[0]
    na, nb, nc1, nc2 = slot_cuts(count)
    flat = na + nb
    nc = nc1 + nc2
    g, d, over_x, over_y, across, sibling = whereami()
    columns = (d, over_x, over_y, across)
    own[...] = w_ref[...].astype(BF16)
    greet(g, ng, (over_x, over_y, sibling))

    def region(gz, dev, first=0, size=count):
        return out.at[pl.ds((gz * nd + dev) * count + first, size)]

    def wide(t):
        return count if t == 0 else flat

    def kind(n, t):
        return (
            (d, 0, wide(t), over_x),
            (d, 0, wide(t), over_y),
            (d, 0, wide(t), sibling),
            (over_x, 0, na, over_y),
            (over_y, na, nb, over_x),
            (over_x, 0, wide(t), sibling),
            (over_y, 0, wide(t), sibling),
            (across, 0, na, sibling),
            (across, na, nb, sibling),
            (over_x, flat, nc1, over_y),
            (over_y, flat + nc1, nc2, over_x),
            (across, flat, nc1, sibling),
            (across, flat + nc1, nc2, sibling),
            (d, flat, nc, sibling),
            (over_x, flat, nc, sibling),
            (over_y, flat, nc, sibling),
            (across, flat, nc, sibling),
        )[n]

    def kinds(t):
        return range(13) if t == 0 else tuple(range(9)) + tuple(range(13, 17))

    def plane(n, t, src=None):
        gz = near_order(t, g, ng)
        dev, first, size, to = kind(n, t)
        at = region(gz, dev, first, size)
        return remote(at if src is None else src, at, ss.at[n, gz], sr.at[n, gz], (g, to))

    def landed(n, t, dev):
        gz = near_order(t, g, ng)
        _, first, size, _ = kind(n, t)
        arrived(region(gz, dev, first, size), sr.at[n, gz])

    def line(gz, up, src=None):
        at = region(gz, d, 0, flat)
        to = g + 1 if up else g - 1
        return remote(at if src is None else src, at, zs.at[gz, int(up)], zr.at[gz], (to, d))

    def corner_line(gz, c, up, src=None):
        at = region(gz, columns[c], flat, nc)
        to = g + 1 if up else g - 1
        return remote(at if src is None else src, at, cs.at[gz, c, int(up)], cr.at[gz, c], (to, d))

    def both_ways(gz, make):
        @pl.when((gz <= g) & (g < ng - 1))
        def _():
            make(True)

        @pl.when((gz >= g) & (g > 0))
        def _():
            make(False)

    mine = pltpu.make_async_copy(own, region(g, d), local_sem.at[0])
    mine.start()

    def column(t):
        gz = near_order(t, g, ng)
        if t == 0:
            both_ways(gz, lambda up: line(gz, up, cut(own, 0, flat)).start())
            for n in range(3):
                plane(n, t, own).start()
            both_ways(gz, lambda up: corner_line(gz, 0, up, cut(own, flat, nc)).start())
            return
        arrived(region(gz, d, 0, flat), zr.at[gz])
        both_ways(gz, lambda up: line(gz, up).start())
        for n in range(3):
            plane(n, t).start()

    def sides(t):
        gz = near_order(t, g, ng)
        landed(0, t, over_x)
        plane(3, t).start()
        if t == 0:
            plane(9, t).start()
            both_ways(gz, lambda up: corner_line(gz, 1, up).start())
        plane(5, t).start()
        landed(1, t, over_y)
        plane(4, t).start()
        if t == 0:
            plane(10, t).start()
            both_ways(gz, lambda up: corner_line(gz, 2, up).start())
        plane(6, t).start()

    def corner(t):
        gz = near_order(t, g, ng)
        if t == 0:
            landed(9, t, across)
            landed(10, t, across)
            both_ways(gz, lambda up: corner_line(gz, 3, up).start())
            plane(11, t).start()
            plane(12, t).start()
        landed(3, t, across)
        plane(7, t).start()
        landed(4, t, across)
        plane(8, t).start()

    def far_corner(t):
        gz = near_order(t, g, ng)
        for c in range(4):
            arrived(region(gz, columns[c], flat, nc), cr.at[gz, c])
            both_ways(gz, lambda up: corner_line(gz, c, up).start())
            plane(13 + c, t).start()

    plan = [(t, f) for t in range(ng) for f in (0, 1, 2, 3) if t > 0 or f < 3]
    lag = {0: 0, 1: 1.5, 2: 2.6, 3: 2.2}
    for t, f in sorted(plan, key=lambda e: e[0] * 1.0 + lag[e[1]]):
        (column, sides, corner, far_corner)[f](t)
        if (t, f) == (0, 0):
            prepare(x_ref, block_ref, vin_ref, h1_ref, slot_ref, vec_ref)

    for t in range(ng):
        for n in kinds(t):
            dev, _, _, to = kind(n, t)
            if to is sibling:
                landed(n, t, dev + sibling - d)
    mine.wait()
    for t in range(ng):
        gz = near_order(t, g, ng)
        for n in kinds(t):
            plane(n, t).wait_send()
        both_ways(gz, lambda up: line(gz, up).wait_send())
        for c in range(4):
            both_ways(gz, lambda up: corner_line(gz, c, up).wait_send())


def run_gather(w, x, blocks, vin, ng, nd):
    count, side, _ = w.shape
    dma = pltpu.SemaphoreType.DMA
    return pl.pallas_call(
        functools.partial(gather_kernel, ng=ng, nd=nd),
        out_shape=(sds((ng * nd * count, side, side), BF16),) + prepared_shapes(x, blocks, vin),
        in_specs=[vmem()] * 4,
        out_specs=(hbm(), vmem(), vmem(), vmem()),
        scratch_shapes=[
            pltpu.VMEM((count, side, side), BF16),
            dma((1,)),
            dma((ng, 2)),
            dma((ng,)),
            dma((ng, 4, 2)),
            dma((ng, 4)),
            dma((17, ng)),
            dma((17, ng)),
        ],
        compiler_params=params(collective_id=0, has_side_effects=True),
        name="gather",
    )(w, x, blocks, vin)


def add_blocks(dst, src, size):
    step = 4 if size % 4 == 0 else 2 if size % 2 == 0 else 1

    @pl.loop(0, size // step)
    def _(n):
        for k in range(step):
            dst[n * step + k] = dst[n * step + k] + src[n * step + k]


def scatter_kernel(
    grads, sums2_ref, vec_ref, vin_ref, cat_in, x_in, dx1_in, wq_in, out_ref, vout_ref, vnew_ref, ig_out,
    cat, x, dx1, wq, dh1, sem_in, mine, r0, r1y, r1x, r2x, r2y, rz, cz, cy, cx, cx2, cy2, vwork, vxy, vz,
    load, s0, w0, s1, w1, s2, w2, sz, wz, sc, wc, s3, w3, vs, vw, *, ng, nd, rate
):
    count = out_ref.shape[0]
    na, nb, nc1, nc2 = slot_cuts(count)
    flat = na + nb
    nc = nc1 + nc2
    g, d, over_x, over_y, across, sibling = whereami()
    columns = (d, over_x, over_y, across)

    def region(gz, dev):
        return grads.at[pl.ds((gz * nd + dev) * count, count)]

    def order(t):
        return near_order(ng - 1 - t, g, ng)

    for t in range(ng):
        for c in range(4):
            pltpu.make_async_copy(region(order(t), columns[c]), mine.at[order(t), c], load.at[order(t), c]).start()
    greet(g, ng, (over_x, over_y, sibling))

    def to_sibling(gz, c):
        return remote(
            region(gz, columns[c] + sibling - d), r0.at[gz, c], s0.at[gz, c], w0.at[gz, c], (g, sibling)
        )

    peers = (sibling, over_x, over_y)

    def vec_copy(n):
        return remote(vwork.at[n], vxy.at[n], vs.at[n], vw.at[n], (g, peers[n]))

    for t in range(ng):
        for c in (3, 2, 1, 0):
            to_sibling(order(t), c).start()
    inputs = [
        pltpu.make_async_copy(cat_in, cat, sem_in.at[0]),
        pltpu.make_async_copy(wq_in, wq, sem_in.at[1]),
        pltpu.make_async_copy(x_in, x, sem_in.at[2]),
        pltpu.make_async_copy(dx1_in, dx1, sem_in.at[3]),
    ]
    for copy in inputs:
        copy.start()
    input_grad = pltpu.make_async_copy(dx1, ig_out, sem_in.at[4])

    def first_norm():
        for copy in inputs:
            copy.wait()
        for part in range(3):
            for half in range(2):
                dh1_dot(cat, wq, dh1, part, half)
        first = first_norm_back(cat, x, dh1, dx1, dx1, vec_ref)
        input_grad.start()
        for n, row in enumerate(vector_rows(first, sums2_ref)):
            vwork[0, n:n + 1, :] = row
        vec_copy(0).start()

    first = (
        (2, 0, na, r1y, 0, over_y),
        (3, 0, na, r1y, 1, over_y),
        (1, na, nb, r1x, 0, over_x),
        (3, na, nb, r1x, 1, over_x),
    )
    second = ((1, 0, na, r2x, over_x), (2, na, nb, r2y, over_y))
    third = (
        (2, flat, nc1, cy.at[0], over_y),
        (3, flat, nc1, cy.at[1], over_y),
        (1, flat + nc1, nc2, cx.at[0], over_x),
        (3, flat + nc1, nc2, cx.at[1], over_x),
        (1, flat, nc1, cx2, over_x),
        (2, flat + nc1, nc2, cy2, over_y),
    )

    def copy1(n, gz):
        c, at, size, buf, place_at, to = first[n]
        return remote(cut(mine.at[gz, c], at, size), buf.at[gz, place_at], s1.at[n, gz], w1.at[n, gz], (g, to))

    def copy2(n, gz):
        c, at, size, buf, to = second[n]
        return remote(cut(mine.at[gz, c], at, size), buf.at[gz], s2.at[n, gz], w2.at[n, gz], (g, to))

    def copy3(n):
        c, at, size, buf, to = third[n]
        return remote(cut(mine.at[g, c], at, size), buf, s3.at[n], w3.at[n], (g, to))

    def flat_part(gz):
        return cut(mine.at[gz, 0], 0, flat)

    def corner_part(gz):
        return mine.at[gz, :, pl.ds(flat, nc)]

    def line(gz, part, buf, sends, waits, up):
        at = gz if up else jnp.where(gz < g - 1, gz, ng)
        to = g + 1 if up else g - 1
        return remote(part(gz), buf.at[at], sends.at[gz], waits.at[at], (to, d))

    def pass_on(gz, part, buf, sends, waits, gather):
        @pl.when(gz > g)
        def _():
            @pl.when(g > 0)
            def _():
                arrived(buf.at[gz], waits.at[gz])
                gather(gz)
            line(gz, part, buf, sends, waits, True).start()

        @pl.when(gz < g)
        def _():
            @pl.when(g < ng - 1)
            def _():
                arrived(buf.at[gz], waits.at[gz])
                gather(gz)
            line(gz, part, buf, sends, waits, False).start()

    def gather_flat(gz):
        add_blocks(flat_part(gz), rz.at[gz], flat)

    def gather_corner(at, gz):
        for c in range(4):
            add_blocks(cut(mine.at[gz, c], flat, nc), cz.at[at, c], nc)

    def sums0(t):
        gz = order(t)
        for c in (3, 2, 1, 0):
            pltpu.make_async_copy(region(gz, columns[c]), mine.at[gz, c], load.at[gz, c]).wait()
            arrived(r0.at[gz, c], w0.at[gz, c])
            add_blocks(mine.at[gz, c], r0.at[gz, c], count)
            if t < ng - 1:
                sends0(t, c)

    def sends0(t, c):
        gz = order(t)
        for n in {3: (1, 3), 2: (0,), 1: (2,), 0: ()}[c]:
            copy1(n, gz).start()

    def along0(t):
        pass_on(order(t), corner_part, cz, sc, wc, lambda gz: gather_corner(gz, gz))

    def stage1(t):
        gz = order(t)
        arrived(r1y.at[gz, 1], w1.at[1, gz])
        add_blocks(cut(mine.at[gz, 1], 0, na), r1y.at[gz, 1], na)
        copy2(0, gz).start()
        arrived(r1x.at[gz, 1], w1.at[3, gz])
        add_blocks(cut(mine.at[gz, 2], na, nb), r1x.at[gz, 1], nb)
        copy2(1, gz).start()
        arrived(r1y.at[gz, 0], w1.at[0, gz])
        add_blocks(cut(mine.at[gz, 0], 0, na), r1y.at[gz, 0], na)
        arrived(r1x.at[gz, 0], w1.at[2, gz])
        add_blocks(cut(mine.at[gz, 0], na, nb), r1x.at[gz, 0], nb)

    def stage2(t):
        gz = order(t)
        arrived(r2x.at[gz], w2.at[0, gz])
        add_blocks(cut(mine.at[gz, 0], 0, na), r2x.at[gz], na)
        arrived(r2y.at[gz], w2.at[1, gz])
        add_blocks(cut(mine.at[gz, 0], na, nb), r2y.at[gz], nb)
        if t < ng - 1:
            pass_on(gz, flat_part, rz, sz, wz, gather_flat)

    def corner0():
        @pl.when(g > 0)
        def _():
            arrived(cz.at[g], wc.at[g])
            gather_corner(g, g)

        @pl.when(g < ng - 1)
        def _():
            arrived(cz.at[ng], wc.at[ng])
            gather_corner(ng, g)
        for n in range(4):
            copy3(n).start()

    def corner1():
        arrived(cy.at[1], w3.at[1])
        add_blocks(cut(mine.at[g, 1], flat, nc1), cy.at[1], nc1)
        copy3(4).start()
        arrived(cx.at[1], w3.at[3])
        add_blocks(cut(mine.at[g, 2], flat + nc1, nc2), cx.at[1], nc2)
        copy3(5).start()
        arrived(cy.at[0], w3.at[0])
        add_blocks(cut(mine.at[g, 0], flat, nc1), cy.at[0], nc1)
        arrived(cx.at[0], w3.at[2])
        add_blocks(cut(mine.at[g, 0], flat + nc1, nc2), cx.at[0], nc2)

    def corner2():
        arrived(cx2, w3.at[4])
        add_blocks(cut(mine.at[g, 0], flat, nc1), cx2, nc1)
        arrived(cy2, w3.at[5])
        add_blocks(cut(mine.at[g, 0], flat + nc1, nc2), cy2, nc2)

    def vec_step(n):
        arrived(vxy.at[n], vw.at[n])
        total = vwork[n] + vxy[n]
        if n < 2:
            vwork[n + 1] = total
            vec_copy(n + 1).start()
        else:
            vz[g] = total

    def vec_line(gz, up):
        to = g + 1 if up else g - 1
        return remote(vz.at[gz], vz.at[gz], vs.at[3 + 2 * gz + int(up)], vw.at[3 + gz], (to, d))

    last = ng - 1
    sums0(0)
    sums0(1)
    first_norm()
    along0(0)
    stage1(0)
    for t in range(2, last):
        sums0(t)
        along0(t - 1)
        vec_step(t - 2)
        stage1(t - 1)
        stage2(t - 2)
    vec_step(1)
    sums0(last)
    along0(last - 1)
    stage1(last - 1)
    for c in (3, 2, 1):
        sends0(last, c)
    corner0()
    vec_step(2)

    @pl.when(g < ng - 1)
    def _():
        vec_line(g, True).start()

    @pl.when(g > 0)
    def _():
        vec_line(g, False).start()
    stage2(last - 2)
    for n in range(1, ng):
        gz = near_order(n, g, ng)
        arrived(vz.at[gz], vw.at[3 + gz])

        @pl.when((gz < g) & (g < ng - 1))
        def _():
            vec_line(gz, True).start()

        @pl.when((gz > g) & (g > 0))
        def _():
            vec_line(gz, False).start()
    stage2(last - 1)
    stage1(last)
    corner1()
    total = vz[0]
    for z in range(1, ng):
        total = total + vz[z]
    vwork[3] = total
    per = total.shape[1] // 128
    for r in range(total.shape[0]):
        for c in range(per):
            row = vwork[3, r:r + 1, c * 128:(c + 1) * 128]
            n = per * r + c
            vout_ref[n:n + 1, :] = row
            vnew_ref[n:n + 1, :] = vin_ref[n:n + 1, :] - rate * row
    stage2(last)
    corner2()

    @pl.when(g > 0)
    def _():
        arrived(rz.at[g], wz.at[g])

    @pl.when(g < ng - 1)
    def _():
        arrived(rz.at[ng], wz.at[ng])

    @pl.when((g > 0) & (g < ng - 1))
    def _():
        @pl.loop(0, flat // 2)
        def _(n):
            for k in range(2):
                i = 2 * n + k
                out_ref[i] = mine[g, 0, i].astype(F32) + rz[g, i].astype(F32) + rz[ng, i].astype(F32)

    @pl.when(g == 0)
    def _():
        @pl.loop(0, flat // 2)
        def _(n):
            for k in range(2):
                i = 2 * n + k
                out_ref[i] = mine[g, 0, i].astype(F32) + rz[ng, i].astype(F32)

    @pl.when((g > 0) & (g == ng - 1))
    def _():
        @pl.loop(0, flat // 2)
        def _(n):
            for k in range(2):
                i = 2 * n + k
                out_ref[i] = mine[g, 0, i].astype(F32) + rz[g, i].astype(F32)

    for i in range(flat, count):
        out_ref[i] = mine[g, 0, i].astype(F32)

    for t in range(ng):
        gz = order(t)
        for c in range(4):
            to_sibling(gz, c).wait_send()
        for n in range(4):
            copy1(n, gz).wait_send()
        for n in range(2):
            copy2(n, gz).wait_send()
        if t < ng - 1:
            arrived(flat_part(gz), sz.at[gz])
            arrived(corner_part(gz), sc.at[gz])
    input_grad.wait()
    for n in range(6):
        copy3(n).wait_send()
    for n in range(3):
        vec_copy(n).wait_send()
    for n in range(ng):
        gz = near_order(n, g, ng)

        @pl.when((gz <= g) & (g < ng - 1))
        def _():
            vec_line(gz, True).wait_send()

        @pl.when((gz >= g) & (g > 0))
        def _():
            vec_line(gz, False).wait_send()


def run_scatter(grads, sums2, vec, vin, cat, x, dx1, wq, ng, nd, rate):
    blocks, side, _ = grads.shape
    count = blocks // (ng * nd)
    na, nb, nc1, nc2 = slot_cuts(count)
    flat = na + nb
    dma = pltpu.SemaphoreType.DMA

    def buf(*lead):
        return pltpu.VMEM(lead + (side, side), BF16)

    def like(v):
        return pltpu.VMEM(v.shape, v.dtype)

    return pl.pallas_call(
        functools.partial(scatter_kernel, ng=ng, nd=nd, rate=rate),
        out_shape=(
            sds((count, side, side), F32),
            sds(vin.shape, F32),
            sds(vin.shape, F32),
            sds(dx1.shape, F32),
        ),
        in_specs=[hbm(), vmem(), vmem(), vmem()] + [hbm()] * 4,
        out_specs=(vmem(), vmem(), vmem(), hbm()),
        scratch_shapes=[
            like(cat),
            like(x),
            like(dx1),
            like(wq),
            like(dx1),
            dma((5,)),
            buf(ng, 4, count),
            buf(ng, 4, count),
            buf(ng, 2, na),
            buf(ng, 2, nb),
            buf(ng, na),
            buf(ng, nb),
            buf(ng + 1, flat),
            buf(ng + 1, 4, nc1 + nc2),
            buf(2, nc1),
            buf(2, nc2),
            buf(nc1),
            buf(nc2),
            pltpu.VMEM((4,) + vec.shape, F32),
            pltpu.VMEM((3,) + vec.shape, F32),
            pltpu.VMEM((ng,) + vec.shape, F32),
            dma((ng, 4)),
            dma((ng, 4)),
            dma((ng, 4)),
            dma((4, ng)),
            dma((4, ng)),
            dma((2, ng)),
            dma((2, ng)),
            dma((ng,)),
            dma((ng + 1,)),
            dma((ng,)),
            dma((ng + 1,)),
            dma((6,)),
            dma((6,)),
            dma((3 + 2 * ng,)),
            dma((3 + ng,)),
        ],
        compiler_params=params(61, collective_id=1, has_side_effects=True),
        name="scatter",
    )(grads, sums2, vec, vin, cat, x, dx1, wq)


def blocks_kernel(*refs, handed):
    g_ref, w_ref, ls_ref, rs_ref, lr_ref, rr_ref = refs[:6]
    wg_out, nl_out, nr_out, nw_out = refs[6 + handed:10 + handed]
    for n in range(handed):
        refs[10 + handed + n][...] = refs[6 + n][...]

    for i in range(g_ref.shape[0]):
        grad = g_ref[i]
        wg_out[i] = grad
        hi = grad.astype(BF16)
        low = (grad - hi.astype(F32)).astype(BF16)
        nl_out[i] = 0.5 * ls_ref[i] + 0.5 * dot_nt(hi, hi)
        turned = grad.T
        hi_t = turned.astype(BF16)
        nr_out[i] = 0.5 * rs_ref[i] + 0.5 * dot_nt(hi_t, hi_t)
        left = lr_ref[i]
        left_hi = left.astype(BF16)
        left_low = (left - left_hi.astype(F32)).astype(BF16)
        shaped = dot_nn(left_hi, hi) + dot_nn(left_hi, low) + dot_nn(left_low, hi)
        right = rr_ref[i]
        right_hi = right.astype(BF16)
        right_low = (right - right_hi.astype(F32)).astype(BF16)
        sh_hi = shaped.astype(BF16)
        sh_low = (shaped - sh_hi.astype(F32)).astype(BF16)
        shaped = dot_nn(sh_hi, right_hi) + dot_nn(sh_low, right_hi) + dot_nn(sh_hi, right_low)
        nw_out[i] = w_ref[i] - weight_rate * shaped


def run_blocks(grads, weights, left_stats, right_stats, left_roots, right_roots, *passing):
    count, side, _ = grads.shape
    steps = math.gcd(count, 4)
    step = count // steps
    spec = pl.BlockSpec((step, side, side), lambda n: (n, 0, 0))
    through = []
    for v in passing:
        part = v.shape[0] // steps
        if part % 8 == 0:
            through.append(pl.BlockSpec((part, v.shape[1]), lambda n: (n, 0)))
        else:
            through.append(pl.BlockSpec(v.shape, lambda n: (0, 0)))
    return pl.pallas_call(
        functools.partial(blocks_kernel, handed=len(passing)),
        grid=(steps,),
        out_shape=tuple([sds(grads.shape, F32)] * 4) + tuple(sds(v.shape, v.dtype) for v in passing),
        in_specs=[spec] * 6 + through,
        out_specs=tuple([spec] * 4) + tuple(through),
        compiler_params=params(),
        name="blocks",
    )(grads, weights, left_stats, right_stats, left_roots, right_roots, *passing)


def local(
    inputs,
    cotangent,
    weight_slots,
    slot_block,
    left_stats,
    right_stats,
    left_roots,
    right_roots,
    vectors,
    span_start,
):
    seq_count, tok_count, width = inputs.shape
    rows = seq_count * tok_count
    nd = lax.axis_size("dev")
    ng = lax.axis_size("grp")
    side = weight_slots.shape[1]
    hpd = H // nd
    lanes = width // nd
    head = lax.axis_index("dev") * hpd + jnp.arange(hpd, dtype=jnp.int32)
    slopes = jnp.exp2(-8.0 * (head.astype(F32) + 1.0) / H)
    vin = vectors.reshape(-1, 128)
    held = slot_block.reshape(-1, 128)
    x = inputs.reshape(rows, width)
    dy = cotangent.reshape(rows, width)
    rate = vector_rate / math.sqrt(rows * nd * ng)

    direct = nd == 8
    if direct:
        gath, h1, slot_of, vec = run_gather(weight_slots, x, held, vin, ng, nd)
    else:
        gath = lax.all_gather(weight_slots.astype(BF16), ("grp", "dev"), axis=0, tiled=True)
        h1, slot_of, vec = run_prepare(x, held, vin)
    qkv, wq = run_qkv(slot_of, h1, vec, gath, nd)
    qkv, o, o32, lse = run_attn_fwd(
        span_start, slopes, qkv.reshape(nd, 3, seq_count, tok_count, lanes), hpd
    )
    att = side_by_side(o, 1, rows)
    act, dx1, do, sums2, grads = run_mlp(slot_of, att, x, dy, vec, gath, nd)
    do = do.reshape(nd, seq_count, tok_count, lanes)
    cat = side_by_side(run_attn_bwd(span_start, slopes, qkv, do, o32, lse, hpd), 3, rows)
    grads = run_wgrad(slot_of, h1, cat, grads)
    if direct:
        weight_grads, vector_grads, new_vectors, ig = run_scatter(
            grads, sums2, vec, vin, cat, x, dx1, wq, ng, nd, rate
        )
        passing = (ig, vector_grads, new_vectors)
    else:
        ig, vsum = run_dh1(cat, x, dx1, vec, wq, sums2)
        vector_grads = lax.psum(vsum.reshape(-1), ("grp", "dev"))
        new_vectors = vectors - rate * vector_grads
        weight_grads = lax.psum_scatter(grads, ("grp", "dev"), scatter_dimension=0, tiled=True)
        weight_grads = weight_grads.astype(F32)
        passing = ()
    weight_grads, new_left, new_right, new_weights, *passed = run_blocks(
        weight_grads, weight_slots, left_stats, right_stats, left_roots, right_roots, *passing
    )
    if direct:
        ig, vector_grads, new_vectors = passed
    return (
        act.reshape(inputs.shape),
        ig.reshape(inputs.shape),
        weight_grads,
        new_left,
        new_right,
        new_weights,
        vector_grads.reshape(-1),
        new_vectors.reshape(-1),
    )


def solution(mesh):
    return jax.shard_map(
        local,
        mesh=mesh,
        in_specs=(
            P("grp", "dev", None),
            P("grp", "dev", None),
            P(("grp", "dev"), None, None),
            P(),
            P(("grp", "dev"), None, None),
            P(("grp", "dev"), None, None),
            P(("grp", "dev"), None, None),
            P(("grp", "dev"), None, None),
            P(),
            P("grp"),
        ),
        out_specs=(
            P("grp", "dev", None),
            P("grp", "dev", None),
            P(("grp", "dev"), None, None),
            P(("grp", "dev"), None, None),
            P(("grp", "dev"), None, None),
            P(("grp", "dev"), None, None),
            P(),
            P(),
        ),
        check_vma=False,
    )
```

```python
import functools
import math

import jax
import jax.numpy as jnp
from jax import lax
from jax.experimental import pallas as pl
from jax.experimental.pallas import tpu as pltpu
from jax.sharding import PartitionSpec as P

H = 16
FF = 4096
PIC = 256

eps = 1e-05
weight_rate = 0.5
vector_rate = 0.5
big_negative = -1e30
highest = lax.Precision.HIGHEST
F32 = jnp.float32
BF16 = jnp.bfloat16
LOG2E = 1.4426950408889634
MIB = 1024 * 1024

GAIN1, SHIFT1, BQ, BV, BO, GAIN2, SHIFT2, BDOWN, BUP = range(9)


def dot_nn(a, b):
    return lax.dot_general(a, b, (((1,), (0,)), ((), ())), preferred_element_type=F32)


def dot_nt(a, b):
    return lax.dot_general(a, b, (((1,), (1,)), ((), ())), preferred_element_type=F32)


def turn(v):
    return v.astype(F32).T.astype(BF16)


def vmem():
    return pl.BlockSpec(memory_space=pltpu.VMEM)


def smem():
    return pl.BlockSpec(memory_space=pltpu.SMEM)


def hbm():
    return pl.BlockSpec(memory_space=pl.ANY)


def sds(shape, dtype):
    return jax.ShapeDtypeStruct(shape, dtype)


def params(mib=58, **kw):
    return pltpu.CompilerParams(vmem_limit_bytes=mib * MIB, **kw)


def layer_stats(v):
    middle = jnp.mean(v, axis=-1, keepdims=True)
    centred = v - middle
    spread = jnp.mean(centred * centred, axis=-1, keepdims=True)
    return centred, lax.rsqrt(spread + eps)


def fold_rows(v):
    return jnp.sum(v.reshape(v.shape[0] // 8, 8, v.shape[1]), axis=0)


def slot_at(slot_ref, block):
    lanes = slot_ref.shape[1]
    if isinstance(block, int):
        return slot_ref[block // lanes, block % lanes]
    return slot_ref[lax.div(block, lanes), lax.rem(block, lanes)]


def fetch_block(gath, slot, dst, row, col, sem, side):
    return pltpu.make_async_copy(
        gath.at[slot], dst.at[pl.ds(row, side), pl.ds(col, side)], sem
    )


def prepare(x_ref, block_ref, vin_ref, h1_ref, slot_ref, vec_ref):
    rows, width = x_ref.shape
    per = width // 128
    for r in range(vec_ref.shape[0]):
        for c in range(per):
            vec_ref[r:r + 1, c * 128:(c + 1) * 128] = vin_ref[per * r + c:per * r + c + 1, :]
    chunk = 128

    @pl.loop(0, rows // chunk)
    def _(r):
        at = pl.ds(pl.multiple_of(r * chunk, chunk), chunk)
        centred, inv = layer_stats(x_ref[at, :].astype(F32))
        h1_ref[at, :] = (
            centred * inv * vec_ref[GAIN1:GAIN1 + 1, :] + vec_ref[SHIFT1:SHIFT1 + 1, :]
        ).astype(BF16)

    tiles, lanes = slot_ref.shape
    line = lax.broadcasted_iota(jnp.int32, (8, lanes), 0)
    lane = lax.broadcasted_iota(jnp.int32, (8, lanes), 1).astype(F32)
    block = lax.broadcasted_iota(jnp.int32, (lanes, lanes), 0)
    for t in range(tiles):
        found = jnp.zeros((8, lanes), F32)
        for r in range(tiles):
            held = (block_ref[r:r + 1, :] == block + t * lanes).astype(F32).astype(BF16)
            found = found + dot_nt(jnp.where(line == 0, lane, float(r)).astype(BF16), held)
        slot_ref[t:t + 1, :] = (found[0:1] + float(lanes) * found[1:2]).astype(jnp.int32)


def prepared_shapes(x, blocks, vin):
    rows, width = x.shape
    return (
        sds((rows, width), BF16),
        sds(blocks.shape, jnp.int32),
        sds((vin.size // width, width), F32),
    )


def run_prepare(x, blocks, vin):
    return pl.pallas_call(
        prepare,
        out_shape=prepared_shapes(x, blocks, vin),
        in_specs=[vmem()] * 3,
        out_specs=tuple([vmem()] * 3),
        compiler_params=params(),
        name="prepare",
    )(x, blocks, vin)


def qkv_kernel(slot_ref, h1_ref, vec_ref, gath, out_ref, wq_out, wbuf, sems, sem_w, *, nd):
    rows, width = h1_ref.shape
    side = gath.shape[1]
    per = width // side
    lanes = out_ref.shape[3]
    for part in range(3):
        for i in range(per):
            for j in range(per):
                slot = slot_at(slot_ref, i * 3 * per + part * per + j)
                fetch_block(gath, slot, wbuf.at[part], i * side, j * side, sems.at[part], side).start()

    def keep(part):
        return pltpu.make_async_copy(wbuf.at[part], wq_out.at[part], sem_w.at[part])

    for part in range(3):
        pltpu.make_async_copy(wbuf.at[part], wbuf.at[part], sems.at[part]).wait()
        keep(part).start()
        for half in range(2):
            cols = slice(half * width // 2, (half + 1) * width // 2)
            res = dot_nn(h1_ref[...], wbuf[part, :, cols])
            if part == 0:
                res = res + vec_ref[BQ:BQ + 1, cols]
            if part == 2:
                res = res + vec_ref[BV:BV + 1, cols]
            res = res.astype(BF16)
            for d in range(nd // 2):
                out_ref[half * (nd // 2) + d, part, :, :] = res[:, d * lanes:(d + 1) * lanes]
    for part in range(3):
        keep(part).wait()


def run_qkv(slot_of, h1, vec, gath, nd):
    rows, width = h1.shape
    lanes = width // nd
    return pl.pallas_call(
        functools.partial(qkv_kernel, nd=nd),
        out_shape=(sds((nd, 3, rows, lanes), BF16), sds((3, width, width), BF16)),
        in_specs=[smem(), vmem(), vmem(), hbm()],
        out_specs=(vmem(), hbm()),
        scratch_shapes=[
            pltpu.VMEM((3, width, width), BF16),
            pltpu.SemaphoreType.DMA((3,)),
            pltpu.SemaphoreType.DMA((3,)),
        ],
        compiler_params=params(),
        name="qkv",
    )(slot_of, h1, vec, gath)


MESH = pl.DeviceIdType.MESH


def remote(src, dst, send, recv, device):
    return pltpu.make_async_remote_copy(
        src_ref=src, dst_ref=dst, send_sem=send, recv_sem=recv, device_id=device, device_id_type=MESH
    )


def arrived(ref, sem):
    pltpu.make_async_copy(ref, ref, sem).wait()


def cut(ref, first, size):
    return ref.at[pl.ds(first, size)]


def greet_plane(g, d, nd):
    barrier = pltpu.get_barrier_semaphore()
    for p in range(1, nd):
        pl.semaphore_signal(barrier, inc=1, device_id=(g, lax.rem(d + p, nd)), device_id_type=MESH)
    pl.semaphore_wait(barrier, nd - 1)


def landing(ref, part, source, q, tok, lanes, parts):
    if lanes % 128 == 0:
        first = (part * (ref.shape[1] // parts)) + source * lanes
        return ref.at[pl.ds(q * tok, tok), pl.ds(pl.multiple_of(first, lanes), lanes)]
    return ref.at[source, part, q]


def landing_shape(parts, nb, seqs, tok, lanes):
    if lanes % 128 == 0:
        return sds((seqs * tok, parts * nb * lanes), BF16)
    return sds((nb, parts, seqs, tok, lanes), BF16)


def side_by_side(got, parts, rows):
    if got.ndim == 2:
        return got
    nb, _, seqs, tok, lanes = got.shape
    return got.transpose(2, 3, 1, 0, 4).reshape(rows, parts * nb * lanes)


def parts3(v):
    hi = v.astype(BF16)
    mid = (v - hi.astype(F32)).astype(BF16)
    lo = (v - hi.astype(F32) - mid.astype(F32)).astype(BF16)
    return hi.astype(F32), mid.astype(F32), lo.astype(F32)


def own_lanes(h, shape, hpd, lanes):
    lane = lax.broadcasted_iota(jnp.int32, shape, 1)
    size = lanes // hpd
    return (lane >= h * size) & (lane < (h + 1) * size)


def place(values, base, tok, width):
    lane = lax.broadcasted_iota(jnp.int32, (tok, width), 1)
    out = jnp.zeros((tok, width), F32)
    for n, v in enumerate(values):
        out = jnp.where(lane == base + n, v, out)
    return out


def spare(h, hpd, lanes):
    return (lanes // hpd) * (1 - h) if hpd > 1 else 0


def column_tables(slope_ref, qbase, kbase, kfar, hpd, lanes):
    _, tok, _ = qbase.shape
    u = lax.broadcasted_iota(jnp.int32, (tok, 128), 0).astype(F32)
    for h in range(hpd):
        slope = slope_ref[h] * LOG2E
        base = spare(h, hpd, lanes)
        near = parts3(jnp.full((tok, 128), slope, F32))
        far = parts3(jnp.full((tok, 128), slope * tok, F32))
        qbase[h] = place(near + far, base, tok, 128)
        kbase[h] = place([u] * 3 + [0.0] * 3 + [1.0] * 3, base, tok, 128)
        kfar[h] = place([0.0] * 3 + [1.0] * 3, base, tok, 128)


def extra_lanes(columns, extra, h, hpd, lanes):
    lane = lax.broadcasted_iota(jnp.int32, columns.shape, 1)
    for n, v in enumerate(extra):
        columns = jnp.where(lane == spare(h, hpd, lanes) + 6 + n, v, columns)
    return columns


def q_columns(q, h, hpd, columns, extra):
    tok, lanes = q.shape
    scaled = q.astype(F32) * ((lanes // hpd) ** (-0.5) * LOG2E)
    hi = scaled.astype(BF16).astype(F32)
    low = scaled - hi
    if extra:
        columns = extra_lanes(columns, extra, h, hpd, lanes)
    if hpd > 1:
        own = own_lanes(h, (tok, lanes), hpd, lanes)
        return jnp.concatenate(
            [jnp.where(own, hi, 0.0), jnp.where(own, low, columns)], axis=1
        ).astype(BF16)
    return jnp.concatenate([hi, low, columns], axis=1).astype(BF16)


def k_columns(k, h, hpd, columns):
    tok, lanes = k.shape
    wide = k.astype(F32)
    if hpd > 1:
        own = own_lanes(h, (tok, lanes), hpd, lanes)
        return jnp.concatenate([wide, jnp.where(own, wide, columns)], axis=1).astype(BF16)
    return jnp.concatenate([wide, wide, columns], axis=1).astype(BF16)


def far_side(slope, tok):
    u = lax.broadcasted_iota(jnp.int32, (tok, tok), 0)
    t = lax.broadcasted_iota(jnp.int32, (tok, tok), 1)
    after = u > t
    return (
        jnp.where(after, big_negative, 0.0),
        jnp.where(after, (2.0 * slope) * (t - u).astype(F32), 0.0),
    )


def attn_fwd_kernel(
    span_ref, slope_ref, src, got, o_got, o32_ref, lse_ref,
    qa, ka, vt, scores, tops_ref, corr, qbase, kbase, kfar, o_out, ss, sr, os, orr, loc, *, hpd, nd
):
    nb, _, seqs, tok, lanes = got.shape
    size = lanes // hpd
    pair = 2 * tok
    g = lax.axis_index("grp")
    d = lax.axis_index("dev")

    for q in range(seqs):
        pltpu.make_async_copy(src.at[d, :, q], got.at[d, :, q], loc.at[q]).start()
    greet_plane(g, d, nd)

    def kind_of(kind):
        return pl.ds(2 * kind, 2 - kind)

    def send(q, kind, p):
        to = lax.rem(d + p, nd)
        return remote(
            src.at[to, kind_of(kind), q], got.at[d, kind_of(kind), q],
            ss.at[q, kind, p], sr.at[q, kind, p], (g, to),
        )

    def send_all(q, kind):
        @pl.loop(1, nd)
        def _(p):
            send(q, kind, p).start()

    def have(q, kind):
        @pl.loop(1, nd)
        def _(p):
            arrived(got.at[lax.rem(d + nd - p, nd), kind_of(kind), q], sr.at[q, kind, p])

    send_all(0, 0)
    send_all(0, 1)

    def o_place(source, q):
        return landing(o_got, 0, source, q, tok, lanes, 1)

    def send_o(q, i, p):
        return remote(o_out.at[i, q], o_place(d, q), os.at[q, i], orr.at[q, p], (g, i))

    column_tables(slope_ref, qbase, kbase, kfar, hpd, lanes)
    for h in range(hpd):
        mask, span = far_side(slope_ref[h] * LOG2E, tok)
        for n, (one, two) in enumerate(((mask, mask), (span, mask), (mask, span))):
            corr[h, n, 0:tok, 0:tok] = one
            corr[h, n, tok:, tok:] = two
            corr[h, n, 0:tok, tok:] = jnp.zeros((tok, tok), F32)
            corr[h, n, tok:, 0:tok] = jnp.full((tok, tok), big_negative, F32)

    def fold(v, how):
        return how(v.reshape(v.shape[0] // 8, 8, v.shape[1]), axis=0)

    whole = scores.shape[1] > nb // 2

    def tile_at(i, n):
        return (i * (i + 1)) // 2 + n if whole else n

    @pl.loop(0, seqs)
    def _(q):
        pltpu.make_async_copy(src.at[d, :, q], got.at[d, :, q], loc.at[q]).wait()
        start = span_ref[q]

        def score(i):
            flag = (start == i * pair).astype(jnp.int32) + 2 * (start == i * pair + tok).astype(jnp.int32)
            at_i = slice(i * pair, (i + 1) * pair)
            for h in range(hpd):
                top = None
                for n in range(i + 1):
                    s = dot_nt(ka[h, n * pair:(n + 1) * pair, :], qa[h, at_i, :])
                    if n == i:
                        s = s + corr[h, flag]
                    scores[h, tile_at(i, n)] = s
                    here = fold(s, jnp.max)
                    top = here if top is None else jnp.maximum(top, here)
                tops_ref[h, i] = jnp.broadcast_to(jnp.max(top, axis=0, keepdims=True), (8, pair))

        have(q, 0)

        @pl.when(q + 1 < seqs)
        def _():
            send_all(q + 1, 0)

        @pl.loop(0, nb)
        def _(j):
            at_j = pl.ds(pl.multiple_of(j * tok, tok), tok)
            block = jnp.full((tok, 128), j, jnp.int32).astype(F32)
            for h in range(hpd):
                qa[h, at_j, :] = q_columns(got[j, 0, q], h, hpd, qbase[h], [])
                ka[h, at_j, :] = k_columns(got[j, 1, q], h, hpd, kbase[h] + block * kfar[h])

        if whole:
            for i in range(nb // 2):
                score(i)
        have(q, 1)

        @pl.when(q + 1 < seqs)
        def _():
            send_all(q + 1, 1)

        @pl.loop(0, nb)
        def _(j):
            vt[0:lanes, pl.ds(pl.multiple_of(j * tok, tok), tok)] = turn(got[j, 2, q])

        for i in range(nb // 2):
            if not whole:
                score(i)
            outs = []
            logs = []
            for h in range(hpd):
                acc = total = None
                top = tops_ref[h, i][0:1]
                for n in range(i + 1):
                    p = jnp.exp2(scores[h, tile_at(i, n)] - top)
                    here = fold(p, jnp.sum)
                    part = dot_nn(vt[h * size:(h + 1) * size, n * pair:(n + 1) * pair], p.astype(BF16))
                    total = here if total is None else total + here
                    acc = part if acc is None else acc + part
                total = jnp.sum(total, axis=0, keepdims=True)
                outs.append(acc / total)
                logs.append(jnp.broadcast_to(top + jnp.log2(total), (128 // hpd, pair)))
            out = (jnp.concatenate(outs, axis=0) if hpd > 1 else outs[0]).T
            log = (jnp.concatenate(logs[::-1], axis=0) if hpd > 1 else logs[0]).T
            for k in range(2):
                at = 2 * i + k
                o32_ref[at, q] = out[k * tok:(k + 1) * tok]
                o_out[at, q] = out[k * tok:(k + 1) * tok].astype(BF16)
                lse_ref[at, q] = log[k * tok:(k + 1) * tok]

                @pl.when(at == d)
                def _():
                    pltpu.make_async_copy(o_out.at[at, q], o_place(d, q), os.at[q, at]).start()

                @pl.when(at != d)
                def _():
                    send_o(q, at, lax.rem(at - d + nd, nd)).start()

    for q in range(seqs):
        @pl.loop(1, nd)
        def _(p):
            arrived(o_place(lax.rem(d + nd - p, nd), q), orr.at[q, p])
            send(q, 0, p).wait_send()
            send(q, 1, p).wait_send()

        @pl.loop(0, nd)
        def _(i):
            arrived(o_out.at[i, q], os.at[q, i])


def run_attn_fwd(span, slopes, qkv, hpd):
    nb, _, seqs, tok, lanes = qkv.shape
    t = nb * tok
    pairs = nb // 2
    tiles = pairs * (pairs + 1) // 2
    if hpd * tiles > 24:
        tiles = pairs
    dma = pltpu.SemaphoreType.DMA
    return pl.pallas_call(
        functools.partial(attn_fwd_kernel, hpd=hpd, nd=nb),
        out_shape=(
            sds(qkv.shape, BF16),
            landing_shape(1, nb, seqs, tok, lanes),
            sds((nb, seqs, tok, lanes), F32),
            sds((nb, seqs, tok, 128), F32),
        ),
        in_specs=[smem(), smem(), hbm()],
        out_specs=(vmem(), vmem(), vmem(), vmem()),
        scratch_shapes=[
            pltpu.VMEM((hpd, t, 256), BF16),
            pltpu.VMEM((hpd, t, 256), BF16),
            pltpu.VMEM((lanes, t), BF16),
            pltpu.VMEM((hpd, tiles, 2 * tok, 2 * tok), F32),
            pltpu.VMEM((hpd, nb // 2, 8, 2 * tok), F32),
            pltpu.VMEM((hpd, 3, 2 * tok, 2 * tok), F32),
            pltpu.VMEM((hpd, tok, 128), F32),
            pltpu.VMEM((hpd, tok, 128), F32),
            pltpu.VMEM((hpd, tok, 128), F32),
            pltpu.VMEM((nb, seqs, tok, lanes), BF16),
            dma((seqs, 2, nb)),
            dma((seqs, 2, nb)),
            dma((seqs, nb)),
            dma((seqs, nb)),
            dma((seqs,)),
        ],
        compiler_params=params(collective_id=2, has_side_effects=True),
        name="attn_fwd",
    )(span, slopes, qkv)


def attn_bwd_kernel(
    span_ref, slope_ref, qkv_in, do_src, o32_in, lse_in, got,
    qkv_ref, o32_ref, lse_ref, sem_in, do_got, out, qa, ka, kt, va, qm, da, dm, dqt, corr, qbase, kbase, kfar, dk_ref, dv_ref,
    ss, sr, gs, gr, loc, *, hpd, nd
):
    nb, _, seqs, tok, lanes = qkv_ref.shape
    inputs = [
        pltpu.make_async_copy(qkv_in, qkv_ref, sem_in.at[0]),
        pltpu.make_async_copy(lse_in, lse_ref, sem_in.at[1]),
        pltpu.make_async_copy(o32_in, o32_ref, sem_in.at[2]),
    ]
    for copy in inputs:
        copy.start()
    size = lanes // hpd
    unit = size ** (-0.5)
    g = lax.axis_index("grp")
    d = lax.axis_index("dev")

    def own_copy(q):
        return pltpu.make_async_copy(do_src.at[d, q], do_got.at[d, q], loc.at[q])

    for q in range(seqs):
        own_copy(q).start()
    greet_plane(g, d, nd)

    def send(q, p):
        to = lax.rem(d + p, nd)
        return remote(do_src.at[to, q], do_got.at[d, q], ss.at[q, p], sr.at[q, p], (g, to))

    def send_all(q):
        @pl.loop(1, nd)
        def _(p):
            send(q, p).start()

    send_all(0)

    def place_back(kind, source, q):
        return landing(got, kind, source, q, tok, lanes, 3)

    def back(q, kind, p):
        to = lax.rem(d + p, nd)
        return remote(
            out.at[to, kind, q], place_back(kind, d, q), gs.at[q, kind, p], gr.at[q, kind, p], (g, to)
        )

    def back_own(q, kind):
        return pltpu.make_async_copy(out.at[d, kind, q], place_back(kind, d, q), gs.at[q, kind, 0])

    for h in range(hpd):
        mask, span = far_side(slope_ref[h] * LOG2E, tok)
        for n, table in enumerate((mask, span)):
            corr[h, n, :, 0:tok] = table
            corr[h, n, :, tok:] = jnp.zeros((tok, tok), F32)
    column_tables(slope_ref, qbase, kbase, kfar, hpd, lanes)
    row = lax.broadcasted_iota(jnp.int32, (lanes, lanes), 0) // size
    col = lax.broadcasted_iota(jnp.int32, (lanes, lanes), 1) // size
    across = (row == hpd - 1 - col).astype(F32).astype(BF16)
    for copy in inputs:
        copy.wait()

    @pl.loop(0, seqs)
    def _(q):
        @pl.loop(0, nb)
        def _(j):
            at_j = pl.ds(pl.multiple_of(j * tok, tok), tok)
            qj = qkv_ref[j, 0, q]
            kj = qkv_ref[j, 1, q]
            vj = qkv_ref[j, 2, q].astype(F32)
            kt[:, at_j] = kj.astype(F32).T.astype(BF16)
            dqt[:, at_j] = jnp.zeros((lanes, tok), F32)
            block = jnp.full((tok, 128), j, jnp.int32).astype(F32)
            low = [-p for p in parts3(lse_ref[j, q])]
            for h in range(hpd):
                qa[h, at_j, :] = q_columns(qj, h, hpd, qbase[h], low)
                ka[h, j] = k_columns(kj, h, hpd, kbase[h] + block * kfar[h])
                if hpd > 1:
                    own = own_lanes(h, (tok, lanes), hpd, lanes)
                    qm[h, at_j, :] = jnp.where(own, qj.astype(F32), 0.0).astype(BF16)
                    va[h, j] = jnp.where(own, vj, kbase[h]).astype(BF16)
                else:
                    qm[h, at_j, :] = qj
                    va[h, j] = jnp.concatenate([vj, kbase[h][:, 0:lanes]], axis=1).astype(BF16)

        own_copy(q).wait()

        @pl.loop(1, nd)
        def _(p):
            arrived(do_got.at[lax.rem(d + nd - p, nd), q], sr.at[q, p])

        @pl.when(q + 1 < seqs)
        def _():
            send_all(q + 1)

        @pl.loop(0, nb)
        def _(j):
            at_j = pl.ds(pl.multiple_of(j * tok, tok), tok)
            do = do_got[j, q].astype(F32)
            delta = jnp.zeros((tok, lanes), F32)
            for p in parts3(do * o32_ref[j, q]):
                delta = delta + dot_nn(p.astype(BF16), across)
            low = [-p for p in parts3(delta)]
            for h in range(hpd):
                if hpd > 1:
                    own = own_lanes(h, (tok, lanes), hpd, lanes)
                    none = jnp.where(own, do, 0.0)
                    da[h, at_j, :] = extra_lanes(none, low, h, hpd, lanes).astype(BF16)
                    dm[h, at_j, :] = none.astype(BF16)
                else:
                    extra = extra_lanes(jnp.zeros((tok, lanes), F32), low, h, hpd, lanes)
                    da[h, at_j, :] = jnp.concatenate([do, extra], axis=1).astype(BF16)
                    dm[h, at_j, :] = do.astype(BF16)

        start = span_ref[q]

        @pl.loop(0, nb)
        def _(n):
            j = lax.rem(d + n, nb)
            at_j = pl.ds(pl.multiple_of(j * tok, tok), tok)
            flag = (start == j * tok).astype(jnp.int32)

            def tile(i, width, near):
                at_i = slice(i * tok, i * tok + width)
                dk = None
                for h in range(hpd):
                    s = dot_nt(ka[h, j], qa[h, at_i, :])
                    if near:
                        s = s + corr[h, flag, :, 0:width]
                    p = jnp.exp2(s)
                    ds = (p * dot_nt(va[h, j], da[h, at_i, :])).astype(BF16)
                    dv_h = dot_nn(p.astype(BF16), dm[h, at_i, :])
                    dk_h = dot_nn(ds, qm[h, at_i, :])
                    dk = dk_h if dk is None else dk + dk_h
                    dv = dv_h if h == 0 else dv + dv_h
                    rows = slice(h * size, (h + 1) * size)
                    dqt[rows, at_i] += dot_nn(kt[rows, at_j], ds)
                return dk, dv

            for case in range(nb):
                @pl.when(j == case)
                def _():
                    odd = (nb - case) % 2
                    sums = tile(case, tok if odd else 2 * tok, True)
                    for i in range(case + 2 - odd, nb, 2):
                        more = tile(i, 2 * tok, False)
                        sums = [a + b for a, b in zip(sums, more)]
                    dk_ref[...], dv_ref[...] = sums

            out[j, 1, q] = (dk_ref[...] * unit).astype(BF16)
            out[j, 2, q] = dv_ref[...].astype(BF16)

            for kind in (1, 2):
                @pl.when(n == 0)
                def _():
                    back_own(q, kind).start()

                @pl.when(n > 0)
                def _():
                    back(q, kind, n).start()

        @pl.loop(0, nb)
        def _(n):
            j = lax.rem(d + n, nb)
            at_j = pl.ds(pl.multiple_of(j * tok, tok), tok)
            out[j, 0, q] = (dqt[:, at_j].T * unit).astype(BF16)

            @pl.when(n == 0)
            def _():
                back_own(q, 0).start()

            @pl.when(n > 0)
            def _():
                back(q, 0, n).start()

    for q in range(seqs):
        for kind in range(3):
            back_own(q, kind).wait()

        @pl.loop(1, nd)
        def _(p):
            send(q, p).wait_send()
            source = lax.rem(d + nd - p, nd)
            for kind in range(3):
                back(q, kind, p).wait_send()
                arrived(place_back(kind, source, q), gr.at[q, kind, p])


def run_attn_bwd(span, slopes, qkv, do, o32, lse, hpd):
    nb, _, seqs, tok, lanes = qkv.shape
    t = nb * tok
    dma = pltpu.SemaphoreType.DMA
    wide = 128 if hpd == 1 else lanes
    return pl.pallas_call(
        functools.partial(attn_bwd_kernel, hpd=hpd, nd=nb),
        out_shape=landing_shape(3, nb, seqs, tok, lanes),
        in_specs=[smem(), smem(), hbm(), hbm(), hbm(), hbm()],
        out_specs=vmem(),
        scratch_shapes=[
            pltpu.VMEM(qkv.shape, BF16),
            pltpu.VMEM(o32.shape, F32),
            pltpu.VMEM(lse.shape, F32),
            dma((3,)),
            pltpu.VMEM((nb, seqs, tok, lanes), BF16),
            pltpu.VMEM(qkv.shape, BF16),
            pltpu.VMEM((hpd, t, 256), BF16),
            pltpu.VMEM((hpd, nb, tok, 256), BF16),
            pltpu.VMEM((lanes, t), BF16),
            pltpu.VMEM((hpd, nb, tok, wide), BF16),
            pltpu.VMEM((hpd, t, lanes), BF16),
            pltpu.VMEM((hpd, t, wide), BF16),
            pltpu.VMEM((hpd, t, lanes), BF16),
            pltpu.VMEM((lanes, t), F32),
            pltpu.VMEM((hpd, 2, tok, 2 * tok), F32),
            pltpu.VMEM((hpd, tok, 128), F32),
            pltpu.VMEM((hpd, tok, 128), F32),
            pltpu.VMEM((hpd, tok, 128), F32),
            pltpu.VMEM((tok, lanes), F32),
            pltpu.VMEM((tok, lanes), F32),
            dma((seqs, nb)),
            dma((seqs, nb)),
            dma((seqs, 3, nb)),
            dma((seqs, 3, nb)),
            dma((seqs,)),
        ],
        compiler_params=params(collective_id=3, has_side_effects=True),
        name="attn_bwd",
    )(span, slopes, qkv, do, o32, lse)


def mlp_kernel(
    slot_ref, att_in, x_in, dy_in, vec_ref, gath,
    act_out, dx1_out, do_out, sums_ref, grads,
    att_ref, x_ref, dy_ref, sem_in, wo, wup, wdn, x1, acc, dh2, h2_ref, h2t, attt, da_ref, act_ref, dx1_ref, g_ref, dz_ref, do_ref, stage,
    sem_o, sem_t, sem_g, sem_w, *, nd, first_o, first_up, first_dn, tile
):
    rows, width = x_ref.shape
    side = gath.shape[1]
    per = width // side
    tiles = wup.shape[0]
    ff = tiles * tile
    cols = tile // side
    lanes = do_ref.shape[2]
    fper = ff // side
    inputs = [
        pltpu.make_async_copy(att_in, att_ref, sem_in.at[0]),
        pltpu.make_async_copy(x_in, x_ref, sem_in.at[1]),
        pltpu.make_async_copy(dy_in, dy_ref, sem_in.at[2]),
    ]
    for copy in inputs:
        copy.start()

    for i in range(per):
        for j in range(per):
            fetch_block(gath, slot_at(slot_ref, first_o + i * per + j), wo, i * side, j * side, sem_o.at[0], side).start()

    def fetch_tile(f):
        for i in range(per):
            for j in range(cols):
                fetch_block(gath, slot_at(slot_ref, first_up + i * fper + f * cols + j), wup.at[f], i * side, j * side, sem_t.at[f], side).start()
            for j in range(cols):
                fetch_block(gath, slot_at(slot_ref, first_dn + (f * cols + j) * per + i), wdn.at[f], j * side, i * side, sem_t.at[f], side).start()

    fetch_tile(0)
    fetch_tile(1)
    for copy in inputs:
        copy.wait()
    for r in range(width // 256):
        attt[r * 256:(r + 1) * 256, :] = turn(att_ref[:, r * 256:(r + 1) * 256])
    pltpu.make_async_copy(wo, wo, sem_o.at[0]).wait()
    for half in range(2):
        c = slice(half * width // 2, (half + 1) * width // 2)
        x1[:, c] = x_ref[:, c].astype(F32) + dot_nn(att_ref[...], wo[:, c]) + vec_ref[BO:BO + 1, c]

    chunk = 128

    def rows_at(r):
        return pl.ds(pl.multiple_of(r * chunk, chunk), chunk)

    @pl.loop(0, rows // chunk)
    def _(r):
        at = rows_at(r)
        centred, inv = layer_stats(x1[at, :])
        h2_ref[at, :] = (centred * inv * vec_ref[GAIN2:GAIN2 + 1, :] + vec_ref[SHIFT2:SHIFT2 + 1, :]).astype(BF16)
        acc[at, :] = x1[at, :] + vec_ref[BDOWN:BDOWN + 1, :]
        dh2[at, :] = jnp.zeros((chunk, width), F32)

    for r in range(width // 256):
        h2t[r * 256:(r + 1) * 256, :] = turn(h2_ref[:, r * 256:(r + 1) * 256])

    def put(slot, first, res, down, across):
        for i in range(down):
            for j in range(across):
                stage[slot, first + i * across + j] = res[i * side:(i + 1) * side, j * side:(j + 1) * side]

    def leave(slot, n, block):
        pltpu.make_async_copy(stage.at[slot, n], grads.at[slot_at(slot_ref, block)], sem_g.at[slot]).start()

    def left(slot, size):
        at = stage.at[slot, pl.ds(0, size)]
        pltpu.make_async_copy(at, at, sem_g.at[slot]).wait()

    full = 2 * per * cols
    piece = 512

    @pl.loop(0, tiles)
    def _(f):
        @pl.when(f + 2 < tiles)
        def _():
            fetch_tile(f + 2)
        pltpu.make_async_copy(wup.at[f], wup.at[f], sem_t.at[f]).wait()
        pltpu.make_async_copy(wdn.at[f], wdn.at[f], sem_t.at[f]).wait()
        for k in range(tile // piece):
            c = slice(k * piece, (k + 1) * piece)
            z = dot_nn(h2_ref[...], wup[f, :, c]) + vec_ref[pl.ds(BUP + f, 1), c]
            dg = dot_nt(dy_ref[...], wdn[f, c, :])
            z2 = z * z
            th = jnp.tanh(z * (0.7978845608028654 + (0.7978845608028654 * 0.044715) * z2))
            half_more = 0.5 + 0.5 * th
            g_ref[:, c] = (z * half_more).astype(BF16)
            slope = half_more + (0.5 * z) * (1.0 - th * th) * (
                0.7978845608028654 + (3.0 * 0.044715 * 0.7978845608028654) * z2
            )
            dz = (dg * slope).astype(BF16)
            dz_ref[:, c] = dz
            sums_ref[pl.ds(pl.multiple_of(8 * (4 + f), 8), 8), c] = fold_rows(dz.astype(F32))
        for k in range(width // piece):
            c = slice(k * piece, (k + 1) * piece)
            acc[:, c] += dot_nn(g_ref[...], wdn[f, :, c])
            dh2[:, c] += dot_nt(dz_ref[...], wup[f, c, :])
        slot = lax.rem(f, 2)

        @pl.when(f >= 2)
        def _():
            left(slot, full)
        per_piece = piece // side
        for k in range(tile // piece):
            c = slice(k * piece, (k + 1) * piece)
            res = dot_nn(turn(g_ref[:, c]), dy_ref[...]).astype(BF16)
            put(slot, k * per_piece * per, res, per_piece, per)
        for k in range(width // piece):
            res = dot_nn(h2t[k * piece:(k + 1) * piece, :], dz_ref[...]).astype(BF16)
            put(slot, per * cols + k * per_piece * cols, res, per_piece, cols)
        for i in range(per):
            for j in range(cols):
                leave(slot, j * per + i, first_dn + (f * cols + j) * per + i)
            for j in range(cols):
                leave(slot, per * cols + i * cols + j, first_up + i * fper + f * cols + j)

    zero = jnp.zeros((8, width), F32)

    def finish(r, carry):
        s_bo, s_gain, s_shift, s_bdown = carry
        at = rows_at(r)
        act_ref[at, :] = acc[at, :].astype(BF16)
        centred, inv = layer_stats(x1[at, :])
        hat = centred * inv
        dh = dh2[at, :]
        dhg = dh * vec_ref[GAIN2:GAIN2 + 1, :]
        back = inv * (
            dhg
            - jnp.mean(dhg, axis=-1, keepdims=True)
            - hat * jnp.mean(dhg * hat, axis=-1, keepdims=True)
        )
        dy = dy_ref[at, :].astype(F32)
        dx1 = dy + back
        dx1_ref[at, :] = dx1
        da = dx1.astype(BF16)
        da_ref[at, :] = da
        return (
            s_bo + fold_rows(da.astype(F32)),
            s_gain + fold_rows(dh * hat),
            s_shift + fold_rows(dh),
            s_bdown + fold_rows(dy),
        )

    carry = lax.fori_loop(0, rows // chunk, finish, (zero, zero, zero, zero))
    for n in range(4):
        sums_ref[8 * n:8 * n + 8, :] = carry[n]
    outs = [
        pltpu.make_async_copy(act_ref, act_out, sem_w.at[0]),
        pltpu.make_async_copy(dx1_ref, dx1_out, sem_w.at[1]),
        pltpu.make_async_copy(do_ref, do_out, sem_w.at[2]),
    ]
    outs[0].start()
    outs[1].start()
    for half in range(2):
        c = slice(half * width // 2, (half + 1) * width // 2)
        res = dot_nt(da_ref[...], wo[c, :]).astype(BF16)
        for d in range(nd // 2):
            do_ref[half * (nd // 2) + d] = res[:, d * lanes:(d + 1) * lanes]
    outs[2].start()
    left(0, full)
    left(1, full)
    half_rows = width // 2
    for half in range(2):
        res = dot_nn(attt[half * half_rows:(half + 1) * half_rows, :], da_ref[...]).astype(BF16)
        put(half, 0, res, per // 2, per)

        for i in range(per // 2):
            for j in range(per):
                leave(half, i * per + j, first_o + (half * (per // 2) + i) * per + j)
    for half in range(2):
        left(half, per * per // 2)
    for copy in outs:
        copy.wait()


def run_mlp(slot_of, att, x, dy, vec, gath, nd):
    rows, width = x.shape
    side = gath.shape[1]
    lanes = width // nd
    per = width // side
    first_o = 3 * per * per
    first_up = first_o + per * per
    first_dn = first_up + per * (FF // side)
    tile = width
    f32_rows = pltpu.VMEM((rows, width), F32)
    bf16_rows = pltpu.VMEM((rows, width), BF16)
    turned = pltpu.VMEM((width, rows), BF16)
    return pl.pallas_call(
        functools.partial(
            mlp_kernel, nd=nd, first_o=first_o, first_up=first_up, first_dn=first_dn, tile=tile
        ),
        out_shape=(
            sds((rows, width), BF16),
            sds((rows, width), F32),
            sds((nd, rows, lanes), BF16),
            sds((8 * (4 + FF // width), width), F32),
            sds(gath.shape, BF16),
        ),
        in_specs=[smem(), hbm(), hbm(), hbm(), vmem(), hbm()],
        out_specs=(hbm(), hbm(), hbm(), vmem(), hbm()),
        scratch_shapes=[
            bf16_rows,
            bf16_rows,
            bf16_rows,
            pltpu.SemaphoreType.DMA((3,)),
            pltpu.VMEM((width, width), BF16),
            pltpu.VMEM((FF // tile, width, tile), BF16),
            pltpu.VMEM((FF // tile, tile, width), BF16),
            f32_rows,
            f32_rows,
            f32_rows,
            bf16_rows,
            turned,
            turned,
            bf16_rows,
            bf16_rows,
            f32_rows,
            bf16_rows,
            bf16_rows,
            pltpu.VMEM((nd, rows, lanes), BF16),
            pltpu.VMEM((2, 2 * per * (tile // side), side, side), BF16),
            pltpu.SemaphoreType.DMA((1,)),
            pltpu.SemaphoreType.DMA((FF // tile,)),
            pltpu.SemaphoreType.DMA((2,)),
            pltpu.SemaphoreType.DMA((3,)),
        ],
        compiler_params=params(),
        name="mlp",
    )(slot_of, att, x, dy, vec, gath)


def dh1_dot(cat, w, dh1, part, half):
    width = dh1.shape[1]
    c = slice(half * width // 2, (half + 1) * width // 2)
    res = dot_nt(cat[:, part * width:(part + 1) * width], w[part, c, :])
    if part == 0:
        dh1[:, c] = res
    else:
        dh1[:, c] += res


def first_norm_back(cat, x, dh1, dx1, ig, vec_ref):
    rows, width = x.shape
    chunk = 128
    zero = jnp.zeros((8, width), F32)

    def finish(r, carry):
        s_gain, s_shift, s_bq, s_bv = carry
        at = pl.ds(pl.multiple_of(r * chunk, chunk), chunk)
        centred, inv = layer_stats(x[at, :].astype(F32))
        hat = centred * inv
        dh = dh1[at, :]
        dhg = dh * vec_ref[GAIN1:GAIN1 + 1, :]
        back = inv * (
            dhg
            - jnp.mean(dhg, axis=-1, keepdims=True)
            - hat * jnp.mean(dhg * hat, axis=-1, keepdims=True)
        )
        ig[at, :] = dx1[at, :] + back
        return (
            s_gain + fold_rows(dh * hat),
            s_shift + fold_rows(dh),
            s_bq + fold_rows(cat[at, 0:width].astype(F32)),
            s_bv + fold_rows(cat[at, 2 * width:3 * width].astype(F32)),
        )

    return lax.fori_loop(0, rows // chunk, finish, (zero, zero, zero, zero))


def vector_rows(first, sums2):
    rows = [jnp.sum(v, axis=0, keepdims=True) for v in first]
    rows += [jnp.sum(sums2[8 * n:8 * n + 8, :], axis=0, keepdims=True) for n in range(sums2.shape[0] // 8)]
    return rows


def dh1_kernel(cat_ref, x_ref, dx1_ref, vec_ref, wq_ref, sums2_ref, ig_ref, vsum_ref, dh1):
    for part in range(3):
        for half in range(2):
            dh1_dot(cat_ref, wq_ref, dh1, part, half)
    first = first_norm_back(cat_ref, x_ref, dh1, dx1_ref, ig_ref, vec_ref)
    for n, row in enumerate(vector_rows(first, sums2_ref)):
        vsum_ref[n:n + 1, :] = row


def run_dh1(cat, x, dx1, vec, wq, sums2):
    rows, width = x.shape
    return pl.pallas_call(
        dh1_kernel,
        out_shape=(sds((rows, width), F32), sds(vec.shape, F32)),
        in_specs=[vmem()] * 6,
        out_specs=(vmem(), vmem()),
        scratch_shapes=[pltpu.VMEM((rows, width), F32)],
        compiler_params=params(),
        name="dh1",
    )(cat, x, dx1, vec, wq, sums2)


def wgrad_kernel(slot_ref, h1_ref, cat_ref, rest, out, a_t, stage, sem_out, *, side, tile):
    del rest
    rows, width = h1_ref.shape
    per = width // side
    cols = tile // side
    steps = cat_ref.shape[1] // tile
    for r in range(width // 256):
        c = slice(r * 256, (r + 1) * 256)
        a_t[c, :] = turn(h1_ref[:, c])

    def left(slot):
        pltpu.make_async_copy(stage.at[slot], stage.at[slot], sem_out.at[slot]).wait()

    @pl.loop(0, steps)
    def _(t):
        slot = lax.rem(t, 2)

        @pl.when(t >= 2)
        def _():
            left(slot)
        res = dot_nn(a_t[...], cat_ref[:, pl.ds(pl.multiple_of(t * tile, tile), tile)]).astype(BF16)
        for i in range(per):
            for j in range(cols):
                stage[slot, i * cols + j] = res[i * side:(i + 1) * side, j * side:(j + 1) * side]

        for i in range(per):
            for j in range(cols):
                dst = slot_at(slot_ref, i * 3 * per + t * cols + j)
                pltpu.make_async_copy(stage.at[slot, i * cols + j], out.at[dst], sem_out.at[slot]).start()

    left(0)
    left(1)


def run_wgrad(slot_of, h1, cat, grads):
    rows, width = h1.shape
    side = grads.shape[1]
    tile = 512
    return pl.pallas_call(
        functools.partial(wgrad_kernel, side=side, tile=tile),
        out_shape=sds(grads.shape, BF16),
        in_specs=[smem(), vmem(), vmem(), hbm()],
        out_specs=hbm(),
        scratch_shapes=[
            pltpu.VMEM((width, rows), BF16),
            pltpu.VMEM((2, (width // side) * (tile // side), side, side), BF16),
            pltpu.SemaphoreType.DMA((2,)),
        ],
        input_output_aliases={3: 0},
        compiler_params=params(),
        name="wgrad",
    )(slot_of, h1, cat, grads)


def whereami():
    g = lax.axis_index("grp")
    d = lax.axis_index("dev")
    core = lax.rem(d, 2)
    x = lax.rem(d // 2, 2)
    y = d // 4
    over_x = d + 2 - 4 * x
    over_y = d + 4 - 8 * y
    across = over_x + 4 - 8 * y
    sibling = d + 1 - 2 * core
    return g, d, over_x, over_y, across, sibling


def near_order(t, g, ng):
    t = ng - 1 - t
    low = jnp.where(t < ng - 1 - g, ng - 1 - t, t - (ng - 1 - g))
    high = jnp.where(t < g, t, ng - 1 - (t - g))
    return jnp.where(2 * g < ng, low, high)


def greet(g, ng, peers):
    barrier = pltpu.get_barrier_semaphore()
    for peer in peers:
        pl.semaphore_signal(barrier, inc=1, device_id=(g, peer), device_id_type=MESH)

    d = lax.axis_index("dev")

    @pl.when(g > 0)
    def _():
        pl.semaphore_signal(barrier, inc=1, device_id=(g - 1, d), device_id_type=MESH)

    @pl.when(g < ng - 1)
    def _():
        pl.semaphore_signal(barrier, inc=1, device_id=(g + 1, d), device_id_type=MESH)

    ends = (g > 0).astype(jnp.int32) + (g < ng - 1).astype(jnp.int32)
    pl.semaphore_wait(barrier, len(peers) + ends)


def slot_cuts(count):
    third = 2 * (count // 12)
    first = (count - third) // 2
    return first, count - third - first, third // 2, third // 2


def gather_kernel(
    w_ref, x_ref, block_ref, vin_ref, out, h1_ref, slot_ref, vec_ref,
    own, local_sem, zs, zr, cs, cr, ss, sr, *, ng, nd
):
    count = w_ref.shape[0]
    na, nb, nc1, nc2 = slot_cuts(count)
    flat = na + nb
    nc = nc1 + nc2
    g, d, over_x, over_y, across, sibling = whereami()
    columns = (d, over_x, over_y, across)
    own[...] = w_ref[...].astype(BF16)
    greet(g, ng, (over_x, over_y, sibling))

    def region(gz, dev, first=0, size=count):
        return out.at[pl.ds((gz * nd + dev) * count + first, size)]

    def wide(t):
        return count if t == 0 else flat

    def kind(n, t):
        return (
            (d, 0, wide(t), over_x),
            (d, 0, wide(t), over_y),
            (d, 0, wide(t), sibling),
            (over_x, 0, na, over_y),
            (over_y, na, nb, over_x),
            (over_x, 0, wide(t), sibling),
            (over_y, 0, wide(t), sibling),
            (across, 0, na, sibling),
            (across, na, nb, sibling),
            (over_x, flat, nc1, over_y),
            (over_y, flat + nc1, nc2, over_x),
            (across, flat, nc1, sibling),
            (across, flat + nc1, nc2, sibling),
            (d, flat, nc, sibling),
            (over_x, flat, nc, sibling),
            (over_y, flat, nc, sibling),
            (across, flat, nc, sibling),
        )[n]

    def kinds(t):
        return range(13) if t == 0 else tuple(range(9)) + tuple(range(13, 17))

    def plane(n, t, src=None):
        gz = near_order(t, g, ng)
        dev, first, size, to = kind(n, t)
        at = region(gz, dev, first, size)
        return remote(at if src is None else src, at, ss.at[n, gz], sr.at[n, gz], (g, to))

    def landed(n, t, dev):
        gz = near_order(t, g, ng)
        _, first, size, _ = kind(n, t)
        arrived(region(gz, dev, first, size), sr.at[n, gz])

    def line(gz, up, src=None):
        at = region(gz, d, 0, flat)
        to = g + 1 if up else g - 1
        return remote(at if src is None else src, at, zs.at[gz, int(up)], zr.at[gz], (to, d))

    def corner_line(gz, c, up, src=None):
        at = region(gz, columns[c], flat, nc)
        to = g + 1 if up else g - 1
        return remote(at if src is None else src, at, cs.at[gz, c, int(up)], cr.at[gz, c], (to, d))

    def both_ways(gz, make):
        @pl.when((gz <= g) & (g < ng - 1))
        def _():
            make(True)

        @pl.when((gz >= g) & (g > 0))
        def _():
            make(False)

    mine = pltpu.make_async_copy(own, region(g, d), local_sem.at[0])
    mine.start()

    def column(t):
        gz = near_order(t, g, ng)
        if t == 0:
            both_ways(gz, lambda up: line(gz, up, cut(own, 0, flat)).start())
            for n in range(3):
                plane(n, t, own).start()
            both_ways(gz, lambda up: corner_line(gz, 0, up, cut(own, flat, nc)).start())
            return
        arrived(region(gz, d, 0, flat), zr.at[gz])
        both_ways(gz, lambda up: line(gz, up).start())
        for n in range(3):
            plane(n, t).start()

    def sides(t):
        gz = near_order(t, g, ng)
        landed(0, t, over_x)
        plane(3, t).start()
        if t == 0:
            plane(9, t).start()
            both_ways(gz, lambda up: corner_line(gz, 1, up).start())
        plane(5, t).start()
        landed(1, t, over_y)
        plane(4, t).start()
        if t == 0:
            plane(10, t).start()
            both_ways(gz, lambda up: corner_line(gz, 2, up).start())
        plane(6, t).start()

    def corner(t):
        gz = near_order(t, g, ng)
        if t == 0:
            landed(9, t, across)
            landed(10, t, across)
            both_ways(gz, lambda up: corner_line(gz, 3, up).start())
            plane(11, t).start()
            plane(12, t).start()
        landed(3, t, across)
        plane(7, t).start()
        landed(4, t, across)
        plane(8, t).start()

    def far_corner(t):
        gz = near_order(t, g, ng)
        for c in range(4):
            arrived(region(gz, columns[c], flat, nc), cr.at[gz, c])
            both_ways(gz, lambda up: corner_line(gz, c, up).start())
            plane(13 + c, t).start()

    plan = [(t, f) for t in range(ng) for f in (0, 1, 2, 3) if t > 0 or f < 3]
    lag = {0: 0, 1: 1.5, 2: 2.6, 3: 2.2}
    for t, f in sorted(plan, key=lambda e: e[0] * 1.0 + lag[e[1]]):
        (column, sides, corner, far_corner)[f](t)
        if (t, f) == (0, 0):
            prepare(x_ref, block_ref, vin_ref, h1_ref, slot_ref, vec_ref)

    for t in range(ng):
        for n in kinds(t):
            dev, _, _, to = kind(n, t)
            if to is sibling:
                landed(n, t, dev + sibling - d)
    mine.wait()
    for t in range(ng):
        gz = near_order(t, g, ng)
        for n in kinds(t):
            plane(n, t).wait_send()
        both_ways(gz, lambda up: line(gz, up).wait_send())
        for c in range(4):
            both_ways(gz, lambda up: corner_line(gz, c, up).wait_send())


def run_gather(w, x, blocks, vin, ng, nd):
    count, side, _ = w.shape
    dma = pltpu.SemaphoreType.DMA
    return pl.pallas_call(
        functools.partial(gather_kernel, ng=ng, nd=nd),
        out_shape=(sds((ng * nd * count, side, side), BF16),) + prepared_shapes(x, blocks, vin),
        in_specs=[vmem()] * 4,
        out_specs=(hbm(), vmem(), vmem(), vmem()),
        scratch_shapes=[
            pltpu.VMEM((count, side, side), BF16),
            dma((1,)),
            dma((ng, 2)),
            dma((ng,)),
            dma((ng, 4, 2)),
            dma((ng, 4)),
            dma((17, ng)),
            dma((17, ng)),
        ],
        compiler_params=params(collective_id=0, has_side_effects=True),
        name="gather",
    )(w, x, blocks, vin)


def add_blocks(dst, src, size):
    step = 4 if size % 4 == 0 else 2 if size % 2 == 0 else 1

    @pl.loop(0, size // step)
    def _(n):
        for k in range(step):
            dst[n * step + k] = dst[n * step + k] + src[n * step + k]


def scatter_kernel(
    grads, sums2_ref, vec_ref, vin_ref, cat_in, x_in, dx1_in, wq_in, out_ref, vout_ref, vnew_ref, ig_out,
    cat, x, dx1, wq, dh1, sem_in, mine, r0, r1y, r1x, r2x, r2y, rz, cz, cy, cx, cx2, cy2, vwork, vxy, vz,
    load, s0, w0, s1, w1, s2, w2, sz, wz, sc, wc, s3, w3, vs, vw, *, ng, nd, rate
):
    count = out_ref.shape[0]
    na, nb, nc1, nc2 = slot_cuts(count)
    flat = na + nb
    nc = nc1 + nc2
    g, d, over_x, over_y, across, sibling = whereami()
    columns = (d, over_x, over_y, across)

    def region(gz, dev):
        return grads.at[pl.ds((gz * nd + dev) * count, count)]

    def order(t):
        return near_order(ng - 1 - t, g, ng)

    for t in range(ng):
        for c in range(4):
            pltpu.make_async_copy(region(order(t), columns[c]), mine.at[order(t), c], load.at[order(t), c]).start()
    greet(g, ng, (over_x, over_y, sibling))

    def to_sibling(gz, c):
        return remote(
            region(gz, columns[c] + sibling - d), r0.at[gz, c], s0.at[gz, c], w0.at[gz, c], (g, sibling)
        )

    peers = (sibling, over_x, over_y)

    def vec_copy(n):
        return remote(vwork.at[n], vxy.at[n], vs.at[n], vw.at[n], (g, peers[n]))

    for t in range(ng):
        for c in (3, 2, 1, 0):
            to_sibling(order(t), c).start()
    inputs = [
        pltpu.make_async_copy(cat_in, cat, sem_in.at[0]),
        pltpu.make_async_copy(wq_in, wq, sem_in.at[1]),
        pltpu.make_async_copy(x_in, x, sem_in.at[2]),
        pltpu.make_async_copy(dx1_in, dx1, sem_in.at[3]),
    ]
    for copy in inputs:
        copy.start()
    input_grad = pltpu.make_async_copy(dx1, ig_out, sem_in.at[4])

    def first_norm():
        for copy in inputs:
            copy.wait()
        for part in range(3):
            for half in range(2):
                dh1_dot(cat, wq, dh1, part, half)
        first = first_norm_back(cat, x, dh1, dx1, dx1, vec_ref)
        input_grad.start()
        for n, row in enumerate(vector_rows(first, sums2_ref)):
            vwork[0, n:n + 1, :] = row
        vec_copy(0).start()

    first = (
        (2, 0, na, r1y, 0, over_y),
        (3, 0, na, r1y, 1, over_y),
        (1, na, nb, r1x, 0, over_x),
        (3, na, nb, r1x, 1, over_x),
    )
    second = ((1, 0, na, r2x, over_x), (2, na, nb, r2y, over_y))
    third = (
        (2, flat, nc1, cy.at[0], over_y),
        (3, flat, nc1, cy.at[1], over_y),
        (1, flat + nc1, nc2, cx.at[0], over_x),
        (3, flat + nc1, nc2, cx.at[1], over_x),
        (1, flat, nc1, cx2, over_x),
        (2, flat + nc1, nc2, cy2, over_y),
    )

    def copy1(n, gz):
        c, at, size, buf, place_at, to = first[n]
        return remote(cut(mine.at[gz, c], at, size), buf.at[gz, place_at], s1.at[n, gz], w1.at[n, gz], (g, to))

    def copy2(n, gz):
        c, at, size, buf, to = second[n]
        return remote(cut(mine.at[gz, c], at, size), buf.at[gz], s2.at[n, gz], w2.at[n, gz], (g, to))

    def copy3(n):
        c, at, size, buf, to = third[n]
        return remote(cut(mine.at[g, c], at, size), buf, s3.at[n], w3.at[n], (g, to))

    def flat_part(gz):
        return cut(mine.at[gz, 0], 0, flat)

    def corner_part(gz):
        return mine.at[gz, :, pl.ds(flat, nc)]

    def line(gz, part, buf, sends, waits, up):
        at = gz if up else jnp.where(gz < g - 1, gz, ng)
        to = g + 1 if up else g - 1
        return remote(part(gz), buf.at[at], sends.at[gz], waits.at[at], (to, d))

    def pass_on(gz, part, buf, sends, waits, gather):
        @pl.when(gz > g)
        def _():
            @pl.when(g > 0)
            def _():
                arrived(buf.at[gz], waits.at[gz])
                gather(gz)
            line(gz, part, buf, sends, waits, True).start()

        @pl.when(gz < g)
        def _():
            @pl.when(g < ng - 1)
            def _():
                arrived(buf.at[gz], waits.at[gz])
                gather(gz)
            line(gz, part, buf, sends, waits, False).start()

    def gather_flat(gz):
        add_blocks(flat_part(gz), rz.at[gz], flat)

    def gather_corner(at, gz):
        for c in range(4):
            add_blocks(cut(mine.at[gz, c], flat, nc), cz.at[at, c], nc)

    def sums0(t, c):
        gz = order(t)
        pltpu.make_async_copy(region(gz, columns[c]), mine.at[gz, c], load.at[gz, c]).wait()
        arrived(r0.at[gz, c], w0.at[gz, c])
        add_blocks(mine.at[gz, c], r0.at[gz, c], count)
        for n in {3: (1, 3), 2: (0,), 1: (2,), 0: ()}[c]:
            copy1(n, gz).start()

    def along0(t):
        pass_on(order(t), corner_part, cz, sc, wc, lambda gz: gather_corner(gz, gz))

    def stage1(t, k):
        gz = order(t)
        if k == 0:
            arrived(r1y.at[gz, 1], w1.at[1, gz])
            add_blocks(cut(mine.at[gz, 1], 0, na), r1y.at[gz, 1], na)
            copy2(0, gz).start()
            arrived(r1x.at[gz, 1], w1.at[3, gz])
            add_blocks(cut(mine.at[gz, 2], na, nb), r1x.at[gz, 1], nb)
            copy2(1, gz).start()
        else:
            arrived(r1y.at[gz, 0], w1.at[0, gz])
            add_blocks(cut(mine.at[gz, 0], 0, na), r1y.at[gz, 0], na)
            arrived(r1x.at[gz, 0], w1.at[2, gz])
            add_blocks(cut(mine.at[gz, 0], na, nb), r1x.at[gz, 0], nb)

    def stage2(t):
        gz = order(t)
        arrived(r2x.at[gz], w2.at[0, gz])
        add_blocks(cut(mine.at[gz, 0], 0, na), r2x.at[gz], na)
        arrived(r2y.at[gz], w2.at[1, gz])
        add_blocks(cut(mine.at[gz, 0], na, nb), r2y.at[gz], nb)
        if t < ng - 1:
            pass_on(gz, flat_part, rz, sz, wz, gather_flat)

    def corner0():
        @pl.when(g > 0)
        def _():
            arrived(cz.at[g], wc.at[g])
            gather_corner(g, g)

        @pl.when(g < ng - 1)
        def _():
            arrived(cz.at[ng], wc.at[ng])
            gather_corner(ng, g)
        for n in range(4):
            copy3(n).start()

    def corner1():
        arrived(cy.at[1], w3.at[1])
        add_blocks(cut(mine.at[g, 1], flat, nc1), cy.at[1], nc1)
        copy3(4).start()
        arrived(cx.at[1], w3.at[3])
        add_blocks(cut(mine.at[g, 2], flat + nc1, nc2), cx.at[1], nc2)
        copy3(5).start()
        arrived(cy.at[0], w3.at[0])
        add_blocks(cut(mine.at[g, 0], flat, nc1), cy.at[0], nc1)
        arrived(cx.at[0], w3.at[2])
        add_blocks(cut(mine.at[g, 0], flat + nc1, nc2), cx.at[0], nc2)

    def corner2():
        arrived(cx2, w3.at[4])
        add_blocks(cut(mine.at[g, 0], flat, nc1), cx2, nc1)
        arrived(cy2, w3.at[5])
        add_blocks(cut(mine.at[g, 0], flat + nc1, nc2), cy2, nc2)

    def vec_step(n):
        arrived(vxy.at[n], vw.at[n])
        total = vwork[n] + vxy[n]
        if n < 2:
            vwork[n + 1] = total
            vec_copy(n + 1).start()
        else:
            vz[g] = total

    def vec_line(gz, up):
        to = g + 1 if up else g - 1
        return remote(vz.at[gz], vz.at[gz], vs.at[3 + 2 * gz + int(up)], vw.at[3 + gz], (to, d))

    def vec_first_line():
        vec_step(2)

        @pl.when(g < ng - 1)
        def _():
            vec_line(g, True).start()

        @pl.when(g > 0)
        def _():
            vec_line(g, False).start()

    def vec_next_line(n):
        gz = near_order(n, g, ng)
        arrived(vz.at[gz], vw.at[3 + gz])

        @pl.when((gz < g) & (g < ng - 1))
        def _():
            vec_line(gz, True).start()

        @pl.when((gz > g) & (g > 0))
        def _():
            vec_line(gz, False).start()

    def vec_out():
        total = vz[0]
        for z in range(1, ng):
            total = total + vz[z]
        vwork[3] = total
        per = total.shape[1] // 128
        for r in range(total.shape[0]):
            for c in range(per):
                row = vwork[3, r:r + 1, c * 128:(c + 1) * 128]
                n = per * r + c
                vout_ref[n:n + 1, :] = row
                vnew_ref[n:n + 1, :] = vin_ref[n:n + 1, :] - rate * row

    last = ng - 1
    plan = [(t + 0.25 * (3 - c), sums0, (t, c)) for t in range(ng) for c in range(4)]
    plan += [(t + 1.2 + 0.3 * k, stage1, (t, k)) for t in range(ng) for k in range(2)]
    plan += [(t + 2.2, stage2, (t,)) for t in range(ng)]
    plan += [(t + 1.15, along0, (t,)) for t in range(last)]
    plan += [(last + 1.3, corner0, ()), (last + 2.19, corner1, ()), (last + 2.4, corner2, ())]
    plan += [(0.3, first_norm, ()), (0.9, vec_step, (0,)), (2.0, vec_step, (1,)), (3.0, vec_first_line, ())]
    plan += [(3.1 + 0.55 * n, vec_next_line, (n,)) for n in range(1, ng)]
    plan += [(last + 2.17, vec_out, ())]
    for _, step, args in sorted(plan, key=lambda e: e[0]):
        step(*args)

    @pl.when(g > 0)
    def _():
        arrived(rz.at[g], wz.at[g])

    @pl.when(g < ng - 1)
    def _():
        arrived(rz.at[ng], wz.at[ng])

    @pl.when((g > 0) & (g < ng - 1))
    def _():
        @pl.loop(0, flat // 2)
        def _(n):
            for k in range(2):
                i = 2 * n + k
                out_ref[i] = mine[g, 0, i].astype(F32) + rz[g, i].astype(F32) + rz[ng, i].astype(F32)

    @pl.when(g == 0)
    def _():
        @pl.loop(0, flat // 2)
        def _(n):
            for k in range(2):
                i = 2 * n + k
                out_ref[i] = mine[g, 0, i].astype(F32) + rz[ng, i].astype(F32)

    @pl.when((g > 0) & (g == ng - 1))
    def _():
        @pl.loop(0, flat // 2)
        def _(n):
            for k in range(2):
                i = 2 * n + k
                out_ref[i] = mine[g, 0, i].astype(F32) + rz[g, i].astype(F32)

    for i in range(flat, count):
        out_ref[i] = mine[g, 0, i].astype(F32)

    for t in range(ng):
        gz = order(t)
        for c in range(4):
            to_sibling(gz, c).wait_send()
        for n in range(4):
            copy1(n, gz).wait_send()
        for n in range(2):
            copy2(n, gz).wait_send()
        if t < ng - 1:
            arrived(flat_part(gz), sz.at[gz])
            arrived(corner_part(gz), sc.at[gz])
    input_grad.wait()
    for n in range(6):
        copy3(n).wait_send()
    for n in range(3):
        vec_copy(n).wait_send()
    for n in range(ng):
        gz = near_order(n, g, ng)

        @pl.when((gz <= g) & (g < ng - 1))
        def _():
            vec_line(gz, True).wait_send()

        @pl.when((gz >= g) & (g > 0))
        def _():
            vec_line(gz, False).wait_send()


def run_scatter(grads, sums2, vec, vin, cat, x, dx1, wq, ng, nd, rate):
    blocks, side, _ = grads.shape
    count = blocks // (ng * nd)
    na, nb, nc1, nc2 = slot_cuts(count)
    flat = na + nb
    dma = pltpu.SemaphoreType.DMA

    def buf(*lead):
        return pltpu.VMEM(lead + (side, side), BF16)

    def like(v):
        return pltpu.VMEM(v.shape, v.dtype)

    return pl.pallas_call(
        functools.partial(scatter_kernel, ng=ng, nd=nd, rate=rate),
        out_shape=(
            sds((count, side, side), F32),
            sds(vin.shape, F32),
            sds(vin.shape, F32),
            sds(dx1.shape, F32),
        ),
        in_specs=[hbm(), vmem(), vmem(), vmem()] + [hbm()] * 4,
        out_specs=(vmem(), vmem(), vmem(), hbm()),
        scratch_shapes=[
            like(cat),
            like(x),
            like(dx1),
            like(wq),
            like(dx1),
            dma((5,)),
            buf(ng, 4, count),
            buf(ng, 4, count),
            buf(ng, 2, na),
            buf(ng, 2, nb),
            buf(ng, na),
            buf(ng, nb),
            buf(ng + 1, flat),
            buf(ng + 1, 4, nc1 + nc2),
            buf(2, nc1),
            buf(2, nc2),
            buf(nc1),
            buf(nc2),
            pltpu.VMEM((4,) + vec.shape, F32),
            pltpu.VMEM((3,) + vec.shape, F32),
            pltpu.VMEM((ng,) + vec.shape, F32),
            dma((ng, 4)),
            dma((ng, 4)),
            dma((ng, 4)),
            dma((4, ng)),
            dma((4, ng)),
            dma((2, ng)),
            dma((2, ng)),
            dma((ng,)),
            dma((ng + 1,)),
            dma((ng,)),
            dma((ng + 1,)),
            dma((6,)),
            dma((6,)),
            dma((3 + 2 * ng,)),
            dma((3 + ng,)),
        ],
        compiler_params=params(61, collective_id=1, has_side_effects=True),
        name="scatter",
    )(grads, sums2, vec, vin, cat, x, dx1, wq)


def blocks_kernel(*refs, handed):
    g_ref, w_ref, ls_ref, rs_ref, lr_ref, rr_ref = refs[:6]
    wg_out, nl_out, nr_out, nw_out = refs[6 + handed:10 + handed]
    for n in range(handed):
        refs[10 + handed + n][...] = refs[6 + n][...]

    for i in range(g_ref.shape[0]):
        grad = g_ref[i]
        wg_out[i] = grad
        hi = grad.astype(BF16)
        low = (grad - hi.astype(F32)).astype(BF16)
        nl_out[i] = 0.5 * ls_ref[i] + 0.5 * dot_nt(hi, hi)
        turned = grad.T
        hi_t = turned.astype(BF16)
        nr_out[i] = 0.5 * rs_ref[i] + 0.5 * dot_nt(hi_t, hi_t)
        left = lr_ref[i]
        left_hi = left.astype(BF16)
        left_low = (left - left_hi.astype(F32)).astype(BF16)
        shaped = dot_nn(left_hi, hi) + dot_nn(left_hi, low) + dot_nn(left_low, hi)
        right = rr_ref[i]
        right_hi = right.astype(BF16)
        right_low = (right - right_hi.astype(F32)).astype(BF16)
        sh_hi = shaped.astype(BF16)
        sh_low = (shaped - sh_hi.astype(F32)).astype(BF16)
        shaped = dot_nn(sh_hi, right_hi) + dot_nn(sh_low, right_hi) + dot_nn(sh_hi, right_low)
        nw_out[i] = w_ref[i] - weight_rate * shaped


def run_blocks(grads, weights, left_stats, right_stats, left_roots, right_roots, *passing):
    count, side, _ = grads.shape
    steps = math.gcd(count, 4)
    step = count // steps
    spec = pl.BlockSpec((step, side, side), lambda n: (n, 0, 0))
    through = []
    for v in passing:
        part = v.shape[0] // steps
        if part % 8 == 0:
            through.append(pl.BlockSpec((part, v.shape[1]), lambda n: (n, 0)))
        else:
            through.append(pl.BlockSpec(v.shape, lambda n: (0, 0)))
    return pl.pallas_call(
        functools.partial(blocks_kernel, handed=len(passing)),
        grid=(steps,),
        out_shape=tuple([sds(grads.shape, F32)] * 4) + tuple(sds(v.shape, v.dtype) for v in passing),
        in_specs=[spec] * 6 + through,
        out_specs=tuple([spec] * 4) + tuple(through),
        compiler_params=params(),
        name="blocks",
    )(grads, weights, left_stats, right_stats, left_roots, right_roots, *passing)


def local(
    inputs,
    cotangent,
    weight_slots,
    slot_block,
    left_stats,
    right_stats,
    left_roots,
    right_roots,
    vectors,
    span_start,
):
    seq_count, tok_count, width = inputs.shape
    rows = seq_count * tok_count
    nd = lax.axis_size("dev")
    ng = lax.axis_size("grp")
    side = weight_slots.shape[1]
    hpd = H // nd
    lanes = width // nd
    head = lax.axis_index("dev") * hpd + jnp.arange(hpd, dtype=jnp.int32)
    slopes = jnp.exp2(-8.0 * (head.astype(F32) + 1.0) / H)
    vin = vectors.reshape(-1, 128)
    held = slot_block.reshape(-1, 128)
    x = inputs.reshape(rows, width)
    dy = cotangent.reshape(rows, width)
    rate = vector_rate / math.sqrt(rows * nd * ng)

    direct = nd == 8
    if direct:
        gath, h1, slot_of, vec = run_gather(weight_slots, x, held, vin, ng, nd)
    else:
        gath = lax.all_gather(weight_slots.astype(BF16), ("grp", "dev"), axis=0, tiled=True)
        h1, slot_of, vec = run_prepare(x, held, vin)
    qkv, wq = run_qkv(slot_of, h1, vec, gath, nd)
    qkv, o, o32, lse = run_attn_fwd(
        span_start, slopes, qkv.reshape(nd, 3, seq_count, tok_count, lanes), hpd
    )
    att = side_by_side(o, 1, rows)
    act, dx1, do, sums2, grads = run_mlp(slot_of, att, x, dy, vec, gath, nd)
    do = do.reshape(nd, seq_count, tok_count, lanes)
    cat = side_by_side(run_attn_bwd(span_start, slopes, qkv, do, o32, lse, hpd), 3, rows)
    grads = run_wgrad(slot_of, h1, cat, grads)
    if direct:
        weight_grads, vector_grads, new_vectors, ig = run_scatter(
            grads, sums2, vec, vin, cat, x, dx1, wq, ng, nd, rate
        )
        passing = (ig, vector_grads, new_vectors)
    else:
        ig, vsum = run_dh1(cat, x, dx1, vec, wq, sums2)
        vector_grads = lax.psum(vsum.reshape(-1), ("grp", "dev"))
        new_vectors = vectors - rate * vector_grads
        weight_grads = lax.psum_scatter(grads, ("grp", "dev"), scatter_dimension=0, tiled=True)
        weight_grads = weight_grads.astype(F32)
        passing = ()
    weight_grads, new_left, new_right, new_weights, *passed = run_blocks(
        weight_grads, weight_slots, left_stats, right_stats, left_roots, right_roots, *passing
    )
    if direct:
        ig, vector_grads, new_vectors = passed
    return (
        act.reshape(inputs.shape),
        ig.reshape(inputs.shape),
        weight_grads,
        new_left,
        new_right,
        new_weights,
        vector_grads.reshape(-1),
        new_vectors.reshape(-1),
    )


def solution(mesh):
    return jax.shard_map(
        local,
        mesh=mesh,
        in_specs=(
            P("grp", "dev", None),
            P("grp", "dev", None),
            P(("grp", "dev"), None, None),
            P(),
            P(("grp", "dev"), None, None),
            P(("grp", "dev"), None, None),
            P(("grp", "dev"), None, None),
            P(("grp", "dev"), None, None),
            P(),
            P("grp"),
        ),
        out_specs=(
            P("grp", "dev", None),
            P("grp", "dev", None),
            P(("grp", "dev"), None, None),
            P(("grp", "dev"), None, None),
            P(("grp", "dev"), None, None),
            P(("grp", "dev"), None, None),
            P(),
            P(),
        ),
        check_vma=False,
    )
```

```python
import functools
import math

import jax
import jax.numpy as jnp
from jax import lax
from jax.experimental import pallas as pl
from jax.experimental.pallas import tpu as pltpu
from jax.sharding import PartitionSpec as P

H = 16
FF = 4096
PIC = 256

eps = 1e-05
weight_rate = 0.5
vector_rate = 0.5
big_negative = -1e30
highest = lax.Precision.HIGHEST
F32 = jnp.float32
BF16 = jnp.bfloat16
LOG2E = 1.4426950408889634
MIB = 1024 * 1024

GAIN1, SHIFT1, BQ, BV, BO, GAIN2, SHIFT2, BDOWN, BUP = range(9)


def dot_nn(a, b):
    return lax.dot_general(a, b, (((1,), (0,)), ((), ())), preferred_element_type=F32)


def dot_nt(a, b):
    return lax.dot_general(a, b, (((1,), (1,)), ((), ())), preferred_element_type=F32)


def turn(v):
    return v.astype(F32).T.astype(BF16)


def vmem():
    return pl.BlockSpec(memory_space=pltpu.VMEM)


def smem():
    return pl.BlockSpec(memory_space=pltpu.SMEM)


def hbm():
    return pl.BlockSpec(memory_space=pl.ANY)


def sds(shape, dtype):
    return jax.ShapeDtypeStruct(shape, dtype)


def params(mib=58, **kw):
    return pltpu.CompilerParams(vmem_limit_bytes=mib * MIB, **kw)


def layer_stats(v):
    middle = jnp.mean(v, axis=-1, keepdims=True)
    centred = v - middle
    spread = jnp.mean(centred * centred, axis=-1, keepdims=True)
    return centred, lax.rsqrt(spread + eps)


def fold_rows(v):
    return jnp.sum(v.reshape(v.shape[0] // 8, 8, v.shape[1]), axis=0)


def slot_at(slot_ref, block):
    lanes = slot_ref.shape[1]
    if isinstance(block, int):
        return slot_ref[block // lanes, block % lanes]
    return slot_ref[lax.div(block, lanes), lax.rem(block, lanes)]


def fetch_block(gath, slot, dst, row, col, sem, side):
    return pltpu.make_async_copy(
        gath.at[slot], dst.at[pl.ds(row, side), pl.ds(col, side)], sem
    )


def prepare(x_ref, block_ref, vin_ref, h1_ref, slot_ref, vec_ref):
    rows, width = x_ref.shape
    per = width // 128
    for r in range(vec_ref.shape[0]):
        for c in range(per):
            vec_ref[r:r + 1, c * 128:(c + 1) * 128] = vin_ref[per * r + c:per * r + c + 1, :]
    chunk = 128

    @pl.loop(0, rows // chunk)
    def _(r):
        at = pl.ds(pl.multiple_of(r * chunk, chunk), chunk)
        centred, inv = layer_stats(x_ref[at, :].astype(F32))
        h1_ref[at, :] = (
            centred * inv * vec_ref[GAIN1:GAIN1 + 1, :] + vec_ref[SHIFT1:SHIFT1 + 1, :]
        ).astype(BF16)

    tiles, lanes = slot_ref.shape
    line = lax.broadcasted_iota(jnp.int32, (8, lanes), 0)
    lane = lax.broadcasted_iota(jnp.int32, (8, lanes), 1).astype(F32)
    block = lax.broadcasted_iota(jnp.int32, (lanes, lanes), 0)
    for t in range(tiles):
        found = jnp.zeros((8, lanes), F32)
        for r in range(tiles):
            held = (block_ref[r:r + 1, :] == block + t * lanes).astype(F32).astype(BF16)
            found = found + dot_nt(jnp.where(line == 0, lane, float(r)).astype(BF16), held)
        slot_ref[t:t + 1, :] = (found[0:1] + float(lanes) * found[1:2]).astype(jnp.int32)


def prepared_shapes(x, blocks, vin):
    rows, width = x.shape
    return (
        sds((rows, width), BF16),
        sds(blocks.shape, jnp.int32),
        sds((vin.size // width, width), F32),
    )


def run_prepare(x, blocks, vin):
    return pl.pallas_call(
        prepare,
        out_shape=prepared_shapes(x, blocks, vin),
        in_specs=[vmem()] * 3,
        out_specs=tuple([vmem()] * 3),
        compiler_params=params(),
        name="prepare",
    )(x, blocks, vin)


def qkv_kernel(slot_ref, h1_ref, vec_ref, gath, out_ref, wq_out, wbuf, sems, sem_w, *, nd):
    rows, width = h1_ref.shape
    side = gath.shape[1]
    per = width // side
    lanes = out_ref.shape[3]
    for part in range(3):
        for i in range(per):
            for j in range(per):
                slot = slot_at(slot_ref, i * 3 * per + part * per + j)
                fetch_block(gath, slot, wbuf.at[part], i * side, j * side, sems.at[part], side).start()

    def keep(part):
        return pltpu.make_async_copy(wbuf.at[part], wq_out.at[part], sem_w.at[part])

    for part in range(3):
        pltpu.make_async_copy(wbuf.at[part], wbuf.at[part], sems.at[part]).wait()
        keep(part).start()
        for half in range(2):
            cols = slice(half * width // 2, (half + 1) * width // 2)
            res = dot_nn(h1_ref[...], wbuf[part, :, cols])
            if part == 0:
                res = res + vec_ref[BQ:BQ + 1, cols]
            if part == 2:
                res = res + vec_ref[BV:BV + 1, cols]
            res = res.astype(BF16)
            for d in range(nd // 2):
                out_ref[half * (nd // 2) + d, part, :, :] = res[:, d * lanes:(d + 1) * lanes]
    for part in range(3):
        keep(part).wait()


def run_qkv(slot_of, h1, vec, gath, nd):
    rows, width = h1.shape
    lanes = width // nd
    return pl.pallas_call(
        functools.partial(qkv_kernel, nd=nd),
        out_shape=(sds((nd, 3, rows, lanes), BF16), sds((3, width, width), BF16)),
        in_specs=[smem(), vmem(), vmem(), hbm()],
        out_specs=(vmem(), hbm()),
        scratch_shapes=[
            pltpu.VMEM((3, width, width), BF16),
            pltpu.SemaphoreType.DMA((3,)),
            pltpu.SemaphoreType.DMA((3,)),
        ],
        compiler_params=params(),
        name="qkv",
    )(slot_of, h1, vec, gath)


MESH = pl.DeviceIdType.MESH


def remote(src, dst, send, recv, device):
    return pltpu.make_async_remote_copy(
        src_ref=src, dst_ref=dst, send_sem=send, recv_sem=recv, device_id=device, device_id_type=MESH
    )


def arrived(ref, sem):
    pltpu.make_async_copy(ref, ref, sem).wait()


def cut(ref, first, size):
    return ref.at[pl.ds(first, size)]


def greet_plane(g, d, nd):
    barrier = pltpu.get_barrier_semaphore()
    for p in range(1, nd):
        pl.semaphore_signal(barrier, inc=1, device_id=(g, lax.rem(d + p, nd)), device_id_type=MESH)
    pl.semaphore_wait(barrier, nd - 1)


def landing(ref, part, source, q, tok, lanes, parts):
    if lanes % 128 == 0:
        first = (part * (ref.shape[1] // parts)) + source * lanes
        return ref.at[pl.ds(q * tok, tok), pl.ds(pl.multiple_of(first, lanes), lanes)]
    return ref.at[source, part, q]


def landing_shape(parts, nb, seqs, tok, lanes):
    if lanes % 128 == 0:
        return sds((seqs * tok, parts * nb * lanes), BF16)
    return sds((nb, parts, seqs, tok, lanes), BF16)


def side_by_side(got, parts, rows):
    if got.ndim == 2:
        return got
    nb, _, seqs, tok, lanes = got.shape
    return got.transpose(2, 3, 1, 0, 4).reshape(rows, parts * nb * lanes)


def parts3(v):
    hi = v.astype(BF16)
    mid = (v - hi.astype(F32)).astype(BF16)
    lo = (v - hi.astype(F32) - mid.astype(F32)).astype(BF16)
    return hi.astype(F32), mid.astype(F32), lo.astype(F32)


def own_lanes(h, shape, hpd, lanes):
    lane = lax.broadcasted_iota(jnp.int32, shape, 1)
    size = lanes // hpd
    return (lane >= h * size) & (lane < (h + 1) * size)


def place(values, base, tok, width):
    lane = lax.broadcasted_iota(jnp.int32, (tok, width), 1)
    out = jnp.zeros((tok, width), F32)
    for n, v in enumerate(values):
        out = jnp.where(lane == base + n, v, out)
    return out


def spare(h, hpd, lanes):
    return (lanes // hpd) * (1 - h) if hpd > 1 else 0


def column_tables(slope_ref, qbase, kbase, kfar, hpd, lanes):
    _, tok, _ = qbase.shape
    u = lax.broadcasted_iota(jnp.int32, (tok, 128), 0).astype(F32)
    for h in range(hpd):
        slope = slope_ref[h] * LOG2E
        base = spare(h, hpd, lanes)
        near = parts3(jnp.full((tok, 128), slope, F32))
        far = parts3(jnp.full((tok, 128), slope * tok, F32))
        qbase[h] = place(near + far, base, tok, 128)
        kbase[h] = place([u] * 3 + [0.0] * 3 + [1.0] * 3, base, tok, 128)
        kfar[h] = place([0.0] * 3 + [1.0] * 3, base, tok, 128)


def extra_lanes(columns, extra, h, hpd, lanes):
    lane = lax.broadcasted_iota(jnp.int32, columns.shape, 1)
    for n, v in enumerate(extra):
        columns = jnp.where(lane == spare(h, hpd, lanes) + 6 + n, v, columns)
    return columns


def q_columns(q, h, hpd, columns, extra):
    tok, lanes = q.shape
    scaled = q.astype(F32) * ((lanes // hpd) ** (-0.5) * LOG2E)
    hi = scaled.astype(BF16).astype(F32)
    low = scaled - hi
    if extra:
        columns = extra_lanes(columns, extra, h, hpd, lanes)
    if hpd > 1:
        own = own_lanes(h, (tok, lanes), hpd, lanes)
        return jnp.concatenate(
            [jnp.where(own, hi, 0.0), jnp.where(own, low, columns)], axis=1
        ).astype(BF16)
    return jnp.concatenate([hi, low, columns], axis=1).astype(BF16)


def k_columns(k, h, hpd, columns):
    tok, lanes = k.shape
    wide = k.astype(F32)
    if hpd > 1:
        own = own_lanes(h, (tok, lanes), hpd, lanes)
        return jnp.concatenate([wide, jnp.where(own, wide, columns)], axis=1).astype(BF16)
    return jnp.concatenate([wide, wide, columns], axis=1).astype(BF16)


def far_side(slope, tok):
    u = lax.broadcasted_iota(jnp.int32, (tok, tok), 0)
    t = lax.broadcasted_iota(jnp.int32, (tok, tok), 1)
    after = u > t
    return (
        jnp.where(after, big_negative, 0.0),
        jnp.where(after, (2.0 * slope) * (t - u).astype(F32), 0.0),
    )


def pair_tables(corr, h, mask, span):
    tok = mask.shape[0]
    for n, (one, two) in enumerate(((mask, mask), (span, mask), (mask, span))):
        corr[h, n, 0:tok, 0:tok] = one
        corr[h, n, tok:, tok:] = two
        corr[h, n, 0:tok, tok:] = jnp.zeros((tok, tok), F32)
        corr[h, n, tok:, 0:tok] = jnp.full((tok, tok), big_negative, F32)


def attn_fwd_kernel(
    span_ref, slope_ref, src, got_out, o_got, o32_out, lse_out,
    got, o32_ref, lse_ref, sem_w, qa, ka, vt, scores, tops_ref, corr, qbase, kbase, kfar, o_out, ss, sr, os, orr, loc, *, hpd, nd
):
    nb, _, seqs, tok, lanes = got.shape
    size = lanes // hpd
    pair = 2 * tok
    g = lax.axis_index("grp")
    d = lax.axis_index("dev")

    for q in range(seqs):
        pltpu.make_async_copy(src.at[d, :, q], got.at[d, :, q], loc.at[q]).start()
    greet_plane(g, d, nd)

    def kind_of(kind):
        return pl.ds(2 * kind, 2 - kind)

    def send(q, kind, p):
        to = lax.rem(d + p, nd)
        return remote(
            src.at[to, kind_of(kind), q], got.at[d, kind_of(kind), q],
            ss.at[q, kind, p], sr.at[q, kind, p], (g, to),
        )

    def send_all(q, kind):
        @pl.loop(1, nd)
        def _(p):
            send(q, kind, p).start()

    def have(q, kind):
        @pl.loop(1, nd)
        def _(p):
            arrived(got.at[lax.rem(d + nd - p, nd), kind_of(kind), q], sr.at[q, kind, p])

    send_all(0, 0)
    send_all(0, 1)

    def o_place(source, q):
        return landing(o_got, 0, source, q, tok, lanes, 1)

    def send_o(q, i, p):
        return remote(o_out.at[i, q], o_place(d, q), os.at[q, i], orr.at[q, p], (g, i))

    column_tables(slope_ref, qbase, kbase, kfar, hpd, lanes)
    for h in range(hpd):
        mask, span = far_side(slope_ref[h] * LOG2E, tok)
        pair_tables(corr, h, mask, span)

    def fold(v, how):
        return how(v.reshape(v.shape[0] // 8, 8, v.shape[1]), axis=0)

    def write(ref, out, n, q, third=False):
        if third:
            return pltpu.make_async_copy(ref.at[:, :, q], out.at[:, :, q], sem_w.at[n, q])
        return pltpu.make_async_copy(ref.at[:, q], out.at[:, q], sem_w.at[n, q])

    whole = scores.shape[1] > nb // 2

    def tile_at(i, n):
        return (i * (i + 1)) // 2 + n if whole else n

    @pl.loop(0, seqs)
    def _(q):
        pltpu.make_async_copy(src.at[d, :, q], got.at[d, :, q], loc.at[q]).wait()
        start = span_ref[q]

        def score(i):
            flag = (start == i * pair).astype(jnp.int32) + 2 * (start == i * pair + tok).astype(jnp.int32)
            at_i = slice(i * pair, (i + 1) * pair)
            for h in range(hpd):
                top = None
                for n in range(i + 1):
                    s = dot_nt(ka[h, n * pair:(n + 1) * pair, :], qa[h, at_i, :])
                    if n == i:
                        s = s + corr[h, flag]
                    scores[h, tile_at(i, n)] = s
                    here = fold(s, jnp.max)
                    top = here if top is None else jnp.maximum(top, here)
                tops_ref[h, i] = jnp.broadcast_to(jnp.max(top, axis=0, keepdims=True), (8, pair))

        have(q, 0)

        @pl.when(q + 1 < seqs)
        def _():
            send_all(q + 1, 0)

        @pl.loop(0, nb)
        def _(j):
            at_j = pl.ds(pl.multiple_of(j * tok, tok), tok)
            block = jnp.full((tok, 128), j, jnp.int32).astype(F32)
            for h in range(hpd):
                qa[h, at_j, :] = q_columns(got[j, 0, q], h, hpd, qbase[h], [])
                ka[h, at_j, :] = k_columns(got[j, 1, q], h, hpd, kbase[h] + block * kfar[h])

        if whole:
            for i in range(nb // 2):
                score(i)
        have(q, 1)

        @pl.when(q + 1 < seqs)
        def _():
            send_all(q + 1, 1)

        write(got, got_out, 0, q, True).start()

        @pl.loop(0, nb)
        def _(j):
            vt[0:lanes, pl.ds(pl.multiple_of(j * tok, tok), tok)] = turn(got[j, 2, q])

        for i in range(nb // 2):
            if not whole:
                score(i)
            outs = []
            logs = []
            for h in range(hpd):
                acc = total = None
                top = tops_ref[h, i][0:1]
                for n in range(i + 1):
                    p = jnp.exp2(scores[h, tile_at(i, n)] - top)
                    here = fold(p, jnp.sum)
                    part = dot_nn(vt[h * size:(h + 1) * size, n * pair:(n + 1) * pair], p.astype(BF16))
                    total = here if total is None else total + here
                    acc = part if acc is None else acc + part
                total = jnp.sum(total, axis=0, keepdims=True)
                outs.append(acc / total)
                logs.append(jnp.broadcast_to(top + jnp.log2(total), (128 // hpd, pair)))
            out = (jnp.concatenate(outs, axis=0) if hpd > 1 else outs[0]).T
            log = (jnp.concatenate(logs[::-1], axis=0) if hpd > 1 else logs[0]).T
            for k in range(2):
                at = 2 * i + k
                o32_ref[at, q] = out[k * tok:(k + 1) * tok]
                o_out[at, q] = out[k * tok:(k + 1) * tok].astype(BF16)
                lse_ref[at, q] = log[k * tok:(k + 1) * tok]

                @pl.when(at == d)
                def _():
                    pltpu.make_async_copy(o_out.at[at, q], o_place(d, q), os.at[q, at]).start()

                @pl.when(at != d)
                def _():
                    send_o(q, at, lax.rem(at - d + nd, nd)).start()

        write(o32_ref, o32_out, 1, q).start()
        write(lse_ref, lse_out, 2, q).start()

    for q in range(seqs):
        @pl.loop(1, nd)
        def _(p):
            arrived(o_place(lax.rem(d + nd - p, nd), q), orr.at[q, p])
            send(q, 0, p).wait_send()
            send(q, 1, p).wait_send()

        @pl.loop(0, nd)
        def _(i):
            arrived(o_out.at[i, q], os.at[q, i])
        write(got, got_out, 0, q, True).wait()
        write(o32_ref, o32_out, 1, q).wait()
        write(lse_ref, lse_out, 2, q).wait()


def run_attn_fwd(span, slopes, qkv, hpd):
    nb, _, seqs, tok, lanes = qkv.shape
    t = nb * tok
    pairs = nb // 2
    tiles = pairs * (pairs + 1) // 2
    if hpd * tiles > 24:
        tiles = pairs
    dma = pltpu.SemaphoreType.DMA
    return pl.pallas_call(
        functools.partial(attn_fwd_kernel, hpd=hpd, nd=nb),
        out_shape=(
            sds(qkv.shape, BF16),
            landing_shape(1, nb, seqs, tok, lanes),
            sds((nb, seqs, tok, lanes), F32),
            sds((nb, seqs, tok, 128), F32),
        ),
        in_specs=[smem(), smem(), hbm()],
        out_specs=(hbm(), vmem(), hbm(), hbm()),
        scratch_shapes=[
            pltpu.VMEM(qkv.shape, BF16),
            pltpu.VMEM((nb, seqs, tok, lanes), F32),
            pltpu.VMEM((nb, seqs, tok, 128), F32),
            dma((3, seqs)),
            pltpu.VMEM((hpd, t, 256), BF16),
            pltpu.VMEM((hpd, t, 256), BF16),
            pltpu.VMEM((lanes, t), BF16),
            pltpu.VMEM((hpd, tiles, 2 * tok, 2 * tok), F32),
            pltpu.VMEM((hpd, nb // 2, 8, 2 * tok), F32),
            pltpu.VMEM((hpd, 3, 2 * tok, 2 * tok), F32),
            pltpu.VMEM((hpd, tok, 128), F32),
            pltpu.VMEM((hpd, tok, 128), F32),
            pltpu.VMEM((hpd, tok, 128), F32),
            pltpu.VMEM((nb, seqs, tok, lanes), BF16),
            dma((seqs, 2, nb)),
            dma((seqs, 2, nb)),
            dma((seqs, nb)),
            dma((seqs, nb)),
            dma((seqs,)),
        ],
        compiler_params=params(collective_id=2, has_side_effects=True),
        name="attn_fwd",
    )(span, slopes, qkv)


def attn_bwd_kernel(
    span_ref, slope_ref, qkv_in, do_src, o32_in, lse_in, got,
    qkv_ref, o32_ref, lse_ref, sem_in, do_got, out, qa, ka, kt, va, qm, da, dm, dqt, corr, qbase, kbase, kfar,
    ss, sr, gs, gr, loc, *, hpd, nd
):
    nb, _, seqs, tok, lanes = qkv_ref.shape
    inputs = [
        pltpu.make_async_copy(qkv_in, qkv_ref, sem_in.at[0]),
        pltpu.make_async_copy(lse_in, lse_ref, sem_in.at[1]),
        pltpu.make_async_copy(o32_in, o32_ref, sem_in.at[2]),
    ]
    for copy in inputs:
        copy.start()
    size = lanes // hpd
    unit = size ** (-0.5)
    pair = 2 * tok
    g = lax.axis_index("grp")
    d = lax.axis_index("dev")

    def own_copy(q):
        return pltpu.make_async_copy(do_src.at[d, q], do_got.at[d, q], loc.at[q])

    for q in range(seqs):
        own_copy(q).start()
    greet_plane(g, d, nd)

    def send(q, p):
        to = lax.rem(d + p, nd)
        return remote(do_src.at[to, q], do_got.at[d, q], ss.at[q, p], sr.at[q, p], (g, to))

    def send_all(q):
        @pl.loop(1, nd)
        def _(p):
            send(q, p).start()

    send_all(0)

    def place_back(kind, source, q):
        return landing(got, kind, source, q, tok, lanes, 3)

    def back(q, kind, p):
        to = lax.rem(d + p, nd)
        return remote(
            out.at[to, kind, q], place_back(kind, d, q), gs.at[q, kind, p], gr.at[q, kind, p], (g, to)
        )

    def back_own(q, kind):
        return pltpu.make_async_copy(out.at[d, kind, q], place_back(kind, d, q), gs.at[q, kind, 0])

    for h in range(hpd):
        mask, span = far_side(slope_ref[h] * LOG2E, tok)
        pair_tables(corr, h, mask, span)
    column_tables(slope_ref, qbase, kbase, kfar, hpd, lanes)
    row = lax.broadcasted_iota(jnp.int32, (lanes, lanes), 0) // size
    col = lax.broadcasted_iota(jnp.int32, (lanes, lanes), 1) // size
    across = (row == hpd - 1 - col).astype(F32).astype(BF16)
    for copy in inputs:
        copy.wait()

    @pl.loop(0, seqs)
    def _(q):
        @pl.loop(0, nb)
        def _(j):
            at_j = pl.ds(pl.multiple_of(j * tok, tok), tok)
            qj = qkv_ref[j, 0, q]
            kj = qkv_ref[j, 1, q]
            vj = qkv_ref[j, 2, q].astype(F32)
            kt[:, at_j] = kj.astype(F32).T.astype(BF16)
            dqt[:, at_j] = jnp.zeros((lanes, tok), F32)
            block = jnp.full((tok, 128), j, jnp.int32).astype(F32)
            low = [-p for p in parts3(lse_ref[j, q])]
            for h in range(hpd):
                qa[h, at_j, :] = q_columns(qj, h, hpd, qbase[h], low)
                ka[h, at_j, :] = k_columns(kj, h, hpd, kbase[h] + block * kfar[h])
                if hpd > 1:
                    own = own_lanes(h, (tok, lanes), hpd, lanes)
                    qm[h, at_j, :] = jnp.where(own, qj.astype(F32), 0.0).astype(BF16)
                    va[h, at_j, :] = jnp.where(own, vj, kbase[h]).astype(BF16)
                else:
                    qm[h, at_j, :] = qj
                    va[h, at_j, :] = jnp.concatenate([vj, kbase[h][:, 0:lanes]], axis=1).astype(BF16)

        own_copy(q).wait()

        @pl.loop(1, nd)
        def _(p):
            arrived(do_got.at[lax.rem(d + nd - p, nd), q], sr.at[q, p])

        @pl.when(q + 1 < seqs)
        def _():
            send_all(q + 1)

        @pl.loop(0, nb)
        def _(j):
            at_j = pl.ds(pl.multiple_of(j * tok, tok), tok)
            do = do_got[j, q].astype(F32)
            delta = jnp.zeros((tok, lanes), F32)
            for p in parts3(do * o32_ref[j, q]):
                delta = delta + dot_nn(p.astype(BF16), across)
            low = [-p for p in parts3(delta)]
            for h in range(hpd):
                if hpd > 1:
                    own = own_lanes(h, (tok, lanes), hpd, lanes)
                    none = jnp.where(own, do, 0.0)
                    da[h, at_j, :] = extra_lanes(none, low, h, hpd, lanes).astype(BF16)
                    dm[h, at_j, :] = none.astype(BF16)
                else:
                    extra = extra_lanes(jnp.zeros((tok, lanes), F32), low, h, hpd, lanes)
                    da[h, at_j, :] = jnp.concatenate([do, extra], axis=1).astype(BF16)
                    dm[h, at_j, :] = do.astype(BF16)

        start = span_ref[q]

        pairs = nb // 2

        def tile(j, i):
            at_j = slice(j * pair, (j + 1) * pair)
            at_i = slice(i * pair, (i + 1) * pair)
            flag = (start == j * pair).astype(jnp.int32) + 2 * (start == j * pair + tok).astype(jnp.int32)
            dk = dv = None
            for h in range(hpd):
                s = dot_nt(ka[h, at_j, :], qa[h, at_i, :])
                if i == j:
                    s = s + corr[h, flag]
                p = jnp.exp2(s)
                ds = (p * dot_nt(va[h, at_j, :], da[h, at_i, :])).astype(BF16)
                dv_h = dot_nn(p.astype(BF16), dm[h, at_i, :])
                dk_h = dot_nn(ds, qm[h, at_i, :])
                dk = dk_h if dk is None else dk + dk_h
                dv = dv_h if dv is None else dv + dv_h
                rows = slice(h * size, (h + 1) * size)
                dqt[rows, at_i] += dot_nn(kt[rows, at_j], ds)
            return dk, dv

        @pl.loop(0, pairs)
        def _(n):
            turn_of = lax.rem(d // 2 + n, pairs)
            for case in range(pairs):
                @pl.when(turn_of == case)
                def _():
                    dk, dv = tile(case, case)
                    for i in range(case + 1, pairs):
                        more = tile(case, i)
                        dk = dk + more[0]
                        dv = dv + more[1]
                    for k in range(2):
                        half = slice(k * tok, (k + 1) * tok)
                        out[2 * case + k, 1, q] = (dk[half] * unit).astype(BF16)
                        out[2 * case + k, 2, q] = dv[half].astype(BF16)

            for k in range(2):
                j = 2 * turn_of + k
                for kind in (1, 2):
                    @pl.when(j == d)
                    def _():
                        back_own(q, kind).start()

                    @pl.when(j != d)
                    def _():
                        back(q, kind, lax.rem(j - d + nd, nd)).start()

        @pl.loop(0, nb)
        def _(n):
            j = lax.rem(d + n, nb)
            at_j = pl.ds(pl.multiple_of(j * tok, tok), tok)
            out[j, 0, q] = (dqt[:, at_j].T * unit).astype(BF16)

            @pl.when(n == 0)
            def _():
                back_own(q, 0).start()

            @pl.when(n > 0)
            def _():
                back(q, 0, n).start()

    for q in range(seqs):
        for kind in range(3):
            back_own(q, kind).wait()

        @pl.loop(1, nd)
        def _(p):
            send(q, p).wait_send()
            source = lax.rem(d + nd - p, nd)
            for kind in range(3):
                back(q, kind, p).wait_send()
                arrived(place_back(kind, source, q), gr.at[q, kind, p])


def run_attn_bwd(span, slopes, qkv, do, o32, lse, hpd):
    nb, _, seqs, tok, lanes = qkv.shape
    t = nb * tok
    dma = pltpu.SemaphoreType.DMA
    wide = 128 if hpd == 1 else lanes
    return pl.pallas_call(
        functools.partial(attn_bwd_kernel, hpd=hpd, nd=nb),
        out_shape=landing_shape(3, nb, seqs, tok, lanes),
        in_specs=[smem(), smem(), hbm(), hbm(), hbm(), hbm()],
        out_specs=vmem(),
        scratch_shapes=[
            pltpu.VMEM(qkv.shape, BF16),
            pltpu.VMEM(o32.shape, F32),
            pltpu.VMEM(lse.shape, F32),
            dma((3,)),
            pltpu.VMEM((nb, seqs, tok, lanes), BF16),
            pltpu.VMEM(qkv.shape, BF16),
            pltpu.VMEM((hpd, t, 256), BF16),
            pltpu.VMEM((hpd, t, 256), BF16),
            pltpu.VMEM((lanes, t), BF16),
            pltpu.VMEM((hpd, t, wide), BF16),
            pltpu.VMEM((hpd, t, lanes), BF16),
            pltpu.VMEM((hpd, t, wide), BF16),
            pltpu.VMEM((hpd, t, lanes), BF16),
            pltpu.VMEM((lanes, t), F32),
            pltpu.VMEM((hpd, 3, 2 * tok, 2 * tok), F32),
            pltpu.VMEM((hpd, tok, 128), F32),
            pltpu.VMEM((hpd, tok, 128), F32),
            pltpu.VMEM((hpd, tok, 128), F32),
            dma((seqs, nb)),
            dma((seqs, nb)),
            dma((seqs, 3, nb)),
            dma((seqs, 3, nb)),
            dma((seqs,)),
        ],
        compiler_params=params(collective_id=3, has_side_effects=True),
        name="attn_bwd",
    )(span, slopes, qkv, do, o32, lse)


def mlp_kernel(
    slot_ref, att_in, x_in, dy_in, vec_ref, gath,
    act_out, dx1_out, do_out, sums_ref, grads,
    att_ref, x_ref, dy_ref, sem_in, wo, wup, wdn, x1, acc, dh2, h2_ref, h2t, attt, da_ref, act_ref, dx1_ref, g_ref, dz_ref, do_ref, stage,
    sem_o, sem_t, sem_g, sem_w, *, nd, first_o, first_up, first_dn, tile
):
    rows, width = x_ref.shape
    side = gath.shape[1]
    per = width // side
    tiles = wup.shape[0]
    ff = tiles * tile
    cols = tile // side
    lanes = do_ref.shape[2]
    fper = ff // side
    inputs = [
        pltpu.make_async_copy(att_in, att_ref, sem_in.at[0]),
        pltpu.make_async_copy(x_in, x_ref, sem_in.at[1]),
        pltpu.make_async_copy(dy_in, dy_ref, sem_in.at[2]),
    ]
    for copy in inputs:
        copy.start()

    for i in range(per):
        for j in range(per):
            fetch_block(gath, slot_at(slot_ref, first_o + i * per + j), wo, i * side, j * side, sem_o.at[0], side).start()

    def fetch_tile(f):
        for i in range(per):
            for j in range(cols):
                fetch_block(gath, slot_at(slot_ref, first_up + i * fper + f * cols + j), wup.at[f], i * side, j * side, sem_t.at[f], side).start()
            for j in range(cols):
                fetch_block(gath, slot_at(slot_ref, first_dn + (f * cols + j) * per + i), wdn.at[f], j * side, i * side, sem_t.at[f], side).start()

    fetch_tile(0)
    fetch_tile(1)
    for copy in inputs:
        copy.wait()
    for r in range(width // 256):
        attt[r * 256:(r + 1) * 256, :] = turn(att_ref[:, r * 256:(r + 1) * 256])
    pltpu.make_async_copy(wo, wo, sem_o.at[0]).wait()
    for half in range(2):
        c = slice(half * width // 2, (half + 1) * width // 2)
        x1[:, c] = x_ref[:, c].astype(F32) + dot_nn(att_ref[...], wo[:, c]) + vec_ref[BO:BO + 1, c]

    chunk = 128

    def rows_at(r):
        return pl.ds(pl.multiple_of(r * chunk, chunk), chunk)

    @pl.loop(0, rows // chunk)
    def _(r):
        at = rows_at(r)
        centred, inv = layer_stats(x1[at, :])
        h2_ref[at, :] = (centred * inv * vec_ref[GAIN2:GAIN2 + 1, :] + vec_ref[SHIFT2:SHIFT2 + 1, :]).astype(BF16)
        acc[at, :] = x1[at, :] + vec_ref[BDOWN:BDOWN + 1, :]
        dh2[at, :] = jnp.zeros((chunk, width), F32)

    for r in range(width // 256):
        h2t[r * 256:(r + 1) * 256, :] = turn(h2_ref[:, r * 256:(r + 1) * 256])

    def put(slot, first, res, down, across):
        for i in range(down):
            for j in range(across):
                stage[slot, first + i * across + j] = res[i * side:(i + 1) * side, j * side:(j + 1) * side]

    def leave(slot, n, block):
        pltpu.make_async_copy(stage.at[slot, n], grads.at[slot_at(slot_ref, block)], sem_g.at[slot]).start()

    def left(slot, size):
        at = stage.at[slot, pl.ds(0, size)]
        pltpu.make_async_copy(at, at, sem_g.at[slot]).wait()

    full = 2 * per * cols
    piece = 512

    @pl.loop(0, tiles)
    def _(f):
        @pl.when(f + 2 < tiles)
        def _():
            fetch_tile(f + 2)
        pltpu.make_async_copy(wup.at[f], wup.at[f], sem_t.at[f]).wait()
        pltpu.make_async_copy(wdn.at[f], wdn.at[f], sem_t.at[f]).wait()
        for k in range(tile // piece):
            c = slice(k * piece, (k + 1) * piece)
            z = dot_nn(h2_ref[...], wup[f, :, c]) + vec_ref[pl.ds(BUP + f, 1), c]
            dg = dot_nt(dy_ref[...], wdn[f, c, :])
            z2 = z * z
            th = jnp.tanh(z * (0.7978845608028654 + (0.7978845608028654 * 0.044715) * z2))
            half_more = 0.5 + 0.5 * th
            g_ref[:, c] = (z * half_more).astype(BF16)
            slope = half_more + (0.5 * z) * (1.0 - th * th) * (
                0.7978845608028654 + (3.0 * 0.044715 * 0.7978845608028654) * z2
            )
            dz = (dg * slope).astype(BF16)
            dz_ref[:, c] = dz
            sums_ref[pl.ds(pl.multiple_of(8 * (4 + f), 8), 8), c] = fold_rows(dz.astype(F32))
        for k in range(width // piece):
            c = slice(k * piece, (k + 1) * piece)
            acc[:, c] += dot_nn(g_ref[...], wdn[f, :, c])
            dh2[:, c] += dot_nt(dz_ref[...], wup[f, c, :])
        slot = lax.rem(f, 2)

        @pl.when(f >= 2)
        def _():
            left(slot, full)
        per_piece = piece // side
        for k in range(tile // piece):
            c = slice(k * piece, (k + 1) * piece)
            res = dot_nn(turn(g_ref[:, c]), dy_ref[...]).astype(BF16)
            put(slot, k * per_piece * per, res, per_piece, per)
        for k in range(width // piece):
            res = dot_nn(h2t[k * piece:(k + 1) * piece, :], dz_ref[...]).astype(BF16)
            put(slot, per * cols + k * per_piece * cols, res, per_piece, cols)
        for i in range(per):
            for j in range(cols):
                leave(slot, j * per + i, first_dn + (f * cols + j) * per + i)
            for j in range(cols):
                leave(slot, per * cols + i * cols + j, first_up + i * fper + f * cols + j)

    zero = jnp.zeros((8, width), F32)

    def finish(r, carry):
        s_bo, s_gain, s_shift, s_bdown = carry
        at = rows_at(r)
        act_ref[at, :] = acc[at, :].astype(BF16)
        centred, inv = layer_stats(x1[at, :])
        hat = centred * inv
        dh = dh2[at, :]
        dhg = dh * vec_ref[GAIN2:GAIN2 + 1, :]
        back = inv * (
            dhg
            - jnp.mean(dhg, axis=-1, keepdims=True)
            - hat * jnp.mean(dhg * hat, axis=-1, keepdims=True)
        )
        dy = dy_ref[at, :].astype(F32)
        dx1 = dy + back
        dx1_ref[at, :] = dx1
        da = dx1.astype(BF16)
        da_ref[at, :] = da
        return (
            s_bo + fold_rows(da.astype(F32)),
            s_gain + fold_rows(dh * hat),
            s_shift + fold_rows(dh),
            s_bdown + fold_rows(dy),
        )

    carry = lax.fori_loop(0, rows // chunk, finish, (zero, zero, zero, zero))
    for n in range(4):
        sums_ref[8 * n:8 * n + 8, :] = carry[n]
    outs = [
        pltpu.make_async_copy(act_ref, act_out, sem_w.at[0]),
        pltpu.make_async_copy(dx1_ref, dx1_out, sem_w.at[1]),
        pltpu.make_async_copy(do_ref, do_out, sem_w.at[2]),
    ]
    outs[0].start()
    outs[1].start()
    for half in range(2):
        c = slice(half * width // 2, (half + 1) * width // 2)
        res = dot_nt(da_ref[...], wo[c, :]).astype(BF16)
        for d in range(nd // 2):
            do_ref[half * (nd // 2) + d] = res[:, d * lanes:(d + 1) * lanes]
    outs[2].start()
    left(0, full)
    left(1, full)
    half_rows = width // 2
    for half in range(2):
        res = dot_nn(attt[half * half_rows:(half + 1) * half_rows, :], da_ref[...]).astype(BF16)
        put(half, 0, res, per // 2, per)

        for i in range(per // 2):
            for j in range(per):
                leave(half, i * per + j, first_o + (half * (per // 2) + i) * per + j)
    for half in range(2):
        left(half, per * per // 2)
    for copy in outs:
        copy.wait()


def run_mlp(slot_of, att, x, dy, vec, gath, nd):
    rows, width = x.shape
    side = gath.shape[1]
    lanes = width // nd
    per = width // side
    first_o = 3 * per * per
    first_up = first_o + per * per
    first_dn = first_up + per * (FF // side)
    tile = width
    f32_rows = pltpu.VMEM((rows, width), F32)
    bf16_rows = pltpu.VMEM((rows, width), BF16)
    turned = pltpu.VMEM((width, rows), BF16)
    return pl.pallas_call(
        functools.partial(
            mlp_kernel, nd=nd, first_o=first_o, first_up=first_up, first_dn=first_dn, tile=tile
        ),
        out_shape=(
            sds((rows, width), BF16),
            sds((rows, width), F32),
            sds((nd, rows, lanes), BF16),
            sds((8 * (4 + FF // width), width), F32),
            sds(gath.shape, BF16),
        ),
        in_specs=[smem(), hbm(), hbm(), hbm(), vmem(), hbm()],
        out_specs=(hbm(), hbm(), hbm(), vmem(), hbm()),
        scratch_shapes=[
            bf16_rows,
            bf16_rows,
            bf16_rows,
            pltpu.SemaphoreType.DMA((3,)),
            pltpu.VMEM((width, width), BF16),
            pltpu.VMEM((FF // tile, width, tile), BF16),
            pltpu.VMEM((FF // tile, tile, width), BF16),
            f32_rows,
            f32_rows,
            f32_rows,
            bf16_rows,
            turned,
            turned,
            bf16_rows,
            bf16_rows,
            f32_rows,
            bf16_rows,
            bf16_rows,
            pltpu.VMEM((nd, rows, lanes), BF16),
            pltpu.VMEM((2, 2 * per * (tile // side), side, side), BF16),
            pltpu.SemaphoreType.DMA((1,)),
            pltpu.SemaphoreType.DMA((FF // tile,)),
            pltpu.SemaphoreType.DMA((2,)),
            pltpu.SemaphoreType.DMA((3,)),
        ],
        compiler_params=params(),
        name="mlp",
    )(slot_of, att, x, dy, vec, gath)


def dh1_dot(cat, w, dh1, part, half):
    width = dh1.shape[1]
    c = slice(half * width // 2, (half + 1) * width // 2)
    res = dot_nt(cat[:, part * width:(part + 1) * width], w[part, c, :])
    if part == 0:
        dh1[:, c] = res
    else:
        dh1[:, c] += res


def first_norm_back(cat, x, dh1, dx1, ig, vec_ref):
    rows, width = x.shape
    chunk = 128
    zero = jnp.zeros((8, width), F32)

    def finish(r, carry):
        s_gain, s_shift, s_bq, s_bv = carry
        at = pl.ds(pl.multiple_of(r * chunk, chunk), chunk)
        centred, inv = layer_stats(x[at, :].astype(F32))
        hat = centred * inv
        dh = dh1[at, :]
        dhg = dh * vec_ref[GAIN1:GAIN1 + 1, :]
        back = inv * (
            dhg
            - jnp.mean(dhg, axis=-1, keepdims=True)
            - hat * jnp.mean(dhg * hat, axis=-1, keepdims=True)
        )
        ig[at, :] = dx1[at, :] + back
        return (
            s_gain + fold_rows(dh * hat),
            s_shift + fold_rows(dh),
            s_bq + fold_rows(cat[at, 0:width].astype(F32)),
            s_bv + fold_rows(cat[at, 2 * width:3 * width].astype(F32)),
        )

    return lax.fori_loop(0, rows // chunk, finish, (zero, zero, zero, zero))


def vector_rows(first, sums2):
    rows = [jnp.sum(v, axis=0, keepdims=True) for v in first]
    rows += [jnp.sum(sums2[8 * n:8 * n + 8, :], axis=0, keepdims=True) for n in range(sums2.shape[0] // 8)]
    return rows


def dh1_kernel(cat_ref, x_ref, dx1_ref, vec_ref, wq_ref, sums2_ref, ig_ref, vsum_ref, dh1):
    for part in range(3):
        for half in range(2):
            dh1_dot(cat_ref, wq_ref, dh1, part, half)
    first = first_norm_back(cat_ref, x_ref, dh1, dx1_ref, ig_ref, vec_ref)
    for n, row in enumerate(vector_rows(first, sums2_ref)):
        vsum_ref[n:n + 1, :] = row


def run_dh1(cat, x, dx1, vec, wq, sums2):
    rows, width = x.shape
    return pl.pallas_call(
        dh1_kernel,
        out_shape=(sds((rows, width), F32), sds(vec.shape, F32)),
        in_specs=[vmem()] * 6,
        out_specs=(vmem(), vmem()),
        scratch_shapes=[pltpu.VMEM((rows, width), F32)],
        compiler_params=params(),
        name="dh1",
    )(cat, x, dx1, vec, wq, sums2)


def wgrad_kernel(slot_ref, h1_ref, cat_ref, rest, out, a_t, stage, sem_out, *, side, tile):
    del rest
    rows, width = h1_ref.shape
    per = width // side
    cols = tile // side
    steps = cat_ref.shape[1] // tile
    for r in range(width // 256):
        c = slice(r * 256, (r + 1) * 256)
        a_t[c, :] = turn(h1_ref[:, c])

    def left(slot):
        pltpu.make_async_copy(stage.at[slot], stage.at[slot], sem_out.at[slot]).wait()

    @pl.loop(0, steps)
    def _(t):
        slot = lax.rem(t, 2)

        @pl.when(t >= 2)
        def _():
            left(slot)
        res = dot_nn(a_t[...], cat_ref[:, pl.ds(pl.multiple_of(t * tile, tile), tile)]).astype(BF16)
        for i in range(per):
            for j in range(cols):
                stage[slot, i * cols + j] = res[i * side:(i + 1) * side, j * side:(j + 1) * side]

        for i in range(per):
            for j in range(cols):
                dst = slot_at(slot_ref, i * 3 * per + t * cols + j)
                pltpu.make_async_copy(stage.at[slot, i * cols + j], out.at[dst], sem_out.at[slot]).start()

    left(0)
    left(1)


def run_wgrad(slot_of, h1, cat, grads):
    rows, width = h1.shape
    side = grads.shape[1]
    tile = 512
    return pl.pallas_call(
        functools.partial(wgrad_kernel, side=side, tile=tile),
        out_shape=sds(grads.shape, BF16),
        in_specs=[smem(), vmem(), vmem(), hbm()],
        out_specs=hbm(),
        scratch_shapes=[
            pltpu.VMEM((width, rows), BF16),
            pltpu.VMEM((2, (width // side) * (tile // side), side, side), BF16),
            pltpu.SemaphoreType.DMA((2,)),
        ],
        input_output_aliases={3: 0},
        compiler_params=params(),
        name="wgrad",
    )(slot_of, h1, cat, grads)


def whereami():
    g = lax.axis_index("grp")
    d = lax.axis_index("dev")
    core = lax.rem(d, 2)
    x = lax.rem(d // 2, 2)
    y = d // 4
    over_x = d + 2 - 4 * x
    over_y = d + 4 - 8 * y
    across = over_x + 4 - 8 * y
    sibling = d + 1 - 2 * core
    return g, d, over_x, over_y, across, sibling


def near_order(t, g, ng):
    t = ng - 1 - t
    low = jnp.where(t < ng - 1 - g, ng - 1 - t, t - (ng - 1 - g))
    high = jnp.where(t < g, t, ng - 1 - (t - g))
    return jnp.where(2 * g < ng, low, high)


def greet(g, ng, peers):
    barrier = pltpu.get_barrier_semaphore()
    for peer in peers:
        pl.semaphore_signal(barrier, inc=1, device_id=(g, peer), device_id_type=MESH)

    d = lax.axis_index("dev")

    @pl.when(g > 0)
    def _():
        pl.semaphore_signal(barrier, inc=1, device_id=(g - 1, d), device_id_type=MESH)

    @pl.when(g < ng - 1)
    def _():
        pl.semaphore_signal(barrier, inc=1, device_id=(g + 1, d), device_id_type=MESH)

    ends = (g > 0).astype(jnp.int32) + (g < ng - 1).astype(jnp.int32)
    pl.semaphore_wait(barrier, len(peers) + ends)


def slot_cuts(count):
    third = (5 * count) // 24
    first = (count - third) // 2
    return first, count - third - first, third - third // 2, third // 2


def gather_kernel(
    w_ref, x_ref, block_ref, vin_ref, out, h1_ref, slot_ref, vec_ref,
    own, local_sem, zs, zr, cs, cr, ss, sr, *, ng, nd
):
    count = w_ref.shape[0]
    na, nb, nc1, nc2 = slot_cuts(count)
    flat = na + nb
    nc = nc1 + nc2
    g, d, over_x, over_y, across, sibling = whereami()
    columns = (d, over_x, over_y, across)
    own[...] = w_ref[...].astype(BF16)
    greet(g, ng, (over_x, over_y, sibling))

    def region(gz, dev, first=0, size=count):
        return out.at[pl.ds((gz * nd + dev) * count + first, size)]

    def wide(t):
        return count if t == 0 else flat

    def kind(n, t):
        return (
            (d, 0, wide(t), over_x),
            (d, 0, wide(t), over_y),
            (d, 0, wide(t), sibling),
            (over_x, 0, na, over_y),
            (over_y, na, nb, over_x),
            (over_x, 0, wide(t), sibling),
            (over_y, 0, wide(t), sibling),
            (across, 0, na, sibling),
            (across, na, nb, sibling),
            (over_x, flat, nc1, over_y),
            (over_y, flat + nc1, nc2, over_x),
            (across, flat, nc1, sibling),
            (across, flat + nc1, nc2, sibling),
            (d, flat, nc, sibling),
            (over_x, flat, nc, sibling),
            (over_y, flat, nc, sibling),
            (across, flat, nc, sibling),
        )[n]

    def kinds(t):
        return range(13) if t == 0 else tuple(range(9)) + tuple(range(13, 17))

    def plane(n, t, src=None):
        gz = near_order(t, g, ng)
        dev, first, size, to = kind(n, t)
        at = region(gz, dev, first, size)
        return remote(at if src is None else src, at, ss.at[n, gz], sr.at[n, gz], (g, to))

    def landed(n, t, dev):
        gz = near_order(t, g, ng)
        _, first, size, _ = kind(n, t)
        arrived(region(gz, dev, first, size), sr.at[n, gz])

    def line(gz, up, src=None):
        at = region(gz, d, 0, flat)
        to = g + 1 if up else g - 1
        return remote(at if src is None else src, at, zs.at[gz, int(up)], zr.at[gz], (to, d))

    def corner_line(gz, c, up, src=None):
        at = region(gz, columns[c], flat, nc)
        to = g + 1 if up else g - 1
        return remote(at if src is None else src, at, cs.at[gz, c, int(up)], cr.at[gz, c], (to, d))

    def both_ways(gz, make):
        @pl.when((gz <= g) & (g < ng - 1))
        def _():
            make(True)

        @pl.when((gz >= g) & (g > 0))
        def _():
            make(False)

    mine = pltpu.make_async_copy(own, region(g, d), local_sem.at[0])
    mine.start()

    def column(t):
        gz = near_order(t, g, ng)
        if t == 0:
            both_ways(gz, lambda up: line(gz, up, cut(own, 0, flat)).start())
            for n in range(3):
                plane(n, t, own).start()
            both_ways(gz, lambda up: corner_line(gz, 0, up, cut(own, flat, nc)).start())
            return
        arrived(region(gz, d, 0, flat), zr.at[gz])
        both_ways(gz, lambda up: line(gz, up).start())
        for n in range(3):
            plane(n, t).start()

    def sides(t):
        gz = near_order(t, g, ng)
        landed(0, t, over_x)
        plane(3, t).start()
        if t == 0:
            plane(9, t).start()
            both_ways(gz, lambda up: corner_line(gz, 1, up).start())
        plane(5, t).start()
        landed(1, t, over_y)
        plane(4, t).start()
        if t == 0:
            plane(10, t).start()
            both_ways(gz, lambda up: corner_line(gz, 2, up).start())
        plane(6, t).start()

    def corner(t):
        gz = near_order(t, g, ng)
        if t == 0:
            landed(9, t, across)
            landed(10, t, across)
            both_ways(gz, lambda up: corner_line(gz, 3, up).start())
            plane(11, t).start()
            plane(12, t).start()
        landed(3, t, across)
        plane(7, t).start()
        landed(4, t, across)
        plane(8, t).start()

    def far_corner(t):
        gz = near_order(t, g, ng)
        for c in range(4):
            arrived(region(gz, columns[c], flat, nc), cr.at[gz, c])
            both_ways(gz, lambda up: corner_line(gz, c, up).start())
            plane(13 + c, t).start()

    plan = [(t, f) for t in range(ng) for f in (0, 1, 2, 3) if t > 0 or f < 3]
    lag = {0: 0, 1: 1.5, 2: 2.6, 3: 2.2}
    for t, f in sorted(plan, key=lambda e: e[0] * 1.0 + lag[e[1]]):
        (column, sides, corner, far_corner)[f](t)
        if (t, f) == (0, 0):
            prepare(x_ref, block_ref, vin_ref, h1_ref, slot_ref, vec_ref)

    for t in range(ng):
        for n in kinds(t):
            dev, _, _, to = kind(n, t)
            if to is sibling:
                landed(n, t, dev + sibling - d)
    mine.wait()
    for t in range(ng):
        gz = near_order(t, g, ng)
        for n in kinds(t):
            plane(n, t).wait_send()
        both_ways(gz, lambda up: line(gz, up).wait_send())
        for c in range(4):
            both_ways(gz, lambda up: corner_line(gz, c, up).wait_send())


def run_gather(w, x, blocks, vin, ng, nd):
    count, side, _ = w.shape
    dma = pltpu.SemaphoreType.DMA
    return pl.pallas_call(
        functools.partial(gather_kernel, ng=ng, nd=nd),
        out_shape=(sds((ng * nd * count, side, side), BF16),) + prepared_shapes(x, blocks, vin),
        in_specs=[vmem()] * 4,
        out_specs=(hbm(), vmem(), vmem(), vmem()),
        scratch_shapes=[
            pltpu.VMEM((count, side, side), BF16),
            dma((1,)),
            dma((ng, 2)),
            dma((ng,)),
            dma((ng, 4, 2)),
            dma((ng, 4)),
            dma((17, ng)),
            dma((17, ng)),
        ],
        compiler_params=params(collective_id=0, has_side_effects=True),
        name="gather",
    )(w, x, blocks, vin)


def add_blocks(dst, src, size):
    step = next(n for n in (4, 5, 3, 2, 1) if size % n == 0)

    @pl.loop(0, size // step)
    def _(n):
        for k in range(step):
            dst[n * step + k] = dst[n * step + k] + src[n * step + k]


def scatter_kernel(
    grads, sums2_ref, vec_ref, vin_ref, cat_in, x_in, dx1_in, wq_in, out_ref, vout_ref, vnew_ref, ig_out,
    cat, x, dx1, wq, dh1, sem_in, mine, r0, r1y, r1x, r2x, r2y, rz, cz, cy, cx, cx2, cy2, vwork, vxy, vz,
    load, s0, w0, s1, w1, s2, w2, sz, wz, sc, wc, s3, w3, vs, vw, *, ng, nd, rate
):
    count = out_ref.shape[0]
    na, nb, nc1, nc2 = slot_cuts(count)
    flat = na + nb
    nc = nc1 + nc2
    g, d, over_x, over_y, across, sibling = whereami()
    columns = (d, over_x, over_y, across)

    def region(gz, dev):
        return grads.at[pl.ds((gz * nd + dev) * count, count)]

    def order(t):
        return near_order(ng - 1 - t, g, ng)

    for t in range(ng):
        for c in range(4):
            pltpu.make_async_copy(region(order(t), columns[c]), mine.at[order(t), c], load.at[order(t), c]).start()
    greet(g, ng, (over_x, over_y, sibling))

    def to_sibling(gz, c):
        return remote(
            region(gz, columns[c] + sibling - d), r0.at[gz, c], s0.at[gz, c], w0.at[gz, c], (g, sibling)
        )

    peers = (sibling, over_x, over_y)

    def vec_copy(n):
        return remote(vwork.at[n], vxy.at[n], vs.at[n], vw.at[n], (g, peers[n]))

    for t in range(ng):
        for c in (3, 2, 1, 0):
            to_sibling(order(t), c).start()
    inputs = [
        pltpu.make_async_copy(cat_in, cat, sem_in.at[0]),
        pltpu.make_async_copy(wq_in, wq, sem_in.at[1]),
        pltpu.make_async_copy(x_in, x, sem_in.at[2]),
        pltpu.make_async_copy(dx1_in, dx1, sem_in.at[3]),
    ]
    for copy in inputs:
        copy.start()
    input_grad = pltpu.make_async_copy(dx1, ig_out, sem_in.at[4])

    def first_norm():
        for copy in inputs:
            copy.wait()
        for part in range(3):
            for half in range(2):
                dh1_dot(cat, wq, dh1, part, half)
        first = first_norm_back(cat, x, dh1, dx1, dx1, vec_ref)
        input_grad.start()
        for n, row in enumerate(vector_rows(first, sums2_ref)):
            vwork[0, n:n + 1, :] = row
        vec_copy(0).start()

    first = (
        (2, 0, na, r1y, 0, over_y),
        (3, 0, na, r1y, 1, over_y),
        (1, na, nb, r1x, 0, over_x),
        (3, na, nb, r1x, 1, over_x),
    )
    second = ((1, 0, na, r2x, over_x), (2, na, nb, r2y, over_y))
    third = (
        (2, flat, nc1, cy.at[0], over_y),
        (3, flat, nc1, cy.at[1], over_y),
        (1, flat + nc1, nc2, cx.at[0], over_x),
        (3, flat + nc1, nc2, cx.at[1], over_x),
        (1, flat, nc1, cx2, over_x),
        (2, flat + nc1, nc2, cy2, over_y),
    )

    def copy1(n, gz):
        c, at, size, buf, place_at, to = first[n]
        return remote(cut(mine.at[gz, c], at, size), buf.at[gz, place_at], s1.at[n, gz], w1.at[n, gz], (g, to))

    def copy2(n, gz):
        c, at, size, buf, to = second[n]
        return remote(cut(mine.at[gz, c], at, size), buf.at[gz], s2.at[n, gz], w2.at[n, gz], (g, to))

    def copy3(n):
        c, at, size, buf, to = third[n]
        return remote(cut(mine.at[g, c], at, size), buf, s3.at[n], w3.at[n], (g, to))

    def flat_part(gz):
        return cut(mine.at[gz, 0], 0, flat)

    def corner_part(gz):
        return mine.at[gz, :, pl.ds(flat, nc)]

    def line(gz, part, buf, sends, waits, up):
        at = gz if up else jnp.where(gz < g - 1, gz, ng)
        to = g + 1 if up else g - 1
        return remote(part(gz), buf.at[at], sends.at[gz], waits.at[at], (to, d))

    def pass_on(gz, part, buf, sends, waits, gather):
        @pl.when(gz > g)
        def _():
            @pl.when(g > 0)
            def _():
                arrived(buf.at[gz], waits.at[gz])
                gather(gz)
            line(gz, part, buf, sends, waits, True).start()

        @pl.when(gz < g)
        def _():
            @pl.when(g < ng - 1)
            def _():
                arrived(buf.at[gz], waits.at[gz])
                gather(gz)
            line(gz, part, buf, sends, waits, False).start()

    def gather_flat(gz):
        add_blocks(flat_part(gz), rz.at[gz], flat)

    def gather_corner(at, gz):
        for c in range(4):
            add_blocks(cut(mine.at[gz, c], flat, nc), cz.at[at, c], nc)

    def sums0(t, c):
        gz = order(t)
        pltpu.make_async_copy(region(gz, columns[c]), mine.at[gz, c], load.at[gz, c]).wait()
        arrived(r0.at[gz, c], w0.at[gz, c])
        add_blocks(mine.at[gz, c], r0.at[gz, c], count)
        for n in {3: (1, 3), 2: (0,), 1: (2,), 0: ()}[c]:
            copy1(n, gz).start()

    def along0(t):
        pass_on(order(t), corner_part, cz, sc, wc, lambda gz: gather_corner(gz, gz))

    def stage1(t, k):
        gz = order(t)
        if k == 0:
            arrived(r1y.at[gz, 1], w1.at[1, gz])
            add_blocks(cut(mine.at[gz, 1], 0, na), r1y.at[gz, 1], na)
            copy2(0, gz).start()
            arrived(r1x.at[gz, 1], w1.at[3, gz])
            add_blocks(cut(mine.at[gz, 2], na, nb), r1x.at[gz, 1], nb)
            copy2(1, gz).start()
        else:
            arrived(r1y.at[gz, 0], w1.at[0, gz])
            add_blocks(cut(mine.at[gz, 0], 0, na), r1y.at[gz, 0], na)
            arrived(r1x.at[gz, 0], w1.at[2, gz])
            add_blocks(cut(mine.at[gz, 0], na, nb), r1x.at[gz, 0], nb)

    def stage2(t):
        gz = order(t)
        arrived(r2x.at[gz], w2.at[0, gz])
        add_blocks(cut(mine.at[gz, 0], 0, na), r2x.at[gz], na)
        arrived(r2y.at[gz], w2.at[1, gz])
        add_blocks(cut(mine.at[gz, 0], na, nb), r2y.at[gz], nb)
        if t < ng - 1:
            pass_on(gz, flat_part, rz, sz, wz, gather_flat)

    def corner0():
        @pl.when(g > 0)
        def _():
            arrived(cz.at[g], wc.at[g])
            gather_corner(g, g)

        @pl.when(g < ng - 1)
        def _():
            arrived(cz.at[ng], wc.at[ng])
            gather_corner(ng, g)
        for n in range(4):
            copy3(n).start()

    def corner1():
        arrived(cy.at[1], w3.at[1])
        add_blocks(cut(mine.at[g, 1], flat, nc1), cy.at[1], nc1)
        copy3(4).start()
        arrived(cx.at[1], w3.at[3])
        add_blocks(cut(mine.at[g, 2], flat + nc1, nc2), cx.at[1], nc2)
        copy3(5).start()
        arrived(cy.at[0], w3.at[0])
        add_blocks(cut(mine.at[g, 0], flat, nc1), cy.at[0], nc1)
        arrived(cx.at[0], w3.at[2])
        add_blocks(cut(mine.at[g, 0], flat + nc1, nc2), cx.at[0], nc2)

    def corner2():
        arrived(cx2, w3.at[4])
        add_blocks(cut(mine.at[g, 0], flat, nc1), cx2, nc1)
        arrived(cy2, w3.at[5])
        add_blocks(cut(mine.at[g, 0], flat + nc1, nc2), cy2, nc2)

    def vec_step(n):
        arrived(vxy.at[n], vw.at[n])
        total = vwork[n] + vxy[n]
        if n < 2:
            vwork[n + 1] = total
            vec_copy(n + 1).start()
        else:
            vz[g] = total

    def vec_line(gz, up):
        to = g + 1 if up else g - 1
        return remote(vz.at[gz], vz.at[gz], vs.at[3 + 2 * gz + int(up)], vw.at[3 + gz], (to, d))

    def vec_first_line():
        vec_step(2)

        @pl.when(g < ng - 1)
        def _():
            vec_line(g, True).start()

        @pl.when(g > 0)
        def _():
            vec_line(g, False).start()

    def vec_next_line(n):
        gz = near_order(n, g, ng)
        arrived(vz.at[gz], vw.at[3 + gz])

        @pl.when((gz < g) & (g < ng - 1))
        def _():
            vec_line(gz, True).start()

        @pl.when((gz > g) & (g > 0))
        def _():
            vec_line(gz, False).start()

    def vec_out():
        total = vz[0]
        for z in range(1, ng):
            total = total + vz[z]
        vwork[3] = total
        per = total.shape[1] // 128
        for r in range(total.shape[0]):
            for c in range(per):
                row = vwork[3, r:r + 1, c * 128:(c + 1) * 128]
                n = per * r + c
                vout_ref[n:n + 1, :] = row
                vnew_ref[n:n + 1, :] = vin_ref[n:n + 1, :] - rate * row

    last = ng - 1
    plan = [(t + 0.25 * (3 - c), sums0, (t, c)) for t in range(ng) for c in range(4)]
    plan += [(t + 1.2 + 0.3 * k, stage1, (t, k)) for t in range(ng) for k in range(2)]
    plan += [(t + 2.2, stage2, (t,)) for t in range(ng)]
    plan += [(t + 1.15, along0, (t,)) for t in range(last)]
    plan += [(last + 1.3, corner0, ()), (last + 2.19, corner1, ()), (last + 2.4, corner2, ())]
    plan += [(0.3, first_norm, ()), (0.9, vec_step, (0,)), (2.0, vec_step, (1,)), (3.0, vec_first_line, ())]
    plan += [(3.1 + 0.55 * n, vec_next_line, (n,)) for n in range(1, ng)]
    plan += [(last + 2.17, vec_out, ())]
    for _, step, args in sorted(plan, key=lambda e: e[0]):
        step(*args)

    @pl.when(g > 0)
    def _():
        arrived(rz.at[g], wz.at[g])

    @pl.when(g < ng - 1)
    def _():
        arrived(rz.at[ng], wz.at[ng])

    @pl.when((g > 0) & (g < ng - 1))
    def _():
        @pl.loop(0, flat)
        def _(i):
            out_ref[i] = mine[g, 0, i].astype(F32) + rz[g, i].astype(F32) + rz[ng, i].astype(F32)

    @pl.when(g == 0)
    def _():
        @pl.loop(0, flat)
        def _(i):
            out_ref[i] = mine[g, 0, i].astype(F32) + rz[ng, i].astype(F32)

    @pl.when((g > 0) & (g == ng - 1))
    def _():
        @pl.loop(0, flat)
        def _(i):
            out_ref[i] = mine[g, 0, i].astype(F32) + rz[g, i].astype(F32)

    for i in range(flat, count):
        out_ref[i] = mine[g, 0, i].astype(F32)

    for t in range(ng):
        gz = order(t)
        for c in range(4):
            to_sibling(gz, c).wait_send()
        for n in range(4):
            copy1(n, gz).wait_send()
        for n in range(2):
            copy2(n, gz).wait_send()
        if t < ng - 1:
            arrived(flat_part(gz), sz.at[gz])
            arrived(corner_part(gz), sc.at[gz])
    input_grad.wait()
    for n in range(6):
        copy3(n).wait_send()
    for n in range(3):
        vec_copy(n).wait_send()
    for n in range(ng):
        gz = near_order(n, g, ng)

        @pl.when((gz <= g) & (g < ng - 1))
        def _():
            vec_line(gz, True).wait_send()

        @pl.when((gz >= g) & (g > 0))
        def _():
            vec_line(gz, False).wait_send()


def run_scatter(grads, sums2, vec, vin, cat, x, dx1, wq, ng, nd, rate):
    blocks, side, _ = grads.shape
    count = blocks // (ng * nd)
    na, nb, nc1, nc2 = slot_cuts(count)
    flat = na + nb
    dma = pltpu.SemaphoreType.DMA

    def buf(*lead):
        return pltpu.VMEM(lead + (side, side), BF16)

    def like(v):
        return pltpu.VMEM(v.shape, v.dtype)

    return pl.pallas_call(
        functools.partial(scatter_kernel, ng=ng, nd=nd, rate=rate),
        out_shape=(
            sds((count, side, side), F32),
            sds(vin.shape, F32),
            sds(vin.shape, F32),
            sds(dx1.shape, F32),
        ),
        in_specs=[hbm(), vmem(), vmem(), vmem()] + [hbm()] * 4,
        out_specs=(vmem(), vmem(), vmem(), hbm()),
        scratch_shapes=[
            like(cat),
            like(x),
            like(dx1),
            like(wq),
            like(dx1),
            dma((5,)),
            buf(ng, 4, count),
            buf(ng, 4, count),
            buf(ng, 2, na),
            buf(ng, 2, nb),
            buf(ng, na),
            buf(ng, nb),
            buf(ng + 1, flat),
            buf(ng + 1, 4, nc1 + nc2),
            buf(2, nc1),
            buf(2, nc2),
            buf(nc1),
            buf(nc2),
            pltpu.VMEM((4,) + vec.shape, F32),
            pltpu.VMEM((3,) + vec.shape, F32),
            pltpu.VMEM((ng,) + vec.shape, F32),
            dma((ng, 4)),
            dma((ng, 4)),
            dma((ng, 4)),
            dma((4, ng)),
            dma((4, ng)),
            dma((2, ng)),
            dma((2, ng)),
            dma((ng,)),
            dma((ng + 1,)),
            dma((ng,)),
            dma((ng + 1,)),
            dma((6,)),
            dma((6,)),
            dma((3 + 2 * ng,)),
            dma((3 + ng,)),
        ],
        compiler_params=params(61, collective_id=1, has_side_effects=True),
        name="scatter",
    )(grads, sums2, vec, vin, cat, x, dx1, wq)


def blocks_kernel(*refs, handed):
    g_ref, w_ref, ls_ref, rs_ref, lr_ref, rr_ref = refs[:6]
    wg_out, nl_out, nr_out, nw_out = refs[6 + handed:10 + handed]
    for n in range(handed):
        refs[10 + handed + n][...] = refs[6 + n][...]

    for i in range(g_ref.shape[0]):
        grad = g_ref[i]
        wg_out[i] = grad
        hi = grad.astype(BF16)
        low = (grad - hi.astype(F32)).astype(BF16)
        nl_out[i] = 0.5 * ls_ref[i] + 0.5 * dot_nt(hi, hi)
        turned = grad.T
        hi_t = turned.astype(BF16)
        nr_out[i] = 0.5 * rs_ref[i] + 0.5 * dot_nt(hi_t, hi_t)
        left = lr_ref[i]
        left_hi = left.astype(BF16)
        left_low = (left - left_hi.astype(F32)).astype(BF16)
        shaped = dot_nn(left_hi, hi) + dot_nn(left_hi, low) + dot_nn(left_low, hi)
        right = rr_ref[i]
        right_hi = right.astype(BF16)
        right_low = (right - right_hi.astype(F32)).astype(BF16)
        sh_hi = shaped.astype(BF16)
        sh_low = (shaped - sh_hi.astype(F32)).astype(BF16)
        shaped = dot_nn(sh_hi, right_hi) + dot_nn(sh_low, right_hi) + dot_nn(sh_hi, right_low)
        nw_out[i] = w_ref[i] - weight_rate * shaped


def run_blocks(grads, weights, left_stats, right_stats, left_roots, right_roots, *passing):
    count, side, _ = grads.shape
    steps = math.gcd(count, 4)
    step = count // steps
    spec = pl.BlockSpec((step, side, side), lambda n: (n, 0, 0))
    through = []
    for v in passing:
        part = v.shape[0] // steps
        if part % 8 == 0:
            through.append(pl.BlockSpec((part, v.shape[1]), lambda n: (n, 0)))
        else:
            through.append(pl.BlockSpec(v.shape, lambda n: (0, 0)))
    return pl.pallas_call(
        functools.partial(blocks_kernel, handed=len(passing)),
        grid=(steps,),
        out_shape=tuple([sds(grads.shape, F32)] * 4) + tuple(sds(v.shape, v.dtype) for v in passing),
        in_specs=[spec] * 6 + through,
        out_specs=tuple([spec] * 4) + tuple(through),
        compiler_params=params(),
        name="blocks",
    )(grads, weights, left_stats, right_stats, left_roots, right_roots, *passing)


def local(
    inputs,
    cotangent,
    weight_slots,
    slot_block,
    left_stats,
    right_stats,
    left_roots,
    right_roots,
    vectors,
    span_start,
):
    seq_count, tok_count, width = inputs.shape
    rows = seq_count * tok_count
    nd = lax.axis_size("dev")
    ng = lax.axis_size("grp")
    side = weight_slots.shape[1]
    hpd = H // nd
    lanes = width // nd
    head = lax.axis_index("dev") * hpd + jnp.arange(hpd, dtype=jnp.int32)
    slopes = jnp.exp2(-8.0 * (head.astype(F32) + 1.0) / H)
    vin = vectors.reshape(-1, 128)
    held = slot_block.reshape(-1, 128)
    x = inputs.reshape(rows, width)
    dy = cotangent.reshape(rows, width)
    rate = vector_rate / math.sqrt(rows * nd * ng)

    direct = nd == 8
    if direct:
        gath, h1, slot_of, vec = run_gather(weight_slots, x, held, vin, ng, nd)
    else:
        gath = lax.all_gather(weight_slots.astype(BF16), ("grp", "dev"), axis=0, tiled=True)
        h1, slot_of, vec = run_prepare(x, held, vin)
    qkv, wq = run_qkv(slot_of, h1, vec, gath, nd)
    qkv, o, o32, lse = run_attn_fwd(
        span_start, slopes, qkv.reshape(nd, 3, seq_count, tok_count, lanes), hpd
    )
    att = side_by_side(o, 1, rows)
    act, dx1, do, sums2, grads = run_mlp(slot_of, att, x, dy, vec, gath, nd)
    do = do.reshape(nd, seq_count, tok_count, lanes)
    cat = side_by_side(run_attn_bwd(span_start, slopes, qkv, do, o32, lse, hpd), 3, rows)
    grads = run_wgrad(slot_of, h1, cat, grads)
    if direct:
        weight_grads, vector_grads, new_vectors, ig = run_scatter(
            grads, sums2, vec, vin, cat, x, dx1, wq, ng, nd, rate
        )
        passing = (ig, vector_grads, new_vectors)
    else:
        ig, vsum = run_dh1(cat, x, dx1, vec, wq, sums2)
        vector_grads = lax.psum(vsum.reshape(-1), ("grp", "dev"))
        new_vectors = vectors - rate * vector_grads
        weight_grads = lax.psum_scatter(grads, ("grp", "dev"), scatter_dimension=0, tiled=True)
        weight_grads = weight_grads.astype(F32)
        passing = ()
    weight_grads, new_left, new_right, new_weights, *passed = run_blocks(
        weight_grads, weight_slots, left_stats, right_stats, left_roots, right_roots, *passing
    )
    if direct:
        ig, vector_grads, new_vectors = passed
    return (
        act.reshape(inputs.shape),
        ig.reshape(inputs.shape),
        weight_grads,
        new_left,
        new_right,
        new_weights,
        vector_grads.reshape(-1),
        new_vectors.reshape(-1),
    )


def solution(mesh):
    return jax.shard_map(
        local,
        mesh=mesh,
        in_specs=(
            P("grp", "dev", None),
            P("grp", "dev", None),
            P(("grp", "dev"), None, None),
            P(),
            P(("grp", "dev"), None, None),
            P(("grp", "dev"), None, None),
            P(("grp", "dev"), None, None),
            P(("grp", "dev"), None, None),
            P(),
            P("grp"),
        ),
        out_specs=(
            P("grp", "dev", None),
            P("grp", "dev", None),
            P(("grp", "dev"), None, None),
            P(("grp", "dev"), None, None),
            P(("grp", "dev"), None, None),
            P(("grp", "dev"), None, None),
            P(),
            P(),
        ),
        check_vma=False,
    )
```

```python
import functools
import math

import jax
import jax.numpy as jnp
from jax import lax
from jax.experimental import pallas as pl
from jax.experimental.pallas import tpu as pltpu
from jax.sharding import PartitionSpec as P

H = 16
FF = 4096
PIC = 256

eps = 1e-05
weight_rate = 0.5
vector_rate = 0.5
big_negative = -1e30
highest = lax.Precision.HIGHEST
F32 = jnp.float32
BF16 = jnp.bfloat16
LOG2E = 1.4426950408889634
MIB = 1024 * 1024

GAIN1, SHIFT1, BQ, BV, BO, GAIN2, SHIFT2, BDOWN, BUP = range(9)


def dot_nn(a, b):
    return lax.dot_general(a, b, (((1,), (0,)), ((), ())), preferred_element_type=F32)


def dot_nt(a, b):
    return lax.dot_general(a, b, (((1,), (1,)), ((), ())), preferred_element_type=F32)


def turn(v):
    return v.astype(F32).T.astype(BF16)


def vmem():
    return pl.BlockSpec(memory_space=pltpu.VMEM)


def smem():
    return pl.BlockSpec(memory_space=pltpu.SMEM)


def hbm():
    return pl.BlockSpec(memory_space=pl.ANY)


def sds(shape, dtype):
    return jax.ShapeDtypeStruct(shape, dtype)


def params(mib=58, **kw):
    return pltpu.CompilerParams(vmem_limit_bytes=mib * MIB, **kw)


def layer_stats(v):
    middle = jnp.mean(v, axis=-1, keepdims=True)
    centred = v - middle
    spread = jnp.mean(centred * centred, axis=-1, keepdims=True)
    return centred, lax.rsqrt(spread + eps)


def fold_rows(v):
    return jnp.sum(v.reshape(v.shape[0] // 8, 8, v.shape[1]), axis=0)


def slot_at(slot_ref, block):
    lanes = slot_ref.shape[1]
    if isinstance(block, int):
        return slot_ref[block // lanes, block % lanes]
    return slot_ref[lax.div(block, lanes), lax.rem(block, lanes)]


def fetch_block(gath, slot, dst, row, col, sem, side):
    return pltpu.make_async_copy(
        gath.at[slot], dst.at[pl.ds(row, side), pl.ds(col, side)], sem
    )


def prepare(x_ref, block_ref, vin_ref, h1_ref, slot_ref, vec_ref):
    rows, width = x_ref.shape
    per = width // 128
    for r in range(vec_ref.shape[0]):
        for c in range(per):
            vec_ref[r:r + 1, c * 128:(c + 1) * 128] = vin_ref[per * r + c:per * r + c + 1, :]
    chunk = 128

    @pl.loop(0, rows // chunk)
    def _(r):
        at = pl.ds(pl.multiple_of(r * chunk, chunk), chunk)
        centred, inv = layer_stats(x_ref[at, :].astype(F32))
        h1_ref[at, :] = (
            centred * inv * vec_ref[GAIN1:GAIN1 + 1, :] + vec_ref[SHIFT1:SHIFT1 + 1, :]
        ).astype(BF16)

    tiles, lanes = slot_ref.shape
    line = lax.broadcasted_iota(jnp.int32, (8, lanes), 0)
    lane = lax.broadcasted_iota(jnp.int32, (8, lanes), 1).astype(F32)
    block = lax.broadcasted_iota(jnp.int32, (lanes, lanes), 0)
    for t in range(tiles):
        found = jnp.zeros((8, lanes), F32)
        for r in range(tiles):
            held = (block_ref[r:r + 1, :] == block + t * lanes).astype(F32).astype(BF16)
            found = found + dot_nt(jnp.where(line == 0, lane, float(r)).astype(BF16), held)
        slot_ref[t:t + 1, :] = (found[0:1] + float(lanes) * found[1:2]).astype(jnp.int32)


def prepared_shapes(x, blocks, vin):
    rows, width = x.shape
    return (
        sds((rows, width), BF16),
        sds(blocks.shape, jnp.int32),
        sds((vin.size // width, width), F32),
    )


def run_prepare(x, blocks, vin):
    return pl.pallas_call(
        prepare,
        out_shape=prepared_shapes(x, blocks, vin),
        in_specs=[vmem()] * 3,
        out_specs=tuple([vmem()] * 3),
        compiler_params=params(),
        name="prepare",
    )(x, blocks, vin)


def qkv_kernel(slot_ref, h1_ref, vec_ref, gath, out_ref, wq_out, wbuf, sems, sem_w, *, nd):
    rows, width = h1_ref.shape
    side = gath.shape[1]
    per = width // side
    lanes = out_ref.shape[3]
    for part in range(3):
        for i in range(per):
            for j in range(per):
                slot = slot_at(slot_ref, i * 3 * per + part * per + j)
                fetch_block(gath, slot, wbuf.at[part], i * side, j * side, sems.at[part], side).start()

    def keep(part):
        return pltpu.make_async_copy(wbuf.at[part], wq_out.at[part], sem_w.at[part])

    for part in range(3):
        pltpu.make_async_copy(wbuf.at[part], wbuf.at[part], sems.at[part]).wait()
        keep(part).start()
        for half in range(2):
            cols = slice(half * width // 2, (half + 1) * width // 2)
            res = dot_nn(h1_ref[...], wbuf[part, :, cols])
            if part == 0:
                res = res + vec_ref[BQ:BQ + 1, cols]
            if part == 2:
                res = res + vec_ref[BV:BV + 1, cols]
            res = res.astype(BF16)
            for d in range(nd // 2):
                out_ref[half * (nd // 2) + d, part, :, :] = res[:, d * lanes:(d + 1) * lanes]
    for part in range(3):
        keep(part).wait()


def run_qkv(slot_of, h1, vec, gath, nd):
    rows, width = h1.shape
    lanes = width // nd
    return pl.pallas_call(
        functools.partial(qkv_kernel, nd=nd),
        out_shape=(sds((nd, 3, rows, lanes), BF16), sds((3, width, width), BF16)),
        in_specs=[smem(), vmem(), vmem(), hbm()],
        out_specs=(vmem(), hbm()),
        scratch_shapes=[
            pltpu.VMEM((3, width, width), BF16),
            pltpu.SemaphoreType.DMA((3,)),
            pltpu.SemaphoreType.DMA((3,)),
        ],
        compiler_params=params(),
        name="qkv",
    )(slot_of, h1, vec, gath)


MESH = pl.DeviceIdType.MESH


def remote(src, dst, send, recv, device):
    return pltpu.make_async_remote_copy(
        src_ref=src, dst_ref=dst, send_sem=send, recv_sem=recv, device_id=device, device_id_type=MESH
    )


def arrived(ref, sem):
    pltpu.make_async_copy(ref, ref, sem).wait()


def cut(ref, first, size):
    return ref.at[pl.ds(first, size)]


def greet_plane(g, d, nd):
    barrier = pltpu.get_barrier_semaphore()
    for p in range(1, nd):
        pl.semaphore_signal(barrier, inc=1, device_id=(g, lax.rem(d + p, nd)), device_id_type=MESH)
    pl.semaphore_wait(barrier, nd - 1)


def landing(ref, part, source, q, tok, lanes, parts):
    if lanes % 128 == 0:
        first = (part * (ref.shape[1] // parts)) + source * lanes
        return ref.at[pl.ds(q * tok, tok), pl.ds(pl.multiple_of(first, lanes), lanes)]
    return ref.at[source, part, q]


def landing_shape(parts, nb, seqs, tok, lanes):
    if lanes % 128 == 0:
        return sds((seqs * tok, parts * nb * lanes), BF16)
    return sds((nb, parts, seqs, tok, lanes), BF16)


def side_by_side(got, parts, rows):
    if got.ndim == 2:
        return got
    nb, _, seqs, tok, lanes = got.shape
    return got.transpose(2, 3, 1, 0, 4).reshape(rows, parts * nb * lanes)


def parts3(v):
    hi = v.astype(BF16)
    mid = (v - hi.astype(F32)).astype(BF16)
    lo = (v - hi.astype(F32) - mid.astype(F32)).astype(BF16)
    return hi.astype(F32), mid.astype(F32), lo.astype(F32)


def own_lanes(h, shape, hpd, lanes):
    lane = lax.broadcasted_iota(jnp.int32, shape, 1)
    size = lanes // hpd
    return (lane >= h * size) & (lane < (h + 1) * size)


def place(values, base, tok, width):
    lane = lax.broadcasted_iota(jnp.int32, (tok, width), 1)
    out = jnp.zeros((tok, width), F32)
    for n, v in enumerate(values):
        out = jnp.where(lane == base + n, v, out)
    return out


def spare(h, hpd, lanes):
    return (lanes // hpd) * (1 - h) if hpd > 1 else 0


def column_tables(slope_ref, qbase, kbase, kfar, hpd, lanes):
    _, tok, _ = qbase.shape
    u = lax.broadcasted_iota(jnp.int32, (tok, 128), 0).astype(F32)
    for h in range(hpd):
        slope = slope_ref[h] * LOG2E
        base = spare(h, hpd, lanes)
        near = parts3(jnp.full((tok, 128), slope, F32))
        far = parts3(jnp.full((tok, 128), slope * tok, F32))
        qbase[h] = place(near + far, base, tok, 128)
        kbase[h] = place([u] * 3 + [0.0] * 3 + [1.0] * 3, base, tok, 128)
        kfar[h] = place([0.0] * 3 + [1.0] * 3, base, tok, 128)


def extra_lanes(columns, extra, h, hpd, lanes):
    lane = lax.broadcasted_iota(jnp.int32, columns.shape, 1)
    for n, v in enumerate(extra):
        columns = jnp.where(lane == spare(h, hpd, lanes) + 6 + n, v, columns)
    return columns


def q_columns(q, h, hpd, columns, extra):
    tok, lanes = q.shape
    scaled = q.astype(F32) * ((lanes // hpd) ** (-0.5) * LOG2E)
    hi = scaled.astype(BF16).astype(F32)
    low = scaled - hi
    if extra:
        columns = extra_lanes(columns, extra, h, hpd, lanes)
    if hpd > 1:
        own = own_lanes(h, (tok, lanes), hpd, lanes)
        return jnp.concatenate(
            [jnp.where(own, hi, 0.0), jnp.where(own, low, columns)], axis=1
        ).astype(BF16)
    return jnp.concatenate([hi, low, columns], axis=1).astype(BF16)


def k_columns(k, h, hpd, columns):
    tok, lanes = k.shape
    wide = k.astype(F32)
    if hpd > 1:
        own = own_lanes(h, (tok, lanes), hpd, lanes)
        return jnp.concatenate([wide, jnp.where(own, wide, columns)], axis=1).astype(BF16)
    return jnp.concatenate([wide, wide, columns], axis=1).astype(BF16)


def far_side(slope, tok):
    u = lax.broadcasted_iota(jnp.int32, (tok, tok), 0)
    t = lax.broadcasted_iota(jnp.int32, (tok, tok), 1)
    after = u > t
    return (
        jnp.where(after, big_negative, 0.0),
        jnp.where(after, (2.0 * slope) * (t - u).astype(F32), 0.0),
    )


def pair_tables(corr, h, mask, span):
    tok = mask.shape[0]
    for n, (one, two) in enumerate(((mask, mask), (span, mask), (mask, span))):
        corr[h, n, 0:tok, 0:tok] = one
        corr[h, n, tok:, tok:] = two
        corr[h, n, 0:tok, tok:] = jnp.zeros((tok, tok), F32)
        corr[h, n, tok:, 0:tok] = jnp.full((tok, tok), big_negative, F32)


def attn_fwd_kernel(
    span_ref, slope_ref, src, got_out, o_got, o32_out, lse_out,
    got, o32_ref, lse_ref, sem_w, qa, ka, vt, scores, weights, tops_ref, corr, qbase, kbase, kfar, o_out, ss, sr, os, orr, loc, *, hpd, nd
):
    nb, _, seqs, tok, lanes = got.shape
    size = lanes // hpd
    pair = 2 * tok
    strip = 32
    g = lax.axis_index("grp")
    d = lax.axis_index("dev")

    for q in range(seqs):
        pltpu.make_async_copy(src.at[d, :, q], got.at[d, :, q], loc.at[q]).start()
    greet_plane(g, d, nd)

    def kind_of(kind):
        return pl.ds(2 * kind, 2 - kind)

    def send(q, kind, p):
        to = lax.rem(d + p, nd)
        return remote(
            src.at[to, kind_of(kind), q], got.at[d, kind_of(kind), q],
            ss.at[q, kind, p], sr.at[q, kind, p], (g, to),
        )

    def send_all(q, kind):
        @pl.loop(1, nd)
        def _(p):
            send(q, kind, p).start()

    def have(q, kind):
        @pl.loop(1, nd)
        def _(p):
            arrived(got.at[lax.rem(d + nd - p, nd), kind_of(kind), q], sr.at[q, kind, p])

    send_all(0, 0)
    send_all(0, 1)

    def o_place(source, q):
        return landing(o_got, 0, source, q, tok, lanes, 1)

    def send_o(q, i, p):
        return remote(o_out.at[i, q], o_place(d, q), os.at[q, i], orr.at[q, p], (g, i))

    column_tables(slope_ref, qbase, kbase, kfar, hpd, lanes)
    for h in range(hpd):
        mask, span = far_side(slope_ref[h] * LOG2E, tok)
        pair_tables(corr, h, mask, span)

    def fold(v, how):
        return how(v.reshape(v.shape[0] // 8, 8, v.shape[1]), axis=0)

    def write(ref, out, n, q, third=False):
        if third:
            return pltpu.make_async_copy(ref.at[:, :, q], out.at[:, :, q], sem_w.at[n, q])
        return pltpu.make_async_copy(ref.at[:, q], out.at[:, q], sem_w.at[n, q])

    whole = scores.shape[1] > nb // 2

    def tile_at(i, n):
        return (i * (i + 1)) // 2 + n if whole else n

    @pl.loop(0, seqs)
    def _(q):
        pltpu.make_async_copy(src.at[d, :, q], got.at[d, :, q], loc.at[q]).wait()
        start = span_ref[q]

        def score(i):
            flag = (start == i * pair).astype(jnp.int32) + 2 * (start == i * pair + tok).astype(jnp.int32)
            at_i = slice(i * pair, (i + 1) * pair)
            for h in range(hpd):
                top = None
                for n in range(i + 1):
                    at = tile_at(i, n)
                    scores[h, at] = dot_nt(ka[h, n * pair:(n + 1) * pair, :], qa[h, at_i, :])
                    for r in range(0, pair, strip):
                        rows = slice(r, r + strip)
                        v = scores[h, at, rows, :]
                        if n == i:
                            v = v + corr[h, flag, rows, :]
                            scores[h, at, rows, :] = v
                        here = fold(v, jnp.max)
                        top = here if top is None else jnp.maximum(top, here)
                tops_ref[h, i] = jnp.broadcast_to(jnp.max(top, axis=0, keepdims=True), (8, pair))

        have(q, 0)

        @pl.when(q + 1 < seqs)
        def _():
            send_all(q + 1, 0)

        @pl.loop(0, nb)
        def _(j):
            at_j = pl.ds(pl.multiple_of(j * tok, tok), tok)
            block = jnp.full((tok, 128), j, jnp.int32).astype(F32)
            for h in range(hpd):
                qa[h, at_j, :] = q_columns(got[j, 0, q], h, hpd, qbase[h], [])
                ka[h, at_j, :] = k_columns(got[j, 1, q], h, hpd, kbase[h] + block * kfar[h])

        if whole:
            for i in range(nb // 2):
                score(i)
        have(q, 1)

        @pl.when(q + 1 < seqs)
        def _():
            send_all(q + 1, 1)

        write(got, got_out, 0, q, True).start()

        @pl.loop(0, nb)
        def _(j):
            vt[0:lanes, pl.ds(pl.multiple_of(j * tok, tok), tok)] = turn(got[j, 2, q])

        for i in range(nb // 2):
            if not whole:
                score(i)
            outs = []
            logs = []
            for h in range(hpd):
                acc = total = None
                top = tops_ref[h, i][0:1]
                for n in range(i + 1):
                    at = tile_at(i, n)
                    for r in range(0, pair, strip):
                        rows = slice(r, r + strip)
                        p = jnp.exp2(scores[h, at, rows, :] - top)
                        here = fold(p, jnp.sum)
                        total = here if total is None else total + here
                        weights[h, n % 2, rows, :] = p.astype(BF16)
                    part = dot_nn(vt[h * size:(h + 1) * size, n * pair:(n + 1) * pair], weights[h, n % 2])
                    acc = part if acc is None else acc + part
                total = jnp.sum(total, axis=0, keepdims=True)
                outs.append(acc / total)
                logs.append(jnp.broadcast_to(top + jnp.log2(total), (128 // hpd, pair)))
            out = (jnp.concatenate(outs, axis=0) if hpd > 1 else outs[0]).T
            log = (jnp.concatenate(logs[::-1], axis=0) if hpd > 1 else logs[0]).T
            for k in range(2):
                at = 2 * i + k
                o32_ref[at, q] = out[k * tok:(k + 1) * tok]
                o_out[at, q] = out[k * tok:(k + 1) * tok].astype(BF16)
                lse_ref[at, q] = log[k * tok:(k + 1) * tok]

                @pl.when(at == d)
                def _():
                    pltpu.make_async_copy(o_out.at[at, q], o_place(d, q), os.at[q, at]).start()

                @pl.when(at != d)
                def _():
                    send_o(q, at, lax.rem(at - d + nd, nd)).start()

        write(o32_ref, o32_out, 1, q).start()
        write(lse_ref, lse_out, 2, q).start()

    for q in range(seqs):
        @pl.loop(1, nd)
        def _(p):
            arrived(o_place(lax.rem(d + nd - p, nd), q), orr.at[q, p])
            send(q, 0, p).wait_send()
            send(q, 1, p).wait_send()

        @pl.loop(0, nd)
        def _(i):
            arrived(o_out.at[i, q], os.at[q, i])
        write(got, got_out, 0, q, True).wait()
        write(o32_ref, o32_out, 1, q).wait()
        write(lse_ref, lse_out, 2, q).wait()


def run_attn_fwd(span, slopes, qkv, hpd):
    nb, _, seqs, tok, lanes = qkv.shape
    t = nb * tok
    pairs = nb // 2
    tiles = pairs * (pairs + 1) // 2
    if hpd * tiles > 24:
        tiles = pairs
    dma = pltpu.SemaphoreType.DMA
    return pl.pallas_call(
        functools.partial(attn_fwd_kernel, hpd=hpd, nd=nb),
        out_shape=(
            sds(qkv.shape, BF16),
            landing_shape(1, nb, seqs, tok, lanes),
            sds((nb, seqs, tok, lanes), F32),
            sds((nb, seqs, tok, 128), F32),
        ),
        in_specs=[smem(), smem(), hbm()],
        out_specs=(hbm(), vmem(), hbm(), hbm()),
        scratch_shapes=[
            pltpu.VMEM(qkv.shape, BF16),
            pltpu.VMEM((nb, seqs, tok, lanes), F32),
            pltpu.VMEM((nb, seqs, tok, 128), F32),
            dma((3, seqs)),
            pltpu.VMEM((hpd, t, 256), BF16),
            pltpu.VMEM((hpd, t, 256), BF16),
            pltpu.VMEM((lanes, t), BF16),
            pltpu.VMEM((hpd, tiles, 2 * tok, 2 * tok), F32),
            pltpu.VMEM((hpd, 2, 2 * tok, 2 * tok), BF16),
            pltpu.VMEM((hpd, nb // 2, 8, 2 * tok), F32),
            pltpu.VMEM((hpd, 3, 2 * tok, 2 * tok), F32),
            pltpu.VMEM((hpd, tok, 128), F32),
            pltpu.VMEM((hpd, tok, 128), F32),
            pltpu.VMEM((hpd, tok, 128), F32),
            pltpu.VMEM((nb, seqs, tok, lanes), BF16),
            dma((seqs, 2, nb)),
            dma((seqs, 2, nb)),
            dma((seqs, nb)),
            dma((seqs, nb)),
            dma((seqs,)),
        ],
        compiler_params=params(collective_id=2, has_side_effects=True),
        name="attn_fwd",
    )(span, slopes, qkv)


def attn_bwd_kernel(
    span_ref, slope_ref, qkv_in, do_src, o32_in, lse_in, got,
    qkv_ref, o32_ref, lse_ref, sem_in, do_got, out, qa, ka, kt, va, qm, da, dm, dqt, corr, qbase, kbase, kfar,
    s_ref, dp_ref, p_ref, ds_ref, ss, sr, gs, gr, loc, *, hpd, nd
):
    nb, _, seqs, tok, lanes = qkv_ref.shape
    inputs = [
        pltpu.make_async_copy(qkv_in, qkv_ref, sem_in.at[0]),
        pltpu.make_async_copy(lse_in, lse_ref, sem_in.at[1]),
        pltpu.make_async_copy(o32_in, o32_ref, sem_in.at[2]),
    ]
    for copy in inputs:
        copy.start()
    size = lanes // hpd
    unit = size ** (-0.5)
    pair = 2 * tok
    strip = 32
    g = lax.axis_index("grp")
    d = lax.axis_index("dev")

    def own_copy(q):
        return pltpu.make_async_copy(do_src.at[d, q], do_got.at[d, q], loc.at[q])

    for q in range(seqs):
        own_copy(q).start()
    greet_plane(g, d, nd)

    def send(q, p):
        to = lax.rem(d + p, nd)
        return remote(do_src.at[to, q], do_got.at[d, q], ss.at[q, p], sr.at[q, p], (g, to))

    def send_all(q):
        @pl.loop(1, nd)
        def _(p):
            send(q, p).start()

    send_all(0)

    def place_back(kind, source, q):
        return landing(got, kind, source, q, tok, lanes, 3)

    def back(q, kind, p):
        to = lax.rem(d + p, nd)
        return remote(
            out.at[to, kind, q], place_back(kind, d, q), gs.at[q, kind, p], gr.at[q, kind, p], (g, to)
        )

    def back_own(q, kind):
        return pltpu.make_async_copy(out.at[d, kind, q], place_back(kind, d, q), gs.at[q, kind, 0])

    for h in range(hpd):
        mask, span = far_side(slope_ref[h] * LOG2E, tok)
        pair_tables(corr, h, mask, span)
    column_tables(slope_ref, qbase, kbase, kfar, hpd, lanes)
    row = lax.broadcasted_iota(jnp.int32, (lanes, lanes), 0) // size
    col = lax.broadcasted_iota(jnp.int32, (lanes, lanes), 1) // size
    across = (row == hpd - 1 - col).astype(F32).astype(BF16)
    for copy in inputs:
        copy.wait()

    @pl.loop(0, seqs)
    def _(q):
        @pl.loop(0, nb)
        def _(j):
            at_j = pl.ds(pl.multiple_of(j * tok, tok), tok)
            qj = qkv_ref[j, 0, q]
            kj = qkv_ref[j, 1, q]
            vj = qkv_ref[j, 2, q].astype(F32)
            kt[:, at_j] = kj.astype(F32).T.astype(BF16)
            dqt[:, at_j] = jnp.zeros((lanes, tok), F32)
            block = jnp.full((tok, 128), j, jnp.int32).astype(F32)
            low = [-p for p in parts3(lse_ref[j, q])]
            for h in range(hpd):
                qa[h, at_j, :] = q_columns(qj, h, hpd, qbase[h], low)
                ka[h, at_j, :] = k_columns(kj, h, hpd, kbase[h] + block * kfar[h])
                if hpd > 1:
                    own = own_lanes(h, (tok, lanes), hpd, lanes)
                    qm[h, at_j, :] = jnp.where(own, qj.astype(F32), 0.0).astype(BF16)
                    va[h, at_j, :] = jnp.where(own, vj, kbase[h]).astype(BF16)
                else:
                    qm[h, at_j, :] = qj
                    va[h, at_j, :] = jnp.concatenate([vj, kbase[h][:, 0:lanes]], axis=1).astype(BF16)

        own_copy(q).wait()

        @pl.loop(1, nd)
        def _(p):
            arrived(do_got.at[lax.rem(d + nd - p, nd), q], sr.at[q, p])

        @pl.when(q + 1 < seqs)
        def _():
            send_all(q + 1)

        @pl.loop(0, nb)
        def _(j):
            at_j = pl.ds(pl.multiple_of(j * tok, tok), tok)
            do = do_got[j, q].astype(F32)
            delta = jnp.zeros((tok, lanes), F32)
            for p in parts3(do * o32_ref[j, q]):
                delta = delta + dot_nn(p.astype(BF16), across)
            low = [-p for p in parts3(delta)]
            for h in range(hpd):
                if hpd > 1:
                    own = own_lanes(h, (tok, lanes), hpd, lanes)
                    none = jnp.where(own, do, 0.0)
                    da[h, at_j, :] = extra_lanes(none, low, h, hpd, lanes).astype(BF16)
                    dm[h, at_j, :] = none.astype(BF16)
                else:
                    extra = extra_lanes(jnp.zeros((tok, lanes), F32), low, h, hpd, lanes)
                    da[h, at_j, :] = jnp.concatenate([do, extra], axis=1).astype(BF16)
                    dm[h, at_j, :] = do.astype(BF16)

        start = span_ref[q]

        pairs = nb // 2

        def tile(j, i):
            at_j = slice(j * pair, (j + 1) * pair)
            at_i = slice(i * pair, (i + 1) * pair)
            flag = (start == j * pair).astype(jnp.int32) + 2 * (start == j * pair + tok).astype(jnp.int32)
            dk = dv = None
            for h in range(hpd):
                s_ref[h] = dot_nt(ka[h, at_j, :], qa[h, at_i, :])
                dp_ref[h] = dot_nt(va[h, at_j, :], da[h, at_i, :])
                for r in range(0, pair, strip):
                    rows = slice(r, r + strip)
                    s = s_ref[h, rows, :]
                    if i == j:
                        s = s + corr[h, flag, rows, :]
                    p = jnp.exp2(s)
                    p_ref[h, rows, :] = p.astype(BF16)
                    ds_ref[h, rows, :] = (p * dp_ref[h, rows, :]).astype(BF16)
                ds = ds_ref[h]
                dv_h = dot_nn(p_ref[h], dm[h, at_i, :])
                dk_h = dot_nn(ds, qm[h, at_i, :])
                dk = dk_h if dk is None else dk + dk_h
                dv = dv_h if dv is None else dv + dv_h
                rows = slice(h * size, (h + 1) * size)
                dqt[rows, at_i] += dot_nn(kt[rows, at_j], ds)
            return dk, dv

        @pl.loop(0, pairs)
        def _(n):
            turn_of = lax.rem(d // 2 + n, pairs)
            for case in range(pairs):
                @pl.when(turn_of == case)
                def _():
                    dk, dv = tile(case, case)
                    for i in range(case + 1, pairs):
                        more = tile(case, i)
                        dk = dk + more[0]
                        dv = dv + more[1]
                    for k in range(2):
                        half = slice(k * tok, (k + 1) * tok)
                        out[2 * case + k, 1, q] = (dk[half] * unit).astype(BF16)
                        out[2 * case + k, 2, q] = dv[half].astype(BF16)

            for k in range(2):
                j = 2 * turn_of + k
                for kind in (1, 2):
                    @pl.when(j == d)
                    def _():
                        back_own(q, kind).start()

                    @pl.when(j != d)
                    def _():
                        back(q, kind, lax.rem(j - d + nd, nd)).start()

        @pl.loop(0, nb)
        def _(n):
            j = lax.rem(d + n, nb)
            at_j = pl.ds(pl.multiple_of(j * tok, tok), tok)
            out[j, 0, q] = (dqt[:, at_j].T * unit).astype(BF16)

            @pl.when(n == 0)
            def _():
                back_own(q, 0).start()

            @pl.when(n > 0)
            def _():
                back(q, 0, n).start()

    for q in range(seqs):
        for kind in range(3):
            back_own(q, kind).wait()

        @pl.loop(1, nd)
        def _(p):
            send(q, p).wait_send()
            source = lax.rem(d + nd - p, nd)
            for kind in range(3):
                back(q, kind, p).wait_send()
                arrived(place_back(kind, source, q), gr.at[q, kind, p])


def run_attn_bwd(span, slopes, qkv, do, o32, lse, hpd):
    nb, _, seqs, tok, lanes = qkv.shape
    t = nb * tok
    dma = pltpu.SemaphoreType.DMA
    wide = 128 if hpd == 1 else lanes
    return pl.pallas_call(
        functools.partial(attn_bwd_kernel, hpd=hpd, nd=nb),
        out_shape=landing_shape(3, nb, seqs, tok, lanes),
        in_specs=[smem(), smem(), hbm(), hbm(), hbm(), hbm()],
        out_specs=vmem(),
        scratch_shapes=[
            pltpu.VMEM(qkv.shape, BF16),
            pltpu.VMEM(o32.shape, F32),
            pltpu.VMEM(lse.shape, F32),
            dma((3,)),
            pltpu.VMEM((nb, seqs, tok, lanes), BF16),
            pltpu.VMEM(qkv.shape, BF16),
            pltpu.VMEM((hpd, t, 256), BF16),
            pltpu.VMEM((hpd, t, 256), BF16),
            pltpu.VMEM((lanes, t), BF16),
            pltpu.VMEM((hpd, t, wide), BF16),
            pltpu.VMEM((hpd, t, lanes), BF16),
            pltpu.VMEM((hpd, t, wide), BF16),
            pltpu.VMEM((hpd, t, lanes), BF16),
            pltpu.VMEM((lanes, t), F32),
            pltpu.VMEM((hpd, 3, 2 * tok, 2 * tok), F32),
            pltpu.VMEM((hpd, tok, 128), F32),
            pltpu.VMEM((hpd, tok, 128), F32),
            pltpu.VMEM((hpd, tok, 128), F32),
            pltpu.VMEM((hpd, 2 * tok, 2 * tok), F32),
            pltpu.VMEM((hpd, 2 * tok, 2 * tok), F32),
            pltpu.VMEM((hpd, 2 * tok, 2 * tok), BF16),
            pltpu.VMEM((hpd, 2 * tok, 2 * tok), BF16),
            dma((seqs, nb)),
            dma((seqs, nb)),
            dma((seqs, 3, nb)),
            dma((seqs, 3, nb)),
            dma((seqs,)),
        ],
        compiler_params=params(collective_id=3, has_side_effects=True),
        name="attn_bwd",
    )(span, slopes, qkv, do, o32, lse)


def mlp_kernel(
    slot_ref, att_in, x_in, dy_in, vec_ref, gath,
    act_out, dx1_out, do_out, sums_ref, grads,
    att_ref, x_ref, dy_ref, sem_in, wo, wup, wdn, x1, acc, dh2, h2_ref, h2t, attt, act_ref, z_ref, dg_ref, g_ref, dz_ref, do_ref, stage,
    sem_o, sem_t, sem_g, sem_w, *, nd, first_o, first_up, first_dn, tile
):
    rows, width = x_ref.shape
    side = gath.shape[1]
    per = width // side
    ff = sums_ref.shape[0] // 8 * width - 4 * width
    tiles = ff // tile
    cols = tile // side
    lanes = do_ref.shape[2]
    fper = ff // side
    inputs = [
        pltpu.make_async_copy(att_in, att_ref, sem_in.at[0]),
        pltpu.make_async_copy(x_in, x_ref, sem_in.at[1]),
        pltpu.make_async_copy(dy_in, dy_ref, sem_in.at[2]),
    ]
    for copy in inputs:
        copy.start()

    for i in range(per):
        for j in range(per):
            fetch_block(gath, slot_at(slot_ref, first_o + i * per + j), wo, i * side, j * side, sem_o.at[0], side).start()

    ring = wup.shape[0]

    def fetch_tile(f):
        at = f % ring
        for i in range(per):
            for j in range(cols):
                fetch_block(gath, slot_at(slot_ref, first_up + i * fper + f * cols + j), wup.at[at], i * side, j * side, sem_t.at[at], side).start()
            for j in range(cols):
                fetch_block(gath, slot_at(slot_ref, first_dn + (f * cols + j) * per + i), wdn.at[at], j * side, i * side, sem_t.at[at], side).start()

    for f in range(min(ring, tiles)):
        fetch_tile(f)
    for copy in inputs:
        copy.wait()
    for r in range(width // 256):
        attt[r * 256:(r + 1) * 256, :] = turn(att_ref[:, r * 256:(r + 1) * 256])
    pltpu.make_async_copy(wo, wo, sem_o.at[0]).wait()
    for half in range(2):
        c = slice(half * width // 2, (half + 1) * width // 2)
        x1[:, c] = x_ref[:, c].astype(F32) + dot_nn(att_ref[...], wo[:, c]) + vec_ref[BO:BO + 1, c]

    chunk = 128

    def rows_at(r):
        return pl.ds(pl.multiple_of(r * chunk, chunk), chunk)

    @pl.loop(0, rows // chunk)
    def _(r):
        at = rows_at(r)
        centred, inv = layer_stats(x1[at, :])
        h2_ref[at, :] = (centred * inv * vec_ref[GAIN2:GAIN2 + 1, :] + vec_ref[SHIFT2:SHIFT2 + 1, :]).astype(BF16)
        acc[at, :] = x1[at, :] + vec_ref[BDOWN:BDOWN + 1, :]
        dh2[at, :] = jnp.zeros((chunk, width), F32)

    for r in range(width // 256):
        h2t[r * 256:(r + 1) * 256, :] = turn(h2_ref[:, r * 256:(r + 1) * 256])

    def put(slot, first, res, down, across):
        for i in range(down):
            for j in range(across):
                stage[slot, first + i * across + j] = res[i * side:(i + 1) * side, j * side:(j + 1) * side]

    def leave(slot, n, block):
        pltpu.make_async_copy(stage.at[slot, n], grads.at[slot_at(slot_ref, block)], sem_g.at[slot]).start()

    def left(slot, size):
        at = stage.at[slot, pl.ds(0, size)]
        pltpu.make_async_copy(at, at, sem_g.at[slot]).wait()

    full = 2 * per * cols
    piece = 512
    per_piece = piece // side
    strip = 16

    def pieces(size):
        return [slice(k * piece, (k + 1) * piece) for k in range(size // piece)]

    def into_tile(f):
        at = f % ring
        arrived(wup.at[at], sem_t.at[at])
        arrived(wdn.at[at], sem_t.at[at])
        for c in pieces(tile):
            z_ref[:, c] = dot_nn(h2_ref[...], wup[at, :, c])
            dg_ref[:, c] = dot_nt(dy_ref[...], wdn[at, c, :])

    def gelu_strips(f, first, last):
        total = None
        for r in range(first, last, strip):
            at = slice(r, r + strip)
            z = z_ref[at, :] + vec_ref[BUP + f:BUP + f + 1, :]
            z2 = z * z
            th = jnp.tanh(z * (0.7978845608028654 + (0.7978845608028654 * 0.044715) * z2))
            half_more = 0.5 + 0.5 * th
            g_ref[f % 2, at, :] = (z * half_more).astype(BF16)
            slope = half_more + (0.5 * z) * (1.0 - th * th) * (
                0.7978845608028654 + (3.0 * 0.044715 * 0.7978845608028654) * z2
            )
            dz = (dg_ref[at, :] * slope).astype(BF16)
            dz_ref[f % 2, at, :] = dz
            here = fold_rows(dz.astype(F32))
            total = here if total is None else total + here
        at = slice(8 * (4 + f), 8 * (4 + f) + 8)
        if first == 0:
            sums_ref[at, :] = total
        else:
            sums_ref[at, :] += total

    def out_of_tile(f):
        at = f % ring
        slot = f % 2

        def up(c):
            acc[:, c] += dot_nn(g_ref[slot], wdn[at, :, c])
            dh2[:, c] += dot_nt(dz_ref[slot], wup[at, c, :])

        def grad_down(k, c):
            res = dot_nn(turn(g_ref[slot, :, c]), dy_ref[...]).astype(BF16)
            put(slot, k * per_piece * per, res, per_piece, per)

        def grad_up(k, c):
            res = dot_nn(h2t[c, :], dz_ref[slot]).astype(BF16)
            put(slot, per * cols + k * per_piece * cols, res, per_piece, cols)

        steps = [functools.partial(up, c) for c in pieces(width)]
        steps += [functools.partial(grad_down, k, c) for k, c in enumerate(pieces(tile))]
        steps += [functools.partial(grad_up, k, c) for k, c in enumerate(pieces(width))]
        return steps

    def send_tile(f):
        slot = f % 2
        for i in range(per):
            for j in range(cols):
                leave(slot, j * per + i, first_dn + (f * cols + j) * per + i)
            for j in range(cols):
                leave(slot, per * cols + i * cols + j, first_up + i * fper + f * cols + j)

    for f in range(tiles + 1):
        if f < tiles:
            into_tile(f)
        steps = out_of_tile(f - 1) if f > 0 else []
        if f > 2:
            left((f - 1) % 2, full)
        share = rows // max(len(steps), 1)
        if f < tiles:
            for n in range(max(len(steps), 1)):
                gelu_strips(f, n * share // strip * strip, rows if n + 1 >= len(steps) else (n + 1) * share // strip * strip)
                if steps:
                    steps[n]()
        else:
            for step in steps:
                step()
        if f > 0:
            send_tile(f - 1)
            if f - 1 + ring < tiles:
                fetch_tile(f - 1 + ring)

    zero = jnp.zeros((8, width), F32)
    da_ref = h2_ref
    dx1_ref = x1

    def finish(r, carry):
        s_bo, s_gain, s_shift, s_bdown = carry
        at = rows_at(r)
        act_ref[at, :] = acc[at, :].astype(BF16)
        centred, inv = layer_stats(x1[at, :])
        hat = centred * inv
        dh = dh2[at, :]
        dhg = dh * vec_ref[GAIN2:GAIN2 + 1, :]
        back = inv * (
            dhg
            - jnp.mean(dhg, axis=-1, keepdims=True)
            - hat * jnp.mean(dhg * hat, axis=-1, keepdims=True)
        )
        dy = dy_ref[at, :].astype(F32)
        dx1 = dy + back
        dx1_ref[at, :] = dx1
        da = dx1.astype(BF16)
        da_ref[at, :] = da
        return (
            s_bo + fold_rows(da.astype(F32)),
            s_gain + fold_rows(dh * hat),
            s_shift + fold_rows(dh),
            s_bdown + fold_rows(dy),
        )

    carry = lax.fori_loop(0, rows // chunk, finish, (zero, zero, zero, zero))
    for n in range(4):
        sums_ref[8 * n:8 * n + 8, :] = carry[n]
    outs = [
        pltpu.make_async_copy(act_ref, act_out, sem_w.at[0]),
        pltpu.make_async_copy(dx1_ref, dx1_out, sem_w.at[1]),
        pltpu.make_async_copy(do_ref, do_out, sem_w.at[2]),
    ]
    outs[0].start()
    outs[1].start()
    for half in range(2):
        c = slice(half * width // 2, (half + 1) * width // 2)
        res = dot_nt(da_ref[...], wo[c, :]).astype(BF16)
        for d in range(nd // 2):
            do_ref[half * (nd // 2) + d] = res[:, d * lanes:(d + 1) * lanes]
    outs[2].start()
    left(0, full)
    left(1, full)
    half_rows = width // 2
    for half in range(2):
        res = dot_nn(attt[half * half_rows:(half + 1) * half_rows, :], da_ref[...]).astype(BF16)
        put(half, 0, res, per // 2, per)

        for i in range(per // 2):
            for j in range(per):
                leave(half, i * per + j, first_o + (half * (per // 2) + i) * per + j)
    for half in range(2):
        left(half, per * per // 2)
    for copy in outs:
        copy.wait()


def run_mlp(slot_of, att, x, dy, vec, gath, nd):
    rows, width = x.shape
    side = gath.shape[1]
    lanes = width // nd
    per = width // side
    first_o = 3 * per * per
    first_up = first_o + per * per
    first_dn = first_up + per * (FF // side)
    tile = width
    f32_rows = pltpu.VMEM((rows, width), F32)
    bf16_rows = pltpu.VMEM((rows, width), BF16)
    turned = pltpu.VMEM((width, rows), BF16)
    return pl.pallas_call(
        functools.partial(
            mlp_kernel, nd=nd, first_o=first_o, first_up=first_up, first_dn=first_dn, tile=tile
        ),
        out_shape=(
            sds((rows, width), BF16),
            sds((rows, width), F32),
            sds((nd, rows, lanes), BF16),
            sds((8 * (4 + FF // width), width), F32),
            sds(gath.shape, BF16),
        ),
        in_specs=[smem(), hbm(), hbm(), hbm(), vmem(), hbm()],
        out_specs=(hbm(), hbm(), hbm(), vmem(), hbm()),
        scratch_shapes=[
            bf16_rows,
            bf16_rows,
            bf16_rows,
            pltpu.SemaphoreType.DMA((3,)),
            pltpu.VMEM((width, width), BF16),
            pltpu.VMEM((3, width, tile), BF16),
            pltpu.VMEM((3, tile, width), BF16),
            f32_rows,
            f32_rows,
            f32_rows,
            bf16_rows,
            turned,
            turned,
            bf16_rows,
            pltpu.VMEM((rows, tile), F32),
            pltpu.VMEM((rows, tile), F32),
            pltpu.VMEM((2, rows, tile), BF16),
            pltpu.VMEM((2, rows, tile), BF16),
            pltpu.VMEM((nd, rows, lanes), BF16),
            pltpu.VMEM((2, 2 * per * (tile // side), side, side), BF16),
            pltpu.SemaphoreType.DMA((1,)),
            pltpu.SemaphoreType.DMA((FF // tile,)),
            pltpu.SemaphoreType.DMA((2,)),
            pltpu.SemaphoreType.DMA((3,)),
        ],
        compiler_params=params(),
        name="mlp",
    )(slot_of, att, x, dy, vec, gath)


def dh1_dot(cat, w, dh1, part, half):
    width = dh1.shape[1]
    c = slice(half * width // 2, (half + 1) * width // 2)
    res = dot_nt(cat[:, part * width:(part + 1) * width], w[part, c, :])
    if part == 0:
        dh1[:, c] = res
    else:
        dh1[:, c] += res


def first_norm_back(cat, x, dh1, dx1, ig, vec_ref):
    rows, width = x.shape
    chunk = 128
    zero = jnp.zeros((8, width), F32)

    def finish(r, carry):
        s_gain, s_shift, s_bq, s_bv = carry
        at = pl.ds(pl.multiple_of(r * chunk, chunk), chunk)
        centred, inv = layer_stats(x[at, :].astype(F32))
        hat = centred * inv
        dh = dh1[at, :]
        dhg = dh * vec_ref[GAIN1:GAIN1 + 1, :]
        back = inv * (
            dhg
            - jnp.mean(dhg, axis=-1, keepdims=True)
            - hat * jnp.mean(dhg * hat, axis=-1, keepdims=True)
        )
        ig[at, :] = dx1[at, :] + back
        return (
            s_gain + fold_rows(dh * hat),
            s_shift + fold_rows(dh),
            s_bq + fold_rows(cat[at, 0:width].astype(F32)),
            s_bv + fold_rows(cat[at, 2 * width:3 * width].astype(F32)),
        )

    return lax.fori_loop(0, rows // chunk, finish, (zero, zero, zero, zero))


def vector_rows(first, sums2):
    rows = [jnp.sum(v, axis=0, keepdims=True) for v in first]
    rows += [jnp.sum(sums2[8 * n:8 * n + 8, :], axis=0, keepdims=True) for n in range(sums2.shape[0] // 8)]
    return rows


def dh1_kernel(cat_ref, x_ref, dx1_ref, vec_ref, wq_ref, sums2_ref, ig_ref, vsum_ref, dh1):
    for part in range(3):
        for half in range(2):
            dh1_dot(cat_ref, wq_ref, dh1, part, half)
    first = first_norm_back(cat_ref, x_ref, dh1, dx1_ref, ig_ref, vec_ref)
    for n, row in enumerate(vector_rows(first, sums2_ref)):
        vsum_ref[n:n + 1, :] = row


def run_dh1(cat, x, dx1, vec, wq, sums2):
    rows, width = x.shape
    return pl.pallas_call(
        dh1_kernel,
        out_shape=(sds((rows, width), F32), sds(vec.shape, F32)),
        in_specs=[vmem()] * 6,
        out_specs=(vmem(), vmem()),
        scratch_shapes=[pltpu.VMEM((rows, width), F32)],
        compiler_params=params(),
        name="dh1",
    )(cat, x, dx1, vec, wq, sums2)


def wgrad_kernel(slot_ref, h1_ref, cat_ref, rest, out, a_t, stage, sem_out, *, side, tile):
    del rest
    rows, width = h1_ref.shape
    per = width // side
    cols = tile // side
    steps = cat_ref.shape[1] // tile
    for r in range(width // 256):
        c = slice(r * 256, (r + 1) * 256)
        a_t[c, :] = turn(h1_ref[:, c])

    def left(slot):
        pltpu.make_async_copy(stage.at[slot], stage.at[slot], sem_out.at[slot]).wait()

    @pl.loop(0, steps)
    def _(t):
        slot = lax.rem(t, 2)

        @pl.when(t >= 2)
        def _():
            left(slot)
        res = dot_nn(a_t[...], cat_ref[:, pl.ds(pl.multiple_of(t * tile, tile), tile)]).astype(BF16)
        for i in range(per):
            for j in range(cols):
                stage[slot, i * cols + j] = res[i * side:(i + 1) * side, j * side:(j + 1) * side]

        for i in range(per):
            for j in range(cols):
                dst = slot_at(slot_ref, i * 3 * per + t * cols + j)
                pltpu.make_async_copy(stage.at[slot, i * cols + j], out.at[dst], sem_out.at[slot]).start()

    left(0)
    left(1)


def run_wgrad(slot_of, h1, cat, grads):
    rows, width = h1.shape
    side = grads.shape[1]
    tile = 512
    return pl.pallas_call(
        functools.partial(wgrad_kernel, side=side, tile=tile),
        out_shape=sds(grads.shape, BF16),
        in_specs=[smem(), vmem(), vmem(), hbm()],
        out_specs=hbm(),
        scratch_shapes=[
            pltpu.VMEM((width, rows), BF16),
            pltpu.VMEM((2, (width // side) * (tile // side), side, side), BF16),
            pltpu.SemaphoreType.DMA((2,)),
        ],
        input_output_aliases={3: 0},
        compiler_params=params(),
        name="wgrad",
    )(slot_of, h1, cat, grads)


def whereami():
    g = lax.axis_index("grp")
    d = lax.axis_index("dev")
    core = lax.rem(d, 2)
    x = lax.rem(d // 2, 2)
    y = d // 4
    over_x = d + 2 - 4 * x
    over_y = d + 4 - 8 * y
    across = over_x + 4 - 8 * y
    sibling = d + 1 - 2 * core
    return g, d, over_x, over_y, across, sibling


def near_order(t, g, ng):
    t = ng - 1 - t
    low = jnp.where(t < ng - 1 - g, ng - 1 - t, t - (ng - 1 - g))
    high = jnp.where(t < g, t, ng - 1 - (t - g))
    return jnp.where(2 * g < ng, low, high)


def greet(g, ng, peers):
    barrier = pltpu.get_barrier_semaphore()
    for peer in peers:
        pl.semaphore_signal(barrier, inc=1, device_id=(g, peer), device_id_type=MESH)

    d = lax.axis_index("dev")

    @pl.when(g > 0)
    def _():
        pl.semaphore_signal(barrier, inc=1, device_id=(g - 1, d), device_id_type=MESH)

    @pl.when(g < ng - 1)
    def _():
        pl.semaphore_signal(barrier, inc=1, device_id=(g + 1, d), device_id_type=MESH)

    ends = (g > 0).astype(jnp.int32) + (g < ng - 1).astype(jnp.int32)
    pl.semaphore_wait(barrier, len(peers) + ends)


def slot_cuts(count):
    third = 2 * (count // 12)
    first = (count - third) // 2
    return first, count - third - first, third // 2, third // 2


def gather_kernel(
    w_ref, x_ref, block_ref, vin_ref, out, h1_ref, slot_ref, vec_ref,
    own, local_sem, zs, zr, cs, cr, ss, sr, *, ng, nd
):
    count = w_ref.shape[0]
    na, nb, nc1, nc2 = slot_cuts(count)
    flat = na + nb
    nc = nc1 + nc2
    g, d, over_x, over_y, across, sibling = whereami()
    columns = (d, over_x, over_y, across)
    own[...] = w_ref[...].astype(BF16)
    greet(g, ng, (over_x, over_y, sibling))

    def region(gz, dev, first=0, size=count):
        return out.at[pl.ds((gz * nd + dev) * count + first, size)]

    def wide(t):
        return count if t == 0 else flat

    def kind(n, t):
        return (
            (d, 0, wide(t), over_x),
            (d, 0, wide(t), over_y),
            (d, 0, wide(t), sibling),
            (over_x, 0, na, over_y),
            (over_y, na, nb, over_x),
            (over_x, 0, wide(t), sibling),
            (over_y, 0, wide(t), sibling),
            (across, 0, na, sibling),
            (across, na, nb, sibling),
            (over_x, flat, nc1, over_y),
            (over_y, flat + nc1, nc2, over_x),
            (across, flat, nc1, sibling),
            (across, flat + nc1, nc2, sibling),
            (d, flat, nc, sibling),
            (over_x, flat, nc, sibling),
            (over_y, flat, nc, sibling),
            (across, flat, nc, sibling),
        )[n]

    def kinds(t):
        return range(13) if t == 0 else tuple(range(9)) + tuple(range(13, 17))

    def plane(n, t, src=None):
        gz = near_order(t, g, ng)
        dev, first, size, to = kind(n, t)
        at = region(gz, dev, first, size)
        return remote(at if src is None else src, at, ss.at[n, gz], sr.at[n, gz], (g, to))

    def landed(n, t, dev):
        gz = near_order(t, g, ng)
        _, first, size, _ = kind(n, t)
        arrived(region(gz, dev, first, size), sr.at[n, gz])

    def line(gz, up, src=None):
        at = region(gz, d, 0, flat)
        to = g + 1 if up else g - 1
        return remote(at if src is None else src, at, zs.at[gz, int(up)], zr.at[gz], (to, d))

    def corner_line(gz, c, up, src=None):
        at = region(gz, columns[c], flat, nc)
        to = g + 1 if up else g - 1
        return remote(at if src is None else src, at, cs.at[gz, c, int(up)], cr.at[gz, c], (to, d))

    def both_ways(gz, make):
        @pl.when((gz <= g) & (g < ng - 1))
        def _():
            make(True)

        @pl.when((gz >= g) & (g > 0))
        def _():
            make(False)

    mine = pltpu.make_async_copy(own, region(g, d), local_sem.at[0])
    mine.start()

    def column(t):
        gz = near_order(t, g, ng)
        if t == 0:
            both_ways(gz, lambda up: line(gz, up, cut(own, 0, flat)).start())
            for n in range(3):
                plane(n, t, own).start()
            both_ways(gz, lambda up: corner_line(gz, 0, up, cut(own, flat, nc)).start())
            return
        arrived(region(gz, d, 0, flat), zr.at[gz])
        both_ways(gz, lambda up: line(gz, up).start())
        for n in range(3):
            plane(n, t).start()

    def sides(t):
        gz = near_order(t, g, ng)
        landed(0, t, over_x)
        plane(3, t).start()
        if t == 0:
            plane(9, t).start()
            both_ways(gz, lambda up: corner_line(gz, 1, up).start())
        plane(5, t).start()
        landed(1, t, over_y)
        plane(4, t).start()
        if t == 0:
            plane(10, t).start()
            both_ways(gz, lambda up: corner_line(gz, 2, up).start())
        plane(6, t).start()

    def corner(t):
        gz = near_order(t, g, ng)
        if t == 0:
            landed(9, t, across)
            landed(10, t, across)
            both_ways(gz, lambda up: corner_line(gz, 3, up).start())
            plane(11, t).start()
            plane(12, t).start()
        landed(3, t, across)
        plane(7, t).start()
        landed(4, t, across)
        plane(8, t).start()

    def far_corner(t):
        gz = near_order(t, g, ng)
        for c in range(4):
            arrived(region(gz, columns[c], flat, nc), cr.at[gz, c])
            both_ways(gz, lambda up: corner_line(gz, c, up).start())
            plane(13 + c, t).start()

    plan = [(t, f) for t in range(ng) for f in (0, 1, 2, 3) if t > 0 or f < 3]
    lag = {0: 0, 1: 1.5, 2: 2.6, 3: 2.2}
    for t, f in sorted(plan, key=lambda e: e[0] * 1.0 + lag[e[1]]):
        (column, sides, corner, far_corner)[f](t)
        if (t, f) == (0, 0):
            prepare(x_ref, block_ref, vin_ref, h1_ref, slot_ref, vec_ref)

    for t in range(ng):
        for n in kinds(t):
            dev, _, _, to = kind(n, t)
            if to is sibling:
                landed(n, t, dev + sibling - d)
    mine.wait()
    for t in range(ng):
        gz = near_order(t, g, ng)
        for n in kinds(t):
            plane(n, t).wait_send()
        both_ways(gz, lambda up: line(gz, up).wait_send())
        for c in range(4):
            both_ways(gz, lambda up: corner_line(gz, c, up).wait_send())


def run_gather(w, x, blocks, vin, ng, nd):
    count, side, _ = w.shape
    dma = pltpu.SemaphoreType.DMA
    return pl.pallas_call(
        functools.partial(gather_kernel, ng=ng, nd=nd),
        out_shape=(sds((ng * nd * count, side, side), BF16),) + prepared_shapes(x, blocks, vin),
        in_specs=[vmem()] * 4,
        out_specs=(hbm(), vmem(), vmem(), vmem()),
        scratch_shapes=[
            pltpu.VMEM((count, side, side), BF16),
            dma((1,)),
            dma((ng, 2)),
            dma((ng,)),
            dma((ng, 4, 2)),
            dma((ng, 4)),
            dma((17, ng)),
            dma((17, ng)),
        ],
        compiler_params=params(collective_id=0, has_side_effects=True),
        name="gather",
    )(w, x, blocks, vin)


def add_blocks(dst, src, size):
    step = next(n for n in (4, 5, 3, 2, 1) if size % n == 0)

    @pl.loop(0, size // step)
    def _(n):
        for k in range(step):
            dst[n * step + k] = dst[n * step + k] + src[n * step + k]


def scatter_kernel(
    grads, sums2_ref, vec_ref, vin_ref, cat_in, x_in, dx1_in, wq_in, out_ref, vout_ref, vnew_ref, ig_out,
    cat, x, dx1, wq, dh1, sem_in, mine, r0, r1y, r1x, r2x, r2y, rz, cz, cy, cx, cx2, cy2, vwork, vxy, vz,
    load, s0, w0, s1, w1, s2, w2, sz, wz, sc, wc, s3, w3, vs, vw, *, ng, nd, rate
):
    count = out_ref.shape[0]
    na, nb, nc1, nc2 = slot_cuts(count)
    flat = na + nb
    nc = nc1 + nc2
    g, d, over_x, over_y, across, sibling = whereami()
    columns = (d, over_x, over_y, across)

    def region(gz, dev):
        return grads.at[pl.ds((gz * nd + dev) * count, count)]

    def order(t):
        return near_order(ng - 1 - t, g, ng)

    for t in range(ng):
        for c in range(4):
            pltpu.make_async_copy(region(order(t), columns[c]), mine.at[order(t), c], load.at[order(t), c]).start()
    greet(g, ng, (over_x, over_y, sibling))

    def to_sibling(gz, c):
        return remote(
            region(gz, columns[c] + sibling - d), r0.at[gz, c], s0.at[gz, c], w0.at[gz, c], (g, sibling)
        )

    peers = (sibling, over_x, over_y)

    def vec_copy(n):
        return remote(vwork.at[n], vxy.at[n], vs.at[n], vw.at[n], (g, peers[n]))

    for t in range(ng):
        for c in (3, 2, 1, 0):
            to_sibling(order(t), c).start()
    inputs = [
        pltpu.make_async_copy(cat_in, cat, sem_in.at[0]),
        pltpu.make_async_copy(wq_in, wq, sem_in.at[1]),
        pltpu.make_async_copy(x_in, x, sem_in.at[2]),
        pltpu.make_async_copy(dx1_in, dx1, sem_in.at[3]),
    ]
    for copy in inputs:
        copy.start()
    input_grad = pltpu.make_async_copy(dx1, ig_out, sem_in.at[4])

    def first_norm():
        for copy in inputs:
            copy.wait()
        for part in range(3):
            for half in range(2):
                dh1_dot(cat, wq, dh1, part, half)
        first = first_norm_back(cat, x, dh1, dx1, dx1, vec_ref)
        input_grad.start()
        for n, row in enumerate(vector_rows(first, sums2_ref)):
            vwork[0, n:n + 1, :] = row
        vec_copy(0).start()

    first = (
        (2, 0, na, r1y, 0, over_y),
        (3, 0, na, r1y, 1, over_y),
        (1, na, nb, r1x, 0, over_x),
        (3, na, nb, r1x, 1, over_x),
    )
    second = ((1, 0, na, r2x, over_x), (2, na, nb, r2y, over_y))
    third = (
        (2, flat, nc1, cy.at[0], over_y),
        (3, flat, nc1, cy.at[1], over_y),
        (1, flat + nc1, nc2, cx.at[0], over_x),
        (3, flat + nc1, nc2, cx.at[1], over_x),
        (1, flat, nc1, cx2, over_x),
        (2, flat + nc1, nc2, cy2, over_y),
    )

    def copy1(n, gz):
        c, at, size, buf, place_at, to = first[n]
        return remote(cut(mine.at[gz, c], at, size), buf.at[gz, place_at], s1.at[n, gz], w1.at[n, gz], (g, to))

    def copy2(n, gz):
        c, at, size, buf, to = second[n]
        return remote(cut(mine.at[gz, c], at, size), buf.at[gz], s2.at[n, gz], w2.at[n, gz], (g, to))

    def copy3(n):
        c, at, size, buf, to = third[n]
        return remote(cut(mine.at[g, c], at, size), buf, s3.at[n], w3.at[n], (g, to))

    def flat_part(gz):
        return cut(mine.at[gz, 0], 0, flat)

    def corner_part(gz):
        return mine.at[gz, :, pl.ds(flat, nc)]

    def line(gz, part, buf, sends, waits, up):
        at = gz if up else jnp.where(gz < g - 1, gz, ng)
        to = g + 1 if up else g - 1
        return remote(part(gz), buf.at[at], sends.at[gz], waits.at[at], (to, d))

    def pass_on(gz, part, buf, sends, waits, gather):
        @pl.when(gz > g)
        def _():
            @pl.when(g > 0)
            def _():
                arrived(buf.at[gz], waits.at[gz])
                gather(gz)
            line(gz, part, buf, sends, waits, True).start()

        @pl.when(gz < g)
        def _():
            @pl.when(g < ng - 1)
            def _():
                arrived(buf.at[gz], waits.at[gz])
                gather(gz)
            line(gz, part, buf, sends, waits, False).start()

    def gather_flat(gz):
        add_blocks(flat_part(gz), rz.at[gz], flat)

    def gather_corner(at, gz):
        for c in range(4):
            add_blocks(cut(mine.at[gz, c], flat, nc), cz.at[at, c], nc)

    def sums0(t, c):
        gz = order(t)
        pltpu.make_async_copy(region(gz, columns[c]), mine.at[gz, c], load.at[gz, c]).wait()
        arrived(r0.at[gz, c], w0.at[gz, c])
        add_blocks(mine.at[gz, c], r0.at[gz, c], count)
        for n in {3: (1, 3), 2: (0,), 1: (2,), 0: ()}[c]:
            copy1(n, gz).start()

    def along0(t):
        pass_on(order(t), corner_part, cz, sc, wc, lambda gz: gather_corner(gz, gz))

    def stage1(t, k):
        gz = order(t)
        c, at, size, buf, n = (
            (1, 0, na, r1y.at[gz, 1], 1),
            (2, na, nb, r1x.at[gz, 1], 3),
            (0, 0, na, r1y.at[gz, 0], 0),
            (0, na, nb, r1x.at[gz, 0], 2),
        )[k]
        arrived(buf, w1.at[n, gz])
        add_blocks(cut(mine.at[gz, c], at, size), buf, size)
        if k < 2:
            copy2(k, gz).start()

    def stage2(t, k):
        gz = order(t)
        at, size, buf = ((0, na, r2x.at[gz]), (na, nb, r2y.at[gz]))[k]
        arrived(buf, w2.at[k, gz])
        add_blocks(cut(mine.at[gz, 0], at, size), buf, size)

    def along1(t):
        pass_on(order(t), flat_part, rz, sz, wz, gather_flat)

    def corner0():
        @pl.when(g > 0)
        def _():
            arrived(cz.at[g], wc.at[g])
            gather_corner(g, g)

        @pl.when(g < ng - 1)
        def _():
            arrived(cz.at[ng], wc.at[ng])
            gather_corner(ng, g)
        for n in range(4):
            copy3(n).start()

    def corner1():
        arrived(cy.at[1], w3.at[1])
        add_blocks(cut(mine.at[g, 1], flat, nc1), cy.at[1], nc1)
        copy3(4).start()
        arrived(cx.at[1], w3.at[3])
        add_blocks(cut(mine.at[g, 2], flat + nc1, nc2), cx.at[1], nc2)
        copy3(5).start()
        arrived(cy.at[0], w3.at[0])
        add_blocks(cut(mine.at[g, 0], flat, nc1), cy.at[0], nc1)
        arrived(cx.at[0], w3.at[2])
        add_blocks(cut(mine.at[g, 0], flat + nc1, nc2), cx.at[0], nc2)

    def corner2():
        arrived(cx2, w3.at[4])
        add_blocks(cut(mine.at[g, 0], flat, nc1), cx2, nc1)
        arrived(cy2, w3.at[5])
        add_blocks(cut(mine.at[g, 0], flat + nc1, nc2), cy2, nc2)

    def vec_step(n):
        arrived(vxy.at[n], vw.at[n])
        total = vwork[n] + vxy[n]
        if n < 2:
            vwork[n + 1] = total
            vec_copy(n + 1).start()
        else:
            vz[g] = total

    def vec_line(gz, up):
        to = g + 1 if up else g - 1
        return remote(vz.at[gz], vz.at[gz], vs.at[3 + 2 * gz + int(up)], vw.at[3 + gz], (to, d))

    def vec_first_line():
        vec_step(2)

        @pl.when(g < ng - 1)
        def _():
            vec_line(g, True).start()

        @pl.when(g > 0)
        def _():
            vec_line(g, False).start()

    def vec_next_line(n):
        gz = near_order(n, g, ng)
        arrived(vz.at[gz], vw.at[3 + gz])

        @pl.when((gz < g) & (g < ng - 1))
        def _():
            vec_line(gz, True).start()

        @pl.when((gz > g) & (g > 0))
        def _():
            vec_line(gz, False).start()

    def vec_out():
        total = vz[0]
        for z in range(1, ng):
            total = total + vz[z]
        vwork[3] = total
        per = total.shape[1] // 128
        for r in range(total.shape[0]):
            for c in range(per):
                row = vwork[3, r:r + 1, c * 128:(c + 1) * 128]
                n = per * r + c
                vout_ref[n:n + 1, :] = row
                vnew_ref[n:n + 1, :] = vin_ref[n:n + 1, :] - rate * row

    last = ng - 1
    plan = [(t + 0.25 * (3 - c), sums0, (t, c)) for t in range(ng) for c in range(4)]
    plan += [(t + 1.2 + 0.3 * (k // 2), stage1, (t, k)) for t in range(ng) for k in range(4)]
    plan += [(t + 2.2, stage2, (t, k)) for t in range(ng) for k in range(2)]
    plan += [(t + 1.15, along0, (t,)) for t in range(last)]
    plan += [(t + 2.21, along1, (t,)) for t in range(last)]
    plan += [(last + 1.3, corner0, ()), (last + 2.19, corner1, ()), (last + 2.4, corner2, ())]
    plan += [(0.3, first_norm, ()), (0.9, vec_step, (0,)), (2.0, vec_step, (1,)), (3.0, vec_first_line, ())]
    plan += [(3.1 + 0.55 * n, vec_next_line, (n,)) for n in range(1, ng)]
    plan += [(last + 2.17, vec_out, ())]
    plan = [(step, args) for _, step, args in sorted(plan, key=lambda e: e[0])]
    if ng == 4:
        plan = [
            (sums0, (0, 3)), (sums0, (0, 2)), (first_norm, ()), (sums0, (0, 1)),
            (sums0, (0, 0)), (stage1, (0, 1)), (sums0, (1, 3)), (vec_step, (0,)),
            (along0, (0,)), (stage1, (0, 0)), (sums0, (1, 2)), (sums0, (1, 0)),
            (sums0, (1, 1)), (along0, (1,)), (stage1, (1, 1)), (stage1, (0, 3)),
            (vec_step, (1,)), (sums0, (2, 3)), (stage2, (0, 0)), (stage1, (1, 0)),
            (stage1, (0, 2)), (stage2, (0, 1)), (sums0, (2, 1)), (along1, (0,)),
            (sums0, (2, 2)), (sums0, (2, 0)), (along0, (2,)), (stage1, (1, 2)), (vec_first_line, ()),
            (sums0, (3, 3)), (stage2, (1, 0)), (sums0, (3, 0)),
            (stage1, (2, 1)), (sums0, (3, 2)), (stage1, (2, 0)),
            (stage1, (1, 3)), (stage2, (1, 1)), (stage1, (2, 2)), (vec_next_line, (1,)), (sums0, (3, 1)),
            (along1, (1,)), (stage2, (2, 0)), (stage2, (2, 1)), (stage1, (2, 3)),
            (stage1, (3, 1)), (along1, (2,)), (corner0, ()), (vec_next_line, (2,)),
            (stage1, (3, 0)), (stage2, (3, 1)), (stage1, (3, 2)), (stage1, (3, 3)),
            (vec_next_line, (3,)), (corner1, ()), (vec_out, ()), (corner2, ()),
            (stage2, (3, 0)),
        ]
    for step, args in plan:
        step(*args)

    @pl.when(g > 0)
    def _():
        arrived(rz.at[g], wz.at[g])

    @pl.when(g < ng - 1)
    def _():
        arrived(rz.at[ng], wz.at[ng])

    @pl.when((g > 0) & (g < ng - 1))
    def _():
        @pl.loop(0, flat)
        def _(i):
            out_ref[i] = mine[g, 0, i].astype(F32) + rz[g, i].astype(F32) + rz[ng, i].astype(F32)

    @pl.when(g == 0)
    def _():
        @pl.loop(0, flat)
        def _(i):
            out_ref[i] = mine[g, 0, i].astype(F32) + rz[ng, i].astype(F32)

    @pl.when((g > 0) & (g == ng - 1))
    def _():
        @pl.loop(0, flat)
        def _(i):
            out_ref[i] = mine[g, 0, i].astype(F32) + rz[g, i].astype(F32)

    for i in range(flat, count):
        out_ref[i] = mine[g, 0, i].astype(F32)

    for t in range(ng):
        gz = order(t)
        for c in range(4):
            to_sibling(gz, c).wait_send()
        for n in range(4):
            copy1(n, gz).wait_send()
        for n in range(2):
            copy2(n, gz).wait_send()
        if t < ng - 1:
            arrived(flat_part(gz), sz.at[gz])
            arrived(corner_part(gz), sc.at[gz])
    input_grad.wait()
    for n in range(6):
        copy3(n).wait_send()
    for n in range(3):
        vec_copy(n).wait_send()
    for n in range(ng):
        gz = near_order(n, g, ng)

        @pl.when((gz <= g) & (g < ng - 1))
        def _():
            vec_line(gz, True).wait_send()

        @pl.when((gz >= g) & (g > 0))
        def _():
            vec_line(gz, False).wait_send()


def run_scatter(grads, sums2, vec, vin, cat, x, dx1, wq, ng, nd, rate):
    blocks, side, _ = grads.shape
    count = blocks // (ng * nd)
    na, nb, nc1, nc2 = slot_cuts(count)
    flat = na + nb
    dma = pltpu.SemaphoreType.DMA

    def buf(*lead):
        return pltpu.VMEM(lead + (side, side), BF16)

    def like(v):
        return pltpu.VMEM(v.shape, v.dtype)

    return pl.pallas_call(
        functools.partial(scatter_kernel, ng=ng, nd=nd, rate=rate),
        out_shape=(
            sds((count, side, side), F32),
            sds(vin.shape, F32),
            sds(vin.shape, F32),
            sds(dx1.shape, F32),
        ),
        in_specs=[hbm(), vmem(), vmem(), vmem()] + [hbm()] * 4,
        out_specs=(vmem(), vmem(), vmem(), hbm()),
        scratch_shapes=[
            like(cat),
            like(x),
            like(dx1),
            like(wq),
            like(dx1),
            dma((5,)),
            buf(ng, 4, count),
            buf(ng, 4, count),
            buf(ng, 2, na),
            buf(ng, 2, nb),
            buf(ng, na),
            buf(ng, nb),
            buf(ng + 1, flat),
            buf(ng + 1, 4, nc1 + nc2),
            buf(2, nc1),
            buf(2, nc2),
            buf(nc1),
            buf(nc2),
            pltpu.VMEM((4,) + vec.shape, F32),
            pltpu.VMEM((3,) + vec.shape, F32),
            pltpu.VMEM((ng,) + vec.shape, F32),
            dma((ng, 4)),
            dma((ng, 4)),
            dma((ng, 4)),
            dma((4, ng)),
            dma((4, ng)),
            dma((2, ng)),
            dma((2, ng)),
            dma((ng,)),
            dma((ng + 1,)),
            dma((ng,)),
            dma((ng + 1,)),
            dma((6,)),
            dma((6,)),
            dma((3 + 2 * ng,)),
            dma((3 + ng,)),
        ],
        compiler_params=params(61, collective_id=1, has_side_effects=True),
        name="scatter",
    )(grads, sums2, vec, vin, cat, x, dx1, wq)


def blocks_kernel(*refs, handed):
    g_ref, w_ref, ls_ref, rs_ref, lr_ref, rr_ref = refs[:6]
    wg_out, nl_out, nr_out, nw_out = refs[6 + handed:10 + handed]
    for n in range(handed):
        refs[10 + handed + n][...] = refs[6 + n][...]

    for i in range(g_ref.shape[0]):
        grad = g_ref[i]
        wg_out[i] = grad
        hi = grad.astype(BF16)
        low = (grad - hi.astype(F32)).astype(BF16)
        nl_out[i] = 0.5 * ls_ref[i] + 0.5 * dot_nt(hi, hi)
        turned = grad.T
        hi_t = turned.astype(BF16)
        nr_out[i] = 0.5 * rs_ref[i] + 0.5 * dot_nt(hi_t, hi_t)
        left = lr_ref[i]
        left_hi = left.astype(BF16)
        left_low = (left - left_hi.astype(F32)).astype(BF16)
        shaped = dot_nn(left_hi, hi) + dot_nn(left_hi, low) + dot_nn(left_low, hi)
        right = rr_ref[i]
        right_hi = right.astype(BF16)
        right_low = (right - right_hi.astype(F32)).astype(BF16)
        sh_hi = shaped.astype(BF16)
        sh_low = (shaped - sh_hi.astype(F32)).astype(BF16)
        shaped = dot_nn(sh_hi, right_hi) + dot_nn(sh_low, right_hi) + dot_nn(sh_hi, right_low)
        nw_out[i] = w_ref[i] - weight_rate * shaped


def run_blocks(grads, weights, left_stats, right_stats, left_roots, right_roots, *passing):
    count, side, _ = grads.shape
    steps = math.gcd(count, 4)
    step = count // steps
    spec = pl.BlockSpec((step, side, side), lambda n: (n, 0, 0))
    through = []
    for v in passing:
        part = v.shape[0] // steps
        if part % 8 == 0:
            through.append(pl.BlockSpec((part, v.shape[1]), lambda n: (n, 0)))
        else:
            through.append(pl.BlockSpec(v.shape, lambda n: (0, 0)))
    return pl.pallas_call(
        functools.partial(blocks_kernel, handed=len(passing)),
        grid=(steps,),
        out_shape=tuple([sds(grads.shape, F32)] * 4) + tuple(sds(v.shape, v.dtype) for v in passing),
        in_specs=[spec] * 6 + through,
        out_specs=tuple([spec] * 4) + tuple(through),
        compiler_params=params(),
        name="blocks",
    )(grads, weights, left_stats, right_stats, left_roots, right_roots, *passing)


def local(
    inputs,
    cotangent,
    weight_slots,
    slot_block,
    left_stats,
    right_stats,
    left_roots,
    right_roots,
    vectors,
    span_start,
):
    seq_count, tok_count, width = inputs.shape
    rows = seq_count * tok_count
    nd = lax.axis_size("dev")
    ng = lax.axis_size("grp")
    side = weight_slots.shape[1]
    hpd = H // nd
    lanes = width // nd
    head = lax.axis_index("dev") * hpd + jnp.arange(hpd, dtype=jnp.int32)
    slopes = jnp.exp2(-8.0 * (head.astype(F32) + 1.0) / H)
    vin = vectors.reshape(-1, 128)
    held = slot_block.reshape(-1, 128)
    x = inputs.reshape(rows, width)
    dy = cotangent.reshape(rows, width)
    rate = vector_rate / math.sqrt(rows * nd * ng)

    direct = nd == 8
    if direct:
        gath, h1, slot_of, vec = run_gather(weight_slots, x, held, vin, ng, nd)
    else:
        gath = lax.all_gather(weight_slots.astype(BF16), ("grp", "dev"), axis=0, tiled=True)
        h1, slot_of, vec = run_prepare(x, held, vin)
    qkv, wq = run_qkv(slot_of, h1, vec, gath, nd)
    qkv, o, o32, lse = run_attn_fwd(
        span_start, slopes, qkv.reshape(nd, 3, seq_count, tok_count, lanes), hpd
    )
    att = side_by_side(o, 1, rows)
    act, dx1, do, sums2, grads = run_mlp(slot_of, att, x, dy, vec, gath, nd)
    do = do.reshape(nd, seq_count, tok_count, lanes)
    cat = side_by_side(run_attn_bwd(span_start, slopes, qkv, do, o32, lse, hpd), 3, rows)
    grads = run_wgrad(slot_of, h1, cat, grads)
    if direct:
        weight_grads, vector_grads, new_vectors, ig = run_scatter(
            grads, sums2, vec, vin, cat, x, dx1, wq, ng, nd, rate
        )
        passing = (ig, vector_grads, new_vectors)
    else:
        ig, vsum = run_dh1(cat, x, dx1, vec, wq, sums2)
        vector_grads = lax.psum(vsum.reshape(-1), ("grp", "dev"))
        new_vectors = vectors - rate * vector_grads
        weight_grads = lax.psum_scatter(grads, ("grp", "dev"), scatter_dimension=0, tiled=True)
        weight_grads = weight_grads.astype(F32)
        passing = ()
    weight_grads, new_left, new_right, new_weights, *passed = run_blocks(
        weight_grads, weight_slots, left_stats, right_stats, left_roots, right_roots, *passing
    )
    if direct:
        ig, vector_grads, new_vectors = passed
    return (
        act.reshape(inputs.shape),
        ig.reshape(inputs.shape),
        weight_grads,
        new_left,
        new_right,
        new_weights,
        vector_grads.reshape(-1),
        new_vectors.reshape(-1),
    )


def solution(mesh):
    return jax.shard_map(
        local,
        mesh=mesh,
        in_specs=(
            P("grp", "dev", None),
            P("grp", "dev", None),
            P(("grp", "dev"), None, None),
            P(),
            P(("grp", "dev"), None, None),
            P(("grp", "dev"), None, None),
            P(("grp", "dev"), None, None),
            P(("grp", "dev"), None, None),
            P(),
            P("grp"),
        ),
        out_specs=(
            P("grp", "dev", None),
            P("grp", "dev", None),
            P(("grp", "dev"), None, None),
            P(("grp", "dev"), None, None),
            P(("grp", "dev"), None, None),
            P(("grp", "dev"), None, None),
            P(),
            P(),
        ),
        check_vma=False,
    )
```

```python
import functools
import math

import jax
import jax.numpy as jnp
from jax import lax
from jax.experimental import pallas as pl
from jax.experimental.pallas import tpu as pltpu
from jax.sharding import PartitionSpec as P

H = 16
FF = 4096
PIC = 256

eps = 1e-05
weight_rate = 0.5
vector_rate = 0.5
big_negative = -1e30
highest = lax.Precision.HIGHEST
F32 = jnp.float32
BF16 = jnp.bfloat16
MIB = 1024 * 1024

GAIN1, SHIFT1, BQ, BV, BO, GAIN2, SHIFT2, BDOWN, BUP = range(9)


def dot_nn(a, b):
    return lax.dot_general(a, b, (((1,), (0,)), ((), ())), preferred_element_type=F32)


def dot_nt(a, b):
    return lax.dot_general(a, b, (((1,), (1,)), ((), ())), preferred_element_type=F32)


def turn(v):
    return v.astype(F32).T.astype(BF16)


def vmem():
    return pl.BlockSpec(memory_space=pltpu.VMEM)


def smem():
    return pl.BlockSpec(memory_space=pltpu.SMEM)


def hbm():
    return pl.BlockSpec(memory_space=pl.ANY)


def sds(shape, dtype):
    return jax.ShapeDtypeStruct(shape, dtype)


def params(mib=58, **kw):
    return pltpu.CompilerParams(vmem_limit_bytes=mib * MIB, **kw)


def layer_stats(v):
    middle = jnp.mean(v, axis=-1, keepdims=True)
    centred = v - middle
    spread = jnp.mean(centred * centred, axis=-1, keepdims=True)
    return centred, lax.rsqrt(spread + eps)


def fold_rows(v):
    return jnp.sum(v.reshape(v.shape[0] // 8, 8, v.shape[1]), axis=0)


def slot_at(slot_ref, block):
    lanes = slot_ref.shape[1]
    if isinstance(block, int):
        return slot_ref[block // lanes, block % lanes]
    return slot_ref[lax.div(block, lanes), lax.rem(block, lanes)]


def fetch_block(gath, slot, dst, row, col, sem, side):
    return pltpu.make_async_copy(
        gath.at[slot], dst.at[pl.ds(row, side), pl.ds(col, side)], sem
    )


def prepare(x_ref, block_ref, vin_ref, h1_ref, slot_ref, vec_ref):
    rows, width = x_ref.shape
    per = width // 128
    for r in range(vec_ref.shape[0]):
        for c in range(per):
            vec_ref[r:r + 1, c * 128:(c + 1) * 128] = vin_ref[per * r + c:per * r + c + 1, :]
    chunk = 128

    @pl.loop(0, rows // chunk)
    def _(r):
        at = pl.ds(pl.multiple_of(r * chunk, chunk), chunk)
        centred, inv = layer_stats(x_ref[at, :].astype(F32))
        h1_ref[at, :] = (
            centred * inv * vec_ref[GAIN1:GAIN1 + 1, :] + vec_ref[SHIFT1:SHIFT1 + 1, :]
        ).astype(BF16)

    tiles, lanes = slot_ref.shape
    line = lax.broadcasted_iota(jnp.int32, (8, lanes), 0)
    lane = lax.broadcasted_iota(jnp.int32, (8, lanes), 1).astype(F32)
    block = lax.broadcasted_iota(jnp.int32, (lanes, lanes), 0)
    for t in range(tiles):
        found = jnp.zeros((8, lanes), F32)
        for r in range(tiles):
            held = (block_ref[r:r + 1, :] == block + t * lanes).astype(F32).astype(BF16)
            found = found + dot_nt(jnp.where(line == 0, lane, float(r)).astype(BF16), held)
        slot_ref[t:t + 1, :] = (found[0:1] + float(lanes) * found[1:2]).astype(jnp.int32)


def prepared_shapes(x, blocks, vin):
    rows, width = x.shape
    return (
        sds((rows, width), BF16),
        sds(blocks.shape, jnp.int32),
        sds((vin.size // width, width), F32),
    )


def run_prepare(x, blocks, vin):
    return pl.pallas_call(
        prepare,
        out_shape=prepared_shapes(x, blocks, vin),
        in_specs=[vmem()] * 3,
        out_specs=tuple([vmem()] * 3),
        compiler_params=params(),
        name="prepare",
    )(x, blocks, vin)


def qkv_kernel(slot_ref, h1_ref, vec_ref, gath, out_ref, wq_out, wbuf, sems, sem_w, *, nd):
    rows, width = h1_ref.shape
    side = gath.shape[1]
    per = width // side
    lanes = out_ref.shape[3]
    for part in range(3):
        for i in range(per):
            for j in range(per):
                slot = slot_at(slot_ref, i * 3 * per + part * per + j)
                fetch_block(gath, slot, wbuf.at[part], i * side, j * side, sems.at[part], side).start()

    def keep(part):
        return pltpu.make_async_copy(wbuf.at[part], wq_out.at[part], sem_w.at[part])

    for part in range(3):
        pltpu.make_async_copy(wbuf.at[part], wbuf.at[part], sems.at[part]).wait()
        keep(part).start()
        for half in range(2):
            cols = slice(half * width // 2, (half + 1) * width // 2)
            res = dot_nn(h1_ref[...], wbuf[part, :, cols])
            if part == 0:
                res = res + vec_ref[BQ:BQ + 1, cols]
            if part == 2:
                res = res + vec_ref[BV:BV + 1, cols]
            res = res.astype(BF16)
            for d in range(nd // 2):
                out_ref[half * (nd // 2) + d, part, :, :] = res[:, d * lanes:(d + 1) * lanes]
    for part in range(3):
        keep(part).wait()


def run_qkv(slot_of, h1, vec, gath, nd):
    rows, width = h1.shape
    lanes = width // nd
    return pl.pallas_call(
        functools.partial(qkv_kernel, nd=nd),
        out_shape=(sds((nd, 3, rows, lanes), BF16), sds((3, width, width), BF16)),
        in_specs=[smem(), vmem(), vmem(), hbm()],
        out_specs=(vmem(), hbm()),
        scratch_shapes=[
            pltpu.VMEM((3, width, width), BF16),
            pltpu.SemaphoreType.DMA((3,)),
            pltpu.SemaphoreType.DMA((3,)),
        ],
        compiler_params=params(),
        name="qkv",
    )(slot_of, h1, vec, gath)


MESH = pl.DeviceIdType.MESH


def remote(src, dst, send, recv, device):
    return pltpu.make_async_remote_copy(
        src_ref=src, dst_ref=dst, send_sem=send, recv_sem=recv, device_id=device, device_id_type=MESH
    )


def arrived(ref, sem):
    pltpu.make_async_copy(ref, ref, sem).wait()


def cut(ref, first, size):
    return ref.at[pl.ds(first, size)]


def greet_plane(g, d, nd):
    barrier = pltpu.get_barrier_semaphore()
    for p in range(1, nd):
        pl.semaphore_signal(barrier, inc=1, device_id=(g, lax.rem(d + p, nd)), device_id_type=MESH)
    pl.semaphore_wait(barrier, nd - 1)


def landing(ref, part, source, q, tok, lanes, parts):
    if lanes % 128 == 0:
        first = (part * (ref.shape[1] // parts)) + source * lanes
        return ref.at[pl.ds(q * tok, tok), pl.ds(pl.multiple_of(first, lanes), lanes)]
    return ref.at[source, part, q]


def landing_shape(parts, nb, seqs, tok, lanes):
    if lanes % 128 == 0:
        return sds((seqs * tok, parts * nb * lanes), BF16)
    return sds((nb, parts, seqs, tok, lanes), BF16)


def side_by_side(got, parts, rows):
    if got.ndim == 2:
        return got
    nb, _, seqs, tok, lanes = got.shape
    return got.transpose(2, 3, 1, 0, 4).reshape(rows, parts * nb * lanes)


def parts3(v):
    hi = v.astype(BF16)
    mid = (v - hi.astype(F32)).astype(BF16)
    lo = (v - hi.astype(F32) - mid.astype(F32)).astype(BF16)
    return hi.astype(F32), mid.astype(F32), lo.astype(F32)


def own_lanes(h, shape, hpd, lanes):
    lane = lax.broadcasted_iota(jnp.int32, shape, 1)
    size = lanes // hpd
    return (lane >= h * size) & (lane < (h + 1) * size)


def place(values, base, tok, width):
    lane = lax.broadcasted_iota(jnp.int32, (tok, width), 1)
    out = jnp.zeros((tok, width), F32)
    for n, v in enumerate(values):
        out = jnp.where(lane == base + n, v, out)
    return out


def spare(h, hpd, lanes):
    return (lanes // hpd) * (1 - h) if hpd > 1 else 0


def column_tables(slope_ref, qbase, kbase, kfar, hpd, lanes):
    _, tok, _ = qbase.shape
    u = lax.broadcasted_iota(jnp.int32, (tok, 128), 0).astype(F32)
    for h in range(hpd):
        slope = slope_ref[h]
        base = spare(h, hpd, lanes)
        near = parts3(jnp.full((tok, 128), slope, F32))
        far = parts3(jnp.full((tok, 128), slope * tok, F32))
        qbase[h] = place(near + far, base, tok, 128)
        kbase[h] = place([u] * 3 + [0.0] * 3 + [1.0] * 3, base, tok, 128)
        kfar[h] = place([0.0] * 3 + [1.0] * 3, base, tok, 128)


def extra_lanes(columns, extra, h, hpd, lanes):
    lane = lax.broadcasted_iota(jnp.int32, columns.shape, 1)
    for n, v in enumerate(extra):
        columns = jnp.where(lane == spare(h, hpd, lanes) + 6 + n, v, columns)
    return columns


def with_columns(v, h, hpd, columns):
    tok, lanes = v.shape
    if hpd > 1:
        return jnp.where(own_lanes(h, (tok, lanes), hpd, lanes), v, columns).astype(BF16)
    return jnp.concatenate([v, columns[:, 0:128 - lanes]], axis=1).astype(BF16)


def q_columns(q, h, hpd, columns, extra):
    lanes = q.shape[1]
    if extra:
        columns = extra_lanes(columns, extra, h, hpd, lanes)
    return with_columns(q.astype(F32) * ((lanes // hpd) ** (-0.5)), h, hpd, columns)


def k_columns(k, h, hpd, columns):
    return with_columns(k.astype(F32), h, hpd, columns)


def far_side(slope, tok):
    u = lax.broadcasted_iota(jnp.int32, (tok, tok), 0)
    t = lax.broadcasted_iota(jnp.int32, (tok, tok), 1)
    after = u > t
    return (
        jnp.where(after, big_negative, 0.0),
        jnp.where(after, (2.0 * slope) * (t - u).astype(F32), 0.0),
    )


def pair_tables(corr, h, mask, span):
    tok = mask.shape[0]
    for n, (one, two) in enumerate(((mask, mask), (span, mask), (mask, span))):
        corr[h, n, 0:tok, 0:tok] = one
        corr[h, n, tok:, tok:] = two
        corr[h, n, 0:tok, tok:] = jnp.zeros((tok, tok), F32)
        corr[h, n, tok:, 0:tok] = jnp.full((tok, tok), big_negative, F32)


def attn_fwd_kernel(
    span_ref, slope_ref, src, got_out, o_got, o32_out, lse_out,
    got, o32_ref, lse_ref, sem_w, qa, ka, vt, scores, tops_ref, corr, qbase, kbase, kfar, o_out, ss, sr, os, orr, loc, *, hpd, nd
):
    nb, _, seqs, tok, lanes = got.shape
    size = lanes // hpd
    pair = 2 * tok
    g = lax.axis_index("grp")
    d = lax.axis_index("dev")

    for q in range(seqs):
        pltpu.make_async_copy(src.at[d, :, q], got.at[d, :, q], loc.at[q]).start()
    greet_plane(g, d, nd)

    def kind_of(kind):
        return pl.ds(2 * kind, 2 - kind)

    def send(q, kind, p):
        to = lax.rem(d + p, nd)
        return remote(
            src.at[to, kind_of(kind), q], got.at[d, kind_of(kind), q],
            ss.at[q, kind, p], sr.at[q, kind, p], (g, to),
        )

    def send_all(q, kind):
        @pl.loop(1, nd)
        def _(p):
            send(q, kind, p).start()

    def have(q, kind):
        @pl.loop(1, nd)
        def _(p):
            arrived(got.at[lax.rem(d + nd - p, nd), kind_of(kind), q], sr.at[q, kind, p])

    send_all(0, 0)
    send_all(0, 1)

    def o_place(source, q):
        return landing(o_got, 0, source, q, tok, lanes, 1)

    def send_o(q, i, p):
        return remote(o_out.at[i, q], o_place(d, q), os.at[q, i], orr.at[q, p], (g, i))

    column_tables(slope_ref, qbase, kbase, kfar, hpd, lanes)
    for h in range(hpd):
        mask, span = far_side(slope_ref[h], tok)
        pair_tables(corr, h, mask, span)

    def fold(v, how):
        return how(v.reshape(v.shape[0] // 8, 8, v.shape[1]), axis=0)

    def write(ref, out, n, q, third=False):
        if third:
            return pltpu.make_async_copy(ref.at[:, :, q], out.at[:, :, q], sem_w.at[n, q])
        return pltpu.make_async_copy(ref.at[:, q], out.at[:, q], sem_w.at[n, q])

    whole = scores.shape[1] > nb // 2

    def tile_at(i, n):
        return (i * (i + 1)) // 2 + n if whole else n

    @pl.loop(0, seqs)
    def _(q):
        pltpu.make_async_copy(src.at[d, :, q], got.at[d, :, q], loc.at[q]).wait()
        start = span_ref[q]

        def score(i):
            flag = (start == i * pair).astype(jnp.int32) + 2 * (start == i * pair + tok).astype(jnp.int32)
            at_i = slice(i * pair, (i + 1) * pair)
            for h in range(hpd):
                top = None
                for n in range(i + 1):
                    s = dot_nt(ka[h, n * pair:(n + 1) * pair, :], qa[h, at_i, :])
                    if n == i:
                        s = s + corr[h, flag]
                    scores[h, tile_at(i, n)] = s
                    here = fold(s, jnp.max)
                    top = here if top is None else jnp.maximum(top, here)
                tops_ref[h, i] = jnp.broadcast_to(jnp.max(top, axis=0, keepdims=True), (8, pair))

        have(q, 0)

        @pl.when(q + 1 < seqs)
        def _():
            send_all(q + 1, 0)

        @pl.loop(0, nb)
        def _(j):
            at_j = pl.ds(pl.multiple_of(j * tok, tok), tok)
            block = jnp.full((tok, 128), j, jnp.int32).astype(F32)
            for h in range(hpd):
                qa[h, at_j, :] = q_columns(got[j, 0, q], h, hpd, qbase[h], [])
                ka[h, at_j, :] = k_columns(got[j, 1, q], h, hpd, kbase[h] + block * kfar[h])

        if whole:
            for i in range(nb // 2):
                score(i)
        have(q, 1)

        @pl.when(q + 1 < seqs)
        def _():
            send_all(q + 1, 1)

        write(got, got_out, 0, q, True).start()

        @pl.loop(0, nb)
        def _(j):
            vt[0:lanes, pl.ds(pl.multiple_of(j * tok, tok), tok)] = turn(got[j, 2, q])

        for i in range(nb // 2):
            if not whole:
                score(i)
            outs = []
            logs = []
            for h in range(hpd):
                acc = total = None
                top = tops_ref[h, i][0:1]
                for n in range(i + 1):
                    p = jnp.exp(scores[h, tile_at(i, n)] - top)
                    here = fold(p, jnp.sum)
                    part = dot_nn(vt[h * size:(h + 1) * size, n * pair:(n + 1) * pair], p.astype(BF16))
                    total = here if total is None else total + here
                    acc = part if acc is None else acc + part
                total = jnp.sum(total, axis=0, keepdims=True)
                outs.append(acc / total)
                logs.append(jnp.broadcast_to(top + jnp.log(total), (128 // hpd, pair)))
            out = (jnp.concatenate(outs, axis=0) if hpd > 1 else outs[0]).T
            log = (jnp.concatenate(logs[::-1], axis=0) if hpd > 1 else logs[0]).T
            for k in range(2):
                at = 2 * i + k
                o32_ref[at, q] = out[k * tok:(k + 1) * tok]
                o_out[at, q] = out[k * tok:(k + 1) * tok].astype(BF16)
                lse_ref[at, q] = log[k * tok:(k + 1) * tok]

                @pl.when(at == d)
                def _():
                    pltpu.make_async_copy(o_out.at[at, q], o_place(d, q), os.at[q, at]).start()

                @pl.when(at != d)
                def _():
                    send_o(q, at, lax.rem(at - d + nd, nd)).start()

        write(o32_ref, o32_out, 1, q).start()
        write(lse_ref, lse_out, 2, q).start()

    for q in range(seqs):
        @pl.loop(1, nd)
        def _(p):
            arrived(o_place(lax.rem(d + nd - p, nd), q), orr.at[q, p])
            send(q, 0, p).wait_send()
            send(q, 1, p).wait_send()

        @pl.loop(0, nd)
        def _(i):
            arrived(o_out.at[i, q], os.at[q, i])
        write(got, got_out, 0, q, True).wait()
        write(o32_ref, o32_out, 1, q).wait()
        write(lse_ref, lse_out, 2, q).wait()


def run_attn_fwd(span, slopes, qkv, hpd):
    nb, _, seqs, tok, lanes = qkv.shape
    t = nb * tok
    pairs = nb // 2
    tiles = pairs * (pairs + 1) // 2
    if hpd * tiles > 24:
        tiles = pairs
    dma = pltpu.SemaphoreType.DMA
    return pl.pallas_call(
        functools.partial(attn_fwd_kernel, hpd=hpd, nd=nb),
        out_shape=(
            sds(qkv.shape, BF16),
            landing_shape(1, nb, seqs, tok, lanes),
            sds((nb, seqs, tok, lanes), F32),
            sds((nb, seqs, tok, 128), F32),
        ),
        in_specs=[smem(), smem(), hbm()],
        out_specs=(hbm(), vmem(), hbm(), hbm()),
        scratch_shapes=[
            pltpu.VMEM(qkv.shape, BF16),
            pltpu.VMEM((nb, seqs, tok, lanes), F32),
            pltpu.VMEM((nb, seqs, tok, 128), F32),
            dma((3, seqs)),
            pltpu.VMEM((hpd, t, 128), BF16),
            pltpu.VMEM((hpd, t, 128), BF16),
            pltpu.VMEM((lanes, t), BF16),
            pltpu.VMEM((hpd, tiles, 2 * tok, 2 * tok), F32),
            pltpu.VMEM((hpd, nb // 2, 8, 2 * tok), F32),
            pltpu.VMEM((hpd, 3, 2 * tok, 2 * tok), F32),
            pltpu.VMEM((hpd, tok, 128), F32),
            pltpu.VMEM((hpd, tok, 128), F32),
            pltpu.VMEM((hpd, tok, 128), F32),
            pltpu.VMEM((nb, seqs, tok, lanes), BF16),
            dma((seqs, 2, nb)),
            dma((seqs, 2, nb)),
            dma((seqs, nb)),
            dma((seqs, nb)),
            dma((seqs,)),
        ],
        compiler_params=params(collective_id=2, has_side_effects=True),
        name="attn_fwd",
    )(span, slopes, qkv)


def attn_bwd_kernel(
    span_ref, slope_ref, qkv_in, do_src, o32_in, lse_in, got,
    qkv_ref, o32_ref, lse_ref, sem_in, do_got, out, qa, ka, kt, va, qm, da, dm, dqt, corr, qbase, kbase, kfar,
    ss, sr, gs, gr, loc, *, hpd, nd
):
    nb, _, seqs, tok, lanes = qkv_ref.shape
    inputs = [
        pltpu.make_async_copy(qkv_in, qkv_ref, sem_in.at[0]),
        pltpu.make_async_copy(lse_in, lse_ref, sem_in.at[1]),
        pltpu.make_async_copy(o32_in, o32_ref, sem_in.at[2]),
    ]
    for copy in inputs:
        copy.start()
    size = lanes // hpd
    unit = size ** (-0.5)
    pair = 2 * tok
    g = lax.axis_index("grp")
    d = lax.axis_index("dev")

    def own_copy(q):
        return pltpu.make_async_copy(do_src.at[d, q], do_got.at[d, q], loc.at[q])

    for q in range(seqs):
        own_copy(q).start()
    greet_plane(g, d, nd)

    def send(q, p):
        to = lax.rem(d + p, nd)
        return remote(do_src.at[to, q], do_got.at[d, q], ss.at[q, p], sr.at[q, p], (g, to))

    def send_all(q):
        @pl.loop(1, nd)
        def _(p):
            send(q, p).start()

    send_all(0)

    def place_back(kind, source, q):
        return landing(got, kind, source, q, tok, lanes, 3)

    def back(q, kind, p):
        to = lax.rem(d + p, nd)
        return remote(
            out.at[to, kind, q], place_back(kind, d, q), gs.at[q, kind, p], gr.at[q, kind, p], (g, to)
        )

    def back_own(q, kind):
        return pltpu.make_async_copy(out.at[d, kind, q], place_back(kind, d, q), gs.at[q, kind, 0])

    for h in range(hpd):
        mask, span = far_side(slope_ref[h], tok)
        pair_tables(corr, h, mask, span)
    column_tables(slope_ref, qbase, kbase, kfar, hpd, lanes)
    row = lax.broadcasted_iota(jnp.int32, (lanes, lanes), 0) // size
    col = lax.broadcasted_iota(jnp.int32, (lanes, lanes), 1) // size
    across = (row == hpd - 1 - col).astype(F32).astype(BF16)
    for copy in inputs:
        copy.wait()

    @pl.loop(0, seqs)
    def _(q):
        @pl.loop(0, nb)
        def _(j):
            at_j = pl.ds(pl.multiple_of(j * tok, tok), tok)
            qj = qkv_ref[j, 0, q]
            kj = qkv_ref[j, 1, q]
            vj = qkv_ref[j, 2, q].astype(F32)
            kt[:, at_j] = kj.astype(F32).T.astype(BF16)
            dqt[:, at_j] = jnp.zeros((lanes, tok), F32)
            block = jnp.full((tok, 128), j, jnp.int32).astype(F32)
            low = [-p for p in parts3(lse_ref[j, q])]
            for h in range(hpd):
                qa[h, at_j, :] = q_columns(qj, h, hpd, qbase[h], low)
                ka[h, at_j, :] = k_columns(kj, h, hpd, kbase[h] + block * kfar[h])
                if hpd > 1:
                    own = own_lanes(h, (tok, lanes), hpd, lanes)
                    qm[h, at_j, :] = jnp.where(own, qj.astype(F32), 0.0).astype(BF16)
                    va[h, at_j, :] = jnp.where(own, vj, kbase[h]).astype(BF16)
                else:
                    qm[h, at_j, :] = qj
                    va[h, at_j, :] = jnp.concatenate([vj, kbase[h][:, 0:lanes]], axis=1).astype(BF16)

        own_copy(q).wait()

        @pl.loop(1, nd)
        def _(p):
            arrived(do_got.at[lax.rem(d + nd - p, nd), q], sr.at[q, p])

        @pl.when(q + 1 < seqs)
        def _():
            send_all(q + 1)

        @pl.loop(0, nb)
        def _(j):
            at_j = pl.ds(pl.multiple_of(j * tok, tok), tok)
            do = do_got[j, q].astype(F32)
            delta = jnp.zeros((tok, lanes), F32)
            for p in parts3(do * o32_ref[j, q]):
                delta = delta + dot_nn(p.astype(BF16), across)
            low = [-p for p in parts3(delta)]
            for h in range(hpd):
                if hpd > 1:
                    own = own_lanes(h, (tok, lanes), hpd, lanes)
                    none = jnp.where(own, do, 0.0)
                    da[h, at_j, :] = extra_lanes(none, low, h, hpd, lanes).astype(BF16)
                    dm[h, at_j, :] = none.astype(BF16)
                else:
                    extra = extra_lanes(jnp.zeros((tok, lanes), F32), low, h, hpd, lanes)
                    da[h, at_j, :] = jnp.concatenate([do, extra], axis=1).astype(BF16)
                    dm[h, at_j, :] = do.astype(BF16)

        start = span_ref[q]

        pairs = nb // 2

        def tile(j, i):
            at_j = slice(j * pair, (j + 1) * pair)
            at_i = slice(i * pair, (i + 1) * pair)
            flag = (start == j * pair).astype(jnp.int32) + 2 * (start == j * pair + tok).astype(jnp.int32)
            dk = dv = None
            for h in range(hpd):
                s = dot_nt(ka[h, at_j, :], qa[h, at_i, :])
                if i == j:
                    s = s + corr[h, flag]
                p = jnp.exp(s)
                ds = (p * dot_nt(va[h, at_j, :], da[h, at_i, :])).astype(BF16)
                dv_h = dot_nn(p.astype(BF16), dm[h, at_i, :])
                dk_h = dot_nn(ds, qm[h, at_i, :])
                dk = dk_h if dk is None else dk + dk_h
                dv = dv_h if dv is None else dv + dv_h
                rows = slice(h * size, (h + 1) * size)
                dqt[rows, at_i] += dot_nn(kt[rows, at_j], ds)
            return dk, dv

        @pl.loop(0, pairs)
        def _(n):
            turn_of = lax.rem(d // 2 + n, pairs)
            for case in range(pairs):
                @pl.when(turn_of == case)
                def _():
                    dk, dv = tile(case, case)
                    for i in range(case + 1, pairs):
                        more = tile(case, i)
                        dk = dk + more[0]
                        dv = dv + more[1]
                    for k in range(2):
                        half = slice(k * tok, (k + 1) * tok)
                        out[2 * case + k, 1, q] = (dk[half] * unit).astype(BF16)
                        out[2 * case + k, 2, q] = dv[half].astype(BF16)

            for k in range(2):
                j = 2 * turn_of + k
                for kind in (1, 2):
                    @pl.when(j == d)
                    def _():
                        back_own(q, kind).start()

                    @pl.when(j != d)
                    def _():
                        back(q, kind, lax.rem(j - d + nd, nd)).start()

        @pl.loop(0, nb)
        def _(n):
            j = lax.rem(d + n, nb)
            at_j = pl.ds(pl.multiple_of(j * tok, tok), tok)
            out[j, 0, q] = (dqt[:, at_j].T * unit).astype(BF16)

            @pl.when(n == 0)
            def _():
                back_own(q, 0).start()

            @pl.when(n > 0)
            def _():
                back(q, 0, n).start()

    for q in range(seqs):
        for kind in range(3):
            back_own(q, kind).wait()

        @pl.loop(1, nd)
        def _(p):
            send(q, p).wait_send()
            source = lax.rem(d + nd - p, nd)
            for kind in range(3):
                back(q, kind, p).wait_send()
                arrived(place_back(kind, source, q), gr.at[q, kind, p])


def run_attn_bwd(span, slopes, qkv, do, o32, lse, hpd):
    nb, _, seqs, tok, lanes = qkv.shape
    t = nb * tok
    dma = pltpu.SemaphoreType.DMA
    wide = 128 if hpd == 1 else lanes
    return pl.pallas_call(
        functools.partial(attn_bwd_kernel, hpd=hpd, nd=nb),
        out_shape=landing_shape(3, nb, seqs, tok, lanes),
        in_specs=[smem(), smem(), hbm(), hbm(), hbm(), hbm()],
        out_specs=vmem(),
        scratch_shapes=[
            pltpu.VMEM(qkv.shape, BF16),
            pltpu.VMEM(o32.shape, F32),
            pltpu.VMEM(lse.shape, F32),
            dma((3,)),
            pltpu.VMEM((nb, seqs, tok, lanes), BF16),
            pltpu.VMEM(qkv.shape, BF16),
            pltpu.VMEM((hpd, t, 128), BF16),
            pltpu.VMEM((hpd, t, 128), BF16),
            pltpu.VMEM((lanes, t), BF16),
            pltpu.VMEM((hpd, t, wide), BF16),
            pltpu.VMEM((hpd, t, lanes), BF16),
            pltpu.VMEM((hpd, t, wide), BF16),
            pltpu.VMEM((hpd, t, lanes), BF16),
            pltpu.VMEM((lanes, t), F32),
            pltpu.VMEM((hpd, 3, 2 * tok, 2 * tok), F32),
            pltpu.VMEM((hpd, tok, 128), F32),
            pltpu.VMEM((hpd, tok, 128), F32),
            pltpu.VMEM((hpd, tok, 128), F32),
            dma((seqs, nb)),
            dma((seqs, nb)),
            dma((seqs, 3, nb)),
            dma((seqs, 3, nb)),
            dma((seqs,)),
        ],
        compiler_params=params(collective_id=3, has_side_effects=True),
        name="attn_bwd",
    )(span, slopes, qkv, do, o32, lse)


def mlp_kernel(
    slot_ref, att_in, x_in, dy_in, vec_ref, gath,
    act_out, dx1_out, do_out, sums_ref, grads,
    att_ref, x_ref, dy_ref, sem_in, wo, wup, wdn, x1, acc, dh2, h2_ref, h2t, attt, gt, act_ref, z_ref, dg_ref, g_ref, dz_ref, do_ref, stage,
    sem_o, sem_t, sem_g, sem_w, *, nd, first_o, first_up, first_dn, tile
):
    rows, width = x_ref.shape
    side = gath.shape[1]
    per = width // side
    ff = sums_ref.shape[0] // 8 * width - 4 * width
    tiles = ff // tile
    cols = tile // side
    lanes = do_ref.shape[2]
    fper = ff // side
    inputs = [
        pltpu.make_async_copy(att_in, att_ref, sem_in.at[0]),
        pltpu.make_async_copy(x_in, x_ref, sem_in.at[1]),
        pltpu.make_async_copy(dy_in, dy_ref, sem_in.at[2]),
    ]
    for copy in inputs:
        copy.start()

    for i in range(per):
        for j in range(per):
            fetch_block(gath, slot_at(slot_ref, first_o + i * per + j), wo, i * side, j * side, sem_o.at[0], side).start()

    ring = wup.shape[0]

    def fetch_tile(f):
        at = f % ring
        for i in range(per):
            for j in range(cols):
                fetch_block(gath, slot_at(slot_ref, first_up + i * fper + f * cols + j), wup.at[at], i * side, j * side, sem_t.at[at], side).start()
            for j in range(cols):
                fetch_block(gath, slot_at(slot_ref, first_dn + (f * cols + j) * per + i), wdn.at[at], j * side, i * side, sem_t.at[at], side).start()

    for f in range(min(ring, tiles)):
        fetch_tile(f)
    for copy in inputs:
        copy.wait()
    for r in range(width // 256):
        attt[r * 256:(r + 1) * 256, :] = turn(att_ref[:, r * 256:(r + 1) * 256])
    pltpu.make_async_copy(wo, wo, sem_o.at[0]).wait()
    for half in range(2):
        c = slice(half * width // 2, (half + 1) * width // 2)
        x1[:, c] = x_ref[:, c].astype(F32) + dot_nn(att_ref[...], wo[:, c]) + vec_ref[BO:BO + 1, c]

    chunk = 128

    def rows_at(r):
        return pl.ds(pl.multiple_of(r * chunk, chunk), chunk)

    @pl.loop(0, rows // chunk)
    def _(r):
        at = rows_at(r)
        centred, inv = layer_stats(x1[at, :])
        h2_ref[at, :] = (centred * inv * vec_ref[GAIN2:GAIN2 + 1, :] + vec_ref[SHIFT2:SHIFT2 + 1, :]).astype(BF16)
        acc[at, :] = x1[at, :] + vec_ref[BDOWN:BDOWN + 1, :]
        dh2[at, :] = jnp.zeros((chunk, width), F32)

    for r in range(width // 256):
        h2t[r * 256:(r + 1) * 256, :] = turn(h2_ref[:, r * 256:(r + 1) * 256])

    def put(slot, first, res, down, across, stride):
        for i in range(down):
            for j in range(across):
                stage[slot, first + i * stride + j] = res[i * side:(i + 1) * side, j * side:(j + 1) * side]

    def leave(slot, n, block):
        pltpu.make_async_copy(stage.at[slot, n], grads.at[slot_at(slot_ref, block)], sem_g.at[slot]).start()

    def left(slot, size):
        at = stage.at[slot, pl.ds(0, size)]
        pltpu.make_async_copy(at, at, sem_g.at[slot]).wait()

    full = 2 * per * cols
    piece = 512
    per_piece = piece // side
    strip = 16

    def pieces(size):
        return [slice(k * piece, (k + 1) * piece) for k in range(size // piece)]

    def into_tile(f):
        at = f % ring
        arrived(wup.at[at], sem_t.at[at])
        arrived(wdn.at[at], sem_t.at[at])
        for c in pieces(tile):
            z_ref[:, c] = dot_nn(h2_ref[...], wup[at, :, c])
            dg_ref[:, c] = dot_nt(dy_ref[...], wdn[at, c, :])

    def gelu_strips(f, first, last):
        total = None
        for r in range(first, last, strip):
            at = slice(r, r + strip)
            z = z_ref[at, :] + vec_ref[BUP + f:BUP + f + 1, :]
            z2 = z * z
            th = jnp.tanh(z * (0.7978845608028654 + (0.7978845608028654 * 0.044715) * z2))
            half_more = 0.5 + 0.5 * th
            g_ref[f % 2, at, :] = (z * half_more).astype(BF16)
            slope = half_more + (0.5 * z) * (1.0 - th * th) * (
                0.7978845608028654 + (3.0 * 0.044715 * 0.7978845608028654) * z2
            )
            dz = (dg_ref[at, :] * slope).astype(BF16)
            dz_ref[f % 2, at, :] = dz
            here = fold_rows(dz.astype(F32))
            total = here if total is None else total + here
        at = slice(8 * (4 + f), 8 * (4 + f) + 8)
        if first == 0:
            sums_ref[at, :] = total
        else:
            sums_ref[at, :] += total

    def out_of_tile(f):
        at = f % ring
        slot = f % 2

        def up(c):
            acc[:, c] += dot_nn(g_ref[slot], wdn[at, :, c])
            dh2[:, c] += dot_nt(dz_ref[slot], wup[at, c, :])

        def turn_g(c):
            gt[c, :] = turn(g_ref[slot, :, c])

        def grad_down(k, c):
            put(slot, k * per_piece, dot_nn(gt[...], dy_ref[:, c]).astype(BF16), cols, per_piece, per)

        def grad_up(k, c):
            first = per * cols + k * per_piece
            put(slot, first, dot_nn(h2t[...], dz_ref[slot, :, c]).astype(BF16), per, per_piece, cols)

        steps = [functools.partial(up, c) for c in pieces(width)]
        steps += [functools.partial(grad_up, k, c) for k, c in enumerate(pieces(tile))]
        steps += [functools.partial(turn_g, c) for c in pieces(tile)]
        steps += [functools.partial(grad_down, k, c) for k, c in enumerate(pieces(width))]
        return steps

    def send_tile(f):
        slot = f % 2
        for i in range(per):
            for j in range(cols):
                leave(slot, j * per + i, first_dn + (f * cols + j) * per + i)
            for j in range(cols):
                leave(slot, per * cols + i * cols + j, first_up + i * fper + f * cols + j)

    for f in range(tiles + 1):
        if f < tiles:
            into_tile(f)
        steps = out_of_tile(f - 1) if f > 0 else []
        if f > 2:
            left((f - 1) % 2, full)
        share = rows // max(len(steps), 1)
        if f < tiles:
            for n in range(max(len(steps), 1)):
                gelu_strips(f, n * share // strip * strip, rows if n + 1 >= len(steps) else (n + 1) * share // strip * strip)
                if steps:
                    steps[n]()
        else:
            for step in steps:
                step()
        if f > 0:
            send_tile(f - 1)
            if f - 1 + ring < tiles:
                fetch_tile(f - 1 + ring)

    zero = jnp.zeros((8, width), F32)
    da_ref = h2_ref
    dx1_ref = x1

    def finish(r, carry):
        s_bo, s_gain, s_shift, s_bdown = carry
        at = rows_at(r)
        act_ref[at, :] = acc[at, :].astype(BF16)
        centred, inv = layer_stats(x1[at, :])
        hat = centred * inv
        dh = dh2[at, :]
        dhg = dh * vec_ref[GAIN2:GAIN2 + 1, :]
        back = inv * (
            dhg
            - jnp.mean(dhg, axis=-1, keepdims=True)
            - hat * jnp.mean(dhg * hat, axis=-1, keepdims=True)
        )
        dy = dy_ref[at, :].astype(F32)
        dx1 = dy + back
        dx1_ref[at, :] = dx1
        da = dx1.astype(BF16)
        da_ref[at, :] = da
        return (
            s_bo + fold_rows(da.astype(F32)),
            s_gain + fold_rows(dh * hat),
            s_shift + fold_rows(dh),
            s_bdown + fold_rows(dy),
        )

    carry = lax.fori_loop(0, rows // chunk, finish, (zero, zero, zero, zero))
    for n in range(4):
        sums_ref[8 * n:8 * n + 8, :] = carry[n]
    outs = [
        pltpu.make_async_copy(act_ref, act_out, sem_w.at[0]),
        pltpu.make_async_copy(dx1_ref, dx1_out, sem_w.at[1]),
        pltpu.make_async_copy(do_ref, do_out, sem_w.at[2]),
    ]
    outs[0].start()
    outs[1].start()
    for half in range(2):
        c = slice(half * width // 2, (half + 1) * width // 2)
        res = dot_nt(da_ref[...], wo[c, :]).astype(BF16)
        for d in range(nd // 2):
            do_ref[half * (nd // 2) + d] = res[:, d * lanes:(d + 1) * lanes]
    outs[2].start()
    left(0, full)
    left(1, full)
    half_rows = width // 2
    for half in range(2):
        res = dot_nn(attt[half * half_rows:(half + 1) * half_rows, :], da_ref[...]).astype(BF16)
        put(half, 0, res, per // 2, per, per)

        for i in range(per // 2):
            for j in range(per):
                leave(half, i * per + j, first_o + (half * (per // 2) + i) * per + j)
    for half in range(2):
        left(half, per * per // 2)
    for copy in outs:
        copy.wait()


def run_mlp(slot_of, att, x, dy, vec, gath, nd):
    rows, width = x.shape
    side = gath.shape[1]
    lanes = width // nd
    per = width // side
    first_o = 3 * per * per
    first_up = first_o + per * per
    first_dn = first_up + per * (FF // side)
    tile = width
    f32_rows = pltpu.VMEM((rows, width), F32)
    bf16_rows = pltpu.VMEM((rows, width), BF16)
    turned = pltpu.VMEM((width, rows), BF16)
    return pl.pallas_call(
        functools.partial(
            mlp_kernel, nd=nd, first_o=first_o, first_up=first_up, first_dn=first_dn, tile=tile
        ),
        out_shape=(
            sds((rows, width), BF16),
            sds((rows, width), F32),
            sds((nd, rows, lanes), BF16),
            sds((8 * (4 + FF // width), width), F32),
            sds(gath.shape, BF16),
        ),
        in_specs=[smem(), hbm(), hbm(), hbm(), vmem(), hbm()],
        out_specs=(hbm(), hbm(), hbm(), vmem(), hbm()),
        scratch_shapes=[
            bf16_rows,
            bf16_rows,
            bf16_rows,
            pltpu.SemaphoreType.DMA((3,)),
            pltpu.VMEM((width, width), BF16),
            pltpu.VMEM((3, width, tile), BF16),
            pltpu.VMEM((3, tile, width), BF16),
            f32_rows,
            f32_rows,
            f32_rows,
            bf16_rows,
            turned,
            turned,
            pltpu.VMEM((tile, rows), BF16),
            bf16_rows,
            pltpu.VMEM((rows, tile), F32),
            pltpu.VMEM((rows, tile), F32),
            pltpu.VMEM((2, rows, tile), BF16),
            pltpu.VMEM((2, rows, tile), BF16),
            pltpu.VMEM((nd, rows, lanes), BF16),
            pltpu.VMEM((2, 2 * per * (tile // side), side, side), BF16),
            pltpu.SemaphoreType.DMA((1,)),
            pltpu.SemaphoreType.DMA((FF // tile,)),
            pltpu.SemaphoreType.DMA((2,)),
            pltpu.SemaphoreType.DMA((3,)),
        ],
        compiler_params=params(),
        name="mlp",
    )(slot_of, att, x, dy, vec, gath)


def dh1_dot(cat, w, dh1, part, half):
    width = dh1.shape[1]
    c = slice(half * width // 2, (half + 1) * width // 2)
    res = dot_nt(cat[:, part * width:(part + 1) * width], w[part, c, :])
    if part == 0:
        dh1[:, c] = res
    else:
        dh1[:, c] += res


def first_norm_back(cat, x, dh1, dx1, ig, vec_ref):
    rows, width = x.shape
    chunk = 128
    zero = jnp.zeros((8, width), F32)

    def finish(r, carry):
        s_gain, s_shift, s_bq, s_bv = carry
        at = pl.ds(pl.multiple_of(r * chunk, chunk), chunk)
        centred, inv = layer_stats(x[at, :].astype(F32))
        hat = centred * inv
        dh = dh1[at, :]
        dhg = dh * vec_ref[GAIN1:GAIN1 + 1, :]
        back = inv * (
            dhg
            - jnp.mean(dhg, axis=-1, keepdims=True)
            - hat * jnp.mean(dhg * hat, axis=-1, keepdims=True)
        )
        ig[at, :] = dx1[at, :] + back
        return (
            s_gain + fold_rows(dh * hat),
            s_shift + fold_rows(dh),
            s_bq + fold_rows(cat[at, 0:width].astype(F32)),
            s_bv + fold_rows(cat[at, 2 * width:3 * width].astype(F32)),
        )

    return lax.fori_loop(0, rows // chunk, finish, (zero, zero, zero, zero))


def vector_rows(first, sums2):
    rows = [jnp.sum(v, axis=0, keepdims=True) for v in first]
    rows += [jnp.sum(sums2[8 * n:8 * n + 8, :], axis=0, keepdims=True) for n in range(sums2.shape[0] // 8)]
    return rows


def dh1_kernel(cat_ref, x_ref, dx1_ref, vec_ref, wq_ref, sums2_ref, ig_ref, vsum_ref, dh1):
    for part in range(3):
        for half in range(2):
            dh1_dot(cat_ref, wq_ref, dh1, part, half)
    first = first_norm_back(cat_ref, x_ref, dh1, dx1_ref, ig_ref, vec_ref)
    for n, row in enumerate(vector_rows(first, sums2_ref)):
        vsum_ref[n:n + 1, :] = row


def run_dh1(cat, x, dx1, vec, wq, sums2):
    rows, width = x.shape
    return pl.pallas_call(
        dh1_kernel,
        out_shape=(sds((rows, width), F32), sds(vec.shape, F32)),
        in_specs=[vmem()] * 6,
        out_specs=(vmem(), vmem()),
        scratch_shapes=[pltpu.VMEM((rows, width), F32)],
        compiler_params=params(),
        name="dh1",
    )(cat, x, dx1, vec, wq, sums2)


def wgrad_kernel(slot_ref, h1_ref, cat_ref, rest, out, a_t, stage, sem_out, *, side, tile):
    del rest
    rows, width = h1_ref.shape
    per = width // side
    cols = tile // side
    steps = cat_ref.shape[1] // tile
    for r in range(width // 256):
        c = slice(r * 256, (r + 1) * 256)
        a_t[c, :] = turn(h1_ref[:, c])

    def left(slot):
        pltpu.make_async_copy(stage.at[slot], stage.at[slot], sem_out.at[slot]).wait()

    @pl.loop(0, steps)
    def _(t):
        slot = lax.rem(t, 2)

        @pl.when(t >= 2)
        def _():
            left(slot)
        res = dot_nn(a_t[...], cat_ref[:, pl.ds(pl.multiple_of(t * tile, tile), tile)]).astype(BF16)
        for i in range(per):
            for j in range(cols):
                stage[slot, i * cols + j] = res[i * side:(i + 1) * side, j * side:(j + 1) * side]

        for i in range(per):
            for j in range(cols):
                dst = slot_at(slot_ref, i * 3 * per + t * cols + j)
                pltpu.make_async_copy(stage.at[slot, i * cols + j], out.at[dst], sem_out.at[slot]).start()

    left(0)
    left(1)


def run_wgrad(slot_of, h1, cat, grads):
    rows, width = h1.shape
    side = grads.shape[1]
    tile = 512
    return pl.pallas_call(
        functools.partial(wgrad_kernel, side=side, tile=tile),
        out_shape=sds(grads.shape, BF16),
        in_specs=[smem(), vmem(), vmem(), hbm()],
        out_specs=hbm(),
        scratch_shapes=[
            pltpu.VMEM((width, rows), BF16),
            pltpu.VMEM((2, (width // side) * (tile // side), side, side), BF16),
            pltpu.SemaphoreType.DMA((2,)),
        ],
        input_output_aliases={3: 0},
        compiler_params=params(),
        name="wgrad",
    )(slot_of, h1, cat, grads)


def whereami():
    g = lax.axis_index("grp")
    d = lax.axis_index("dev")
    core = lax.rem(d, 2)
    x = lax.rem(d // 2, 2)
    y = d // 4
    over_x = d + 2 - 4 * x
    over_y = d + 4 - 8 * y
    across = over_x + 4 - 8 * y
    sibling = d + 1 - 2 * core
    return g, d, over_x, over_y, across, sibling


def near_order(t, g, ng):
    t = ng - 1 - t
    low = jnp.where(t < ng - 1 - g, ng - 1 - t, t - (ng - 1 - g))
    high = jnp.where(t < g, t, ng - 1 - (t - g))
    return jnp.where(2 * g < ng, low, high)


def greet(g, ng, peers):
    barrier = pltpu.get_barrier_semaphore()
    for peer in peers:
        pl.semaphore_signal(barrier, inc=1, device_id=(g, peer), device_id_type=MESH)

    d = lax.axis_index("dev")

    @pl.when(g > 0)
    def _():
        pl.semaphore_signal(barrier, inc=1, device_id=(g - 1, d), device_id_type=MESH)

    @pl.when(g < ng - 1)
    def _():
        pl.semaphore_signal(barrier, inc=1, device_id=(g + 1, d), device_id_type=MESH)

    ends = (g > 0).astype(jnp.int32) + (g < ng - 1).astype(jnp.int32)
    pl.semaphore_wait(barrier, len(peers) + ends)


def slot_cuts(count):
    third = 2 * (count // 12)
    first = (count - third) // 2
    return first, count - third - first, third // 2, third // 2


def gather_kernel(
    w_ref, x_ref, block_ref, vin_ref, out, h1_ref, slot_ref, vec_ref,
    own, local_sem, zs, zr, cs, cr, ss, sr, *, ng, nd
):
    count = w_ref.shape[0]
    na, nb, nc1, nc2 = slot_cuts(count)
    flat = na + nb
    nc = nc1 + nc2
    g, d, over_x, over_y, across, sibling = whereami()
    columns = (d, over_x, over_y, across)
    own[...] = w_ref[...].astype(BF16)
    greet(g, ng, (over_x, over_y, sibling))

    def region(gz, dev, first=0, size=count):
        return out.at[pl.ds((gz * nd + dev) * count + first, size)]

    def wide(t):
        return count if t == 0 else flat

    def kind(n, t):
        return (
            (d, 0, wide(t), over_x),
            (d, 0, wide(t), over_y),
            (d, 0, wide(t), sibling),
            (over_x, 0, na, over_y),
            (over_y, na, nb, over_x),
            (over_x, 0, wide(t), sibling),
            (over_y, 0, wide(t), sibling),
            (across, 0, na, sibling),
            (across, na, nb, sibling),
            (over_x, flat, nc1, over_y),
            (over_y, flat + nc1, nc2, over_x),
            (across, flat, nc1, sibling),
            (across, flat + nc1, nc2, sibling),
            (d, flat, nc, sibling),
            (over_x, flat, nc, sibling),
            (over_y, flat, nc, sibling),
            (across, flat, nc, sibling),
        )[n]

    def kinds(t):
        return range(13) if t == 0 else tuple(range(9)) + tuple(range(13, 17))

    def plane(n, t, src=None):
        gz = near_order(t, g, ng)
        dev, first, size, to = kind(n, t)
        at = region(gz, dev, first, size)
        return remote(at if src is None else src, at, ss.at[n, gz], sr.at[n, gz], (g, to))

    def landed(n, t, dev):
        gz = near_order(t, g, ng)
        _, first, size, _ = kind(n, t)
        arrived(region(gz, dev, first, size), sr.at[n, gz])

    def line(gz, up, src=None):
        at = region(gz, d, 0, flat)
        to = g + 1 if up else g - 1
        return remote(at if src is None else src, at, zs.at[gz, int(up)], zr.at[gz], (to, d))

    def corner_line(gz, c, up, src=None):
        at = region(gz, columns[c], flat, nc)
        to = g + 1 if up else g - 1
        return remote(at if src is None else src, at, cs.at[gz, c, int(up)], cr.at[gz, c], (to, d))

    def both_ways(gz, make):
        @pl.when((gz <= g) & (g < ng - 1))
        def _():
            make(True)

        @pl.when((gz >= g) & (g > 0))
        def _():
            make(False)

    mine = pltpu.make_async_copy(own, region(g, d), local_sem.at[0])
    mine.start()

    def column(t):
        gz = near_order(t, g, ng)
        if t == 0:
            both_ways(gz, lambda up: line(gz, up, cut(own, 0, flat)).start())
            for n in range(3):
                plane(n, t, own).start()
            both_ways(gz, lambda up: corner_line(gz, 0, up, cut(own, flat, nc)).start())
            return
        arrived(region(gz, d, 0, flat), zr.at[gz])
        both_ways(gz, lambda up: line(gz, up).start())
        for n in range(3):
            plane(n, t).start()

    def over_x_side(t):
        gz = near_order(t, g, ng)
        landed(0, t, over_x)
        plane(3, t).start()
        if t == 0:
            plane(9, t).start()
            both_ways(gz, lambda up: corner_line(gz, 1, up).start())
        plane(5, t).start()

    def over_y_side(t):
        gz = near_order(t, g, ng)
        landed(1, t, over_y)
        plane(4, t).start()
        if t == 0:
            plane(10, t).start()
            both_ways(gz, lambda up: corner_line(gz, 2, up).start())
        plane(6, t).start()

    def first_corner():
        landed(9, 0, across)
        landed(10, 0, across)
        both_ways(g, lambda up: corner_line(g, 3, up).start())
        plane(11, 0).start()
        plane(12, 0).start()

    def corner_x(t):
        landed(3, t, across)
        plane(7, t).start()

    def corner_y(t):
        landed(4, t, across)
        plane(8, t).start()

    def far_corner(t, c):
        gz = near_order(t, g, ng)
        arrived(region(gz, columns[c], flat, nc), cr.at[gz, c])
        both_ways(gz, lambda up: corner_line(gz, c, up).start())
        plane(13 + c, t).start()

    plan = [(t, column, (t,)) for t in range(ng)]
    plan += [(t + 1.5, side, (t,)) for t in range(ng) for side in (over_x_side, over_y_side)]
    plan += [(t + 2.61, side, (t,)) for t in range(ng) for side in (corner_x, corner_y)]
    plan += [(t + 2.2, far_corner, (t, c)) for t in range(1, ng) for c in range(4)]
    plan += [(2.6, first_corner, ())]
    plan = [(step, args) for _, step, args in sorted(plan, key=lambda e: e[0])]
    if ng == 4:
        plan = [
            (column, (0,)), (column, (1,)), (over_y_side, (0,)), (over_x_side, (0,)),
            (column, (2,)), (far_corner, (1, 1)), (over_x_side, (1,)), (over_y_side, (1,)),
            (column, (3,)), (first_corner, ()), (over_y_side, (2,)), (corner_y, (0,)),
            (far_corner, (2, 1)), (far_corner, (1, 3)), (far_corner, (1, 0)), (corner_y, (1,)),
            (over_x_side, (2,)), (far_corner, (2, 2)), (far_corner, (1, 2)), (corner_x, (1,)),
            (far_corner, (3, 3)), (corner_x, (0,)), (far_corner, (2, 3)), (far_corner, (3, 1)),
            (far_corner, (3, 0)), (over_x_side, (3,)), (over_y_side, (3,)), (far_corner, (2, 0)),
            (corner_y, (2,)), (far_corner, (3, 2)), (corner_x, (2,)), (corner_y, (3,)),
            (corner_x, (3,)),
        ]
    for n, (step, args) in enumerate(plan):
        step(*args)
        if n == 0:
            prepare(x_ref, block_ref, vin_ref, h1_ref, slot_ref, vec_ref)

    for t in range(ng):
        for n in kinds(t):
            dev, _, _, to = kind(n, t)
            if to is sibling:
                landed(n, t, dev + sibling - d)
    mine.wait()
    for t in range(ng):
        gz = near_order(t, g, ng)
        for n in kinds(t):
            plane(n, t).wait_send()
        both_ways(gz, lambda up: line(gz, up).wait_send())
        for c in range(4):
            both_ways(gz, lambda up: corner_line(gz, c, up).wait_send())


def run_gather(w, x, blocks, vin, ng, nd):
    count, side, _ = w.shape
    dma = pltpu.SemaphoreType.DMA
    return pl.pallas_call(
        functools.partial(gather_kernel, ng=ng, nd=nd),
        out_shape=(sds((ng * nd * count, side, side), BF16),) + prepared_shapes(x, blocks, vin),
        in_specs=[vmem()] * 4,
        out_specs=(hbm(), vmem(), vmem(), vmem()),
        scratch_shapes=[
            pltpu.VMEM((count, side, side), BF16),
            dma((1,)),
            dma((ng, 2)),
            dma((ng,)),
            dma((ng, 4, 2)),
            dma((ng, 4)),
            dma((17, ng)),
            dma((17, ng)),
        ],
        compiler_params=params(collective_id=0, has_side_effects=True),
        name="gather",
    )(w, x, blocks, vin)


def add_blocks(dst, src, size):
    step = next(n for n in (4, 5, 3, 2, 1) if size % n == 0)

    @pl.loop(0, size // step)
    def _(n):
        for k in range(step):
            dst[n * step + k] = dst[n * step + k] + src[n * step + k]


def scatter_kernel(
    grads, sums2_ref, vec_ref, vin_ref, cat_in, x_in, dx1_in, wq_in, out_ref, vout_ref, vnew_ref, ig_out,
    cat, x, dx1, wq, dh1, sem_in, mine, r0, r1y, r1x, r2x, r2y, rz, cz, cy, cx, cx2, cy2, vwork, vxy, vz,
    load, s0, w0, s1, w1, s2, w2, sz, wz, sc, wc, s3, w3, vs, vw, *, ng, nd, rate
):
    count = out_ref.shape[0]
    na, nb, nc1, nc2 = slot_cuts(count)
    flat = na + nb
    nc = nc1 + nc2
    g, d, over_x, over_y, across, sibling = whereami()
    columns = (d, over_x, over_y, across)

    def region(gz, dev):
        return grads.at[pl.ds((gz * nd + dev) * count, count)]

    def order(t):
        return near_order(ng - 1 - t, g, ng)

    for t in range(ng):
        for c in range(4):
            pltpu.make_async_copy(region(order(t), columns[c]), mine.at[order(t), c], load.at[order(t), c]).start()
    greet(g, ng, (over_x, over_y, sibling))

    def to_sibling(gz, c):
        return remote(
            region(gz, columns[c] + sibling - d), r0.at[gz, c], s0.at[gz, c], w0.at[gz, c], (g, sibling)
        )

    peers = (sibling, over_x, over_y)

    def vec_copy(n):
        return remote(vwork.at[n], vxy.at[n], vs.at[n], vw.at[n], (g, peers[n]))

    for t in range(ng):
        for c in (3, 2, 1, 0):
            to_sibling(order(t), c).start()
    inputs = [
        pltpu.make_async_copy(cat_in, cat, sem_in.at[0]),
        pltpu.make_async_copy(wq_in, wq, sem_in.at[1]),
        pltpu.make_async_copy(x_in, x, sem_in.at[2]),
        pltpu.make_async_copy(dx1_in, dx1, sem_in.at[3]),
    ]
    for copy in inputs:
        copy.start()
    input_grad = pltpu.make_async_copy(dx1, ig_out, sem_in.at[4])

    def first_norm():
        for copy in inputs:
            copy.wait()
        for part in range(3):
            for half in range(2):
                dh1_dot(cat, wq, dh1, part, half)
        first = first_norm_back(cat, x, dh1, dx1, dx1, vec_ref)
        input_grad.start()
        for n, row in enumerate(vector_rows(first, sums2_ref)):
            vwork[0, n:n + 1, :] = row
        vec_copy(0).start()

    first = (
        (2, 0, na, r1y, 0, over_y),
        (3, 0, na, r1y, 1, over_y),
        (1, na, nb, r1x, 0, over_x),
        (3, na, nb, r1x, 1, over_x),
    )
    second = ((1, 0, na, r2x, over_x), (2, na, nb, r2y, over_y))
    third = (
        (2, flat, nc1, cy.at[0], over_y),
        (3, flat, nc1, cy.at[1], over_y),
        (1, flat + nc1, nc2, cx.at[0], over_x),
        (3, flat + nc1, nc2, cx.at[1], over_x),
        (1, flat, nc1, cx2, over_x),
        (2, flat + nc1, nc2, cy2, over_y),
    )

    def copy1(n, gz):
        c, at, size, buf, place_at, to = first[n]
        return remote(cut(mine.at[gz, c], at, size), buf.at[gz, place_at], s1.at[n, gz], w1.at[n, gz], (g, to))

    def copy2(n, gz):
        c, at, size, buf, to = second[n]
        return remote(cut(mine.at[gz, c], at, size), buf.at[gz], s2.at[n, gz], w2.at[n, gz], (g, to))

    def copy3(n):
        c, at, size, buf, to = third[n]
        return remote(cut(mine.at[g, c], at, size), buf, s3.at[n], w3.at[n], (g, to))

    def flat_part(gz):
        return cut(mine.at[gz, 0], 0, flat)

    def corner_part(gz):
        return mine.at[gz, :, pl.ds(flat, nc)]

    def line(gz, part, buf, sends, waits, up):
        at = gz if up else jnp.where(gz < g - 1, gz, ng)
        to = g + 1 if up else g - 1
        return remote(part(gz), buf.at[at], sends.at[gz], waits.at[at], (to, d))

    def pass_on(gz, part, buf, sends, waits, gather):
        @pl.when(gz > g)
        def _():
            @pl.when(g > 0)
            def _():
                arrived(buf.at[gz], waits.at[gz])
                gather(gz)
            line(gz, part, buf, sends, waits, True).start()

        @pl.when(gz < g)
        def _():
            @pl.when(g < ng - 1)
            def _():
                arrived(buf.at[gz], waits.at[gz])
                gather(gz)
            line(gz, part, buf, sends, waits, False).start()

    def gather_flat(gz):
        add_blocks(flat_part(gz), rz.at[gz], flat)

    def gather_corner(at, gz):
        for c in range(4):
            add_blocks(cut(mine.at[gz, c], flat, nc), cz.at[at, c], nc)

    def sums0(t, c):
        gz = order(t)
        pltpu.make_async_copy(region(gz, columns[c]), mine.at[gz, c], load.at[gz, c]).wait()
        arrived(r0.at[gz, c], w0.at[gz, c])
        add_blocks(mine.at[gz, c], r0.at[gz, c], count)
        for n in {3: (1, 3), 2: (0,), 1: (2,), 0: ()}[c]:
            copy1(n, gz).start()

    def along0(t):
        pass_on(order(t), corner_part, cz, sc, wc, lambda gz: gather_corner(gz, gz))

    def stage1(t, k):
        gz = order(t)
        c, at, size, buf, n = (
            (1, 0, na, r1y.at[gz, 1], 1),
            (2, na, nb, r1x.at[gz, 1], 3),
            (0, 0, na, r1y.at[gz, 0], 0),
            (0, na, nb, r1x.at[gz, 0], 2),
        )[k]
        arrived(buf, w1.at[n, gz])
        add_blocks(cut(mine.at[gz, c], at, size), buf, size)
        if k < 2:
            copy2(k, gz).start()

    def stage2(t, k):
        gz = order(t)
        at, size, buf = ((0, na, r2x.at[gz]), (na, nb, r2y.at[gz]))[k]
        arrived(buf, w2.at[k, gz])
        add_blocks(cut(mine.at[gz, 0], at, size), buf, size)

    def along1(t):
        pass_on(order(t), flat_part, rz, sz, wz, gather_flat)

    def corner0():
        @pl.when(g > 0)
        def _():
            arrived(cz.at[g], wc.at[g])
            gather_corner(g, g)

        @pl.when(g < ng - 1)
        def _():
            arrived(cz.at[ng], wc.at[ng])
            gather_corner(ng, g)
        for n in range(4):
            copy3(n).start()

    def corner1():
        arrived(cy.at[1], w3.at[1])
        add_blocks(cut(mine.at[g, 1], flat, nc1), cy.at[1], nc1)
        copy3(4).start()
        arrived(cx.at[1], w3.at[3])
        add_blocks(cut(mine.at[g, 2], flat + nc1, nc2), cx.at[1], nc2)
        copy3(5).start()
        arrived(cy.at[0], w3.at[0])
        add_blocks(cut(mine.at[g, 0], flat, nc1), cy.at[0], nc1)
        arrived(cx.at[0], w3.at[2])
        add_blocks(cut(mine.at[g, 0], flat + nc1, nc2), cx.at[0], nc2)

    def corner2():
        arrived(cx2, w3.at[4])
        add_blocks(cut(mine.at[g, 0], flat, nc1), cx2, nc1)
        arrived(cy2, w3.at[5])
        add_blocks(cut(mine.at[g, 0], flat + nc1, nc2), cy2, nc2)

    def vec_step(n):
        arrived(vxy.at[n], vw.at[n])
        total = vwork[n] + vxy[n]
        if n < 2:
            vwork[n + 1] = total
            vec_copy(n + 1).start()
        else:
            vz[g] = total

    def vec_line(gz, up):
        to = g + 1 if up else g - 1
        return remote(vz.at[gz], vz.at[gz], vs.at[3 + 2 * gz + int(up)], vw.at[3 + gz], (to, d))

    def vec_first_line():
        vec_step(2)

        @pl.when(g < ng - 1)
        def _():
            vec_line(g, True).start()

        @pl.when(g > 0)
        def _():
            vec_line(g, False).start()

    def vec_next_line(n):
        gz = near_order(n, g, ng)
        arrived(vz.at[gz], vw.at[3 + gz])

        @pl.when((gz < g) & (g < ng - 1))
        def _():
            vec_line(gz, True).start()

        @pl.when((gz > g) & (g > 0))
        def _():
            vec_line(gz, False).start()

    def vec_out():
        total = vz[0]
        for z in range(1, ng):
            total = total + vz[z]
        vwork[3] = total
        per = total.shape[1] // 128
        for r in range(total.shape[0]):
            for c in range(per):
                row = vwork[3, r:r + 1, c * 128:(c + 1) * 128]
                n = per * r + c
                vout_ref[n:n + 1, :] = row
                vnew_ref[n:n + 1, :] = vin_ref[n:n + 1, :] - rate * row

    last = ng - 1
    plan = [(t + 0.25 * (3 - c), sums0, (t, c)) for t in range(ng) for c in range(4)]
    plan += [(t + 1.2 + 0.3 * (k // 2), stage1, (t, k)) for t in range(ng) for k in range(4)]
    plan += [(t + 2.2, stage2, (t, k)) for t in range(ng) for k in range(2)]
    plan += [(t + 1.15, along0, (t,)) for t in range(last)]
    plan += [(t + 2.21, along1, (t,)) for t in range(last)]
    plan += [(last + 1.3, corner0, ()), (last + 2.19, corner1, ()), (last + 2.4, corner2, ())]
    plan += [(0.3, first_norm, ()), (0.9, vec_step, (0,)), (2.0, vec_step, (1,)), (3.0, vec_first_line, ())]
    plan += [(3.1 + 0.55 * n, vec_next_line, (n,)) for n in range(1, ng)]
    plan += [(last + 2.17, vec_out, ())]
    plan = [(step, args) for _, step, args in sorted(plan, key=lambda e: e[0])]
    if ng == 4:
        plan = [
            (sums0, (0, 3)), (sums0, (0, 2)), (first_norm, ()), (sums0, (0, 1)),
            (sums0, (0, 0)), (stage1, (0, 1)), (sums0, (1, 3)), (vec_step, (0,)),
            (along0, (0,)), (stage1, (0, 0)), (sums0, (1, 2)), (sums0, (1, 0)),
            (sums0, (1, 1)), (along0, (1,)), (stage1, (1, 1)), (stage1, (0, 3)),
            (vec_step, (1,)), (sums0, (2, 3)), (stage2, (0, 0)), (stage1, (1, 0)),
            (stage1, (0, 2)), (stage2, (0, 1)), (sums0, (2, 1)), (along1, (0,)),
            (sums0, (2, 2)), (sums0, (2, 0)), (along0, (2,)), (stage1, (1, 2)), (vec_first_line, ()),
            (sums0, (3, 3)), (stage2, (1, 0)), (sums0, (3, 0)),
            (stage1, (2, 1)), (sums0, (3, 2)), (stage1, (2, 0)),
            (stage1, (1, 3)), (stage2, (1, 1)), (stage1, (2, 2)), (vec_next_line, (1,)), (sums0, (3, 1)),
            (along1, (1,)), (stage2, (2, 0)), (stage2, (2, 1)), (stage1, (2, 3)),
            (stage1, (3, 1)), (along1, (2,)), (corner0, ()), (vec_next_line, (2,)),
            (stage1, (3, 0)), (stage2, (3, 1)), (stage1, (3, 2)), (stage1, (3, 3)),
            (vec_next_line, (3,)), (corner1, ()), (vec_out, ()), (corner2, ()),
            (stage2, (3, 0)),
        ]
    for step, args in plan:
        step(*args)

    @pl.when(g > 0)
    def _():
        arrived(rz.at[g], wz.at[g])

    @pl.when(g < ng - 1)
    def _():
        arrived(rz.at[ng], wz.at[ng])

    @pl.when((g > 0) & (g < ng - 1))
    def _():
        @pl.loop(0, flat)
        def _(i):
            out_ref[i] = mine[g, 0, i].astype(F32) + rz[g, i].astype(F32) + rz[ng, i].astype(F32)

    @pl.when(g == 0)
    def _():
        @pl.loop(0, flat)
        def _(i):
            out_ref[i] = mine[g, 0, i].astype(F32) + rz[ng, i].astype(F32)

    @pl.when((g > 0) & (g == ng - 1))
    def _():
        @pl.loop(0, flat)
        def _(i):
            out_ref[i] = mine[g, 0, i].astype(F32) + rz[g, i].astype(F32)

    for i in range(flat, count):
        out_ref[i] = mine[g, 0, i].astype(F32)

    for t in range(ng):
        gz = order(t)
        for c in range(4):
            to_sibling(gz, c).wait_send()
        for n in range(4):
            copy1(n, gz).wait_send()
        for n in range(2):
            copy2(n, gz).wait_send()
        if t < ng - 1:
            arrived(flat_part(gz), sz.at[gz])
            arrived(corner_part(gz), sc.at[gz])
    input_grad.wait()
    for n in range(6):
        copy3(n).wait_send()
    for n in range(3):
        vec_copy(n).wait_send()
    for n in range(ng):
        gz = near_order(n, g, ng)

        @pl.when((gz <= g) & (g < ng - 1))
        def _():
            vec_line(gz, True).wait_send()

        @pl.when((gz >= g) & (g > 0))
        def _():
            vec_line(gz, False).wait_send()


def run_scatter(grads, sums2, vec, vin, cat, x, dx1, wq, ng, nd, rate):
    blocks, side, _ = grads.shape
    count = blocks // (ng * nd)
    na, nb, nc1, nc2 = slot_cuts(count)
    flat = na + nb
    dma = pltpu.SemaphoreType.DMA

    def buf(*lead):
        return pltpu.VMEM(lead + (side, side), BF16)

    def like(v):
        return pltpu.VMEM(v.shape, v.dtype)

    return pl.pallas_call(
        functools.partial(scatter_kernel, ng=ng, nd=nd, rate=rate),
        out_shape=(
            sds((count, side, side), F32),
            sds(vin.shape, F32),
            sds(vin.shape, F32),
            sds(dx1.shape, F32),
        ),
        in_specs=[hbm(), vmem(), vmem(), vmem()] + [hbm()] * 4,
        out_specs=(vmem(), vmem(), vmem(), hbm()),
        scratch_shapes=[
            like(cat),
            like(x),
            like(dx1),
            like(wq),
            like(dx1),
            dma((5,)),
            buf(ng, 4, count),
            buf(ng, 4, count),
            buf(ng, 2, na),
            buf(ng, 2, nb),
            buf(ng, na),
            buf(ng, nb),
            buf(ng + 1, flat),
            buf(ng + 1, 4, nc1 + nc2),
            buf(2, nc1),
            buf(2, nc2),
            buf(nc1),
            buf(nc2),
            pltpu.VMEM((4,) + vec.shape, F32),
            pltpu.VMEM((3,) + vec.shape, F32),
            pltpu.VMEM((ng,) + vec.shape, F32),
            dma((ng, 4)),
            dma((ng, 4)),
            dma((ng, 4)),
            dma((4, ng)),
            dma((4, ng)),
            dma((2, ng)),
            dma((2, ng)),
            dma((ng,)),
            dma((ng + 1,)),
            dma((ng,)),
            dma((ng + 1,)),
            dma((6,)),
            dma((6,)),
            dma((3 + 2 * ng,)),
            dma((3 + ng,)),
        ],
        compiler_params=params(61, collective_id=1, has_side_effects=True),
        name="scatter",
    )(grads, sums2, vec, vin, cat, x, dx1, wq)


def blocks_kernel(*refs, handed):
    g_ref, w_ref, ls_ref, rs_ref, lr_ref, rr_ref = refs[:6]
    wg_out, nl_out, nr_out, nw_out = refs[6 + handed:10 + handed]
    for n in range(handed):
        refs[10 + handed + n][...] = refs[6 + n][...]

    for i in range(g_ref.shape[0]):
        grad = g_ref[i]
        wg_out[i] = grad
        hi = grad.astype(BF16)
        low = (grad - hi.astype(F32)).astype(BF16)
        nl_out[i] = 0.5 * ls_ref[i] + 0.5 * dot_nt(hi, hi)
        turned = grad.T
        hi_t = turned.astype(BF16)
        nr_out[i] = 0.5 * rs_ref[i] + 0.5 * dot_nt(hi_t, hi_t)
        left = lr_ref[i]
        left_hi = left.astype(BF16)
        left_low = (left - left_hi.astype(F32)).astype(BF16)
        shaped = dot_nn(left_hi, hi) + dot_nn(left_hi, low) + dot_nn(left_low, hi)
        right = rr_ref[i]
        right_hi = right.astype(BF16)
        right_low = (right - right_hi.astype(F32)).astype(BF16)
        sh_hi = shaped.astype(BF16)
        sh_low = (shaped - sh_hi.astype(F32)).astype(BF16)
        shaped = dot_nn(sh_hi, right_hi) + dot_nn(sh_low, right_hi) + dot_nn(sh_hi, right_low)
        nw_out[i] = w_ref[i] - weight_rate * shaped


def run_blocks(grads, weights, left_stats, right_stats, left_roots, right_roots, *passing):
    count, side, _ = grads.shape
    steps = math.gcd(count, 4)
    step = count // steps
    spec = pl.BlockSpec((step, side, side), lambda n: (n, 0, 0))
    through = []
    for v in passing:
        part = v.shape[0] // steps
        if part % 8 == 0:
            through.append(pl.BlockSpec((part, v.shape[1]), lambda n: (n, 0)))
        else:
            through.append(pl.BlockSpec(v.shape, lambda n: (0, 0)))
    return pl.pallas_call(
        functools.partial(blocks_kernel, handed=len(passing)),
        grid=(steps,),
        out_shape=tuple([sds(grads.shape, F32)] * 4) + tuple(sds(v.shape, v.dtype) for v in passing),
        in_specs=[spec] * 6 + through,
        out_specs=tuple([spec] * 4) + tuple(through),
        compiler_params=params(),
        name="blocks",
    )(grads, weights, left_stats, right_stats, left_roots, right_roots, *passing)


def local(
    inputs,
    cotangent,
    weight_slots,
    slot_block,
    left_stats,
    right_stats,
    left_roots,
    right_roots,
    vectors,
    span_start,
):
    seq_count, tok_count, width = inputs.shape
    rows = seq_count * tok_count
    nd = lax.axis_size("dev")
    ng = lax.axis_size("grp")
    side = weight_slots.shape[1]
    hpd = H // nd
    lanes = width // nd
    head = lax.axis_index("dev") * hpd + jnp.arange(hpd, dtype=jnp.int32)
    slopes = jnp.exp2(-8.0 * (head.astype(F32) + 1.0) / H)
    vin = vectors.reshape(-1, 128)
    held = slot_block.reshape(-1, 128)
    x = inputs.reshape(rows, width)
    dy = cotangent.reshape(rows, width)
    rate = vector_rate / math.sqrt(rows * nd * ng)

    direct = nd == 8
    if direct:
        gath, h1, slot_of, vec = run_gather(weight_slots, x, held, vin, ng, nd)
    else:
        gath = lax.all_gather(weight_slots.astype(BF16), ("grp", "dev"), axis=0, tiled=True)
        h1, slot_of, vec = run_prepare(x, held, vin)
    qkv, wq = run_qkv(slot_of, h1, vec, gath, nd)
    qkv, o, o32, lse = run_attn_fwd(
        span_start, slopes, qkv.reshape(nd, 3, seq_count, tok_count, lanes), hpd
    )
    att = side_by_side(o, 1, rows)
    act, dx1, do, sums2, grads = run_mlp(slot_of, att, x, dy, vec, gath, nd)
    do = do.reshape(nd, seq_count, tok_count, lanes)
    cat = side_by_side(run_attn_bwd(span_start, slopes, qkv, do, o32, lse, hpd), 3, rows)
    grads = run_wgrad(slot_of, h1, cat, grads)
    if direct:
        weight_grads, vector_grads, new_vectors, ig = run_scatter(
            grads, sums2, vec, vin, cat, x, dx1, wq, ng, nd, rate
        )
        passing = (ig, vector_grads, new_vectors)
    else:
        ig, vsum = run_dh1(cat, x, dx1, vec, wq, sums2)
        vector_grads = lax.psum(vsum.reshape(-1), ("grp", "dev"))
        new_vectors = vectors - rate * vector_grads
        weight_grads = lax.psum_scatter(grads, ("grp", "dev"), scatter_dimension=0, tiled=True)
        weight_grads = weight_grads.astype(F32)
        passing = ()
    weight_grads, new_left, new_right, new_weights, *passed = run_blocks(
        weight_grads, weight_slots, left_stats, right_stats, left_roots, right_roots, *passing
    )
    if direct:
        ig, vector_grads, new_vectors = passed
    return (
        act.reshape(inputs.shape),
        ig.reshape(inputs.shape),
        weight_grads,
        new_left,
        new_right,
        new_weights,
        vector_grads.reshape(-1),
        new_vectors.reshape(-1),
    )


def solution(mesh):
    return jax.shard_map(
        local,
        mesh=mesh,
        in_specs=(
            P("grp", "dev", None),
            P("grp", "dev", None),
            P(("grp", "dev"), None, None),
            P(),
            P(("grp", "dev"), None, None),
            P(("grp", "dev"), None, None),
            P(("grp", "dev"), None, None),
            P(("grp", "dev"), None, None),
            P(),
            P("grp"),
        ),
        out_specs=(
            P("grp", "dev", None),
            P("grp", "dev", None),
            P(("grp", "dev"), None, None),
            P(("grp", "dev"), None, None),
            P(("grp", "dev"), None, None),
            P(("grp", "dev"), None, None),
            P(),
            P(),
        ),
        check_vma=False,
    )
```

```python
import functools
import math

import jax
import jax.numpy as jnp
from jax import lax
from jax.experimental import pallas as pl
from jax.experimental.pallas import tpu as pltpu
from jax.sharding import PartitionSpec as P

H = 16
FF = 4096
PIC = 256

eps = 1e-05
weight_rate = 0.5
vector_rate = 0.5
big_negative = -1e30
highest = lax.Precision.HIGHEST
F32 = jnp.float32
BF16 = jnp.bfloat16
MIB = 1024 * 1024

GAIN1, SHIFT1, BQ, BV, BO, GAIN2, SHIFT2, BDOWN, BUP = range(9)


def dot_nn(a, b):
    return lax.dot_general(a, b, (((1,), (0,)), ((), ())), preferred_element_type=F32)


def dot_nt(a, b):
    return lax.dot_general(a, b, (((1,), (1,)), ((), ())), preferred_element_type=F32)


def turn(v):
    return v.astype(F32).T.astype(BF16)


def vmem():
    return pl.BlockSpec(memory_space=pltpu.VMEM)


def smem():
    return pl.BlockSpec(memory_space=pltpu.SMEM)


def hbm():
    return pl.BlockSpec(memory_space=pl.ANY)


def sds(shape, dtype):
    return jax.ShapeDtypeStruct(shape, dtype)


def params(mib=58, **kw):
    return pltpu.CompilerParams(vmem_limit_bytes=mib * MIB, **kw)


def layer_stats(v):
    middle = jnp.mean(v, axis=-1, keepdims=True)
    centred = v - middle
    spread = jnp.mean(centred * centred, axis=-1, keepdims=True)
    return centred, lax.rsqrt(spread + eps)


def fold_rows(v):
    return jnp.sum(v.reshape(v.shape[0] // 8, 8, v.shape[1]), axis=0)


def slot_at(slot_ref, block):
    lanes = slot_ref.shape[1]
    if isinstance(block, int):
        return slot_ref[block // lanes, block % lanes]
    return slot_ref[lax.div(block, lanes), lax.rem(block, lanes)]


def fetch_block(gath, slot, dst, row, col, sem, side):
    return pltpu.make_async_copy(
        gath.at[slot], dst.at[pl.ds(row, side), pl.ds(col, side)], sem
    )


def prepare(x_ref, block_ref, vin_ref, h1_ref, slot_ref, vec_ref):
    rows, width = x_ref.shape
    per = width // 128
    for r in range(vec_ref.shape[0]):
        for c in range(per):
            vec_ref[r:r + 1, c * 128:(c + 1) * 128] = vin_ref[per * r + c:per * r + c + 1, :]
    chunk = 128

    @pl.loop(0, rows // chunk)
    def _(r):
        at = pl.ds(pl.multiple_of(r * chunk, chunk), chunk)
        centred, inv = layer_stats(x_ref[at, :].astype(F32))
        h1_ref[at, :] = (
            centred * inv * vec_ref[GAIN1:GAIN1 + 1, :] + vec_ref[SHIFT1:SHIFT1 + 1, :]
        ).astype(BF16)

    tiles, lanes = slot_ref.shape
    line = lax.broadcasted_iota(jnp.int32, (8, lanes), 0)
    lane = lax.broadcasted_iota(jnp.int32, (8, lanes), 1).astype(F32)
    block = lax.broadcasted_iota(jnp.int32, (lanes, lanes), 0)
    for t in range(tiles):
        found = jnp.zeros((8, lanes), F32)
        for r in range(tiles):
            held = (block_ref[r:r + 1, :] == block + t * lanes).astype(F32).astype(BF16)
            found = found + dot_nt(jnp.where(line == 0, lane, float(r)).astype(BF16), held)
        slot_ref[t:t + 1, :] = (found[0:1] + float(lanes) * found[1:2]).astype(jnp.int32)


def prepared_shapes(x, blocks, vin):
    rows, width = x.shape
    return (
        sds((rows, width), BF16),
        sds(blocks.shape, jnp.int32),
        sds((vin.size // width, width), F32),
    )


def run_prepare(x, blocks, vin):
    return pl.pallas_call(
        prepare,
        out_shape=prepared_shapes(x, blocks, vin),
        in_specs=[vmem()] * 3,
        out_specs=tuple([vmem()] * 3),
        compiler_params=params(),
        name="prepare",
    )(x, blocks, vin)


def qkv_kernel(slot_ref, h1_ref, vec_ref, gath, out, wq_out, out_ref, wbuf, sems, sem_w, sem_o, *, nd):
    rows, width = h1_ref.shape
    side = gath.shape[1]
    per = width // side
    lanes = out_ref.shape[3]
    for part in range(3):
        for i in range(per):
            for j in range(per):
                slot = slot_at(slot_ref, i * 3 * per + part * per + j)
                fetch_block(gath, slot, wbuf.at[part], i * side, j * side, sems.at[part], side).start()

    def leave(part):
        return pltpu.make_async_copy(out_ref.at[:, part], out.at[:, part], sem_o.at[part])

    def keep(part):
        return pltpu.make_async_copy(wbuf.at[part], wq_out.at[part], sem_w.at[part])

    for part in range(3):
        pltpu.make_async_copy(wbuf.at[part], wbuf.at[part], sems.at[part]).wait()
        keep(part).start()
        for half in range(2):
            cols = slice(half * width // 2, (half + 1) * width // 2)
            res = dot_nn(h1_ref[...], wbuf[part, :, cols])
            if part == 0:
                res = res + vec_ref[BQ:BQ + 1, cols]
            if part == 2:
                res = res + vec_ref[BV:BV + 1, cols]
            res = res.astype(BF16)
            for d in range(nd // 2):
                out_ref[half * (nd // 2) + d, part, :, :] = res[:, d * lanes:(d + 1) * lanes]
        leave(part).start()
    for part in range(3):
        keep(part).wait()
        leave(part).wait()


def run_qkv(slot_of, h1, vec, gath, nd):
    rows, width = h1.shape
    lanes = width // nd
    return pl.pallas_call(
        functools.partial(qkv_kernel, nd=nd),
        out_shape=(sds((nd, 3, rows, lanes), BF16), sds((3, width, width), BF16)),
        in_specs=[smem(), vmem(), vmem(), hbm()],
        out_specs=(hbm(), hbm()),
        scratch_shapes=[
            pltpu.VMEM((nd, 3, rows, lanes), BF16),
            pltpu.VMEM((3, width, width), BF16),
            pltpu.SemaphoreType.DMA((3,)),
            pltpu.SemaphoreType.DMA((3,)),
            pltpu.SemaphoreType.DMA((3,)),
        ],
        compiler_params=params(),
        name="qkv",
    )(slot_of, h1, vec, gath)


MESH = pl.DeviceIdType.MESH


def remote(src, dst, send, recv, device):
    return pltpu.make_async_remote_copy(
        src_ref=src, dst_ref=dst, send_sem=send, recv_sem=recv, device_id=device, device_id_type=MESH
    )


def arrived(ref, sem):
    pltpu.make_async_copy(ref, ref, sem).wait()


def cut(ref, first, size):
    return ref.at[pl.ds(first, size)]


def greet_plane(g, d, nd):
    barrier = pltpu.get_barrier_semaphore()
    for p in range(1, nd):
        pl.semaphore_signal(barrier, inc=1, device_id=(g, lax.rem(d + p, nd)), device_id_type=MESH)
    pl.semaphore_wait(barrier, nd - 1)


def landing(ref, part, source, q, tok, lanes, parts):
    if lanes % 128 == 0:
        first = (part * (ref.shape[1] // parts)) + source * lanes
        return ref.at[pl.ds(q * tok, tok), pl.ds(pl.multiple_of(first, lanes), lanes)]
    return ref.at[source, part, q]


def landing_shape(parts, nb, seqs, tok, lanes):
    if lanes % 128 == 0:
        return sds((seqs * tok, parts * nb * lanes), BF16)
    return sds((nb, parts, seqs, tok, lanes), BF16)


def side_by_side(got, parts, rows):
    if got.ndim == 2:
        return got
    nb, _, seqs, tok, lanes = got.shape
    return got.transpose(2, 3, 1, 0, 4).reshape(rows, parts * nb * lanes)


def parts3(v):
    hi = v.astype(BF16)
    mid = (v - hi.astype(F32)).astype(BF16)
    lo = (v - hi.astype(F32) - mid.astype(F32)).astype(BF16)
    return hi.astype(F32), mid.astype(F32), lo.astype(F32)


def own_lanes(h, shape, hpd, lanes):
    lane = lax.broadcasted_iota(jnp.int32, shape, 1)
    size = lanes // hpd
    return (lane >= h * size) & (lane < (h + 1) * size)


def place(values, base, tok, width):
    lane = lax.broadcasted_iota(jnp.int32, (tok, width), 1)
    out = jnp.zeros((tok, width), F32)
    for n, v in enumerate(values):
        out = jnp.where(lane == base + n, v, out)
    return out


def spare(h, hpd, lanes):
    return (lanes // hpd) * (1 - h) if hpd > 1 else 0


def column_tables(slope_ref, qbase, kbase, kfar, hpd, lanes):
    _, tok, _ = qbase.shape
    u = lax.broadcasted_iota(jnp.int32, (tok, 128), 0).astype(F32)
    for h in range(hpd):
        slope = slope_ref[h]
        base = spare(h, hpd, lanes)
        near = parts3(jnp.full((tok, 128), slope, F32))
        far = parts3(jnp.full((tok, 128), slope * tok, F32))
        qbase[h] = place(near + far, base, tok, 128)
        kbase[h] = place([u] * 3 + [0.0] * 3 + [1.0] * 3, base, tok, 128)
        kfar[h] = place([0.0] * 3 + [1.0] * 3, base, tok, 128)


def extra_lanes(columns, extra, h, hpd, lanes):
    lane = lax.broadcasted_iota(jnp.int32, columns.shape, 1)
    for n, v in enumerate(extra):
        columns = jnp.where(lane == spare(h, hpd, lanes) + 6 + n, v, columns)
    return columns


def with_columns(v, h, hpd, columns):
    tok, lanes = v.shape
    if hpd > 1:
        return jnp.where(own_lanes(h, (tok, lanes), hpd, lanes), v, columns).astype(BF16)
    return jnp.concatenate([v, columns[:, 0:128 - lanes]], axis=1).astype(BF16)


def q_columns(q, h, hpd, columns, extra):
    lanes = q.shape[1]
    if extra:
        columns = extra_lanes(columns, extra, h, hpd, lanes)
    return with_columns(q.astype(F32) * ((lanes // hpd) ** (-0.5)), h, hpd, columns)


def k_columns(k, h, hpd, columns):
    return with_columns(k.astype(F32), h, hpd, columns)


def far_side(slope, tok):
    u = lax.broadcasted_iota(jnp.int32, (tok, tok), 0)
    t = lax.broadcasted_iota(jnp.int32, (tok, tok), 1)
    after = u > t
    return (
        jnp.where(after, big_negative, 0.0),
        jnp.where(after, (2.0 * slope) * (t - u).astype(F32), 0.0),
    )


def pair_tables(corr, h, mask, span):
    tok = mask.shape[0]
    for n, (one, two) in enumerate(((mask, mask), (span, mask), (mask, span))):
        corr[h, n, 0:tok, 0:tok] = one
        corr[h, n, tok:, tok:] = two
        corr[h, n, 0:tok, tok:] = jnp.zeros((tok, tok), F32)
        corr[h, n, tok:, 0:tok] = jnp.full((tok, tok), big_negative, F32)


def attn_fwd_kernel(
    span_ref, slope_ref, src, got_out, o_got, o32_out, lse_out,
    got, o32_ref, lse_ref, sem_w, qa, ka, vt, scores, tops_ref, corr, qbase, kbase, kfar, o_out, ss, sr, os, orr, loc, *, hpd, nd
):
    nb, _, seqs, tok, lanes = got.shape
    size = lanes // hpd
    pair = 2 * tok
    g = lax.axis_index("grp")
    d = lax.axis_index("dev")

    for q in range(seqs):
        pltpu.make_async_copy(src.at[d, :, q], got.at[d, :, q], loc.at[q]).start()
    greet_plane(g, d, nd)

    def kind_of(kind):
        return pl.ds(2 * kind, 2 - kind)

    def send(q, kind, p):
        to = lax.rem(d + p, nd)
        return remote(
            src.at[to, kind_of(kind), q], got.at[d, kind_of(kind), q],
            ss.at[q, kind, p], sr.at[q, kind, p], (g, to),
        )

    def send_all(q, kind):
        @pl.loop(1, nd)
        def _(p):
            send(q, kind, p).start()

    def have(q, kind):
        @pl.loop(1, nd)
        def _(p):
            arrived(got.at[lax.rem(d + nd - p, nd), kind_of(kind), q], sr.at[q, kind, p])

    send_all(0, 0)
    send_all(0, 1)

    def o_place(source, q):
        return landing(o_got, 0, source, q, tok, lanes, 1)

    def send_o(q, i, p):
        return remote(o_out.at[i, q], o_place(d, q), os.at[q, i], orr.at[q, p], (g, i))

    column_tables(slope_ref, qbase, kbase, kfar, hpd, lanes)
    for h in range(hpd):
        mask, span = far_side(slope_ref[h], tok)
        pair_tables(corr, h, mask, span)

    def fold(v, how):
        return how(v.reshape(v.shape[0] // 8, 8, v.shape[1]), axis=0)

    def write(ref, out, n, q, third=False):
        if third:
            return pltpu.make_async_copy(ref.at[:, :, q], out.at[:, :, q], sem_w.at[n, q])
        return pltpu.make_async_copy(ref.at[:, q], out.at[:, q], sem_w.at[n, q])

    whole = scores.shape[1] > nb // 2

    def tile_at(i, n):
        return (i * (i + 1)) // 2 + n if whole else n

    @pl.loop(0, seqs)
    def _(q):
        pltpu.make_async_copy(src.at[d, :, q], got.at[d, :, q], loc.at[q]).wait()
        start = span_ref[q]

        def score(i):
            flag = (start == i * pair).astype(jnp.int32) + 2 * (start == i * pair + tok).astype(jnp.int32)
            at_i = slice(i * pair, (i + 1) * pair)
            for h in range(hpd):
                top = None
                for n in range(i + 1):
                    s = dot_nt(ka[h, n * pair:(n + 1) * pair, :], qa[h, at_i, :])
                    if n == i:
                        s = s + corr[h, flag]
                    scores[h, tile_at(i, n)] = s
                    here = fold(s, jnp.max)
                    top = here if top is None else jnp.maximum(top, here)
                tops_ref[h, i] = jnp.broadcast_to(jnp.max(top, axis=0, keepdims=True), (8, pair))

        have(q, 0)

        @pl.when(q + 1 < seqs)
        def _():
            send_all(q + 1, 0)

        @pl.loop(0, nb)
        def _(j):
            at_j = pl.ds(pl.multiple_of(j * tok, tok), tok)
            block = jnp.full((tok, 128), j, jnp.int32).astype(F32)
            for h in range(hpd):
                qa[h, at_j, :] = q_columns(got[j, 0, q], h, hpd, qbase[h], [])
                ka[h, at_j, :] = k_columns(got[j, 1, q], h, hpd, kbase[h] + block * kfar[h])

        if whole:
            for i in range(nb // 2):
                score(i)
        have(q, 1)

        @pl.when(q + 1 < seqs)
        def _():
            send_all(q + 1, 1)

        write(got, got_out, 0, q, True).start()

        @pl.loop(0, nb)
        def _(j):
            vt[0:lanes, pl.ds(pl.multiple_of(j * tok, tok), tok)] = turn(got[j, 2, q])

        for i in range(nb // 2):
            if not whole:
                score(i)
            outs = []
            logs = []
            for h in range(hpd):
                acc = total = None
                top = tops_ref[h, i][0:1]
                for n in range(i + 1):
                    p = jnp.exp(scores[h, tile_at(i, n)] - top)
                    here = fold(p, jnp.sum)
                    part = dot_nn(vt[h * size:(h + 1) * size, n * pair:(n + 1) * pair], p.astype(BF16))
                    total = here if total is None else total + here
                    acc = part if acc is None else acc + part
                total = jnp.sum(total, axis=0, keepdims=True)
                outs.append(acc / total)
                logs.append(jnp.broadcast_to(top + jnp.log(total), (128 // hpd, pair)))
            out = (jnp.concatenate(outs, axis=0) if hpd > 1 else outs[0]).T
            log = (jnp.concatenate(logs[::-1], axis=0) if hpd > 1 else logs[0]).T
            for k in range(2):
                at = 2 * i + k
                o32_ref[at, q] = out[k * tok:(k + 1) * tok]
                o_out[at, q] = out[k * tok:(k + 1) * tok].astype(BF16)
                lse_ref[at, q] = log[k * tok:(k + 1) * tok]

                @pl.when(at == d)
                def _():
                    pltpu.make_async_copy(o_out.at[at, q], o_place(d, q), os.at[q, at]).start()

                @pl.when(at != d)
                def _():
                    send_o(q, at, lax.rem(at - d + nd, nd)).start()

        write(o32_ref, o32_out, 1, q).start()
        write(lse_ref, lse_out, 2, q).start()

    for q in range(seqs):
        @pl.loop(1, nd)
        def _(p):
            arrived(o_place(lax.rem(d + nd - p, nd), q), orr.at[q, p])
            send(q, 0, p).wait_send()
            send(q, 1, p).wait_send()

        @pl.loop(0, nd)
        def _(i):
            arrived(o_out.at[i, q], os.at[q, i])
        write(got, got_out, 0, q, True).wait()
        write(o32_ref, o32_out, 1, q).wait()
        write(lse_ref, lse_out, 2, q).wait()


def run_attn_fwd(span, slopes, qkv, hpd):
    nb, _, seqs, tok, lanes = qkv.shape
    t = nb * tok
    pairs = nb // 2
    tiles = pairs * (pairs + 1) // 2
    if hpd * tiles > 24:
        tiles = pairs
    dma = pltpu.SemaphoreType.DMA
    return pl.pallas_call(
        functools.partial(attn_fwd_kernel, hpd=hpd, nd=nb),
        out_shape=(
            sds(qkv.shape, BF16),
            landing_shape(1, nb, seqs, tok, lanes),
            sds((nb, seqs, tok, lanes), F32),
            sds((nb, seqs, tok, 128), F32),
        ),
        in_specs=[smem(), smem(), hbm()],
        out_specs=(hbm(), vmem(), hbm(), hbm()),
        scratch_shapes=[
            pltpu.VMEM(qkv.shape, BF16),
            pltpu.VMEM((nb, seqs, tok, lanes), F32),
            pltpu.VMEM((nb, seqs, tok, 128), F32),
            dma((3, seqs)),
            pltpu.VMEM((hpd, t, 128), BF16),
            pltpu.VMEM((hpd, t, 128), BF16),
            pltpu.VMEM((lanes, t), BF16),
            pltpu.VMEM((hpd, tiles, 2 * tok, 2 * tok), F32),
            pltpu.VMEM((hpd, nb // 2, 8, 2 * tok), F32),
            pltpu.VMEM((hpd, 3, 2 * tok, 2 * tok), F32),
            pltpu.VMEM((hpd, tok, 128), F32),
            pltpu.VMEM((hpd, tok, 128), F32),
            pltpu.VMEM((hpd, tok, 128), F32),
            pltpu.VMEM((nb, seqs, tok, lanes), BF16),
            dma((seqs, 2, nb)),
            dma((seqs, 2, nb)),
            dma((seqs, nb)),
            dma((seqs, nb)),
            dma((seqs,)),
        ],
        compiler_params=params(collective_id=2, has_side_effects=True),
        name="attn_fwd",
    )(span, slopes, qkv)


def attn_bwd_kernel(
    span_ref, slope_ref, qkv_in, do_src, o32_in, lse_in, got,
    qkv_ref, o32_ref, lse_ref, sem_in, do_got, out, qa, ka, kt, va, qm, da, dm, dqt, corr, qbase, kbase, kfar,
    ss, sr, gs, gr, loc, *, hpd, nd
):
    nb, _, seqs, tok, lanes = qkv_ref.shape
    inputs = [
        pltpu.make_async_copy(qkv_in, qkv_ref, sem_in.at[0]),
        pltpu.make_async_copy(lse_in, lse_ref, sem_in.at[1]),
        pltpu.make_async_copy(o32_in, o32_ref, sem_in.at[2]),
    ]
    for copy in inputs:
        copy.start()
    size = lanes // hpd
    unit = size ** (-0.5)
    pair = 2 * tok
    g = lax.axis_index("grp")
    d = lax.axis_index("dev")

    def own_copy(q):
        return pltpu.make_async_copy(do_src.at[d, q], do_got.at[d, q], loc.at[q])

    for q in range(seqs):
        own_copy(q).start()
    greet_plane(g, d, nd)

    def send(q, p):
        to = lax.rem(d + p, nd)
        return remote(do_src.at[to, q], do_got.at[d, q], ss.at[q, p], sr.at[q, p], (g, to))

    def send_all(q):
        @pl.loop(1, nd)
        def _(p):
            send(q, p).start()

    send_all(0)

    def place_back(kind, source, q):
        return landing(got, kind, source, q, tok, lanes, 3)

    def back(q, kind, p):
        to = lax.rem(d + p, nd)
        return remote(
            out.at[to, kind, q], place_back(kind, d, q), gs.at[q, kind, p], gr.at[q, kind, p], (g, to)
        )

    def back_own(q, kind):
        return pltpu.make_async_copy(out.at[d, kind, q], place_back(kind, d, q), gs.at[q, kind, 0])

    for h in range(hpd):
        mask, span = far_side(slope_ref[h], tok)
        pair_tables(corr, h, mask, span)
    column_tables(slope_ref, qbase, kbase, kfar, hpd, lanes)
    row = lax.broadcasted_iota(jnp.int32, (lanes, lanes), 0) // size
    col = lax.broadcasted_iota(jnp.int32, (lanes, lanes), 1) // size
    across = (row == hpd - 1 - col).astype(F32).astype(BF16)
    for copy in inputs:
        copy.wait()

    @pl.loop(0, seqs)
    def _(q):
        @pl.loop(0, nb)
        def _(j):
            at_j = pl.ds(pl.multiple_of(j * tok, tok), tok)
            qj = qkv_ref[j, 0, q]
            kj = qkv_ref[j, 1, q]
            vj = qkv_ref[j, 2, q].astype(F32)
            kt[:, at_j] = kj.astype(F32).T.astype(BF16)
            dqt[:, at_j] = jnp.zeros((lanes, tok), F32)
            block = jnp.full((tok, 128), j, jnp.int32).astype(F32)
            low = [-p for p in parts3(lse_ref[j, q])]
            for h in range(hpd):
                qa[h, at_j, :] = q_columns(qj, h, hpd, qbase[h], low)
                ka[h, at_j, :] = k_columns(kj, h, hpd, kbase[h] + block * kfar[h])
                if hpd > 1:
                    own = own_lanes(h, (tok, lanes), hpd, lanes)
                    qm[h, at_j, :] = jnp.where(own, qj.astype(F32), 0.0).astype(BF16)
                    va[h, at_j, :] = jnp.where(own, vj, kbase[h]).astype(BF16)
                else:
                    qm[h, at_j, :] = qj
                    va[h, at_j, :] = jnp.concatenate([vj, kbase[h][:, 0:lanes]], axis=1).astype(BF16)

        own_copy(q).wait()

        @pl.loop(1, nd)
        def _(p):
            arrived(do_got.at[lax.rem(d + nd - p, nd), q], sr.at[q, p])

        @pl.when(q + 1 < seqs)
        def _():
            send_all(q + 1)

        @pl.loop(0, nb)
        def _(j):
            at_j = pl.ds(pl.multiple_of(j * tok, tok), tok)
            do = do_got[j, q].astype(F32)
            delta = jnp.zeros((tok, lanes), F32)
            for p in parts3(do * o32_ref[j, q]):
                delta = delta + dot_nn(p.astype(BF16), across)
            low = [-p for p in parts3(delta)]
            for h in range(hpd):
                if hpd > 1:
                    own = own_lanes(h, (tok, lanes), hpd, lanes)
                    none = jnp.where(own, do, 0.0)
                    da[h, at_j, :] = extra_lanes(none, low, h, hpd, lanes).astype(BF16)
                    dm[h, at_j, :] = none.astype(BF16)
                else:
                    extra = extra_lanes(jnp.zeros((tok, lanes), F32), low, h, hpd, lanes)
                    da[h, at_j, :] = jnp.concatenate([do, extra], axis=1).astype(BF16)
                    dm[h, at_j, :] = do.astype(BF16)

        start = span_ref[q]

        pairs = nb // 2

        def tile(j, i):
            at_j = slice(j * pair, (j + 1) * pair)
            at_i = slice(i * pair, (i + 1) * pair)
            flag = (start == j * pair).astype(jnp.int32) + 2 * (start == j * pair + tok).astype(jnp.int32)
            dk = dv = None
            for h in range(hpd):
                s = dot_nt(ka[h, at_j, :], qa[h, at_i, :])
                if i == j:
                    s = s + corr[h, flag]
                p = jnp.exp(s)
                ds = (p * dot_nt(va[h, at_j, :], da[h, at_i, :])).astype(BF16)
                dv_h = dot_nn(p.astype(BF16), dm[h, at_i, :])
                dk_h = dot_nn(ds, qm[h, at_i, :])
                dk = dk_h if dk is None else dk + dk_h
                dv = dv_h if dv is None else dv + dv_h
                rows = slice(h * size, (h + 1) * size)
                dqt[rows, at_i] += dot_nn(kt[rows, at_j], ds)
            return dk, dv

        @pl.loop(0, pairs)
        def _(n):
            turn_of = lax.rem(d // 2 + n, pairs)
            for case in range(pairs):
                @pl.when(turn_of == case)
                def _():
                    dk, dv = tile(case, case)
                    for i in range(case + 1, pairs):
                        more = tile(case, i)
                        dk = dk + more[0]
                        dv = dv + more[1]
                    for k in range(2):
                        half = slice(k * tok, (k + 1) * tok)
                        out[2 * case + k, 1, q] = (dk[half] * unit).astype(BF16)
                        out[2 * case + k, 2, q] = dv[half].astype(BF16)

            for k in range(2):
                j = 2 * turn_of + k
                for kind in (1, 2):
                    @pl.when(j == d)
                    def _():
                        back_own(q, kind).start()

                    @pl.when(j != d)
                    def _():
                        back(q, kind, lax.rem(j - d + nd, nd)).start()

        @pl.loop(0, nb)
        def _(n):
            j = lax.rem(d + n, nb)
            at_j = pl.ds(pl.multiple_of(j * tok, tok), tok)
            out[j, 0, q] = (dqt[:, at_j].T * unit).astype(BF16)

            @pl.when(n == 0)
            def _():
                back_own(q, 0).start()

            @pl.when(n > 0)
            def _():
                back(q, 0, n).start()

    for q in range(seqs):
        for kind in range(3):
            back_own(q, kind).wait()

        @pl.loop(1, nd)
        def _(p):
            send(q, p).wait_send()
            source = lax.rem(d + nd - p, nd)
            for kind in range(3):
                back(q, kind, p).wait_send()
                arrived(place_back(kind, source, q), gr.at[q, kind, p])


def run_attn_bwd(span, slopes, qkv, do, o32, lse, hpd):
    nb, _, seqs, tok, lanes = qkv.shape
    t = nb * tok
    dma = pltpu.SemaphoreType.DMA
    wide = 128 if hpd == 1 else lanes
    return pl.pallas_call(
        functools.partial(attn_bwd_kernel, hpd=hpd, nd=nb),
        out_shape=landing_shape(3, nb, seqs, tok, lanes),
        in_specs=[smem(), smem(), hbm(), hbm(), hbm(), hbm()],
        out_specs=vmem(),
        scratch_shapes=[
            pltpu.VMEM(qkv.shape, BF16),
            pltpu.VMEM(o32.shape, F32),
            pltpu.VMEM(lse.shape, F32),
            dma((3,)),
            pltpu.VMEM((nb, seqs, tok, lanes), BF16),
            pltpu.VMEM(qkv.shape, BF16),
            pltpu.VMEM((hpd, t, 128), BF16),
            pltpu.VMEM((hpd, t, 128), BF16),
            pltpu.VMEM((lanes, t), BF16),
            pltpu.VMEM((hpd, t, wide), BF16),
            pltpu.VMEM((hpd, t, lanes), BF16),
            pltpu.VMEM((hpd, t, wide), BF16),
            pltpu.VMEM((hpd, t, lanes), BF16),
            pltpu.VMEM((lanes, t), F32),
            pltpu.VMEM((hpd, 3, 2 * tok, 2 * tok), F32),
            pltpu.VMEM((hpd, tok, 128), F32),
            pltpu.VMEM((hpd, tok, 128), F32),
            pltpu.VMEM((hpd, tok, 128), F32),
            dma((seqs, nb)),
            dma((seqs, nb)),
            dma((seqs, 3, nb)),
            dma((seqs, 3, nb)),
            dma((seqs,)),
        ],
        compiler_params=params(collective_id=3, has_side_effects=True),
        name="attn_bwd",
    )(span, slopes, qkv, do, o32, lse)


def mlp_kernel(
    slot_ref, att_in, x_in, dy_in, vec_ref, gath,
    act_out, dx1_out, do_out, sums_ref, grads,
    att_ref, x_ref, dy_ref, sem_in, wo, wup, wdn, x1, acc, dh2, h2_ref, h2t, attt, gt, act_ref, z_ref, dg_ref, g_ref, dz_ref, do_ref, stage,
    sem_o, sem_t, sem_g, sem_w, *, nd, first_o, first_up, first_dn, tile
):
    rows, width = x_ref.shape
    side = gath.shape[1]
    per = width // side
    ff = sums_ref.shape[0] // 8 * width - 4 * width
    tiles = ff // tile
    cols = tile // side
    lanes = do_ref.shape[2]
    fper = ff // side
    inputs = [
        pltpu.make_async_copy(att_in, att_ref, sem_in.at[0]),
        pltpu.make_async_copy(x_in, x_ref, sem_in.at[1]),
        pltpu.make_async_copy(dy_in, dy_ref, sem_in.at[2]),
    ]
    for copy in inputs:
        copy.start()

    for i in range(per):
        for j in range(per):
            fetch_block(gath, slot_at(slot_ref, first_o + i * per + j), wo, i * side, j * side, sem_o.at[0], side).start()

    ring = wup.shape[0]

    def fetch_tile(f):
        at = f % ring
        for i in range(per):
            for j in range(cols):
                fetch_block(gath, slot_at(slot_ref, first_up + i * fper + f * cols + j), wup.at[at], i * side, j * side, sem_t.at[at], side).start()
            for j in range(cols):
                fetch_block(gath, slot_at(slot_ref, first_dn + (f * cols + j) * per + i), wdn.at[at], j * side, i * side, sem_t.at[at], side).start()

    for f in range(min(ring, tiles)):
        fetch_tile(f)
    for copy in inputs:
        copy.wait()
    for r in range(width // 256):
        attt[r * 256:(r + 1) * 256, :] = turn(att_ref[:, r * 256:(r + 1) * 256])
    pltpu.make_async_copy(wo, wo, sem_o.at[0]).wait()
    for half in range(2):
        c = slice(half * width // 2, (half + 1) * width // 2)
        x1[:, c] = x_ref[:, c].astype(F32) + dot_nn(att_ref[...], wo[:, c]) + vec_ref[BO:BO + 1, c]

    chunk = 128

    def rows_at(r):
        return pl.ds(pl.multiple_of(r * chunk, chunk), chunk)

    @pl.loop(0, rows // chunk)
    def _(r):
        at = rows_at(r)
        centred, inv = layer_stats(x1[at, :])
        h2_ref[at, :] = (centred * inv * vec_ref[GAIN2:GAIN2 + 1, :] + vec_ref[SHIFT2:SHIFT2 + 1, :]).astype(BF16)
        acc[at, :] = x1[at, :] + vec_ref[BDOWN:BDOWN + 1, :]
        dh2[at, :] = jnp.zeros((chunk, width), F32)

    for r in range(width // 256):
        h2t[r * 256:(r + 1) * 256, :] = turn(h2_ref[:, r * 256:(r + 1) * 256])

    def put(slot, first, res, down, across, stride):
        for i in range(down):
            for j in range(across):
                stage[slot, first + i * stride + j] = res[i * side:(i + 1) * side, j * side:(j + 1) * side]

    def leave(slot, n, block):
        pltpu.make_async_copy(stage.at[slot, n], grads.at[slot_at(slot_ref, block)], sem_g.at[slot]).start()

    def left(slot, size):
        at = stage.at[slot, pl.ds(0, size)]
        pltpu.make_async_copy(at, at, sem_g.at[slot]).wait()

    full = 2 * per * cols
    piece = 512
    per_piece = piece // side
    strip = 16

    def pieces(size):
        return [slice(k * piece, (k + 1) * piece) for k in range(size // piece)]

    def into_tile(f):
        at = f % ring
        arrived(wup.at[at], sem_t.at[at])
        arrived(wdn.at[at], sem_t.at[at])
        for c in pieces(tile):
            z_ref[:, c] = dot_nn(h2_ref[...], wup[at, :, c])
            dg_ref[:, c] = dot_nt(dy_ref[...], wdn[at, c, :])

    def gelu_strips(f, first, last):
        total = None
        for r in range(first, last, strip):
            at = slice(r, r + strip)
            z = z_ref[at, :] + vec_ref[BUP + f:BUP + f + 1, :]
            z2 = z * z
            th = jnp.tanh(z * (0.7978845608028654 + (0.7978845608028654 * 0.044715) * z2))
            half_more = 0.5 + 0.5 * th
            g_ref[f % 2, at, :] = (z * half_more).astype(BF16)
            slope = half_more + (0.5 * z) * (1.0 - th * th) * (
                0.7978845608028654 + (3.0 * 0.044715 * 0.7978845608028654) * z2
            )
            dz = (dg_ref[at, :] * slope).astype(BF16)
            dz_ref[f % 2, at, :] = dz
            here = fold_rows(dz.astype(F32))
            total = here if total is None else total + here
        at = slice(8 * (4 + f), 8 * (4 + f) + 8)
        if first == 0:
            sums_ref[at, :] = total
        else:
            sums_ref[at, :] += total

    def out_of_tile(f):
        at = f % ring
        slot = f % 2

        def up(c):
            acc[:, c] += dot_nn(g_ref[slot], wdn[at, :, c])
            dh2[:, c] += dot_nt(dz_ref[slot], wup[at, c, :])

        def turn_g(c):
            gt[c, :] = turn(g_ref[slot, :, c])

        def grad_down(k, c):
            put(slot, k * per_piece, dot_nn(gt[...], dy_ref[:, c]).astype(BF16), cols, per_piece, per)

        def grad_up(k, c):
            first = per * cols + k * per_piece
            put(slot, first, dot_nn(h2t[...], dz_ref[slot, :, c]).astype(BF16), per, per_piece, cols)

        steps = [functools.partial(up, c) for c in pieces(width)]
        steps += [functools.partial(grad_up, k, c) for k, c in enumerate(pieces(tile))]
        steps += [functools.partial(turn_g, c) for c in pieces(tile)]
        steps += [functools.partial(grad_down, k, c) for k, c in enumerate(pieces(width))]
        return steps

    def send_tile(f):
        slot = f % 2
        for i in range(per):
            for j in range(cols):
                leave(slot, j * per + i, first_dn + (f * cols + j) * per + i)
            for j in range(cols):
                leave(slot, per * cols + i * cols + j, first_up + i * fper + f * cols + j)

    for f in range(tiles + 1):
        if f < tiles:
            into_tile(f)
        steps = out_of_tile(f - 1) if f > 0 else []
        if f > 2:
            left((f - 1) % 2, full)
        share = rows // max(len(steps), 1)
        if f < tiles:
            for n in range(max(len(steps), 1)):
                gelu_strips(f, n * share // strip * strip, rows if n + 1 >= len(steps) else (n + 1) * share // strip * strip)
                if steps:
                    steps[n]()
        else:
            for step in steps:
                step()
        if f > 0:
            send_tile(f - 1)
            if f - 1 + ring < tiles:
                fetch_tile(f - 1 + ring)

    zero = jnp.zeros((8, width), F32)
    da_ref = h2_ref
    dx1_ref = x1

    def finish(r, carry):
        s_bo, s_gain, s_shift, s_bdown = carry
        at = rows_at(r)
        act_ref[at, :] = acc[at, :].astype(BF16)
        centred, inv = layer_stats(x1[at, :])
        hat = centred * inv
        dh = dh2[at, :]
        dhg = dh * vec_ref[GAIN2:GAIN2 + 1, :]
        back = inv * (
            dhg
            - jnp.mean(dhg, axis=-1, keepdims=True)
            - hat * jnp.mean(dhg * hat, axis=-1, keepdims=True)
        )
        dy = dy_ref[at, :].astype(F32)
        dx1 = dy + back
        dx1_ref[at, :] = dx1
        da = dx1.astype(BF16)
        da_ref[at, :] = da
        return (
            s_bo + fold_rows(da.astype(F32)),
            s_gain + fold_rows(dh * hat),
            s_shift + fold_rows(dh),
            s_bdown + fold_rows(dy),
        )

    carry = lax.fori_loop(0, rows // chunk, finish, (zero, zero, zero, zero))
    for n in range(4):
        sums_ref[8 * n:8 * n + 8, :] = carry[n]
    outs = [
        pltpu.make_async_copy(act_ref, act_out, sem_w.at[0]),
        pltpu.make_async_copy(dx1_ref, dx1_out, sem_w.at[1]),
        pltpu.make_async_copy(do_ref, do_out, sem_w.at[2]),
    ]
    outs[0].start()
    outs[1].start()
    for half in range(2):
        c = slice(half * width // 2, (half + 1) * width // 2)
        res = dot_nt(da_ref[...], wo[c, :]).astype(BF16)
        for d in range(nd // 2):
            do_ref[half * (nd // 2) + d] = res[:, d * lanes:(d + 1) * lanes]
    outs[2].start()
    left(0, full)
    left(1, full)
    half_rows = width // 2
    for half in range(2):
        res = dot_nn(attt[half * half_rows:(half + 1) * half_rows, :], da_ref[...]).astype(BF16)
        put(half, 0, res, per // 2, per, per)

        for i in range(per // 2):
            for j in range(per):
                leave(half, i * per + j, first_o + (half * (per // 2) + i) * per + j)
    for half in range(2):
        left(half, per * per // 2)
    for copy in outs:
        copy.wait()


def run_mlp(slot_of, att, x, dy, vec, gath, nd):
    rows, width = x.shape
    side = gath.shape[1]
    lanes = width // nd
    per = width // side
    first_o = 3 * per * per
    first_up = first_o + per * per
    first_dn = first_up + per * (FF // side)
    tile = width
    f32_rows = pltpu.VMEM((rows, width), F32)
    bf16_rows = pltpu.VMEM((rows, width), BF16)
    turned = pltpu.VMEM((width, rows), BF16)
    return pl.pallas_call(
        functools.partial(
            mlp_kernel, nd=nd, first_o=first_o, first_up=first_up, first_dn=first_dn, tile=tile
        ),
        out_shape=(
            sds((rows, width), BF16),
            sds((rows, width), F32),
            sds((nd, rows, lanes), BF16),
            sds((8 * (4 + FF // width), width), F32),
            sds(gath.shape, BF16),
        ),
        in_specs=[smem(), hbm(), hbm(), hbm(), vmem(), hbm()],
        out_specs=(hbm(), hbm(), hbm(), vmem(), hbm()),
        scratch_shapes=[
            bf16_rows,
            bf16_rows,
            bf16_rows,
            pltpu.SemaphoreType.DMA((3,)),
            pltpu.VMEM((width, width), BF16),
            pltpu.VMEM((3, width, tile), BF16),
            pltpu.VMEM((3, tile, width), BF16),
            f32_rows,
            f32_rows,
            f32_rows,
            bf16_rows,
            turned,
            turned,
            pltpu.VMEM((tile, rows), BF16),
            bf16_rows,
            pltpu.VMEM((rows, tile), F32),
            pltpu.VMEM((rows, tile), F32),
            pltpu.VMEM((2, rows, tile), BF16),
            pltpu.VMEM((2, rows, tile), BF16),
            pltpu.VMEM((nd, rows, lanes), BF16),
            pltpu.VMEM((2, 2 * per * (tile // side), side, side), BF16),
            pltpu.SemaphoreType.DMA((1,)),
            pltpu.SemaphoreType.DMA((FF // tile,)),
            pltpu.SemaphoreType.DMA((2,)),
            pltpu.SemaphoreType.DMA((3,)),
        ],
        compiler_params=params(),
        name="mlp",
    )(slot_of, att, x, dy, vec, gath)


def dh1_dot(cat, w, dh1, part, half):
    width = dh1.shape[1]
    c = slice(half * width // 2, (half + 1) * width // 2)
    res = dot_nt(cat[:, part * width:(part + 1) * width], w[part, c, :])
    if part == 0:
        dh1[:, c] = res
    else:
        dh1[:, c] += res


def first_norm_back(cat, x, dh1, dx1, ig, vec_ref):
    rows, width = x.shape
    chunk = 128
    zero = jnp.zeros((8, width), F32)

    def finish(r, carry):
        s_gain, s_shift, s_bq, s_bv = carry
        at = pl.ds(pl.multiple_of(r * chunk, chunk), chunk)
        centred, inv = layer_stats(x[at, :].astype(F32))
        hat = centred * inv
        dh = dh1[at, :]
        dhg = dh * vec_ref[GAIN1:GAIN1 + 1, :]
        back = inv * (
            dhg
            - jnp.mean(dhg, axis=-1, keepdims=True)
            - hat * jnp.mean(dhg * hat, axis=-1, keepdims=True)
        )
        ig[at, :] = dx1[at, :] + back
        return (
            s_gain + fold_rows(dh * hat),
            s_shift + fold_rows(dh),
            s_bq + fold_rows(cat[at, 0:width].astype(F32)),
            s_bv + fold_rows(cat[at, 2 * width:3 * width].astype(F32)),
        )

    return lax.fori_loop(0, rows // chunk, finish, (zero, zero, zero, zero))


def vector_rows(first, sums2):
    rows = [jnp.sum(v, axis=0, keepdims=True) for v in first]
    rows += [jnp.sum(sums2[8 * n:8 * n + 8, :], axis=0, keepdims=True) for n in range(sums2.shape[0] // 8)]
    return rows


def dh1_kernel(cat_ref, x_ref, dx1_ref, vec_ref, wq_ref, sums2_ref, ig_ref, vsum_ref, dh1):
    for part in range(3):
        for half in range(2):
            dh1_dot(cat_ref, wq_ref, dh1, part, half)
    first = first_norm_back(cat_ref, x_ref, dh1, dx1_ref, ig_ref, vec_ref)
    for n, row in enumerate(vector_rows(first, sums2_ref)):
        vsum_ref[n:n + 1, :] = row


def run_dh1(cat, x, dx1, vec, wq, sums2):
    rows, width = x.shape
    return pl.pallas_call(
        dh1_kernel,
        out_shape=(sds((rows, width), F32), sds(vec.shape, F32)),
        in_specs=[vmem()] * 6,
        out_specs=(vmem(), vmem()),
        scratch_shapes=[pltpu.VMEM((rows, width), F32)],
        compiler_params=params(),
        name="dh1",
    )(cat, x, dx1, vec, wq, sums2)


def wgrad_kernel(slot_ref, h1_in, cat_in, rest, out, h1_ref, cat_ref, a_t, stage, sem_in, sem_out, *, side, tile):
    del rest
    rows, width = h1_ref.shape
    per = width // side
    cols = tile // side
    steps = cat_ref.shape[1] // tile
    per_part = width // tile
    first = pltpu.make_async_copy(h1_in, h1_ref, sem_in.at[0])
    first.start()

    def part(n):
        c = slice(n * width, (n + 1) * width)
        return pltpu.make_async_copy(cat_in.at[:, c], cat_ref.at[:, c], sem_in.at[1 + n])

    for n in range(steps // per_part):
        part(n).start()
    first.wait()
    for r in range(width // 256):
        c = slice(r * 256, (r + 1) * 256)
        a_t[c, :] = turn(h1_ref[:, c])

    def left(slot):
        pltpu.make_async_copy(stage.at[slot], stage.at[slot], sem_out.at[slot]).wait()

    for t in range(steps):
        slot = t % 2
        if t % per_part == 0:
            part(t // per_part).wait()
        if t >= 2:
            left(slot)
        res = dot_nn(a_t[...], cat_ref[:, t * tile:(t + 1) * tile]).astype(BF16)
        for i in range(per):
            for j in range(cols):
                stage[slot, i * cols + j] = res[i * side:(i + 1) * side, j * side:(j + 1) * side]
        for i in range(per):
            for j in range(cols):
                dst = slot_at(slot_ref, i * 3 * per + t * cols + j)
                pltpu.make_async_copy(stage.at[slot, i * cols + j], out.at[dst], sem_out.at[slot]).start()

    left(0)
    left(1)


def run_wgrad(slot_of, h1, cat, grads):
    rows, width = h1.shape
    side = grads.shape[1]
    tile = 512
    return pl.pallas_call(
        functools.partial(wgrad_kernel, side=side, tile=tile),
        out_shape=sds(grads.shape, BF16),
        in_specs=[smem(), hbm(), hbm(), hbm()],
        out_specs=hbm(),
        scratch_shapes=[
            pltpu.VMEM(h1.shape, BF16),
            pltpu.VMEM(cat.shape, BF16),
            pltpu.VMEM((width, rows), BF16),
            pltpu.VMEM((2, (width // side) * (tile // side), side, side), BF16),
            pltpu.SemaphoreType.DMA((4,)),
            pltpu.SemaphoreType.DMA((2,)),
        ],
        input_output_aliases={3: 0},
        compiler_params=params(),
        name="wgrad",
    )(slot_of, h1, cat, grads)


def whereami():
    g = lax.axis_index("grp")
    d = lax.axis_index("dev")
    core = lax.rem(d, 2)
    x = lax.rem(d // 2, 2)
    y = d // 4
    over_x = d + 2 - 4 * x
    over_y = d + 4 - 8 * y
    across = over_x + 4 - 8 * y
    sibling = d + 1 - 2 * core
    return g, d, over_x, over_y, across, sibling


def near_order(t, g, ng):
    t = ng - 1 - t
    low = jnp.where(t < ng - 1 - g, ng - 1 - t, t - (ng - 1 - g))
    high = jnp.where(t < g, t, ng - 1 - (t - g))
    return jnp.where(2 * g < ng, low, high)


def far_order(t, g, ng):
    def low(g):
        u = t - (ng - 1 - 2 * g)
        k = g - jnp.maximum(u, 0) // 2
        return jnp.where(u < 0, ng - 1 - t, jnp.where(u % 2 == 0, g - k, g + k))

    return jnp.where(2 * g < ng, low(g), ng - 1 - low(ng - 1 - g))


def greet(g, ng, peers):
    barrier = pltpu.get_barrier_semaphore()
    for peer in peers:
        pl.semaphore_signal(barrier, inc=1, device_id=(g, peer), device_id_type=MESH)

    d = lax.axis_index("dev")

    @pl.when(g > 0)
    def _():
        pl.semaphore_signal(barrier, inc=1, device_id=(g - 1, d), device_id_type=MESH)

    @pl.when(g < ng - 1)
    def _():
        pl.semaphore_signal(barrier, inc=1, device_id=(g + 1, d), device_id_type=MESH)

    ends = (g > 0).astype(jnp.int32) + (g < ng - 1).astype(jnp.int32)
    pl.semaphore_wait(barrier, len(peers) + ends)


def slot_cuts(count):
    third = 2 * (count // 12)
    first = (count - third) // 2
    return first, count - third - first, third // 2, third // 2


def gather_kernel(
    w_ref, x_ref, block_ref, vin_ref, out, h1_ref, slot_ref, vec_ref,
    own, local_sem, zs, zr, cs, cr, ss, sr, *, ng, nd
):
    count = w_ref.shape[0]
    na, nb, nc1, nc2 = slot_cuts(count)
    flat = na + nb
    nc = nc1 + nc2
    g, d, over_x, over_y, across, sibling = whereami()
    columns = (d, over_x, over_y, across)
    own[...] = w_ref[...].astype(BF16)
    greet(g, ng, (over_x, over_y, sibling))

    def region(gz, dev, first=0, size=count):
        return out.at[pl.ds((gz * nd + dev) * count + first, size)]

    def wide(t):
        return count if t == 0 else flat

    def kind(n, t):
        return (
            (d, 0, wide(t), over_x),
            (d, 0, wide(t), over_y),
            (d, 0, wide(t), sibling),
            (over_x, 0, na, over_y),
            (over_y, na, nb, over_x),
            (over_x, 0, wide(t), sibling),
            (over_y, 0, wide(t), sibling),
            (across, 0, na, sibling),
            (across, na, nb, sibling),
            (over_x, flat, nc1, over_y),
            (over_y, flat + nc1, nc2, over_x),
            (across, flat, nc1, sibling),
            (across, flat + nc1, nc2, sibling),
            (d, flat, nc, sibling),
            (over_x, flat, nc, sibling),
            (over_y, flat, nc, sibling),
            (across, flat, nc, sibling),
        )[n]

    def kinds(t):
        return range(13) if t == 0 else tuple(range(9)) + tuple(range(13, 17))

    def plane(n, t, src=None):
        gz = near_order(t, g, ng)
        dev, first, size, to = kind(n, t)
        at = region(gz, dev, first, size)
        return remote(at if src is None else src, at, ss.at[n, gz], sr.at[n, gz], (g, to))

    def landed(n, t, dev):
        gz = near_order(t, g, ng)
        _, first, size, _ = kind(n, t)
        arrived(region(gz, dev, first, size), sr.at[n, gz])

    def line(gz, up, src=None):
        at = region(gz, d, 0, flat)
        to = g + 1 if up else g - 1
        return remote(at if src is None else src, at, zs.at[gz, int(up)], zr.at[gz], (to, d))

    def corner_line(gz, c, up, src=None):
        at = region(gz, columns[c], flat, nc)
        to = g + 1 if up else g - 1
        return remote(at if src is None else src, at, cs.at[gz, c, int(up)], cr.at[gz, c], (to, d))

    def both_ways(gz, make):
        @pl.when((gz <= g) & (g < ng - 1))
        def _():
            make(True)

        @pl.when((gz >= g) & (g > 0))
        def _():
            make(False)

    mine = pltpu.make_async_copy(own, region(g, d), local_sem.at[0])
    mine.start()

    def column(t):
        gz = near_order(t, g, ng)
        if t == 0:
            both_ways(gz, lambda up: line(gz, up, cut(own, 0, flat)).start())
            for n in range(3):
                plane(n, t, own).start()
            both_ways(gz, lambda up: corner_line(gz, 0, up, cut(own, flat, nc)).start())
            return
        arrived(region(gz, d, 0, flat), zr.at[gz])
        both_ways(gz, lambda up: line(gz, up).start())
        for n in range(3):
            plane(n, t).start()

    def over_x_side(t):
        gz = near_order(t, g, ng)
        landed(0, t, over_x)
        plane(3, t).start()
        if t == 0:
            plane(9, t).start()
            both_ways(gz, lambda up: corner_line(gz, 1, up).start())
        plane(5, t).start()

    def over_y_side(t):
        gz = near_order(t, g, ng)
        landed(1, t, over_y)
        plane(4, t).start()
        if t == 0:
            plane(10, t).start()
            both_ways(gz, lambda up: corner_line(gz, 2, up).start())
        plane(6, t).start()

    def first_corner():
        landed(9, 0, across)
        landed(10, 0, across)
        both_ways(g, lambda up: corner_line(g, 3, up).start())
        plane(11, 0).start()
        plane(12, 0).start()

    def corner_x(t):
        landed(3, t, across)
        plane(7, t).start()

    def corner_y(t):
        landed(4, t, across)
        plane(8, t).start()

    def far_corner(t, c):
        gz = near_order(t, g, ng)
        arrived(region(gz, columns[c], flat, nc), cr.at[gz, c])
        both_ways(gz, lambda up: corner_line(gz, c, up).start())
        plane(13 + c, t).start()

    plan = [(t, column, (t,)) for t in range(ng)]
    plan += [(t + 1.5, side, (t,)) for t in range(ng) for side in (over_x_side, over_y_side)]
    plan += [(t + 2.61, side, (t,)) for t in range(ng) for side in (corner_x, corner_y)]
    plan += [(t + 2.2, far_corner, (t, c)) for t in range(1, ng) for c in range(4)]
    plan += [(2.6, first_corner, ())]
    plan = [(step, args) for _, step, args in sorted(plan, key=lambda e: e[0])]
    if ng == 4:
        plan = [
            (column, (0,)), (column, (1,)), (over_y_side, (0,)), (over_x_side, (0,)),
            (column, (2,)), (far_corner, (1, 1)), (over_x_side, (1,)), (over_y_side, (1,)),
            (column, (3,)), (first_corner, ()), (over_y_side, (2,)), (corner_y, (0,)),
            (far_corner, (2, 1)), (far_corner, (1, 3)), (far_corner, (1, 0)), (corner_y, (1,)),
            (over_x_side, (2,)), (far_corner, (2, 2)), (far_corner, (1, 2)), (corner_x, (1,)),
            (far_corner, (3, 3)), (corner_x, (0,)), (far_corner, (2, 3)), (far_corner, (3, 1)),
            (far_corner, (3, 0)), (over_x_side, (3,)), (over_y_side, (3,)), (far_corner, (2, 0)),
            (corner_y, (2,)), (far_corner, (3, 2)), (corner_x, (2,)), (corner_y, (3,)),
            (corner_x, (3,)),
        ]
    for n, (step, args) in enumerate(plan):
        step(*args)
        if n == 0:
            prepare(x_ref, block_ref, vin_ref, h1_ref, slot_ref, vec_ref)

    for t in range(ng):
        for n in kinds(t):
            dev, _, _, to = kind(n, t)
            if to is sibling:
                landed(n, t, dev + sibling - d)
    mine.wait()
    for t in range(ng):
        gz = near_order(t, g, ng)
        for n in kinds(t):
            plane(n, t).wait_send()
        both_ways(gz, lambda up: line(gz, up).wait_send())
        for c in range(4):
            both_ways(gz, lambda up: corner_line(gz, c, up).wait_send())


def run_gather(w, x, blocks, vin, ng, nd):
    count, side, _ = w.shape
    dma = pltpu.SemaphoreType.DMA
    return pl.pallas_call(
        functools.partial(gather_kernel, ng=ng, nd=nd),
        out_shape=(sds((ng * nd * count, side, side), BF16),) + prepared_shapes(x, blocks, vin),
        in_specs=[vmem()] * 4,
        out_specs=(hbm(), vmem(), vmem(), vmem()),
        scratch_shapes=[
            pltpu.VMEM((count, side, side), BF16),
            dma((1,)),
            dma((ng, 2)),
            dma((ng,)),
            dma((ng, 4, 2)),
            dma((ng, 4)),
            dma((17, ng)),
            dma((17, ng)),
        ],
        compiler_params=params(collective_id=0, has_side_effects=True),
        name="gather",
    )(w, x, blocks, vin)


def add_blocks(dst, src, size):
    step = next(n for n in (4, 5, 3, 2, 1) if size % n == 0)

    @pl.loop(0, size // step)
    def _(n):
        for k in range(step):
            dst[n * step + k] = dst[n * step + k] + src[n * step + k]


def scatter_kernel(
    grads, sums2_ref, vec_ref, vin_ref, cat_in, x_in, dx1_in, wq_in, out_ref, vout_ref, vnew_ref, ig_out,
    cat, x, dx1, wq, dh1, sem_in, mine, r0, r1y, r1x, r2x, r2y, rz, cz, cy, cx, cx2, cy2, vwork, vxy, vz,
    load, s0, w0, s1, w1, s2, w2, sz, wz, sc, wc, s3, w3, vs, vw, *, ng, nd, rate
):
    count = out_ref.shape[0]
    na, nb, nc1, nc2 = slot_cuts(count)
    flat = na + nb
    nc = nc1 + nc2
    g, d, over_x, over_y, across, sibling = whereami()
    columns = (d, over_x, over_y, across)

    def region(gz, dev):
        return grads.at[pl.ds((gz * nd + dev) * count, count)]

    def order(t):
        return far_order(t, g, ng)

    for t in range(ng):
        for c in range(4):
            pltpu.make_async_copy(region(order(t), columns[c]), mine.at[order(t), c], load.at[order(t), c]).start()
    greet(g, ng, (over_x, over_y, sibling))

    def to_sibling(gz, c):
        return remote(
            region(gz, columns[c] + sibling - d), r0.at[gz, c], s0.at[gz, c], w0.at[gz, c], (g, sibling)
        )

    peers = (sibling, over_x, over_y)

    def vec_copy(n):
        return remote(vwork.at[n], vxy.at[n], vs.at[n], vw.at[n], (g, peers[n]))

    for t in range(ng):
        for c in (3, 2, 1, 0):
            to_sibling(order(t), c).start()
    inputs = [
        pltpu.make_async_copy(cat_in, cat, sem_in.at[0]),
        pltpu.make_async_copy(wq_in, wq, sem_in.at[1]),
        pltpu.make_async_copy(x_in, x, sem_in.at[2]),
        pltpu.make_async_copy(dx1_in, dx1, sem_in.at[3]),
    ]
    for copy in inputs:
        copy.start()
    input_grad = pltpu.make_async_copy(dx1, ig_out, sem_in.at[4])

    def first_norm():
        for copy in inputs:
            copy.wait()
        for part in range(3):
            for half in range(2):
                dh1_dot(cat, wq, dh1, part, half)
        first = first_norm_back(cat, x, dh1, dx1, dx1, vec_ref)
        input_grad.start()
        for n, row in enumerate(vector_rows(first, sums2_ref)):
            vwork[0, n:n + 1, :] = row
        vec_copy(0).start()

    first = (
        (2, 0, na, r1y, 0, over_y),
        (3, 0, na, r1y, 1, over_y),
        (1, na, nb, r1x, 0, over_x),
        (3, na, nb, r1x, 1, over_x),
    )
    second = ((1, 0, na, r2x, over_x), (2, na, nb, r2y, over_y))
    third = (
        (2, flat, nc1, cy.at[0], over_y),
        (3, flat, nc1, cy.at[1], over_y),
        (1, flat + nc1, nc2, cx.at[0], over_x),
        (3, flat + nc1, nc2, cx.at[1], over_x),
        (1, flat, nc1, cx2, over_x),
        (2, flat + nc1, nc2, cy2, over_y),
    )

    def copy1(n, gz):
        c, at, size, buf, place_at, to = first[n]
        return remote(cut(mine.at[gz, c], at, size), buf.at[gz, place_at], s1.at[n, gz], w1.at[n, gz], (g, to))

    def copy2(n, gz):
        c, at, size, buf, to = second[n]
        return remote(cut(mine.at[gz, c], at, size), buf.at[gz], s2.at[n, gz], w2.at[n, gz], (g, to))

    def copy3(n):
        c, at, size, buf, to = third[n]
        return remote(cut(mine.at[g, c], at, size), buf, s3.at[n], w3.at[n], (g, to))

    def flat_part(gz):
        return cut(mine.at[gz, 0], 0, flat)

    def corner_part(gz):
        return mine.at[gz, :, pl.ds(flat, nc)]

    def line(gz, part, buf, sends, waits, up):
        at = gz if up else jnp.where(gz < g - 1, gz, ng)
        to = g + 1 if up else g - 1
        return remote(part(gz), buf.at[at], sends.at[gz], waits.at[at], (to, d))

    def pass_on(gz, part, buf, sends, waits, gather):
        @pl.when(gz > g)
        def _():
            @pl.when(g > 0)
            def _():
                arrived(buf.at[gz], waits.at[gz])
                gather(gz)
            line(gz, part, buf, sends, waits, True).start()

        @pl.when(gz < g)
        def _():
            @pl.when(g < ng - 1)
            def _():
                arrived(buf.at[gz], waits.at[gz])
                gather(gz)
            line(gz, part, buf, sends, waits, False).start()

    def gather_flat(gz):
        add_blocks(flat_part(gz), rz.at[gz], flat)

    def gather_corner(at, gz):
        for c in range(4):
            add_blocks(cut(mine.at[gz, c], flat, nc), cz.at[at, c], nc)

    def sums0(t, c):
        gz = order(t)
        pltpu.make_async_copy(region(gz, columns[c]), mine.at[gz, c], load.at[gz, c]).wait()
        arrived(r0.at[gz, c], w0.at[gz, c])
        add_blocks(mine.at[gz, c], r0.at[gz, c], count)
        for n in {3: (1, 3), 2: (0,), 1: (2,), 0: ()}[c]:
            copy1(n, gz).start()

    def along0(t):
        pass_on(order(t), corner_part, cz, sc, wc, lambda gz: gather_corner(gz, gz))

    def stage1(t, k):
        gz = order(t)
        c, at, size, buf, n = (
            (1, 0, na, r1y.at[gz, 1], 1),
            (2, na, nb, r1x.at[gz, 1], 3),
            (0, 0, na, r1y.at[gz, 0], 0),
            (0, na, nb, r1x.at[gz, 0], 2),
        )[k]
        arrived(buf, w1.at[n, gz])
        add_blocks(cut(mine.at[gz, c], at, size), buf, size)
        if k < 2:
            copy2(k, gz).start()

    def stage2(t, k):
        gz = order(t)
        at, size, buf = ((0, na, r2x.at[gz]), (na, nb, r2y.at[gz]))[k]
        arrived(buf, w2.at[k, gz])
        add_blocks(cut(mine.at[gz, 0], at, size), buf, size)

    def along1(t):
        pass_on(order(t), flat_part, rz, sz, wz, gather_flat)

    def corner0():
        @pl.when(g > 0)
        def _():
            arrived(cz.at[g], wc.at[g])
            gather_corner(g, g)

        @pl.when(g < ng - 1)
        def _():
            arrived(cz.at[ng], wc.at[ng])
            gather_corner(ng, g)
        for n in range(4):
            copy3(n).start()

    def corner1():
        arrived(cy.at[1], w3.at[1])
        add_blocks(cut(mine.at[g, 1], flat, nc1), cy.at[1], nc1)
        copy3(4).start()
        arrived(cx.at[1], w3.at[3])
        add_blocks(cut(mine.at[g, 2], flat + nc1, nc2), cx.at[1], nc2)
        copy3(5).start()
        arrived(cy.at[0], w3.at[0])
        add_blocks(cut(mine.at[g, 0], flat, nc1), cy.at[0], nc1)
        arrived(cx.at[0], w3.at[2])
        add_blocks(cut(mine.at[g, 0], flat + nc1, nc2), cx.at[0], nc2)

    def corner2():
        arrived(cx2, w3.at[4])
        add_blocks(cut(mine.at[g, 0], flat, nc1), cx2, nc1)
        arrived(cy2, w3.at[5])
        add_blocks(cut(mine.at[g, 0], flat + nc1, nc2), cy2, nc2)

    def vec_step(n):
        arrived(vxy.at[n], vw.at[n])
        total = vwork[n] + vxy[n]
        if n < 2:
            vwork[n + 1] = total
            vec_copy(n + 1).start()
        else:
            vz[g] = total

    def vec_line(gz, up):
        to = g + 1 if up else g - 1
        return remote(vz.at[gz], vz.at[gz], vs.at[3 + 2 * gz + int(up)], vw.at[3 + gz], (to, d))

    def vec_first_line():
        vec_step(2)

        @pl.when(g < ng - 1)
        def _():
            vec_line(g, True).start()

        @pl.when(g > 0)
        def _():
            vec_line(g, False).start()

    def vec_next_line(n):
        gz = near_order(n, g, ng)
        arrived(vz.at[gz], vw.at[3 + gz])

        @pl.when((gz < g) & (g < ng - 1))
        def _():
            vec_line(gz, True).start()

        @pl.when((gz > g) & (g > 0))
        def _():
            vec_line(gz, False).start()

    def vec_out():
        total = vz[0]
        for z in range(1, ng):
            total = total + vz[z]
        vwork[3] = total
        per = total.shape[1] // 128
        for r in range(total.shape[0]):
            for c in range(per):
                row = vwork[3, r:r + 1, c * 128:(c + 1) * 128]
                n = per * r + c
                vout_ref[n:n + 1, :] = row
                vnew_ref[n:n + 1, :] = vin_ref[n:n + 1, :] - rate * row

    last = ng - 1
    plan = [(t + 0.25 * (3 - c), sums0, (t, c)) for t in range(ng) for c in range(4)]
    plan += [(t + 1.2 + 0.3 * (k // 2), stage1, (t, k)) for t in range(ng) for k in range(4)]
    plan += [(t + 2.2, stage2, (t, k)) for t in range(ng) for k in range(2)]
    plan += [(t + 1.15, along0, (t,)) for t in range(last)]
    plan += [(t + 2.21, along1, (t,)) for t in range(last)]
    plan += [(last + 1.3, corner0, ()), (last + 2.19, corner1, ()), (last + 2.4, corner2, ())]
    plan += [(0.3, first_norm, ()), (0.9, vec_step, (0,)), (2.0, vec_step, (1,)), (3.0, vec_first_line, ())]
    plan += [(3.1 + 0.55 * n, vec_next_line, (n,)) for n in range(1, ng)]
    plan += [(last + 2.17, vec_out, ())]
    plan = [(step, args) for _, step, args in sorted(plan, key=lambda e: e[0])]
    if ng == 4:
        plan = [
            (sums0, (0, 3)), (sums0, (0, 2)), (first_norm, ()), (sums0, (0, 1)),
            (sums0, (0, 0)), (stage1, (0, 1)), (sums0, (1, 3)), (vec_step, (0,)),
            (along0, (0,)), (stage1, (0, 0)), (sums0, (1, 2)), (sums0, (1, 0)),
            (sums0, (1, 1)), (along0, (1,)), (stage1, (1, 1)), (stage1, (0, 3)),
            (vec_step, (1,)), (sums0, (2, 3)), (stage2, (0, 0)), (stage1, (1, 0)),
            (stage1, (0, 2)), (stage2, (0, 1)), (sums0, (2, 1)), (along1, (0,)),
            (sums0, (2, 2)), (sums0, (2, 0)), (along0, (2,)), (stage1, (1, 2)), (vec_first_line, ()),
            (sums0, (3, 3)), (stage2, (1, 0)), (sums0, (3, 0)),
            (stage1, (2, 1)), (sums0, (3, 2)), (stage1, (2, 0)),
            (stage1, (1, 3)), (stage2, (1, 1)), (stage1, (2, 2)), (vec_next_line, (1,)), (sums0, (3, 1)),
            (along1, (1,)), (stage2, (2, 0)), (stage2, (2, 1)), (stage1, (2, 3)),
            (stage1, (3, 1)), (along1, (2,)), (corner0, ()), (vec_next_line, (2,)),
            (stage1, (3, 0)), (stage2, (3, 1)), (stage1, (3, 2)), (stage1, (3, 3)),
            (vec_next_line, (3,)), (corner1, ()), (vec_out, ()), (corner2, ()),
            (stage2, (3, 0)),
        ]
    for step, args in plan:
        step(*args)

    @pl.when(g > 0)
    def _():
        arrived(rz.at[g], wz.at[g])

    @pl.when(g < ng - 1)
    def _():
        arrived(rz.at[ng], wz.at[ng])

    @pl.when((g > 0) & (g < ng - 1))
    def _():
        @pl.loop(0, flat)
        def _(i):
            out_ref[i] = mine[g, 0, i].astype(F32) + rz[g, i].astype(F32) + rz[ng, i].astype(F32)

    @pl.when(g == 0)
    def _():
        @pl.loop(0, flat)
        def _(i):
            out_ref[i] = mine[g, 0, i].astype(F32) + rz[ng, i].astype(F32)

    @pl.when((g > 0) & (g == ng - 1))
    def _():
        @pl.loop(0, flat)
        def _(i):
            out_ref[i] = mine[g, 0, i].astype(F32) + rz[g, i].astype(F32)

    for i in range(flat, count):
        out_ref[i] = mine[g, 0, i].astype(F32)

    for t in range(ng):
        gz = order(t)
        for c in range(4):
            to_sibling(gz, c).wait_send()
        for n in range(4):
            copy1(n, gz).wait_send()
        for n in range(2):
            copy2(n, gz).wait_send()
        if t < ng - 1:
            arrived(flat_part(gz), sz.at[gz])
            arrived(corner_part(gz), sc.at[gz])
    input_grad.wait()
    for n in range(6):
        copy3(n).wait_send()
    for n in range(3):
        vec_copy(n).wait_send()
    for n in range(ng):
        gz = near_order(n, g, ng)

        @pl.when((gz <= g) & (g < ng - 1))
        def _():
            vec_line(gz, True).wait_send()

        @pl.when((gz >= g) & (g > 0))
        def _():
            vec_line(gz, False).wait_send()


def run_scatter(grads, sums2, vec, vin, cat, x, dx1, wq, ng, nd, rate):
    blocks, side, _ = grads.shape
    count = blocks // (ng * nd)
    na, nb, nc1, nc2 = slot_cuts(count)
    flat = na + nb
    dma = pltpu.SemaphoreType.DMA

    def buf(*lead):
        return pltpu.VMEM(lead + (side, side), BF16)

    def like(v):
        return pltpu.VMEM(v.shape, v.dtype)

    return pl.pallas_call(
        functools.partial(scatter_kernel, ng=ng, nd=nd, rate=rate),
        out_shape=(
            sds((count, side, side), F32),
            sds(vin.shape, F32),
            sds(vin.shape, F32),
            sds(dx1.shape, F32),
        ),
        in_specs=[hbm(), vmem(), vmem(), vmem()] + [hbm()] * 4,
        out_specs=(vmem(), vmem(), vmem(), hbm()),
        scratch_shapes=[
            like(cat),
            like(x),
            like(dx1),
            like(wq),
            like(dx1),
            dma((5,)),
            buf(ng, 4, count),
            buf(ng, 4, count),
            buf(ng, 2, na),
            buf(ng, 2, nb),
            buf(ng, na),
            buf(ng, nb),
            buf(ng + 1, flat),
            buf(ng + 1, 4, nc1 + nc2),
            buf(2, nc1),
            buf(2, nc2),
            buf(nc1),
            buf(nc2),
            pltpu.VMEM((4,) + vec.shape, F32),
            pltpu.VMEM((3,) + vec.shape, F32),
            pltpu.VMEM((ng,) + vec.shape, F32),
            dma((ng, 4)),
            dma((ng, 4)),
            dma((ng, 4)),
            dma((4, ng)),
            dma((4, ng)),
            dma((2, ng)),
            dma((2, ng)),
            dma((ng,)),
            dma((ng + 1,)),
            dma((ng,)),
            dma((ng + 1,)),
            dma((6,)),
            dma((6,)),
            dma((3 + 2 * ng,)),
            dma((3 + ng,)),
        ],
        compiler_params=params(61, collective_id=1, has_side_effects=True),
        name="scatter",
    )(grads, sums2, vec, vin, cat, x, dx1, wq)


def blocks_kernel(*refs, handed):
    g_ref, w_ref, ls_ref, rs_ref, lr_ref, rr_ref = refs[:6]
    wg_out, nl_out, nr_out, nw_out = refs[6 + handed:10 + handed]
    for n in range(handed):
        refs[10 + handed + n][...] = refs[6 + n][...]

    for i in range(g_ref.shape[0]):
        grad = g_ref[i]
        wg_out[i] = grad
        hi = grad.astype(BF16)
        low = (grad - hi.astype(F32)).astype(BF16)
        nl_out[i] = 0.5 * ls_ref[i] + 0.5 * dot_nt(hi, hi)
        turned = grad.T
        hi_t = turned.astype(BF16)
        nr_out[i] = 0.5 * rs_ref[i] + 0.5 * dot_nt(hi_t, hi_t)
        left = lr_ref[i]
        left_hi = left.astype(BF16)
        left_low = (left - left_hi.astype(F32)).astype(BF16)
        shaped = dot_nn(left_hi, hi) + dot_nn(left_hi, low) + dot_nn(left_low, hi)
        right = rr_ref[i]
        right_hi = right.astype(BF16)
        right_low = (right - right_hi.astype(F32)).astype(BF16)
        sh_hi = shaped.astype(BF16)
        sh_low = (shaped - sh_hi.astype(F32)).astype(BF16)
        shaped = dot_nn(sh_hi, right_hi) + dot_nn(sh_low, right_hi) + dot_nn(sh_hi, right_low)
        nw_out[i] = w_ref[i] - weight_rate * shaped


def run_blocks(grads, weights, left_stats, right_stats, left_roots, right_roots, *passing):
    count, side, _ = grads.shape
    steps = math.gcd(count, 4)
    step = count // steps
    spec = pl.BlockSpec((step, side, side), lambda n: (n, 0, 0))
    through = []
    for v in passing:
        part = v.shape[0] // steps
        if part % 8 == 0:
            through.append(pl.BlockSpec((part, v.shape[1]), lambda n: (n, 0)))
        else:
            through.append(pl.BlockSpec(v.shape, lambda n: (0, 0)))
    return pl.pallas_call(
        functools.partial(blocks_kernel, handed=len(passing)),
        grid=(steps,),
        out_shape=tuple([sds(grads.shape, F32)] * 4) + tuple(sds(v.shape, v.dtype) for v in passing),
        in_specs=[spec] * 6 + through,
        out_specs=tuple([spec] * 4) + tuple(through),
        compiler_params=params(),
        name="blocks",
    )(grads, weights, left_stats, right_stats, left_roots, right_roots, *passing)


def local(
    inputs,
    cotangent,
    weight_slots,
    slot_block,
    left_stats,
    right_stats,
    left_roots,
    right_roots,
    vectors,
    span_start,
):
    seq_count, tok_count, width = inputs.shape
    rows = seq_count * tok_count
    nd = lax.axis_size("dev")
    ng = lax.axis_size("grp")
    side = weight_slots.shape[1]
    hpd = H // nd
    lanes = width // nd
    head = lax.axis_index("dev") * hpd + jnp.arange(hpd, dtype=jnp.int32)
    slopes = jnp.exp2(-8.0 * (head.astype(F32) + 1.0) / H)
    vin = vectors.reshape(-1, 128)
    held = slot_block.reshape(-1, 128)
    x = inputs.reshape(rows, width)
    dy = cotangent.reshape(rows, width)
    rate = vector_rate / math.sqrt(rows * nd * ng)

    direct = nd == 8
    if direct:
        gath, h1, slot_of, vec = run_gather(weight_slots, x, held, vin, ng, nd)
    else:
        gath = lax.all_gather(weight_slots.astype(BF16), ("grp", "dev"), axis=0, tiled=True)
        h1, slot_of, vec = run_prepare(x, held, vin)
    qkv, wq = run_qkv(slot_of, h1, vec, gath, nd)
    qkv, o, o32, lse = run_attn_fwd(
        span_start, slopes, qkv.reshape(nd, 3, seq_count, tok_count, lanes), hpd
    )
    att = side_by_side(o, 1, rows)
    act, dx1, do, sums2, grads = run_mlp(slot_of, att, x, dy, vec, gath, nd)
    do = do.reshape(nd, seq_count, tok_count, lanes)
    cat = side_by_side(run_attn_bwd(span_start, slopes, qkv, do, o32, lse, hpd), 3, rows)
    grads = run_wgrad(slot_of, h1, cat, grads)
    if direct:
        weight_grads, vector_grads, new_vectors, ig = run_scatter(
            grads, sums2, vec, vin, cat, x, dx1, wq, ng, nd, rate
        )
        passing = (ig, vector_grads, new_vectors)
    else:
        ig, vsum = run_dh1(cat, x, dx1, vec, wq, sums2)
        vector_grads = lax.psum(vsum.reshape(-1), ("grp", "dev"))
        new_vectors = vectors - rate * vector_grads
        weight_grads = lax.psum_scatter(grads, ("grp", "dev"), scatter_dimension=0, tiled=True)
        weight_grads = weight_grads.astype(F32)
        passing = ()
    weight_grads, new_left, new_right, new_weights, *passed = run_blocks(
        weight_grads, weight_slots, left_stats, right_stats, left_roots, right_roots, *passing
    )
    if direct:
        ig, vector_grads, new_vectors = passed
    return (
        act.reshape(inputs.shape),
        ig.reshape(inputs.shape),
        weight_grads,
        new_left,
        new_right,
        new_weights,
        vector_grads.reshape(-1),
        new_vectors.reshape(-1),
    )


def solution(mesh):
    return jax.shard_map(
        local,
        mesh=mesh,
        in_specs=(
            P("grp", "dev", None),
            P("grp", "dev", None),
            P(("grp", "dev"), None, None),
            P(),
            P(("grp", "dev"), None, None),
            P(("grp", "dev"), None, None),
            P(("grp", "dev"), None, None),
            P(("grp", "dev"), None, None),
            P(),
            P("grp"),
        ),
        out_specs=(
            P("grp", "dev", None),
            P("grp", "dev", None),
            P(("grp", "dev"), None, None),
            P(("grp", "dev"), None, None),
            P(("grp", "dev"), None, None),
            P(("grp", "dev"), None, None),
            P(),
            P(),
        ),
        check_vma=False,
    )
```
